32 devices in a mesh: head: 2 (over y), fsdp: 16 (over z, x, core).
Axes of the slice: x: 2, y: 2, z: 4, core: 2. Of those that a mesh axis runs over, the one named last changes fastest.
Arguments:
- tokens: float32 [16, 256, 2304], P('fsdp', 'head'), may hold values from -8 to 8
- cotangent: float32 [16, 256, 2304], P('fsdp', 'head'), may hold values from -6 to 6
- gains: float32 [4, 2304], P(None, ('head', 'fsdp')), may hold values from -0.3 to 0.3
- gains_first: float32 [4, 2304], P(None, ('head', 'fsdp')), may hold values from -40 to 40
- gains_second: float32 [4, 2304], P(None, ('head', 'fsdp')), may hold values from 106.496 to 1720.32
- attn_weight: float32 [3, 2048, 2304], P(None, ('head', 'fsdp')), may hold values from -0.133680556 to 0.133680556
- attn_first: float32 [3, 2048, 2304], P(None, ('head', 'fsdp')), may hold values from -28 to 28
- attn_second: float32 [3, 2048, 2304], P(None, ('head', 'fsdp')), may hold values from 27.0336 to 1720.32
- ffn_weight: float32 [9216, 3, 2304], P(('head', 'fsdp')), may hold values from -0.125 to 0.125
- ffn_first: float32 [9216, 3, 2304], P(('head', 'fsdp')), may hold values from -40 to 40
- ffn_second: float32 [9216, 3, 2304], P(('head', 'fsdp')), may hold values from 106.496 to 1720.32
Outputs:
- output: float32 [16, 256, 2304], P('fsdp', 'head')
- tokens_grad: float32 [16, 256, 2304], P('fsdp', 'head')
- gains_first_new: float32 [4, 2304], P(None, ('head', 'fsdp'))
- gains_second_new: float32 [4, 2304], P(None, ('head', 'fsdp'))
- gains_new: float32 [4, 2304], P(None, ('head', 'fsdp'))
- attn_first_new: float32 [3, 2048, 2304], P(None, ('head', 'fsdp'))
- attn_second_new: float32 [3, 2048, 2304], P(None, ('head', 'fsdp'))
- attn_weight_new: float32 [3, 2048, 2304], P(None, ('head', 'fsdp'))
- ffn_first_new: float32 [9216, 3, 2304], P(('head', 'fsdp'))
- ffn_second_new: float32 [9216, 3, 2304], P(('head', 'fsdp'))
- ffn_weight_new: float32 [9216, 3, 2304], P(('head', 'fsdp'))
The draws below stay inside these ranges and needn't reach their ends.
All inputs are finite; a program needn't handle non-finite values.
Results may differ from the reference program's by a relative error of at most 0.023.
Values may be sent and summed in bfloat16 or wider, within the bound.
A program may use at most 576 MiB of HBM per device.

```python
import math
import jax
import jax.numpy as jnp
from jax import lax

D = 2304
HQ = 8
HK = 4
HD = 256
FF = 9216
WIN = 4096
STEP = 10
STRETCH = 256
SEQ = 4096
LENGTH = 4096
N_FSDP = 16


low_pairs = 8


key_common = 5.0


offset_low = 12.0


offset_high = 30.0


def shared_vector(key):
    return jnp.clip(jax.random.normal(key, (D,), jnp.float32), -4.0, 4.0)


def draw_tokens(key, part):
    shared = shared_vector(key)
    key = jax.random.fold_in(key, 11)
    noise = jnp.clip(jax.random.normal(key, (N_FSDP, STRETCH, D), jnp.float32), -4.0, 4.0)
    return shared[None, None, :] + noise


def draw_attn_weight(key, part):
    shared = shared_vector(key)
    key = jax.random.fold_in(key, 12)
    base_key, size_key, sign_key = jax.random.split(key, 3)
    shape = (3, HQ * HD, D)
    base = jnp.clip(jax.random.normal(base_key, shape, jnp.float32), -5.0, 5.0)
    offsets = jnp.exp(jax.random.uniform(size_key, (HQ,), jnp.float32, math.log(offset_low), math.log(offset_high)))
    signs = (2 * jax.random.randint(sign_key, (HQ,), 0, 2) - 1).astype(jnp.float32)
    query_common = signs * offsets * 16.0 / (low_pairs * key_common)
    rows = jnp.arange(HQ * HD, dtype=jnp.int32)
    within = rows % HD
    head_of = rows // HD
    half = HD // 2
    in_first = (within >= half - low_pairs) & (within < half)
    in_second = within >= HD - low_pairs
    pair = jnp.where(in_second, within - half, within).astype(jnp.float32)
    phase = 0.5 * WIN * 10000.0 ** (-2.0 * pair / HD)
    query_coef = query_common[head_of] * jnp.where(in_first, jnp.cos(phase), jnp.where(in_second, -jnp.sin(phase), 0.0))
    key_coef = jnp.where(in_first & (rows < HK * HD), key_common, 0.0)
    coef = jnp.stack([query_coef, key_coef, jnp.zeros_like(key_coef)])
    return base / math.sqrt(D) + coef[:, :, None] * shared[None, None, :] * (math.sqrt(2.0) / D)


def steps_of(key, shape, pieces, low, top_value):
    loudness = 1.0
    for position, blocks in pieces:
        steps = jax.random.uniform(jax.random.fold_in(jax.random.fold_in(key, 6), position), (blocks,), jnp.float32, low / len(pieces), top_value / len(pieces))
        loudness = loudness * jnp.repeat(jnp.exp(steps), shape[position] // blocks).reshape((-1,) + (1,) * (len(shape) - 1 - position))
    return loudness


def gaussian(rng, extent, width, limit, shards=(), kind=jnp.bfloat16):
    values = width * jax.random.normal(rng, extent, jnp.float32)
    if shards:
        values = values * steps_of(rng, extent, shards, -0.22, 0.18)
    return jnp.clip(values, -limit, limit).astype(kind)


def setup_inputs(seed: int = 0) -> dict:
    splits = jax.random.split(jax.random.key(seed), 12)
    return {
        "tokens": draw_tokens(jax.random.fold_in(splits[11], 71), 0),
        "cotangent": gaussian(splits[1], (N_FSDP, STRETCH, D), 1.0, 6.0, ((0, 16), (1, 2)), jnp.float32),
        "gains": jnp.clip(jax.random.uniform(splits[2], (4, D), jnp.float32, -0.3, 0.3) * steps_of(splits[2], (4, D), ((1, 32),), -0.4, 0.0), -0.3, 0.3),
        "gains_first": gaussian(splits[3], (4, D), (0.11 * SEQ ** 0.5), 40.0, ((1, 32),), jnp.float32),
        "gains_second": jnp.clip(jnp.exp(math.log(1720.32) - 2.7821581 * jax.random.uniform(splits[4], (4, D), jnp.float32) ** steps_of(splits[4], (4, D), ((1, 32),), -0.2, 0.2)), 106.496, 1720.32),
        "attn_weight": draw_attn_weight(jax.random.fold_in(splits[11], 71), 0),
        "attn_first": gaussian(splits[6], (3, HQ * HD, D), (0.07 * SEQ ** 0.5), 28.0, ((1, 32),), jnp.float32),
        "attn_second": jnp.clip(jnp.exp(math.log(1720.32) - 4.153185 * jax.random.uniform(splits[7], (3, HQ * HD, D), jnp.float32) ** steps_of(splits[7], (3, HQ * HD, D), ((1, 32),), -0.2, 0.2)), 27.0336, 1720.32),
        "ffn_weight": gaussian(splits[8], (FF, 3, D), D ** -0.5, 0.125, ((0, 32),), jnp.float32),
        "ffn_first": gaussian(splits[9], (FF, 3, D), (0.11 * SEQ ** 0.5), 40.0, ((0, 32),), jnp.float32),
        "ffn_second": jnp.clip(jnp.exp(math.log(1720.32) - 2.7821581 * jax.random.uniform(splits[10], (FF, 3, D), jnp.float32) ** steps_of(splits[10], (FF, 3, D), ((0, 32),), -0.2, 0.2)), 106.496, 1720.32),
    }


@jax.custom_vjp
def low(v):
    return lax.optimization_barrier(v.astype(jnp.bfloat16)).astype(jnp.float32)

@jax.custom_vjp
def low_back(v):
    return v

def low_keep(v):
    return (low(v), None)

def low_pass(kept, grad):
    return (grad,)

def back_keep(v):
    return (v, None)

def back_low(kept, grad):
    return (low(grad),)
low.defvjp(low_keep, low_pass)
low_back.defvjp(back_keep, back_low)
highest = lax.Precision.HIGHEST
eps_norm = 1e-06
softcap = 50.0
beta_one = 0.9
beta_two = 0.95
adam_eps = 1e-08
rate_matrix = 0.02
rate_gain = 0.2
decay_matrix = 0.1

def norm_scale(values, scales):
    return values * lax.rsqrt(lax.optimization_barrier(jnp.mean(values * values, axis=-1, keepdims=True)) + eps_norm) * (1.0 + scales)

def turn_angles(positions, head_width):
    halfway = head_width // 2
    inverse_freq = 10000.0 ** (-(jnp.arange(halfway, dtype=jnp.float32) * 2.0) / head_width)
    return positions.astype(jnp.float32)[:, None] * inverse_freq[None, :]

def rotate(values, angles, direction):
    halfway = values.shape[-1] // 2
    cosine = jnp.cos(angles)[:, None, :]
    sine_part = direction * jnp.sin(angles)[:, None, :]
    former = values[..., :halfway]
    latter = values[..., halfway:]
    return jnp.concatenate([former * cosine - latter * sine_part, latter * cosine + former * sine_part], axis=-1)

def adamw(weight, moment, second, gradient, step_rate, decay_rate):
    moment = beta_one * moment + (1.0 - beta_one) * gradient
    second = beta_two * second + (1.0 - beta_two) * gradient * gradient
    update = moment / (1.0 - beta_one ** STEP) / (jnp.sqrt(second / (1.0 - beta_two ** STEP)) + adam_eps) + decay_rate * weight
    return (moment, second, weight - step_rate * update)

def layer(tokens_in, gains, attn_weight, ffn_weight):
    scales = low(gains)
    w_query = low(attn_weight[0])
    w_keyval = low(attn_weight[1])
    w_out = low(attn_weight[2])
    normed_one = low(norm_scale(tokens_in, scales[0]))
    query_raw = low_back(jnp.dot(normed_one, w_query.T, precision=highest))
    keyval_raw = jnp.dot(normed_one, w_keyval.T, precision=highest)
    key_raw = low_back(keyval_raw[:, :HK * HD])
    value_all = low(low_back(keyval_raw[:, HK * HD:])).reshape(SEQ, HK, HD)
    places = jnp.arange(SEQ, dtype=jnp.int32) % LENGTH
    angles = turn_angles(places, HD)
    query_all = low(low_back(rotate(query_raw.reshape(SEQ, HQ, HD), angles, 1.0)))
    key_all = low(low_back(rotate(key_raw.reshape(SEQ, HK, HD), angles, 1.0)))
    query_grouped = query_all.reshape(SEQ, HK, HQ // HK, HD)
    query_block = min(512, SEQ)
    key_span = min(WIN + query_block, SEQ)
    scale = 1.0 / math.sqrt(HD)

    def attend(block):
        query_start = block * query_block
        key_start = jnp.clip(query_start + query_block - key_span, 0, SEQ - key_span).astype(jnp.int32)
        query_rows = lax.dynamic_slice_in_dim(query_grouped, query_start, query_block, 0)
        key_rows = lax.dynamic_slice_in_dim(key_all, key_start, key_span, 0)
        value_rows = lax.dynamic_slice_in_dim(value_all, key_start, key_span, 0)
        query_pos = query_start + jnp.arange(query_block, dtype=jnp.int32)
        key_pos = key_start + jnp.arange(key_span, dtype=jnp.int32)
        distance = query_pos[:, None] - key_pos[None, :]
        same_seq = (query_pos // LENGTH)[:, None] == (key_pos // LENGTH)[None, :]
        allowed = (distance >= 0) & (distance < WIN) & same_seq
        raw_scores = low_back(jnp.einsum('qhgd,khd->hgqk', query_rows, key_rows, precision=highest) * scale)
        capped = softcap * jnp.tanh(raw_scores / softcap)
        probs = jax.nn.softmax(jnp.where(allowed, capped, -1e+30), axis=-1)
        result = jnp.einsum('hgqk,khd->qhgd', low(probs), value_rows, precision=highest)
        return result.reshape(query_block, HQ * HD)
    block_ids = jnp.arange(SEQ // query_block, dtype=jnp.int32)
    attended = lax.map(jax.checkpoint(attend), block_ids).reshape(SEQ, HQ * HD)
    attended = low(low_back(attended))
    projected = low_back(jnp.dot(attended, w_out, precision=highest))
    resid_mid = tokens_in + norm_scale(projected, scales[1])
    normed_two = low(norm_scale(resid_mid, scales[2]))
    w_gate = low(ffn_weight[:, 0])
    w_up = low(ffn_weight[:, 1])
    w_down = low(ffn_weight[:, 2])
    ffn_block = min(4096, SEQ)

    def feed(rows_in):
        gate = low_back(jnp.dot(rows_in, w_gate.T, precision=highest))
        upward = low_back(jnp.dot(rows_in, w_up.T, precision=highest))
        hidden = low(jax.nn.gelu(gate, approximate=True) * upward)
        return low_back(jnp.dot(hidden, w_down, precision=highest))
    ffn_out = lax.map(jax.checkpoint(feed), normed_two.reshape(SEQ // ffn_block, ffn_block, D)).reshape(SEQ, D)
    return resid_mid + norm_scale(ffn_out, scales[3])

def reference(tokens, cotangent, gains, gains_first, gains_second, attn_weight, attn_first, attn_second, ffn_weight, ffn_first, ffn_second):
    flat_in = tokens.reshape(SEQ, D)
    result, back_fn = jax.vjp(layer, flat_in, gains, attn_weight, ffn_weight)
    grad_in, grad_gain, grad_attn, grad_ffn = back_fn(cotangent.reshape(SEQ, D))
    gains_first_new, gains_second_new, gains_new = adamw(gains, gains_first, gains_second, grad_gain, rate_gain, 0.0)
    attn_first_new, attn_second_new, attn_weight_new = adamw(attn_weight, attn_first, attn_second, grad_attn, rate_matrix, decay_matrix)
    ffn_first_new, ffn_second_new, ffn_weight_new = adamw(ffn_weight, ffn_first, ffn_second, grad_ffn, rate_matrix, decay_matrix)
    return (result.reshape(tokens.shape), grad_in.reshape(tokens.shape), gains_first_new, gains_second_new, gains_new, attn_first_new, attn_second_new, attn_weight_new, ffn_first_new, ffn_second_new, ffn_weight_new)
```

```python
import functools
import math

import jax
import jax.numpy as jnp
from jax import lax
from jax.experimental import pallas as pl
from jax.experimental.pallas import tpu as pltpu
from jax.sharding import PartitionSpec as P

HQ = 8
HK = 4
HD = 256
WIN = 4096
STEP = 10
SEQ_LEN = 8192


eps_norm = 1e-06
softcap = 50.0
beta_one = 0.9
beta_two = 0.95
adam_eps = 1e-08
rate_matrix = 0.02
rate_gain = 0.2
decay_matrix = 0.1

bfloat = jnp.bfloat16
single = jnp.float32
MESH = pl.DeviceIdType.MESH


def norm_scale(values, scales):
    return (
        values
        * lax.rsqrt(jnp.mean(values * values, axis=-1, keepdims=True) + eps_norm)
        * (1.0 + scales)
    )


def turn_angles(positions, head_width):
    halfway = head_width // 2
    inverse_freq = 10000.0 ** (-(jnp.arange(halfway, dtype=jnp.float32) * 2.0) / head_width)
    return positions.astype(jnp.float32)[:, None] * inverse_freq[None, :]


def rotate(values, angles, direction):
    halfway = values.shape[-1] // 2
    cosine = jnp.cos(angles)[:, None, :]
    sine_part = direction * jnp.sin(angles)[:, None, :]
    former = values[..., :halfway]
    latter = values[..., halfway:]
    return jnp.concatenate(
        [former * cosine - latter * sine_part, latter * cosine + former * sine_part], axis=-1
    )


def adamw(weight, moment, second, gradient, step_rate, decay_rate):
    moment = beta_one * moment + (1.0 - beta_one) * gradient
    second = beta_two * second + (1.0 - beta_two) * gradient * gradient
    update = (
        moment / (1.0 - beta_one**STEP) / (jnp.sqrt(second / (1.0 - beta_two**STEP)) + adam_eps)
        + decay_rate * weight
    )
    return (moment, second, weight - step_rate * update)


def hidden_unit(gate_part, up_part):
    return jax.nn.gelu(gate_part, approximate=True) * up_part


def ring_of(chip, chips):
    wide = chips // 4
    deep, side = chip // wide, chip % wide
    return side * 4 + deep + (side % 2) * (3 - 2 * deep)


def chip_of(ring, chips):
    wide = chips // 4
    side, along = ring // 4, ring % 4
    return (along + (side % 2) * (3 - 2 * along)) * wide + side


def ring_places(chips):
    index = lax.axis_index("fsdp")
    core, chip = index % 2, index // 2
    ring = ring_of(chip, chips)
    right = 2 * chip_of((ring + 1) % chips, chips) + core
    left = 2 * chip_of((ring + chips - 1) % chips, chips) + core
    return chip, ring, right, left


def ring_barrier(right, left):
    barrier = pltpu.get_barrier_semaphore()
    for neighbour in (left, right):
        pl.semaphore_signal(barrier, inc=1, device_id={"fsdp": neighbour}, device_id_type=MESH)
    pl.semaphore_wait(barrier, 2)


def region(shape, pieces, way, piece):
    rows, columns = shape
    if rows % 32 == 0:
        size = rows // 2 // pieces
        start = way * (rows // 2) + piece * size
        return (pl.ds(start, size), pl.ds(0, columns)), (pl.ds(piece * size, size), pl.ds(0, columns))
    size = columns // 2
    return (pl.ds(0, rows), pl.ds(way * size, size)), (pl.ds(0, rows), pl.ds(0, size))


def half_shape(rows, columns):
    return (rows // 2, columns) if rows % 32 == 0 else (rows, columns // 2)


def gather_kernel(chips, pieces, own_ref, all_ref, local_sem, send_sem, recv_sem):
    chip, ring, right, left = ring_places(chips)
    ring_barrier(right, left)
    keep = pltpu.make_async_copy(own_ref, all_ref.at[chip], local_sem)
    keep.start()

    def copy(way, step, piece, first):
        owner = chip_of((ring + (chips - step if way == 0 else step)) % chips, chips)
        part, ignored = region(own_ref.shape, pieces, way, piece)
        there = all_ref.at[(owner,) + part]
        return pltpu.make_async_remote_copy(
            src_ref=own_ref.at[part] if first else there,
            dst_ref=there,
            send_sem=send_sem.at[way, piece, step],
            recv_sem=recv_sem.at[way, piece, step],
            device_id={"fsdp": right if way == 0 else left},
            device_id_type=MESH,
        )

    streams = [(way, piece) for piece in range(pieces) for way in range(2)]
    for way, piece in streams:
        copy(way, 0, piece, True).start()

    def body(step, carried):
        for way, piece in streams:
            copy(way, step - 1, piece, False).wait_recv()
            copy(way, step, piece, False).start()
        return carried

    lax.fori_loop(1, chips - 1, body, 0)
    for way, piece in streams:
        copy(way, chips - 2, piece, False).wait_recv()

    def finish(step, carried):
        for way, piece in streams:
            copy(way, step, piece, False).wait_send()
        return carried

    lax.fori_loop(0, chips - 1, finish, 0)
    keep.wait()


def ring_gather(own, chips, ident):
    rows, columns = own.shape
    pieces = 2 if rows % 64 == 0 else 1
    return pl.pallas_call(
        functools.partial(gather_kernel, chips, pieces),
        out_shape=jax.ShapeDtypeStruct((chips, rows, columns), own.dtype),
        in_specs=[pl.BlockSpec(memory_space=pl.ANY)],
        out_specs=pl.BlockSpec(memory_space=pl.ANY),
        scratch_shapes=[
            pltpu.SemaphoreType.DMA,
            pltpu.SemaphoreType.DMA((2, pieces, chips - 1)),
            pltpu.SemaphoreType.DMA((2, pieces, chips - 1)),
        ],
        compiler_params=pltpu.CompilerParams(collective_id=ident, has_side_effects=True),
    )(own)


def scatter_kernel(chips, pieces, parts_ref, sum_ref, held, send_sem, recv_sem):
    chip, ring, right, left = ring_places(chips)
    ring_barrier(right, left)

    def owner_of(way, step):
        shift = chips - 1 - step if way == 0 else 1 + step
        return chip_of((ring + shift) % chips, chips)

    def copy(way, step, piece, first):
        part, place = region(sum_ref.shape, pieces, way, piece)
        return pltpu.make_async_remote_copy(
            src_ref=(
                parts_ref.at[(owner_of(way, step),) + part]
                if first
                else held.at[(way, step - 1) + place]
            ),
            dst_ref=held.at[(way, step) + place],
            send_sem=send_sem.at[way, piece, step],
            recv_sem=recv_sem.at[way, piece, step],
            device_id={"fsdp": right if way == 0 else left},
            device_id_type=MESH,
        )

    streams = [(way, piece) for piece in range(pieces) for way in range(2)]
    for way, piece in streams:
        copy(way, 0, piece, True).start()

    def arrived(way, step, piece):
        copy(way, step, piece, True).wait_recv()
        part, place = region(sum_ref.shape, pieces, way, piece)
        here = parts_ref[(owner_of(way, step + 1),) + part]
        return held[(way, step) + place].astype(single) + here.astype(single)

    def body(step, carried):
        for way, piece in streams:
            total = arrived(way, step - 1, piece)
            part, place = region(sum_ref.shape, pieces, way, piece)
            held[(way, step - 1) + place] = total.astype(held.dtype)
            copy(way, step, piece, False).start()
        return carried

    lax.fori_loop(1, chips - 1, body, 0)
    for way, piece in streams:
        part, place = region(sum_ref.shape, pieces, way, piece)
        sum_ref[part] = arrived(way, chips - 2, piece)

    def finish(step, carried):
        for way, piece in streams:
            copy(way, step, piece, True).wait_send()
        return carried

    lax.fori_loop(0, chips - 1, finish, 0)


def ring_scatter(parts, chips, ident):
    rows, columns = parts.shape[1:]
    pieces = 2 if rows % 64 == 0 else 1
    return pl.pallas_call(
        functools.partial(scatter_kernel, chips, pieces),
        out_shape=jax.ShapeDtypeStruct((rows, columns), single),
        in_specs=[pl.BlockSpec(memory_space=pltpu.VMEM)],
        out_specs=pl.BlockSpec(memory_space=pltpu.VMEM),
        scratch_shapes=[
            pltpu.VMEM((2, chips - 1) + half_shape(rows, columns), parts.dtype),
            pltpu.SemaphoreType.DMA((2, pieces, chips - 1)),
            pltpu.SemaphoreType.DMA((2, pieces, chips - 1)),
        ],
        compiler_params=pltpu.CompilerParams(
            collective_id=ident, has_side_effects=True, vmem_limit_bytes=56 * 2**20
        ),
    )(parts)


def per_device(
    tokens,
    cotangent,
    gains,
    gains_first,
    gains_second,
    attn_weight,
    attn_first,
    attn_second,
    ffn_weight,
    ffn_first,
    ffn_second,
):
    devices = lax.axis_size("fsdp")
    chips = devices // 2
    side = lax.axis_index("head")
    place = lax.axis_index("fsdp")
    core, chip = place % 2, place // 2
    tok_rows = tokens.shape[1]
    super_rows = 4 * tok_rows
    seq_len = min(SEQ_LEN, super_rows * chips)
    share = attn_weight.shape[1]
    pairs = chips // 4
    width = tokens.shape[2]
    scale = 1.0 / math.sqrt(HD)

    def swap_core(value):
        return lax.ppermute(value, "fsdp", [(index, index ^ 1) for index in range(devices)])

    def swap_side(value):
        return lax.ppermute(value, "head", [(0, 1), (1, 0)])

    def in_order(own, other, index, axis):
        return jnp.where(
            index == 0, jnp.stack([own, other], axis), jnp.stack([other, own], axis)
        )

    def pick(value, index, axis=0):
        return lax.dynamic_index_in_dim(value, index, axis, keepdims=False)

    def quad_gather(value):
        value = in_order(value, swap_side(value), side, 0)
        value = in_order(value, swap_core(value), core, 0)
        return value.reshape((super_rows,) + value.shape[3:])

    def quad_scatter(partial):
        partial = partial.reshape(2, 2, tok_rows, width)
        mine = pick(partial, core) + swap_core(pick(partial, 1 - core).astype(bfloat)).astype(single)
        return pick(mine, side) + swap_side(pick(mine, 1 - side).astype(bfloat)).astype(single)

    scales = lax.all_gather(gains.astype(bfloat), ("head", "fsdp"), axis=1, tiled=True).astype(single)
    attn_low = attn_weight.astype(bfloat)
    ffn_low = ffn_weight.astype(bfloat).transpose(1, 0, 2)
    ffn_pair = jnp.concatenate([ffn_low, swap_side(ffn_low)], axis=1)

    ring_rows = ring_gather(attn_low.reshape(3 * share, width), chips, 0)
    ring_rows = ring_rows.reshape(2, 2, pairs, 3, share, width)

    def query_rows(slot):
        rows = ring_rows[:, :, :, slot]
        other = swap_core(pick(rows, 1 - core))
        return in_order(pick(rows, core), other, core, 2).reshape(2 * HD, width)

    def keyval_rows():
        rows = ring_rows[:, :, :, 1]
        other = swap_core(pick(rows, 1 - core, 1))
        return in_order(pick(rows, core, 1), other, core, 2).reshape(2 * HD, width)

    w_query, w_keyval, w_out = query_rows(0), keyval_rows(), query_rows(2)

    resid_in = tokens[0]
    grad_out = cotangent[0]
    normed_one = norm_scale(resid_in, scales[0]).astype(bfloat)
    normed_all = quad_gather(normed_one)
    positions = chip * super_rows + jnp.arange(super_rows, dtype=jnp.int32)
    angles = turn_angles(positions % seq_len, HD)
    query_raw = jnp.einsum("td,fd->tf", normed_all, w_query, preferred_element_type=single)
    keyval_raw = jnp.einsum("td,fd->tf", normed_all, w_keyval, preferred_element_type=single)
    query = rotate(query_raw.reshape(super_rows, 2, HD), angles, 1.0).astype(bfloat)
    key_angles = jnp.where(side == 0, angles, 0.0)
    keyval = rotate(keyval_raw.reshape(super_rows, 2, HD), key_angles, 1.0).astype(bfloat)
    keyval = in_order(pick(keyval, side, 1), swap_side(pick(keyval, 1 - side, 1)), side, 0)
    keyval_all = ring_gather(keyval.reshape(2 * super_rows, HD), chips, 1)
    keyval_all = keyval_all.reshape(chips, 2, super_rows, HD)
    key_all = keyval_all[:, 0].reshape(chips * super_rows, HD)
    value_all = keyval_all[:, 1].reshape(chips * super_rows, HD)

    key_pos = jnp.arange(chips * super_rows, dtype=jnp.int32)
    distance = positions[:, None] - key_pos[None, :]
    same_seq = (positions // seq_len)[:, None] == (key_pos // seq_len)[None, :]
    allowed = (distance >= 0) & (distance < WIN) & same_seq

    def score_block():
        raw = jnp.einsum("qgd,kd->gqk", query, key_all, preferred_element_type=single)
        bent = jnp.tanh(raw * (scale / softcap))
        return bent, jnp.where(allowed, jnp.exp(softcap * bent), 0.0)

    bent, powers = score_block()
    total = jnp.sum(powers, axis=-1, keepdims=True)
    attended = jnp.einsum(
        "gqk,kd->gqd", powers.astype(bfloat), value_all, preferred_element_type=single
    )
    attended = (attended / total).transpose(1, 0, 2).reshape(super_rows, 2 * HD).astype(bfloat)
    projected = quad_scatter(jnp.dot(attended, w_out, preferred_element_type=single))
    resid_mid = resid_in + norm_scale(projected, scales[1])
    normed_two = norm_scale(resid_mid, scales[2]).astype(bfloat)

    ffn_all = jnp.concatenate([ffn_pair, swap_core(ffn_pair)], axis=1)
    w_gate, w_up, w_down = ffn_all[0], ffn_all[1], ffn_all[2]
    ring_tokens = chips * tok_rows
    normed_ring = ring_gather(normed_two, chips, 2).reshape(ring_tokens, width)
    gate_part = jnp.einsum("td,rd->tr", normed_ring, w_gate, preferred_element_type=single)
    up_part = jnp.einsum("td,rd->tr", normed_ring, w_up, preferred_element_type=single)
    hidden = hidden_unit(gate_part, up_part).astype(bfloat)
    ffn_part = jnp.dot(hidden, w_down, preferred_element_type=single).astype(bfloat)
    ffn_acc = ring_scatter(ffn_part.reshape(chips, tok_rows, width), chips, 3)
    result = resid_mid + norm_scale(ffn_acc, scales[3])

    ignored, post_back = jax.vjp(norm_scale, ffn_acc, scales[3])
    d_ffn, d_gain3 = post_back(grad_out)
    d_ffn_ring = ring_gather(d_ffn.astype(bfloat), chips, 4).reshape(ring_tokens, width)
    d_hidden = jnp.einsum("td,rd->tr", d_ffn_ring, w_down, preferred_element_type=single)
    ignored, unit_back = jax.vjp(hidden_unit, gate_part, up_part)
    d_gate, d_up = unit_back(d_hidden)
    d_gate = d_gate.astype(bfloat)
    d_up = d_up.astype(bfloat)
    d_normed = jnp.dot(d_gate, w_gate, preferred_element_type=single)
    d_normed = (d_normed + jnp.dot(d_up, w_up, preferred_element_type=single)).astype(bfloat)
    d_normed_two = ring_scatter(d_normed.reshape(chips, tok_rows, width), chips, 5)

    def ffn_rows(left, right):
        return jnp.einsum("tr,td->rd", left, right, preferred_element_type=single)

    ffn_terms = jnp.stack(
        [ffn_rows(d_gate, normed_ring), ffn_rows(d_up, normed_ring), ffn_rows(hidden, d_ffn_ring)]
    )
    units = ffn_weight.shape[0]
    ffn_terms = ffn_terms.reshape(3, 2, 2, units, width)
    ffn_terms = ffn_terms[:, 0] + swap_core(ffn_terms[:, 1].astype(bfloat)).astype(single)
    grad_ffn = ffn_terms[:, 0] + swap_side(ffn_terms[:, 1].astype(bfloat)).astype(single)

    ignored, mid_back = jax.vjp(norm_scale, resid_mid, scales[2])
    d_mid_norm, d_gain2 = mid_back(d_normed_two)
    d_mid = grad_out + d_mid_norm
    ignored, proj_back = jax.vjp(norm_scale, projected, scales[1])
    d_projected, d_gain1 = proj_back(d_mid)
    d_proj_all = quad_gather(d_projected.astype(bfloat))
    d_attended = jnp.einsum("td,fd->tf", d_proj_all, w_out, preferred_element_type=single)
    d_attended = d_attended.astype(bfloat).reshape(super_rows, 2, HD)

    bent, powers = score_block()
    probs = powers / total
    d_probs = jnp.einsum("qgd,kd->gqk", d_attended, value_all, preferred_element_type=single)
    row_dot = jnp.sum(d_probs * probs, axis=-1, keepdims=True)
    d_raw = (probs * (d_probs - row_dot) * (1.0 - bent * bent)).astype(bfloat)
    d_query = jnp.einsum("gqk,kd->qgd", d_raw, key_all, preferred_element_type=single) * scale
    d_keys = jnp.einsum("gqk,qgd->kd", d_raw, query, preferred_element_type=single) * scale
    d_values = jnp.einsum(
        "gqk,qgd->kd", probs.astype(bfloat), d_attended, preferred_element_type=single
    )
    d_pieces = jnp.stack(
        [d_keys.reshape(chips, super_rows, HD), d_values.reshape(chips, super_rows, HD)], axis=1
    ).astype(bfloat)
    d_keyval = ring_scatter(d_pieces.reshape(chips, 2 * super_rows, HD), chips, 6)
    d_keyval = d_keyval.reshape(2, super_rows, HD).astype(bfloat)
    d_keyval = in_order(pick(d_keyval, side), swap_side(pick(d_keyval, 1 - side)), side, 1)
    d_query_raw = rotate(d_query, angles, -1.0).reshape(super_rows, 2 * HD).astype(bfloat)
    d_keyval_raw = rotate(d_keyval.astype(single), key_angles, -1.0)
    d_keyval_raw = d_keyval_raw.reshape(super_rows, 2 * HD).astype(bfloat)
    d_normed_one = jnp.dot(d_query_raw, w_query, preferred_element_type=single)
    d_normed_one = d_normed_one + jnp.dot(d_keyval_raw, w_keyval, preferred_element_type=single)
    d_normed_one = quad_scatter(d_normed_one)
    ignored, first_back = jax.vjp(norm_scale, resid_in, scales[0])
    d_in_norm, d_gain0 = first_back(d_normed_one)
    tokens_grad = d_mid + d_in_norm

    def attn_rows(left, right):
        rows = jnp.einsum("tf,td->fd", left, right, preferred_element_type=single).astype(bfloat)
        return rows.reshape(2, pairs, 2, share, width)

    term_query = attn_rows(d_query_raw, normed_all)
    term_keyval = attn_rows(d_keyval_raw, normed_all)
    term_out = attn_rows(attended, d_proj_all)

    def to_core(term, axis):
        return in_order(pick(term, core, 2), swap_core(pick(term, 1 - core, 2)), core, axis)

    terms = jnp.stack([to_core(term_query, 0), to_core(term_keyval, 1), to_core(term_out, 0)], axis=3)
    grad_attn = ring_scatter(terms.reshape(chips, 3 * share, width), chips, 7)
    grad_attn = grad_attn.reshape(3, share, width)
    term_gain = jnp.stack([d_gain0, d_gain1, d_gain2, d_gain3])
    grad_gain = lax.psum_scatter(term_gain, ("head", "fsdp"), scatter_dimension=1, tiled=True)

    gains_first_new, gains_second_new, gains_new = adamw(
        gains, gains_first, gains_second, grad_gain, rate_gain, 0.0
    )
    attn_first_new, attn_second_new, attn_weight_new = adamw(
        attn_weight, attn_first, attn_second, grad_attn, rate_matrix, decay_matrix
    )
    ffn_first_new, ffn_second_new, ffn_weight_new = adamw(
        ffn_weight, ffn_first, ffn_second, grad_ffn.transpose(1, 0, 2), rate_matrix, decay_matrix
    )
    return (
        result[None],
        tokens_grad[None],
        gains_first_new,
        gains_second_new,
        gains_new,
        attn_first_new,
        attn_second_new,
        attn_weight_new,
        ffn_first_new,
        ffn_second_new,
        ffn_weight_new,
    )


def solution(mesh):
    by_token = P("fsdp", "head", None)
    by_column = P(None, ("head", "fsdp"))
    by_row = P(None, ("head", "fsdp"), None)
    by_unit = P(("head", "fsdp"), None, None)
    placed = (by_token,) * 2 + (by_column,) * 3 + (by_row,) * 3 + (by_unit,) * 3
    return jax.shard_map(
        per_device, mesh=mesh, in_specs=placed, out_specs=placed, check_vma=False
    )
```

```python
import functools
import math

import jax
import jax.numpy as jnp
from jax import lax
from jax.experimental import pallas as pl
from jax.experimental.pallas import tpu as pltpu
from jax.sharding import PartitionSpec as P

HQ = 8
HK = 4
HD = 256
WIN = 4096
STEP = 10
SEQ_LEN = 8192


eps_norm = 1e-06
softcap = 50.0
beta_one = 0.9
beta_two = 0.95
adam_eps = 1e-08
rate_matrix = 0.02
rate_gain = 0.2
decay_matrix = 0.1

bfloat = jnp.bfloat16
single = jnp.float32
MESH = pl.DeviceIdType.MESH


def norm_scale(values, scales):
    return (
        values
        * lax.rsqrt(jnp.mean(values * values, axis=-1, keepdims=True) + eps_norm)
        * (1.0 + scales)
    )


def turn_angles(positions, head_width):
    halfway = head_width // 2
    inverse_freq = 10000.0 ** (-(jnp.arange(halfway, dtype=jnp.float32) * 2.0) / head_width)
    return positions.astype(jnp.float32)[:, None] * inverse_freq[None, :]


def rotate(values, angles, direction):
    halfway = values.shape[-1] // 2
    cosine = jnp.cos(angles)[:, None, :]
    sine_part = direction * jnp.sin(angles)[:, None, :]
    former = values[..., :halfway]
    latter = values[..., halfway:]
    return jnp.concatenate(
        [former * cosine - latter * sine_part, latter * cosine + former * sine_part], axis=-1
    )


def adamw(weight, moment, second, gradient, step_rate, decay_rate):
    moment = beta_one * moment + (1.0 - beta_one) * gradient
    second = beta_two * second + (1.0 - beta_two) * gradient * gradient
    update = (
        moment / (1.0 - beta_one**STEP) / (jnp.sqrt(second / (1.0 - beta_two**STEP)) + adam_eps)
        + decay_rate * weight
    )
    return (moment, second, weight - step_rate * update)


def hidden_unit(gate_part, up_part):
    return jax.nn.gelu(gate_part, approximate=True) * up_part


def ring_of(chip, chips):
    wide = chips // 4
    deep, side = chip // wide, chip % wide
    return side * 4 + deep + (side % 2) * (3 - 2 * deep)


def chip_of(ring, chips):
    wide = chips // 4
    side, along = ring // 4, ring % 4
    return (along + (side % 2) * (3 - 2 * along)) * wide + side


def ring_places(chips):
    index = lax.axis_index("fsdp")
    core, chip = index % 2, index // 2
    ring = ring_of(chip, chips)
    right = 2 * chip_of((ring + 1) % chips, chips) + core
    left = 2 * chip_of((ring + chips - 1) % chips, chips) + core
    return chip, ring, right, left


def ring_barrier(right, left):
    barrier = pltpu.get_barrier_semaphore()
    for neighbour in (left, right):
        pl.semaphore_signal(barrier, inc=1, device_id={"fsdp": neighbour}, device_id_type=MESH)
    pl.semaphore_wait(barrier, 2)


def region(shape, pieces, way, piece):
    rows, columns = shape
    if rows % 32 == 0:
        size = rows // 2 // pieces
        start = way * (rows // 2) + piece * size
        return (pl.ds(start, size), pl.ds(0, columns)), (pl.ds(piece * size, size), pl.ds(0, columns))
    size = columns // 2
    return (pl.ds(0, rows), pl.ds(way * size, size)), (pl.ds(0, rows), pl.ds(0, size))


def half_shape(rows, columns):
    return (rows // 2, columns) if rows % 32 == 0 else (rows, columns // 2)


def gather_kernel(chips, pieces, own_ref, all_ref, local_sem, send_sem, recv_sem):
    chip, ring, right, left = ring_places(chips)
    ring_barrier(right, left)
    keep = pltpu.make_async_copy(own_ref, all_ref.at[chip], local_sem)
    keep.start()

    def copy(way, step, piece, first):
        owner = chip_of((ring + (chips - step if way == 0 else step)) % chips, chips)
        part, ignored = region(own_ref.shape, pieces, way, piece)
        there = all_ref.at[(owner,) + part]
        return pltpu.make_async_remote_copy(
            src_ref=own_ref.at[part] if first else there,
            dst_ref=there,
            send_sem=send_sem.at[way, piece, step],
            recv_sem=recv_sem.at[way, piece, step],
            device_id={"fsdp": right if way == 0 else left},
            device_id_type=MESH,
        )

    streams = [(way, piece) for piece in range(pieces) for way in range(2)]
    for way, piece in streams:
        copy(way, 0, piece, True).start()

    def body(step, carried):
        for way, piece in streams:
            copy(way, step - 1, piece, False).wait_recv()
            copy(way, step, piece, False).start()
        return carried

    lax.fori_loop(1, chips - 1, body, 0)
    for way, piece in streams:
        copy(way, chips - 2, piece, False).wait_recv()

    def finish(step, carried):
        for way, piece in streams:
            copy(way, step, piece, False).wait_send()
        return carried

    lax.fori_loop(0, chips - 1, finish, 0)
    keep.wait()


def ring_gather(own, chips, ident):
    rows, columns = own.shape
    pieces = 2 if rows % 64 == 0 else 1
    return pl.pallas_call(
        functools.partial(gather_kernel, chips, pieces),
        out_shape=jax.ShapeDtypeStruct((chips, rows, columns), own.dtype),
        in_specs=[pl.BlockSpec(memory_space=pl.ANY)],
        out_specs=pl.BlockSpec(memory_space=pl.ANY),
        scratch_shapes=[
            pltpu.SemaphoreType.DMA,
            pltpu.SemaphoreType.DMA((2, pieces, chips - 1)),
            pltpu.SemaphoreType.DMA((2, pieces, chips - 1)),
        ],
        compiler_params=pltpu.CompilerParams(collective_id=ident, has_side_effects=True),
    )(own)


def scatter_kernel(chips, pieces, parts_ref, sum_ref, held, send_sem, recv_sem):
    chip, ring, right, left = ring_places(chips)
    ring_barrier(right, left)

    def owner_of(way, step):
        shift = chips - 1 - step if way == 0 else 1 + step
        return chip_of((ring + shift) % chips, chips)

    def copy(way, step, piece, first):
        part, place = region(sum_ref.shape, pieces, way, piece)
        return pltpu.make_async_remote_copy(
            src_ref=(
                parts_ref.at[(owner_of(way, step),) + part]
                if first
                else held.at[(way, step - 1) + place]
            ),
            dst_ref=held.at[(way, step) + place],
            send_sem=send_sem.at[way, piece, step],
            recv_sem=recv_sem.at[way, piece, step],
            device_id={"fsdp": right if way == 0 else left},
            device_id_type=MESH,
        )

    streams = [(way, piece) for piece in range(pieces) for way in range(2)]
    for way, piece in streams:
        copy(way, 0, piece, True).start()

    def arrived(way, step, piece):
        copy(way, step, piece, True).wait_recv()
        part, place = region(sum_ref.shape, pieces, way, piece)
        here = parts_ref[(owner_of(way, step + 1),) + part]
        return held[(way, step) + place].astype(single) + here.astype(single)

    def body(step, carried):
        for way, piece in streams:
            total = arrived(way, step - 1, piece)
            part, place = region(sum_ref.shape, pieces, way, piece)
            held[(way, step - 1) + place] = total.astype(held.dtype)
            copy(way, step, piece, False).start()
        return carried

    lax.fori_loop(1, chips - 1, body, 0)
    for way, piece in streams:
        part, place = region(sum_ref.shape, pieces, way, piece)
        sum_ref[part] = arrived(way, chips - 2, piece)

    def finish(step, carried):
        for way, piece in streams:
            copy(way, step, piece, True).wait_send()
        return carried

    lax.fori_loop(0, chips - 1, finish, 0)


def ring_scatter(parts, chips, ident):
    rows, columns = parts.shape[1:]
    pieces = 2 if rows % 64 == 0 else 1
    return pl.pallas_call(
        functools.partial(scatter_kernel, chips, pieces),
        out_shape=jax.ShapeDtypeStruct((rows, columns), single),
        in_specs=[pl.BlockSpec(memory_space=pltpu.VMEM)],
        out_specs=pl.BlockSpec(memory_space=pltpu.VMEM),
        scratch_shapes=[
            pltpu.VMEM((2, chips - 1) + half_shape(rows, columns), parts.dtype),
            pltpu.SemaphoreType.DMA((2, pieces, chips - 1)),
            pltpu.SemaphoreType.DMA((2, pieces, chips - 1)),
        ],
        compiler_params=pltpu.CompilerParams(
            collective_id=ident, has_side_effects=True, vmem_limit_bytes=56 * 2**20
        ),
    )(parts)


def norm_back(values, scales, grad):
    inverse = lax.rsqrt(jnp.mean(values * values, axis=-1, keepdims=True) + eps_norm)
    bent = grad * (1.0 + scales)
    slope = jnp.mean(bent * values, axis=-1, keepdims=True) * (inverse * inverse * inverse)
    return bent * inverse - values * slope, jnp.sum(grad * values * inverse, axis=0, keepdims=True)


def gelu_parts(gate):
    root = math.sqrt(2.0 / math.pi)
    square = gate * gate
    bend = jnp.tanh(root * gate * (1.0 + 0.044715 * square))
    half = 0.5 * (1.0 + bend)
    slope = half + 0.5 * gate * (1.0 - bend * bend) * (root * (1.0 + 3.0 * 0.044715 * square))
    return gate * half, slope


def dot_nt(left, right):
    return lax.dot_general(left, right, (((1,), (1,)), ((), ())), preferred_element_type=single)


def dot_nn(left, right):
    return lax.dot_general(left, right, (((1,), (0,)), ((), ())), preferred_element_type=single)


def dot_tn(left, right):
    return lax.dot_general(left, right, (((0,), (0,)), ((), ())), preferred_element_type=single)


class Ring:
    def __init__(self, chips, pieces, rows, send_sem, recv_sem):
        self.chips, self.pieces, self.half = chips, pieces, rows // 2
        self.size = rows // 2 // pieces
        self.chip, self.ring, self.right, self.left = ring_places(chips)
        self.send_sem, self.recv_sem = send_sem, recv_sem
        self.streams = [(way, piece) for piece in range(pieces) for way in range(2)]

    def owner(self, way, step):
        shift = self.chips - step if way == 0 else step
        return chip_of((self.ring + shift) % self.chips, self.chips)

    def copy(self, source, target, way, piece, step):
        return pltpu.make_async_remote_copy(
            src_ref=source,
            dst_ref=target,
            send_sem=self.send_sem.at[way, piece, step],
            recv_sem=self.recv_sem.at[way, piece, step],
            device_id={"fsdp": self.right if way == 0 else self.left},
            device_id_type=MESH,
        )

    def part(self, way, piece):
        return pl.ds(way * self.half + piece * self.size, self.size)

    def place(self, piece):
        return pl.ds(piece * self.size, self.size)

    def gather_copy(self, all_ref, way, piece, step):
        there = all_ref.at[self.owner(way, step), self.part(way, piece)]
        return self.copy(there, there, way, piece, step)

    def gather_step(self, all_ref, step):
        for way, piece in self.streams:

            @pl.when(step > 0)
            def _():
                self.gather_copy(all_ref, way, piece, step - 1).wait_recv()

            @pl.when(step < self.chips - 1)
            def _():
                self.gather_copy(all_ref, way, piece, step).start()

    def scatter_copy(self, parts_ref, held, way, piece, step, first):
        source = (
            parts_ref.at[self.owner(way, step + 1), self.part(way, piece)]
            if first
            else held.at[way, step - 1, self.place(piece)]
        )
        return self.copy(source, held.at[way, step, self.place(piece)], way, piece, step)

    def scatter_total(self, parts_ref, held, way, piece, step):
        self.scatter_copy(parts_ref, held, way, piece, step, True).wait_recv()
        here = parts_ref[self.owner(way, step + 2), self.part(way, piece)]
        return held[way, step, self.place(piece)].astype(single) + here.astype(single)

    def scatter_step(self, parts_ref, held, step):
        for way, piece in self.streams:

            @pl.when(step == 0)
            def _():
                self.scatter_copy(parts_ref, held, way, piece, 0, True).start()

            @pl.when(step > 0)
            def _():
                total = self.scatter_total(parts_ref, held, way, piece, step - 1)
                held[way, step - 1, self.place(piece)] = total.astype(held.dtype)
                self.scatter_copy(parts_ref, held, way, piece, step, False).start()

    def scatter_end(self, parts_ref, held, sum_ref):
        for way, piece in self.streams:
            sum_ref[self.part(way, piece)] = self.scatter_total(
                parts_ref, held, way, piece, self.chips - 2
            )

    def finish(self, example):
        def body(step, carried):
            for way, piece in self.streams:
                self.copy(example, example, way, piece, step).wait_send()
            return carried

        lax.fori_loop(0, self.chips - 1, body, 0)


def feed_kernel(
    chips,
    pieces,
    resid_ref,
    projected_ref,
    dy_ref,
    scales_ref,
    rows0_ref,
    rows1_ref,
    rows2_ref,
    rows3_ref,
    result_ref,
    d_mid_ref,
    d_projected_ref,
    d_gains_ref,
    terms_ref,
    weights,
    x_all,
    y_all,
    mid,
    both,
    hidden,
    part,
    held_one,
    held_two,
    chunk,
    wide,
    stage,
    load_sem,
    stage_sem,
    send_sem,
    recv_sem,
):
    tok_rows, width = resid_ref.shape
    units = rows0_ref.shape[1]
    whole = 4 * units
    half = tok_rows // 2
    rings = [
        Ring(chips, pieces, tok_rows, send_sem.at[phase], recv_sem.at[phase]) for phase in range(4)
    ]
    chip = rings[0].chip
    loads = []
    for slot, ref in enumerate((rows0_ref, rows1_ref, rows2_ref, rows3_ref)):
        for kind in range(3):
            loads.append(
                pltpu.make_async_copy(
                    ref.at[kind],
                    weights.at[pl.ds(kind * whole + slot * units, units)],
                    load_sem.at[slot, kind],
                )
            )
    for load in loads:
        load.start()
    mid[...] = resid_ref[...] + norm_scale(projected_ref[...], scales_ref[1:2])
    x_all[chip] = norm_scale(mid[...], scales_ref[2:3]).astype(bfloat)
    ring_barrier(rings[0].right, rings[0].left)
    span = width // 3

    def fetch(all_ref, step):
        chunk[0:half] = all_ref[rings[0].owner(0, step), 0:half]
        chunk[half:] = all_ref[rings[0].owner(1, step), half:]

    def put(ref, step, columns, value):
        ref[rings[0].owner(0, step), 0:half, columns] = value[0:half].astype(ref.dtype)
        ref[rings[0].owner(1, step), half:, columns] = value[half:].astype(ref.dtype)

    def take(ref, step, columns):
        return jnp.concatenate(
            [
                ref[rings[0].owner(0, step), 0:half, columns],
                ref[rings[0].owner(1, step), half:, columns],
            ],
            axis=0,
        )

    def forward(step, carried):
        rings[0].gather_step(x_all, step)

        @pl.when(step == 0)
        def _():
            for load in loads:
                load.wait()

        fetch(x_all, step)

        def gate_up(tile, carried):
            rows = pl.ds(pl.multiple_of(tile * span, span), span)
            wide[:, rows] = dot_nt(chunk[...], weights[rows])
            return carried

        lax.fori_loop(0, 3, gate_up, 0)
        put(both, step, slice(None), wide[...])
        gate = wide[:, 0:whole]
        value, slope = gelu_parts(gate)
        unit = (value * wide[:, whole:]).astype(bfloat)
        put(hidden, step, slice(None), unit)

        def down(tile, carried):
            columns = pl.ds(pl.multiple_of(tile * span, span), span)
            product = dot_nn(take(hidden, step, slice(None)), weights[2 * whole :, columns])
            put(part, step, columns, product)
            return carried

        lax.fori_loop(0, 3, down, 0)
        return carried

    lax.fori_loop(0, chips, forward, 0)

    def spread(step, carried):
        rings[1].scatter_step(part, held_one, step)
        return carried

    lax.fori_loop(0, chips - 1, spread, 0)
    rings[1].scatter_end(part, held_one, wide)
    result_ref[...] = mid[...] + norm_scale(wide[...], scales_ref[3:4])
    d_ffn, d_gain = norm_back(wide[...], scales_ref[3:4], dy_ref[...])
    d_gains_ref[3:4] = d_gain
    y_all[chip] = d_ffn.astype(bfloat)
    rings[0].finish(x_all.at[0, 0 : rings[0].size])
    rings[1].finish(x_all.at[0, 0 : rings[0].size])

    def backward(step, carried):
        rings[2].gather_step(y_all, step)
        fetch(y_all, step)
        third = whole // 3

        def d_units(tile, carried):
            columns = pl.ds(pl.multiple_of(tile * third, third), third)
            rows = pl.ds(pl.multiple_of(2 * whole + tile * third, third), third)
            ups = pl.ds(pl.multiple_of(whole + tile * third, third), third)
            d_hidden = dot_nt(chunk[...], weights[rows])
            gate = take(both, step, columns).astype(single)
            upper = take(both, step, ups).astype(single)
            value, slope = gelu_parts(gate)
            put(both, step, columns, d_hidden * upper * slope)
            put(both, step, ups, d_hidden * value)
            return carried

        lax.fori_loop(0, 3, d_units, 0)

        def d_input(tile, carried):
            columns = pl.ds(pl.multiple_of(tile * span, span), span)
            product = dot_nn(take(both, step, slice(None)), weights[0 : 2 * whole, columns])
            put(part, step, columns, product)
            return carried

        lax.fori_loop(0, 3, d_input, 0)
        return carried

    lax.fori_loop(0, chips, backward, 0)
    rows_tile = stage.shape[1]
    tiles = 3 * whole // rows_tile
    upper_tiles = 2 * whole // rows_tile

    def keep(tile):
        rows = pl.ds(pl.multiple_of(tile * rows_tile, rows_tile), rows_tile)
        return pltpu.make_async_copy(stage.at[tile % 2], terms_ref.at[rows], stage_sem.at[tile % 2])

    def grads(tile):
        @pl.when(tile >= 2)
        def _():
            keep(tile - 2).wait()

        @pl.when(tile < upper_tiles)
        def _():
            columns = pl.ds(pl.multiple_of(tile * rows_tile, rows_tile), rows_tile)
            left = both[:, :, columns].reshape(chips * tok_rows, rows_tile)
            stage[tile % 2] = dot_tn(left, x_all[...].reshape(chips * tok_rows, width)).astype(bfloat)

        @pl.when(tile >= upper_tiles)
        def _():
            columns = pl.ds(
                pl.multiple_of((tile - upper_tiles) * rows_tile, rows_tile), rows_tile
            )
            left = hidden[:, :, columns].reshape(chips * tok_rows, rows_tile)
            stage[tile % 2] = dot_tn(left, y_all[...].reshape(chips * tok_rows, width)).astype(bfloat)

        keep(tile).start()

    def spread_back(step, carried):
        rings[3].scatter_step(part, held_two, step)
        grads(step)
        return carried

    lax.fori_loop(0, chips - 1, spread_back, 0)

    def rest(tile, carried):
        grads(tile)
        return carried

    lax.fori_loop(chips - 1, tiles, rest, 0)
    rings[3].scatter_end(part, held_two, wide)
    d_norm, d_gain = norm_back(mid[...], scales_ref[2:3], wide[...])
    d_gains_ref[2:3] = d_gain
    d_mid_ref[...] = dy_ref[...] + d_norm
    d_projected, d_gain = norm_back(projected_ref[...], scales_ref[1:2], d_mid_ref[...])
    d_gains_ref[1:2] = d_gain
    d_projected_ref[...] = d_projected.astype(bfloat)
    rings[2].finish(x_all.at[0, 0 : rings[0].size])
    rings[3].finish(x_all.at[0, 0 : rings[0].size])
    keep(tiles - 2).wait()
    keep(tiles - 1).wait()


def feed_forward(resid_in, projected, grad_out, scales, shares, chips, ident):
    tok_rows, width = resid_in.shape
    units = shares[0].shape[1]
    whole = 4 * units
    pieces = 2
    vmem = pl.BlockSpec(memory_space=pltpu.VMEM)
    anywhere = pl.BlockSpec(memory_space=pl.ANY)
    return pl.pallas_call(
        functools.partial(feed_kernel, chips, pieces),
        out_shape=(
            jax.ShapeDtypeStruct((tok_rows, width), single),
            jax.ShapeDtypeStruct((tok_rows, width), single),
            jax.ShapeDtypeStruct((tok_rows, width), bfloat),
            jax.ShapeDtypeStruct((4, width), single),
            jax.ShapeDtypeStruct((3 * whole, width), bfloat),
        ),
        in_specs=[vmem] * 4 + [anywhere] * 4,
        out_specs=(vmem, vmem, vmem, vmem, anywhere),
        scratch_shapes=[
            pltpu.VMEM((3 * whole, width), bfloat),
            pltpu.VMEM((chips, tok_rows, width), bfloat),
            pltpu.VMEM((chips, tok_rows, width), bfloat),
            pltpu.VMEM((tok_rows, width), single),
            pltpu.VMEM((chips, tok_rows, 2 * whole), bfloat),
            pltpu.VMEM((chips, tok_rows, whole), bfloat),
            pltpu.VMEM((chips, tok_rows, width), bfloat),
            pltpu.VMEM((2, chips - 1, tok_rows // 2, width), bfloat),
            pltpu.VMEM((2, chips - 1, tok_rows // 2, width), bfloat),
            pltpu.VMEM((tok_rows, width), bfloat),
            pltpu.VMEM((tok_rows, width), single),
            pltpu.VMEM((2, whole // 3, width), bfloat),
            pltpu.SemaphoreType.DMA((4, 3)),
            pltpu.SemaphoreType.DMA((2,)),
            pltpu.SemaphoreType.DMA((4, 2, pieces, chips - 1)),
            pltpu.SemaphoreType.DMA((4, 2, pieces, chips - 1)),
        ],
        compiler_params=pltpu.CompilerParams(
            collective_id=ident, has_side_effects=True, vmem_limit_bytes=63 * 2**20
        ),
    )(resid_in, projected, grad_out, scales, *shares)


def per_device(
    tokens,
    cotangent,
    gains,
    gains_first,
    gains_second,
    attn_weight,
    attn_first,
    attn_second,
    ffn_weight,
    ffn_first,
    ffn_second,
):
    devices = lax.axis_size("fsdp")
    chips = devices // 2
    side = lax.axis_index("head")
    place = lax.axis_index("fsdp")
    core, chip = place % 2, place // 2
    tok_rows = tokens.shape[1]
    super_rows = 4 * tok_rows
    seq_len = min(SEQ_LEN, super_rows * chips)
    share = attn_weight.shape[1]
    pairs = chips // 4
    width = tokens.shape[2]
    scale = 1.0 / math.sqrt(HD)

    def swap_core(value):
        return lax.ppermute(value, "fsdp", [(index, index ^ 1) for index in range(devices)])

    def swap_side(value):
        return lax.ppermute(value, "head", [(0, 1), (1, 0)])

    def in_order(own, other, index, axis):
        return jnp.where(
            index == 0, jnp.stack([own, other], axis), jnp.stack([other, own], axis)
        )

    def pick(value, index, axis=0):
        return lax.dynamic_index_in_dim(value, index, axis, keepdims=False)

    def quad_gather(value):
        value = in_order(value, swap_side(value), side, 0)
        value = in_order(value, swap_core(value), core, 0)
        return value.reshape((super_rows,) + value.shape[3:])

    def quad_scatter(partial):
        partial = partial.reshape(2, 2, tok_rows, width)
        mine = pick(partial, core) + swap_core(pick(partial, 1 - core).astype(bfloat)).astype(single)
        return pick(mine, side) + swap_side(pick(mine, 1 - side).astype(bfloat)).astype(single)

    scales = lax.all_gather(gains.astype(bfloat), ("head", "fsdp"), axis=1, tiled=True).astype(single)
    attn_low = attn_weight.astype(bfloat)
    ffn_low = ffn_weight.astype(bfloat).transpose(1, 0, 2)
    ffn_side = swap_side(ffn_low)
    shares = (ffn_low, ffn_side, swap_core(ffn_low), swap_core(ffn_side))

    ring_rows = ring_gather(attn_low.reshape(3 * share, width), chips, 0)
    ring_rows = ring_rows.reshape(2, 2, pairs, 3, share, width)

    def query_rows(slot):
        rows = ring_rows[:, :, :, slot]
        other = swap_core(pick(rows, 1 - core))
        return in_order(pick(rows, core), other, core, 2).reshape(2 * HD, width)

    def keyval_rows():
        rows = ring_rows[:, :, :, 1]
        other = swap_core(pick(rows, 1 - core, 1))
        return in_order(pick(rows, core, 1), other, core, 2).reshape(2 * HD, width)

    w_query, w_keyval, w_out = query_rows(0), keyval_rows(), query_rows(2)

    resid_in = tokens[0]
    grad_out = cotangent[0]
    normed_one = norm_scale(resid_in, scales[0]).astype(bfloat)
    normed_all = quad_gather(normed_one)
    positions = chip * super_rows + jnp.arange(super_rows, dtype=jnp.int32)
    angles = turn_angles(positions % seq_len, HD)
    query_raw = jnp.einsum("td,fd->tf", normed_all, w_query, preferred_element_type=single)
    keyval_raw = jnp.einsum("td,fd->tf", normed_all, w_keyval, preferred_element_type=single)
    query = rotate(query_raw.reshape(super_rows, 2, HD), angles, 1.0).astype(bfloat)
    key_angles = jnp.where(side == 0, angles, 0.0)
    keyval = rotate(keyval_raw.reshape(super_rows, 2, HD), key_angles, 1.0).astype(bfloat)
    keyval = in_order(pick(keyval, side, 1), swap_side(pick(keyval, 1 - side, 1)), side, 0)
    keyval_all = ring_gather(keyval.reshape(2 * super_rows, HD), chips, 1)
    keyval_all = keyval_all.reshape(chips, 2, super_rows, HD)
    key_all = keyval_all[:, 0].reshape(chips * super_rows, HD)
    value_all = keyval_all[:, 1].reshape(chips * super_rows, HD)

    key_pos = jnp.arange(chips * super_rows, dtype=jnp.int32)
    distance = positions[:, None] - key_pos[None, :]
    same_seq = (positions // seq_len)[:, None] == (key_pos // seq_len)[None, :]
    allowed = (distance >= 0) & (distance < WIN) & same_seq

    def score_block():
        raw = jnp.einsum("qgd,kd->gqk", query, key_all, preferred_element_type=single)
        bent = jnp.tanh(raw * (scale / softcap))
        return bent, jnp.where(allowed, jnp.exp(softcap * bent), 0.0)

    bent, powers = score_block()
    total = jnp.sum(powers, axis=-1, keepdims=True)
    attended = jnp.einsum(
        "gqk,kd->gqd", powers.astype(bfloat), value_all, preferred_element_type=single
    )
    attended = (attended / total).transpose(1, 0, 2).reshape(super_rows, 2 * HD).astype(bfloat)
    projected = quad_scatter(jnp.dot(attended, w_out, preferred_element_type=single))
    if chips * tok_rows <= 1024:
        result, d_mid, d_proj_low, gain_rows, ffn_terms = feed_forward(
            resid_in, projected, grad_out, scales, shares, chips, 2
        )
        d_gains = [gain_rows[1], gain_rows[2], gain_rows[3]]
    else:
        resid_mid = resid_in + norm_scale(projected, scales[1])
        normed_two = norm_scale(resid_mid, scales[2]).astype(bfloat)

        ffn_all = jnp.concatenate(shares, axis=1)
        w_gate, w_up, w_down = ffn_all[0], ffn_all[1], ffn_all[2]
        ring_tokens = chips * tok_rows
        normed_ring = ring_gather(normed_two, chips, 2).reshape(ring_tokens, width)
        gate_part = jnp.einsum("td,rd->tr", normed_ring, w_gate, preferred_element_type=single)
        up_part = jnp.einsum("td,rd->tr", normed_ring, w_up, preferred_element_type=single)
        hidden = hidden_unit(gate_part, up_part).astype(bfloat)
        ffn_part = jnp.dot(hidden, w_down, preferred_element_type=single).astype(bfloat)
        ffn_acc = ring_scatter(ffn_part.reshape(chips, tok_rows, width), chips, 3)
        result = resid_mid + norm_scale(ffn_acc, scales[3])

        ignored, post_back = jax.vjp(norm_scale, ffn_acc, scales[3])
        d_ffn, d_gain3 = post_back(grad_out)
        d_ffn_ring = ring_gather(d_ffn.astype(bfloat), chips, 4).reshape(ring_tokens, width)
        d_hidden = jnp.einsum("td,rd->tr", d_ffn_ring, w_down, preferred_element_type=single)
        ignored, unit_back = jax.vjp(hidden_unit, gate_part, up_part)
        d_gate, d_up = unit_back(d_hidden)
        d_gate = d_gate.astype(bfloat)
        d_up = d_up.astype(bfloat)
        d_normed = jnp.dot(d_gate, w_gate, preferred_element_type=single)
        d_normed = (d_normed + jnp.dot(d_up, w_up, preferred_element_type=single)).astype(bfloat)
        d_normed_two = ring_scatter(d_normed.reshape(chips, tok_rows, width), chips, 5)

        def ffn_rows(left, right):
            return jnp.einsum("tr,td->rd", left, right, preferred_element_type=single)

        ffn_terms = jnp.stack(
            [ffn_rows(d_gate, normed_ring), ffn_rows(d_up, normed_ring), ffn_rows(hidden, d_ffn_ring)]
        )
        ignored, mid_back = jax.vjp(norm_scale, resid_mid, scales[2])
        d_mid_norm, d_gain2 = mid_back(d_normed_two)
        d_mid = grad_out + d_mid_norm
        ignored, proj_back = jax.vjp(norm_scale, projected, scales[1])
        d_projected, d_gain1 = proj_back(d_mid)
        d_proj_low = d_projected.astype(bfloat)
        d_gains = [d_gain1, d_gain2, d_gain3]
    units = ffn_weight.shape[0]
    ffn_terms = ffn_terms.reshape(3, 2, 2, units, width)
    ffn_terms = ffn_terms[:, 0].astype(single) + swap_core(ffn_terms[:, 1].astype(bfloat)).astype(single)
    grad_ffn = ffn_terms[:, 0] + swap_side(ffn_terms[:, 1].astype(bfloat)).astype(single)

    d_proj_all = quad_gather(d_proj_low)
    d_attended = jnp.einsum("td,fd->tf", d_proj_all, w_out, preferred_element_type=single)
    d_attended = d_attended.astype(bfloat).reshape(super_rows, 2, HD)

    bent, powers = score_block()
    probs = powers / total
    d_probs = jnp.einsum("qgd,kd->gqk", d_attended, value_all, preferred_element_type=single)
    row_dot = jnp.sum(d_probs * probs, axis=-1, keepdims=True)
    d_raw = (probs * (d_probs - row_dot) * (1.0 - bent * bent)).astype(bfloat)
    d_query = jnp.einsum("gqk,kd->qgd", d_raw, key_all, preferred_element_type=single) * scale
    d_keys = jnp.einsum("gqk,qgd->kd", d_raw, query, preferred_element_type=single) * scale
    d_values = jnp.einsum(
        "gqk,qgd->kd", probs.astype(bfloat), d_attended, preferred_element_type=single
    )
    d_pieces = jnp.stack(
        [d_keys.reshape(chips, super_rows, HD), d_values.reshape(chips, super_rows, HD)], axis=1
    ).astype(bfloat)
    d_keyval = ring_scatter(d_pieces.reshape(chips, 2 * super_rows, HD), chips, 6)
    d_keyval = d_keyval.reshape(2, super_rows, HD).astype(bfloat)
    d_keyval = in_order(pick(d_keyval, side), swap_side(pick(d_keyval, 1 - side)), side, 1)
    d_query_raw = rotate(d_query, angles, -1.0).reshape(super_rows, 2 * HD).astype(bfloat)
    d_keyval_raw = rotate(d_keyval.astype(single), key_angles, -1.0)
    d_keyval_raw = d_keyval_raw.reshape(super_rows, 2 * HD).astype(bfloat)
    d_normed_one = jnp.dot(d_query_raw, w_query, preferred_element_type=single)
    d_normed_one = d_normed_one + jnp.dot(d_keyval_raw, w_keyval, preferred_element_type=single)
    d_normed_one = quad_scatter(d_normed_one)
    ignored, first_back = jax.vjp(norm_scale, resid_in, scales[0])
    d_in_norm, d_gain0 = first_back(d_normed_one)
    tokens_grad = d_mid + d_in_norm

    def attn_rows(left, right):
        rows = jnp.einsum("tf,td->fd", left, right, preferred_element_type=single).astype(bfloat)
        return rows.reshape(2, pairs, 2, share, width)

    term_query = attn_rows(d_query_raw, normed_all)
    term_keyval = attn_rows(d_keyval_raw, normed_all)
    term_out = attn_rows(attended, d_proj_all)

    def to_core(term, axis):
        return in_order(pick(term, core, 2), swap_core(pick(term, 1 - core, 2)), core, axis)

    terms = jnp.stack([to_core(term_query, 0), to_core(term_keyval, 1), to_core(term_out, 0)], axis=3)
    grad_attn = ring_scatter(terms.reshape(chips, 3 * share, width), chips, 7)
    grad_attn = grad_attn.reshape(3, share, width)
    term_gain = jnp.stack([d_gain0] + d_gains)
    grad_gain = lax.psum_scatter(term_gain, ("head", "fsdp"), scatter_dimension=1, tiled=True)

    gains_first_new, gains_second_new, gains_new = adamw(
        gains, gains_first, gains_second, grad_gain, rate_gain, 0.0
    )
    attn_first_new, attn_second_new, attn_weight_new = adamw(
        attn_weight, attn_first, attn_second, grad_attn, rate_matrix, decay_matrix
    )
    ffn_first_new, ffn_second_new, ffn_weight_new = adamw(
        ffn_weight, ffn_first, ffn_second, grad_ffn.transpose(1, 0, 2), rate_matrix, decay_matrix
    )
    return (
        result[None],
        tokens_grad[None],
        gains_first_new,
        gains_second_new,
        gains_new,
        attn_first_new,
        attn_second_new,
        attn_weight_new,
        ffn_first_new,
        ffn_second_new,
        ffn_weight_new,
    )


def solution(mesh):
    by_token = P("fsdp", "head", None)
    by_column = P(None, ("head", "fsdp"))
    by_row = P(None, ("head", "fsdp"), None)
    by_unit = P(("head", "fsdp"), None, None)
    placed = (by_token,) * 2 + (by_column,) * 3 + (by_row,) * 3 + (by_unit,) * 3
    return jax.shard_map(
        per_device, mesh=mesh, in_specs=placed, out_specs=placed, check_vma=False
    )
```

```python
import functools
import math

import jax
import jax.numpy as jnp
from jax import lax
from jax.experimental import pallas as pl
from jax.experimental.pallas import tpu as pltpu
from jax.sharding import PartitionSpec as P

HQ = 8
HK = 4
HD = 256
WIN = 4096
STEP = 10
SEQ_LEN = 8192


eps_norm = 1e-06
softcap = 50.0
beta_one = 0.9
beta_two = 0.95
adam_eps = 1e-08
rate_matrix = 0.02
rate_gain = 0.2
decay_matrix = 0.1

bfloat = jnp.bfloat16
single = jnp.float32
MESH = pl.DeviceIdType.MESH


def norm_scale(values, scales):
    return (
        values
        * lax.rsqrt(jnp.mean(values * values, axis=-1, keepdims=True) + eps_norm)
        * (1.0 + scales)
    )


def turn_angles(positions, head_width):
    halfway = head_width // 2
    inverse_freq = 10000.0 ** (-(jnp.arange(halfway, dtype=jnp.float32) * 2.0) / head_width)
    return positions.astype(jnp.float32)[:, None] * inverse_freq[None, :]


def rotate(values, angles, direction):
    halfway = values.shape[-1] // 2
    cosine = jnp.cos(angles)[:, None, :]
    sine_part = direction * jnp.sin(angles)[:, None, :]
    former = values[..., :halfway]
    latter = values[..., halfway:]
    return jnp.concatenate(
        [former * cosine - latter * sine_part, latter * cosine + former * sine_part], axis=-1
    )


def adamw(weight, moment, second, gradient, step_rate, decay_rate):
    moment = beta_one * moment + (1.0 - beta_one) * gradient
    second = beta_two * second + (1.0 - beta_two) * gradient * gradient
    update = (
        moment / (1.0 - beta_one**STEP) / (jnp.sqrt(second / (1.0 - beta_two**STEP)) + adam_eps)
        + decay_rate * weight
    )
    return (moment, second, weight - step_rate * update)


def hidden_unit(gate_part, up_part):
    return jax.nn.gelu(gate_part, approximate=True) * up_part


def ring_of(chip, chips):
    wide = chips // 4
    deep, side = chip // wide, chip % wide
    return side * 4 + deep + (side % 2) * (3 - 2 * deep)


def chip_of(ring, chips):
    wide = chips // 4
    side, along = ring // 4, ring % 4
    return (along + (side % 2) * (3 - 2 * along)) * wide + side


def ring_places(chips):
    index = lax.axis_index("fsdp")
    core, chip = index % 2, index // 2
    ring = ring_of(chip, chips)
    right = 2 * chip_of((ring + 1) % chips, chips) + core
    left = 2 * chip_of((ring + chips - 1) % chips, chips) + core
    return chip, ring, right, left


def ring_barrier(right, left):
    barrier = pltpu.get_barrier_semaphore()
    for neighbour in (left, right):
        pl.semaphore_signal(barrier, inc=1, device_id={"fsdp": neighbour}, device_id_type=MESH)
    pl.semaphore_wait(barrier, 2)


def region(shape, pieces, way, piece):
    rows, columns = shape
    if rows % 32 == 0:
        size = rows // 2 // pieces
        start = way * (rows // 2) + piece * size
        return (pl.ds(start, size), pl.ds(0, columns)), (pl.ds(piece * size, size), pl.ds(0, columns))
    size = columns // 2
    return (pl.ds(0, rows), pl.ds(way * size, size)), (pl.ds(0, rows), pl.ds(0, size))


def half_shape(rows, columns):
    return (rows // 2, columns) if rows % 32 == 0 else (rows, columns // 2)


def gather_kernel(chips, pieces, own_ref, all_ref, local_sem, send_sem, recv_sem):
    chip, ring, right, left = ring_places(chips)
    ring_barrier(right, left)
    keep = pltpu.make_async_copy(own_ref, all_ref.at[chip], local_sem)
    keep.start()

    def copy(way, step, piece, first):
        owner = chip_of((ring + (chips - step if way == 0 else step)) % chips, chips)
        part, ignored = region(own_ref.shape, pieces, way, piece)
        there = all_ref.at[(owner,) + part]
        return pltpu.make_async_remote_copy(
            src_ref=own_ref.at[part] if first else there,
            dst_ref=there,
            send_sem=send_sem.at[way, piece, step],
            recv_sem=recv_sem.at[way, piece, step],
            device_id={"fsdp": right if way == 0 else left},
            device_id_type=MESH,
        )

    streams = [(way, piece) for piece in range(pieces) for way in range(2)]
    for way, piece in streams:
        copy(way, 0, piece, True).start()

    def body(step, carried):
        for way, piece in streams:
            copy(way, step - 1, piece, False).wait_recv()
            copy(way, step, piece, False).start()
        return carried

    lax.fori_loop(1, chips - 1, body, 0)
    for way, piece in streams:
        copy(way, chips - 2, piece, False).wait_recv()

    def finish(step, carried):
        for way, piece in streams:
            copy(way, step, piece, False).wait_send()
        return carried

    lax.fori_loop(0, chips - 1, finish, 0)
    keep.wait()


def ring_gather(own, chips, ident):
    rows, columns = own.shape
    pieces = 2 if rows % 64 == 0 else 1
    return pl.pallas_call(
        functools.partial(gather_kernel, chips, pieces),
        out_shape=jax.ShapeDtypeStruct((chips, rows, columns), own.dtype),
        in_specs=[pl.BlockSpec(memory_space=pl.ANY)],
        out_specs=pl.BlockSpec(memory_space=pl.ANY),
        scratch_shapes=[
            pltpu.SemaphoreType.DMA,
            pltpu.SemaphoreType.DMA((2, pieces, chips - 1)),
            pltpu.SemaphoreType.DMA((2, pieces, chips - 1)),
        ],
        compiler_params=pltpu.CompilerParams(collective_id=ident, has_side_effects=True),
        cost_estimate=cost(45),
    )(own)


def scatter_kernel(chips, pieces, parts_ref, sum_ref, held, send_sem, recv_sem):
    chip, ring, right, left = ring_places(chips)
    ring_barrier(right, left)

    def owner_of(way, step):
        shift = chips - 1 - step if way == 0 else 1 + step
        return chip_of((ring + shift) % chips, chips)

    def copy(way, step, piece, first):
        part, place = region(sum_ref.shape, pieces, way, piece)
        return pltpu.make_async_remote_copy(
            src_ref=(
                parts_ref.at[(owner_of(way, step),) + part]
                if first
                else held.at[(way, step - 1) + place]
            ),
            dst_ref=held.at[(way, step) + place],
            send_sem=send_sem.at[way, piece, step],
            recv_sem=recv_sem.at[way, piece, step],
            device_id={"fsdp": right if way == 0 else left},
            device_id_type=MESH,
        )

    streams = [(way, piece) for piece in range(pieces) for way in range(2)]
    for way, piece in streams:
        copy(way, 0, piece, True).start()

    def arrived(way, step, piece):
        copy(way, step, piece, True).wait_recv()
        part, place = region(sum_ref.shape, pieces, way, piece)
        here = parts_ref[(owner_of(way, step + 1),) + part]
        return held[(way, step) + place].astype(single) + here.astype(single)

    def body(step, carried):
        for way, piece in streams:
            total = arrived(way, step - 1, piece)
            part, place = region(sum_ref.shape, pieces, way, piece)
            held[(way, step - 1) + place] = total.astype(held.dtype)
            copy(way, step, piece, False).start()
        return carried

    lax.fori_loop(1, chips - 1, body, 0)
    for way, piece in streams:
        part, place = region(sum_ref.shape, pieces, way, piece)
        sum_ref[part] = arrived(way, chips - 2, piece)

    def finish(step, carried):
        for way, piece in streams:
            copy(way, step, piece, True).wait_send()
        return carried

    lax.fori_loop(0, chips - 1, finish, 0)


def ring_scatter(parts, chips, ident):
    rows, columns = parts.shape[1:]
    pieces = 2 if rows % 64 == 0 else 1
    return pl.pallas_call(
        functools.partial(scatter_kernel, chips, pieces),
        out_shape=jax.ShapeDtypeStruct((rows, columns), single),
        in_specs=[pl.BlockSpec(memory_space=pltpu.VMEM)],
        out_specs=pl.BlockSpec(memory_space=pltpu.VMEM),
        scratch_shapes=[
            pltpu.VMEM((2, chips - 1) + half_shape(rows, columns), parts.dtype),
            pltpu.SemaphoreType.DMA((2, pieces, chips - 1)),
            pltpu.SemaphoreType.DMA((2, pieces, chips - 1)),
        ],
        compiler_params=pltpu.CompilerParams(
            collective_id=ident, has_side_effects=True, vmem_limit_bytes=56 * 2**20
        ),
        cost_estimate=cost(45),
    )(parts)


def norm_back(values, scales, grad):
    inverse = lax.rsqrt(jnp.mean(values * values, axis=-1, keepdims=True) + eps_norm)
    bent = grad * (1.0 + scales)
    slope = jnp.mean(bent * values, axis=-1, keepdims=True) * (inverse * inverse * inverse)
    return bent * inverse - values * slope, jnp.sum(grad * values * inverse, axis=0, keepdims=True)


def gelu_parts(gate):
    root = math.sqrt(2.0 / math.pi)
    square = gate * gate
    bend = jnp.tanh(root * gate * (1.0 + 0.044715 * square))
    half = 0.5 * (1.0 + bend)
    slope = half + 0.5 * gate * (1.0 - bend * bend) * (root * (1.0 + 3.0 * 0.044715 * square))
    return gate * half, slope


def dot_nt(left, right):
    return lax.dot_general(left, right, (((1,), (1,)), ((), ())), preferred_element_type=single)


def dot_nn(left, right):
    return lax.dot_general(left, right, (((1,), (0,)), ((), ())), preferred_element_type=single)


def dot_tn(left, right):
    return lax.dot_general(left, right, (((0,), (0,)), ((), ())), preferred_element_type=single)


class Ring:
    def __init__(self, chips, pieces, rows, send_sem, recv_sem):
        self.chips, self.pieces, self.half = chips, pieces, rows // 2
        self.size = rows // 2 // pieces
        self.chip, self.ring, self.right, self.left = ring_places(chips)
        self.send_sem, self.recv_sem = send_sem, recv_sem
        self.streams = [(way, piece) for piece in range(pieces) for way in range(2)]

    def owner(self, way, step):
        shift = self.chips - step if way == 0 else step
        return chip_of((self.ring + shift) % self.chips, self.chips)

    def copy(self, source, target, way, piece, step):
        return pltpu.make_async_remote_copy(
            src_ref=source,
            dst_ref=target,
            send_sem=self.send_sem.at[way, piece, step],
            recv_sem=self.recv_sem.at[way, piece, step],
            device_id={"fsdp": self.right if way == 0 else self.left},
            device_id_type=MESH,
        )

    def part(self, way, piece):
        return pl.ds(way * self.half + piece * self.size, self.size)

    def place(self, piece):
        return pl.ds(piece * self.size, self.size)

    def gather_copy(self, all_ref, way, piece, step):
        there = all_ref.at[self.owner(way, step), self.part(way, piece)]
        return self.copy(there, there, way, piece, step)

    def gather_step(self, all_ref, step):
        for way, piece in self.streams:

            @pl.when(step > 0)
            def _():
                self.gather_copy(all_ref, way, piece, step - 1).wait_recv()

            @pl.when(step < self.chips - 1)
            def _():
                self.gather_copy(all_ref, way, piece, step).start()

    def scatter_copy(self, parts_ref, held, way, piece, step, first):
        source = (
            parts_ref.at[self.owner(way, step + 1), self.part(way, piece)]
            if first
            else held.at[way, step - 1, self.place(piece)]
        )
        return self.copy(source, held.at[way, step, self.place(piece)], way, piece, step)

    def scatter_total(self, parts_ref, held, way, piece, step):
        self.scatter_copy(parts_ref, held, way, piece, step, True).wait_recv()
        here = parts_ref[self.owner(way, step + 2), self.part(way, piece)]
        return held[way, step, self.place(piece)].astype(single) + here.astype(single)

    def scatter_step(self, parts_ref, held, step):
        for way, piece in self.streams:

            @pl.when(step == 0)
            def _():
                self.scatter_copy(parts_ref, held, way, piece, 0, True).start()

            @pl.when(step > 0)
            def _():
                total = self.scatter_total(parts_ref, held, way, piece, step - 1)
                held[way, step - 1, self.place(piece)] = total.astype(held.dtype)
                self.scatter_copy(parts_ref, held, way, piece, step, False).start()

    def scatter_end(self, parts_ref, held, sum_ref):
        for way, piece in self.streams:
            sum_ref[self.part(way, piece)] = self.scatter_total(
                parts_ref, held, way, piece, self.chips - 2
            )

    def finish(self, example):
        def body(step, carried):
            for way, piece in self.streams:
                self.copy(example, example, way, piece, step).wait_send()
            return carried

        lax.fori_loop(0, self.chips - 1, body, 0)


def quad_peers(chips):
    side = lax.axis_index("head")
    index = lax.axis_index("fsdp")
    chip, core = index // 2, index % 2
    ring = ring_of(chip, chips)
    around = [2 * chip_of((ring + hop) % chips, chips) + core for hop in range(1, chips)]
    return side, core, {"head": 1 - side}, {"fsdp": 2 * chip + 1 - core}, around


def wide_barrier(to_side, to_core, around):
    barrier = pltpu.get_barrier_semaphore()
    for target in [to_side, to_core] + [{"fsdp": other} for other in around]:
        pl.semaphore_signal(barrier, inc=1, device_id=target, device_id_type=MESH)
    pl.semaphore_wait(barrier, 2 + len(around))


def remote(source, target, send_sem, recv_sem, device):
    return pltpu.make_async_remote_copy(
        src_ref=source,
        dst_ref=target,
        send_sem=send_sem,
        recv_sem=recv_sem,
        device_id=device,
        device_id_type=MESH,
    )


class Total:
    def __init__(self, value, near, blocks, send_sem, recv_sem, peers, chip):
        self.value, self.near, self.blocks = value, near, blocks
        self.send_sem, self.recv_sem = send_sem, recv_sem
        side, core, self.to_side, self.to_core, self.around = peers
        self.chip = chip
        self.first = remote(value.at[0], near.at[0], send_sem.at[0], recv_sem.at[0], self.to_side)
        self.second = remote(value.at[1], near.at[1], send_sem.at[1], recv_sem.at[1], self.to_core)

    def spread(self, hop):
        here = self.blocks.at[self.chip]
        return remote(
            here,
            here,
            self.send_sem.at[1 + hop],
            self.recv_sem.at[1 + hop],
            {"fsdp": self.around[hop - 1]},
        )

    def start(self):
        self.first.start()

    def over_cores(self):
        self.first.wait_recv()
        self.value[1] = self.value[0] + self.near[0]
        self.second.start()

    def over_ring(self):
        self.second.wait_recv()
        self.blocks[self.chip] = self.value[1] + self.near[1]
        for hop in range(1, len(self.around) + 1):
            self.spread(hop).start()

    def end(self):
        for hop in range(1, len(self.around) + 1):
            self.spread(hop).wait_recv()
        total = self.blocks[0]
        for other in range(1, len(self.around) + 1):
            total = total + self.blocks[other]
        self.first.wait_send()
        self.second.wait_send()
        for hop in range(1, len(self.around) + 1):
            self.spread(hop).wait_send()
        return total


def total_scratch(chips, width):
    return [
        pltpu.VMEM((2, 4, width), single),
        pltpu.VMEM((2, 4, width), single),
        pltpu.VMEM((chips, 4, width), single),
        pltpu.SemaphoreType.DMA((chips + 1,)),
        pltpu.SemaphoreType.DMA((chips + 1,)),
    ]


def turn(raw, cosine, sine):
    halfway = raw.shape[1] // 2
    former, latter = raw[:, :halfway], raw[:, halfway:]
    return jnp.concatenate(
        [former * cosine - latter * sine, latter * cosine + former * sine], axis=1
    )


def front_kernel(
    chips,
    own_ref,
    gains_ref,
    resid_ref,
    cosine_ref,
    sine_ref,
    key_cosine_ref,
    key_sine_ref,
    rows_ref,
    scales_ref,
    normed_ref,
    query_ref,
    keyval_ref,
    all_rows,
    both,
    value,
    near,
    blocks,
    total_send,
    total_recv,
    send_sem,
    recv_sem,
    place_sem,
    peer_sem,
    quad_send,
    quad_recv,
    load_sem,
):
    share, width = own_ref.shape[1:]
    half = width // 2
    pairs = chips // 4
    chip, ring, right, left = ring_places(chips)
    peers = quad_peers(chips)
    side, core, to_side, to_core, around = peers
    load = pltpu.make_async_copy(own_ref, all_rows.at[chip], load_sem)
    load.start()
    value[0] = gains_ref[...].astype(bfloat).astype(single)
    load.wait()
    wide_barrier(to_side, to_core, around)
    gains_total = Total(value, near, blocks, total_send, total_recv, peers, chip)
    gains_total.start()
    streams = [(way, slot) for slot in range(3) for way in range(2)]

    def owner_of(way, step):
        return chip_of((ring + (chips - step if way == 0 else step)) % chips, chips)

    def hop(way, slot, step):
        there = all_rows.at[owner_of(way, step), slot, :, pl.ds(way * half, half)]
        return remote(
            there,
            there,
            send_sem.at[way, slot, step],
            recv_sem.at[way, slot, step],
            {"fsdp": right if way == 0 else left},
        )

    def goal(way, slot, step):
        owner = owner_of(way, step)
        deep = owner // pairs
        unit = (owner % pairs) * 2 + core
        taker, head = (deep % 2, deep // 2) if slot == 1 else (deep // 2, deep % 2)
        columns = pl.ds(way * half, half)
        source = all_rows.at[owner, slot, :, columns]
        start = pl.multiple_of(head * HD + unit * share, share)
        target = rows_ref.at[slot, pl.ds(start, share), columns]
        here = pltpu.make_async_copy(source, target, place_sem.at[way, slot, step])
        there = remote(
            source, target, place_sem.at[way, slot, step], peer_sem.at[way, slot, step], to_core
        )
        return taker, here, there

    def place(way, slot, step):
        taker, here, there = goal(way, slot, step)

        @pl.when(taker == core)
        def _():
            here.start()

        @pl.when(taker != core)
        def _():
            there.start()

    for way, slot in streams:
        hop(way, slot, 0).start()
    gains_total.over_cores()
    for way, slot in streams:
        place(way, slot, 0)
    gains_total.over_ring()
    scales_ref[...] = gains_total.end()
    normed_ref[core, side] = norm_scale(resid_ref[...], scales_ref[0:1]).astype(bfloat)
    along = remote(
        normed_ref.at[core, side],
        normed_ref.at[core, side],
        quad_send.at[0],
        quad_recv.at[0],
        to_side,
    )
    across = remote(
        normed_ref.at[core], normed_ref.at[core], quad_send.at[1], quad_recv.at[1], to_core
    )
    along.start()

    def body(step, carried):
        for way, slot in streams:
            hop(way, slot, step - 1).wait_recv()

            @pl.when(step < chips - 1)
            def _():
                hop(way, slot, step).start()

            place(way, slot, step)

        @pl.when(step == 2)
        def _():
            along.wait()
            across.start()

        return carried

    lax.fori_loop(1, chips, body, 0)

    def settle(step, carried):
        for way, slot in streams:
            taker, here, there = goal(way, slot, step)

            @pl.when(taker == core)
            def _():
                here.wait()
                there.wait_recv()

            @pl.when(taker != core)
            def _():
                there.wait_send()

            @pl.when(step < chips - 1)
            def _():
                hop(way, slot, step).wait_send()

        return carried

    across.wait()
    lax.fori_loop(0, chips, settle, 0)
    tokens = 4 * resid_ref.shape[0]
    normed = normed_ref[...].reshape(tokens, width)
    for head in range(2):
        rows = slice(head * HD, head * HD + HD)
        raw = dot_nt(normed, rows_ref[1, rows])
        both[head] = turn(raw, key_cosine_ref[...], key_sine_ref[...]).astype(bfloat)
    swap = remote(
        both.at[1 - side], keyval_ref.at[side], quad_send.at[2], quad_recv.at[2], to_side
    )
    swap.start()
    keyval_ref[side] = both[side]
    for head in range(2):
        rows = slice(head * HD, head * HD + HD)
        raw = dot_nt(normed, rows_ref[0, rows])
        query_ref[head] = turn(raw, cosine_ref[...], sine_ref[...]).astype(bfloat)
    swap.wait()


def cost(micros):
    return pl.CostEstimate(flops=int(micros * 1e9), bytes_accessed=0, transcendentals=0)


def front(attn_low, gains, resid_in, cosine, sine, key_cosine, key_sine, chips, ident):
    share, width = attn_low.shape[1:]
    tok_rows = resid_in.shape[0]
    vmem = pl.BlockSpec(memory_space=pltpu.VMEM)
    anywhere = pl.BlockSpec(memory_space=pl.ANY)
    return pl.pallas_call(
        functools.partial(front_kernel, chips),
        out_shape=(
            jax.ShapeDtypeStruct((3, 2 * HD, width), bfloat),
            jax.ShapeDtypeStruct((4, width), single),
            jax.ShapeDtypeStruct((2, 2, tok_rows, width), bfloat),
            jax.ShapeDtypeStruct((2, 4 * tok_rows, HD), bfloat),
            jax.ShapeDtypeStruct((2, 4 * tok_rows, HD), bfloat),
        ),
        in_specs=[anywhere] + [vmem] * 6,
        out_specs=(vmem,) * 5,
        scratch_shapes=[
            pltpu.VMEM((chips, 3, share, width), bfloat),
            pltpu.VMEM((2, 4 * tok_rows, HD), bfloat),
        ]
        + total_scratch(chips, width)
        + [
            pltpu.SemaphoreType.DMA((2, 3, chips - 1)),
            pltpu.SemaphoreType.DMA((2, 3, chips - 1)),
            pltpu.SemaphoreType.DMA((2, 3, chips)),
            pltpu.SemaphoreType.DMA((2, 3, chips)),
            pltpu.SemaphoreType.DMA((3,)),
            pltpu.SemaphoreType.DMA((3,)),
            pltpu.SemaphoreType.DMA,
        ],
        compiler_params=pltpu.CompilerParams(
            collective_id=ident, has_side_effects=True, vmem_limit_bytes=48 * 2**20
        ),
        cost_estimate=cost(75),
    )(attn_low, gains, resid_in, cosine, sine, key_cosine, key_sine)


def last_kernel(
    chips,
    pieces,
    parts_ref,
    quads_ref,
    resid_ref,
    d_mid_ref,
    scales_ref,
    gains_ref,
    sum_ref,
    tokens_ref,
    total_ref,
    held,
    across_got,
    along_put,
    along_got,
    kept,
    value,
    near,
    blocks,
    total_send,
    total_recv,
    send_sem,
    recv_sem,
    quad_send,
    quad_recv,
):
    peers = quad_peers(chips)
    side, core, to_side, to_core, around = peers
    ring = Ring(chips, pieces, sum_ref.shape[0], send_sem, recv_sem)
    wide_barrier(to_side, to_core, around)
    gains_total = Total(value, near, blocks, total_send, total_recv, peers, ring.chip)
    across = remote(
        quads_ref.at[1 - core], across_got, quad_send.at[0], quad_recv.at[0], to_core
    )
    along = remote(along_put, along_got, quad_send.at[1], quad_recv.at[1], to_side)
    across.start()

    def body(step, carried):
        ring.scatter_step(parts_ref, held, step)

        @pl.when(step == 1)
        def _():
            across.wait()
            other = quads_ref[core, 1 - side].astype(single)
            along_put[...] = (other + across_got[1 - side].astype(single)).astype(bfloat)
            along.start()
            kept[...] = quads_ref[core, side].astype(single) + across_got[side].astype(single)

        @pl.when(step == 3)
        def _():
            along.wait()
            kept[...] = kept[...] + along_got[...].astype(single)
            d_norm, d_gain = norm_back(resid_ref[...], scales_ref[0:1], kept[...])
            tokens_ref[...] = d_mid_ref[...] + d_norm
            value[0] = gains_ref[...]
            value[0, 0:1] = d_gain
            gains_total.start()

        @pl.when(step == 4)
        def _():
            gains_total.over_cores()

        @pl.when(step == 5)
        def _():
            gains_total.over_ring()

        return carried

    lax.fori_loop(0, chips - 1, body, 0)
    total_ref[...] = gains_total.end()
    ring.scatter_end(parts_ref, held, sum_ref)
    ring.finish(parts_ref.at[0, 0 : ring.size])


def last(parts, quads, resid_in, d_mid, scales, gain_rows, chips, ident):
    rows, width = parts.shape[1:]
    tok_rows = resid_in.shape[0]
    pieces = 2
    vmem = pl.BlockSpec(memory_space=pltpu.VMEM)
    return pl.pallas_call(
        functools.partial(last_kernel, chips, pieces),
        out_shape=(
            jax.ShapeDtypeStruct((rows, width), single),
            jax.ShapeDtypeStruct((tok_rows, width), single),
            jax.ShapeDtypeStruct((4, width), single),
        ),
        in_specs=[vmem] * 6,
        out_specs=(vmem,) * 3,
        scratch_shapes=[
            pltpu.VMEM((2, chips - 1, rows // 2, width), bfloat),
            pltpu.VMEM((2, tok_rows, width), bfloat),
            pltpu.VMEM((tok_rows, width), bfloat),
            pltpu.VMEM((tok_rows, width), bfloat),
            pltpu.VMEM((tok_rows, width), single),
        ]
        + total_scratch(chips, width)
        + [
            pltpu.SemaphoreType.DMA((2, pieces, chips - 1)),
            pltpu.SemaphoreType.DMA((2, pieces, chips - 1)),
            pltpu.SemaphoreType.DMA((2,)),
            pltpu.SemaphoreType.DMA((2,)),
        ],
        compiler_params=pltpu.CompilerParams(
            collective_id=ident, has_side_effects=True, vmem_limit_bytes=48 * 2**20
        ),
        cost_estimate=cost(75),
    )(parts, quads, resid_in, d_mid, scales, gain_rows)


def feed_kernel(
    chips,
    pieces,
    resid_ref,
    projected_ref,
    dy_ref,
    scales_ref,
    rows0_ref,
    rows1_ref,
    rows2_ref,
    rows3_ref,
    result_ref,
    d_mid_ref,
    d_projected_ref,
    d_gains_ref,
    terms_ref,
    other_ref,
    weights,
    x_all,
    y_all,
    mid,
    both,
    hidden,
    part,
    held_one,
    held_two,
    chunk,
    wide,
    stage,
    load_sem,
    stage_sem,
    other_sem,
    send_sem,
    recv_sem,
):
    tok_rows, width = resid_ref.shape
    units = rows0_ref.shape[1]
    whole = 4 * units
    half = tok_rows // 2
    rings = [
        Ring(chips, pieces, tok_rows, send_sem.at[phase], recv_sem.at[phase]) for phase in range(4)
    ]
    chip = rings[0].chip
    loads = []
    for slot, ref in enumerate((rows0_ref, rows1_ref, rows2_ref, rows3_ref)):
        for kind in range(3):
            loads.append(
                pltpu.make_async_copy(
                    ref.at[kind],
                    weights.at[pl.ds(kind * whole + slot * units, units)],
                    load_sem.at[slot, kind],
                )
            )
    for load in loads:
        load.start()
    mid[...] = resid_ref[...] + norm_scale(projected_ref[...], scales_ref[1:2])
    x_all[chip] = norm_scale(mid[...], scales_ref[2:3]).astype(bfloat)
    core = lax.axis_index("fsdp") % 2
    to_core = {"fsdp": 2 * chip + 1 - core}
    barrier = pltpu.get_barrier_semaphore()
    for target in ({"fsdp": rings[0].right}, {"fsdp": rings[0].left}, to_core):
        pl.semaphore_signal(barrier, inc=1, device_id=target, device_id_type=MESH)
    pl.semaphore_wait(barrier, 3)
    span = width // 3

    def fetch(all_ref, step):
        chunk[0:half] = all_ref[rings[0].owner(0, step), 0:half]
        chunk[half:] = all_ref[rings[0].owner(1, step), half:]

    def put(ref, step, columns, value):
        ref[rings[0].owner(0, step), 0:half, columns] = value[0:half].astype(ref.dtype)
        ref[rings[0].owner(1, step), half:, columns] = value[half:].astype(ref.dtype)

    def take(ref, step, columns):
        return jnp.concatenate(
            [
                ref[rings[0].owner(0, step), 0:half, columns],
                ref[rings[0].owner(1, step), half:, columns],
            ],
            axis=0,
        )

    def forward(step, carried):
        rings[0].gather_step(x_all, step)

        @pl.when(step == 0)
        def _():
            for load in loads:
                load.wait()

        fetch(x_all, step)

        def gate_up(tile, carried):
            rows = pl.ds(pl.multiple_of(tile * span, span), span)
            wide[:, rows] = dot_nt(chunk[...], weights[rows])
            return carried

        lax.fori_loop(0, 3, gate_up, 0)
        put(both, step, slice(None), wide[...])
        gate = wide[:, 0:whole]
        value, slope = gelu_parts(gate)
        unit = (value * wide[:, whole:]).astype(bfloat)
        put(hidden, step, slice(None), unit)

        def down(tile, carried):
            columns = pl.ds(pl.multiple_of(tile * span, span), span)
            product = dot_nn(take(hidden, step, slice(None)), weights[2 * whole :, columns])
            put(part, step, columns, product)
            return carried

        lax.fori_loop(0, 3, down, 0)
        return carried

    lax.fori_loop(0, chips, forward, 0)

    def spread(step, carried):
        rings[1].scatter_step(part, held_one, step)
        return carried

    lax.fori_loop(0, chips - 1, spread, 0)
    rings[1].scatter_end(part, held_one, wide)
    result_ref[...] = mid[...] + norm_scale(wide[...], scales_ref[3:4])
    d_ffn, d_gain = norm_back(wide[...], scales_ref[3:4], dy_ref[...])
    d_gains_ref[0:1] = jnp.zeros_like(d_gain)
    d_gains_ref[3:4] = d_gain
    y_all[chip] = d_ffn.astype(bfloat)
    rings[0].finish(x_all.at[0, 0 : rings[0].size])
    rings[1].finish(x_all.at[0, 0 : rings[0].size])

    def backward(step, carried):
        rings[2].gather_step(y_all, step)
        fetch(y_all, step)
        third = whole // 3

        def d_units(tile, carried):
            columns = pl.ds(pl.multiple_of(tile * third, third), third)
            rows = pl.ds(pl.multiple_of(2 * whole + tile * third, third), third)
            ups = pl.ds(pl.multiple_of(whole + tile * third, third), third)
            d_hidden = dot_nt(chunk[...], weights[rows])
            gate = take(both, step, columns).astype(single)
            upper = take(both, step, ups).astype(single)
            value, slope = gelu_parts(gate)
            put(both, step, columns, d_hidden * upper * slope)
            put(both, step, ups, d_hidden * value)
            return carried

        lax.fori_loop(0, 3, d_units, 0)

        def d_input(tile, carried):
            columns = pl.ds(pl.multiple_of(tile * span, span), span)
            product = dot_nn(take(both, step, slice(None)), weights[0 : 2 * whole, columns])
            put(part, step, columns, product)
            return carried

        lax.fori_loop(0, 3, d_input, 0)
        return carried

    lax.fori_loop(0, chips, backward, 0)
    rows_tile = stage.shape[1]
    tiles = 3 * whole // rows_tile
    upper_tiles = 2 * whole // rows_tile

    cut = units // 3

    def pieces_of(tile):
        for quarter in range(4):
            block = 4 * tile + quarter
            kind, slot, third = block // 12, (block // 3) % 4, block % 3
            source = stage.at[tile % 2, pl.ds(quarter * cut, cut)]
            rows = pl.ds(pl.multiple_of(third * cut, cut), cut)
            here = pltpu.make_async_copy(
                source, terms_ref.at[slot, kind, rows], stage_sem.at[tile % 2, quarter]
            )
            there = remote(
                source,
                other_ref.at[slot - 2, kind, rows],
                stage_sem.at[tile % 2, quarter],
                other_sem.at[tile, quarter],
                to_core,
            )
            yield slot, here, there

    def keep(tile):
        for slot, here, there in pieces_of(tile):

            @pl.when(slot < 2)
            def _():
                here.start()

            @pl.when(slot >= 2)
            def _():
                there.start()

    def kept(tile):
        for slot, here, there in pieces_of(tile):

            @pl.when(slot < 2)
            def _():
                here.wait()

            @pl.when(slot >= 2)
            def _():
                there.wait_send()

    def grads(tile):
        @pl.when(tile >= 2)
        def _():
            kept(tile - 2)

        @pl.when(tile < upper_tiles)
        def _():
            columns = pl.ds(pl.multiple_of(tile * rows_tile, rows_tile), rows_tile)
            left = both[:, :, columns].reshape(chips * tok_rows, rows_tile)
            stage[tile % 2] = dot_tn(left, x_all[...].reshape(chips * tok_rows, width)).astype(bfloat)

        @pl.when(tile >= upper_tiles)
        def _():
            columns = pl.ds(
                pl.multiple_of((tile - upper_tiles) * rows_tile, rows_tile), rows_tile
            )
            left = hidden[:, :, columns].reshape(chips * tok_rows, rows_tile)
            stage[tile % 2] = dot_tn(left, y_all[...].reshape(chips * tok_rows, width)).astype(bfloat)

        keep(tile)

    def spread_back(step, carried):
        rings[3].scatter_step(part, held_two, step)
        grads(step)
        return carried

    lax.fori_loop(0, chips - 1, spread_back, 0)

    def rest(tile, carried):
        grads(tile)
        return carried

    lax.fori_loop(chips - 1, tiles, rest, 0)
    rings[3].scatter_end(part, held_two, wide)
    d_norm, d_gain = norm_back(mid[...], scales_ref[2:3], wide[...])
    d_gains_ref[2:3] = d_gain
    d_mid_ref[...] = dy_ref[...] + d_norm
    d_projected, d_gain = norm_back(projected_ref[...], scales_ref[1:2], d_mid_ref[...])
    d_gains_ref[1:2] = d_gain
    d_projected_ref[...] = d_projected.astype(bfloat)
    rings[2].finish(x_all.at[0, 0 : rings[0].size])
    rings[3].finish(x_all.at[0, 0 : rings[0].size])
    kept(tiles - 2)
    kept(tiles - 1)

    def gained(tile, carried):
        for slot, here, there in pieces_of(tile):

            @pl.when(slot >= 2)
            def _():
                there.wait_recv()

        return carried

    lax.fori_loop(0, tiles, gained, 0)


def feed_forward(resid_in, projected, grad_out, scales, shares, chips, ident):
    tok_rows, width = resid_in.shape
    units = shares[0].shape[1]
    whole = 4 * units
    pieces = 2
    vmem = pl.BlockSpec(memory_space=pltpu.VMEM)
    anywhere = pl.BlockSpec(memory_space=pl.ANY)
    return pl.pallas_call(
        functools.partial(feed_kernel, chips, pieces),
        out_shape=(
            jax.ShapeDtypeStruct((tok_rows, width), single),
            jax.ShapeDtypeStruct((tok_rows, width), single),
            jax.ShapeDtypeStruct((tok_rows, width), bfloat),
            jax.ShapeDtypeStruct((4, width), single),
            jax.ShapeDtypeStruct((2, 3, units, width), bfloat),
            jax.ShapeDtypeStruct((2, 3, units, width), bfloat),
        ),
        in_specs=[vmem] * 4 + [anywhere] * 4,
        out_specs=(vmem, vmem, vmem, vmem, anywhere, anywhere),
        scratch_shapes=[
            pltpu.VMEM((3 * whole, width), bfloat),
            pltpu.VMEM((chips, tok_rows, width), bfloat),
            pltpu.VMEM((chips, tok_rows, width), bfloat),
            pltpu.VMEM((tok_rows, width), single),
            pltpu.VMEM((chips, tok_rows, 2 * whole), bfloat),
            pltpu.VMEM((chips, tok_rows, whole), bfloat),
            pltpu.VMEM((chips, tok_rows, width), bfloat),
            pltpu.VMEM((2, chips - 1, tok_rows // 2, width), bfloat),
            pltpu.VMEM((2, chips - 1, tok_rows // 2, width), bfloat),
            pltpu.VMEM((tok_rows, width), bfloat),
            pltpu.VMEM((tok_rows, width), single),
            pltpu.VMEM((2, whole // 3, width), bfloat),
            pltpu.SemaphoreType.DMA((4, 3)),
            pltpu.SemaphoreType.DMA((2, 4)),
            pltpu.SemaphoreType.DMA((9, 4)),
            pltpu.SemaphoreType.DMA((4, 2, pieces, chips - 1)),
            pltpu.SemaphoreType.DMA((4, 2, pieces, chips - 1)),
        ],
        compiler_params=pltpu.CompilerParams(
            collective_id=ident, has_side_effects=True, vmem_limit_bytes=63 * 2**20
        ),
        cost_estimate=cost(205),
    )(resid_in, projected, grad_out, scales, *shares)


def general_device(
    tokens,
    cotangent,
    gains,
    gains_first,
    gains_second,
    attn_weight,
    attn_first,
    attn_second,
    ffn_weight,
    ffn_first,
    ffn_second,
):
    devices = lax.axis_size("fsdp")
    chips = devices // 2
    side = lax.axis_index("head")
    place = lax.axis_index("fsdp")
    core, chip = place % 2, place // 2
    tok_rows = tokens.shape[1]
    super_rows = 4 * tok_rows
    seq_len = min(SEQ_LEN, super_rows * chips)
    share = attn_weight.shape[1]
    pairs = chips // 4
    width = tokens.shape[2]
    scale = 1.0 / math.sqrt(HD)

    def swap_core(value):
        return lax.ppermute(value, "fsdp", [(index, index ^ 1) for index in range(devices)])

    def swap_side(value):
        return lax.ppermute(value, "head", [(0, 1), (1, 0)])

    def in_order(own, other, index, axis):
        return jnp.where(
            index == 0, jnp.stack([own, other], axis), jnp.stack([other, own], axis)
        )

    def pick(value, index, axis=0):
        return lax.dynamic_index_in_dim(value, index, axis, keepdims=False)

    def quad_gather(value):
        value = in_order(value, swap_side(value), side, 0)
        value = in_order(value, swap_core(value), core, 0)
        return value.reshape((super_rows,) + value.shape[3:])

    def quad_scatter(partial):
        partial = partial.reshape(2, 2, tok_rows, width)
        mine = pick(partial, core) + swap_core(pick(partial, 1 - core).astype(bfloat)).astype(single)
        return pick(mine, side) + swap_side(pick(mine, 1 - side).astype(bfloat)).astype(single)

    scales = lax.all_gather(gains.astype(bfloat), ("head", "fsdp"), axis=1, tiled=True).astype(single)
    attn_low = attn_weight.astype(bfloat)
    ffn_low = ffn_weight.astype(bfloat).transpose(1, 0, 2)
    ffn_pair = jnp.concatenate([ffn_low, swap_side(ffn_low)], axis=1)

    ring_rows = ring_gather(attn_low.reshape(3 * share, width), chips, 0)
    ring_rows = ring_rows.reshape(2, 2, pairs, 3, share, width)

    def query_rows(slot):
        rows = ring_rows[:, :, :, slot]
        other = swap_core(pick(rows, 1 - core))
        return in_order(pick(rows, core), other, core, 2).reshape(2 * HD, width)

    def keyval_rows():
        rows = ring_rows[:, :, :, 1]
        other = swap_core(pick(rows, 1 - core, 1))
        return in_order(pick(rows, core, 1), other, core, 2).reshape(2 * HD, width)

    w_query, w_keyval, w_out = query_rows(0), keyval_rows(), query_rows(2)

    resid_in = tokens[0]
    grad_out = cotangent[0]
    normed_one = norm_scale(resid_in, scales[0]).astype(bfloat)
    normed_all = quad_gather(normed_one)
    positions = chip * super_rows + jnp.arange(super_rows, dtype=jnp.int32)
    angles = turn_angles(positions % seq_len, HD)
    query_raw = jnp.einsum("td,fd->tf", normed_all, w_query, preferred_element_type=single)
    keyval_raw = jnp.einsum("td,fd->tf", normed_all, w_keyval, preferred_element_type=single)
    query = rotate(query_raw.reshape(super_rows, 2, HD), angles, 1.0).astype(bfloat)
    key_angles = jnp.where(side == 0, angles, 0.0)
    keyval = rotate(keyval_raw.reshape(super_rows, 2, HD), key_angles, 1.0).astype(bfloat)
    keyval = in_order(pick(keyval, side, 1), swap_side(pick(keyval, 1 - side, 1)), side, 0)
    keyval_all = ring_gather(keyval.reshape(2 * super_rows, HD), chips, 1)
    keyval_all = keyval_all.reshape(chips, 2, super_rows, HD)
    key_all = keyval_all[:, 0].reshape(chips * super_rows, HD)
    value_all = keyval_all[:, 1].reshape(chips * super_rows, HD)

    key_pos = jnp.arange(chips * super_rows, dtype=jnp.int32)
    distance = positions[:, None] - key_pos[None, :]
    same_seq = (positions // seq_len)[:, None] == (key_pos // seq_len)[None, :]
    allowed = (distance >= 0) & (distance < WIN) & same_seq

    def score_block():
        raw = jnp.einsum("qgd,kd->gqk", query, key_all, preferred_element_type=single)
        bent = jnp.tanh(raw * (scale / softcap))
        return bent, jnp.where(allowed, jnp.exp(softcap * bent), 0.0)

    bent, powers = score_block()
    total = jnp.sum(powers, axis=-1, keepdims=True)
    attended = jnp.einsum(
        "gqk,kd->gqd", powers.astype(bfloat), value_all, preferred_element_type=single
    )
    attended = (attended / total).transpose(1, 0, 2).reshape(super_rows, 2 * HD).astype(bfloat)
    projected = quad_scatter(jnp.dot(attended, w_out, preferred_element_type=single))
    resid_mid = resid_in + norm_scale(projected, scales[1])
    normed_two = norm_scale(resid_mid, scales[2]).astype(bfloat)

    ffn_all = jnp.concatenate([ffn_pair, swap_core(ffn_pair)], axis=1)
    w_gate, w_up, w_down = ffn_all[0], ffn_all[1], ffn_all[2]
    ring_tokens = chips * tok_rows
    normed_ring = ring_gather(normed_two, chips, 2).reshape(ring_tokens, width)
    gate_part = jnp.einsum("td,rd->tr", normed_ring, w_gate, preferred_element_type=single)
    up_part = jnp.einsum("td,rd->tr", normed_ring, w_up, preferred_element_type=single)
    hidden = hidden_unit(gate_part, up_part).astype(bfloat)
    ffn_part = jnp.dot(hidden, w_down, preferred_element_type=single).astype(bfloat)
    ffn_acc = ring_scatter(ffn_part.reshape(chips, tok_rows, width), chips, 3)
    result = resid_mid + norm_scale(ffn_acc, scales[3])

    ignored, post_back = jax.vjp(norm_scale, ffn_acc, scales[3])
    d_ffn, d_gain3 = post_back(grad_out)
    d_ffn_ring = ring_gather(d_ffn.astype(bfloat), chips, 4).reshape(ring_tokens, width)
    d_hidden = jnp.einsum("td,rd->tr", d_ffn_ring, w_down, preferred_element_type=single)
    ignored, unit_back = jax.vjp(hidden_unit, gate_part, up_part)
    d_gate, d_up = unit_back(d_hidden)
    d_gate = d_gate.astype(bfloat)
    d_up = d_up.astype(bfloat)
    d_normed = jnp.dot(d_gate, w_gate, preferred_element_type=single)
    d_normed = (d_normed + jnp.dot(d_up, w_up, preferred_element_type=single)).astype(bfloat)
    d_normed_two = ring_scatter(d_normed.reshape(chips, tok_rows, width), chips, 5)

    def ffn_rows(left, right):
        return jnp.einsum("tr,td->rd", left, right, preferred_element_type=single)

    ffn_terms = jnp.stack(
        [ffn_rows(d_gate, normed_ring), ffn_rows(d_up, normed_ring), ffn_rows(hidden, d_ffn_ring)]
    )
    units = ffn_weight.shape[0]
    ffn_terms = ffn_terms.reshape(3, 2, 2, units, width)
    ffn_terms = ffn_terms[:, 0] + swap_core(ffn_terms[:, 1].astype(bfloat)).astype(single)
    grad_ffn = ffn_terms[:, 0] + swap_side(ffn_terms[:, 1].astype(bfloat)).astype(single)

    ignored, mid_back = jax.vjp(norm_scale, resid_mid, scales[2])
    d_mid_norm, d_gain2 = mid_back(d_normed_two)
    d_mid = grad_out + d_mid_norm
    ignored, proj_back = jax.vjp(norm_scale, projected, scales[1])
    d_projected, d_gain1 = proj_back(d_mid)
    d_proj_all = quad_gather(d_projected.astype(bfloat))
    d_attended = jnp.einsum("td,fd->tf", d_proj_all, w_out, preferred_element_type=single)
    d_attended = d_attended.astype(bfloat).reshape(super_rows, 2, HD)

    bent, powers = score_block()
    probs = powers / total
    d_probs = jnp.einsum("qgd,kd->gqk", d_attended, value_all, preferred_element_type=single)
    row_dot = jnp.sum(d_probs * probs, axis=-1, keepdims=True)
    d_raw = (probs * (d_probs - row_dot) * (1.0 - bent * bent)).astype(bfloat)
    d_query = jnp.einsum("gqk,kd->qgd", d_raw, key_all, preferred_element_type=single) * scale
    d_keys = jnp.einsum("gqk,qgd->kd", d_raw, query, preferred_element_type=single) * scale
    d_values = jnp.einsum(
        "gqk,qgd->kd", probs.astype(bfloat), d_attended, preferred_element_type=single
    )
    d_pieces = jnp.stack(
        [d_keys.reshape(chips, super_rows, HD), d_values.reshape(chips, super_rows, HD)], axis=1
    ).astype(bfloat)
    d_keyval = ring_scatter(d_pieces.reshape(chips, 2 * super_rows, HD), chips, 6)
    d_keyval = d_keyval.reshape(2, super_rows, HD).astype(bfloat)
    d_keyval = in_order(pick(d_keyval, side), swap_side(pick(d_keyval, 1 - side)), side, 1)
    d_query_raw = rotate(d_query, angles, -1.0).reshape(super_rows, 2 * HD).astype(bfloat)
    d_keyval_raw = rotate(d_keyval.astype(single), key_angles, -1.0)
    d_keyval_raw = d_keyval_raw.reshape(super_rows, 2 * HD).astype(bfloat)
    d_normed_one = jnp.dot(d_query_raw, w_query, preferred_element_type=single)
    d_normed_one = d_normed_one + jnp.dot(d_keyval_raw, w_keyval, preferred_element_type=single)
    d_normed_one = quad_scatter(d_normed_one)
    ignored, first_back = jax.vjp(norm_scale, resid_in, scales[0])
    d_in_norm, d_gain0 = first_back(d_normed_one)
    tokens_grad = d_mid + d_in_norm

    def attn_rows(left, right):
        rows = jnp.einsum("tf,td->fd", left, right, preferred_element_type=single).astype(bfloat)
        return rows.reshape(2, pairs, 2, share, width)

    term_query = attn_rows(d_query_raw, normed_all)
    term_keyval = attn_rows(d_keyval_raw, normed_all)
    term_out = attn_rows(attended, d_proj_all)

    def to_core(term, axis):
        return in_order(pick(term, core, 2), swap_core(pick(term, 1 - core, 2)), core, axis)

    terms = jnp.stack([to_core(term_query, 0), to_core(term_keyval, 1), to_core(term_out, 0)], axis=3)
    grad_attn = ring_scatter(terms.reshape(chips, 3 * share, width), chips, 7)
    grad_attn = grad_attn.reshape(3, share, width)
    term_gain = jnp.stack([d_gain0, d_gain1, d_gain2, d_gain3])
    grad_gain = lax.psum_scatter(term_gain, ("head", "fsdp"), scatter_dimension=1, tiled=True)

    gains_first_new, gains_second_new, gains_new = adamw(
        gains, gains_first, gains_second, grad_gain, rate_gain, 0.0
    )
    attn_first_new, attn_second_new, attn_weight_new = adamw(
        attn_weight, attn_first, attn_second, grad_attn, rate_matrix, decay_matrix
    )
    ffn_first_new, ffn_second_new, ffn_weight_new = adamw(
        ffn_weight, ffn_first, ffn_second, grad_ffn.transpose(1, 0, 2), rate_matrix, decay_matrix
    )
    return (
        result[None],
        tokens_grad[None],
        gains_first_new,
        gains_second_new,
        gains_new,
        attn_first_new,
        attn_second_new,
        attn_weight_new,
        ffn_first_new,
        ffn_second_new,
        ffn_weight_new,
    )


def per_device(
    tokens,
    cotangent,
    gains,
    gains_first,
    gains_second,
    attn_weight,
    attn_first,
    attn_second,
    ffn_weight,
    ffn_first,
    ffn_second,
):
    devices = lax.axis_size("fsdp")
    chips = devices // 2
    side = lax.axis_index("head")
    place = lax.axis_index("fsdp")
    core, chip = place % 2, place // 2
    tok_rows = tokens.shape[1]
    super_rows = 4 * tok_rows
    seq_len = min(SEQ_LEN, super_rows * chips)
    share = attn_weight.shape[1]
    pairs = chips // 4
    width = tokens.shape[2]
    units = ffn_weight.shape[0]
    gain_columns = gains.shape[1]
    gain_start = (side * devices + place) * gain_columns
    scale = 1.0 / math.sqrt(HD)

    def swap_core(value):
        return lax.ppermute(value, "fsdp", [(index, index ^ 1) for index in range(devices)])

    def swap_side(value):
        return lax.ppermute(value, "head", [(0, 1), (1, 0)])

    def in_order(own, other, index, axis):
        return jnp.where(
            index == 0, jnp.stack([own, other], axis), jnp.stack([other, own], axis)
        )

    def pick(value, index, axis=0):
        return lax.dynamic_index_in_dim(value, index, axis, keepdims=False)

    def quad_gather(value):
        value = in_order(value, swap_side(value), side, 0)
        value = in_order(value, swap_core(value), core, 0)
        return value.reshape((super_rows,) + value.shape[3:])

    def quad_scatter(partial):
        partial = partial.reshape(2, 2, tok_rows, width)
        mine = pick(partial, core) + swap_core(pick(partial, 1 - core).astype(bfloat)).astype(single)
        return pick(mine, side) + swap_side(pick(mine, 1 - side).astype(bfloat)).astype(single)

    ffn_low = ffn_weight.astype(bfloat).transpose(1, 0, 2)
    ffn_side = swap_side(ffn_low)
    shares = (ffn_low, ffn_side, swap_core(ffn_low), swap_core(ffn_side))
    resid_in = tokens[0]
    grad_out = cotangent[0]
    positions = chip * super_rows + jnp.arange(super_rows, dtype=jnp.int32)
    angles = turn_angles(positions % seq_len, HD)
    key_angles = jnp.where(side == 0, angles, 0.0)
    gains_placed = lax.dynamic_update_slice(
        jnp.zeros((4, width), single), gains, (0, gain_start)
    )
    attn_rows, scales, normed_all, query, keyval = front(
        attn_weight.astype(bfloat),
        gains_placed,
        resid_in,
        jnp.cos(angles),
        jnp.sin(angles),
        jnp.cos(key_angles),
        jnp.sin(key_angles),
        chips,
        0,
    )
    w_query, w_keyval, w_out = attn_rows[0], attn_rows[1], attn_rows[2]
    normed_all = normed_all.reshape(super_rows, width)
    keyval_all = ring_gather(keyval.reshape(2 * super_rows, HD), chips, 1)
    keyval_all = keyval_all.reshape(chips, 2, super_rows, HD)
    key_all = keyval_all[:, 0].reshape(chips * super_rows, HD)
    value_all = keyval_all[:, 1].reshape(chips * super_rows, HD)

    key_pos = jnp.arange(chips * super_rows, dtype=jnp.int32)
    distance = positions[:, None] - key_pos[None, :]
    same_seq = (positions // seq_len)[:, None] == (key_pos // seq_len)[None, :]
    allowed = (distance >= 0) & (distance < WIN) & same_seq

    def score_block():
        raw = jnp.einsum("gqd,kd->gqk", query, key_all, preferred_element_type=single)
        bent = jnp.tanh(raw * (scale / softcap))
        return bent, jnp.where(allowed, jnp.exp(softcap * bent), 0.0)

    bent, powers = score_block()
    total = jnp.sum(powers, axis=-1, keepdims=True)
    attended = jnp.einsum(
        "gqk,kd->gqd", powers.astype(bfloat), value_all, preferred_element_type=single
    )
    attended = (attended / total).transpose(1, 0, 2).reshape(super_rows, 2 * HD).astype(bfloat)
    projected = quad_scatter(jnp.dot(attended, w_out, preferred_element_type=single))

    result, d_mid, d_proj_low, gain_rows, terms_own, terms_other = feed_forward(
        resid_in, projected, grad_out, scales, shares, chips, 2
    )
    ffn_terms = terms_own.astype(single) + terms_other.astype(single)
    grad_ffn = ffn_terms[0] + swap_side(ffn_terms[1].astype(bfloat)).astype(single)

    d_proj_all = quad_gather(d_proj_low)
    d_attended = jnp.einsum("td,fd->tf", d_proj_all, w_out, preferred_element_type=single)
    d_attended = d_attended.astype(bfloat).reshape(super_rows, 2, HD)
    bent, powers = score_block()
    probs = powers / total
    d_probs = jnp.einsum("qgd,kd->gqk", d_attended, value_all, preferred_element_type=single)
    row_dot = jnp.sum(d_probs * probs, axis=-1, keepdims=True)
    d_raw = (probs * (d_probs - row_dot) * (1.0 - bent * bent)).astype(bfloat)
    d_query = jnp.einsum("gqk,kd->qgd", d_raw, key_all, preferred_element_type=single) * scale
    d_keys = jnp.einsum("gqk,gqd->kd", d_raw, query, preferred_element_type=single) * scale
    d_values = jnp.einsum(
        "gqk,qgd->kd", probs.astype(bfloat), d_attended, preferred_element_type=single
    )
    d_pieces = jnp.stack(
        [d_keys.reshape(chips, super_rows, HD), d_values.reshape(chips, super_rows, HD)], axis=1
    ).astype(bfloat)
    d_keyval = ring_scatter(d_pieces.reshape(chips, 2 * super_rows, HD), chips, 3)
    d_keyval = d_keyval.reshape(2, super_rows, HD).astype(bfloat)
    d_keyval = in_order(pick(d_keyval, side), swap_side(pick(d_keyval, 1 - side)), side, 1)
    d_query_raw = rotate(d_query, angles, -1.0).reshape(super_rows, 2 * HD).astype(bfloat)
    d_keyval_raw = rotate(d_keyval.astype(single), key_angles, -1.0)
    d_keyval_raw = d_keyval_raw.reshape(super_rows, 2 * HD).astype(bfloat)
    d_normed_one = jnp.dot(d_query_raw, w_query, preferred_element_type=single)
    d_normed_one = d_normed_one + jnp.dot(d_keyval_raw, w_keyval, preferred_element_type=single)

    def term_rows(left, right):
        rows = jnp.einsum("tf,td->fd", left, right, preferred_element_type=single).astype(bfloat)
        return rows.reshape(2, pairs, 2, share, width)

    term_query = term_rows(d_query_raw, normed_all)
    term_keyval = term_rows(d_keyval_raw, normed_all)
    term_out = term_rows(attended, d_proj_all)

    def to_core(term, axis):
        return in_order(pick(term, core, 2), swap_core(pick(term, 1 - core, 2)), core, axis)

    terms = jnp.stack([to_core(term_query, 0), to_core(term_keyval, 1), to_core(term_out, 0)], axis=3)
    grad_attn, tokens_grad, gain_total = last(
        terms.reshape(chips, 3 * share, width),
        d_normed_one.astype(bfloat).reshape(2, 2, tok_rows, width),
        resid_in,
        d_mid,
        scales,
        gain_rows,
        chips,
        4,
    )
    grad_attn = grad_attn.reshape(3, share, width)
    grad_gain = lax.dynamic_slice(gain_total, (0, gain_start), gains.shape)

    gains_first_new, gains_second_new, gains_new = adamw(
        gains, gains_first, gains_second, grad_gain, rate_gain, 0.0
    )
    attn_first_new, attn_second_new, attn_weight_new = adamw(
        attn_weight, attn_first, attn_second, grad_attn, rate_matrix, decay_matrix
    )
    ffn_first_new, ffn_second_new, ffn_weight_new = adamw(
        ffn_weight, ffn_first, ffn_second, grad_ffn.transpose(1, 0, 2), rate_matrix, decay_matrix
    )
    return (
        result[None],
        tokens_grad[None],
        gains_first_new,
        gains_second_new,
        gains_new,
        attn_first_new,
        attn_second_new,
        attn_weight_new,
        ffn_first_new,
        ffn_second_new,
        ffn_weight_new,
    )


def solution(mesh):
    by_token = P("fsdp", "head", None)
    by_column = P(None, ("head", "fsdp"))
    by_row = P(None, ("head", "fsdp"), None)
    by_unit = P(("head", "fsdp"), None, None)
    placed = (by_token,) * 2 + (by_column,) * 3 + (by_row,) * 3 + (by_unit,) * 3
    body = per_device if mesh.shape["fsdp"] == 16 else general_device
    return jax.shard_map(
        body, mesh=mesh, in_specs=placed, out_specs=placed, check_vma=False
    )
```

```python
import functools
import math

import jax
import jax.numpy as jnp
from jax import lax
from jax.experimental import pallas as pl
from jax.experimental.pallas import tpu as pltpu
from jax.sharding import PartitionSpec as P

HQ = 8
HK = 4
HD = 256
WIN = 4096
STEP = 10
SEQ_LEN = 8192


eps_norm = 1e-06
softcap = 50.0
beta_one = 0.9
beta_two = 0.95
adam_eps = 1e-08
rate_matrix = 0.02
rate_gain = 0.2
decay_matrix = 0.1

bfloat = jnp.bfloat16
single = jnp.float32
MESH = pl.DeviceIdType.MESH


def norm_scale(values, scales):
    return (
        values
        * lax.rsqrt(jnp.mean(values * values, axis=-1, keepdims=True) + eps_norm)
        * (1.0 + scales)
    )


def turn_angles(positions, head_width):
    halfway = head_width // 2
    inverse_freq = 10000.0 ** (-(jnp.arange(halfway, dtype=jnp.float32) * 2.0) / head_width)
    return positions.astype(jnp.float32)[:, None] * inverse_freq[None, :]


def rotate(values, angles, direction):
    halfway = values.shape[-1] // 2
    cosine = jnp.cos(angles)[:, None, :]
    sine_part = direction * jnp.sin(angles)[:, None, :]
    former = values[..., :halfway]
    latter = values[..., halfway:]
    return jnp.concatenate(
        [former * cosine - latter * sine_part, latter * cosine + former * sine_part], axis=-1
    )


def adamw(weight, moment, second, gradient, step_rate, decay_rate):
    moment = beta_one * moment + (1.0 - beta_one) * gradient
    second = beta_two * second + (1.0 - beta_two) * gradient * gradient
    update = (
        moment / (1.0 - beta_one**STEP) / (jnp.sqrt(second / (1.0 - beta_two**STEP)) + adam_eps)
        + decay_rate * weight
    )
    return (moment, second, weight - step_rate * update)


def hidden_unit(gate_part, up_part):
    return jax.nn.gelu(gate_part, approximate=True) * up_part


def ring_of(chip, chips):
    wide = chips // 4
    deep, side = chip // wide, chip % wide
    return side * 4 + deep + (side % 2) * (3 - 2 * deep)


def chip_of(ring, chips):
    wide = chips // 4
    side, along = ring // 4, ring % 4
    return (along + (side % 2) * (3 - 2 * along)) * wide + side


def ring_places(chips):
    index = lax.axis_index("fsdp")
    core, chip = index % 2, index // 2
    ring = ring_of(chip, chips)
    right = 2 * chip_of((ring + 1) % chips, chips) + core
    left = 2 * chip_of((ring + chips - 1) % chips, chips) + core
    return chip, ring, right, left


def ring_barrier(right, left):
    barrier = pltpu.get_barrier_semaphore()
    for neighbour in (left, right):
        pl.semaphore_signal(barrier, inc=1, device_id={"fsdp": neighbour}, device_id_type=MESH)
    pl.semaphore_wait(barrier, 2)


def region(shape, pieces, way, piece):
    rows, columns = shape
    if rows % 32 == 0:
        size = rows // 2 // pieces
        start = way * (rows // 2) + piece * size
        return (pl.ds(start, size), pl.ds(0, columns)), (pl.ds(piece * size, size), pl.ds(0, columns))
    size = columns // 2
    return (pl.ds(0, rows), pl.ds(way * size, size)), (pl.ds(0, rows), pl.ds(0, size))


def half_shape(rows, columns):
    return (rows // 2, columns) if rows % 32 == 0 else (rows, columns // 2)


def gather_kernel(chips, pieces, own_ref, all_ref, local_sem, send_sem, recv_sem):
    chip, ring, right, left = ring_places(chips)
    ring_barrier(right, left)
    keep = pltpu.make_async_copy(own_ref, all_ref.at[chip], local_sem)
    keep.start()

    def copy(way, step, piece, first):
        owner = chip_of((ring + (chips - step if way == 0 else step)) % chips, chips)
        part, ignored = region(own_ref.shape, pieces, way, piece)
        there = all_ref.at[(owner,) + part]
        return pltpu.make_async_remote_copy(
            src_ref=own_ref.at[part] if first else there,
            dst_ref=there,
            send_sem=send_sem.at[way, piece, step],
            recv_sem=recv_sem.at[way, piece, step],
            device_id={"fsdp": right if way == 0 else left},
            device_id_type=MESH,
        )

    streams = [(way, piece) for piece in range(pieces) for way in range(2)]
    for way, piece in streams:
        copy(way, 0, piece, True).start()

    def body(step, carried):
        for way, piece in streams:
            copy(way, step - 1, piece, False).wait_recv()
            copy(way, step, piece, False).start()
        return carried

    lax.fori_loop(1, chips - 1, body, 0)
    for way, piece in streams:
        copy(way, chips - 2, piece, False).wait_recv()

    def finish(step, carried):
        for way, piece in streams:
            copy(way, step, piece, False).wait_send()
        return carried

    lax.fori_loop(0, chips - 1, finish, 0)
    keep.wait()


def ring_gather(own, chips, ident):
    rows, columns = own.shape
    pieces = 2 if rows % 64 == 0 else 1
    return pl.pallas_call(
        functools.partial(gather_kernel, chips, pieces),
        out_shape=jax.ShapeDtypeStruct((chips, rows, columns), own.dtype),
        in_specs=[pl.BlockSpec(memory_space=pl.ANY)],
        out_specs=pl.BlockSpec(memory_space=pl.ANY),
        scratch_shapes=[
            pltpu.SemaphoreType.DMA,
            pltpu.SemaphoreType.DMA((2, pieces, chips - 1)),
            pltpu.SemaphoreType.DMA((2, pieces, chips - 1)),
        ],
        compiler_params=pltpu.CompilerParams(collective_id=ident, has_side_effects=True),
        cost_estimate=cost(45),
    )(own)


def scatter_kernel(chips, pieces, parts_ref, sum_ref, held, send_sem, recv_sem):
    chip, ring, right, left = ring_places(chips)
    ring_barrier(right, left)

    def owner_of(way, step):
        shift = chips - 1 - step if way == 0 else 1 + step
        return chip_of((ring + shift) % chips, chips)

    def copy(way, step, piece, first):
        part, place = region(sum_ref.shape, pieces, way, piece)
        return pltpu.make_async_remote_copy(
            src_ref=(
                parts_ref.at[(owner_of(way, step),) + part]
                if first
                else held.at[(way, step - 1) + place]
            ),
            dst_ref=held.at[(way, step) + place],
            send_sem=send_sem.at[way, piece, step],
            recv_sem=recv_sem.at[way, piece, step],
            device_id={"fsdp": right if way == 0 else left},
            device_id_type=MESH,
        )

    streams = [(way, piece) for piece in range(pieces) for way in range(2)]
    for way, piece in streams:
        copy(way, 0, piece, True).start()

    def arrived(way, step, piece):
        copy(way, step, piece, True).wait_recv()
        part, place = region(sum_ref.shape, pieces, way, piece)
        here = parts_ref[(owner_of(way, step + 1),) + part]
        return held[(way, step) + place].astype(single) + here.astype(single)

    def body(step, carried):
        for way, piece in streams:
            total = arrived(way, step - 1, piece)
            part, place = region(sum_ref.shape, pieces, way, piece)
            held[(way, step - 1) + place] = total.astype(held.dtype)
            copy(way, step, piece, False).start()
        return carried

    lax.fori_loop(1, chips - 1, body, 0)
    for way, piece in streams:
        part, place = region(sum_ref.shape, pieces, way, piece)
        sum_ref[part] = arrived(way, chips - 2, piece)

    def finish(step, carried):
        for way, piece in streams:
            copy(way, step, piece, True).wait_send()
        return carried

    lax.fori_loop(0, chips - 1, finish, 0)


def ring_scatter(parts, chips, ident):
    rows, columns = parts.shape[1:]
    pieces = 2 if rows % 64 == 0 else 1
    return pl.pallas_call(
        functools.partial(scatter_kernel, chips, pieces),
        out_shape=jax.ShapeDtypeStruct((rows, columns), single),
        in_specs=[pl.BlockSpec(memory_space=pltpu.VMEM)],
        out_specs=pl.BlockSpec(memory_space=pltpu.VMEM),
        scratch_shapes=[
            pltpu.VMEM((2, chips - 1) + half_shape(rows, columns), parts.dtype),
            pltpu.SemaphoreType.DMA((2, pieces, chips - 1)),
            pltpu.SemaphoreType.DMA((2, pieces, chips - 1)),
        ],
        compiler_params=pltpu.CompilerParams(
            collective_id=ident, has_side_effects=True, vmem_limit_bytes=56 * 2**20
        ),
        cost_estimate=cost(45),
    )(parts)


def norm_back(values, scales, grad):
    inverse = lax.rsqrt(jnp.mean(values * values, axis=-1, keepdims=True) + eps_norm)
    bent = grad * (1.0 + scales)
    slope = jnp.mean(bent * values, axis=-1, keepdims=True) * (inverse * inverse * inverse)
    return bent * inverse - values * slope, jnp.sum(grad * values * inverse, axis=0, keepdims=True)


def gelu_parts(gate):
    root = math.sqrt(2.0 / math.pi)
    square = gate * gate
    bend = jnp.tanh(root * gate * (1.0 + 0.044715 * square))
    half = 0.5 * (1.0 + bend)
    slope = half + 0.5 * gate * (1.0 - bend * bend) * (root * (1.0 + 3.0 * 0.044715 * square))
    return gate * half, slope


def dot_nt(left, right):
    return lax.dot_general(left, right, (((1,), (1,)), ((), ())), preferred_element_type=single)


def dot_nn(left, right):
    return lax.dot_general(left, right, (((1,), (0,)), ((), ())), preferred_element_type=single)


def dot_tn(left, right):
    return lax.dot_general(left, right, (((0,), (0,)), ((), ())), preferred_element_type=single)


class Ring:
    def __init__(self, chips, pieces, rows, send_sem, recv_sem):
        self.chips, self.pieces, self.half = chips, pieces, rows // 2
        self.size = rows // 2 // pieces
        self.chip, self.ring, self.right, self.left = ring_places(chips)
        self.send_sem, self.recv_sem = send_sem, recv_sem
        self.streams = [(way, piece) for piece in range(pieces) for way in range(2)]

    def owner(self, way, step):
        shift = self.chips - step if way == 0 else step
        return chip_of((self.ring + shift) % self.chips, self.chips)

    def copy(self, source, target, way, piece, step):
        return pltpu.make_async_remote_copy(
            src_ref=source,
            dst_ref=target,
            send_sem=self.send_sem.at[way, piece, step],
            recv_sem=self.recv_sem.at[way, piece, step],
            device_id={"fsdp": self.right if way == 0 else self.left},
            device_id_type=MESH,
        )

    def part(self, way, piece):
        return pl.ds(way * self.half + piece * self.size, self.size)

    def place(self, piece):
        return pl.ds(piece * self.size, self.size)

    def gather_copy(self, all_ref, way, piece, step):
        there = all_ref.at[self.owner(way, step), self.part(way, piece)]
        return self.copy(there, there, way, piece, step)

    def gather_step(self, all_ref, step):
        for way, piece in self.streams:

            @pl.when(step > 0)
            def _():
                self.gather_copy(all_ref, way, piece, step - 1).wait_recv()

            @pl.when(step < self.chips - 1)
            def _():
                self.gather_copy(all_ref, way, piece, step).start()

    def scatter_copy(self, parts_ref, held, way, piece, step, first):
        source = (
            parts_ref.at[self.owner(way, step + 1), self.part(way, piece)]
            if first
            else held.at[way, step - 1, self.place(piece)]
        )
        return self.copy(source, held.at[way, step, self.place(piece)], way, piece, step)

    def scatter_total(self, parts_ref, held, way, piece, step):
        self.scatter_copy(parts_ref, held, way, piece, step, True).wait_recv()
        here = parts_ref[self.owner(way, step + 2), self.part(way, piece)]
        return held[way, step, self.place(piece)].astype(single) + here.astype(single)

    def scatter_step(self, parts_ref, held, step):
        for way, piece in self.streams:

            @pl.when(step == 0)
            def _():
                self.scatter_copy(parts_ref, held, way, piece, 0, True).start()

            @pl.when(step > 0)
            def _():
                total = self.scatter_total(parts_ref, held, way, piece, step - 1)
                held[way, step - 1, self.place(piece)] = total.astype(held.dtype)
                self.scatter_copy(parts_ref, held, way, piece, step, False).start()

    def scatter_end(self, parts_ref, held, sum_ref):
        for way, piece in self.streams:
            sum_ref[self.part(way, piece)] = self.scatter_total(
                parts_ref, held, way, piece, self.chips - 2
            )

    def finish(self, example):
        def body(step, carried):
            for way, piece in self.streams:
                self.copy(example, example, way, piece, step).wait_send()
            return carried

        lax.fori_loop(0, self.chips - 1, body, 0)


def quad_peers(chips):
    side = lax.axis_index("head")
    index = lax.axis_index("fsdp")
    chip, core = index // 2, index % 2
    ring = ring_of(chip, chips)
    around = [2 * chip_of((ring + hop) % chips, chips) + core for hop in range(1, chips)]
    return side, core, {"head": 1 - side}, {"fsdp": 2 * chip + 1 - core}, around


def wide_barrier(to_side, to_core, around):
    barrier = pltpu.get_barrier_semaphore()
    for target in [to_side, to_core] + [{"fsdp": other} for other in around]:
        pl.semaphore_signal(barrier, inc=1, device_id=target, device_id_type=MESH)
    pl.semaphore_wait(barrier, 2 + len(around))


def remote(source, target, send_sem, recv_sem, device):
    return pltpu.make_async_remote_copy(
        src_ref=source,
        dst_ref=target,
        send_sem=send_sem,
        recv_sem=recv_sem,
        device_id=device,
        device_id_type=MESH,
    )


class Total:
    def __init__(self, value, near, blocks, send_sem, recv_sem, peers, chip):
        self.value, self.near, self.blocks = value, near, blocks
        self.send_sem, self.recv_sem = send_sem, recv_sem
        side, core, self.to_side, self.to_core, self.around = peers
        self.chip = chip
        self.first = remote(value.at[0], near.at[0], send_sem.at[0], recv_sem.at[0], self.to_side)
        self.second = remote(value.at[1], near.at[1], send_sem.at[1], recv_sem.at[1], self.to_core)

    def spread(self, hop):
        here = self.blocks.at[self.chip]
        return remote(
            here,
            here,
            self.send_sem.at[1 + hop],
            self.recv_sem.at[1 + hop],
            {"fsdp": self.around[hop - 1]},
        )

    def start(self):
        self.first.start()

    def over_cores(self):
        self.first.wait_recv()
        self.value[1] = self.value[0] + self.near[0]
        self.second.start()

    def over_ring(self):
        self.second.wait_recv()
        self.blocks[self.chip] = self.value[1] + self.near[1]
        for hop in range(1, len(self.around) + 1):
            self.spread(hop).start()

    def end(self):
        for hop in range(1, len(self.around) + 1):
            self.spread(hop).wait_recv()
        total = self.blocks[0]
        for other in range(1, len(self.around) + 1):
            total = total + self.blocks[other]
        self.first.wait_send()
        self.second.wait_send()
        for hop in range(1, len(self.around) + 1):
            self.spread(hop).wait_send()
        return total


def total_scratch(chips, width):
    return [
        pltpu.VMEM((2, 4, width), single),
        pltpu.VMEM((2, 4, width), single),
        pltpu.VMEM((chips, 4, width), single),
        pltpu.SemaphoreType.DMA((chips + 1,)),
        pltpu.SemaphoreType.DMA((chips + 1,)),
    ]


def turn(raw, cosine, sine):
    halfway = raw.shape[1] // 2
    former, latter = raw[:, :halfway], raw[:, halfway:]
    return jnp.concatenate(
        [former * cosine - latter * sine, latter * cosine + former * sine], axis=1
    )


def front_kernel(
    chips,
    own_ref,
    gains_ref,
    resid_ref,
    cosine_ref,
    sine_ref,
    key_cosine_ref,
    key_sine_ref,
    units_ref,
    rows_ref,
    scales_ref,
    normed_ref,
    query_ref,
    keyval_ref,
    side_units_ref,
    core_units_ref,
    all_rows,
    both,
    value,
    near,
    blocks,
    total_send,
    total_recv,
    send_sem,
    recv_sem,
    place_sem,
    peer_sem,
    quad_send,
    quad_recv,
    load_sem,
    bulk_send,
    bulk_recv,
):
    share, width = own_ref.shape[1:]
    half = width // 2
    pairs = chips // 4
    chip, ring, right, left = ring_places(chips)
    peers = quad_peers(chips)
    side, core, to_side, to_core, around = peers
    load = pltpu.make_async_copy(own_ref, all_rows.at[chip], load_sem)
    load.start()
    value[0] = gains_ref[...].astype(bfloat).astype(single)
    load.wait()
    wide_barrier(to_side, to_core, around)
    gains_total = Total(value, near, blocks, total_send, total_recv, peers, chip)
    gains_total.start()
    streams = [(way, slot) for slot in range(3) for way in range(2)]

    def owner_of(way, step):
        return chip_of((ring + (chips - step if way == 0 else step)) % chips, chips)

    def hop(way, slot, step):
        there = all_rows.at[owner_of(way, step), slot, :, pl.ds(way * half, half)]
        return remote(
            there,
            there,
            send_sem.at[way, slot, step],
            recv_sem.at[way, slot, step],
            {"fsdp": right if way == 0 else left},
        )

    def goal(way, slot, step):
        owner = owner_of(way, step)
        deep = owner // pairs
        unit = (owner % pairs) * 2 + core
        taker, head = (deep % 2, deep // 2) if slot == 1 else (deep // 2, deep % 2)
        columns = pl.ds(way * half, half)
        source = all_rows.at[owner, slot, :, columns]
        start = pl.multiple_of(head * HD + unit * share, share)
        target = rows_ref.at[slot, pl.ds(start, share), columns]
        sem = place_sem.at[way, slot, step]

        def here():
            return pltpu.make_async_copy(source, target, sem)

        def there():
            return remote(source, target, sem, peer_sem.at[way, slot, step], to_core)

        return taker, here, there

    def place(way, slot, step):
        taker, here, there = goal(way, slot, step)

        @pl.when(taker == core)
        def _():
            here().start()

        @pl.when(taker != core)
        def _():
            there().start()

    for way, slot in streams:
        hop(way, slot, 0).start()
    gains_total.over_cores()
    for way, slot in streams:
        place(way, slot, 0)
    gains_total.over_ring()
    scales_ref[...] = gains_total.end()
    normed_ref[core, side] = norm_scale(resid_ref[...], scales_ref[0:1]).astype(bfloat)
    along = remote(
        normed_ref.at[core, side],
        normed_ref.at[core, side],
        quad_send.at[0],
        quad_recv.at[0],
        to_side,
    )
    across = remote(
        normed_ref.at[core], normed_ref.at[core], quad_send.at[1], quad_recv.at[1], to_core
    )
    along.start()
    bulk_side = remote(
        units_ref.at[0:2], side_units_ref, bulk_send.at[0], bulk_recv.at[0], to_side
    )
    bulk_core = remote(units_ref, core_units_ref, bulk_send.at[1], bulk_recv.at[1], to_core)

    def body(step, carried):
        for way, slot in streams:
            hop(way, slot, step - 1).wait_recv()

            @pl.when(step < chips - 1)
            def _():
                hop(way, slot, step).start()

            place(way, slot, step)

        @pl.when(step == 2)
        def _():
            along.wait()
            across.start()
            bulk_side.start()
            bulk_core.start()

        return carried

    lax.fori_loop(1, chips, body, 0)

    def settle(step, carried):
        for way, slot in streams:
            taker, here, there = goal(way, slot, step)

            @pl.when(taker == core)
            def _():
                here().wait()
                there().wait_recv()

            @pl.when(taker != core)
            def _():
                there().wait_send()

            @pl.when(step < chips - 1)
            def _():
                hop(way, slot, step).wait_send()

        return carried

    across.wait()
    lax.fori_loop(0, chips, settle, 0)
    tokens = 4 * resid_ref.shape[0]
    normed = normed_ref[...].reshape(tokens, width)
    for head in range(2):
        rows = slice(head * HD, head * HD + HD)
        raw = dot_nt(normed, rows_ref[1, rows])
        both[head] = turn(raw, key_cosine_ref[...], key_sine_ref[...]).astype(bfloat)
    swap = remote(
        both.at[1 - side], keyval_ref.at[side], quad_send.at[2], quad_recv.at[2], to_side
    )
    swap.start()
    keyval_ref[side] = both[side]
    for head in range(2):
        rows = slice(head * HD, head * HD + HD)
        raw = dot_nt(normed, rows_ref[0, rows])
        query_ref[head] = turn(raw, cosine_ref[...], sine_ref[...]).astype(bfloat)
    swap.wait()
    bulk_side.wait()
    bulk_core.wait()


def cost(micros):
    return pl.CostEstimate(flops=int(micros * 1e9), bytes_accessed=0, transcendentals=0)


def front(attn_low, gains, resid_in, cosine, sine, key_cosine, key_sine, ffn_low, chips, ident):
    share, width = attn_low.shape[1:]
    tok_rows = resid_in.shape[0]
    vmem = pl.BlockSpec(memory_space=pltpu.VMEM)
    anywhere = pl.BlockSpec(memory_space=pl.ANY)
    return pl.pallas_call(
        functools.partial(front_kernel, chips),
        out_shape=(
            jax.ShapeDtypeStruct((3, 2 * HD, width), bfloat),
            jax.ShapeDtypeStruct((4, width), single),
            jax.ShapeDtypeStruct((2, 2, tok_rows, width), bfloat),
            jax.ShapeDtypeStruct((2, 4 * tok_rows, HD), bfloat),
            jax.ShapeDtypeStruct((2, 4 * tok_rows, HD), bfloat),
            jax.ShapeDtypeStruct((2,) + ffn_low.shape[1:], bfloat),
            jax.ShapeDtypeStruct(ffn_low.shape, bfloat),
        ),
        in_specs=[anywhere] + [vmem] * 6 + [anywhere],
        out_specs=(vmem,) * 5 + (anywhere,) * 2,
        scratch_shapes=[
            pltpu.VMEM((chips, 3, share, width), bfloat),
            pltpu.VMEM((2, 4 * tok_rows, HD), bfloat),
        ]
        + total_scratch(chips, width)
        + [
            pltpu.SemaphoreType.DMA((2, 3, chips - 1)),
            pltpu.SemaphoreType.DMA((2, 3, chips - 1)),
            pltpu.SemaphoreType.DMA((2, 3, chips)),
            pltpu.SemaphoreType.DMA((2, 3, chips)),
            pltpu.SemaphoreType.DMA((3,)),
            pltpu.SemaphoreType.DMA((3,)),
            pltpu.SemaphoreType.DMA,
            pltpu.SemaphoreType.DMA((2,)),
            pltpu.SemaphoreType.DMA((2,)),
        ],
        compiler_params=pltpu.CompilerParams(
            collective_id=ident, has_side_effects=True, vmem_limit_bytes=48 * 2**20
        ),
        cost_estimate=cost(75),
    )(attn_low, gains, resid_in, cosine, sine, key_cosine, key_sine, ffn_low)


def attend_kernel(
    chips,
    query_ref,
    own_ref,
    rows_ref,
    units_ref,
    side_units_ref,
    keyval_ref,
    attended_ref,
    inverse_ref,
    projected_ref,
    side_last_ref,
    diag_ref,
    diag_last_ref,
    w_out,
    total,
    sums,
    product,
    across_put,
    across_got,
    along_put,
    along_got,
    load_sem,
    send_sem,
    recv_sem,
    quad_send,
    quad_recv,
    bulk_send,
    bulk_recv,
):
    tokens = query_ref.shape[1]
    half = tokens // 2
    width = w_out.shape[1]
    tok_rows = tokens // 4
    scale = 1.0 / math.sqrt(HD)
    chip, ring, right, left = ring_places(chips)
    side, core, to_side, to_core, around = quad_peers(chips)
    load = pltpu.make_async_copy(rows_ref.at[2], w_out, load_sem.at[0])
    load.start()
    keep = pltpu.make_async_copy(own_ref, keyval_ref.at[chip], load_sem.at[1])
    keep.start()
    total[...] = jnp.zeros_like(total)
    sums[...] = jnp.zeros_like(sums)
    keep.wait()
    quad_barrier(to_side, to_core, right, left)
    bulk_side = remote(
        units_ref.at[2:3], side_last_ref, bulk_send.at[0], bulk_recv.at[0], to_side
    )
    bulk_core = remote(side_units_ref, diag_ref, bulk_send.at[1], bulk_recv.at[1], to_core)
    bulk_last = remote(side_last_ref, diag_last_ref, bulk_send.at[2], bulk_recv.at[2], to_core)
    bulk_side.start()
    streams = [(way, kind) for kind in range(2) for way in range(2)]

    def owner_of(way, step):
        return chip_of((ring + (chips - step if way == 0 else step)) % chips, chips)

    def hop(way, kind, step):
        there = keyval_ref.at[owner_of(way, step), kind, pl.ds(way * half, half)]
        return remote(
            there,
            there,
            send_sem.at[way, kind, step],
            recv_sem.at[way, kind, step],
            {"fsdp": right if way == 0 else left},
        )

    def block(way, owner):
        key = keyval_ref[owner, 0, way * half : way * half + half]
        val = keyval_ref[owner, 1, way * half : way * half + half]
        row = lax.broadcasted_iota(jnp.int32, (tokens, half), 0)
        column = lax.broadcasted_iota(jnp.int32, (tokens, half), 1)
        allowed = row + (chip - owner) * tokens - way * half >= column

        def one_head(head, carried):
            bent = jnp.tanh(dot_nt(query_ref[head], key) * (scale / softcap))
            powers = jnp.where(allowed, jnp.exp(softcap * bent), 0.0)
            sums[head] += powers[:, : half // 2] + powers[:, half // 2 :]
            total[head] += dot_nn(powers.astype(bfloat), val)
            return carried

        lax.fori_loop(0, 2, one_head, 0)

    def body(step, carried):
        for way, kind in streams:

            @pl.when(step > 0)
            def _():
                hop(way, kind, step - 1).wait_recv()

            @pl.when(step < chips - 1)
            def _():
                hop(way, kind, step).start()

        @pl.when(step == 0)
        def _():
            bulk_core.start()

        for way in range(2):
            owner = owner_of(way, step)

            @pl.when(owner <= chip)
            def _():
                block(way, owner)

        return carried

    lax.fori_loop(0, chips, body, 0)
    bulk_side.wait_recv()
    bulk_last.start()
    load.wait()
    for head in range(2):
        inverse = 1.0 / jnp.sum(sums[head], axis=-1, keepdims=True)
        inverse_ref[head] = jnp.broadcast_to(inverse, inverse_ref.shape[1:])
        attended_ref[:, head * HD : head * HD + HD] = (total[head] * inverse).astype(bfloat)
    span = width // 3
    across = remote(across_put, across_got, quad_send.at[0], quad_recv.at[0], to_core)
    along = remote(along_put, along_got, quad_send.at[1], quad_recv.at[1], to_side)

    def project(part, ref):
        first = pl.ds(pl.multiple_of(part * 2 * tok_rows, 2 * tok_rows), 2 * tok_rows)

        def columns(tile, carried):
            span_of = pl.ds(pl.multiple_of(tile * span, span), span)
            made = dot_nn(attended_ref[first], w_out[:, span_of])
            ref[:, :, span_of] = made.reshape(2, tok_rows, span).astype(ref.dtype)
            return carried

        lax.fori_loop(0, 3, columns, 0)

    project(1 - core, across_put)
    across.start()
    project(core, product)
    across.wait()
    along_put[...] = (product[1 - side] + across_got[1 - side].astype(single)).astype(bfloat)
    along.start()
    kept = product[side] + across_got[side].astype(single)

    def settle(step, carried):
        for way, kind in streams:
            hop(way, kind, step).wait_send()
        return carried

    lax.fori_loop(0, chips - 1, settle, 0)
    bulk_side.wait_send()
    bulk_core.wait()
    bulk_last.wait()
    along.wait()
    projected_ref[...] = kept + along_got[...].astype(single)


def quad_barrier(to_side, to_core, right, left):
    barrier = pltpu.get_barrier_semaphore()
    for target in (to_side, to_core, {"fsdp": right}, {"fsdp": left}):
        pl.semaphore_signal(barrier, inc=1, device_id=target, device_id_type=MESH)
    pl.semaphore_wait(barrier, 4)


def attend(query, keyval, attn_rows, ffn_low, side_units, chips, ident):
    tokens = query.shape[1]
    width = attn_rows.shape[2]
    tok_rows = tokens // 4
    vmem = pl.BlockSpec(memory_space=pltpu.VMEM)
    anywhere = pl.BlockSpec(memory_space=pl.ANY)
    return pl.pallas_call(
        functools.partial(attend_kernel, chips),
        out_shape=(
            jax.ShapeDtypeStruct((chips, 2, tokens, HD), bfloat),
            jax.ShapeDtypeStruct((tokens, 2 * HD), bfloat),
            jax.ShapeDtypeStruct((2, tokens, 128), single),
            jax.ShapeDtypeStruct((tok_rows, width), single),
            jax.ShapeDtypeStruct((1,) + ffn_low.shape[1:], bfloat),
            jax.ShapeDtypeStruct((2,) + ffn_low.shape[1:], bfloat),
            jax.ShapeDtypeStruct((1,) + ffn_low.shape[1:], bfloat),
        ),
        in_specs=[vmem] + [anywhere] * 4,
        out_specs=(vmem,) * 4 + (anywhere,) * 3,
        scratch_shapes=[
            pltpu.VMEM((2 * HD, width), bfloat),
            pltpu.VMEM((2, tokens, HD), single),
            pltpu.VMEM((2, tokens, tokens // 4), single),
            pltpu.VMEM((2, tok_rows, width), single),
            pltpu.VMEM((2, tok_rows, width), bfloat),
            pltpu.VMEM((2, tok_rows, width), bfloat),
            pltpu.VMEM((tok_rows, width), bfloat),
            pltpu.VMEM((tok_rows, width), bfloat),
            pltpu.SemaphoreType.DMA((2,)),
            pltpu.SemaphoreType.DMA((2, 2, chips - 1)),
            pltpu.SemaphoreType.DMA((2, 2, chips - 1)),
            pltpu.SemaphoreType.DMA((2,)),
            pltpu.SemaphoreType.DMA((2,)),
            pltpu.SemaphoreType.DMA((3,)),
            pltpu.SemaphoreType.DMA((3,)),
        ],
        compiler_params=pltpu.CompilerParams(
            collective_id=ident, has_side_effects=True, vmem_limit_bytes=48 * 2**20
        ),
        cost_estimate=cost(60),
    )(query, keyval, attn_rows, ffn_low, side_units)


def tail_kernel(
    chips,
    pieces,
    d_proj_ref,
    query_ref,
    keyval_ref,
    attended_ref,
    inverse_ref,
    rows_ref,
    normed_ref,
    cosine_ref,
    sine_ref,
    key_cosine_ref,
    key_sine_ref,
    resid_ref,
    d_mid_ref,
    scales_ref,
    gains_ref,
    units_ref,
    sum_ref,
    tokens_ref,
    total_ref,
    units_got_ref,
    d_all,
    d_out,
    delta,
    d_query,
    d_block,
    first_put,
    held_keys,
    swapped,
    d_raw,
    out_rows,
    parts,
    held,
    across_got,
    along_put,
    along_got,
    value,
    near,
    blocks,
    total_send,
    total_recv,
    key_send,
    key_recv,
    place_sem,
    peer_sem,
    send_sem,
    recv_sem,
    quad_send,
    quad_recv,
    bulk_send,
    bulk_recv,
):
    tokens = query_ref.shape[1]
    half = tokens // 2
    width = resid_ref.shape[1]
    share = parts.shape[2]
    pairs = chips // 4
    scale = 1.0 / math.sqrt(HD)
    peers = quad_peers(chips)
    side, core, to_side, to_core, around = peers
    ring = Ring(chips, pieces, 3 * share, send_sem, recv_sem)
    chip = ring.chip
    gains_total = Total(value, near, blocks, total_send, total_recv, peers, chip)
    d_all[core, side] = d_proj_ref[...]
    wide_barrier(to_side, to_core, around)

    def quad_copy(source, target, index, device):
        return remote(source, target, quad_send.at[index], quad_recv.at[index], device)

    def bulk(kind):
        return remote(
            units_ref.at[kind],
            units_got_ref.at[kind],
            bulk_send.at[kind],
            bulk_recv.at[kind],
            to_side,
        )

    along = quad_copy(d_all.at[core, side], d_all.at[core, side], 0, to_side)
    across = quad_copy(d_all.at[core], d_all.at[core], 1, to_core)
    along.start()
    d_query[...] = jnp.zeros_like(d_query)
    along.wait()
    across.start()
    bulk(0).start()
    bulk(1).start()
    across.wait()
    d_rows = d_all[...].reshape(tokens, width)
    for head in range(2):
        columns = slice(head * HD, head * HD + HD)
        made = dot_nt(d_rows, rows_ref[2, columns]).astype(bfloat)
        d_out[head] = made
        row_dot = jnp.sum(
            made.astype(single) * attended_ref[:, columns].astype(single), axis=-1, keepdims=True
        )
        delta[head] = jnp.broadcast_to(row_dot, delta.shape[1:])

    def block(way, owner):
        key = keyval_ref[owner, 0, way * half : way * half + half]
        val = keyval_ref[owner, 1, way * half : way * half + half]
        row = lax.broadcasted_iota(jnp.int32, (tokens, half), 0)
        column = lax.broadcasted_iota(jnp.int32, (tokens, half), 1)
        allowed = row + (chip - owner) * tokens - way * half >= column

        def one_head(head, carried):
            bent = jnp.tanh(dot_nt(query_ref[head], key) * (scale / softcap))
            inverse = jnp.concatenate([inverse_ref[head]] * (half // 128), axis=1)
            row_dot = jnp.concatenate([delta[head]] * (half // 128), axis=1)
            probs = jnp.where(allowed, jnp.exp(softcap * bent), 0.0) * inverse
            d_probs = dot_nt(d_out[head], val)
            d_scores = (probs * (d_probs - row_dot) * (1.0 - bent * bent)).astype(bfloat)
            d_block[way, 0] += dot_tn(d_scores, query_ref[head]) * scale
            d_block[way, 1] += dot_tn(probs.astype(bfloat), d_out[head])
            d_query[head] += dot_nn(d_scores, key)
            return carried

        lax.fori_loop(0, 2, one_head, 0)

    def key_copy(way, kind, step, first):
        return remote(
            first_put.at[way, kind] if first else held_keys.at[way, step - 1, kind],
            held_keys.at[way, step, kind],
            key_send.at[way, kind, step],
            key_recv.at[way, kind, step],
            {"fsdp": ring.right if way == 0 else ring.left},
        )

    streams = [(way, kind) for kind in range(2) for way in range(2)]

    def key_blocks(step):
        for way in range(2):
            owner = ring.owner(way, step + 1)
            d_block[way] = jnp.zeros(d_block.shape[1:], single)

            @pl.when(owner <= chip)
            def _():
                block(way, owner)

    def key_body(step, carried):
        key_blocks(step)
        for way, kind in streams:

            @pl.when(step == 0)
            def _():
                first_put[way, kind] = d_block[way, kind].astype(bfloat)
                key_copy(way, kind, 0, True).start()

            @pl.when(step > 0)
            def _():
                key_copy(way, kind, step - 1, True).wait_recv()
                summed = held_keys[way, step - 1, kind].astype(single) + d_block[way, kind]
                held_keys[way, step - 1, kind] = summed.astype(bfloat)
                key_copy(way, kind, step, False).start()

        return carried

    lax.fori_loop(0, chips - 1, key_body, 0)

    def place(slot, head, start):
        deep = 2 * head + core if slot == 1 else 2 * core + head
        for unit in range(4):
            source = out_rows.at[slot, head, pl.ds(unit * share, share)]
            target = parts.at[deep * pairs + unit // 2, slot]
            sem = place_sem.at[slot, head, unit]

            def here():
                return pltpu.make_async_copy(source, target, sem)

            def there():
                return remote(source, target, sem, peer_sem.at[slot, head, unit], to_core)

            @pl.when(core == unit % 2)
            def _():
                if start:
                    here().start()
                else:
                    here().wait()
                    there().wait_recv()

            @pl.when(core != unit % 2)
            def _():
                if start:
                    there().start()
                else:
                    there().wait_send()

    def term(slot, head, left, right):
        out_rows[slot, head] = dot_tn(left, right).astype(bfloat)
        place(slot, head, True)

    normed = normed_ref[...].reshape(tokens, width)
    for head in range(2):
        term(2, head, attended_ref[:, head * HD : head * HD + HD], d_all[...].reshape(tokens, width))
    key_blocks(chips - 1)
    for way in range(2):
        rows = slice(way * half, way * half + half)
        for kind in range(2):
            key_copy(way, kind, chips - 2, True).wait_recv()
            summed = held_keys[way, chips - 2, kind].astype(single) + d_block[way, kind]
            swapped[2 + kind, rows] = summed.astype(bfloat)
    swap = quad_copy(swapped.at[3 - side], swapped.at[side], 2, to_side)
    swap.start()
    for head in range(2):
        turned = turn(d_query[head] * scale, cosine_ref[...], -sine_ref[...])
        d_raw[head] = turned.astype(bfloat)
        term(0, head, d_raw[head], normed)
    swap.wait()
    bulk(2).start()
    swapped[side] = swapped[2 + side]
    for head in range(2):
        turned = turn(swapped[head].astype(single), key_cosine_ref[...], -key_sine_ref[...])
        d_raw[2 + head] = turned.astype(bfloat)
        term(1, head, d_raw[2 + head], normed)
    span = width // 3

    def d_input(tile, carried):
        columns = pl.ds(pl.multiple_of(tile * span, span), span)
        made = dot_nn(d_raw[0], rows_ref[0, 0:HD, columns])
        made = made + dot_nn(d_raw[1], rows_ref[0, HD:, columns])
        made = made + dot_nn(d_raw[2], rows_ref[1, 0:HD, columns])
        made = made + dot_nn(d_raw[3], rows_ref[1, HD:, columns])
        out_rows[0, :, :, columns] = made.reshape(2, half, span).astype(bfloat)
        return carried

    for slot in range(3):
        for head in range(2):
            place(slot, head, False)
    blocks_ref = parts.reshape(chips, 3 * share, width)
    ring.scatter_step(blocks_ref, held, 0)
    lax.fori_loop(0, 3, d_input, 0)
    across = quad_copy(out_rows.at[0, 1 - core], across_got, 3, to_core)
    mine = pl.ds(pl.multiple_of(side * (half // 2), half // 2), half // 2)
    other = pl.ds(pl.multiple_of((1 - side) * (half // 2), half // 2), half // 2)
    along = quad_copy(along_put, along_got, 4, to_side)
    across.start()

    def body(step, carried):
        ring.scatter_step(blocks_ref, held, step)

        @pl.when(step == 1)
        def _():
            across.wait()
            given = out_rows[0, core, other].astype(single) + across_got[other].astype(single)
            along_put[...] = given.astype(bfloat)
            along.start()
            tokens_ref[...] = out_rows[0, core, mine].astype(single) + across_got[mine].astype(single)

        @pl.when(step == 4)
        def _():
            along.wait()
            tokens_ref[...] = tokens_ref[...] + along_got[...].astype(single)
            d_norm, d_gain = norm_back(resid_ref[...], scales_ref[0:1], tokens_ref[...])
            tokens_ref[...] = d_mid_ref[...] + d_norm
            value[0] = gains_ref[...]
            value[0, 0:1] = d_gain
            gains_total.start()

        @pl.when(step == 5)
        def _():
            gains_total.over_cores()

        @pl.when(step == 6)
        def _():
            gains_total.over_ring()

        return carried

    lax.fori_loop(1, chips - 1, body, 0)
    total_ref[...] = gains_total.end()
    ring.scatter_end(blocks_ref, held, sum_ref)
    ring.finish(held.at[0, 0, 0 : ring.size])

    def settle(step, carried):
        for way, kind in streams:
            key_copy(way, kind, step, True).wait_send()
        return carried

    lax.fori_loop(0, chips - 1, settle, 0)
    for kind in range(3):
        bulk(kind).wait()


def tail(d_proj, query, keyval, attended, inverse, rows, normed, turns, locals_, units, chips, ident):
    tokens = query.shape[1]
    tok_rows = tokens // 4
    width = rows.shape[2]
    share = tokens // 8
    half = tokens // 2
    pieces = 3
    vmem = pl.BlockSpec(memory_space=pltpu.VMEM)
    anywhere = pl.BlockSpec(memory_space=pl.ANY)
    return pl.pallas_call(
        functools.partial(tail_kernel, chips, pieces),
        out_shape=(
            jax.ShapeDtypeStruct((3 * share, width), single),
            jax.ShapeDtypeStruct((tok_rows, width), single),
            jax.ShapeDtypeStruct((4, width), single),
            jax.ShapeDtypeStruct(units.shape, bfloat),
        ),
        in_specs=[vmem] * 15 + [anywhere],
        out_specs=(vmem,) * 3 + (anywhere,),
        scratch_shapes=[
            pltpu.VMEM((2, 2, tok_rows, width), bfloat),
            pltpu.VMEM((2, tokens, HD), bfloat),
            pltpu.VMEM((2, tokens, 128), single),
            pltpu.VMEM((2, tokens, HD), single),
            pltpu.VMEM((2, 2, half, HD), single),
            pltpu.VMEM((2, 2, half, HD), bfloat),
            pltpu.VMEM((2, chips - 1, 2, half, HD), bfloat),
            pltpu.VMEM((4, tokens, HD), bfloat),
            pltpu.VMEM((4, tokens, HD), bfloat),
            pltpu.VMEM((3, 2, HD, width), bfloat),
            pltpu.VMEM((chips, 3, share, width), bfloat),
            pltpu.VMEM((2, chips - 1, 3 * share // 2, width), bfloat),
            pltpu.VMEM((2 * tok_rows, width), bfloat),
            pltpu.VMEM((tok_rows, width), bfloat),
            pltpu.VMEM((tok_rows, width), bfloat),
        ]
        + total_scratch(chips, width)
        + [
            pltpu.SemaphoreType.DMA((2, 2, chips - 1)),
            pltpu.SemaphoreType.DMA((2, 2, chips - 1)),
            pltpu.SemaphoreType.DMA((3, 2, 4)),
            pltpu.SemaphoreType.DMA((3, 2, 4)),
            pltpu.SemaphoreType.DMA((2, pieces, chips - 1)),
            pltpu.SemaphoreType.DMA((2, pieces, chips - 1)),
            pltpu.SemaphoreType.DMA((5,)),
            pltpu.SemaphoreType.DMA((5,)),
            pltpu.SemaphoreType.DMA((3,)),
            pltpu.SemaphoreType.DMA((3,)),
        ],
        compiler_params=pltpu.CompilerParams(
            collective_id=ident, has_side_effects=True, vmem_limit_bytes=63 * 2**20
        ),
        cost_estimate=cost(160),
    )(d_proj, query, keyval, attended, inverse, rows, normed, *turns, *locals_, units)


def feed_kernel(
    chips,
    pieces,
    resid_ref,
    projected_ref,
    dy_ref,
    scales_ref,
    own_ref,
    core_ref,
    side_ref,
    side_last_ref,
    diag_ref,
    diag_last_ref,
    result_ref,
    d_mid_ref,
    d_projected_ref,
    d_gains_ref,
    terms_ref,
    other_ref,
    weights,
    x_all,
    y_all,
    mid,
    both,
    hidden,
    part,
    held_one,
    held_two,
    chunk,
    wide,
    stage,
    load_sem,
    stage_sem,
    other_sem,
    send_sem,
    recv_sem,
):
    tok_rows, width = resid_ref.shape
    units = own_ref.shape[1]
    whole = 4 * units
    half = tok_rows // 2
    rings = [
        Ring(chips, pieces, tok_rows, send_sem.at[phase], recv_sem.at[phase]) for phase in range(4)
    ]
    chip = rings[0].chip
    loads = []
    sources = (
        [own_ref.at[kind] for kind in range(3)],
        [side_ref.at[0], side_ref.at[1], side_last_ref.at[0]],
        [core_ref.at[kind] for kind in range(3)],
        [diag_ref.at[0], diag_ref.at[1], diag_last_ref.at[0]],
    )
    for slot, kinds in enumerate(sources):
        for kind in range(3):
            loads.append(
                pltpu.make_async_copy(
                    kinds[kind],
                    weights.at[pl.ds(kind * whole + slot * units, units)],
                    load_sem.at[slot, kind],
                )
            )
    for load in loads:
        load.start()
    mid[...] = resid_ref[...] + norm_scale(projected_ref[...], scales_ref[1:2])
    x_all[chip] = norm_scale(mid[...], scales_ref[2:3]).astype(bfloat)
    core = lax.axis_index("fsdp") % 2
    to_core = {"fsdp": 2 * chip + 1 - core}
    barrier = pltpu.get_barrier_semaphore()
    for target in ({"fsdp": rings[0].right}, {"fsdp": rings[0].left}, to_core):
        pl.semaphore_signal(barrier, inc=1, device_id=target, device_id_type=MESH)
    pl.semaphore_wait(barrier, 3)
    span = width // 3

    def fetch(all_ref, step):
        chunk[0:half] = all_ref[rings[0].owner(0, step), 0:half]
        chunk[half:] = all_ref[rings[0].owner(1, step), half:]

    def put(ref, step, columns, value):
        ref[rings[0].owner(0, step), 0:half, columns] = value[0:half].astype(ref.dtype)
        ref[rings[0].owner(1, step), half:, columns] = value[half:].astype(ref.dtype)

    def take(ref, step, columns):
        return jnp.concatenate(
            [
                ref[rings[0].owner(0, step), 0:half, columns],
                ref[rings[0].owner(1, step), half:, columns],
            ],
            axis=0,
        )

    def forward(step, carried):
        rings[0].gather_step(x_all, step)

        @pl.when(step == 0)
        def _():
            for load in loads:
                load.wait()

        fetch(x_all, step)

        def gate_up(tile, carried):
            rows = pl.ds(pl.multiple_of(tile * span, span), span)
            wide[:, rows] = dot_nt(chunk[...], weights[rows])
            return carried

        lax.fori_loop(0, 3, gate_up, 0)
        put(both, step, slice(None), wide[...])
        gate = wide[:, 0:whole]
        value, slope = gelu_parts(gate)
        unit = (value * wide[:, whole:]).astype(bfloat)
        put(hidden, step, slice(None), unit)

        def down(tile, carried):
            columns = pl.ds(pl.multiple_of(tile * span, span), span)
            product = dot_nn(take(hidden, step, slice(None)), weights[2 * whole :, columns])
            put(part, step, columns, product)
            return carried

        lax.fori_loop(0, 3, down, 0)
        return carried

    lax.fori_loop(0, chips, forward, 0)

    def spread(step, carried):
        rings[1].scatter_step(part, held_one, step)
        return carried

    lax.fori_loop(0, chips - 1, spread, 0)
    rings[1].scatter_end(part, held_one, wide)
    result_ref[...] = mid[...] + norm_scale(wide[...], scales_ref[3:4])
    d_ffn, d_gain = norm_back(wide[...], scales_ref[3:4], dy_ref[...])
    d_gains_ref[0:1] = jnp.zeros_like(d_gain)
    d_gains_ref[3:4] = d_gain
    y_all[chip] = d_ffn.astype(bfloat)
    rings[0].finish(x_all.at[0, 0 : rings[0].size])
    rings[1].finish(x_all.at[0, 0 : rings[0].size])

    def backward(step, carried):
        rings[2].gather_step(y_all, step)
        fetch(y_all, step)
        third = whole // 3

        def d_units(tile, carried):
            columns = pl.ds(pl.multiple_of(tile * third, third), third)
            rows = pl.ds(pl.multiple_of(2 * whole + tile * third, third), third)
            ups = pl.ds(pl.multiple_of(whole + tile * third, third), third)
            d_hidden = dot_nt(chunk[...], weights[rows])
            gate = take(both, step, columns).astype(single)
            upper = take(both, step, ups).astype(single)
            value, slope = gelu_parts(gate)
            put(both, step, columns, d_hidden * upper * slope)
            put(both, step, ups, d_hidden * value)
            return carried

        lax.fori_loop(0, 3, d_units, 0)

        def d_input(tile, carried):
            columns = pl.ds(pl.multiple_of(tile * span, span), span)
            product = dot_nn(take(both, step, slice(None)), weights[0 : 2 * whole, columns])
            put(part, step, columns, product)
            return carried

        lax.fori_loop(0, 3, d_input, 0)
        return carried

    lax.fori_loop(0, chips, backward, 0)
    rows_tile = stage.shape[1]
    tiles = 3 * whole // rows_tile
    upper_tiles = 2 * whole // rows_tile

    cut = units // 3

    def pieces_of(tile):
        for quarter in range(4):
            block = 4 * tile + quarter
            kind, slot, third = block // 12, (block // 3) % 4, block % 3
            source = stage.at[tile % 2, pl.ds(quarter * cut, cut)]
            rows = pl.ds(pl.multiple_of(third * cut, cut), cut)
            sem = stage_sem.at[tile % 2, quarter]
            goal = terms_ref.at[slot, kind, rows], other_ref.at[slot - 2, kind, rows]
            there = functools.partial(
                remote, source, goal[1], sem, other_sem.at[tile, quarter], to_core
            )
            yield slot, functools.partial(pltpu.make_async_copy, source, goal[0], sem), there

    def keep(tile):
        for slot, here, there in pieces_of(tile):

            @pl.when(slot < 2)
            def _():
                here().start()

            @pl.when(slot >= 2)
            def _():
                there().start()

    def kept(tile):
        for slot, here, there in pieces_of(tile):

            @pl.when(slot < 2)
            def _():
                here().wait()

            @pl.when(slot >= 2)
            def _():
                there().wait_send()

    def grads(tile):
        @pl.when(tile >= 2)
        def _():
            kept(tile - 2)

        @pl.when(tile < upper_tiles)
        def _():
            columns = pl.ds(pl.multiple_of(tile * rows_tile, rows_tile), rows_tile)
            left = both[:, :, columns].reshape(chips * tok_rows, rows_tile)
            stage[tile % 2] = dot_tn(left, x_all[...].reshape(chips * tok_rows, width)).astype(bfloat)

        @pl.when(tile >= upper_tiles)
        def _():
            columns = pl.ds(
                pl.multiple_of((tile - upper_tiles) * rows_tile, rows_tile), rows_tile
            )
            left = hidden[:, :, columns].reshape(chips * tok_rows, rows_tile)
            stage[tile % 2] = dot_tn(left, y_all[...].reshape(chips * tok_rows, width)).astype(bfloat)

        keep(tile)

    def spread_back(step, carried):
        rings[3].scatter_step(part, held_two, step)
        grads(step)
        return carried

    lax.fori_loop(0, chips - 1, spread_back, 0)

    def rest(tile, carried):
        grads(tile)
        return carried

    lax.fori_loop(chips - 1, tiles, rest, 0)
    rings[3].scatter_end(part, held_two, wide)
    d_norm, d_gain = norm_back(mid[...], scales_ref[2:3], wide[...])
    d_gains_ref[2:3] = d_gain
    d_mid_ref[...] = dy_ref[...] + d_norm
    d_projected, d_gain = norm_back(projected_ref[...], scales_ref[1:2], d_mid_ref[...])
    d_gains_ref[1:2] = d_gain
    d_projected_ref[...] = d_projected.astype(bfloat)
    rings[2].finish(x_all.at[0, 0 : rings[0].size])
    rings[3].finish(x_all.at[0, 0 : rings[0].size])
    kept(tiles - 2)
    kept(tiles - 1)

    def gained(tile, carried):
        for slot, here, there in pieces_of(tile):

            @pl.when(slot >= 2)
            def _():
                there().wait_recv()

        return carried

    lax.fori_loop(0, tiles, gained, 0)


def feed_forward(resid_in, projected, grad_out, scales, shares, chips, ident):
    tok_rows, width = resid_in.shape
    units = shares[0].shape[1]
    whole = 4 * units
    pieces = 2
    vmem = pl.BlockSpec(memory_space=pltpu.VMEM)
    anywhere = pl.BlockSpec(memory_space=pl.ANY)
    return pl.pallas_call(
        functools.partial(feed_kernel, chips, pieces),
        out_shape=(
            jax.ShapeDtypeStruct((tok_rows, width), single),
            jax.ShapeDtypeStruct((tok_rows, width), single),
            jax.ShapeDtypeStruct((tok_rows, width), bfloat),
            jax.ShapeDtypeStruct((4, width), single),
            jax.ShapeDtypeStruct((2, 3, units, width), bfloat),
            jax.ShapeDtypeStruct((2, 3, units, width), bfloat),
        ),
        in_specs=[vmem] * 4 + [anywhere] * 6,
        out_specs=(vmem, vmem, vmem, vmem, anywhere, anywhere),
        scratch_shapes=[
            pltpu.VMEM((3 * whole, width), bfloat),
            pltpu.VMEM((chips, tok_rows, width), bfloat),
            pltpu.VMEM((chips, tok_rows, width), bfloat),
            pltpu.VMEM((tok_rows, width), single),
            pltpu.VMEM((chips, tok_rows, 2 * whole), bfloat),
            pltpu.VMEM((chips, tok_rows, whole), bfloat),
            pltpu.VMEM((chips, tok_rows, width), bfloat),
            pltpu.VMEM((2, chips - 1, tok_rows // 2, width), bfloat),
            pltpu.VMEM((2, chips - 1, tok_rows // 2, width), bfloat),
            pltpu.VMEM((tok_rows, width), bfloat),
            pltpu.VMEM((tok_rows, width), single),
            pltpu.VMEM((2, whole // 3, width), bfloat),
            pltpu.SemaphoreType.DMA((4, 3)),
            pltpu.SemaphoreType.DMA((2, 4)),
            pltpu.SemaphoreType.DMA((9, 4)),
            pltpu.SemaphoreType.DMA((4, 2, pieces, chips - 1)),
            pltpu.SemaphoreType.DMA((4, 2, pieces, chips - 1)),
        ],
        compiler_params=pltpu.CompilerParams(
            collective_id=ident, has_side_effects=True, vmem_limit_bytes=63 * 2**20
        ),
        cost_estimate=cost(205),
    )(resid_in, projected, grad_out, scales, *shares)


def general_device(
    tokens,
    cotangent,
    gains,
    gains_first,
    gains_second,
    attn_weight,
    attn_first,
    attn_second,
    ffn_weight,
    ffn_first,
    ffn_second,
):
    devices = lax.axis_size("fsdp")
    chips = devices // 2
    side = lax.axis_index("head")
    place = lax.axis_index("fsdp")
    core, chip = place % 2, place // 2
    tok_rows = tokens.shape[1]
    super_rows = 4 * tok_rows
    seq_len = min(SEQ_LEN, super_rows * chips)
    share = attn_weight.shape[1]
    pairs = chips // 4
    width = tokens.shape[2]
    scale = 1.0 / math.sqrt(HD)

    def swap_core(value):
        return lax.ppermute(value, "fsdp", [(index, index ^ 1) for index in range(devices)])

    def swap_side(value):
        return lax.ppermute(value, "head", [(0, 1), (1, 0)])

    def in_order(own, other, index, axis):
        return jnp.where(
            index == 0, jnp.stack([own, other], axis), jnp.stack([other, own], axis)
        )

    def pick(value, index, axis=0):
        return lax.dynamic_index_in_dim(value, index, axis, keepdims=False)

    def quad_gather(value):
        value = in_order(value, swap_side(value), side, 0)
        value = in_order(value, swap_core(value), core, 0)
        return value.reshape((super_rows,) + value.shape[3:])

    def quad_scatter(partial):
        partial = partial.reshape(2, 2, tok_rows, width)
        mine = pick(partial, core) + swap_core(pick(partial, 1 - core).astype(bfloat)).astype(single)
        return pick(mine, side) + swap_side(pick(mine, 1 - side).astype(bfloat)).astype(single)

    scales = lax.all_gather(gains.astype(bfloat), ("head", "fsdp"), axis=1, tiled=True).astype(single)
    attn_low = attn_weight.astype(bfloat)
    ffn_low = ffn_weight.astype(bfloat).transpose(1, 0, 2)
    ffn_pair = jnp.concatenate([ffn_low, swap_side(ffn_low)], axis=1)

    ring_rows = ring_gather(attn_low.reshape(3 * share, width), chips, 0)
    ring_rows = ring_rows.reshape(2, 2, pairs, 3, share, width)

    def query_rows(slot):
        rows = ring_rows[:, :, :, slot]
        other = swap_core(pick(rows, 1 - core))
        return in_order(pick(rows, core), other, core, 2).reshape(2 * HD, width)

    def keyval_rows():
        rows = ring_rows[:, :, :, 1]
        other = swap_core(pick(rows, 1 - core, 1))
        return in_order(pick(rows, core, 1), other, core, 2).reshape(2 * HD, width)

    w_query, w_keyval, w_out = query_rows(0), keyval_rows(), query_rows(2)

    resid_in = tokens[0]
    grad_out = cotangent[0]
    normed_one = norm_scale(resid_in, scales[0]).astype(bfloat)
    normed_all = quad_gather(normed_one)
    positions = chip * super_rows + jnp.arange(super_rows, dtype=jnp.int32)
    angles = turn_angles(positions % seq_len, HD)
    query_raw = jnp.einsum("td,fd->tf", normed_all, w_query, preferred_element_type=single)
    keyval_raw = jnp.einsum("td,fd->tf", normed_all, w_keyval, preferred_element_type=single)
    query = rotate(query_raw.reshape(super_rows, 2, HD), angles, 1.0).astype(bfloat)
    key_angles = jnp.where(side == 0, angles, 0.0)
    keyval = rotate(keyval_raw.reshape(super_rows, 2, HD), key_angles, 1.0).astype(bfloat)
    keyval = in_order(pick(keyval, side, 1), swap_side(pick(keyval, 1 - side, 1)), side, 0)
    keyval_all = ring_gather(keyval.reshape(2 * super_rows, HD), chips, 1)
    keyval_all = keyval_all.reshape(chips, 2, super_rows, HD)
    key_all = keyval_all[:, 0].reshape(chips * super_rows, HD)
    value_all = keyval_all[:, 1].reshape(chips * super_rows, HD)

    key_pos = jnp.arange(chips * super_rows, dtype=jnp.int32)
    distance = positions[:, None] - key_pos[None, :]
    same_seq = (positions // seq_len)[:, None] == (key_pos // seq_len)[None, :]
    allowed = (distance >= 0) & (distance < WIN) & same_seq

    def score_block():
        raw = jnp.einsum("qgd,kd->gqk", query, key_all, preferred_element_type=single)
        bent = jnp.tanh(raw * (scale / softcap))
        return bent, jnp.where(allowed, jnp.exp(softcap * bent), 0.0)

    bent, powers = score_block()
    total = jnp.sum(powers, axis=-1, keepdims=True)
    attended = jnp.einsum(
        "gqk,kd->gqd", powers.astype(bfloat), value_all, preferred_element_type=single
    )
    attended = (attended / total).transpose(1, 0, 2).reshape(super_rows, 2 * HD).astype(bfloat)
    projected = quad_scatter(jnp.dot(attended, w_out, preferred_element_type=single))
    resid_mid = resid_in + norm_scale(projected, scales[1])
    normed_two = norm_scale(resid_mid, scales[2]).astype(bfloat)

    ffn_all = jnp.concatenate([ffn_pair, swap_core(ffn_pair)], axis=1)
    w_gate, w_up, w_down = ffn_all[0], ffn_all[1], ffn_all[2]
    ring_tokens = chips * tok_rows
    normed_ring = ring_gather(normed_two, chips, 2).reshape(ring_tokens, width)
    gate_part = jnp.einsum("td,rd->tr", normed_ring, w_gate, preferred_element_type=single)
    up_part = jnp.einsum("td,rd->tr", normed_ring, w_up, preferred_element_type=single)
    hidden = hidden_unit(gate_part, up_part).astype(bfloat)
    ffn_part = jnp.dot(hidden, w_down, preferred_element_type=single).astype(bfloat)
    ffn_acc = ring_scatter(ffn_part.reshape(chips, tok_rows, width), chips, 3)
    result = resid_mid + norm_scale(ffn_acc, scales[3])

    ignored, post_back = jax.vjp(norm_scale, ffn_acc, scales[3])
    d_ffn, d_gain3 = post_back(grad_out)
    d_ffn_ring = ring_gather(d_ffn.astype(bfloat), chips, 4).reshape(ring_tokens, width)
    d_hidden = jnp.einsum("td,rd->tr", d_ffn_ring, w_down, preferred_element_type=single)
    ignored, unit_back = jax.vjp(hidden_unit, gate_part, up_part)
    d_gate, d_up = unit_back(d_hidden)
    d_gate = d_gate.astype(bfloat)
    d_up = d_up.astype(bfloat)
    d_normed = jnp.dot(d_gate, w_gate, preferred_element_type=single)
    d_normed = (d_normed + jnp.dot(d_up, w_up, preferred_element_type=single)).astype(bfloat)
    d_normed_two = ring_scatter(d_normed.reshape(chips, tok_rows, width), chips, 5)

    def ffn_rows(left, right):
        return jnp.einsum("tr,td->rd", left, right, preferred_element_type=single)

    ffn_terms = jnp.stack(
        [ffn_rows(d_gate, normed_ring), ffn_rows(d_up, normed_ring), ffn_rows(hidden, d_ffn_ring)]
    )
    units = ffn_weight.shape[0]
    ffn_terms = ffn_terms.reshape(3, 2, 2, units, width)
    ffn_terms = ffn_terms[:, 0] + swap_core(ffn_terms[:, 1].astype(bfloat)).astype(single)
    grad_ffn = ffn_terms[:, 0] + swap_side(ffn_terms[:, 1].astype(bfloat)).astype(single)

    ignored, mid_back = jax.vjp(norm_scale, resid_mid, scales[2])
    d_mid_norm, d_gain2 = mid_back(d_normed_two)
    d_mid = grad_out + d_mid_norm
    ignored, proj_back = jax.vjp(norm_scale, projected, scales[1])
    d_projected, d_gain1 = proj_back(d_mid)
    d_proj_all = quad_gather(d_projected.astype(bfloat))
    d_attended = jnp.einsum("td,fd->tf", d_proj_all, w_out, preferred_element_type=single)
    d_attended = d_attended.astype(bfloat).reshape(super_rows, 2, HD)

    bent, powers = score_block()
    probs = powers / total
    d_probs = jnp.einsum("qgd,kd->gqk", d_attended, value_all, preferred_element_type=single)
    row_dot = jnp.sum(d_probs * probs, axis=-1, keepdims=True)
    d_raw = (probs * (d_probs - row_dot) * (1.0 - bent * bent)).astype(bfloat)
    d_query = jnp.einsum("gqk,kd->qgd", d_raw, key_all, preferred_element_type=single) * scale
    d_keys = jnp.einsum("gqk,qgd->kd", d_raw, query, preferred_element_type=single) * scale
    d_values = jnp.einsum(
        "gqk,qgd->kd", probs.astype(bfloat), d_attended, preferred_element_type=single
    )
    d_pieces = jnp.stack(
        [d_keys.reshape(chips, super_rows, HD), d_values.reshape(chips, super_rows, HD)], axis=1
    ).astype(bfloat)
    d_keyval = ring_scatter(d_pieces.reshape(chips, 2 * super_rows, HD), chips, 6)
    d_keyval = d_keyval.reshape(2, super_rows, HD).astype(bfloat)
    d_keyval = in_order(pick(d_keyval, side), swap_side(pick(d_keyval, 1 - side)), side, 1)
    d_query_raw = rotate(d_query, angles, -1.0).reshape(super_rows, 2 * HD).astype(bfloat)
    d_keyval_raw = rotate(d_keyval.astype(single), key_angles, -1.0)
    d_keyval_raw = d_keyval_raw.reshape(super_rows, 2 * HD).astype(bfloat)
    d_normed_one = jnp.dot(d_query_raw, w_query, preferred_element_type=single)
    d_normed_one = d_normed_one + jnp.dot(d_keyval_raw, w_keyval, preferred_element_type=single)
    d_normed_one = quad_scatter(d_normed_one)
    ignored, first_back = jax.vjp(norm_scale, resid_in, scales[0])
    d_in_norm, d_gain0 = first_back(d_normed_one)
    tokens_grad = d_mid + d_in_norm

    def attn_rows(left, right):
        rows = jnp.einsum("tf,td->fd", left, right, preferred_element_type=single).astype(bfloat)
        return rows.reshape(2, pairs, 2, share, width)

    term_query = attn_rows(d_query_raw, normed_all)
    term_keyval = attn_rows(d_keyval_raw, normed_all)
    term_out = attn_rows(attended, d_proj_all)

    def to_core(term, axis):
        return in_order(pick(term, core, 2), swap_core(pick(term, 1 - core, 2)), core, axis)

    terms = jnp.stack([to_core(term_query, 0), to_core(term_keyval, 1), to_core(term_out, 0)], axis=3)
    grad_attn = ring_scatter(terms.reshape(chips, 3 * share, width), chips, 7)
    grad_attn = grad_attn.reshape(3, share, width)
    term_gain = jnp.stack([d_gain0, d_gain1, d_gain2, d_gain3])
    grad_gain = lax.psum_scatter(term_gain, ("head", "fsdp"), scatter_dimension=1, tiled=True)

    gains_first_new, gains_second_new, gains_new = adamw(
        gains, gains_first, gains_second, grad_gain, rate_gain, 0.0
    )
    attn_first_new, attn_second_new, attn_weight_new = adamw(
        attn_weight, attn_first, attn_second, grad_attn, rate_matrix, decay_matrix
    )
    ffn_first_new, ffn_second_new, ffn_weight_new = adamw(
        ffn_weight, ffn_first, ffn_second, grad_ffn.transpose(1, 0, 2), rate_matrix, decay_matrix
    )
    return (
        result[None],
        tokens_grad[None],
        gains_first_new,
        gains_second_new,
        gains_new,
        attn_first_new,
        attn_second_new,
        attn_weight_new,
        ffn_first_new,
        ffn_second_new,
        ffn_weight_new,
    )


def per_device(
    tokens,
    cotangent,
    gains,
    gains_first,
    gains_second,
    attn_weight,
    attn_first,
    attn_second,
    ffn_weight,
    ffn_first,
    ffn_second,
):
    devices = lax.axis_size("fsdp")
    chips = devices // 2
    side = lax.axis_index("head")
    place = lax.axis_index("fsdp")
    chip = place // 2
    tok_rows = tokens.shape[1]
    super_rows = 4 * tok_rows
    seq_len = min(SEQ_LEN, super_rows * chips)
    share = attn_weight.shape[1]
    width = tokens.shape[2]
    gain_columns = gains.shape[1]
    gain_start = (side * devices + place) * gain_columns

    ffn_low = ffn_weight.astype(bfloat).transpose(1, 0, 2)
    resid_in = tokens[0]
    grad_out = cotangent[0]
    positions = chip * super_rows + jnp.arange(super_rows, dtype=jnp.int32)
    angles = turn_angles(positions % seq_len, HD)
    key_angles = jnp.where(side == 0, angles, 0.0)
    gains_placed = lax.dynamic_update_slice(
        jnp.zeros((4, width), single), gains, (0, gain_start)
    )
    turns = (jnp.cos(angles), jnp.sin(angles), jnp.cos(key_angles), jnp.sin(key_angles))
    attn_rows, scales, normed_all, query, keyval, side_units, core_units = front(
        attn_weight.astype(bfloat), gains_placed, resid_in, *turns, ffn_low, chips, 0
    )
    keyval_all, attended, inverse, projected, side_last, diag_units, diag_last = attend(
        query, keyval, attn_rows, ffn_low, side_units, chips, 1
    )
    units = (ffn_low, core_units, side_units, side_last, diag_units, diag_last)
    result, d_mid, d_proj_low, gain_rows, terms_own, terms_other = feed_forward(
        resid_in, projected, grad_out, scales, units, chips, 2
    )
    ffn_terms = terms_own.astype(single) + terms_other.astype(single)
    grad_attn, tokens_grad, gain_total, terms_side = tail(
        d_proj_low,
        query,
        keyval_all,
        attended,
        inverse,
        attn_rows,
        normed_all,
        turns,
        (resid_in, d_mid, scales, gain_rows),
        ffn_terms[1].astype(bfloat),
        chips,
        3,
    )
    grad_ffn = ffn_terms[0] + terms_side.astype(single)
    grad_attn = grad_attn.reshape(3, share, width)
    grad_gain = lax.dynamic_slice(gain_total, (0, gain_start), gains.shape)

    gains_first_new, gains_second_new, gains_new = adamw(
        gains, gains_first, gains_second, grad_gain, rate_gain, 0.0
    )
    attn_first_new, attn_second_new, attn_weight_new = adamw(
        attn_weight, attn_first, attn_second, grad_attn, rate_matrix, decay_matrix
    )
    ffn_first_new, ffn_second_new, ffn_weight_new = adamw(
        ffn_weight, ffn_first, ffn_second, grad_ffn.transpose(1, 0, 2), rate_matrix, decay_matrix
    )
    return (
        result[None],
        tokens_grad[None],
        gains_first_new,
        gains_second_new,
        gains_new,
        attn_first_new,
        attn_second_new,
        attn_weight_new,
        ffn_first_new,
        ffn_second_new,
        ffn_weight_new,
    )


def solution(mesh):
    by_token = P("fsdp", "head", None)
    by_column = P(None, ("head", "fsdp"))
    by_row = P(None, ("head", "fsdp"), None)
    by_unit = P(("head", "fsdp"), None, None)
    placed = (by_token,) * 2 + (by_column,) * 3 + (by_row,) * 3 + (by_unit,) * 3
    body = per_device if mesh.shape["fsdp"] == 16 else general_device
    return jax.shard_map(
        body, mesh=mesh, in_specs=placed, out_specs=placed, check_vma=False
    )
```

```python
import functools
import math

import jax
import jax.numpy as jnp
from jax import lax
from jax.experimental import pallas as pl
from jax.experimental.pallas import tpu as pltpu
from jax.sharding import PartitionSpec as P

HQ = 8
HK = 4
HD = 256
WIN = 4096
STEP = 10
SEQ_LEN = 8192


eps_norm = 1e-06
softcap = 50.0
beta_one = 0.9
beta_two = 0.95
adam_eps = 1e-08
rate_matrix = 0.02
rate_gain = 0.2
decay_matrix = 0.1

bfloat = jnp.bfloat16
single = jnp.float32
MESH = pl.DeviceIdType.MESH


def norm_scale(values, scales):
    return (
        values
        * lax.rsqrt(jnp.mean(values * values, axis=-1, keepdims=True) + eps_norm)
        * (1.0 + scales)
    )


def turn_angles(positions, head_width):
    halfway = head_width // 2
    inverse_freq = 10000.0 ** (-(jnp.arange(halfway, dtype=jnp.float32) * 2.0) / head_width)
    return positions.astype(jnp.float32)[:, None] * inverse_freq[None, :]


def rotate(values, angles, direction):
    halfway = values.shape[-1] // 2
    cosine = jnp.cos(angles)[:, None, :]
    sine_part = direction * jnp.sin(angles)[:, None, :]
    former = values[..., :halfway]
    latter = values[..., halfway:]
    return jnp.concatenate(
        [former * cosine - latter * sine_part, latter * cosine + former * sine_part], axis=-1
    )


def adamw(weight, moment, second, gradient, step_rate, decay_rate):
    moment = beta_one * moment + (1.0 - beta_one) * gradient
    second = beta_two * second + (1.0 - beta_two) * gradient * gradient
    update = (
        moment / (1.0 - beta_one**STEP) / (jnp.sqrt(second / (1.0 - beta_two**STEP)) + adam_eps)
        + decay_rate * weight
    )
    return (moment, second, weight - step_rate * update)


def hidden_unit(gate_part, up_part):
    return jax.nn.gelu(gate_part, approximate=True) * up_part


def ring_of(chip, chips):
    wide = chips // 4
    deep, side = chip // wide, chip % wide
    return side * 4 + deep + (side % 2) * (3 - 2 * deep)


def chip_of(ring, chips):
    wide = chips // 4
    side, along = ring // 4, ring % 4
    return (along + (side % 2) * (3 - 2 * along)) * wide + side


def ring_places(chips):
    index = lax.axis_index("fsdp")
    core, chip = index % 2, index // 2
    ring = ring_of(chip, chips)
    right = 2 * chip_of((ring + 1) % chips, chips) + core
    left = 2 * chip_of((ring + chips - 1) % chips, chips) + core
    return chip, ring, right, left


def ring_barrier(right, left):
    barrier = pltpu.get_barrier_semaphore()
    for neighbour in (left, right):
        pl.semaphore_signal(barrier, inc=1, device_id={"fsdp": neighbour}, device_id_type=MESH)
    pl.semaphore_wait(barrier, 2)


def region(shape, pieces, way, piece):
    rows, columns = shape
    if rows % 32 == 0:
        size = rows // 2 // pieces
        start = way * (rows // 2) + piece * size
        return (pl.ds(start, size), pl.ds(0, columns)), (pl.ds(piece * size, size), pl.ds(0, columns))
    size = columns // 2
    return (pl.ds(0, rows), pl.ds(way * size, size)), (pl.ds(0, rows), pl.ds(0, size))


def half_shape(rows, columns):
    return (rows // 2, columns) if rows % 32 == 0 else (rows, columns // 2)


def gather_kernel(chips, pieces, own_ref, all_ref, local_sem, send_sem, recv_sem):
    chip, ring, right, left = ring_places(chips)
    ring_barrier(right, left)
    keep = pltpu.make_async_copy(own_ref, all_ref.at[chip], local_sem)
    keep.start()

    def copy(way, step, piece, first):
        owner = chip_of((ring + (chips - step if way == 0 else step)) % chips, chips)
        part, ignored = region(own_ref.shape, pieces, way, piece)
        there = all_ref.at[(owner,) + part]
        return pltpu.make_async_remote_copy(
            src_ref=own_ref.at[part] if first else there,
            dst_ref=there,
            send_sem=send_sem.at[way, piece, step],
            recv_sem=recv_sem.at[way, piece, step],
            device_id={"fsdp": right if way == 0 else left},
            device_id_type=MESH,
        )

    streams = [(way, piece) for piece in range(pieces) for way in range(2)]
    for way, piece in streams:
        copy(way, 0, piece, True).start()

    def body(step, carried):
        for way, piece in streams:
            copy(way, step - 1, piece, False).wait_recv()
            copy(way, step, piece, False).start()
        return carried

    lax.fori_loop(1, chips - 1, body, 0)
    for way, piece in streams:
        copy(way, chips - 2, piece, False).wait_recv()

    def finish(step, carried):
        for way, piece in streams:
            copy(way, step, piece, False).wait_send()
        return carried

    lax.fori_loop(0, chips - 1, finish, 0)
    keep.wait()


def ring_gather(own, chips, ident):
    rows, columns = own.shape
    pieces = 2 if rows % 64 == 0 else 1
    return pl.pallas_call(
        functools.partial(gather_kernel, chips, pieces),
        out_shape=jax.ShapeDtypeStruct((chips, rows, columns), own.dtype),
        in_specs=[pl.BlockSpec(memory_space=pl.ANY)],
        out_specs=pl.BlockSpec(memory_space=pl.ANY),
        scratch_shapes=[
            pltpu.SemaphoreType.DMA,
            pltpu.SemaphoreType.DMA((2, pieces, chips - 1)),
            pltpu.SemaphoreType.DMA((2, pieces, chips - 1)),
        ],
        compiler_params=pltpu.CompilerParams(collective_id=ident, has_side_effects=True),
        cost_estimate=cost(45),
    )(own)


def scatter_kernel(chips, pieces, parts_ref, sum_ref, held, send_sem, recv_sem):
    chip, ring, right, left = ring_places(chips)
    ring_barrier(right, left)

    def owner_of(way, step):
        shift = chips - 1 - step if way == 0 else 1 + step
        return chip_of((ring + shift) % chips, chips)

    def copy(way, step, piece, first):
        part, place = region(sum_ref.shape, pieces, way, piece)
        return pltpu.make_async_remote_copy(
            src_ref=(
                parts_ref.at[(owner_of(way, step),) + part]
                if first
                else held.at[(way, step - 1) + place]
            ),
            dst_ref=held.at[(way, step) + place],
            send_sem=send_sem.at[way, piece, step],
            recv_sem=recv_sem.at[way, piece, step],
            device_id={"fsdp": right if way == 0 else left},
            device_id_type=MESH,
        )

    streams = [(way, piece) for piece in range(pieces) for way in range(2)]
    for way, piece in streams:
        copy(way, 0, piece, True).start()

    def arrived(way, step, piece):
        copy(way, step, piece, True).wait_recv()
        part, place = region(sum_ref.shape, pieces, way, piece)
        here = parts_ref[(owner_of(way, step + 1),) + part]
        return held[(way, step) + place].astype(single) + here.astype(single)

    def body(step, carried):
        for way, piece in streams:
            total = arrived(way, step - 1, piece)
            part, place = region(sum_ref.shape, pieces, way, piece)
            held[(way, step - 1) + place] = total.astype(held.dtype)
            copy(way, step, piece, False).start()
        return carried

    lax.fori_loop(1, chips - 1, body, 0)
    for way, piece in streams:
        part, place = region(sum_ref.shape, pieces, way, piece)
        sum_ref[part] = arrived(way, chips - 2, piece)

    def finish(step, carried):
        for way, piece in streams:
            copy(way, step, piece, True).wait_send()
        return carried

    lax.fori_loop(0, chips - 1, finish, 0)


def ring_scatter(parts, chips, ident):
    rows, columns = parts.shape[1:]
    pieces = 2 if rows % 64 == 0 else 1
    return pl.pallas_call(
        functools.partial(scatter_kernel, chips, pieces),
        out_shape=jax.ShapeDtypeStruct((rows, columns), single),
        in_specs=[pl.BlockSpec(memory_space=pltpu.VMEM)],
        out_specs=pl.BlockSpec(memory_space=pltpu.VMEM),
        scratch_shapes=[
            pltpu.VMEM((2, chips - 1) + half_shape(rows, columns), parts.dtype),
            pltpu.SemaphoreType.DMA((2, pieces, chips - 1)),
            pltpu.SemaphoreType.DMA((2, pieces, chips - 1)),
        ],
        compiler_params=pltpu.CompilerParams(
            collective_id=ident, has_side_effects=True, vmem_limit_bytes=56 * 2**20
        ),
        cost_estimate=cost(45),
    )(parts)


def norm_back(values, scales, grad):
    inverse = lax.rsqrt(jnp.mean(values * values, axis=-1, keepdims=True) + eps_norm)
    bent = grad * (1.0 + scales)
    slope = jnp.mean(bent * values, axis=-1, keepdims=True) * (inverse * inverse * inverse)
    return bent * inverse - values * slope, jnp.sum(grad * values * inverse, axis=0, keepdims=True)


def gelu_parts(gate):
    root = math.sqrt(2.0 / math.pi)
    square = gate * gate
    bend = jnp.tanh(root * gate * (1.0 + 0.044715 * square))
    half = 0.5 * (1.0 + bend)
    slope = half + 0.5 * gate * (1.0 - bend * bend) * (root * (1.0 + 3.0 * 0.044715 * square))
    return gate * half, slope


def dot_nt(left, right):
    return lax.dot_general(left, right, (((1,), (1,)), ((), ())), preferred_element_type=single)


def dot_nn(left, right):
    return lax.dot_general(left, right, (((1,), (0,)), ((), ())), preferred_element_type=single)


def dot_tn(left, right):
    return lax.dot_general(left, right, (((0,), (0,)), ((), ())), preferred_element_type=single)


class Ring:
    def __init__(self, chips, pieces, rows, send_sem, recv_sem):
        self.chips, self.pieces, self.half = chips, pieces, rows // 2
        self.size = rows // 2 // pieces
        self.chip, self.ring, self.right, self.left = ring_places(chips)
        self.send_sem, self.recv_sem = send_sem, recv_sem
        self.streams = [(way, piece) for piece in range(pieces) for way in range(2)]

    def owner(self, way, step):
        shift = self.chips - step if way == 0 else step
        return chip_of((self.ring + shift) % self.chips, self.chips)

    def copy(self, source, target, way, piece, step):
        return pltpu.make_async_remote_copy(
            src_ref=source,
            dst_ref=target,
            send_sem=self.send_sem.at[way, piece, step],
            recv_sem=self.recv_sem.at[way, piece, step],
            device_id={"fsdp": self.right if way == 0 else self.left},
            device_id_type=MESH,
        )

    def part(self, way, piece):
        return pl.ds(way * self.half + piece * self.size, self.size)

    def place(self, piece):
        return pl.ds(piece * self.size, self.size)

    def gather_copy(self, all_ref, way, piece, step):
        there = all_ref.at[self.owner(way, step), self.part(way, piece)]
        return self.copy(there, there, way, piece, step)

    def gather_step(self, all_ref, step):
        for way, piece in self.streams:

            @pl.when(step > 0)
            def _():
                self.gather_copy(all_ref, way, piece, step - 1).wait_recv()

            @pl.when(step < self.chips - 1)
            def _():
                self.gather_copy(all_ref, way, piece, step).start()

    def scatter_copy(self, parts_ref, held, way, piece, step, first):
        source = (
            parts_ref.at[self.owner(way, step + 1), self.part(way, piece)]
            if first
            else held.at[way, step - 1, self.place(piece)]
        )
        return self.copy(source, held.at[way, step, self.place(piece)], way, piece, step)

    def scatter_total(self, parts_ref, held, way, piece, step):
        self.scatter_copy(parts_ref, held, way, piece, step, True).wait_recv()
        here = parts_ref[self.owner(way, step + 2), self.part(way, piece)]
        return held[way, step, self.place(piece)].astype(single) + here.astype(single)

    def scatter_step(self, parts_ref, held, step):
        for way, piece in self.streams:

            @pl.when(step == 0)
            def _():
                self.scatter_copy(parts_ref, held, way, piece, 0, True).start()

            @pl.when(step > 0)
            def _():
                total = self.scatter_total(parts_ref, held, way, piece, step - 1)
                held[way, step - 1, self.place(piece)] = total.astype(held.dtype)
                self.scatter_copy(parts_ref, held, way, piece, step, False).start()

    def scatter_end(self, parts_ref, held, sum_ref):
        for way, piece in self.streams:
            sum_ref[self.part(way, piece)] = self.scatter_total(
                parts_ref, held, way, piece, self.chips - 2
            )

    def finish(self, example):
        def body(step, carried):
            for way, piece in self.streams:
                self.copy(example, example, way, piece, step).wait_send()
            return carried

        lax.fori_loop(0, self.chips - 1, body, 0)


def quad_peers(chips):
    side = lax.axis_index("head")
    index = lax.axis_index("fsdp")
    chip, core = index // 2, index % 2
    ring = ring_of(chip, chips)
    around = [2 * chip_of((ring + hop) % chips, chips) + core for hop in range(1, chips)]
    return side, core, {"head": 1 - side}, {"fsdp": 2 * chip + 1 - core}, around


def wide_barrier(to_side, to_core, around):
    barrier = pltpu.get_barrier_semaphore()
    for target in [to_side, to_core] + [{"fsdp": other} for other in around]:
        pl.semaphore_signal(barrier, inc=1, device_id=target, device_id_type=MESH)
    pl.semaphore_wait(barrier, 2 + len(around))


def remote(source, target, send_sem, recv_sem, device):
    return pltpu.make_async_remote_copy(
        src_ref=source,
        dst_ref=target,
        send_sem=send_sem,
        recv_sem=recv_sem,
        device_id=device,
        device_id_type=MESH,
    )


class Total:
    def __init__(self, value, near, blocks, send_sem, recv_sem, peers, chip):
        self.value, self.near, self.blocks = value, near, blocks
        self.send_sem, self.recv_sem = send_sem, recv_sem
        side, core, self.to_side, self.to_core, self.around = peers
        self.chip = chip
        self.first = remote(value.at[0], near.at[0], send_sem.at[0], recv_sem.at[0], self.to_side)
        self.second = remote(value.at[1], near.at[1], send_sem.at[1], recv_sem.at[1], self.to_core)

    def spread(self, hop):
        here = self.blocks.at[self.chip]
        return remote(
            here,
            here,
            self.send_sem.at[1 + hop],
            self.recv_sem.at[1 + hop],
            {"fsdp": self.around[hop - 1]},
        )

    def start(self):
        self.first.start()

    def over_cores(self):
        self.first.wait_recv()
        self.value[1] = self.value[0] + self.near[0]
        self.second.start()

    def over_ring(self):
        self.second.wait_recv()
        self.blocks[self.chip] = self.value[1] + self.near[1]
        for hop in range(1, len(self.around) + 1):
            self.spread(hop).start()

    def end(self):
        for hop in range(1, len(self.around) + 1):
            self.spread(hop).wait_recv()
        total = self.blocks[0]
        for other in range(1, len(self.around) + 1):
            total = total + self.blocks[other]
        self.first.wait_send()
        self.second.wait_send()
        for hop in range(1, len(self.around) + 1):
            self.spread(hop).wait_send()
        return total


def total_scratch(chips, width):
    return [
        pltpu.VMEM((2, 4, width), single),
        pltpu.VMEM((2, 4, width), single),
        pltpu.VMEM((chips, 4, width), single),
        pltpu.SemaphoreType.DMA((chips + 1,)),
        pltpu.SemaphoreType.DMA((chips + 1,)),
    ]


def turn(raw, cosine, sine):
    halfway = raw.shape[1] // 2
    former, latter = raw[:, :halfway], raw[:, halfway:]
    return jnp.concatenate(
        [former * cosine - latter * sine, latter * cosine + former * sine], axis=1
    )


def front_kernel(
    chips,
    first_units,
    own_ref,
    gains_ref,
    resid_ref,
    cosine_ref,
    sine_ref,
    key_cosine_ref,
    key_sine_ref,
    wide_units_ref,
    rows_ref,
    scales_ref,
    normed_ref,
    query_ref,
    keyval_ref,
    attended_ref,
    inverse_ref,
    projected_ref,
    own_units_ref,
    core_units_ref,
    side_units_ref,
    diag_units_ref,
    all_rows,
    both,
    total,
    sums,
    product,
    across_put,
    across_got,
    along_put,
    along_got,
    cast_in,
    cast_out,
    value,
    near,
    blocks,
    total_send,
    total_recv,
    send_sem,
    recv_sem,
    place_sem,
    peer_sem,
    key_send,
    key_recv,
    quad_send,
    quad_recv,
    cast_sem,
    bulk_send,
    bulk_recv,
):
    share, width = own_ref.shape[1:]
    tok_rows = resid_ref.shape[0]
    tokens = 4 * tok_rows
    half = width // 2
    pairs = chips // 4
    scale = 1.0 / math.sqrt(HD)
    chip, ring, right, left = ring_places(chips)
    peers = quad_peers(chips)
    side, core, to_side, to_core, around = peers
    cast_rows = cast_in.shape[1]
    casts = wide_units_ref.shape[0] // cast_rows

    def cast_load(tile):
        rows = pl.ds(tile * cast_rows, cast_rows)
        return pltpu.make_async_copy(
            wide_units_ref.at[rows], cast_in.at[tile % 2], cast_sem.at[0, tile % 2]
        )

    def cast_store(tile):
        rows = pl.ds(tile * cast_rows, cast_rows)
        return pltpu.make_async_copy(
            cast_out.at[tile % 2], own_units_ref.at[rows], cast_sem.at[1, tile % 2]
        )

    def cast(first, last):
        for tile in range(first, last):
            cast_load(tile).wait()
            if tile >= 2:
                cast_store(tile - 2).wait()
            cast_out[tile % 2] = cast_in[tile % 2].astype(bfloat)
            cast_store(tile).start()
            if tile + 2 < casts:
                cast_load(tile + 2).start()

    cast_load(0).start()
    cast_load(1).start()
    all_rows[chip] = own_ref[...].astype(bfloat)
    value[0] = gains_ref[...].astype(bfloat).astype(single)
    wide_barrier(to_side, to_core, around)
    gains_total = Total(value, near, blocks, total_send, total_recv, peers, chip)
    gains_total.start()
    streams = [(way, slot) for slot in range(2) for way in range(2)]
    out_streams = [(way, 2) for way in range(2)]
    key_streams = [(way, kind) for kind in range(2) for way in range(2)]

    def owner_of(way, step):
        return chip_of((ring + (chips - step if way == 0 else step)) % chips, chips)

    def hop(way, slot, step):
        there = all_rows.at[owner_of(way, step), slot, :, pl.ds(way * half, half)]
        return remote(
            there,
            there,
            send_sem.at[way, slot, step],
            recv_sem.at[way, slot, step],
            {"fsdp": right if way == 0 else left},
        )

    def key_hop(way, kind, step):
        there = keyval_ref.at[owner_of(way, step), kind, pl.ds(way * (tokens // 2), tokens // 2)]
        return remote(
            there,
            there,
            key_send.at[way, kind, step],
            key_recv.at[way, kind, step],
            {"fsdp": right if way == 0 else left},
        )

    def goal(way, slot, step):
        owner = owner_of(way, step)
        deep = owner // pairs
        unit = (owner % pairs) * 2 + core
        taker, head = (deep % 2, deep // 2) if slot == 1 else (deep // 2, deep % 2)
        columns = pl.ds(way * half, half)
        source = all_rows.at[owner, slot, :, columns]
        start = pl.multiple_of(head * HD + unit * share, share)
        target = rows_ref.at[slot, pl.ds(start, share), columns]
        sem = place_sem.at[way, slot, step]

        def here():
            return pltpu.make_async_copy(source, target, sem)

        def there():
            return remote(source, target, sem, peer_sem.at[way, slot, step], to_core)

        return taker, here, there

    def place(way, slot, step):
        taker, here, there = goal(way, slot, step)

        @pl.when(taker == core)
        def _():
            here().start()

        @pl.when(taker != core)
        def _():
            there().start()

    def placed(way, slot, step):
        taker, here, there = goal(way, slot, step)

        @pl.when(taker == core)
        def _():
            here().wait()
            there().wait_recv()

        @pl.when(taker != core)
        def _():
            there().wait_send()

    def pass_on(which, step):
        for way, slot in which:

            @pl.when(step > 0)
            def _():
                hop(way, slot, step - 1).wait_recv()

            @pl.when(step < chips - 1)
            def _():
                hop(way, slot, step).start()

            place(way, slot, step)

    def settle(which):
        def body(step, carried):
            for way, slot in which:
                placed(way, slot, step)

                @pl.when(step < chips - 1)
                def _():
                    hop(way, slot, step).wait_send()

            return carried

        lax.fori_loop(0, chips, body, 0)

    for way, slot in streams:
        hop(way, slot, 0).start()
    cast(0, 2)
    gains_total.over_cores()
    for way, slot in streams:
        place(way, slot, 0)
    cast(2, 4)
    gains_total.over_ring()
    cast(4, casts)
    scales_ref[...] = gains_total.end()
    normed_ref[core, side] = norm_scale(resid_ref[...], scales_ref[0:1]).astype(bfloat)

    def quad_copy(source, target, index, device):
        return remote(source, target, quad_send.at[index], quad_recv.at[index], device)

    mine = normed_ref.at[core, side]
    along = quad_copy(mine, mine, 0, to_side)
    across = quad_copy(normed_ref.at[core], normed_ref.at[core], 1, to_core)
    along.start()
    cast_store(casts - 2).wait()
    cast_store(casts - 1).wait()
    bulk_rows = (
        pl.ds(0, first_units),
        pl.ds(first_units, wide_units_ref.shape[0] - first_units),
    )

    def bulk_side(part):
        return remote(
            own_units_ref.at[bulk_rows[part]],
            side_units_ref.at[bulk_rows[part]],
            bulk_send.at[part],
            bulk_recv.at[part],
            to_side,
        )

    def bulk_diag(part):
        return remote(
            side_units_ref.at[bulk_rows[part]],
            diag_units_ref.at[bulk_rows[part]],
            bulk_send.at[2 + part],
            bulk_recv.at[2 + part],
            to_core,
        )

    bulk_core = remote(own_units_ref, core_units_ref, bulk_send.at[4], bulk_recv.at[4], to_core)

    def body(step, carried):
        pass_on(streams, step)

        @pl.when(step == 2)
        def _():
            along.wait()
            across.start()
            bulk_side(0).start()

        return carried

    lax.fori_loop(1, chips, body, 0)
    pass_on(out_streams, 0)
    across.wait()
    settle(streams)
    bulk_core.start()

    def project(slot, head):
        rows = slice(head * HD, head * HD + HD)
        return dot_nt(normed_ref[...].reshape(tokens, width), rows_ref[slot, rows])

    for head in range(2):
        raw = project(1, head)
        both[head] = turn(raw, key_cosine_ref[...], key_sine_ref[...]).astype(bfloat)
    swap = quad_copy(both.at[1 - side], keyval_ref.at[chip, side], 2, to_side)
    bulk_side(0).wait_recv()
    swap.start()
    bulk_side(1).start()
    bulk_diag(0).start()
    pass_on(out_streams, 1)
    keyval_ref[chip, side] = both[side]
    for head in range(2):
        raw = project(0, head)
        query_ref[head] = turn(raw, cosine_ref[...], sine_ref[...]).astype(bfloat)
        pass_on(out_streams, 2 + head)
    total[...] = jnp.zeros_like(total)
    sums[...] = jnp.zeros_like(sums)
    swap.wait()

    def block(way, owner):
        part = tokens // 2
        key = keyval_ref[owner, 0, way * part : way * part + part]
        val = keyval_ref[owner, 1, way * part : way * part + part]
        row = lax.broadcasted_iota(jnp.int32, (tokens, part), 0)
        column = lax.broadcasted_iota(jnp.int32, (tokens, part), 1)
        allowed = row + (chip - owner) * tokens - way * part >= column

        def one_head(head, carried):
            bent = jnp.tanh(dot_nt(query_ref[head], key) * (scale / softcap))
            powers = jnp.where(allowed, jnp.exp(softcap * bent), 0.0)
            sums[head] += powers[:, : part // 2] + powers[:, part // 2 :]
            total[head] += dot_nn(powers.astype(bfloat), val)
            return carried

        lax.fori_loop(0, 2, one_head, 0)

    def key_body(step, carried):
        for way, kind in key_streams:

            @pl.when(step > 0)
            def _():
                key_hop(way, kind, step - 1).wait_recv()

            @pl.when(step < chips - 1)
            def _():
                key_hop(way, kind, step).start()

        @pl.when(step < chips - 4)
        def _():
            pass_on(out_streams, step + 4)

        for way in range(2):
            owner = owner_of(way, step)

            @pl.when(owner <= chip)
            def _():
                block(way, owner)

        return carried

    lax.fori_loop(0, chips, key_body, 0)
    bulk_side(1).wait_recv()
    bulk_diag(1).start()
    settle(out_streams)
    for head in range(2):
        inverse = 1.0 / jnp.sum(sums[head], axis=-1, keepdims=True)
        inverse_ref[head] = jnp.broadcast_to(inverse, inverse_ref.shape[1:])
        attended_ref[:, head * HD : head * HD + HD] = (total[head] * inverse).astype(bfloat)
    span = width // 3
    tiles = [slice(tile * span, tile * span + span) for tile in range(3)]

    def project_out(part, ref, columns):
        first = pl.ds(pl.multiple_of(part * 2 * tok_rows, 2 * tok_rows), 2 * tok_rows)
        made = dot_nn(attended_ref[first], rows_ref[2, :, columns])
        ref[:, :, columns] = made.reshape(2, tok_rows, span).astype(ref.dtype)

    across = [
        quad_copy(across_put.at[:, :, columns], across_got.at[:, :, columns], 3 + tile, to_core)
        for tile, columns in enumerate(tiles)
    ]
    along = [
        quad_copy(along_put.at[:, columns], along_got.at[:, columns], 6 + tile, to_side)
        for tile, columns in enumerate(tiles)
    ]
    for tile, columns in enumerate(tiles):
        project_out(1 - core, across_put, columns)
        across[tile].start()
        project_out(core, product, columns)
    for tile, columns in enumerate(tiles):
        across[tile].wait()
        given = product[1 - side, :, columns] + across_got[1 - side, :, columns].astype(single)
        along_put[:, columns] = given.astype(bfloat)
        along[tile].start()

    def key_settle(step, carried):
        for way, kind in key_streams:
            key_hop(way, kind, step).wait_send()
        return carried

    lax.fori_loop(0, chips - 1, key_settle, 0)
    bulk_side(0).wait_send()
    bulk_side(1).wait_send()
    bulk_core.wait()
    bulk_diag(0).wait()
    bulk_diag(1).wait()
    for tile, columns in enumerate(tiles):
        along[tile].wait()
        kept = product[side, :, columns] + across_got[side, :, columns].astype(single)
        projected_ref[:, columns] = kept + along_got[:, columns].astype(single)


def cost(micros):
    return pl.CostEstimate(flops=int(micros * 1e9), bytes_accessed=0, transcendentals=0)


def front(attn_weight, gains, resid_in, turns, ffn_wide, chips, ident):
    share, width = attn_weight.shape[1:]
    tok_rows = resid_in.shape[0]
    tokens = 4 * tok_rows
    units = ffn_wide.shape[0]
    vmem = pl.BlockSpec(memory_space=pltpu.VMEM)
    anywhere = pl.BlockSpec(memory_space=pl.ANY)
    return pl.pallas_call(
        functools.partial(front_kernel, chips, 304),
        out_shape=(
            jax.ShapeDtypeStruct((3, 2 * HD, width), bfloat),
            jax.ShapeDtypeStruct((4, width), single),
            jax.ShapeDtypeStruct((2, 2, tok_rows, width), bfloat),
            jax.ShapeDtypeStruct((2, tokens, HD), bfloat),
            jax.ShapeDtypeStruct((chips, 2, tokens, HD), bfloat),
            jax.ShapeDtypeStruct((tokens, 2 * HD), bfloat),
            jax.ShapeDtypeStruct((2, tokens, 128), single),
            jax.ShapeDtypeStruct((tok_rows, width), single),
        )
        + (jax.ShapeDtypeStruct((units, width), bfloat),) * 4,
        in_specs=[vmem] * 7 + [anywhere],
        out_specs=(vmem,) * 8 + (anywhere,) * 4,
        scratch_shapes=[
            pltpu.VMEM((chips, 3, share, width), bfloat),
            pltpu.VMEM((2, tokens, HD), bfloat),
            pltpu.VMEM((2, tokens, HD), single),
            pltpu.VMEM((2, tokens, 128), single),
            pltpu.VMEM((2, tok_rows, width), single),
            pltpu.VMEM((2, tok_rows, width), bfloat),
            pltpu.VMEM((2, tok_rows, width), bfloat),
            pltpu.VMEM((tok_rows, width), bfloat),
            pltpu.VMEM((tok_rows, width), bfloat),
            pltpu.VMEM((2, units // 9, width), single),
            pltpu.VMEM((2, units // 9, width), bfloat),
        ]
        + total_scratch(chips, width)
        + [
            pltpu.SemaphoreType.DMA((2, 3, chips - 1)),
            pltpu.SemaphoreType.DMA((2, 3, chips - 1)),
            pltpu.SemaphoreType.DMA((2, 3, chips)),
            pltpu.SemaphoreType.DMA((2, 3, chips)),
            pltpu.SemaphoreType.DMA((2, 2, chips - 1)),
            pltpu.SemaphoreType.DMA((2, 2, chips - 1)),
            pltpu.SemaphoreType.DMA((9,)),
            pltpu.SemaphoreType.DMA((9,)),
            pltpu.SemaphoreType.DMA((2, 2)),
            pltpu.SemaphoreType.DMA((5,)),
            pltpu.SemaphoreType.DMA((5,)),
        ],
        compiler_params=pltpu.CompilerParams(
            collective_id=ident, has_side_effects=True, vmem_limit_bytes=60 * 2**20
        ),
        cost_estimate=cost(140),
    )(attn_weight, gains, resid_in, *turns, ffn_wide)


def tail_kernel(
    chips,
    d_proj_ref,
    query_ref,
    keyval_ref,
    attended_ref,
    inverse_ref,
    rows_ref,
    normed_ref,
    cosine_ref,
    sine_ref,
    key_cosine_ref,
    key_sine_ref,
    resid_ref,
    d_mid_ref,
    scales_ref,
    gains_ref,
    units_own_ref,
    units_other_ref,
    sum_ref,
    tokens_ref,
    total_ref,
    units_ref,
    units_got_ref,
    d_all,
    d_out,
    delta,
    d_query,
    d_block,
    first_put,
    held_keys,
    swapped,
    d_raw,
    out_rows,
    parts,
    out_parts,
    held,
    out_held,
    across_got,
    along_put,
    along_got,
    value,
    near,
    blocks,
    total_send,
    total_recv,
    key_send,
    key_recv,
    place_sem,
    peer_sem,
    send_sem,
    recv_sem,
    out_send,
    out_recv,
    quad_send,
    quad_recv,
    load_sem,
    bulk_send,
    bulk_recv,
):
    tokens = query_ref.shape[1]
    half = tokens // 2
    width = resid_ref.shape[1]
    share = out_parts.shape[1]
    pairs = chips // 4
    scale = 1.0 / math.sqrt(HD)
    peers = quad_peers(chips)
    side, core, to_side, to_core, around = peers
    ring = Ring(chips, 2, 2 * share, send_sem, recv_sem)
    out_ring = Ring(chips, 1, share, out_send, out_recv)
    chip = ring.chip
    gains_total = Total(value, near, blocks, total_send, total_recv, peers, chip)
    d_all[core, side] = d_proj_ref[...]
    wide_barrier(to_side, to_core, around)

    def quad_copy(source, target, index, device):
        return remote(source, target, quad_send.at[index], quad_recv.at[index], device)

    def bulk(kind):
        return remote(
            units_ref.at[pl.ds(kind * (units_ref.shape[0] // 3), units_ref.shape[0] // 3)],
            units_got_ref.at[pl.ds(kind * (units_ref.shape[0] // 3), units_ref.shape[0] // 3)],
            bulk_send.at[kind],
            bulk_recv.at[kind],
            to_side,
        )

    units = units_ref.shape[0]
    ours = out_rows.reshape(6 * HD, width).at[pl.ds(0, units)]
    theirs = parts.reshape(2 * chips * share, width).at[pl.ds(0, units)]
    loads = (
        pltpu.make_async_copy(units_own_ref.at[1], ours, load_sem.at[0]),
        pltpu.make_async_copy(units_other_ref.at[1], theirs, load_sem.at[1]),
    )
    store = pltpu.make_async_copy(ours, units_ref, load_sem.at[2])
    for load in loads:
        load.start()
    quarter = tokens // 8
    halves = [slice(part * quarter, part * quarter + quarter) for part in range(2)]
    along = [
        quad_copy(d_all.at[core, side, rows], d_all.at[core, side, rows], part, to_side)
        for part, rows in enumerate(halves)
    ]
    across = quad_copy(d_all.at[core, side], d_all.at[core, side], 2, to_core)
    relay = [
        quad_copy(d_all.at[core, 1 - side, rows], d_all.at[core, 1 - side, rows], 3 + part, to_core)
        for part, rows in enumerate(halves)
    ]
    for part in range(2):
        along[part].start()
    across.start()
    d_query[...] = jnp.zeros_like(d_query)
    for load in loads:
        load.wait()
    for kind in range(3):
        rows = slice(kind * units // 3, (kind + 1) * units // 3)
        ours[rows] = (ours[rows].astype(single) + theirs[rows].astype(single)).astype(bfloat)
    store.start()
    for part in range(2):
        along[part].wait()
        relay[part].start()
    store.wait()
    bulk(0).start()
    bulk(1).start()
    across.wait()
    for part in range(2):
        relay[part].wait()
    d_rows = d_all[...].reshape(tokens, width)
    for head in range(2):
        columns = slice(head * HD, head * HD + HD)
        made = dot_nt(d_rows, rows_ref[2, columns]).astype(bfloat)
        d_out[head] = made
        row_dot = jnp.sum(
            made.astype(single) * attended_ref[:, columns].astype(single), axis=-1, keepdims=True
        )
        delta[head] = jnp.broadcast_to(row_dot, delta.shape[1:])

    def place(slot, head, start):
        deep = 2 * head + core if slot == 1 else 2 * core + head
        for unit in range(4):
            source = out_rows.at[slot, head, pl.ds(unit * share, share)]
            owner = deep * pairs + unit // 2
            target = out_parts.at[owner] if slot == 2 else parts.at[owner, slot]
            sem = place_sem.at[slot, head, unit]

            def here():
                return pltpu.make_async_copy(source, target, sem)

            def there():
                return remote(source, target, sem, peer_sem.at[slot, head, unit], to_core)

            @pl.when(core == unit % 2)
            def _():
                if start:
                    here().start()
                else:
                    here().wait()
                    there().wait_recv()

            @pl.when(core != unit % 2)
            def _():
                if start:
                    there().start()
                else:
                    there().wait_send()

    def term(slot, head, left, right):
        out_rows[slot, head] = dot_tn(left, right).astype(bfloat)
        place(slot, head, True)

    for head in range(2):
        term(2, head, attended_ref[:, head * HD : head * HD + HD], d_all[...].reshape(tokens, width))
    def block(way, owner):
        key = keyval_ref[owner, 0, way * half : way * half + half]
        val = keyval_ref[owner, 1, way * half : way * half + half]
        row = lax.broadcasted_iota(jnp.int32, (tokens, half), 0)
        column = lax.broadcasted_iota(jnp.int32, (tokens, half), 1)
        allowed = row + (chip - owner) * tokens - way * half >= column

        def one_head(head, carried):
            bent = jnp.tanh(dot_nt(query_ref[head], key) * (scale / softcap))
            inverse = jnp.concatenate([inverse_ref[head]] * (half // 128), axis=1)
            row_dot = jnp.concatenate([delta[head]] * (half // 128), axis=1)
            probs = jnp.where(allowed, jnp.exp(softcap * bent), 0.0) * inverse
            d_probs = dot_nt(d_out[head], val)
            d_scores = (probs * (d_probs - row_dot) * (1.0 - bent * bent)).astype(bfloat)
            d_block[way, 0] += dot_tn(d_scores, query_ref[head]) * scale
            d_block[way, 1] += dot_tn(probs.astype(bfloat), d_out[head])
            d_query[head] += dot_nn(d_scores, key)
            return carried

        lax.fori_loop(0, 2, one_head, 0)

    def key_copy(way, kind, step, first):
        return remote(
            first_put.at[way, kind] if first else held_keys.at[way, step - 1, kind],
            held_keys.at[way, step, kind],
            key_send.at[way, kind, step],
            key_recv.at[way, kind, step],
            {"fsdp": ring.right if way == 0 else ring.left},
        )

    streams = [(way, kind) for kind in range(2) for way in range(2)]

    def key_blocks(step):
        for way in range(2):
            owner = ring.owner(way, step + 1)
            d_block[way] = jnp.zeros(d_block.shape[1:], single)

            @pl.when(owner <= chip)
            def _():
                block(way, owner)

    def key_body(step, carried):
        key_blocks(step)
        for way, kind in streams:

            @pl.when(step == 0)
            def _():
                first_put[way, kind] = d_block[way, kind].astype(bfloat)
                key_copy(way, kind, 0, True).start()

            @pl.when(step > 0)
            def _():
                key_copy(way, kind, step - 1, True).wait_recv()
                summed = held_keys[way, step - 1, kind].astype(single) + d_block[way, kind]
                held_keys[way, step - 1, kind] = summed.astype(bfloat)
                key_copy(way, kind, step, False).start()

        @pl.when(step == 0)
        def _():
            for head in range(2):
                place(2, head, False)

        out_ring.scatter_step(out_parts, out_held, step)
        return carried

    lax.fori_loop(0, chips - 1, key_body, 0)

    normed = normed_ref[...].reshape(tokens, width)
    key_blocks(chips - 1)
    for way in range(2):
        rows = slice(way * half, way * half + half)
        for kind in range(2):
            key_copy(way, kind, chips - 2, True).wait_recv()
            summed = held_keys[way, chips - 2, kind].astype(single) + d_block[way, kind]
            swapped[2 + kind, rows] = summed.astype(bfloat)
    swap = quad_copy(swapped.at[3 - side], swapped.at[side], 5, to_side)
    swap.start()
    for head in range(2):
        turned = turn(d_query[head] * scale, cosine_ref[...], -sine_ref[...])
        d_raw[head] = turned.astype(bfloat)
        term(0, head, d_raw[head], normed)
    swap.wait()
    bulk(2).start()
    swapped[side] = swapped[2 + side]
    for head in range(2):
        turned = turn(swapped[head].astype(single), key_cosine_ref[...], -key_sine_ref[...])
        d_raw[2 + head] = turned.astype(bfloat)
        term(1, head, d_raw[2 + head], normed)
    span = width // 3

    def d_input(tile, carried):
        columns = pl.ds(pl.multiple_of(tile * span, span), span)
        made = dot_nn(d_raw[0], rows_ref[0, 0:HD, columns])
        made = made + dot_nn(d_raw[1], rows_ref[0, HD:, columns])
        made = made + dot_nn(d_raw[2], rows_ref[1, 0:HD, columns])
        made = made + dot_nn(d_raw[3], rows_ref[1, HD:, columns])
        out_rows[0, :, :, columns] = made.reshape(2, half, span).astype(bfloat)
        return carried

    for slot in range(2):
        for head in range(2):
            place(slot, head, False)
    blocks_ref = parts.reshape(chips, 2 * share, width)
    ring.scatter_step(blocks_ref, held, 0)
    lax.fori_loop(0, 3, d_input, 0)
    across = quad_copy(out_rows.at[0, 1 - core], across_got, 6, to_core)
    mine = pl.ds(pl.multiple_of(side * (half // 2), half // 2), half // 2)
    other = pl.ds(pl.multiple_of((1 - side) * (half // 2), half // 2), half // 2)
    along = quad_copy(along_put, along_got, 7, to_side)
    across.start()

    def body(step, carried):
        ring.scatter_step(blocks_ref, held, step)

        @pl.when(step == 1)
        def _():
            across.wait()
            given = out_rows[0, core, other].astype(single) + across_got[other].astype(single)
            along_put[...] = given.astype(bfloat)
            along.start()
            tokens_ref[...] = out_rows[0, core, mine].astype(single) + across_got[mine].astype(single)

        @pl.when(step == 4)
        def _():
            along.wait()
            tokens_ref[...] = tokens_ref[...] + along_got[...].astype(single)
            d_norm, d_gain = norm_back(resid_ref[...], scales_ref[0:1], tokens_ref[...])
            tokens_ref[...] = d_mid_ref[...] + d_norm
            value[0] = gains_ref[...]
            value[0, 0:1] = d_gain
            gains_total.start()

        @pl.when(step == 5)
        def _():
            gains_total.over_cores()

        @pl.when(step == 6)
        def _():
            gains_total.over_ring()

        return carried

    lax.fori_loop(1, chips - 1, body, 0)
    total_ref[...] = gains_total.end()
    out_ring.scatter_end(out_parts, out_held, sum_ref.at[pl.ds(2 * share, share)])
    ring.scatter_end(blocks_ref, held, sum_ref.at[pl.ds(0, 2 * share)])
    ring.finish(held.at[0, 0, 0 : ring.size])
    out_ring.finish(out_held.at[0, 0, 0 : out_ring.size])

    def settle(step, carried):
        for way, kind in streams:
            key_copy(way, kind, step, True).wait_send()
        return carried

    lax.fori_loop(0, chips - 1, settle, 0)
    for kind in range(3):
        bulk(kind).wait()


def tail(
    d_proj, query, keyval, attended, inverse, rows, normed, turns, locals_, own, other, chips, ident
):
    tokens = query.shape[1]
    tok_rows = tokens // 4
    width = rows.shape[2]
    share = tokens // 8
    half = tokens // 2
    vmem = pl.BlockSpec(memory_space=pltpu.VMEM)
    anywhere = pl.BlockSpec(memory_space=pl.ANY)
    return pl.pallas_call(
        functools.partial(tail_kernel, chips),
        out_shape=(
            jax.ShapeDtypeStruct((3 * share, width), single),
            jax.ShapeDtypeStruct((tok_rows, width), single),
            jax.ShapeDtypeStruct((4, width), single),
            jax.ShapeDtypeStruct(own.shape[1:], bfloat),
            jax.ShapeDtypeStruct(own.shape[1:], bfloat),
        ),
        in_specs=[vmem] * 15 + [anywhere] * 2,
        out_specs=(vmem,) * 3 + (anywhere,) * 2,
        scratch_shapes=[
            pltpu.VMEM((2, 2, tok_rows, width), bfloat),
            pltpu.VMEM((2, tokens, HD), bfloat),
            pltpu.VMEM((2, tokens, 128), single),
            pltpu.VMEM((2, tokens, HD), single),
            pltpu.VMEM((2, 2, half, HD), single),
            pltpu.VMEM((2, 2, half, HD), bfloat),
            pltpu.VMEM((2, chips - 1, 2, half, HD), bfloat),
            pltpu.VMEM((4, tokens, HD), bfloat),
            pltpu.VMEM((4, tokens, HD), bfloat),
            pltpu.VMEM((3, 2, HD, width), bfloat),
            pltpu.VMEM((chips, 2, share, width), bfloat),
            pltpu.VMEM((chips, share, width), bfloat),
            pltpu.VMEM((2, chips - 1, share, width), bfloat),
            pltpu.VMEM((2, chips - 1, share // 2, width), bfloat),
            pltpu.VMEM((2 * tok_rows, width), bfloat),
            pltpu.VMEM((tok_rows, width), bfloat),
            pltpu.VMEM((tok_rows, width), bfloat),
        ]
        + total_scratch(chips, width)
        + [
            pltpu.SemaphoreType.DMA((2, 2, chips - 1)),
            pltpu.SemaphoreType.DMA((2, 2, chips - 1)),
            pltpu.SemaphoreType.DMA((3, 2, 4)),
            pltpu.SemaphoreType.DMA((3, 2, 4)),
            pltpu.SemaphoreType.DMA((2, 2, chips - 1)),
            pltpu.SemaphoreType.DMA((2, 2, chips - 1)),
            pltpu.SemaphoreType.DMA((2, 1, chips - 1)),
            pltpu.SemaphoreType.DMA((2, 1, chips - 1)),
            pltpu.SemaphoreType.DMA((8,)),
            pltpu.SemaphoreType.DMA((8,)),
            pltpu.SemaphoreType.DMA((3,)),
            pltpu.SemaphoreType.DMA((3,)),
            pltpu.SemaphoreType.DMA((3,)),
        ],
        compiler_params=pltpu.CompilerParams(
            collective_id=ident, has_side_effects=True, vmem_limit_bytes=63 * 2**20
        ),
        cost_estimate=cost(160),
    )(d_proj, query, keyval, attended, inverse, rows, normed, *turns, *locals_, own, other)


def feed_kernel(
    chips,
    pieces,
    resid_ref,
    projected_ref,
    dy_ref,
    scales_ref,
    own_ref,
    side_ref,
    core_ref,
    diag_ref,
    result_ref,
    d_mid_ref,
    d_projected_ref,
    d_gains_ref,
    terms_ref,
    other_ref,
    weights,
    x_all,
    y_all,
    mid,
    both,
    hidden,
    part,
    held_one,
    held_two,
    chunk,
    wide,
    stage,
    load_sem,
    stage_sem,
    other_sem,
    send_sem,
    recv_sem,
):
    tok_rows, width = resid_ref.shape
    units = own_ref.shape[0] // 3
    whole = 4 * units
    half = tok_rows // 2
    rings = [
        Ring(chips, pieces, tok_rows, send_sem.at[phase], recv_sem.at[phase]) for phase in range(4)
    ]
    chip = rings[0].chip
    loads = []
    for slot, ref in enumerate((own_ref, side_ref, core_ref, diag_ref)):
        for kind in range(3):
            loads.append(
                pltpu.make_async_copy(
                    ref.at[pl.ds(kind * units, units)],
                    weights.at[pl.ds(kind * whole + slot * units, units)],
                    load_sem.at[slot, kind],
                )
            )
    for load in loads:
        load.start()
    mid[...] = resid_ref[...] + norm_scale(projected_ref[...], scales_ref[1:2])
    x_all[chip] = norm_scale(mid[...], scales_ref[2:3]).astype(bfloat)
    core = lax.axis_index("fsdp") % 2
    to_core = {"fsdp": 2 * chip + 1 - core}
    barrier = pltpu.get_barrier_semaphore()
    for target in ({"fsdp": rings[0].right}, {"fsdp": rings[0].left}, to_core):
        pl.semaphore_signal(barrier, inc=1, device_id=target, device_id_type=MESH)
    pl.semaphore_wait(barrier, 3)
    span = width // 3

    def fetch(all_ref, step):
        chunk[0:half] = all_ref[rings[0].owner(0, step), 0:half]
        chunk[half:] = all_ref[rings[0].owner(1, step), half:]

    def put(ref, step, columns, value):
        ref[rings[0].owner(0, step), 0:half, columns] = value[0:half].astype(ref.dtype)
        ref[rings[0].owner(1, step), half:, columns] = value[half:].astype(ref.dtype)

    def take(ref, step, columns):
        return jnp.concatenate(
            [
                ref[rings[0].owner(0, step), 0:half, columns],
                ref[rings[0].owner(1, step), half:, columns],
            ],
            axis=0,
        )

    def forward(step, carried):
        rings[0].gather_step(x_all, step)

        @pl.when(step == 0)
        def _():
            for load in loads:
                load.wait()

        fetch(x_all, step)

        def gate_up(tile, carried):
            rows = pl.ds(pl.multiple_of(tile * span, span), span)
            wide[:, rows] = dot_nt(chunk[...], weights[rows])
            return carried

        lax.fori_loop(0, 3, gate_up, 0)
        put(both, step, slice(None), wide[...])
        gate = wide[:, 0:whole]
        value, slope = gelu_parts(gate)
        unit = (value * wide[:, whole:]).astype(bfloat)
        put(hidden, step, slice(None), unit)

        def down(tile, carried):
            columns = pl.ds(pl.multiple_of(tile * span, span), span)
            product = dot_nn(take(hidden, step, slice(None)), weights[2 * whole :, columns])
            put(part, step, columns, product)
            return carried

        lax.fori_loop(0, 3, down, 0)
        return carried

    lax.fori_loop(0, chips, forward, 0)

    def spread(step, carried):
        rings[1].scatter_step(part, held_one, step)
        return carried

    lax.fori_loop(0, chips - 1, spread, 0)
    rings[1].scatter_end(part, held_one, wide)
    result_ref[...] = mid[...] + norm_scale(wide[...], scales_ref[3:4])
    d_ffn, d_gain = norm_back(wide[...], scales_ref[3:4], dy_ref[...])
    d_gains_ref[0:1] = jnp.zeros_like(d_gain)
    d_gains_ref[3:4] = d_gain
    y_all[chip] = d_ffn.astype(bfloat)
    rings[0].finish(x_all.at[0, 0 : rings[0].size])
    rings[1].finish(x_all.at[0, 0 : rings[0].size])

    def backward(step, carried):
        rings[2].gather_step(y_all, step)
        fetch(y_all, step)
        third = whole // 3

        def d_units(tile, carried):
            columns = pl.ds(pl.multiple_of(tile * third, third), third)
            rows = pl.ds(pl.multiple_of(2 * whole + tile * third, third), third)
            ups = pl.ds(pl.multiple_of(whole + tile * third, third), third)
            d_hidden = dot_nt(chunk[...], weights[rows])
            gate = take(both, step, columns).astype(single)
            upper = take(both, step, ups).astype(single)
            value, slope = gelu_parts(gate)
            put(both, step, columns, d_hidden * upper * slope)
            put(both, step, ups, d_hidden * value)
            return carried

        lax.fori_loop(0, 3, d_units, 0)

        def d_input(tile, carried):
            columns = pl.ds(pl.multiple_of(tile * span, span), span)
            product = dot_nn(take(both, step, slice(None)), weights[0 : 2 * whole, columns])
            put(part, step, columns, product)
            return carried

        lax.fori_loop(0, 3, d_input, 0)
        return carried

    lax.fori_loop(0, chips, backward, 0)
    rows_tile = stage.shape[1]
    tiles = 3 * whole // rows_tile
    upper_tiles = 2 * whole // rows_tile

    cut = units // 3

    def pieces_of(tile):
        for quarter in range(4):
            block = 4 * tile + quarter
            kind, slot, third = block // 12, (block // 3) % 4, block % 3
            source = stage.at[tile % 2, pl.ds(quarter * cut, cut)]
            rows = pl.ds(pl.multiple_of(kind * units + third * cut, cut), cut)
            sem = stage_sem.at[tile % 2, quarter]
            goal = terms_ref.at[slot, rows], other_ref.at[slot - 2, rows]
            there = functools.partial(
                remote, source, goal[1], sem, other_sem.at[tile, quarter], to_core
            )
            yield slot, functools.partial(pltpu.make_async_copy, source, goal[0], sem), there

    def keep(tile):
        for slot, here, there in pieces_of(tile):

            @pl.when(slot < 2)
            def _():
                here().start()

            @pl.when(slot >= 2)
            def _():
                there().start()

    def kept(tile):
        for slot, here, there in pieces_of(tile):

            @pl.when(slot < 2)
            def _():
                here().wait()

            @pl.when(slot >= 2)
            def _():
                there().wait_send()

    def grads(tile):
        @pl.when(tile >= 2)
        def _():
            kept(tile - 2)

        @pl.when(tile < upper_tiles)
        def _():
            columns = pl.ds(pl.multiple_of(tile * rows_tile, rows_tile), rows_tile)
            left = both[:, :, columns].reshape(chips * tok_rows, rows_tile)
            stage[tile % 2] = dot_tn(left, x_all[...].reshape(chips * tok_rows, width)).astype(bfloat)

        @pl.when(tile >= upper_tiles)
        def _():
            columns = pl.ds(
                pl.multiple_of((tile - upper_tiles) * rows_tile, rows_tile), rows_tile
            )
            left = hidden[:, :, columns].reshape(chips * tok_rows, rows_tile)
            stage[tile % 2] = dot_tn(left, y_all[...].reshape(chips * tok_rows, width)).astype(bfloat)

        keep(tile)

    def spread_back(step, carried):
        rings[3].scatter_step(part, held_two, step)
        grads(step)
        return carried

    lax.fori_loop(0, chips - 1, spread_back, 0)

    def rest(tile, carried):
        grads(tile)
        return carried

    lax.fori_loop(chips - 1, tiles, rest, 0)
    rings[3].scatter_end(part, held_two, wide)
    d_norm, d_gain = norm_back(mid[...], scales_ref[2:3], wide[...])
    d_gains_ref[2:3] = d_gain
    d_mid_ref[...] = dy_ref[...] + d_norm
    d_projected, d_gain = norm_back(projected_ref[...], scales_ref[1:2], d_mid_ref[...])
    d_gains_ref[1:2] = d_gain
    d_projected_ref[...] = d_projected.astype(bfloat)
    rings[2].finish(x_all.at[0, 0 : rings[0].size])
    rings[3].finish(x_all.at[0, 0 : rings[0].size])
    kept(tiles - 2)
    kept(tiles - 1)

    def gained(tile, carried):
        for slot, here, there in pieces_of(tile):

            @pl.when(slot >= 2)
            def _():
                there().wait_recv()

        return carried

    lax.fori_loop(0, tiles, gained, 0)


def feed_forward(resid_in, projected, grad_out, scales, shares, chips, ident):
    tok_rows, width = resid_in.shape
    units = shares[0].shape[0] // 3
    whole = 4 * units
    pieces = 2
    vmem = pl.BlockSpec(memory_space=pltpu.VMEM)
    anywhere = pl.BlockSpec(memory_space=pl.ANY)
    return pl.pallas_call(
        functools.partial(feed_kernel, chips, pieces),
        out_shape=(
            jax.ShapeDtypeStruct((tok_rows, width), single),
            jax.ShapeDtypeStruct((tok_rows, width), single),
            jax.ShapeDtypeStruct((tok_rows, width), bfloat),
            jax.ShapeDtypeStruct((4, width), single),
            jax.ShapeDtypeStruct((2, 3 * units, width), bfloat),
            jax.ShapeDtypeStruct((2, 3 * units, width), bfloat),
        ),
        in_specs=[vmem] * 4 + [anywhere] * 4,
        out_specs=(vmem, vmem, vmem, vmem, anywhere, anywhere),
        scratch_shapes=[
            pltpu.VMEM((3 * whole, width), bfloat),
            pltpu.VMEM((chips, tok_rows, width), bfloat),
            pltpu.VMEM((chips, tok_rows, width), bfloat),
            pltpu.VMEM((tok_rows, width), single),
            pltpu.VMEM((chips, tok_rows, 2 * whole), bfloat),
            pltpu.VMEM((chips, tok_rows, whole), bfloat),
            pltpu.VMEM((chips, tok_rows, width), bfloat),
            pltpu.VMEM((2, chips - 1, tok_rows // 2, width), bfloat),
            pltpu.VMEM((2, chips - 1, tok_rows // 2, width), bfloat),
            pltpu.VMEM((tok_rows, width), bfloat),
            pltpu.VMEM((tok_rows, width), single),
            pltpu.VMEM((2, whole // 3, width), bfloat),
            pltpu.SemaphoreType.DMA((4, 3)),
            pltpu.SemaphoreType.DMA((2, 4)),
            pltpu.SemaphoreType.DMA((9, 4)),
            pltpu.SemaphoreType.DMA((4, 2, pieces, chips - 1)),
            pltpu.SemaphoreType.DMA((4, 2, pieces, chips - 1)),
        ],
        compiler_params=pltpu.CompilerParams(
            collective_id=ident, has_side_effects=True, vmem_limit_bytes=63 * 2**20
        ),
        cost_estimate=cost(205),
    )(resid_in, projected, grad_out, scales, *shares)


def general_device(
    tokens,
    cotangent,
    gains,
    gains_first,
    gains_second,
    attn_weight,
    attn_first,
    attn_second,
    ffn_weight,
    ffn_first,
    ffn_second,
):
    devices = lax.axis_size("fsdp")
    chips = devices // 2
    side = lax.axis_index("head")
    place = lax.axis_index("fsdp")
    core, chip = place % 2, place // 2
    tok_rows = tokens.shape[1]
    super_rows = 4 * tok_rows
    seq_len = min(SEQ_LEN, super_rows * chips)
    share = attn_weight.shape[1]
    pairs = chips // 4
    width = tokens.shape[2]
    scale = 1.0 / math.sqrt(HD)

    def swap_core(value):
        return lax.ppermute(value, "fsdp", [(index, index ^ 1) for index in range(devices)])

    def swap_side(value):
        return lax.ppermute(value, "head", [(0, 1), (1, 0)])

    def in_order(own, other, index, axis):
        return jnp.where(
            index == 0, jnp.stack([own, other], axis), jnp.stack([other, own], axis)
        )

    def pick(value, index, axis=0):
        return lax.dynamic_index_in_dim(value, index, axis, keepdims=False)

    def quad_gather(value):
        value = in_order(value, swap_side(value), side, 0)
        value = in_order(value, swap_core(value), core, 0)
        return value.reshape((super_rows,) + value.shape[3:])

    def quad_scatter(partial):
        partial = partial.reshape(2, 2, tok_rows, width)
        mine = pick(partial, core) + swap_core(pick(partial, 1 - core).astype(bfloat)).astype(single)
        return pick(mine, side) + swap_side(pick(mine, 1 - side).astype(bfloat)).astype(single)

    scales = lax.all_gather(gains.astype(bfloat), ("head", "fsdp"), axis=1, tiled=True).astype(single)
    attn_low = attn_weight.astype(bfloat)
    ffn_low = ffn_weight.astype(bfloat).transpose(1, 0, 2)
    ffn_pair = jnp.concatenate([ffn_low, swap_side(ffn_low)], axis=1)

    ring_rows = ring_gather(attn_low.reshape(3 * share, width), chips, 0)
    ring_rows = ring_rows.reshape(2, 2, pairs, 3, share, width)

    def query_rows(slot):
        rows = ring_rows[:, :, :, slot]
        other = swap_core(pick(rows, 1 - core))
        return in_order(pick(rows, core), other, core, 2).reshape(2 * HD, width)

    def keyval_rows():
        rows = ring_rows[:, :, :, 1]
        other = swap_core(pick(rows, 1 - core, 1))
        return in_order(pick(rows, core, 1), other, core, 2).reshape(2 * HD, width)

    w_query, w_keyval, w_out = query_rows(0), keyval_rows(), query_rows(2)

    resid_in = tokens[0]
    grad_out = cotangent[0]
    normed_one = norm_scale(resid_in, scales[0]).astype(bfloat)
    normed_all = quad_gather(normed_one)
    positions = chip * super_rows + jnp.arange(super_rows, dtype=jnp.int32)
    angles = turn_angles(positions % seq_len, HD)
    query_raw = jnp.einsum("td,fd->tf", normed_all, w_query, preferred_element_type=single)
    keyval_raw = jnp.einsum("td,fd->tf", normed_all, w_keyval, preferred_element_type=single)
    query = rotate(query_raw.reshape(super_rows, 2, HD), angles, 1.0).astype(bfloat)
    key_angles = jnp.where(side == 0, angles, 0.0)
    keyval = rotate(keyval_raw.reshape(super_rows, 2, HD), key_angles, 1.0).astype(bfloat)
    keyval = in_order(pick(keyval, side, 1), swap_side(pick(keyval, 1 - side, 1)), side, 0)
    keyval_all = ring_gather(keyval.reshape(2 * super_rows, HD), chips, 1)
    keyval_all = keyval_all.reshape(chips, 2, super_rows, HD)
    key_all = keyval_all[:, 0].reshape(chips * super_rows, HD)
    value_all = keyval_all[:, 1].reshape(chips * super_rows, HD)

    key_pos = jnp.arange(chips * super_rows, dtype=jnp.int32)
    distance = positions[:, None] - key_pos[None, :]
    same_seq = (positions // seq_len)[:, None] == (key_pos // seq_len)[None, :]
    allowed = (distance >= 0) & (distance < WIN) & same_seq

    def score_block():
        raw = jnp.einsum("qgd,kd->gqk", query, key_all, preferred_element_type=single)
        bent = jnp.tanh(raw * (scale / softcap))
        return bent, jnp.where(allowed, jnp.exp(softcap * bent), 0.0)

    bent, powers = score_block()
    total = jnp.sum(powers, axis=-1, keepdims=True)
    attended = jnp.einsum(
        "gqk,kd->gqd", powers.astype(bfloat), value_all, preferred_element_type=single
    )
    attended = (attended / total).transpose(1, 0, 2).reshape(super_rows, 2 * HD).astype(bfloat)
    projected = quad_scatter(jnp.dot(attended, w_out, preferred_element_type=single))
    resid_mid = resid_in + norm_scale(projected, scales[1])
    normed_two = norm_scale(resid_mid, scales[2]).astype(bfloat)

    ffn_all = jnp.concatenate([ffn_pair, swap_core(ffn_pair)], axis=1)
    w_gate, w_up, w_down = ffn_all[0], ffn_all[1], ffn_all[2]
    ring_tokens = chips * tok_rows
    normed_ring = ring_gather(normed_two, chips, 2).reshape(ring_tokens, width)
    gate_part = jnp.einsum("td,rd->tr", normed_ring, w_gate, preferred_element_type=single)
    up_part = jnp.einsum("td,rd->tr", normed_ring, w_up, preferred_element_type=single)
    hidden = hidden_unit(gate_part, up_part).astype(bfloat)
    ffn_part = jnp.dot(hidden, w_down, preferred_element_type=single).astype(bfloat)
    ffn_acc = ring_scatter(ffn_part.reshape(chips, tok_rows, width), chips, 3)
    result = resid_mid + norm_scale(ffn_acc, scales[3])

    ignored, post_back = jax.vjp(norm_scale, ffn_acc, scales[3])
    d_ffn, d_gain3 = post_back(grad_out)
    d_ffn_ring = ring_gather(d_ffn.astype(bfloat), chips, 4).reshape(ring_tokens, width)
    d_hidden = jnp.einsum("td,rd->tr", d_ffn_ring, w_down, preferred_element_type=single)
    ignored, unit_back = jax.vjp(hidden_unit, gate_part, up_part)
    d_gate, d_up = unit_back(d_hidden)
    d_gate = d_gate.astype(bfloat)
    d_up = d_up.astype(bfloat)
    d_normed = jnp.dot(d_gate, w_gate, preferred_element_type=single)
    d_normed = (d_normed + jnp.dot(d_up, w_up, preferred_element_type=single)).astype(bfloat)
    d_normed_two = ring_scatter(d_normed.reshape(chips, tok_rows, width), chips, 5)

    def ffn_rows(left, right):
        return jnp.einsum("tr,td->rd", left, right, preferred_element_type=single)

    ffn_terms = jnp.stack(
        [ffn_rows(d_gate, normed_ring), ffn_rows(d_up, normed_ring), ffn_rows(hidden, d_ffn_ring)]
    )
    units = ffn_weight.shape[0]
    ffn_terms = ffn_terms.reshape(3, 2, 2, units, width)
    ffn_terms = ffn_terms[:, 0] + swap_core(ffn_terms[:, 1].astype(bfloat)).astype(single)
    grad_ffn = ffn_terms[:, 0] + swap_side(ffn_terms[:, 1].astype(bfloat)).astype(single)

    ignored, mid_back = jax.vjp(norm_scale, resid_mid, scales[2])
    d_mid_norm, d_gain2 = mid_back(d_normed_two)
    d_mid = grad_out + d_mid_norm
    ignored, proj_back = jax.vjp(norm_scale, projected, scales[1])
    d_projected, d_gain1 = proj_back(d_mid)
    d_proj_all = quad_gather(d_projected.astype(bfloat))
    d_attended = jnp.einsum("td,fd->tf", d_proj_all, w_out, preferred_element_type=single)
    d_attended = d_attended.astype(bfloat).reshape(super_rows, 2, HD)

    bent, powers = score_block()
    probs = powers / total
    d_probs = jnp.einsum("qgd,kd->gqk", d_attended, value_all, preferred_element_type=single)
    row_dot = jnp.sum(d_probs * probs, axis=-1, keepdims=True)
    d_raw = (probs * (d_probs - row_dot) * (1.0 - bent * bent)).astype(bfloat)
    d_query = jnp.einsum("gqk,kd->qgd", d_raw, key_all, preferred_element_type=single) * scale
    d_keys = jnp.einsum("gqk,qgd->kd", d_raw, query, preferred_element_type=single) * scale
    d_values = jnp.einsum(
        "gqk,qgd->kd", probs.astype(bfloat), d_attended, preferred_element_type=single
    )
    d_pieces = jnp.stack(
        [d_keys.reshape(chips, super_rows, HD), d_values.reshape(chips, super_rows, HD)], axis=1
    ).astype(bfloat)
    d_keyval = ring_scatter(d_pieces.reshape(chips, 2 * super_rows, HD), chips, 6)
    d_keyval = d_keyval.reshape(2, super_rows, HD).astype(bfloat)
    d_keyval = in_order(pick(d_keyval, side), swap_side(pick(d_keyval, 1 - side)), side, 1)
    d_query_raw = rotate(d_query, angles, -1.0).reshape(super_rows, 2 * HD).astype(bfloat)
    d_keyval_raw = rotate(d_keyval.astype(single), key_angles, -1.0)
    d_keyval_raw = d_keyval_raw.reshape(super_rows, 2 * HD).astype(bfloat)
    d_normed_one = jnp.dot(d_query_raw, w_query, preferred_element_type=single)
    d_normed_one = d_normed_one + jnp.dot(d_keyval_raw, w_keyval, preferred_element_type=single)
    d_normed_one = quad_scatter(d_normed_one)
    ignored, first_back = jax.vjp(norm_scale, resid_in, scales[0])
    d_in_norm, d_gain0 = first_back(d_normed_one)
    tokens_grad = d_mid + d_in_norm

    def attn_rows(left, right):
        rows = jnp.einsum("tf,td->fd", left, right, preferred_element_type=single).astype(bfloat)
        return rows.reshape(2, pairs, 2, share, width)

    term_query = attn_rows(d_query_raw, normed_all)
    term_keyval = attn_rows(d_keyval_raw, normed_all)
    term_out = attn_rows(attended, d_proj_all)

    def to_core(term, axis):
        return in_order(pick(term, core, 2), swap_core(pick(term, 1 - core, 2)), core, axis)

    terms = jnp.stack([to_core(term_query, 0), to_core(term_keyval, 1), to_core(term_out, 0)], axis=3)
    grad_attn = ring_scatter(terms.reshape(chips, 3 * share, width), chips, 7)
    grad_attn = grad_attn.reshape(3, share, width)
    term_gain = jnp.stack([d_gain0, d_gain1, d_gain2, d_gain3])
    grad_gain = lax.psum_scatter(term_gain, ("head", "fsdp"), scatter_dimension=1, tiled=True)

    gains_first_new, gains_second_new, gains_new = adamw(
        gains, gains_first, gains_second, grad_gain, rate_gain, 0.0
    )
    attn_first_new, attn_second_new, attn_weight_new = adamw(
        attn_weight, attn_first, attn_second, grad_attn, rate_matrix, decay_matrix
    )
    ffn_first_new, ffn_second_new, ffn_weight_new = adamw(
        ffn_weight, ffn_first, ffn_second, grad_ffn.transpose(1, 0, 2), rate_matrix, decay_matrix
    )
    return (
        result[None],
        tokens_grad[None],
        gains_first_new,
        gains_second_new,
        gains_new,
        attn_first_new,
        attn_second_new,
        attn_weight_new,
        ffn_first_new,
        ffn_second_new,
        ffn_weight_new,
    )


def per_device(
    tokens,
    cotangent,
    gains,
    gains_first,
    gains_second,
    attn_weight,
    attn_first,
    attn_second,
    ffn_weight,
    ffn_first,
    ffn_second,
):
    devices = lax.axis_size("fsdp")
    chips = devices // 2
    side = lax.axis_index("head")
    place = lax.axis_index("fsdp")
    chip = place // 2
    tok_rows = tokens.shape[1]
    super_rows = 4 * tok_rows
    seq_len = min(SEQ_LEN, super_rows * chips)
    share = attn_weight.shape[1]
    width = tokens.shape[2]
    gain_columns = gains.shape[1]
    gain_start = (side * devices + place) * gain_columns

    units = ffn_weight.shape[0]
    ffn_wide = ffn_weight.transpose(1, 0, 2).reshape(3 * units, width)
    resid_in = tokens[0]
    grad_out = cotangent[0]
    positions = chip * super_rows + jnp.arange(super_rows, dtype=jnp.int32)
    angles = turn_angles(positions % seq_len, HD)
    key_angles = jnp.where(side == 0, angles, 0.0)
    gains_placed = lax.dynamic_update_slice(
        jnp.zeros((4, width), single), gains, (0, gain_start)
    )
    turns = (jnp.cos(angles), jnp.sin(angles), jnp.cos(key_angles), jnp.sin(key_angles))
    made = front(attn_weight, gains_placed, resid_in, turns, ffn_wide, chips, 0)
    attn_rows, scales, normed_all, query, keyval, attended, inverse, projected = made[:8]
    own_units, core_units, side_units, diag_units = made[8:]
    result, d_mid, d_proj_low, gain_rows, terms_own, terms_other = feed_forward(
        resid_in,
        projected,
        grad_out,
        scales,
        (own_units, side_units, core_units, diag_units),
        chips,
        1,
    )
    grad_attn, tokens_grad, gain_total, terms_sent, terms_side = tail(
        d_proj_low,
        query,
        keyval,
        attended,
        inverse,
        attn_rows,
        normed_all,
        turns,
        (resid_in, d_mid, scales, gain_rows),
        terms_own,
        terms_other,
        chips,
        2,
    )
    grad_ffn = terms_own[0].astype(single) + terms_other[0].astype(single)
    grad_ffn = (grad_ffn + terms_side.astype(single)).reshape(3, units, width)
    grad_attn = grad_attn.reshape(3, share, width)
    grad_gain = lax.dynamic_slice(gain_total, (0, gain_start), gains.shape)

    gains_first_new, gains_second_new, gains_new = adamw(
        gains, gains_first, gains_second, grad_gain, rate_gain, 0.0
    )
    attn_first_new, attn_second_new, attn_weight_new = adamw(
        attn_weight, attn_first, attn_second, grad_attn, rate_matrix, decay_matrix
    )
    ffn_first_new, ffn_second_new, ffn_weight_new = adamw(
        ffn_weight, ffn_first, ffn_second, grad_ffn.transpose(1, 0, 2), rate_matrix, decay_matrix
    )
    return (
        result[None],
        tokens_grad[None],
        gains_first_new,
        gains_second_new,
        gains_new,
        attn_first_new,
        attn_second_new,
        attn_weight_new,
        ffn_first_new,
        ffn_second_new,
        ffn_weight_new,
    )


def solution(mesh):
    by_token = P("fsdp", "head", None)
    by_column = P(None, ("head", "fsdp"))
    by_row = P(None, ("head", "fsdp"), None)
    by_unit = P(("head", "fsdp"), None, None)
    placed = (by_token,) * 2 + (by_column,) * 3 + (by_row,) * 3 + (by_unit,) * 3
    body = per_device if mesh.shape["fsdp"] == 16 else general_device
    return jax.shard_map(
        body, mesh=mesh, in_specs=placed, out_specs=placed, check_vma=False
    )
```

```python
import functools
import math

import jax
import jax.numpy as jnp
from jax import lax
from jax.experimental import pallas as pl
from jax.experimental.pallas import tpu as pltpu
from jax.sharding import PartitionSpec as P

HQ = 8
HK = 4
HD = 256
WIN = 4096
STEP = 10
SEQ_LEN = 8192


eps_norm = 1e-06
softcap = 50.0
beta_one = 0.9
beta_two = 0.95
adam_eps = 1e-08
rate_matrix = 0.02
rate_gain = 0.2
decay_matrix = 0.1

bfloat = jnp.bfloat16
single = jnp.float32
MESH = pl.DeviceIdType.MESH


def norm_scale(values, scales):
    return (
        values
        * lax.rsqrt(jnp.mean(values * values, axis=-1, keepdims=True) + eps_norm)
        * (1.0 + scales)
    )


def turn_angles(positions, head_width):
    halfway = head_width // 2
    inverse_freq = 10000.0 ** (-(jnp.arange(halfway, dtype=jnp.float32) * 2.0) / head_width)
    return positions.astype(jnp.float32)[:, None] * inverse_freq[None, :]


def rotate(values, angles, direction):
    halfway = values.shape[-1] // 2
    cosine = jnp.cos(angles)[:, None, :]
    sine_part = direction * jnp.sin(angles)[:, None, :]
    former = values[..., :halfway]
    latter = values[..., halfway:]
    return jnp.concatenate(
        [former * cosine - latter * sine_part, latter * cosine + former * sine_part], axis=-1
    )


def adamw(weight, moment, second, gradient, step_rate, decay_rate):
    moment = beta_one * moment + (1.0 - beta_one) * gradient
    second = beta_two * second + (1.0 - beta_two) * gradient * gradient
    update = (
        moment / (1.0 - beta_one**STEP) / (jnp.sqrt(second / (1.0 - beta_two**STEP)) + adam_eps)
        + decay_rate * weight
    )
    return (moment, second, weight - step_rate * update)


def hidden_unit(gate_part, up_part):
    return jax.nn.gelu(gate_part, approximate=True) * up_part


def ring_of(chip, chips):
    wide = chips // 4
    deep, side = chip // wide, chip % wide
    return side * 4 + deep + (side % 2) * (3 - 2 * deep)


def chip_of(ring, chips):
    wide = chips // 4
    side, along = ring // 4, ring % 4
    return (along + (side % 2) * (3 - 2 * along)) * wide + side


def ring_places(chips):
    index = lax.axis_index("fsdp")
    core, chip = index % 2, index // 2
    ring = ring_of(chip, chips)
    right = 2 * chip_of((ring + 1) % chips, chips) + core
    left = 2 * chip_of((ring + chips - 1) % chips, chips) + core
    return chip, ring, right, left


def ring_barrier(right, left):
    barrier = pltpu.get_barrier_semaphore()
    for neighbour in (left, right):
        pl.semaphore_signal(barrier, inc=1, device_id={"fsdp": neighbour}, device_id_type=MESH)
    pl.semaphore_wait(barrier, 2)


def region(shape, pieces, way, piece):
    rows, columns = shape
    if rows % 32 == 0:
        size = rows // 2 // pieces
        start = way * (rows // 2) + piece * size
        return (pl.ds(start, size), pl.ds(0, columns)), (pl.ds(piece * size, size), pl.ds(0, columns))
    size = columns // 2
    return (pl.ds(0, rows), pl.ds(way * size, size)), (pl.ds(0, rows), pl.ds(0, size))


def half_shape(rows, columns):
    return (rows // 2, columns) if rows % 32 == 0 else (rows, columns // 2)


def gather_kernel(chips, pieces, own_ref, all_ref, local_sem, send_sem, recv_sem):
    chip, ring, right, left = ring_places(chips)
    ring_barrier(right, left)
    keep = pltpu.make_async_copy(own_ref, all_ref.at[chip], local_sem)
    keep.start()

    def copy(way, step, piece, first):
        owner = chip_of((ring + (chips - step if way == 0 else step)) % chips, chips)
        part, ignored = region(own_ref.shape, pieces, way, piece)
        there = all_ref.at[(owner,) + part]
        return pltpu.make_async_remote_copy(
            src_ref=own_ref.at[part] if first else there,
            dst_ref=there,
            send_sem=send_sem.at[way, piece, step],
            recv_sem=recv_sem.at[way, piece, step],
            device_id={"fsdp": right if way == 0 else left},
            device_id_type=MESH,
        )

    streams = [(way, piece) for piece in range(pieces) for way in range(2)]
    for way, piece in streams:
        copy(way, 0, piece, True).start()

    def body(step, carried):
        for way, piece in streams:
            copy(way, step - 1, piece, False).wait_recv()
            copy(way, step, piece, False).start()
        return carried

    lax.fori_loop(1, chips - 1, body, 0)
    for way, piece in streams:
        copy(way, chips - 2, piece, False).wait_recv()

    def finish(step, carried):
        for way, piece in streams:
            copy(way, step, piece, False).wait_send()
        return carried

    lax.fori_loop(0, chips - 1, finish, 0)
    keep.wait()


def ring_gather(own, chips, ident):
    rows, columns = own.shape
    pieces = 2 if rows % 64 == 0 else 1
    return pl.pallas_call(
        functools.partial(gather_kernel, chips, pieces),
        out_shape=jax.ShapeDtypeStruct((chips, rows, columns), own.dtype),
        in_specs=[pl.BlockSpec(memory_space=pl.ANY)],
        out_specs=pl.BlockSpec(memory_space=pl.ANY),
        scratch_shapes=[
            pltpu.SemaphoreType.DMA,
            pltpu.SemaphoreType.DMA((2, pieces, chips - 1)),
            pltpu.SemaphoreType.DMA((2, pieces, chips - 1)),
        ],
        compiler_params=pltpu.CompilerParams(collective_id=ident, has_side_effects=True),
        cost_estimate=cost(45),
    )(own)


def scatter_kernel(chips, pieces, parts_ref, sum_ref, held, send_sem, recv_sem):
    chip, ring, right, left = ring_places(chips)
    ring_barrier(right, left)

    def owner_of(way, step):
        shift = chips - 1 - step if way == 0 else 1 + step
        return chip_of((ring + shift) % chips, chips)

    def copy(way, step, piece, first):
        part, place = region(sum_ref.shape, pieces, way, piece)
        return pltpu.make_async_remote_copy(
            src_ref=(
                parts_ref.at[(owner_of(way, step),) + part]
                if first
                else held.at[(way, step - 1) + place]
            ),
            dst_ref=held.at[(way, step) + place],
            send_sem=send_sem.at[way, piece, step],
            recv_sem=recv_sem.at[way, piece, step],
            device_id={"fsdp": right if way == 0 else left},
            device_id_type=MESH,
        )

    streams = [(way, piece) for piece in range(pieces) for way in range(2)]
    for way, piece in streams:
        copy(way, 0, piece, True).start()

    def arrived(way, step, piece):
        copy(way, step, piece, True).wait_recv()
        part, place = region(sum_ref.shape, pieces, way, piece)
        here = parts_ref[(owner_of(way, step + 1),) + part]
        return held[(way, step) + place].astype(single) + here.astype(single)

    def body(step, carried):
        for way, piece in streams:
            total = arrived(way, step - 1, piece)
            part, place = region(sum_ref.shape, pieces, way, piece)
            held[(way, step - 1) + place] = total.astype(held.dtype)
            copy(way, step, piece, False).start()
        return carried

    lax.fori_loop(1, chips - 1, body, 0)
    for way, piece in streams:
        part, place = region(sum_ref.shape, pieces, way, piece)
        sum_ref[part] = arrived(way, chips - 2, piece)

    def finish(step, carried):
        for way, piece in streams:
            copy(way, step, piece, True).wait_send()
        return carried

    lax.fori_loop(0, chips - 1, finish, 0)


def ring_scatter(parts, chips, ident):
    rows, columns = parts.shape[1:]
    pieces = 2 if rows % 64 == 0 else 1
    return pl.pallas_call(
        functools.partial(scatter_kernel, chips, pieces),
        out_shape=jax.ShapeDtypeStruct((rows, columns), single),
        in_specs=[pl.BlockSpec(memory_space=pltpu.VMEM)],
        out_specs=pl.BlockSpec(memory_space=pltpu.VMEM),
        scratch_shapes=[
            pltpu.VMEM((2, chips - 1) + half_shape(rows, columns), parts.dtype),
            pltpu.SemaphoreType.DMA((2, pieces, chips - 1)),
            pltpu.SemaphoreType.DMA((2, pieces, chips - 1)),
        ],
        compiler_params=pltpu.CompilerParams(
            collective_id=ident, has_side_effects=True, vmem_limit_bytes=56 * 2**20
        ),
        cost_estimate=cost(45),
    )(parts)


def norm_back(values, scales, grad):
    inverse = lax.rsqrt(jnp.mean(values * values, axis=-1, keepdims=True) + eps_norm)
    bent = grad * (1.0 + scales)
    slope = jnp.mean(bent * values, axis=-1, keepdims=True) * (inverse * inverse * inverse)
    return bent * inverse - values * slope, jnp.sum(grad * values * inverse, axis=0, keepdims=True)


def gelu_parts(gate):
    root = math.sqrt(2.0 / math.pi)
    square = gate * gate
    bend = jnp.tanh(root * gate * (1.0 + 0.044715 * square))
    half = 0.5 * (1.0 + bend)
    slope = half + 0.5 * gate * (1.0 - bend * bend) * (root * (1.0 + 3.0 * 0.044715 * square))
    return gate * half, slope


def dot_nt(left, right):
    return lax.dot_general(left, right, (((1,), (1,)), ((), ())), preferred_element_type=single)


def dot_nn(left, right):
    return lax.dot_general(left, right, (((1,), (0,)), ((), ())), preferred_element_type=single)


def dot_tn(left, right):
    return lax.dot_general(left, right, (((0,), (0,)), ((), ())), preferred_element_type=single)


class Ring:
    def __init__(self, chips, pieces, rows, send_sem, recv_sem):
        self.chips, self.pieces, self.half = chips, pieces, rows // 2
        self.size = rows // 2 // pieces
        self.chip, self.ring, self.right, self.left = ring_places(chips)
        self.send_sem, self.recv_sem = send_sem, recv_sem
        self.streams = [(way, piece) for piece in range(pieces) for way in range(2)]

    def owner(self, way, step):
        shift = self.chips - step if way == 0 else step
        return chip_of((self.ring + shift) % self.chips, self.chips)

    def copy(self, source, target, way, piece, step):
        return pltpu.make_async_remote_copy(
            src_ref=source,
            dst_ref=target,
            send_sem=self.send_sem.at[way, piece, step],
            recv_sem=self.recv_sem.at[way, piece, step],
            device_id={"fsdp": self.right if way == 0 else self.left},
            device_id_type=MESH,
        )

    def part(self, way, piece):
        return pl.ds(way * self.half + piece * self.size, self.size)

    def place(self, piece):
        return pl.ds(piece * self.size, self.size)

    def gather_copy(self, all_ref, way, piece, step):
        there = all_ref.at[self.owner(way, step), self.part(way, piece)]
        return self.copy(there, there, way, piece, step)

    def gather_step(self, all_ref, step):
        for way, piece in self.streams:

            @pl.when(step > 0)
            def _():
                self.gather_copy(all_ref, way, piece, step - 1).wait_recv()

            @pl.when(step < self.chips - 1)
            def _():
                self.gather_copy(all_ref, way, piece, step).start()

    def scatter_copy(self, parts_ref, held, way, piece, step, first):
        source = (
            parts_ref.at[self.owner(way, step + 1), self.part(way, piece)]
            if first
            else held.at[way, step - 1, self.place(piece)]
        )
        return self.copy(source, held.at[way, step, self.place(piece)], way, piece, step)

    def scatter_total(self, parts_ref, held, way, piece, step):
        self.scatter_copy(parts_ref, held, way, piece, step, True).wait_recv()
        here = parts_ref[self.owner(way, step + 2), self.part(way, piece)]
        return held[way, step, self.place(piece)].astype(single) + here.astype(single)

    def scatter_step(self, parts_ref, held, step):
        for way, piece in self.streams:

            @pl.when(step == 0)
            def _():
                self.scatter_copy(parts_ref, held, way, piece, 0, True).start()

            @pl.when(step > 0)
            def _():
                total = self.scatter_total(parts_ref, held, way, piece, step - 1)
                held[way, step - 1, self.place(piece)] = total.astype(held.dtype)
                self.scatter_copy(parts_ref, held, way, piece, step, False).start()

    def scatter_end(self, parts_ref, held, sum_ref):
        for way, piece in self.streams:
            sum_ref[self.part(way, piece)] = self.scatter_total(
                parts_ref, held, way, piece, self.chips - 2
            )

    def finish(self, example):
        def body(step, carried):
            for way, piece in self.streams:
                self.copy(example, example, way, piece, step).wait_send()
            return carried

        lax.fori_loop(0, self.chips - 1, body, 0)


def quad_peers(chips):
    side = lax.axis_index("head")
    index = lax.axis_index("fsdp")
    chip, core = index // 2, index % 2
    ring = ring_of(chip, chips)
    around = [2 * chip_of((ring + hop) % chips, chips) + core for hop in range(1, chips)]
    return side, core, {"head": 1 - side}, {"fsdp": 2 * chip + 1 - core}, around


def wide_barrier(to_side, to_core, around):
    barrier = pltpu.get_barrier_semaphore()
    for target in [to_side, to_core] + [{"fsdp": other} for other in around]:
        pl.semaphore_signal(barrier, inc=1, device_id=target, device_id_type=MESH)
    pl.semaphore_wait(barrier, 2 + len(around))


def quad_barrier(to_side, to_core, right, left):
    barrier = pltpu.get_barrier_semaphore()
    for target in (to_side, to_core, {"fsdp": right}, {"fsdp": left}):
        pl.semaphore_signal(barrier, inc=1, device_id=target, device_id_type=MESH)
    pl.semaphore_wait(barrier, 4)


def remote(source, target, send_sem, recv_sem, device):
    return pltpu.make_async_remote_copy(
        src_ref=source,
        dst_ref=target,
        send_sem=send_sem,
        recv_sem=recv_sem,
        device_id=device,
        device_id_type=MESH,
    )


class Total:
    def __init__(self, value, near, blocks, send_sem, recv_sem, peers, chip):
        self.value, self.near, self.blocks = value, near, blocks
        self.send_sem, self.recv_sem = send_sem, recv_sem
        side, core, self.to_side, self.to_core, self.around = peers
        self.chip = chip
        self.first = remote(value.at[0], near.at[0], send_sem.at[0], recv_sem.at[0], self.to_side)
        self.second = remote(value.at[1], near.at[1], send_sem.at[1], recv_sem.at[1], self.to_core)

    def spread(self, hop):
        here = self.blocks.at[self.chip]
        return remote(
            here,
            here,
            self.send_sem.at[1 + hop],
            self.recv_sem.at[1 + hop],
            {"fsdp": self.around[hop - 1]},
        )

    def start(self):
        self.first.start()

    def over_cores(self):
        self.first.wait_recv()
        self.value[1] = self.value[0] + self.near[0]
        self.second.start()

    def over_ring(self):
        self.second.wait_recv()
        self.blocks[self.chip] = self.value[1] + self.near[1]
        for hop in range(1, len(self.around) + 1):
            self.spread(hop).start()

    def end(self):
        for hop in range(1, len(self.around) + 1):
            self.spread(hop).wait_recv()
        total = self.blocks[0]
        for other in range(1, len(self.around) + 1):
            total = total + self.blocks[other]
        self.first.wait_send()
        self.second.wait_send()
        for hop in range(1, len(self.around) + 1):
            self.spread(hop).wait_send()
        return total


def total_scratch(chips, width):
    return [
        pltpu.VMEM((2, 4, width), single),
        pltpu.VMEM((2, 4, width), single),
        pltpu.VMEM((chips, 4, width), single),
        pltpu.SemaphoreType.DMA((chips + 1,)),
        pltpu.SemaphoreType.DMA((chips + 1,)),
    ]


def turn(raw, cosine, sine):
    halfway = raw.shape[1] // 2
    former, latter = raw[:, :halfway], raw[:, halfway:]
    return jnp.concatenate(
        [former * cosine - latter * sine, latter * cosine + former * sine], axis=1
    )


def front_kernel(
    chips,
    cuts,
    own_ref,
    gains_ref,
    resid_ref,
    cosine_ref,
    sine_ref,
    key_cosine_ref,
    key_sine_ref,
    wide_units_ref,
    rows_ref,
    scales_ref,
    normed_ref,
    query_ref,
    keyval_ref,
    attended_ref,
    inverse_ref,
    projected_ref,
    own_units_ref,
    core_units_ref,
    side_units_ref,
    diag_units_ref,
    all_rows,
    both,
    total,
    sums,
    product,
    across_put,
    across_got,
    along_put,
    along_got,
    cast_in,
    cast_out,
    value,
    near,
    blocks,
    total_send,
    total_recv,
    send_sem,
    recv_sem,
    place_sem,
    peer_sem,
    key_send,
    key_recv,
    quad_send,
    quad_recv,
    cast_sem,
    bulk_send,
    bulk_recv,
):
    share, width = own_ref.shape[1:]
    tok_rows = resid_ref.shape[0]
    tokens = 4 * tok_rows
    half = width // 2
    pairs = chips // 4
    scale = 1.0 / math.sqrt(HD)
    chip, ring, right, left = ring_places(chips)
    peers = quad_peers(chips)
    side, core, to_side, to_core, around = peers
    cast_rows = cast_in.shape[1]
    casts = wide_units_ref.shape[0] // cast_rows

    def cast_load(tile):
        rows = pl.ds(tile * cast_rows, cast_rows)
        return pltpu.make_async_copy(
            wide_units_ref.at[rows], cast_in.at[tile % 2], cast_sem.at[0, tile % 2]
        )

    def cast_store(tile):
        rows = pl.ds(tile * cast_rows, cast_rows)
        return pltpu.make_async_copy(
            cast_out.at[tile % 2], own_units_ref.at[rows], cast_sem.at[1, tile % 2]
        )

    def cast(first, last):
        for tile in range(first, last):
            cast_load(tile).wait()
            if tile >= 3:
                cast_store(tile - 2).wait()
            cast_out[tile % 2] = cast_in[tile % 2].astype(bfloat)
            cast_store(tile).start()
            if tile + 2 < casts:
                cast_load(tile + 2).start()

    cast_load(0).start()
    cast_load(1).start()
    all_rows[chip] = own_ref[...].astype(bfloat)
    value[0] = gains_ref[...].astype(bfloat).astype(single)
    wide_barrier(to_side, to_core, around)
    gains_total = Total(value, near, blocks, total_send, total_recv, peers, chip)
    gains_total.start()
    streams = [(way, slot) for slot in range(2) for way in range(2)]
    out_streams = [(way, 2) for way in range(2)]
    key_streams = [(way, kind) for kind in range(2) for way in range(2)]

    def owner_of(way, step):
        return chip_of((ring + (chips - step if way == 0 else step)) % chips, chips)

    def hop(way, slot, step):
        there = all_rows.at[owner_of(way, step), slot, :, pl.ds(way * half, half)]
        return remote(
            there,
            there,
            send_sem.at[way, slot, step],
            recv_sem.at[way, slot, step],
            {"fsdp": right if way == 0 else left},
        )

    def key_hop(way, kind, step):
        there = keyval_ref.at[owner_of(way, step), kind, pl.ds(way * (tokens // 2), tokens // 2)]
        return remote(
            there,
            there,
            key_send.at[way, kind, step],
            key_recv.at[way, kind, step],
            {"fsdp": right if way == 0 else left},
        )

    def goal(way, slot, step):
        owner = owner_of(way, step)
        deep = owner // pairs
        unit = (owner % pairs) * 2 + core
        taker, head = (deep % 2, deep // 2) if slot == 1 else (deep // 2, deep % 2)
        columns = pl.ds(way * half, half)
        source = all_rows.at[owner, slot, :, columns]
        start = pl.multiple_of(head * HD + unit * share, share)
        target = rows_ref.at[slot, pl.ds(start, share), columns]
        sem = place_sem.at[way, slot, step]

        def here():
            return pltpu.make_async_copy(source, target, sem)

        def there():
            return remote(source, target, sem, peer_sem.at[way, slot, step], to_core)

        return taker, here, there

    def place(way, slot, step):
        taker, here, there = goal(way, slot, step)

        @pl.when(taker == core)
        def _():
            here().start()

        @pl.when(taker != core)
        def _():
            there().start()

    def placed(way, slot, step):
        taker, here, there = goal(way, slot, step)

        @pl.when(taker == core)
        def _():
            here().wait()
            there().wait_recv()

        @pl.when(taker != core)
        def _():
            there().wait_send()

    def pass_on(which, step):
        for way, slot in which:

            @pl.when(step > 0)
            def _():
                hop(way, slot, step - 1).wait_recv()

            @pl.when(step < chips - 1)
            def _():
                hop(way, slot, step).start()

            place(way, slot, step)

    def settle(which):
        def body(step, carried):
            for way, slot in which:
                placed(way, slot, step)

                @pl.when(step < chips - 1)
                def _():
                    hop(way, slot, step).wait_send()

            return carried

        lax.fori_loop(0, chips, body, 0)

    def quad_copy(source, target, index, device):
        return remote(source, target, quad_send.at[index], quad_recv.at[index], device)

    mine = normed_ref.at[core, side]
    along = quad_copy(mine, mine, 0, to_side)
    across = quad_copy(normed_ref.at[core], normed_ref.at[core], 1, to_core)

    def bulk_side(part):
        rows = pl.ds(cuts[part], cuts[part + 1] - cuts[part])
        return remote(
            own_units_ref.at[rows],
            side_units_ref.at[rows],
            bulk_send.at[part],
            bulk_recv.at[part],
            to_side,
        )

    def bulk_diag(part):
        rows = pl.ds(cuts[part], cuts[part + 1] - cuts[part])
        return remote(
            side_units_ref.at[rows],
            diag_units_ref.at[rows],
            bulk_send.at[3 + part],
            bulk_recv.at[3 + part],
            to_core,
        )

    bulk_core = remote(own_units_ref, core_units_ref, bulk_send.at[6], bulk_recv.at[6], to_core)
    for way, slot in streams:
        hop(way, slot, 0).start()
    cast(0, 1)
    cast_store(0).wait()
    bulk_side(0).start()
    gains_total.over_cores()
    for way, slot in streams:
        place(way, slot, 0)
    gains_total.over_ring()
    pass_on(streams, 1)
    cast(1, 3)
    scales_ref[...] = gains_total.end()
    normed_ref[core, side] = norm_scale(resid_ref[...], scales_ref[0:1]).astype(bfloat)
    along.start()
    pass_on(streams, 2)
    cast(3, 5)
    pass_on(streams, 3)
    cast(5, 7)
    along.wait()
    across.start()
    bulk_side(1).start()
    pass_on(streams, 4)
    cast(7, casts)
    cast_store(casts - 2).wait()
    cast_store(casts - 1).wait()
    bulk_core.start()

    def body(step, carried):
        pass_on(streams, step)
        return carried

    lax.fori_loop(5, chips, body, 0)
    pass_on(out_streams, 0)
    across.wait()
    settle(streams)

    def project(slot, head):
        rows = slice(head * HD, head * HD + HD)
        return dot_nt(normed_ref[...].reshape(tokens, width), rows_ref[slot, rows])

    for head in range(2):
        raw = project(1, head)
        both[head] = turn(raw, key_cosine_ref[...], key_sine_ref[...]).astype(bfloat)
    swap = quad_copy(both.at[1 - side], keyval_ref.at[chip, side], 2, to_side)
    swap.start()
    bulk_side(2).start()
    for part in range(2):
        bulk_side(part).wait_recv()
        bulk_diag(part).start()
    pass_on(out_streams, 1)
    keyval_ref[chip, side] = both[side]
    for head in range(2):
        raw = project(0, head)
        query_ref[head] = turn(raw, cosine_ref[...], sine_ref[...]).astype(bfloat)
        pass_on(out_streams, 2 + head)
    total[...] = jnp.zeros_like(total)
    sums[...] = jnp.zeros_like(sums)
    swap.wait()

    def block(way, owner):
        part = tokens // 2
        key = keyval_ref[owner, 0, way * part : way * part + part]
        val = keyval_ref[owner, 1, way * part : way * part + part]
        row = lax.broadcasted_iota(jnp.int32, (tokens, part), 0)
        column = lax.broadcasted_iota(jnp.int32, (tokens, part), 1)
        allowed = row + (chip - owner) * tokens - way * part >= column

        def one_head(head, carried):
            bent = jnp.tanh(dot_nt(query_ref[head], key) * (scale / softcap))
            powers = jnp.where(allowed, jnp.exp(softcap * bent), 0.0)
            sums[head] += powers[:, : part // 2] + powers[:, part // 2 :]
            total[head] += dot_nn(powers.astype(bfloat), val)
            return carried

        for head in range(2):
            one_head(head, 0)

    def key_body(step, carried):
        for way, kind in key_streams:

            @pl.when(step > 0)
            def _():
                key_hop(way, kind, step - 1).wait_recv()

            @pl.when(step < chips - 1)
            def _():
                key_hop(way, kind, step).start()

        @pl.when(step < chips - 4)
        def _():
            pass_on(out_streams, step + 4)

        for way in range(2):
            owner = owner_of(way, step)

            @pl.when(owner <= chip)
            def _():
                block(way, owner)

        return carried

    lax.fori_loop(0, chips, key_body, 0)
    bulk_side(2).wait_recv()
    bulk_diag(2).start()
    settle(out_streams)
    for head in range(2):
        inverse = 1.0 / jnp.sum(sums[head], axis=-1, keepdims=True)
        inverse_ref[head] = jnp.broadcast_to(inverse, inverse_ref.shape[1:])
        attended_ref[:, head * HD : head * HD + HD] = (total[head] * inverse).astype(bfloat)
    span = width // 3
    tiles = [slice(tile * span, tile * span + span) for tile in range(3)]

    def project_out(part, ref, columns):
        first = pl.ds(pl.multiple_of(part * 2 * tok_rows, 2 * tok_rows), 2 * tok_rows)
        made = dot_nn(attended_ref[first], rows_ref[2, :, columns])
        ref[:, :, columns] = made.reshape(2, tok_rows, span).astype(ref.dtype)

    across = [
        quad_copy(across_put.at[:, :, columns], across_got.at[:, :, columns], 3 + tile, to_core)
        for tile, columns in enumerate(tiles)
    ]
    along = [
        quad_copy(along_put.at[:, columns], along_got.at[:, columns], 6 + tile, to_side)
        for tile, columns in enumerate(tiles)
    ]
    for tile, columns in enumerate(tiles):
        project_out(1 - core, across_put, columns)
        across[tile].start()
        project_out(core, product, columns)
    for tile, columns in enumerate(tiles):
        across[tile].wait()
        given = product[1 - side, :, columns] + across_got[1 - side, :, columns].astype(single)
        along_put[:, columns] = given.astype(bfloat)
        along[tile].start()

    def key_settle(step, carried):
        for way, kind in key_streams:
            key_hop(way, kind, step).wait_send()
        return carried

    lax.fori_loop(0, chips - 1, key_settle, 0)
    bulk_core.wait()
    for part in range(3):
        bulk_side(part).wait_send()
        bulk_diag(part).wait()
    for tile, columns in enumerate(tiles):
        along[tile].wait()
        kept = product[side, :, columns] + across_got[side, :, columns].astype(single)
        projected_ref[:, columns] = kept + along_got[:, columns].astype(single)


def cost(micros):
    return pl.CostEstimate(flops=int(micros * 1e9), bytes_accessed=0, transcendentals=0)


def front(attn_weight, gains, resid_in, turns, ffn_wide, chips, ident):
    share, width = attn_weight.shape[1:]
    tok_rows = resid_in.shape[0]
    tokens = 4 * tok_rows
    units = ffn_wide.shape[0]
    cuts = (0, units // 9, units // 3, 2 * units // 3)
    vmem = pl.BlockSpec(memory_space=pltpu.VMEM)
    anywhere = pl.BlockSpec(memory_space=pl.ANY)
    return pl.pallas_call(
        functools.partial(front_kernel, chips, cuts),
        out_shape=(
            jax.ShapeDtypeStruct((3, 2 * HD, width), bfloat),
            jax.ShapeDtypeStruct((4, width), single),
            jax.ShapeDtypeStruct((2, 2, tok_rows, width), bfloat),
            jax.ShapeDtypeStruct((2, tokens, HD), bfloat),
            jax.ShapeDtypeStruct((chips, 2, tokens, HD), bfloat),
            jax.ShapeDtypeStruct((tokens, 2 * HD), bfloat),
            jax.ShapeDtypeStruct((2, tokens, 128), single),
            jax.ShapeDtypeStruct((tok_rows, width), single),
        )
        + (jax.ShapeDtypeStruct((units, width), bfloat),) * 2
        + (jax.ShapeDtypeStruct((2 * units // 3, width), bfloat),) * 2,
        in_specs=[vmem] * 7 + [anywhere],
        out_specs=(vmem,) * 8 + (anywhere,) * 4,
        scratch_shapes=[
            pltpu.VMEM((chips, 3, share, width), bfloat),
            pltpu.VMEM((2, tokens, HD), bfloat),
            pltpu.VMEM((2, tokens, HD), single),
            pltpu.VMEM((2, tokens, 128), single),
            pltpu.VMEM((2, tok_rows, width), single),
            pltpu.VMEM((2, tok_rows, width), bfloat),
            pltpu.VMEM((2, tok_rows, width), bfloat),
            pltpu.VMEM((tok_rows, width), bfloat),
            pltpu.VMEM((tok_rows, width), bfloat),
            pltpu.VMEM((2, units // 9, width), single),
            pltpu.VMEM((2, units // 9, width), bfloat),
        ]
        + total_scratch(chips, width)
        + [
            pltpu.SemaphoreType.DMA((2, 3, chips - 1)),
            pltpu.SemaphoreType.DMA((2, 3, chips - 1)),
            pltpu.SemaphoreType.DMA((2, 3, chips)),
            pltpu.SemaphoreType.DMA((2, 3, chips)),
            pltpu.SemaphoreType.DMA((2, 2, chips - 1)),
            pltpu.SemaphoreType.DMA((2, 2, chips - 1)),
            pltpu.SemaphoreType.DMA((9,)),
            pltpu.SemaphoreType.DMA((9,)),
            pltpu.SemaphoreType.DMA((2, 2)),
            pltpu.SemaphoreType.DMA((7,)),
            pltpu.SemaphoreType.DMA((7,)),
        ],
        compiler_params=pltpu.CompilerParams(
            collective_id=ident, has_side_effects=True, vmem_limit_bytes=60 * 2**20
        ),
        cost_estimate=cost(140),
    )(attn_weight, gains, resid_in, *turns, ffn_wide)


def tail_kernel(
    chips,
    d_proj_ref,
    query_ref,
    keyval_ref,
    attended_ref,
    inverse_ref,
    rows_ref,
    normed_ref,
    cosine_ref,
    sine_ref,
    key_cosine_ref,
    key_sine_ref,
    resid_ref,
    d_mid_ref,
    scales_ref,
    gains_ref,
    units_own_ref,
    units_other_ref,
    sum_ref,
    tokens_ref,
    total_ref,
    units_ref,
    units_got_ref,
    d_all,
    d_out,
    delta,
    d_query,
    d_block,
    first_put,
    held_keys,
    swapped,
    d_raw,
    out_rows,
    parts,
    out_parts,
    held,
    out_held,
    across_got,
    along_put,
    along_got,
    value,
    near,
    blocks,
    total_send,
    total_recv,
    key_send,
    key_recv,
    place_sem,
    peer_sem,
    send_sem,
    recv_sem,
    out_send,
    out_recv,
    quad_send,
    quad_recv,
    load_sem,
    bulk_send,
    bulk_recv,
):
    tokens = query_ref.shape[1]
    half = tokens // 2
    width = resid_ref.shape[1]
    share = out_parts.shape[1]
    pairs = chips // 4
    scale = 1.0 / math.sqrt(HD)
    peers = quad_peers(chips)
    side, core, to_side, to_core, around = peers
    ring = Ring(chips, 2, 2 * share, send_sem, recv_sem)
    out_ring = Ring(chips, 1, share, out_send, out_recv)
    chip = ring.chip
    gains_total = Total(value, near, blocks, total_send, total_recv, peers, chip)
    d_all[core, side] = d_proj_ref[...]
    wide_barrier(to_side, to_core, around)

    def quad_copy(source, target, index, device):
        return remote(source, target, quad_send.at[index], quad_recv.at[index], device)

    def bulk(kind):
        return remote(
            units_ref.at[pl.ds(kind * (units_ref.shape[0] // 3), units_ref.shape[0] // 3)],
            units_got_ref.at[pl.ds(kind * (units_ref.shape[0] // 3), units_ref.shape[0] // 3)],
            bulk_send.at[kind],
            bulk_recv.at[kind],
            to_side,
        )

    units = units_ref.shape[0]
    ours = out_rows.reshape(6 * HD, width).at[pl.ds(0, units)]
    theirs = parts.reshape(2 * chips * share, width).at[pl.ds(0, units)]
    loads = (
        pltpu.make_async_copy(units_own_ref.at[1], ours, load_sem.at[0]),
        pltpu.make_async_copy(units_other_ref.at[1], theirs, load_sem.at[1]),
    )
    store = pltpu.make_async_copy(ours, units_ref, load_sem.at[2])
    for load in loads:
        load.start()
    quarter = tokens // 8
    halves = [slice(part * quarter, part * quarter + quarter) for part in range(2)]
    along = [
        quad_copy(d_all.at[core, side, rows], d_all.at[core, side, rows], part, to_side)
        for part, rows in enumerate(halves)
    ]
    across = quad_copy(d_all.at[core, side], d_all.at[core, side], 2, to_core)
    relay = [
        quad_copy(d_all.at[core, 1 - side, rows], d_all.at[core, 1 - side, rows], 3 + part, to_core)
        for part, rows in enumerate(halves)
    ]
    for part in range(2):
        along[part].start()
    across.start()
    d_query[...] = jnp.zeros_like(d_query)
    for load in loads:
        load.wait()
    for kind in range(3):
        rows = slice(kind * units // 3, (kind + 1) * units // 3)
        ours[rows] = (ours[rows].astype(single) + theirs[rows].astype(single)).astype(bfloat)
    store.start()
    for part in range(2):
        along[part].wait()
        relay[part].start()
    store.wait()
    bulk(0).start()
    bulk(1).start()
    across.wait()
    for part in range(2):
        relay[part].wait()
    d_rows = d_all[...].reshape(tokens, width)
    for head in range(2):
        columns = slice(head * HD, head * HD + HD)
        made = dot_nt(d_rows, rows_ref[2, columns]).astype(bfloat)
        d_out[head] = made
        row_dot = jnp.sum(
            made.astype(single) * attended_ref[:, columns].astype(single), axis=-1, keepdims=True
        )
        delta[head] = jnp.broadcast_to(row_dot, delta.shape[1:])

    def place(slot, head, start):
        deep = 2 * head + core if slot == 1 else 2 * core + head
        for unit in range(4):
            source = out_rows.at[slot, head, pl.ds(unit * share, share)]
            owner = deep * pairs + unit // 2
            target = out_parts.at[owner] if slot == 2 else parts.at[owner, slot]
            sem = place_sem.at[slot, head, unit]

            def here():
                return pltpu.make_async_copy(source, target, sem)

            def there():
                return remote(source, target, sem, peer_sem.at[slot, head, unit], to_core)

            @pl.when(core == unit % 2)
            def _():
                if start:
                    here().start()
                else:
                    here().wait()
                    there().wait_recv()

            @pl.when(core != unit % 2)
            def _():
                if start:
                    there().start()
                else:
                    there().wait_send()

    def term(slot, head, left, right):
        out_rows[slot, head] = dot_tn(left, right).astype(bfloat)
        place(slot, head, True)

    for head in range(2):
        term(2, head, attended_ref[:, head * HD : head * HD + HD], d_all[...].reshape(tokens, width))
    def block(way, owner):
        key = keyval_ref[owner, 0, way * half : way * half + half]
        val = keyval_ref[owner, 1, way * half : way * half + half]
        row = lax.broadcasted_iota(jnp.int32, (tokens, half), 0)
        column = lax.broadcasted_iota(jnp.int32, (tokens, half), 1)
        allowed = row + (chip - owner) * tokens - way * half >= column

        def one_head(head, carried):
            bent = jnp.tanh(dot_nt(query_ref[head], key) * (scale / softcap))
            inverse = jnp.concatenate([inverse_ref[head]] * (half // 128), axis=1)
            row_dot = jnp.concatenate([delta[head]] * (half // 128), axis=1)
            probs = jnp.where(allowed, jnp.exp(softcap * bent), 0.0) * inverse
            d_probs = dot_nt(d_out[head], val)
            d_scores = (probs * (d_probs - row_dot) * (1.0 - bent * bent)).astype(bfloat)
            d_block[way, 0] += dot_tn(d_scores, query_ref[head]) * scale
            d_block[way, 1] += dot_tn(probs.astype(bfloat), d_out[head])
            d_query[head] += dot_nn(d_scores, key)
            return carried

        for head in range(2):
            one_head(head, 0)

    def key_copy(way, kind, step, first):
        return remote(
            first_put.at[way, kind] if first else held_keys.at[way, step - 1, kind],
            held_keys.at[way, step, kind],
            key_send.at[way, kind, step],
            key_recv.at[way, kind, step],
            {"fsdp": ring.right if way == 0 else ring.left},
        )

    streams = [(way, kind) for kind in range(2) for way in range(2)]

    def key_blocks(step):
        for way in range(2):
            owner = ring.owner(way, step + 1)
            d_block[way] = jnp.zeros(d_block.shape[1:], single)

            @pl.when(owner <= chip)
            def _():
                block(way, owner)

    def key_body(step, carried):
        key_blocks(step)
        for way, kind in streams:

            @pl.when(step == 0)
            def _():
                first_put[way, kind] = d_block[way, kind].astype(bfloat)
                key_copy(way, kind, 0, True).start()

            @pl.when(step > 0)
            def _():
                key_copy(way, kind, step - 1, True).wait_recv()
                summed = held_keys[way, step - 1, kind].astype(single) + d_block[way, kind]
                held_keys[way, step - 1, kind] = summed.astype(bfloat)
                key_copy(way, kind, step, False).start()

        @pl.when(step == 0)
        def _():
            for head in range(2):
                place(2, head, False)

        out_ring.scatter_step(out_parts, out_held, step)
        return carried

    lax.fori_loop(0, chips - 1, key_body, 0)

    normed = normed_ref[...].reshape(tokens, width)
    key_blocks(chips - 1)
    for way in range(2):
        rows = slice(way * half, way * half + half)
        for kind in range(2):
            key_copy(way, kind, chips - 2, True).wait_recv()
            summed = held_keys[way, chips - 2, kind].astype(single) + d_block[way, kind]
            swapped[2 + kind, rows] = summed.astype(bfloat)
    swap = quad_copy(swapped.at[3 - side], swapped.at[side], 5, to_side)
    swap.start()
    for head in range(2):
        turned = turn(d_query[head] * scale, cosine_ref[...], -sine_ref[...])
        d_raw[head] = turned.astype(bfloat)
        term(0, head, d_raw[head], normed)
    swap.wait()
    bulk(2).start()
    swapped[side] = swapped[2 + side]
    for head in range(2):
        turned = turn(swapped[head].astype(single), key_cosine_ref[...], -key_sine_ref[...])
        d_raw[2 + head] = turned.astype(bfloat)
        term(1, head, d_raw[2 + head], normed)
    span = width // 3

    def d_input(tile, carried):
        columns = pl.ds(pl.multiple_of(tile * span, span), span)
        made = dot_nn(d_raw[0], rows_ref[0, 0:HD, columns])
        made = made + dot_nn(d_raw[1], rows_ref[0, HD:, columns])
        made = made + dot_nn(d_raw[2], rows_ref[1, 0:HD, columns])
        made = made + dot_nn(d_raw[3], rows_ref[1, HD:, columns])
        out_rows[0, :, :, columns] = made.reshape(2, half, span).astype(bfloat)
        return carried

    for slot in range(2):
        for head in range(2):
            place(slot, head, False)
    blocks_ref = parts.reshape(chips, 2 * share, width)
    ring.scatter_step(blocks_ref, held, 0)
    lax.fori_loop(0, 3, d_input, 0)
    across = quad_copy(out_rows.at[0, 1 - core], across_got, 6, to_core)
    mine = pl.ds(pl.multiple_of(side * (half // 2), half // 2), half // 2)
    other = pl.ds(pl.multiple_of((1 - side) * (half // 2), half // 2), half // 2)
    along = quad_copy(along_put, along_got, 7, to_side)
    across.start()

    def body(step, carried):
        ring.scatter_step(blocks_ref, held, step)

        @pl.when(step == 1)
        def _():
            across.wait()
            given = out_rows[0, core, other].astype(single) + across_got[other].astype(single)
            along_put[...] = given.astype(bfloat)
            along.start()
            tokens_ref[...] = out_rows[0, core, mine].astype(single) + across_got[mine].astype(single)

        @pl.when(step == 4)
        def _():
            along.wait()
            tokens_ref[...] = tokens_ref[...] + along_got[...].astype(single)
            d_norm, d_gain = norm_back(resid_ref[...], scales_ref[0:1], tokens_ref[...])
            tokens_ref[...] = d_mid_ref[...] + d_norm
            value[0] = gains_ref[...]
            value[0, 0:1] = d_gain
            gains_total.start()

        @pl.when(step == 5)
        def _():
            gains_total.over_cores()

        @pl.when(step == 6)
        def _():
            gains_total.over_ring()

        return carried

    lax.fori_loop(1, chips - 1, body, 0)
    total_ref[...] = gains_total.end()
    out_ring.scatter_end(out_parts, out_held, sum_ref.at[pl.ds(2 * share, share)])
    ring.scatter_end(blocks_ref, held, sum_ref.at[pl.ds(0, 2 * share)])
    ring.finish(held.at[0, 0, 0 : ring.size])
    out_ring.finish(out_held.at[0, 0, 0 : out_ring.size])

    def settle(step, carried):
        for way, kind in streams:
            key_copy(way, kind, step, True).wait_send()
        return carried

    lax.fori_loop(0, chips - 1, settle, 0)
    for kind in range(3):
        bulk(kind).wait()


def tail(
    d_proj, query, keyval, attended, inverse, rows, normed, turns, locals_, own, other, chips, ident
):
    tokens = query.shape[1]
    tok_rows = tokens // 4
    width = rows.shape[2]
    share = tokens // 8
    half = tokens // 2
    vmem = pl.BlockSpec(memory_space=pltpu.VMEM)
    anywhere = pl.BlockSpec(memory_space=pl.ANY)
    return pl.pallas_call(
        functools.partial(tail_kernel, chips),
        out_shape=(
            jax.ShapeDtypeStruct((3 * share, width), single),
            jax.ShapeDtypeStruct((tok_rows, width), single),
            jax.ShapeDtypeStruct((4, width), single),
            jax.ShapeDtypeStruct(own.shape[1:], bfloat),
            jax.ShapeDtypeStruct(own.shape[1:], bfloat),
        ),
        in_specs=[vmem] * 15 + [anywhere] * 2,
        out_specs=(vmem,) * 3 + (anywhere,) * 2,
        scratch_shapes=[
            pltpu.VMEM((2, 2, tok_rows, width), bfloat),
            pltpu.VMEM((2, tokens, HD), bfloat),
            pltpu.VMEM((2, tokens, 128), single),
            pltpu.VMEM((2, tokens, HD), single),
            pltpu.VMEM((2, 2, half, HD), single),
            pltpu.VMEM((2, 2, half, HD), bfloat),
            pltpu.VMEM((2, chips - 1, 2, half, HD), bfloat),
            pltpu.VMEM((4, tokens, HD), bfloat),
            pltpu.VMEM((4, tokens, HD), bfloat),
            pltpu.VMEM((3, 2, HD, width), bfloat),
            pltpu.VMEM((chips, 2, share, width), bfloat),
            pltpu.VMEM((chips, share, width), bfloat),
            pltpu.VMEM((2, chips - 1, share, width), bfloat),
            pltpu.VMEM((2, chips - 1, share // 2, width), bfloat),
            pltpu.VMEM((2 * tok_rows, width), bfloat),
            pltpu.VMEM((tok_rows, width), bfloat),
            pltpu.VMEM((tok_rows, width), bfloat),
        ]
        + total_scratch(chips, width)
        + [
            pltpu.SemaphoreType.DMA((2, 2, chips - 1)),
            pltpu.SemaphoreType.DMA((2, 2, chips - 1)),
            pltpu.SemaphoreType.DMA((3, 2, 4)),
            pltpu.SemaphoreType.DMA((3, 2, 4)),
            pltpu.SemaphoreType.DMA((2, 2, chips - 1)),
            pltpu.SemaphoreType.DMA((2, 2, chips - 1)),
            pltpu.SemaphoreType.DMA((2, 1, chips - 1)),
            pltpu.SemaphoreType.DMA((2, 1, chips - 1)),
            pltpu.SemaphoreType.DMA((8,)),
            pltpu.SemaphoreType.DMA((8,)),
            pltpu.SemaphoreType.DMA((3,)),
            pltpu.SemaphoreType.DMA((3,)),
            pltpu.SemaphoreType.DMA((3,)),
        ],
        compiler_params=pltpu.CompilerParams(
            collective_id=ident, has_side_effects=True, vmem_limit_bytes=63 * 2**20
        ),
        cost_estimate=cost(160),
    )(d_proj, query, keyval, attended, inverse, rows, normed, *turns, *locals_, own, other)


def feed_kernel(
    chips,
    pieces,
    resid_ref,
    projected_ref,
    dy_ref,
    scales_ref,
    own_ref,
    side_ref,
    core_ref,
    diag_ref,
    result_ref,
    d_mid_ref,
    d_projected_ref,
    d_gains_ref,
    terms_ref,
    other_ref,
    weights,
    x_all,
    y_all,
    mid,
    both,
    hidden,
    part,
    held_one,
    held_two,
    chunk,
    wide,
    stage,
    load_sem,
    bulk_send,
    bulk_recv,
    stage_sem,
    other_sem,
    send_sem,
    recv_sem,
):
    tok_rows, width = resid_ref.shape
    units = own_ref.shape[0] // 3
    whole = 4 * units
    half = tok_rows // 2
    rings = [
        Ring(chips, pieces, tok_rows, send_sem.at[phase], recv_sem.at[phase]) for phase in range(4)
    ]
    chip = rings[0].chip
    loads = []
    for slot, ref in enumerate((own_ref, side_ref, core_ref, diag_ref)):
        for kind in range(3 if slot % 2 == 0 else 2):
            loads.append(
                pltpu.make_async_copy(
                    ref.at[pl.ds(kind * units, units)],
                    weights.at[pl.ds(kind * whole + slot * units, units)],
                    load_sem.at[slot, kind],
                )
            )
    for load in loads:
        load.start()
    mid[...] = resid_ref[...] + norm_scale(projected_ref[...], scales_ref[1:2])
    x_all[chip] = norm_scale(mid[...], scales_ref[2:3]).astype(bfloat)
    core = lax.axis_index("fsdp") % 2
    to_core = {"fsdp": 2 * chip + 1 - core}
    to_side = {"head": 1 - lax.axis_index("head")}
    quad_barrier(to_side, to_core, rings[0].right, rings[0].left)
    down_rows = [pl.ds(2 * whole + slot * units, units) for slot in range(4)]
    bulk_side = remote(
        own_ref.at[pl.ds(2 * units, units)],
        weights.at[down_rows[1]],
        bulk_send.at[0],
        bulk_recv.at[0],
        to_side,
    )
    bulk_diag = remote(
        weights.at[down_rows[1]],
        weights.at[down_rows[3]],
        bulk_send.at[1],
        bulk_recv.at[1],
        to_core,
    )
    bulk_side.start()
    span = width // 3

    def fetch(all_ref, step):
        chunk[0:half] = all_ref[rings[0].owner(0, step), 0:half]
        chunk[half:] = all_ref[rings[0].owner(1, step), half:]

    def put(ref, step, columns, value):
        ref[rings[0].owner(0, step), 0:half, columns] = value[0:half].astype(ref.dtype)
        ref[rings[0].owner(1, step), half:, columns] = value[half:].astype(ref.dtype)

    def take(ref, step, columns):
        return jnp.concatenate(
            [
                ref[rings[0].owner(0, step), 0:half, columns],
                ref[rings[0].owner(1, step), half:, columns],
            ],
            axis=0,
        )

    def forward(step, carried):
        rings[0].gather_step(x_all, step)

        @pl.when(step == 0)
        def _():
            for load in loads:
                load.wait()

        fetch(x_all, step)

        def gate_up(tile, carried):
            rows = pl.ds(pl.multiple_of(tile * span, span), span)
            wide[:, rows] = dot_nt(chunk[...], weights[rows])
            return carried

        lax.fori_loop(0, 3, gate_up, 0)
        put(both, step, slice(None), wide[...])
        gate = wide[:, 0:whole]
        value, slope = gelu_parts(gate)
        unit = (value * wide[:, whole:]).astype(bfloat)
        put(hidden, step, slice(None), unit)

        @pl.when(step == chips - 1)
        def _():
            bulk_side.wait_recv()
            bulk_diag.start()

        return carried

    lax.fori_loop(0, chips, forward, 0)
    bulk_diag.wait_recv()

    def down(step):
        chunk[:, 0:whole] = take(hidden, step, slice(None))

        def columns_of(tile, carried):
            columns = pl.ds(pl.multiple_of(tile * span, span), span)
            put(part, step, columns, dot_nn(chunk[:, 0:whole], weights[2 * whole :, columns]))
            return carried

        lax.fori_loop(0, 3, columns_of, 0)

    def spread(step, carried):
        down(step + 1)
        rings[1].scatter_step(part, held_one, step)
        return carried

    lax.fori_loop(0, chips - 1, spread, 0)
    down(0)
    rings[1].scatter_end(part, held_one, wide)
    result_ref[...] = mid[...] + norm_scale(wide[...], scales_ref[3:4])
    d_ffn, d_gain = norm_back(wide[...], scales_ref[3:4], dy_ref[...])
    d_gains_ref[0:1] = jnp.zeros_like(d_gain)
    d_gains_ref[3:4] = d_gain
    y_all[chip] = d_ffn.astype(bfloat)
    rings[0].finish(x_all.at[0, 0 : rings[0].size])
    rings[1].finish(x_all.at[0, 0 : rings[0].size])
    bulk_side.wait_send()
    bulk_diag.wait_send()

    def d_input(step):
        chunk[...] = take(both, step, slice(None))

        def columns_of(tile, carried):
            columns = pl.ds(pl.multiple_of(tile * span, span), span)
            put(part, step, columns, dot_nn(chunk[...], weights[0 : 2 * whole, columns]))
            return carried

        lax.fori_loop(0, 3, columns_of, 0)

    early = chips // 2

    def backward(step, carried):
        rings[2].gather_step(y_all, step)
        fetch(y_all, step)
        third = whole // 3
        wide[:, 0:whole] = dot_nt(chunk[...], weights[2 * whole :])

        def d_units(tile, carried):
            columns = pl.ds(pl.multiple_of(tile * third, third), third)
            ups = pl.ds(pl.multiple_of(whole + tile * third, third), third)
            d_hidden = wide[:, columns]
            gate = take(both, step, columns).astype(single)
            upper = take(both, step, ups).astype(single)
            value, slope = gelu_parts(gate)
            put(both, step, columns, d_hidden * upper * slope)
            put(both, step, ups, d_hidden * value)
            return carried

        lax.fori_loop(0, 3, d_units, 0)

        @pl.when(step < early)
        def _():
            d_input(step)

        return carried

    lax.fori_loop(0, chips, backward, 0)
    rows_tile = stage.shape[1]
    tiles = 3 * whole // rows_tile
    upper_tiles = 2 * whole // rows_tile

    cut = units // 3

    def pieces_of(tile):
        for quarter in range(4):
            block = 4 * tile + quarter
            kind, slot, third = block // 12, (block // 3) % 4, block % 3
            source = stage.at[tile % 2, pl.ds(quarter * cut, cut)]
            rows = pl.ds(pl.multiple_of(kind * units + third * cut, cut), cut)
            sem = stage_sem.at[tile % 2, quarter]
            goal = terms_ref.at[slot, rows], other_ref.at[slot - 2, rows]
            there = functools.partial(
                remote, source, goal[1], sem, other_sem.at[tile, quarter], to_core
            )
            yield slot, functools.partial(pltpu.make_async_copy, source, goal[0], sem), there

    def keep(tile):
        for slot, here, there in pieces_of(tile):

            @pl.when(slot < 2)
            def _():
                here().start()

            @pl.when(slot >= 2)
            def _():
                there().start()

    def kept(tile):
        for slot, here, there in pieces_of(tile):

            @pl.when(slot < 2)
            def _():
                here().wait()

            @pl.when(slot >= 2)
            def _():
                there().wait_send()

    def grads(tile):
        @pl.when(tile >= 2)
        def _():
            kept(tile - 2)

        @pl.when(tile < upper_tiles)
        def _():
            columns = pl.ds(pl.multiple_of(tile * rows_tile, rows_tile), rows_tile)
            left = both[:, :, columns].reshape(chips * tok_rows, rows_tile)
            stage[tile % 2] = dot_tn(left, x_all[...].reshape(chips * tok_rows, width)).astype(bfloat)

        @pl.when(tile >= upper_tiles)
        def _():
            columns = pl.ds(
                pl.multiple_of((tile - upper_tiles) * rows_tile, rows_tile), rows_tile
            )
            left = hidden[:, :, columns].reshape(chips * tok_rows, rows_tile)
            stage[tile % 2] = dot_tn(left, y_all[...].reshape(chips * tok_rows, width)).astype(bfloat)

        keep(tile)

    def spread_back(step, carried):
        @pl.when(step + 1 >= early)
        def _():
            d_input(step + 1)

        rings[3].scatter_step(part, held_two, step)
        grads(step)
        return carried

    lax.fori_loop(0, chips - 1, spread_back, 0)

    def rest(tile, carried):
        grads(tile)
        return carried

    lax.fori_loop(chips - 1, tiles, rest, 0)
    rings[3].scatter_end(part, held_two, wide)
    d_norm, d_gain = norm_back(mid[...], scales_ref[2:3], wide[...])
    d_gains_ref[2:3] = d_gain
    d_mid_ref[...] = dy_ref[...] + d_norm
    d_projected, d_gain = norm_back(projected_ref[...], scales_ref[1:2], d_mid_ref[...])
    d_gains_ref[1:2] = d_gain
    d_projected_ref[...] = d_projected.astype(bfloat)
    rings[2].finish(x_all.at[0, 0 : rings[0].size])
    rings[3].finish(x_all.at[0, 0 : rings[0].size])
    kept(tiles - 2)
    kept(tiles - 1)

    def gained(tile, carried):
        for slot, here, there in pieces_of(tile):

            @pl.when(slot >= 2)
            def _():
                there().wait_recv()

        return carried

    lax.fori_loop(0, tiles, gained, 0)


def feed_forward(resid_in, projected, grad_out, scales, shares, chips, ident):
    tok_rows, width = resid_in.shape
    units = shares[0].shape[0] // 3
    whole = 4 * units
    pieces = 2
    vmem = pl.BlockSpec(memory_space=pltpu.VMEM)
    anywhere = pl.BlockSpec(memory_space=pl.ANY)
    return pl.pallas_call(
        functools.partial(feed_kernel, chips, pieces),
        out_shape=(
            jax.ShapeDtypeStruct((tok_rows, width), single),
            jax.ShapeDtypeStruct((tok_rows, width), single),
            jax.ShapeDtypeStruct((tok_rows, width), bfloat),
            jax.ShapeDtypeStruct((4, width), single),
            jax.ShapeDtypeStruct((2, 3 * units, width), bfloat),
            jax.ShapeDtypeStruct((2, 3 * units, width), bfloat),
        ),
        in_specs=[vmem] * 4 + [anywhere] * 4,
        out_specs=(vmem, vmem, vmem, vmem, anywhere, anywhere),
        scratch_shapes=[
            pltpu.VMEM((3 * whole, width), bfloat),
            pltpu.VMEM((chips, tok_rows, width), bfloat),
            pltpu.VMEM((chips, tok_rows, width), bfloat),
            pltpu.VMEM((tok_rows, width), single),
            pltpu.VMEM((chips, tok_rows, 2 * whole), bfloat),
            pltpu.VMEM((chips, tok_rows, whole), bfloat),
            pltpu.VMEM((chips, tok_rows, width), bfloat),
            pltpu.VMEM((2, chips - 1, tok_rows // 2, width), bfloat),
            pltpu.VMEM((2, chips - 1, tok_rows // 2, width), bfloat),
            pltpu.VMEM((tok_rows, width), bfloat),
            pltpu.VMEM((tok_rows, width), single),
            pltpu.VMEM((2, whole // 3, width), bfloat),
            pltpu.SemaphoreType.DMA((4, 3)),
            pltpu.SemaphoreType.DMA((2,)),
            pltpu.SemaphoreType.DMA((2,)),
            pltpu.SemaphoreType.DMA((2, 4)),
            pltpu.SemaphoreType.DMA((9, 4)),
            pltpu.SemaphoreType.DMA((4, 2, pieces, chips - 1)),
            pltpu.SemaphoreType.DMA((4, 2, pieces, chips - 1)),
        ],
        compiler_params=pltpu.CompilerParams(
            collective_id=ident, has_side_effects=True, vmem_limit_bytes=63 * 2**20
        ),
        cost_estimate=cost(205),
    )(resid_in, projected, grad_out, scales, *shares)


def general_device(
    tokens,
    cotangent,
    gains,
    gains_first,
    gains_second,
    attn_weight,
    attn_first,
    attn_second,
    ffn_weight,
    ffn_first,
    ffn_second,
):
    devices = lax.axis_size("fsdp")
    chips = devices // 2
    side = lax.axis_index("head")
    place = lax.axis_index("fsdp")
    core, chip = place % 2, place // 2
    tok_rows = tokens.shape[1]
    super_rows = 4 * tok_rows
    seq_len = min(SEQ_LEN, super_rows * chips)
    share = attn_weight.shape[1]
    pairs = chips // 4
    width = tokens.shape[2]
    scale = 1.0 / math.sqrt(HD)

    def swap_core(value):
        return lax.ppermute(value, "fsdp", [(index, index ^ 1) for index in range(devices)])

    def swap_side(value):
        return lax.ppermute(value, "head", [(0, 1), (1, 0)])

    def in_order(own, other, index, axis):
        return jnp.where(
            index == 0, jnp.stack([own, other], axis), jnp.stack([other, own], axis)
        )

    def pick(value, index, axis=0):
        return lax.dynamic_index_in_dim(value, index, axis, keepdims=False)

    def quad_gather(value):
        value = in_order(value, swap_side(value), side, 0)
        value = in_order(value, swap_core(value), core, 0)
        return value.reshape((super_rows,) + value.shape[3:])

    def quad_scatter(partial):
        partial = partial.reshape(2, 2, tok_rows, width)
        mine = pick(partial, core) + swap_core(pick(partial, 1 - core).astype(bfloat)).astype(single)
        return pick(mine, side) + swap_side(pick(mine, 1 - side).astype(bfloat)).astype(single)

    scales = lax.all_gather(gains.astype(bfloat), ("head", "fsdp"), axis=1, tiled=True).astype(single)
    attn_low = attn_weight.astype(bfloat)
    ffn_low = ffn_weight.astype(bfloat).transpose(1, 0, 2)
    ffn_pair = jnp.concatenate([ffn_low, swap_side(ffn_low)], axis=1)

    ring_rows = ring_gather(attn_low.reshape(3 * share, width), chips, 0)
    ring_rows = ring_rows.reshape(2, 2, pairs, 3, share, width)

    def query_rows(slot):
        rows = ring_rows[:, :, :, slot]
        other = swap_core(pick(rows, 1 - core))
        return in_order(pick(rows, core), other, core, 2).reshape(2 * HD, width)

    def keyval_rows():
        rows = ring_rows[:, :, :, 1]
        other = swap_core(pick(rows, 1 - core, 1))
        return in_order(pick(rows, core, 1), other, core, 2).reshape(2 * HD, width)

    w_query, w_keyval, w_out = query_rows(0), keyval_rows(), query_rows(2)

    resid_in = tokens[0]
    grad_out = cotangent[0]
    normed_one = norm_scale(resid_in, scales[0]).astype(bfloat)
    normed_all = quad_gather(normed_one)
    positions = chip * super_rows + jnp.arange(super_rows, dtype=jnp.int32)
    angles = turn_angles(positions % seq_len, HD)
    query_raw = jnp.einsum("td,fd->tf", normed_all, w_query, preferred_element_type=single)
    keyval_raw = jnp.einsum("td,fd->tf", normed_all, w_keyval, preferred_element_type=single)
    query = rotate(query_raw.reshape(super_rows, 2, HD), angles, 1.0).astype(bfloat)
    key_angles = jnp.where(side == 0, angles, 0.0)
    keyval = rotate(keyval_raw.reshape(super_rows, 2, HD), key_angles, 1.0).astype(bfloat)
    keyval = in_order(pick(keyval, side, 1), swap_side(pick(keyval, 1 - side, 1)), side, 0)
    keyval_all = ring_gather(keyval.reshape(2 * super_rows, HD), chips, 1)
    keyval_all = keyval_all.reshape(chips, 2, super_rows, HD)
    key_all = keyval_all[:, 0].reshape(chips * super_rows, HD)
    value_all = keyval_all[:, 1].reshape(chips * super_rows, HD)

    key_pos = jnp.arange(chips * super_rows, dtype=jnp.int32)
    distance = positions[:, None] - key_pos[None, :]
    same_seq = (positions // seq_len)[:, None] == (key_pos // seq_len)[None, :]
    allowed = (distance >= 0) & (distance < WIN) & same_seq

    def score_block():
        raw = jnp.einsum("qgd,kd->gqk", query, key_all, preferred_element_type=single)
        bent = jnp.tanh(raw * (scale / softcap))
        return bent, jnp.where(allowed, jnp.exp(softcap * bent), 0.0)

    bent, powers = score_block()
    total = jnp.sum(powers, axis=-1, keepdims=True)
    attended = jnp.einsum(
        "gqk,kd->gqd", powers.astype(bfloat), value_all, preferred_element_type=single
    )
    attended = (attended / total).transpose(1, 0, 2).reshape(super_rows, 2 * HD).astype(bfloat)
    projected = quad_scatter(jnp.dot(attended, w_out, preferred_element_type=single))
    resid_mid = resid_in + norm_scale(projected, scales[1])
    normed_two = norm_scale(resid_mid, scales[2]).astype(bfloat)

    ffn_all = jnp.concatenate([ffn_pair, swap_core(ffn_pair)], axis=1)
    w_gate, w_up, w_down = ffn_all[0], ffn_all[1], ffn_all[2]
    ring_tokens = chips * tok_rows
    normed_ring = ring_gather(normed_two, chips, 2).reshape(ring_tokens, width)
    gate_part = jnp.einsum("td,rd->tr", normed_ring, w_gate, preferred_element_type=single)
    up_part = jnp.einsum("td,rd->tr", normed_ring, w_up, preferred_element_type=single)
    hidden = hidden_unit(gate_part, up_part).astype(bfloat)
    ffn_part = jnp.dot(hidden, w_down, preferred_element_type=single).astype(bfloat)
    ffn_acc = ring_scatter(ffn_part.reshape(chips, tok_rows, width), chips, 3)
    result = resid_mid + norm_scale(ffn_acc, scales[3])

    ignored, post_back = jax.vjp(norm_scale, ffn_acc, scales[3])
    d_ffn, d_gain3 = post_back(grad_out)
    d_ffn_ring = ring_gather(d_ffn.astype(bfloat), chips, 4).reshape(ring_tokens, width)
    d_hidden = jnp.einsum("td,rd->tr", d_ffn_ring, w_down, preferred_element_type=single)
    ignored, unit_back = jax.vjp(hidden_unit, gate_part, up_part)
    d_gate, d_up = unit_back(d_hidden)
    d_gate = d_gate.astype(bfloat)
    d_up = d_up.astype(bfloat)
    d_normed = jnp.dot(d_gate, w_gate, preferred_element_type=single)
    d_normed = (d_normed + jnp.dot(d_up, w_up, preferred_element_type=single)).astype(bfloat)
    d_normed_two = ring_scatter(d_normed.reshape(chips, tok_rows, width), chips, 5)

    def ffn_rows(left, right):
        return jnp.einsum("tr,td->rd", left, right, preferred_element_type=single)

    ffn_terms = jnp.stack(
        [ffn_rows(d_gate, normed_ring), ffn_rows(d_up, normed_ring), ffn_rows(hidden, d_ffn_ring)]
    )
    units = ffn_weight.shape[0]
    ffn_terms = ffn_terms.reshape(3, 2, 2, units, width)
    ffn_terms = ffn_terms[:, 0] + swap_core(ffn_terms[:, 1].astype(bfloat)).astype(single)
    grad_ffn = ffn_terms[:, 0] + swap_side(ffn_terms[:, 1].astype(bfloat)).astype(single)

    ignored, mid_back = jax.vjp(norm_scale, resid_mid, scales[2])
    d_mid_norm, d_gain2 = mid_back(d_normed_two)
    d_mid = grad_out + d_mid_norm
    ignored, proj_back = jax.vjp(norm_scale, projected, scales[1])
    d_projected, d_gain1 = proj_back(d_mid)
    d_proj_all = quad_gather(d_projected.astype(bfloat))
    d_attended = jnp.einsum("td,fd->tf", d_proj_all, w_out, preferred_element_type=single)
    d_attended = d_attended.astype(bfloat).reshape(super_rows, 2, HD)

    bent, powers = score_block()
    probs = powers / total
    d_probs = jnp.einsum("qgd,kd->gqk", d_attended, value_all, preferred_element_type=single)
    row_dot = jnp.sum(d_probs * probs, axis=-1, keepdims=True)
    d_raw = (probs * (d_probs - row_dot) * (1.0 - bent * bent)).astype(bfloat)
    d_query = jnp.einsum("gqk,kd->qgd", d_raw, key_all, preferred_element_type=single) * scale
    d_keys = jnp.einsum("gqk,qgd->kd", d_raw, query, preferred_element_type=single) * scale
    d_values = jnp.einsum(
        "gqk,qgd->kd", probs.astype(bfloat), d_attended, preferred_element_type=single
    )
    d_pieces = jnp.stack(
        [d_keys.reshape(chips, super_rows, HD), d_values.reshape(chips, super_rows, HD)], axis=1
    ).astype(bfloat)
    d_keyval = ring_scatter(d_pieces.reshape(chips, 2 * super_rows, HD), chips, 6)
    d_keyval = d_keyval.reshape(2, super_rows, HD).astype(bfloat)
    d_keyval = in_order(pick(d_keyval, side), swap_side(pick(d_keyval, 1 - side)), side, 1)
    d_query_raw = rotate(d_query, angles, -1.0).reshape(super_rows, 2 * HD).astype(bfloat)
    d_keyval_raw = rotate(d_keyval.astype(single), key_angles, -1.0)
    d_keyval_raw = d_keyval_raw.reshape(super_rows, 2 * HD).astype(bfloat)
    d_normed_one = jnp.dot(d_query_raw, w_query, preferred_element_type=single)
    d_normed_one = d_normed_one + jnp.dot(d_keyval_raw, w_keyval, preferred_element_type=single)
    d_normed_one = quad_scatter(d_normed_one)
    ignored, first_back = jax.vjp(norm_scale, resid_in, scales[0])
    d_in_norm, d_gain0 = first_back(d_normed_one)
    tokens_grad = d_mid + d_in_norm

    def attn_rows(left, right):
        rows = jnp.einsum("tf,td->fd", left, right, preferred_element_type=single).astype(bfloat)
        return rows.reshape(2, pairs, 2, share, width)

    term_query = attn_rows(d_query_raw, normed_all)
    term_keyval = attn_rows(d_keyval_raw, normed_all)
    term_out = attn_rows(attended, d_proj_all)

    def to_core(term, axis):
        return in_order(pick(term, core, 2), swap_core(pick(term, 1 - core, 2)), core, axis)

    terms = jnp.stack([to_core(term_query, 0), to_core(term_keyval, 1), to_core(term_out, 0)], axis=3)
    grad_attn = ring_scatter(terms.reshape(chips, 3 * share, width), chips, 7)
    grad_attn = grad_attn.reshape(3, share, width)
    term_gain = jnp.stack([d_gain0, d_gain1, d_gain2, d_gain3])
    grad_gain = lax.psum_scatter(term_gain, ("head", "fsdp"), scatter_dimension=1, tiled=True)

    gains_first_new, gains_second_new, gains_new = adamw(
        gains, gains_first, gains_second, grad_gain, rate_gain, 0.0
    )
    attn_first_new, attn_second_new, attn_weight_new = adamw(
        attn_weight, attn_first, attn_second, grad_attn, rate_matrix, decay_matrix
    )
    ffn_first_new, ffn_second_new, ffn_weight_new = adamw(
        ffn_weight, ffn_first, ffn_second, grad_ffn.transpose(1, 0, 2), rate_matrix, decay_matrix
    )
    return (
        result[None],
        tokens_grad[None],
        gains_first_new,
        gains_second_new,
        gains_new,
        attn_first_new,
        attn_second_new,
        attn_weight_new,
        ffn_first_new,
        ffn_second_new,
        ffn_weight_new,
    )


def per_device(
    tokens,
    cotangent,
    gains,
    gains_first,
    gains_second,
    attn_weight,
    attn_first,
    attn_second,
    ffn_weight,
    ffn_first,
    ffn_second,
):
    devices = lax.axis_size("fsdp")
    chips = devices // 2
    side = lax.axis_index("head")
    place = lax.axis_index("fsdp")
    chip = place // 2
    tok_rows = tokens.shape[1]
    super_rows = 4 * tok_rows
    seq_len = min(SEQ_LEN, super_rows * chips)
    share = attn_weight.shape[1]
    width = tokens.shape[2]
    gain_columns = gains.shape[1]
    gain_start = (side * devices + place) * gain_columns

    units = ffn_weight.shape[0]

    def flat(value):
        return value.transpose(1, 0, 2).reshape(3 * units, width)

    ffn_wide = flat(ffn_weight)
    resid_in = tokens[0]
    grad_out = cotangent[0]
    positions = chip * super_rows + jnp.arange(super_rows, dtype=jnp.int32)
    angles = turn_angles(positions % seq_len, HD)
    key_angles = jnp.where(side == 0, angles, 0.0)
    gains_placed = lax.dynamic_update_slice(
        jnp.zeros((4, width), single), gains, (0, gain_start)
    )
    turns = (jnp.cos(angles), jnp.sin(angles), jnp.cos(key_angles), jnp.sin(key_angles))
    made = front(attn_weight, gains_placed, resid_in, turns, ffn_wide, chips, 0)
    attn_rows, scales, normed_all, query, keyval, attended, inverse, projected = made[:8]
    own_units, core_units, side_units, diag_units = made[8:]
    result, d_mid, d_proj_low, gain_rows, terms_own, terms_other = feed_forward(
        resid_in,
        projected,
        grad_out,
        scales,
        (own_units, side_units, core_units, diag_units),
        chips,
        1,
    )
    grad_attn, tokens_grad, gain_total, terms_sent, terms_side = tail(
        d_proj_low,
        query,
        keyval,
        attended,
        inverse,
        attn_rows,
        normed_all,
        turns,
        (resid_in, d_mid, scales, gain_rows),
        terms_own,
        terms_other,
        chips,
        2,
    )
    grad_ffn = terms_own[0].astype(single) + terms_other[0].astype(single)
    grad_ffn = grad_ffn + terms_side.astype(single)
    grad_attn = grad_attn.reshape(3, share, width)
    grad_gain = lax.dynamic_slice(gain_total, (0, gain_start), gains.shape)

    gains_first_new, gains_second_new, gains_new = adamw(
        gains, gains_first, gains_second, grad_gain, rate_gain, 0.0
    )
    attn_first_new, attn_second_new, attn_weight_new = adamw(
        attn_weight, attn_first, attn_second, grad_attn, rate_matrix, decay_matrix
    )
    ffn_first_new, ffn_second_new, ffn_weight_new = (
        value.reshape(3, units, width).transpose(1, 0, 2)
        for value in adamw(
            ffn_wide, flat(ffn_first), flat(ffn_second), grad_ffn, rate_matrix, decay_matrix
        )
    )
    return (
        result[None],
        tokens_grad[None],
        gains_first_new,
        gains_second_new,
        gains_new,
        attn_first_new,
        attn_second_new,
        attn_weight_new,
        ffn_first_new,
        ffn_second_new,
        ffn_weight_new,
    )


def solution(mesh):
    by_token = P("fsdp", "head", None)
    by_column = P(None, ("head", "fsdp"))
    by_row = P(None, ("head", "fsdp"), None)
    by_unit = P(("head", "fsdp"), None, None)
    placed = (by_token,) * 2 + (by_column,) * 3 + (by_row,) * 3 + (by_unit,) * 3
    body = per_device if mesh.shape["fsdp"] == 16 else general_device
    return jax.shard_map(
        body, mesh=mesh, in_specs=placed, out_specs=placed, check_vma=False
    )
```

```python
import functools
import math

import jax
import jax.numpy as jnp
from jax import lax
from jax.experimental import pallas as pl
from jax.experimental.pallas import tpu as pltpu
from jax.sharding import PartitionSpec as P

HQ = 8
HK = 4
HD = 256
WIN = 4096
STEP = 10
SEQ_LEN = 8192


eps_norm = 1e-06
softcap = 50.0
beta_one = 0.9
beta_two = 0.95
adam_eps = 1e-08
rate_matrix = 0.02
rate_gain = 0.2
decay_matrix = 0.1

bfloat = jnp.bfloat16
single = jnp.float32
MESH = pl.DeviceIdType.MESH


def norm_scale(values, scales):
    return (
        values
        * lax.rsqrt(jnp.mean(values * values, axis=-1, keepdims=True) + eps_norm)
        * (1.0 + scales)
    )


def turn_angles(positions, head_width):
    halfway = head_width // 2
    inverse_freq = 10000.0 ** (-(jnp.arange(halfway, dtype=jnp.float32) * 2.0) / head_width)
    return positions.astype(jnp.float32)[:, None] * inverse_freq[None, :]


def rotate(values, angles, direction):
    halfway = values.shape[-1] // 2
    cosine = jnp.cos(angles)[:, None, :]
    sine_part = direction * jnp.sin(angles)[:, None, :]
    former = values[..., :halfway]
    latter = values[..., halfway:]
    return jnp.concatenate(
        [former * cosine - latter * sine_part, latter * cosine + former * sine_part], axis=-1
    )


def adamw(weight, moment, second, gradient, step_rate, decay_rate):
    moment = beta_one * moment + (1.0 - beta_one) * gradient
    second = beta_two * second + (1.0 - beta_two) * gradient * gradient
    update = (
        moment / (1.0 - beta_one**STEP) / (jnp.sqrt(second / (1.0 - beta_two**STEP)) + adam_eps)
        + decay_rate * weight
    )
    return (moment, second, weight - step_rate * update)


def hidden_unit(gate_part, up_part):
    return jax.nn.gelu(gate_part, approximate=True) * up_part


def ring_of(chip, chips):
    wide = chips // 4
    deep, side = chip // wide, chip % wide
    return side * 4 + deep + (side % 2) * (3 - 2 * deep)


def chip_of(ring, chips):
    wide = chips // 4
    side, along = ring // 4, ring % 4
    return (along + (side % 2) * (3 - 2 * along)) * wide + side


def ring_places(chips):
    index = lax.axis_index("fsdp")
    core, chip = index % 2, index // 2
    ring = ring_of(chip, chips)
    right = 2 * chip_of((ring + 1) % chips, chips) + core
    left = 2 * chip_of((ring + chips - 1) % chips, chips) + core
    return chip, ring, right, left


def ring_barrier(right, left):
    barrier = pltpu.get_barrier_semaphore()
    for neighbour in (left, right):
        pl.semaphore_signal(barrier, inc=1, device_id={"fsdp": neighbour}, device_id_type=MESH)
    pl.semaphore_wait(barrier, 2)


def region(shape, pieces, way, piece):
    rows, columns = shape
    if rows % 32 == 0:
        size = rows // 2 // pieces
        start = way * (rows // 2) + piece * size
        return (pl.ds(start, size), pl.ds(0, columns)), (pl.ds(piece * size, size), pl.ds(0, columns))
    size = columns // 2
    return (pl.ds(0, rows), pl.ds(way * size, size)), (pl.ds(0, rows), pl.ds(0, size))


def half_shape(rows, columns):
    return (rows // 2, columns) if rows % 32 == 0 else (rows, columns // 2)


def gather_kernel(chips, pieces, own_ref, all_ref, local_sem, send_sem, recv_sem):
    chip, ring, right, left = ring_places(chips)
    ring_barrier(right, left)
    keep = pltpu.make_async_copy(own_ref, all_ref.at[chip], local_sem)
    keep.start()

    def copy(way, step, piece, first):
        owner = chip_of((ring + (chips - step if way == 0 else step)) % chips, chips)
        part, ignored = region(own_ref.shape, pieces, way, piece)
        there = all_ref.at[(owner,) + part]
        return pltpu.make_async_remote_copy(
            src_ref=own_ref.at[part] if first else there,
            dst_ref=there,
            send_sem=send_sem.at[way, piece, step],
            recv_sem=recv_sem.at[way, piece, step],
            device_id={"fsdp": right if way == 0 else left},
            device_id_type=MESH,
        )

    streams = [(way, piece) for piece in range(pieces) for way in range(2)]
    for way, piece in streams:
        copy(way, 0, piece, True).start()

    def body(step, carried):
        for way, piece in streams:
            copy(way, step - 1, piece, False).wait_recv()
            copy(way, step, piece, False).start()
        return carried

    lax.fori_loop(1, chips - 1, body, 0)
    for way, piece in streams:
        copy(way, chips - 2, piece, False).wait_recv()

    def finish(step, carried):
        for way, piece in streams:
            copy(way, step, piece, False).wait_send()
        return carried

    lax.fori_loop(0, chips - 1, finish, 0)
    keep.wait()


def ring_gather(own, chips, ident):
    rows, columns = own.shape
    pieces = 2 if rows % 64 == 0 else 1
    return pl.pallas_call(
        functools.partial(gather_kernel, chips, pieces),
        out_shape=jax.ShapeDtypeStruct((chips, rows, columns), own.dtype),
        in_specs=[pl.BlockSpec(memory_space=pl.ANY)],
        out_specs=pl.BlockSpec(memory_space=pl.ANY),
        scratch_shapes=[
            pltpu.SemaphoreType.DMA,
            pltpu.SemaphoreType.DMA((2, pieces, chips - 1)),
            pltpu.SemaphoreType.DMA((2, pieces, chips - 1)),
        ],
        compiler_params=pltpu.CompilerParams(collective_id=ident, has_side_effects=True),
        cost_estimate=cost(45),
    )(own)


def scatter_kernel(chips, pieces, parts_ref, sum_ref, held, send_sem, recv_sem):
    chip, ring, right, left = ring_places(chips)
    ring_barrier(right, left)

    def owner_of(way, step):
        shift = chips - 1 - step if way == 0 else 1 + step
        return chip_of((ring + shift) % chips, chips)

    def copy(way, step, piece, first):
        part, place = region(sum_ref.shape, pieces, way, piece)
        return pltpu.make_async_remote_copy(
            src_ref=(
                parts_ref.at[(owner_of(way, step),) + part]
                if first
                else held.at[(way, step - 1) + place]
            ),
            dst_ref=held.at[(way, step) + place],
            send_sem=send_sem.at[way, piece, step],
            recv_sem=recv_sem.at[way, piece, step],
            device_id={"fsdp": right if way == 0 else left},
            device_id_type=MESH,
        )

    streams = [(way, piece) for piece in range(pieces) for way in range(2)]
    for way, piece in streams:
        copy(way, 0, piece, True).start()

    def arrived(way, step, piece):
        copy(way, step, piece, True).wait_recv()
        part, place = region(sum_ref.shape, pieces, way, piece)
        here = parts_ref[(owner_of(way, step + 1),) + part]
        return held[(way, step) + place].astype(single) + here.astype(single)

    def body(step, carried):
        for way, piece in streams:
            total = arrived(way, step - 1, piece)
            part, place = region(sum_ref.shape, pieces, way, piece)
            held[(way, step - 1) + place] = total.astype(held.dtype)
            copy(way, step, piece, False).start()
        return carried

    lax.fori_loop(1, chips - 1, body, 0)
    for way, piece in streams:
        part, place = region(sum_ref.shape, pieces, way, piece)
        sum_ref[part] = arrived(way, chips - 2, piece)

    def finish(step, carried):
        for way, piece in streams:
            copy(way, step, piece, True).wait_send()
        return carried

    lax.fori_loop(0, chips - 1, finish, 0)


def ring_scatter(parts, chips, ident):
    rows, columns = parts.shape[1:]
    pieces = 2 if rows % 64 == 0 else 1
    return pl.pallas_call(
        functools.partial(scatter_kernel, chips, pieces),
        out_shape=jax.ShapeDtypeStruct((rows, columns), single),
        in_specs=[pl.BlockSpec(memory_space=pltpu.VMEM)],
        out_specs=pl.BlockSpec(memory_space=pltpu.VMEM),
        scratch_shapes=[
            pltpu.VMEM((2, chips - 1) + half_shape(rows, columns), parts.dtype),
            pltpu.SemaphoreType.DMA((2, pieces, chips - 1)),
            pltpu.SemaphoreType.DMA((2, pieces, chips - 1)),
        ],
        compiler_params=pltpu.CompilerParams(
            collective_id=ident, has_side_effects=True, vmem_limit_bytes=56 * 2**20
        ),
        cost_estimate=cost(45),
    )(parts)


def norm_back(values, scales, grad):
    inverse = lax.rsqrt(jnp.mean(values * values, axis=-1, keepdims=True) + eps_norm)
    bent = grad * (1.0 + scales)
    slope = jnp.mean(bent * values, axis=-1, keepdims=True) * (inverse * inverse * inverse)
    return bent * inverse - values * slope, jnp.sum(grad * values * inverse, axis=0, keepdims=True)


def gelu_parts(gate):
    root = math.sqrt(2.0 / math.pi)
    square = gate * gate
    bend = jnp.tanh(root * gate * (1.0 + 0.044715 * square))
    half = 0.5 * (1.0 + bend)
    slope = half + 0.5 * gate * (1.0 - bend * bend) * (root * (1.0 + 3.0 * 0.044715 * square))
    return gate * half, slope


def dot_nt(left, right):
    return lax.dot_general(left, right, (((1,), (1,)), ((), ())), preferred_element_type=single)


def dot_nn(left, right):
    return lax.dot_general(left, right, (((1,), (0,)), ((), ())), preferred_element_type=single)


def dot_tn(left, right):
    return lax.dot_general(left, right, (((0,), (0,)), ((), ())), preferred_element_type=single)


class Ring:
    def __init__(self, chips, pieces, rows, send_sem, recv_sem):
        self.chips, self.pieces, self.half = chips, pieces, rows // 2
        self.size = rows // 2 // pieces
        self.chip, self.ring, self.right, self.left = ring_places(chips)
        self.send_sem, self.recv_sem = send_sem, recv_sem
        self.streams = [(way, piece) for piece in range(pieces) for way in range(2)]

    def owner(self, way, step):
        shift = self.chips - step if way == 0 else step
        return chip_of((self.ring + shift) % self.chips, self.chips)

    def copy(self, source, target, way, piece, step):
        return pltpu.make_async_remote_copy(
            src_ref=source,
            dst_ref=target,
            send_sem=self.send_sem.at[way, piece, step],
            recv_sem=self.recv_sem.at[way, piece, step],
            device_id={"fsdp": self.right if way == 0 else self.left},
            device_id_type=MESH,
        )

    def part(self, way, piece):
        return pl.ds(way * self.half + piece * self.size, self.size)

    def place(self, piece):
        return pl.ds(piece * self.size, self.size)

    def gather_copy(self, all_ref, way, piece, step):
        there = all_ref.at[self.owner(way, step), self.part(way, piece)]
        return self.copy(there, there, way, piece, step)

    def of(self, only):
        return [(way, piece) for way, piece in self.streams if only is None or piece == only]

    def gather_step(self, all_ref, step, only=None):
        for way, piece in self.of(only):

            @pl.when(step > 0)
            def _():
                self.gather_copy(all_ref, way, piece, step - 1).wait_recv()

            @pl.when(step < self.chips - 1)
            def _():
                self.gather_copy(all_ref, way, piece, step).start()

    def scatter_copy(self, parts_ref, held, way, piece, step, first):
        source = (
            parts_ref.at[self.owner(way, step + 1), self.part(way, piece)]
            if first
            else held.at[way, step - 1, self.place(piece)]
        )
        return self.copy(source, held.at[way, step, self.place(piece)], way, piece, step)

    def scatter_total(self, parts_ref, held, way, piece, step):
        self.scatter_copy(parts_ref, held, way, piece, step, True).wait_recv()
        here = parts_ref[self.owner(way, step + 2), self.part(way, piece)]
        return held[way, step, self.place(piece)].astype(single) + here.astype(single)

    def scatter_step(self, parts_ref, held, step, only=None):
        for way, piece in self.of(only):

            @pl.when(step == 0)
            def _():
                self.scatter_copy(parts_ref, held, way, piece, 0, True).start()

            @pl.when(step > 0)
            def _():
                total = self.scatter_total(parts_ref, held, way, piece, step - 1)
                held[way, step - 1, self.place(piece)] = total.astype(held.dtype)
                self.scatter_copy(parts_ref, held, way, piece, step, False).start()

    def scatter_end(self, parts_ref, held, sum_ref):
        for way, piece in self.streams:
            sum_ref[self.part(way, piece)] = self.scatter_total(
                parts_ref, held, way, piece, self.chips - 2
            )

    def finish(self, example):
        def body(step, carried):
            for way, piece in self.streams:
                self.copy(example, example, way, piece, step).wait_send()
            return carried

        lax.fori_loop(0, self.chips - 1, body, 0)


def quad_peers(chips):
    side = lax.axis_index("head")
    index = lax.axis_index("fsdp")
    chip, core = index // 2, index % 2
    ring = ring_of(chip, chips)
    around = [2 * chip_of((ring + hop) % chips, chips) + core for hop in range(1, chips)]
    return side, core, {"head": 1 - side}, {"fsdp": 2 * chip + 1 - core}, around


def wide_barrier(to_side, to_core, around):
    barrier = pltpu.get_barrier_semaphore()
    for target in [to_side, to_core] + [{"fsdp": other} for other in around]:
        pl.semaphore_signal(barrier, inc=1, device_id=target, device_id_type=MESH)
    pl.semaphore_wait(barrier, 2 + len(around))


def quad_barrier(to_side, to_core, right, left):
    barrier = pltpu.get_barrier_semaphore()
    for target in (to_side, to_core, {"fsdp": right}, {"fsdp": left}):
        pl.semaphore_signal(barrier, inc=1, device_id=target, device_id_type=MESH)
    pl.semaphore_wait(barrier, 4)


def remote(source, target, send_sem, recv_sem, device):
    return pltpu.make_async_remote_copy(
        src_ref=source,
        dst_ref=target,
        send_sem=send_sem,
        recv_sem=recv_sem,
        device_id=device,
        device_id_type=MESH,
    )


class Total:
    def __init__(self, value, near, blocks, send_sem, recv_sem, peers, chip):
        self.value, self.near, self.blocks = value, near, blocks
        self.send_sem, self.recv_sem = send_sem, recv_sem
        side, core, self.to_side, self.to_core, self.around = peers
        self.chip = chip
        self.first = remote(value.at[0], near.at[0], send_sem.at[0], recv_sem.at[0], self.to_side)
        self.second = remote(value.at[1], near.at[1], send_sem.at[1], recv_sem.at[1], self.to_core)

    def spread(self, hop):
        here = self.blocks.at[self.chip]
        return remote(
            here,
            here,
            self.send_sem.at[1 + hop],
            self.recv_sem.at[1 + hop],
            {"fsdp": self.around[hop - 1]},
        )

    def start(self):
        self.first.start()

    def over_cores(self):
        self.first.wait_recv()
        self.value[1] = self.value[0] + self.near[0]
        self.second.start()

    def over_ring(self):
        self.second.wait_recv()
        self.blocks[self.chip] = self.value[1] + self.near[1]
        for hop in range(1, len(self.around) + 1):
            self.spread(hop).start()

    def end(self):
        for hop in range(1, len(self.around) + 1):
            self.spread(hop).wait_recv()
        total = self.blocks[0]
        for other in range(1, len(self.around) + 1):
            total = total + self.blocks[other]
        self.first.wait_send()
        self.second.wait_send()
        for hop in range(1, len(self.around) + 1):
            self.spread(hop).wait_send()
        return total


def total_scratch(chips, width):
    return [
        pltpu.VMEM((2, 4, width), single),
        pltpu.VMEM((2, 4, width), single),
        pltpu.VMEM((chips, 4, width), single),
        pltpu.SemaphoreType.DMA((chips + 1,)),
        pltpu.SemaphoreType.DMA((chips + 1,)),
    ]


def turn(raw, cosine, sine):
    halfway = raw.shape[1] // 2
    former, latter = raw[:, :halfway], raw[:, halfway:]
    return jnp.concatenate(
        [former * cosine - latter * sine, latter * cosine + former * sine], axis=1
    )


def front_kernel(
    chips,
    cuts,
    own_ref,
    gains_ref,
    resid_ref,
    cosine_ref,
    sine_ref,
    key_cosine_ref,
    key_sine_ref,
    wide_units_ref,
    rows_out,
    scales_ref,
    normed_out,
    query_ref,
    keyval_out,
    attended_ref,
    inverse_ref,
    projected_ref,
    own_units_ref,
    core_units_ref,
    side_units_ref,
    diag_units_ref,
    rows_ref,
    normed_ref,
    keyval_ref,
    all_rows,
    both,
    total,
    sums,
    product,
    across_put,
    across_got,
    along_put,
    along_got,
    cast_in,
    cast_out,
    value,
    near,
    blocks,
    total_send,
    total_recv,
    send_sem,
    recv_sem,
    place_sem,
    peer_sem,
    key_send,
    key_recv,
    quad_send,
    quad_recv,
    cast_sem,
    out_sem,
    bulk_send,
    bulk_recv,
):
    share, width = own_ref.shape[1:]
    tok_rows = resid_ref.shape[0]
    tokens = 4 * tok_rows
    half = width // 2
    pairs = chips // 4
    scale = 1.0 / math.sqrt(HD)
    chip, ring, right, left = ring_places(chips)
    peers = quad_peers(chips)
    side, core, to_side, to_core, around = peers
    cast_rows = cast_in.shape[1]
    casts = wide_units_ref.shape[0] // cast_rows

    def cast_load(tile):
        rows = pl.ds(tile * cast_rows, cast_rows)
        return pltpu.make_async_copy(
            wide_units_ref.at[rows], cast_in.at[tile % 2], cast_sem.at[0, tile % 2]
        )

    def cast_store(tile):
        rows = pl.ds(tile * cast_rows, cast_rows)
        return pltpu.make_async_copy(
            cast_out.at[tile % 2], own_units_ref.at[rows], cast_sem.at[1, tile % 2]
        )

    def cast(first, last):
        for tile in range(first, last):
            cast_load(tile).wait()
            if tile >= 3:
                cast_store(tile - 2).wait()
            cast_out[tile % 2] = cast_in[tile % 2].astype(bfloat)
            cast_store(tile).start()
            if tile + 2 < casts:
                cast_load(tile + 2).start()

    outs = [
        pltpu.make_async_copy(rows_ref.at[0:2], rows_out.at[0:2], out_sem.at[0]),
        pltpu.make_async_copy(rows_ref.at[2], rows_out.at[2], out_sem.at[1]),
        pltpu.make_async_copy(normed_ref, normed_out, out_sem.at[2]),
        pltpu.make_async_copy(keyval_ref, keyval_out, out_sem.at[3]),
    ]
    cast_load(0).start()
    cast_load(1).start()
    all_rows[chip] = own_ref[...].astype(bfloat)
    value[0] = gains_ref[...].astype(bfloat).astype(single)
    wide_barrier(to_side, to_core, around)
    gains_total = Total(value, near, blocks, total_send, total_recv, peers, chip)
    gains_total.start()
    streams = [(way, slot) for slot in range(2) for way in range(2)]
    out_streams = [(way, 2) for way in range(2)]
    key_streams = [(way, kind) for kind in range(2) for way in range(2)]

    def owner_of(way, step):
        return chip_of((ring + (chips - step if way == 0 else step)) % chips, chips)

    def hop(way, slot, step):
        there = all_rows.at[owner_of(way, step), slot, :, pl.ds(way * half, half)]
        return remote(
            there,
            there,
            send_sem.at[way, slot, step],
            recv_sem.at[way, slot, step],
            {"fsdp": right if way == 0 else left},
        )

    def key_hop(way, kind, step):
        there = keyval_ref.at[owner_of(way, step), kind, pl.ds(way * (tokens // 2), tokens // 2)]
        return remote(
            there,
            there,
            key_send.at[way, kind, step],
            key_recv.at[way, kind, step],
            {"fsdp": right if way == 0 else left},
        )

    def goal(way, slot, step):
        owner = owner_of(way, step)
        deep = owner // pairs
        unit = (owner % pairs) * 2 + core
        taker, head = (deep % 2, deep // 2) if slot == 1 else (deep // 2, deep % 2)
        columns = pl.ds(way * half, half)
        source = all_rows.at[owner, slot, :, columns]
        start = pl.multiple_of(head * HD + unit * share, share)
        target = rows_ref.at[slot, pl.ds(start, share), columns]
        sem = place_sem.at[way, slot, step]

        def here():
            return pltpu.make_async_copy(source, target, sem)

        def there():
            return remote(source, target, sem, peer_sem.at[way, slot, step], to_core)

        return taker, here, there

    def place(way, slot, step):
        taker, here, there = goal(way, slot, step)

        @pl.when(taker == core)
        def _():
            here().start()

        @pl.when(taker != core)
        def _():
            there().start()

    def placed(way, slot, step):
        taker, here, there = goal(way, slot, step)

        @pl.when(taker == core)
        def _():
            here().wait()
            there().wait_recv()

        @pl.when(taker != core)
        def _():
            there().wait_send()

    def pass_on(which, step):
        for way, slot in which:

            @pl.when(step > 0)
            def _():
                hop(way, slot, step - 1).wait_recv()

            @pl.when(step < chips - 1)
            def _():
                hop(way, slot, step).start()

            place(way, slot, step)

    def settle(which):
        def body(step, carried):
            for way, slot in which:
                placed(way, slot, step)

                @pl.when(step < chips - 1)
                def _():
                    hop(way, slot, step).wait_send()

            return carried

        lax.fori_loop(0, chips, body, 0)

    def quad_copy(source, target, index, device):
        return remote(source, target, quad_send.at[index], quad_recv.at[index], device)

    mine = normed_ref.at[core, side]
    along = quad_copy(mine, mine, 0, to_side)
    across = quad_copy(normed_ref.at[core], normed_ref.at[core], 1, to_core)

    def bulk_side(part):
        rows = pl.ds(cuts[part], cuts[part + 1] - cuts[part])
        return remote(
            own_units_ref.at[rows],
            side_units_ref.at[rows],
            bulk_send.at[part],
            bulk_recv.at[part],
            to_side,
        )

    def bulk_diag(part):
        rows = pl.ds(cuts[part], cuts[part + 1] - cuts[part])
        return remote(
            side_units_ref.at[rows],
            diag_units_ref.at[rows],
            bulk_send.at[3 + part],
            bulk_recv.at[3 + part],
            to_core,
        )

    bulk_core = remote(own_units_ref, core_units_ref, bulk_send.at[6], bulk_recv.at[6], to_core)
    for way, slot in streams:
        hop(way, slot, 0).start()
    cast(0, 1)
    cast_store(0).wait()
    bulk_side(0).start()
    gains_total.over_cores()
    for way, slot in streams:
        place(way, slot, 0)
    gains_total.over_ring()
    pass_on(streams, 1)
    cast(1, 3)
    scales_ref[...] = gains_total.end()
    normed_ref[core, side] = norm_scale(resid_ref[...], scales_ref[0:1]).astype(bfloat)
    along.start()
    pass_on(streams, 2)
    cast(3, 5)
    pass_on(streams, 3)
    cast(5, 7)
    along.wait()
    across.start()
    bulk_side(1).start()
    pass_on(streams, 4)
    cast(7, casts)
    cast_store(casts - 2).wait()
    cast_store(casts - 1).wait()
    bulk_core.start()

    def body(step, carried):
        pass_on(streams, step)
        return carried

    lax.fori_loop(5, chips, body, 0)
    pass_on(out_streams, 0)
    across.wait()
    outs[2].start()
    settle(streams)
    outs[0].start()

    def project(slot, head):
        rows = slice(head * HD, head * HD + HD)
        return dot_nt(normed_ref[...].reshape(tokens, width), rows_ref[slot, rows])

    for head in range(2):
        raw = project(1, head)
        both[head] = turn(raw, key_cosine_ref[...], key_sine_ref[...]).astype(bfloat)
    swap = quad_copy(both.at[1 - side], keyval_ref.at[chip, side], 2, to_side)
    swap.start()
    bulk_side(2).start()
    for part in range(2):
        bulk_side(part).wait_recv()
        bulk_diag(part).start()
    pass_on(out_streams, 1)
    keyval_ref[chip, side] = both[side]
    for head in range(2):
        raw = project(0, head)
        query_ref[head] = turn(raw, cosine_ref[...], sine_ref[...]).astype(bfloat)
        pass_on(out_streams, 2 + head)
    total[...] = jnp.zeros_like(total)
    sums[...] = jnp.zeros_like(sums)
    swap.wait()

    def block(way, owner):
        part = tokens // 2
        key = keyval_ref[owner, 0, way * part : way * part + part]
        val = keyval_ref[owner, 1, way * part : way * part + part]
        row = lax.broadcasted_iota(jnp.int32, (tokens, part), 0)
        column = lax.broadcasted_iota(jnp.int32, (tokens, part), 1)
        allowed = row + (chip - owner) * tokens - way * part >= column

        def one_head(head, carried):
            bent = jnp.tanh(dot_nt(query_ref[head], key) * (scale / softcap))
            powers = jnp.where(allowed, jnp.exp(softcap * bent), 0.0)
            sums[head] += powers[:, : part // 2] + powers[:, part // 2 :]
            total[head] += dot_nn(powers.astype(bfloat), val)
            return carried

        for head in range(2):
            one_head(head, 0)

    def key_body(step, carried):
        for way, kind in key_streams:

            @pl.when(step > 0)
            def _():
                key_hop(way, kind, step - 1).wait_recv()

            @pl.when(step < chips - 1)
            def _():
                key_hop(way, kind, step).start()

        for way in range(2):
            owner = owner_of(way, step)

            @pl.when(owner <= chip)
            def _():
                block(way, owner)

            if way == 0:

                @pl.when(step < chips - 4)
                def _():
                    pass_on(out_streams, step + 4)

        return carried

    lax.fori_loop(0, chips, key_body, 0)
    outs[3].start()
    bulk_side(2).wait_recv()
    bulk_diag(2).start()
    settle(out_streams)
    outs[1].start()
    for head in range(2):
        inverse = 1.0 / jnp.sum(sums[head], axis=-1, keepdims=True)
        inverse_ref[head] = jnp.broadcast_to(inverse, inverse_ref.shape[1:])
        attended_ref[:, head * HD : head * HD + HD] = (total[head] * inverse).astype(bfloat)
    span = width // 3
    tiles = [slice(tile * span, tile * span + span) for tile in range(3)]

    def project_out(part, ref, columns):
        first = pl.ds(pl.multiple_of(part * 2 * tok_rows, 2 * tok_rows), 2 * tok_rows)
        made = dot_nn(attended_ref[first], rows_ref[2, :, columns])
        ref[:, :, columns] = made.reshape(2, tok_rows, span).astype(ref.dtype)

    across = [
        quad_copy(across_put.at[:, :, columns], across_got.at[:, :, columns], 3 + tile, to_core)
        for tile, columns in enumerate(tiles)
    ]
    along = [
        quad_copy(along_put.at[:, columns], along_got.at[:, columns], 6 + tile, to_side)
        for tile, columns in enumerate(tiles)
    ]
    for tile, columns in enumerate(tiles):
        project_out(1 - core, across_put, columns)
        across[tile].start()
        project_out(core, product, columns)
    for tile, columns in enumerate(tiles):
        across[tile].wait()
        given = product[1 - side, :, columns] + across_got[1 - side, :, columns].astype(single)
        along_put[:, columns] = given.astype(bfloat)
        along[tile].start()

    def key_settle(step, carried):
        for way, kind in key_streams:
            key_hop(way, kind, step).wait_send()
        return carried

    lax.fori_loop(0, chips - 1, key_settle, 0)
    for out in outs:
        out.wait()
    bulk_core.wait()
    for part in range(3):
        bulk_side(part).wait_send()
        bulk_diag(part).wait()
    for tile, columns in enumerate(tiles):
        along[tile].wait()
        kept = product[side, :, columns] + across_got[side, :, columns].astype(single)
        projected_ref[:, columns] = kept + along_got[:, columns].astype(single)


def cost(micros):
    return pl.CostEstimate(flops=int(micros * 1e9), bytes_accessed=0, transcendentals=0)


def front(attn_weight, gains, resid_in, turns, ffn_wide, chips, ident):
    share, width = attn_weight.shape[1:]
    tok_rows = resid_in.shape[0]
    tokens = 4 * tok_rows
    units = ffn_wide.shape[0]
    cuts = (0, units // 9, units // 3, 2 * units // 3)
    vmem = pl.BlockSpec(memory_space=pltpu.VMEM)
    anywhere = pl.BlockSpec(memory_space=pl.ANY)
    return pl.pallas_call(
        functools.partial(front_kernel, chips, cuts),
        out_shape=(
            jax.ShapeDtypeStruct((3, 2 * HD, width), bfloat),
            jax.ShapeDtypeStruct((4, width), single),
            jax.ShapeDtypeStruct((2, 2, tok_rows, width), bfloat),
            jax.ShapeDtypeStruct((2, tokens, HD), bfloat),
            jax.ShapeDtypeStruct((chips, 2, tokens, HD), bfloat),
            jax.ShapeDtypeStruct((tokens, 2 * HD), bfloat),
            jax.ShapeDtypeStruct((2, tokens, 128), single),
            jax.ShapeDtypeStruct((tok_rows, width), single),
        )
        + (jax.ShapeDtypeStruct((units, width), bfloat),) * 2
        + (jax.ShapeDtypeStruct((2 * units // 3, width), bfloat),) * 2,
        in_specs=[vmem] * 7 + [anywhere],
        out_specs=(anywhere, vmem, anywhere, vmem, anywhere, vmem, vmem, vmem) + (anywhere,) * 4,
        scratch_shapes=[
            pltpu.VMEM((3, 2 * HD, width), bfloat),
            pltpu.VMEM((2, 2, tok_rows, width), bfloat),
            pltpu.VMEM((chips, 2, tokens, HD), bfloat),
            pltpu.VMEM((chips, 3, share, width), bfloat),
            pltpu.VMEM((2, tokens, HD), bfloat),
            pltpu.VMEM((2, tokens, HD), single),
            pltpu.VMEM((2, tokens, 128), single),
            pltpu.VMEM((2, tok_rows, width), single),
            pltpu.VMEM((2, tok_rows, width), bfloat),
            pltpu.VMEM((2, tok_rows, width), bfloat),
            pltpu.VMEM((tok_rows, width), bfloat),
            pltpu.VMEM((tok_rows, width), bfloat),
            pltpu.VMEM((2, units // 9, width), single),
            pltpu.VMEM((2, units // 9, width), bfloat),
        ]
        + total_scratch(chips, width)
        + [
            pltpu.SemaphoreType.DMA((2, 3, chips - 1)),
            pltpu.SemaphoreType.DMA((2, 3, chips - 1)),
            pltpu.SemaphoreType.DMA((2, 3, chips)),
            pltpu.SemaphoreType.DMA((2, 3, chips)),
            pltpu.SemaphoreType.DMA((2, 2, chips - 1)),
            pltpu.SemaphoreType.DMA((2, 2, chips - 1)),
            pltpu.SemaphoreType.DMA((9,)),
            pltpu.SemaphoreType.DMA((9,)),
            pltpu.SemaphoreType.DMA((2, 2)),
            pltpu.SemaphoreType.DMA((4,)),
            pltpu.SemaphoreType.DMA((7,)),
            pltpu.SemaphoreType.DMA((7,)),
        ],
        compiler_params=pltpu.CompilerParams(
            collective_id=ident, has_side_effects=True, vmem_limit_bytes=60 * 2**20
        ),
        cost_estimate=cost(140),
    )(attn_weight, gains, resid_in, *turns, ffn_wide)


def tail_kernel(
    chips,
    d_proj_ref,
    query_ref,
    keyval_in,
    attended_ref,
    inverse_ref,
    rows_in,
    normed_in,
    cosine_ref,
    sine_ref,
    key_cosine_ref,
    key_sine_ref,
    resid_ref,
    d_mid_ref,
    scales_ref,
    gains_ref,
    units_own_ref,
    units_other_ref,
    sum_ref,
    tokens_ref,
    total_ref,
    units_ref,
    units_got_ref,
    keyval_ref,
    rows_ref,
    normed_ref,
    d_all,
    d_out,
    delta,
    d_query,
    d_block,
    first_put,
    held_keys,
    swapped,
    d_raw,
    out_rows,
    parts,
    out_parts,
    held,
    out_held,
    across_got,
    along_put,
    along_got,
    value,
    near,
    blocks,
    total_send,
    total_recv,
    key_send,
    key_recv,
    place_sem,
    peer_sem,
    send_sem,
    recv_sem,
    out_send,
    out_recv,
    quad_send,
    quad_recv,
    load_sem,
    bulk_send,
    bulk_recv,
):
    tokens = query_ref.shape[1]
    half = tokens // 2
    width = resid_ref.shape[1]
    share = out_parts.shape[1]
    pairs = chips // 4
    scale = 1.0 / math.sqrt(HD)
    peers = quad_peers(chips)
    side, core, to_side, to_core, around = peers
    ring = Ring(chips, 2, 2 * share, send_sem, recv_sem)
    out_ring = Ring(chips, 1, share, out_send, out_recv)
    chip = ring.chip
    gains_total = Total(value, near, blocks, total_send, total_recv, peers, chip)
    arrays = [
        pltpu.make_async_copy(rows_in.at[2], rows_ref.at[2], load_sem.at[3]),
        pltpu.make_async_copy(keyval_in, keyval_ref, load_sem.at[4]),
        pltpu.make_async_copy(normed_in, normed_ref, load_sem.at[5]),
        pltpu.make_async_copy(rows_in.at[0:2], rows_ref.at[0:2], load_sem.at[6]),
    ]
    d_all[core, side] = d_proj_ref[...]
    wide_barrier(to_side, to_core, around)

    def quad_copy(source, target, index, device):
        return remote(source, target, quad_send.at[index], quad_recv.at[index], device)

    def bulk(kind):
        return remote(
            units_ref.at[pl.ds(kind * (units_ref.shape[0] // 3), units_ref.shape[0] // 3)],
            units_got_ref.at[pl.ds(kind * (units_ref.shape[0] // 3), units_ref.shape[0] // 3)],
            bulk_send.at[kind],
            bulk_recv.at[kind],
            to_side,
        )

    units = units_ref.shape[0]
    ours = out_rows.reshape(6 * HD, width).at[pl.ds(0, units)]
    theirs = parts.reshape(2 * chips * share, width).at[pl.ds(0, units)]
    loads = (
        pltpu.make_async_copy(units_own_ref.at[1], ours, load_sem.at[0]),
        pltpu.make_async_copy(units_other_ref.at[1], theirs, load_sem.at[1]),
    )
    store = pltpu.make_async_copy(ours, units_ref, load_sem.at[2])
    for load in loads:
        load.start()
    for array in arrays:
        array.start()
    quarter = tokens // 8
    halves = [slice(part * quarter, part * quarter + quarter) for part in range(2)]
    along = [
        quad_copy(d_all.at[core, side, rows], d_all.at[core, side, rows], part, to_side)
        for part, rows in enumerate(halves)
    ]
    across = quad_copy(d_all.at[core, side], d_all.at[core, side], 2, to_core)
    relay = [
        quad_copy(d_all.at[core, 1 - side, rows], d_all.at[core, 1 - side, rows], 3 + part, to_core)
        for part, rows in enumerate(halves)
    ]
    for part in range(2):
        along[part].start()
    across.start()
    d_query[...] = jnp.zeros_like(d_query)
    for load in loads:
        load.wait()
    for kind in range(3):
        rows = slice(kind * units // 3, (kind + 1) * units // 3)
        ours[rows] = (ours[rows].astype(single) + theirs[rows].astype(single)).astype(bfloat)
    store.start()
    for part in range(2):
        along[part].wait()
        relay[part].start()
    store.wait()
    bulk(0).start()
    bulk(1).start()
    across.wait()
    for part in range(2):
        relay[part].wait()
    for array in arrays:
        array.wait()
    d_rows = d_all[...].reshape(tokens, width)
    for head in range(2):
        columns = slice(head * HD, head * HD + HD)
        made = dot_nt(d_rows, rows_ref[2, columns]).astype(bfloat)
        d_out[head] = made
        row_dot = jnp.sum(
            made.astype(single) * attended_ref[:, columns].astype(single), axis=-1, keepdims=True
        )
        delta[head] = jnp.broadcast_to(row_dot, delta.shape[1:])

    def place(slot, head, start):
        deep = 2 * head + core if slot == 1 else 2 * core + head
        for unit in range(4):
            source = out_rows.at[slot, head, pl.ds(unit * share, share)]
            owner = deep * pairs + unit // 2
            target = out_parts.at[owner] if slot == 2 else parts.at[owner, slot]
            sem = place_sem.at[slot, head, unit]

            def here():
                return pltpu.make_async_copy(source, target, sem)

            def there():
                return remote(source, target, sem, peer_sem.at[slot, head, unit], to_core)

            @pl.when(core == unit % 2)
            def _():
                if start:
                    here().start()
                else:
                    here().wait()
                    there().wait_recv()

            @pl.when(core != unit % 2)
            def _():
                if start:
                    there().start()
                else:
                    there().wait_send()

    def term(slot, head, left, right):
        out_rows[slot, head] = dot_tn(left, right).astype(bfloat)
        place(slot, head, True)

    for head in range(2):
        term(2, head, attended_ref[:, head * HD : head * HD + HD], d_all[...].reshape(tokens, width))
    def block(way, owner):
        key = keyval_ref[owner, 0, way * half : way * half + half]
        val = keyval_ref[owner, 1, way * half : way * half + half]
        row = lax.broadcasted_iota(jnp.int32, (tokens, half), 0)
        column = lax.broadcasted_iota(jnp.int32, (tokens, half), 1)
        allowed = row + (chip - owner) * tokens - way * half >= column

        def one_head(head, carried):
            bent = jnp.tanh(dot_nt(query_ref[head], key) * (scale / softcap))
            inverse = jnp.concatenate([inverse_ref[head]] * (half // 128), axis=1)
            row_dot = jnp.concatenate([delta[head]] * (half // 128), axis=1)
            probs = jnp.where(allowed, jnp.exp(softcap * bent), 0.0) * inverse
            d_probs = dot_nt(d_out[head], val)
            d_scores = (probs * (d_probs - row_dot) * (1.0 - bent * bent)).astype(bfloat)
            d_block[way, 0] += dot_tn(d_scores, query_ref[head]) * scale
            d_block[way, 1] += dot_tn(probs.astype(bfloat), d_out[head])
            d_query[head] += dot_nn(d_scores, key)
            return carried

        for head in range(2):
            one_head(head, 0)

    def key_copy(way, kind, step, first):
        return remote(
            first_put.at[way, kind] if first else held_keys.at[way, step - 1, kind],
            held_keys.at[way, step, kind],
            key_send.at[way, kind, step],
            key_recv.at[way, kind, step],
            {"fsdp": ring.right if way == 0 else ring.left},
        )

    streams = [(way, kind) for kind in range(2) for way in range(2)]

    early = 3

    def key_blocks(step):
        for way in range(2):
            owner = ring.owner(way, step + 1)
            d_block[way] = jnp.zeros(d_block.shape[1:], single)
            if way == 1:

                @pl.when((step >= early) & (step < chips - 1))
                def _():
                    out_ring.scatter_step(out_parts, out_held, step - early)

            @pl.when(owner <= chip)
            def _():
                block(way, owner)

    def key_body(step, carried):
        key_blocks(step)
        for way, kind in streams:

            @pl.when(step == 0)
            def _():
                first_put[way, kind] = d_block[way, kind].astype(bfloat)
                key_copy(way, kind, 0, True).start()

            @pl.when(step > 0)
            def _():
                key_copy(way, kind, step - 1, True).wait_recv()
                summed = held_keys[way, step - 1, kind].astype(single) + d_block[way, kind]
                held_keys[way, step - 1, kind] = summed.astype(bfloat)
                key_copy(way, kind, step, False).start()

        return carried

    lax.fori_loop(0, early, key_body, 0)
    for head in range(2):
        place(2, head, False)
    lax.fori_loop(early, chips - 1, key_body, 0)

    normed = normed_ref[...].reshape(tokens, width)
    key_blocks(chips - 1)
    out_ring.scatter_step(out_parts, out_held, chips - 4)
    for way in range(2):
        rows = slice(way * half, way * half + half)
        for kind in range(2):
            key_copy(way, kind, chips - 2, True).wait_recv()
            summed = held_keys[way, chips - 2, kind].astype(single) + d_block[way, kind]
            swapped[2 + kind, rows] = summed.astype(bfloat)
    swap = quad_copy(swapped.at[3 - side], swapped.at[side], 5, to_side)
    swap.start()
    for head in range(2):
        turned = turn(d_query[head] * scale, cosine_ref[...], -sine_ref[...])
        d_raw[head] = turned.astype(bfloat)
        term(0, head, d_raw[head], normed)
        if head == 0:
            out_ring.scatter_step(out_parts, out_held, chips - 3)
    swap.wait()
    out_ring.scatter_step(out_parts, out_held, chips - 2)
    bulk(2).start()
    swapped[side] = swapped[2 + side]
    for head in range(2):
        turned = turn(swapped[head].astype(single), key_cosine_ref[...], -key_sine_ref[...])
        d_raw[2 + head] = turned.astype(bfloat)
        term(1, head, d_raw[2 + head], normed)
    span = width // 3

    def d_input(tile, carried):
        columns = pl.ds(pl.multiple_of(tile * span, span), span)
        made = dot_nn(d_raw[0], rows_ref[0, 0:HD, columns])
        made = made + dot_nn(d_raw[1], rows_ref[0, HD:, columns])
        made = made + dot_nn(d_raw[2], rows_ref[1, 0:HD, columns])
        made = made + dot_nn(d_raw[3], rows_ref[1, HD:, columns])
        out_rows[0, :, :, columns] = made.reshape(2, half, span).astype(bfloat)
        return carried

    for slot in range(2):
        for head in range(2):
            place(slot, head, False)
    blocks_ref = parts.reshape(chips, 2 * share, width)
    ring.scatter_step(blocks_ref, held, 0)
    lax.fori_loop(0, 3, d_input, 0)
    across = quad_copy(out_rows.at[0, 1 - core], across_got, 6, to_core)
    mine = pl.ds(pl.multiple_of(side * (half // 2), half // 2), half // 2)
    other = pl.ds(pl.multiple_of((1 - side) * (half // 2), half // 2), half // 2)
    along = quad_copy(along_put, along_got, 7, to_side)
    across.start()

    def body(step, carried):
        ring.scatter_step(blocks_ref, held, step)

        @pl.when(step == 1)
        def _():
            across.wait()
            given = out_rows[0, core, other].astype(single) + across_got[other].astype(single)
            along_put[...] = given.astype(bfloat)
            along.start()
            tokens_ref[...] = out_rows[0, core, mine].astype(single) + across_got[mine].astype(single)

        @pl.when(step == 4)
        def _():
            along.wait()
            tokens_ref[...] = tokens_ref[...] + along_got[...].astype(single)
            d_norm, d_gain = norm_back(resid_ref[...], scales_ref[0:1], tokens_ref[...])
            tokens_ref[...] = d_mid_ref[...] + d_norm
            value[0] = gains_ref[...]
            value[0, 0:1] = d_gain
            gains_total.start()

        @pl.when(step == 5)
        def _():
            gains_total.over_cores()

        @pl.when(step == 6)
        def _():
            gains_total.over_ring()

        return carried

    lax.fori_loop(1, chips - 1, body, 0)
    total_ref[...] = gains_total.end()
    out_ring.scatter_end(out_parts, out_held, sum_ref.at[pl.ds(2 * share, share)])
    ring.scatter_end(blocks_ref, held, sum_ref.at[pl.ds(0, 2 * share)])
    ring.finish(held.at[0, 0, 0 : ring.size])
    out_ring.finish(out_held.at[0, 0, 0 : out_ring.size])

    def settle(step, carried):
        for way, kind in streams:
            key_copy(way, kind, step, True).wait_send()
        return carried

    lax.fori_loop(0, chips - 1, settle, 0)
    for kind in range(3):
        bulk(kind).wait()


def tail(
    d_proj, query, keyval, attended, inverse, rows, normed, turns, locals_, own, other, chips, ident
):
    tokens = query.shape[1]
    tok_rows = tokens // 4
    width = rows.shape[2]
    share = tokens // 8
    half = tokens // 2
    vmem = pl.BlockSpec(memory_space=pltpu.VMEM)
    anywhere = pl.BlockSpec(memory_space=pl.ANY)
    return pl.pallas_call(
        functools.partial(tail_kernel, chips),
        out_shape=(
            jax.ShapeDtypeStruct((3 * share, width), single),
            jax.ShapeDtypeStruct((tok_rows, width), single),
            jax.ShapeDtypeStruct((4, width), single),
            jax.ShapeDtypeStruct(own.shape[1:], bfloat),
            jax.ShapeDtypeStruct(own.shape[1:], bfloat),
        ),
        in_specs=[vmem] * 2
        + [anywhere, vmem, vmem, anywhere, anywhere]
        + [vmem] * 8
        + [anywhere] * 2,
        out_specs=(vmem,) * 3 + (anywhere,) * 2,
        scratch_shapes=[
            pltpu.VMEM(keyval.shape, bfloat),
            pltpu.VMEM(rows.shape, bfloat),
            pltpu.VMEM(normed.shape, bfloat),
            pltpu.VMEM((2, 2, tok_rows, width), bfloat),
            pltpu.VMEM((2, tokens, HD), bfloat),
            pltpu.VMEM((2, tokens, 128), single),
            pltpu.VMEM((2, tokens, HD), single),
            pltpu.VMEM((2, 2, half, HD), single),
            pltpu.VMEM((2, 2, half, HD), bfloat),
            pltpu.VMEM((2, chips - 1, 2, half, HD), bfloat),
            pltpu.VMEM((4, tokens, HD), bfloat),
            pltpu.VMEM((4, tokens, HD), bfloat),
            pltpu.VMEM((3, 2, HD, width), bfloat),
            pltpu.VMEM((chips, 2, share, width), bfloat),
            pltpu.VMEM((chips, share, width), bfloat),
            pltpu.VMEM((2, chips - 1, share, width), bfloat),
            pltpu.VMEM((2, chips - 1, share // 2, width), bfloat),
            pltpu.VMEM((2 * tok_rows, width), bfloat),
            pltpu.VMEM((tok_rows, width), bfloat),
            pltpu.VMEM((tok_rows, width), bfloat),
        ]
        + total_scratch(chips, width)
        + [
            pltpu.SemaphoreType.DMA((2, 2, chips - 1)),
            pltpu.SemaphoreType.DMA((2, 2, chips - 1)),
            pltpu.SemaphoreType.DMA((3, 2, 4)),
            pltpu.SemaphoreType.DMA((3, 2, 4)),
            pltpu.SemaphoreType.DMA((2, 2, chips - 1)),
            pltpu.SemaphoreType.DMA((2, 2, chips - 1)),
            pltpu.SemaphoreType.DMA((2, 1, chips - 1)),
            pltpu.SemaphoreType.DMA((2, 1, chips - 1)),
            pltpu.SemaphoreType.DMA((8,)),
            pltpu.SemaphoreType.DMA((8,)),
            pltpu.SemaphoreType.DMA((7,)),
            pltpu.SemaphoreType.DMA((3,)),
            pltpu.SemaphoreType.DMA((3,)),
        ],
        compiler_params=pltpu.CompilerParams(
            collective_id=ident, has_side_effects=True, vmem_limit_bytes=63 * 2**20
        ),
        cost_estimate=cost(160),
    )(d_proj, query, keyval, attended, inverse, rows, normed, *turns, *locals_, own, other)


def feed_kernel(
    chips,
    pieces,
    resid_ref,
    projected_ref,
    dy_ref,
    scales_ref,
    own_ref,
    side_ref,
    core_ref,
    diag_ref,
    result_ref,
    d_mid_ref,
    d_projected_ref,
    d_gains_ref,
    terms_ref,
    other_ref,
    weights,
    x_all,
    y_all,
    mid,
    both,
    hidden,
    part,
    held_one,
    held_two,
    chunk,
    wide,
    stage,
    load_sem,
    bulk_send,
    bulk_recv,
    stage_sem,
    other_sem,
    send_sem,
    recv_sem,
):
    tok_rows, width = resid_ref.shape
    units = own_ref.shape[0] // 3
    whole = 4 * units
    half = tok_rows // 2
    rings = [
        Ring(chips, pieces, tok_rows, send_sem.at[phase], recv_sem.at[phase]) for phase in range(4)
    ]
    chip = rings[0].chip
    loads = []
    for slot, ref in enumerate((own_ref, side_ref, core_ref, diag_ref)):
        for kind in range(3 if slot % 2 == 0 else 2):
            loads.append(
                pltpu.make_async_copy(
                    ref.at[pl.ds(kind * units, units)],
                    weights.at[pl.ds(kind * whole + slot * units, units)],
                    load_sem.at[slot, kind],
                )
            )
    for load in loads:
        load.start()
    mid[...] = resid_ref[...] + norm_scale(projected_ref[...], scales_ref[1:2])
    x_all[chip] = norm_scale(mid[...], scales_ref[2:3]).astype(bfloat)
    core = lax.axis_index("fsdp") % 2
    to_core = {"fsdp": 2 * chip + 1 - core}
    to_side = {"head": 1 - lax.axis_index("head")}
    quad_barrier(to_side, to_core, rings[0].right, rings[0].left)
    down_rows = [pl.ds(2 * whole + slot * units, units) for slot in range(4)]
    bulk_side = remote(
        own_ref.at[pl.ds(2 * units, units)],
        weights.at[down_rows[1]],
        bulk_send.at[0],
        bulk_recv.at[0],
        to_side,
    )
    bulk_diag = remote(
        weights.at[down_rows[1]],
        weights.at[down_rows[3]],
        bulk_send.at[1],
        bulk_recv.at[1],
        to_core,
    )
    bulk_side.start()
    span = width // 3

    def fetch(all_ref, step):
        chunk[0:half] = all_ref[rings[0].owner(0, step), 0:half]
        chunk[half:] = all_ref[rings[0].owner(1, step), half:]

    def put(ref, step, columns, value):
        ref[rings[0].owner(0, step), 0:half, columns] = value[0:half].astype(ref.dtype)
        ref[rings[0].owner(1, step), half:, columns] = value[half:].astype(ref.dtype)

    def take(ref, step, columns):
        return jnp.concatenate(
            [
                ref[rings[0].owner(0, step), 0:half, columns],
                ref[rings[0].owner(1, step), half:, columns],
            ],
            axis=0,
        )

    def gate_up(step):
        fetch(x_all, step)

        def rows_of(tile, carried):
            rows = pl.ds(pl.multiple_of(tile * span, span), span)
            wide[:, rows] = dot_nt(chunk[...], weights[rows])
            return carried

        lax.fori_loop(0, 3, rows_of, 0)

    def unit(step):
        put(both, step, slice(None), wide[...])
        value, slope = gelu_parts(wide[:, 0:whole])
        put(hidden, step, slice(None), value * wide[:, whole:])

    def down(step):
        chunk[:, 0:whole] = take(hidden, step, slice(None))

        def columns_of(tile, carried):
            columns = pl.ds(pl.multiple_of(tile * span, span), span)
            put(part, step, columns, dot_nn(chunk[:, 0:whole], weights[2 * whole :, columns]))
            return carried

        lax.fori_loop(0, 3, columns_of, 0)

    def forward(step, carried):
        @pl.when(step < chips)
        def _():
            rings[0].gather_step(x_all, step, 0)

        @pl.when(step == 1)
        def _():
            for load in loads:
                load.wait()

        @pl.when(step == chips)
        def _():
            bulk_side.wait_recv()
            bulk_diag.start()

        @pl.when(step > 0)
        def _():
            gate_up(step - 1)

        @pl.when(step < chips)
        def _():
            rings[0].gather_step(x_all, step, 1)

        @pl.when(step > 0)
        def _():
            unit(step - 1)

        return carried

    lax.fori_loop(0, chips + 1, forward, 0)
    bulk_diag.wait_recv()
    down(1)

    def spread(step, carried):
        rings[1].scatter_step(part, held_one, step, 0)
        down(step + 2)
        rings[1].scatter_step(part, held_one, step, 1)
        return carried

    lax.fori_loop(0, chips - 1, spread, 0)
    rings[1].scatter_end(part, held_one, wide)
    result_ref[...] = mid[...] + norm_scale(wide[...], scales_ref[3:4])
    d_ffn, d_gain = norm_back(wide[...], scales_ref[3:4], dy_ref[...])
    d_gains_ref[0:1] = jnp.zeros_like(d_gain)
    d_gains_ref[3:4] = d_gain
    y_all[chip] = d_ffn.astype(bfloat)
    rings[0].finish(x_all.at[0, 0 : rings[0].size])
    rings[1].finish(x_all.at[0, 0 : rings[0].size])
    bulk_side.wait_send()
    bulk_diag.wait_send()

    def d_input(step):
        chunk[...] = take(both, step, slice(None))

        def columns_of(tile, carried):
            columns = pl.ds(pl.multiple_of(tile * span, span), span)
            put(part, step, columns, dot_nn(chunk[...], weights[0 : 2 * whole, columns]))
            return carried

        lax.fori_loop(0, 3, columns_of, 0)

    early = chips // 2

    def d_hidden(step):
        fetch(y_all, step)
        wide[:, 0:whole] = dot_nt(chunk[...], weights[2 * whole :])

    def d_units(step):
        third = whole // 3

        def columns_of(tile, carried):
            columns = pl.ds(pl.multiple_of(tile * third, third), third)
            ups = pl.ds(pl.multiple_of(whole + tile * third, third), third)
            gate = take(both, step, columns).astype(single)
            upper = take(both, step, ups).astype(single)
            value, slope = gelu_parts(gate)
            put(both, step, columns, wide[:, columns] * upper * slope)
            put(both, step, ups, wide[:, columns] * value)
            return carried

        lax.fori_loop(0, 3, columns_of, 0)

    def backward(step, carried):
        @pl.when(step < chips)
        def _():
            rings[2].gather_step(y_all, step, 0)

        @pl.when(step == chips)
        def _():
            rings[3].scatter_step(part, held_two, 0)

        @pl.when(step > 0)
        def _():
            d_hidden(step - 1)
            d_units(step - 1)

        @pl.when(step < chips)
        def _():
            rings[2].gather_step(y_all, step, 1)

        @pl.when((step > 0) & (step <= early))
        def _():
            d_input(step - 1)

        return carried

    lax.fori_loop(0, chips + 1, backward, 0)
    rows_tile = stage.shape[1]
    tiles = 3 * whole // rows_tile
    upper_tiles = 2 * whole // rows_tile

    cut = units // 3

    def pieces_of(tile):
        for quarter in range(4):
            block = 4 * tile + quarter
            kind, slot, third = block // 12, (block // 3) % 4, block % 3
            source = stage.at[tile % 2, pl.ds(quarter * cut, cut)]
            rows = pl.ds(pl.multiple_of(kind * units + third * cut, cut), cut)
            sem = stage_sem.at[tile % 2, quarter]
            goal = terms_ref.at[slot, rows], other_ref.at[slot - 2, rows]
            there = functools.partial(
                remote, source, goal[1], sem, other_sem.at[tile, quarter], to_core
            )
            yield slot, functools.partial(pltpu.make_async_copy, source, goal[0], sem), there

    def keep(tile):
        for slot, here, there in pieces_of(tile):

            @pl.when(slot < 2)
            def _():
                here().start()

            @pl.when(slot >= 2)
            def _():
                there().start()

    def kept(tile):
        for slot, here, there in pieces_of(tile):

            @pl.when(slot < 2)
            def _():
                here().wait()

            @pl.when(slot >= 2)
            def _():
                there().wait_send()

    def grads(tile):
        @pl.when(tile >= 2)
        def _():
            kept(tile - 2)

        @pl.when(tile < upper_tiles)
        def _():
            columns = pl.ds(pl.multiple_of(tile * rows_tile, rows_tile), rows_tile)
            left = both[:, :, columns].reshape(chips * tok_rows, rows_tile)
            stage[tile % 2] = dot_tn(left, x_all[...].reshape(chips * tok_rows, width)).astype(bfloat)

        @pl.when(tile >= upper_tiles)
        def _():
            columns = pl.ds(
                pl.multiple_of((tile - upper_tiles) * rows_tile, rows_tile), rows_tile
            )
            left = hidden[:, :, columns].reshape(chips * tok_rows, rows_tile)
            stage[tile % 2] = dot_tn(left, y_all[...].reshape(chips * tok_rows, width)).astype(bfloat)

        keep(tile)

    def spread_back(step, carried):
        @pl.when(step > 0)
        def _():
            rings[3].scatter_step(part, held_two, step, 0)

        @pl.when((step + 2 >= early) & (step + 2 < chips))
        def _():
            d_input(step + 2)

        @pl.when(step > 0)
        def _():
            rings[3].scatter_step(part, held_two, step, 1)

        grads(step)
        return carried

    lax.fori_loop(0, chips - 1, spread_back, 0)

    def rest(tile, carried):
        grads(tile)
        return carried

    lax.fori_loop(chips - 1, tiles, rest, 0)
    rings[3].scatter_end(part, held_two, wide)
    d_norm, d_gain = norm_back(mid[...], scales_ref[2:3], wide[...])
    d_gains_ref[2:3] = d_gain
    d_mid_ref[...] = dy_ref[...] + d_norm
    d_projected, d_gain = norm_back(projected_ref[...], scales_ref[1:2], d_mid_ref[...])
    d_gains_ref[1:2] = d_gain
    d_projected_ref[...] = d_projected.astype(bfloat)
    rings[2].finish(x_all.at[0, 0 : rings[0].size])
    rings[3].finish(x_all.at[0, 0 : rings[0].size])
    kept(tiles - 2)
    kept(tiles - 1)

    def gained(tile, carried):
        for slot, here, there in pieces_of(tile):

            @pl.when(slot >= 2)
            def _():
                there().wait_recv()

        return carried

    lax.fori_loop(0, tiles, gained, 0)


def feed_forward(resid_in, projected, grad_out, scales, shares, chips, ident):
    tok_rows, width = resid_in.shape
    units = shares[0].shape[0] // 3
    whole = 4 * units
    pieces = 2
    vmem = pl.BlockSpec(memory_space=pltpu.VMEM)
    anywhere = pl.BlockSpec(memory_space=pl.ANY)
    return pl.pallas_call(
        functools.partial(feed_kernel, chips, pieces),
        out_shape=(
            jax.ShapeDtypeStruct((tok_rows, width), single),
            jax.ShapeDtypeStruct((tok_rows, width), single),
            jax.ShapeDtypeStruct((tok_rows, width), bfloat),
            jax.ShapeDtypeStruct((4, width), single),
            jax.ShapeDtypeStruct((2, 3 * units, width), bfloat),
            jax.ShapeDtypeStruct((2, 3 * units, width), bfloat),
        ),
        in_specs=[vmem] * 4 + [anywhere] * 4,
        out_specs=(vmem, vmem, vmem, vmem, anywhere, anywhere),
        scratch_shapes=[
            pltpu.VMEM((3 * whole, width), bfloat),
            pltpu.VMEM((chips, tok_rows, width), bfloat),
            pltpu.VMEM((chips, tok_rows, width), bfloat),
            pltpu.VMEM((tok_rows, width), single),
            pltpu.VMEM((chips, tok_rows, 2 * whole), bfloat),
            pltpu.VMEM((chips, tok_rows, whole), bfloat),
            pltpu.VMEM((chips, tok_rows, width), bfloat),
            pltpu.VMEM((2, chips - 1, tok_rows // 2, width), bfloat),
            pltpu.VMEM((2, chips - 1, tok_rows // 2, width), bfloat),
            pltpu.VMEM((tok_rows, width), bfloat),
            pltpu.VMEM((tok_rows, width), single),
            pltpu.VMEM((2, whole // 3, width), bfloat),
            pltpu.SemaphoreType.DMA((4, 3)),
            pltpu.SemaphoreType.DMA((2,)),
            pltpu.SemaphoreType.DMA((2,)),
            pltpu.SemaphoreType.DMA((2, 4)),
            pltpu.SemaphoreType.DMA((9, 4)),
            pltpu.SemaphoreType.DMA((4, 2, pieces, chips - 1)),
            pltpu.SemaphoreType.DMA((4, 2, pieces, chips - 1)),
        ],
        compiler_params=pltpu.CompilerParams(
            collective_id=ident, has_side_effects=True, vmem_limit_bytes=63 * 2**20
        ),
        cost_estimate=cost(205),
    )(resid_in, projected, grad_out, scales, *shares)


def general_device(
    tokens,
    cotangent,
    gains,
    gains_first,
    gains_second,
    attn_weight,
    attn_first,
    attn_second,
    ffn_weight,
    ffn_first,
    ffn_second,
):
    devices = lax.axis_size("fsdp")
    chips = devices // 2
    side = lax.axis_index("head")
    place = lax.axis_index("fsdp")
    core, chip = place % 2, place // 2
    tok_rows = tokens.shape[1]
    super_rows = 4 * tok_rows
    seq_len = min(SEQ_LEN, super_rows * chips)
    share = attn_weight.shape[1]
    pairs = chips // 4
    width = tokens.shape[2]
    scale = 1.0 / math.sqrt(HD)

    def swap_core(value):
        return lax.ppermute(value, "fsdp", [(index, index ^ 1) for index in range(devices)])

    def swap_side(value):
        return lax.ppermute(value, "head", [(0, 1), (1, 0)])

    def in_order(own, other, index, axis):
        return jnp.where(
            index == 0, jnp.stack([own, other], axis), jnp.stack([other, own], axis)
        )

    def pick(value, index, axis=0):
        return lax.dynamic_index_in_dim(value, index, axis, keepdims=False)

    def quad_gather(value):
        value = in_order(value, swap_side(value), side, 0)
        value = in_order(value, swap_core(value), core, 0)
        return value.reshape((super_rows,) + value.shape[3:])

    def quad_scatter(partial):
        partial = partial.reshape(2, 2, tok_rows, width)
        mine = pick(partial, core) + swap_core(pick(partial, 1 - core).astype(bfloat)).astype(single)
        return pick(mine, side) + swap_side(pick(mine, 1 - side).astype(bfloat)).astype(single)

    scales = lax.all_gather(gains.astype(bfloat), ("head", "fsdp"), axis=1, tiled=True).astype(single)
    attn_low = attn_weight.astype(bfloat)
    ffn_low = ffn_weight.astype(bfloat).transpose(1, 0, 2)
    ffn_pair = jnp.concatenate([ffn_low, swap_side(ffn_low)], axis=1)

    ring_rows = ring_gather(attn_low.reshape(3 * share, width), chips, 0)
    ring_rows = ring_rows.reshape(2, 2, pairs, 3, share, width)

    def query_rows(slot):
        rows = ring_rows[:, :, :, slot]
        other = swap_core(pick(rows, 1 - core))
        return in_order(pick(rows, core), other, core, 2).reshape(2 * HD, width)

    def keyval_rows():
        rows = ring_rows[:, :, :, 1]
        other = swap_core(pick(rows, 1 - core, 1))
        return in_order(pick(rows, core, 1), other, core, 2).reshape(2 * HD, width)

    w_query, w_keyval, w_out = query_rows(0), keyval_rows(), query_rows(2)

    resid_in = tokens[0]
    grad_out = cotangent[0]
    normed_one = norm_scale(resid_in, scales[0]).astype(bfloat)
    normed_all = quad_gather(normed_one)
    positions = chip * super_rows + jnp.arange(super_rows, dtype=jnp.int32)
    angles = turn_angles(positions % seq_len, HD)
    query_raw = jnp.einsum("td,fd->tf", normed_all, w_query, preferred_element_type=single)
    keyval_raw = jnp.einsum("td,fd->tf", normed_all, w_keyval, preferred_element_type=single)
    query = rotate(query_raw.reshape(super_rows, 2, HD), angles, 1.0).astype(bfloat)
    key_angles = jnp.where(side == 0, angles, 0.0)
    keyval = rotate(keyval_raw.reshape(super_rows, 2, HD), key_angles, 1.0).astype(bfloat)
    keyval = in_order(pick(keyval, side, 1), swap_side(pick(keyval, 1 - side, 1)), side, 0)
    keyval_all = ring_gather(keyval.reshape(2 * super_rows, HD), chips, 1)
    keyval_all = keyval_all.reshape(chips, 2, super_rows, HD)
    key_all = keyval_all[:, 0].reshape(chips * super_rows, HD)
    value_all = keyval_all[:, 1].reshape(chips * super_rows, HD)

    key_pos = jnp.arange(chips * super_rows, dtype=jnp.int32)
    distance = positions[:, None] - key_pos[None, :]
    same_seq = (positions // seq_len)[:, None] == (key_pos // seq_len)[None, :]
    allowed = (distance >= 0) & (distance < WIN) & same_seq

    def score_block():
        raw = jnp.einsum("qgd,kd->gqk", query, key_all, preferred_element_type=single)
        bent = jnp.tanh(raw * (scale / softcap))
        return bent, jnp.where(allowed, jnp.exp(softcap * bent), 0.0)

    bent, powers = score_block()
    total = jnp.sum(powers, axis=-1, keepdims=True)
    attended = jnp.einsum(
        "gqk,kd->gqd", powers.astype(bfloat), value_all, preferred_element_type=single
    )
    attended = (attended / total).transpose(1, 0, 2).reshape(super_rows, 2 * HD).astype(bfloat)
    projected = quad_scatter(jnp.dot(attended, w_out, preferred_element_type=single))
    resid_mid = resid_in + norm_scale(projected, scales[1])
    normed_two = norm_scale(resid_mid, scales[2]).astype(bfloat)

    ffn_all = jnp.concatenate([ffn_pair, swap_core(ffn_pair)], axis=1)
    w_gate, w_up, w_down = ffn_all[0], ffn_all[1], ffn_all[2]
    ring_tokens = chips * tok_rows
    normed_ring = ring_gather(normed_two, chips, 2).reshape(ring_tokens, width)
    gate_part = jnp.einsum("td,rd->tr", normed_ring, w_gate, preferred_element_type=single)
    up_part = jnp.einsum("td,rd->tr", normed_ring, w_up, preferred_element_type=single)
    hidden = hidden_unit(gate_part, up_part).astype(bfloat)
    ffn_part = jnp.dot(hidden, w_down, preferred_element_type=single).astype(bfloat)
    ffn_acc = ring_scatter(ffn_part.reshape(chips, tok_rows, width), chips, 3)
    result = resid_mid + norm_scale(ffn_acc, scales[3])

    ignored, post_back = jax.vjp(norm_scale, ffn_acc, scales[3])
    d_ffn, d_gain3 = post_back(grad_out)
    d_ffn_ring = ring_gather(d_ffn.astype(bfloat), chips, 4).reshape(ring_tokens, width)
    d_hidden = jnp.einsum("td,rd->tr", d_ffn_ring, w_down, preferred_element_type=single)
    ignored, unit_back = jax.vjp(hidden_unit, gate_part, up_part)
    d_gate, d_up = unit_back(d_hidden)
    d_gate = d_gate.astype(bfloat)
    d_up = d_up.astype(bfloat)
    d_normed = jnp.dot(d_gate, w_gate, preferred_element_type=single)
    d_normed = (d_normed + jnp.dot(d_up, w_up, preferred_element_type=single)).astype(bfloat)
    d_normed_two = ring_scatter(d_normed.reshape(chips, tok_rows, width), chips, 5)

    def ffn_rows(left, right):
        return jnp.einsum("tr,td->rd", left, right, preferred_element_type=single)

    ffn_terms = jnp.stack(
        [ffn_rows(d_gate, normed_ring), ffn_rows(d_up, normed_ring), ffn_rows(hidden, d_ffn_ring)]
    )
    units = ffn_weight.shape[0]
    ffn_terms = ffn_terms.reshape(3, 2, 2, units, width)
    ffn_terms = ffn_terms[:, 0] + swap_core(ffn_terms[:, 1].astype(bfloat)).astype(single)
    grad_ffn = ffn_terms[:, 0] + swap_side(ffn_terms[:, 1].astype(bfloat)).astype(single)

    ignored, mid_back = jax.vjp(norm_scale, resid_mid, scales[2])
    d_mid_norm, d_gain2 = mid_back(d_normed_two)
    d_mid = grad_out + d_mid_norm
    ignored, proj_back = jax.vjp(norm_scale, projected, scales[1])
    d_projected, d_gain1 = proj_back(d_mid)
    d_proj_all = quad_gather(d_projected.astype(bfloat))
    d_attended = jnp.einsum("td,fd->tf", d_proj_all, w_out, preferred_element_type=single)
    d_attended = d_attended.astype(bfloat).reshape(super_rows, 2, HD)

    bent, powers = score_block()
    probs = powers / total
    d_probs = jnp.einsum("qgd,kd->gqk", d_attended, value_all, preferred_element_type=single)
    row_dot = jnp.sum(d_probs * probs, axis=-1, keepdims=True)
    d_raw = (probs * (d_probs - row_dot) * (1.0 - bent * bent)).astype(bfloat)
    d_query = jnp.einsum("gqk,kd->qgd", d_raw, key_all, preferred_element_type=single) * scale
    d_keys = jnp.einsum("gqk,qgd->kd", d_raw, query, preferred_element_type=single) * scale
    d_values = jnp.einsum(
        "gqk,qgd->kd", probs.astype(bfloat), d_attended, preferred_element_type=single
    )
    d_pieces = jnp.stack(
        [d_keys.reshape(chips, super_rows, HD), d_values.reshape(chips, super_rows, HD)], axis=1
    ).astype(bfloat)
    d_keyval = ring_scatter(d_pieces.reshape(chips, 2 * super_rows, HD), chips, 6)
    d_keyval = d_keyval.reshape(2, super_rows, HD).astype(bfloat)
    d_keyval = in_order(pick(d_keyval, side), swap_side(pick(d_keyval, 1 - side)), side, 1)
    d_query_raw = rotate(d_query, angles, -1.0).reshape(super_rows, 2 * HD).astype(bfloat)
    d_keyval_raw = rotate(d_keyval.astype(single), key_angles, -1.0)
    d_keyval_raw = d_keyval_raw.reshape(super_rows, 2 * HD).astype(bfloat)
    d_normed_one = jnp.dot(d_query_raw, w_query, preferred_element_type=single)
    d_normed_one = d_normed_one + jnp.dot(d_keyval_raw, w_keyval, preferred_element_type=single)
    d_normed_one = quad_scatter(d_normed_one)
    ignored, first_back = jax.vjp(norm_scale, resid_in, scales[0])
    d_in_norm, d_gain0 = first_back(d_normed_one)
    tokens_grad = d_mid + d_in_norm

    def attn_rows(left, right):
        rows = jnp.einsum("tf,td->fd", left, right, preferred_element_type=single).astype(bfloat)
        return rows.reshape(2, pairs, 2, share, width)

    term_query = attn_rows(d_query_raw, normed_all)
    term_keyval = attn_rows(d_keyval_raw, normed_all)
    term_out = attn_rows(attended, d_proj_all)

    def to_core(term, axis):
        return in_order(pick(term, core, 2), swap_core(pick(term, 1 - core, 2)), core, axis)

    terms = jnp.stack([to_core(term_query, 0), to_core(term_keyval, 1), to_core(term_out, 0)], axis=3)
    grad_attn = ring_scatter(terms.reshape(chips, 3 * share, width), chips, 7)
    grad_attn = grad_attn.reshape(3, share, width)
    term_gain = jnp.stack([d_gain0, d_gain1, d_gain2, d_gain3])
    grad_gain = lax.psum_scatter(term_gain, ("head", "fsdp"), scatter_dimension=1, tiled=True)

    gains_first_new, gains_second_new, gains_new = adamw(
        gains, gains_first, gains_second, grad_gain, rate_gain, 0.0
    )
    attn_first_new, attn_second_new, attn_weight_new = adamw(
        attn_weight, attn_first, attn_second, grad_attn, rate_matrix, decay_matrix
    )
    ffn_first_new, ffn_second_new, ffn_weight_new = adamw(
        ffn_weight, ffn_first, ffn_second, grad_ffn.transpose(1, 0, 2), rate_matrix, decay_matrix
    )
    return (
        result[None],
        tokens_grad[None],
        gains_first_new,
        gains_second_new,
        gains_new,
        attn_first_new,
        attn_second_new,
        attn_weight_new,
        ffn_first_new,
        ffn_second_new,
        ffn_weight_new,
    )


def step_kernel(
    tiles,
    weight_ref,
    first_ref,
    second_ref,
    own_ref,
    other_ref,
    side_ref,
    weight_two_ref,
    first_two_ref,
    second_two_ref,
    grad_two_ref,
    first_out,
    second_out,
    weight_out,
    first_two_out,
    second_two_out,
    weight_two_out,
):
    index = pl.program_id(0)

    @pl.when(index < tiles)
    def _():
        grad = own_ref[0].astype(single) + other_ref[0].astype(single)
        grad = grad + side_ref[...].astype(single)
        first_out[...], second_out[...], weight_out[...] = adamw(
            weight_ref[...], first_ref[...], second_ref[...], grad, rate_matrix, decay_matrix
        )

    @pl.when(index >= tiles)
    def _():
        first_two_out[...], second_two_out[...], weight_two_out[...] = adamw(
            weight_two_ref[...],
            first_two_ref[...],
            second_two_ref[...],
            grad_two_ref[...],
            rate_matrix,
            decay_matrix,
        )


def step_weights(state, own, other, side, state_two, grad_two):
    rows, width = state[0].shape
    rows_two = grad_two.shape[0]
    size = 48
    tiles, tiles_two = rows // size, rows_two // size
    block = pl.BlockSpec((size, width), lambda index: (jnp.minimum(index, tiles - 1), 0))
    half = pl.BlockSpec((1, size, width), lambda index: (0, jnp.minimum(index, tiles - 1), 0))
    block_two = pl.BlockSpec((size, width), lambda index: (jnp.maximum(index - tiles, 0), 0))
    return pl.pallas_call(
        functools.partial(step_kernel, tiles),
        grid=(tiles + tiles_two,),
        out_shape=(jax.ShapeDtypeStruct((rows, width), single),) * 3
        + (jax.ShapeDtypeStruct((rows_two, width), single),) * 3,
        in_specs=[block] * 3 + [half, half, block] + [block_two] * 4,
        out_specs=(block,) * 3 + (block_two,) * 3,
        compiler_params=pltpu.CompilerParams(vmem_limit_bytes=40 * 2**20),
        cost_estimate=cost(20),
    )(*state, own, other, side, *state_two, grad_two)


def per_device(
    tokens,
    cotangent,
    gains,
    gains_first,
    gains_second,
    attn_weight,
    attn_first,
    attn_second,
    ffn_weight,
    ffn_first,
    ffn_second,
):
    devices = lax.axis_size("fsdp")
    chips = devices // 2
    side = lax.axis_index("head")
    place = lax.axis_index("fsdp")
    chip = place // 2
    tok_rows = tokens.shape[1]
    super_rows = 4 * tok_rows
    seq_len = min(SEQ_LEN, super_rows * chips)
    share = attn_weight.shape[1]
    width = tokens.shape[2]
    gain_columns = gains.shape[1]
    gain_start = (side * devices + place) * gain_columns

    units = ffn_weight.shape[0]

    def flat(value):
        return value.transpose(1, 0, 2).reshape(3 * units, width)

    ffn_wide = flat(ffn_weight)
    resid_in = tokens[0]
    grad_out = cotangent[0]
    positions = chip * super_rows + jnp.arange(super_rows, dtype=jnp.int32)
    angles = turn_angles(positions % seq_len, HD)
    key_angles = jnp.where(side == 0, angles, 0.0)
    gains_placed = lax.dynamic_update_slice(
        jnp.zeros((4, width), single), gains, (0, gain_start)
    )
    turns = (jnp.cos(angles), jnp.sin(angles), jnp.cos(key_angles), jnp.sin(key_angles))
    made = front(attn_weight, gains_placed, resid_in, turns, ffn_wide, chips, 0)
    attn_rows, scales, normed_all, query, keyval, attended, inverse, projected = made[:8]
    own_units, core_units, side_units, diag_units = made[8:]
    result, d_mid, d_proj_low, gain_rows, terms_own, terms_other = feed_forward(
        resid_in,
        projected,
        grad_out,
        scales,
        (own_units, side_units, core_units, diag_units),
        chips,
        1,
    )
    grad_attn, tokens_grad, gain_total, terms_sent, terms_side = tail(
        d_proj_low,
        query,
        keyval,
        attended,
        inverse,
        attn_rows,
        normed_all,
        turns,
        (resid_in, d_mid, scales, gain_rows),
        terms_own,
        terms_other,
        chips,
        2,
    )
    grad_ffn = terms_own[0].astype(single) + terms_other[0].astype(single)
    grad_ffn = grad_ffn + terms_side.astype(single)
    grad_gain = lax.dynamic_slice(gain_total, (0, gain_start), gains.shape)

    gains_first_new, gains_second_new, gains_new = adamw(
        gains, gains_first, gains_second, grad_gain, rate_gain, 0.0
    )
    def rows_of(value):
        return value.reshape(3 * share, width)

    stepped = step_weights(
        (ffn_wide, flat(ffn_first), flat(ffn_second)),
        terms_own,
        terms_other,
        terms_side,
        (rows_of(attn_weight), rows_of(attn_first), rows_of(attn_second)),
        grad_attn,
    )
    ffn_first_new, ffn_second_new, ffn_weight_new = (
        value.reshape(3, units, width).transpose(1, 0, 2) for value in stepped[:3]
    )
    attn_first_new, attn_second_new, attn_weight_new = (
        value.reshape(3, share, width) for value in stepped[3:]
    )
    return (
        result[None],
        tokens_grad[None],
        gains_first_new,
        gains_second_new,
        gains_new,
        attn_first_new,
        attn_second_new,
        attn_weight_new,
        ffn_first_new,
        ffn_second_new,
        ffn_weight_new,
    )


def solution(mesh):
    by_token = P("fsdp", "head", None)
    by_column = P(None, ("head", "fsdp"))
    by_row = P(None, ("head", "fsdp"), None)
    by_unit = P(("head", "fsdp"), None, None)
    placed = (by_token,) * 2 + (by_column,) * 3 + (by_row,) * 3 + (by_unit,) * 3
    body = per_device if mesh.shape["fsdp"] == 16 else general_device
    return jax.shard_map(
        body, mesh=mesh, in_specs=placed, out_specs=placed, check_vma=False
    )
```

```python
import functools
import math

import jax
import jax.numpy as jnp
from jax import lax
from jax.experimental import pallas as pl
from jax.experimental.pallas import tpu as pltpu
from jax.sharding import PartitionSpec as P

HQ = 8
HK = 4
HD = 256
WIN = 4096
STEP = 10
SEQ_LEN = 8192


eps_norm = 1e-06
softcap = 50.0
beta_one = 0.9
beta_two = 0.95
adam_eps = 1e-08
rate_matrix = 0.02
rate_gain = 0.2
decay_matrix = 0.1

bfloat = jnp.bfloat16
single = jnp.float32
MESH = pl.DeviceIdType.MESH


def norm_scale(values, scales):
    return (
        values
        * lax.rsqrt(jnp.mean(values * values, axis=-1, keepdims=True) + eps_norm)
        * (1.0 + scales)
    )


def turn_angles(positions, head_width):
    halfway = head_width // 2
    inverse_freq = 10000.0 ** (-(jnp.arange(halfway, dtype=jnp.float32) * 2.0) / head_width)
    return positions.astype(jnp.float32)[:, None] * inverse_freq[None, :]


def rotate(values, angles, direction):
    halfway = values.shape[-1] // 2
    cosine = jnp.cos(angles)[:, None, :]
    sine_part = direction * jnp.sin(angles)[:, None, :]
    former = values[..., :halfway]
    latter = values[..., halfway:]
    return jnp.concatenate(
        [former * cosine - latter * sine_part, latter * cosine + former * sine_part], axis=-1
    )


def adamw(weight, moment, second, gradient, step_rate, decay_rate):
    moment = beta_one * moment + (1.0 - beta_one) * gradient
    second = beta_two * second + (1.0 - beta_two) * gradient * gradient
    update = (
        moment / (1.0 - beta_one**STEP) / (jnp.sqrt(second / (1.0 - beta_two**STEP)) + adam_eps)
        + decay_rate * weight
    )
    return (moment, second, weight - step_rate * update)


def hidden_unit(gate_part, up_part):
    return jax.nn.gelu(gate_part, approximate=True) * up_part


def ring_of(chip, chips):
    wide = chips // 4
    deep, side = chip // wide, chip % wide
    return side * 4 + deep + (side % 2) * (3 - 2 * deep)


def chip_of(ring, chips):
    wide = chips // 4
    side, along = ring // 4, ring % 4
    return (along + (side % 2) * (3 - 2 * along)) * wide + side


def ring_places(chips):
    index = lax.axis_index("fsdp")
    core, chip = index % 2, index // 2
    ring = ring_of(chip, chips)
    right = 2 * chip_of((ring + 1) % chips, chips) + core
    left = 2 * chip_of((ring + chips - 1) % chips, chips) + core
    return chip, ring, right, left


def ring_barrier(right, left):
    barrier = pltpu.get_barrier_semaphore()
    for neighbour in (left, right):
        pl.semaphore_signal(barrier, inc=1, device_id={"fsdp": neighbour}, device_id_type=MESH)
    pl.semaphore_wait(barrier, 2)


def region(shape, pieces, way, piece):
    rows, columns = shape
    if rows % 32 == 0:
        size = rows // 2 // pieces
        start = way * (rows // 2) + piece * size
        return (pl.ds(start, size), pl.ds(0, columns)), (pl.ds(piece * size, size), pl.ds(0, columns))
    size = columns // 2
    return (pl.ds(0, rows), pl.ds(way * size, size)), (pl.ds(0, rows), pl.ds(0, size))


def half_shape(rows, columns):
    return (rows // 2, columns) if rows % 32 == 0 else (rows, columns // 2)


def gather_kernel(chips, pieces, own_ref, all_ref, local_sem, send_sem, recv_sem):
    chip, ring, right, left = ring_places(chips)
    ring_barrier(right, left)
    keep = pltpu.make_async_copy(own_ref, all_ref.at[chip], local_sem)
    keep.start()

    def copy(way, step, piece, first):
        owner = chip_of((ring + (chips - step if way == 0 else step)) % chips, chips)
        part, ignored = region(own_ref.shape, pieces, way, piece)
        there = all_ref.at[(owner,) + part]
        return pltpu.make_async_remote_copy(
            src_ref=own_ref.at[part] if first else there,
            dst_ref=there,
            send_sem=send_sem.at[way, piece, step],
            recv_sem=recv_sem.at[way, piece, step],
            device_id={"fsdp": right if way == 0 else left},
            device_id_type=MESH,
        )

    streams = [(way, piece) for piece in range(pieces) for way in range(2)]
    for way, piece in streams:
        copy(way, 0, piece, True).start()

    def body(step, carried):
        for way, piece in streams:
            copy(way, step - 1, piece, False).wait_recv()
            copy(way, step, piece, False).start()
        return carried

    lax.fori_loop(1, chips - 1, body, 0)
    for way, piece in streams:
        copy(way, chips - 2, piece, False).wait_recv()

    def finish(step, carried):
        for way, piece in streams:
            copy(way, step, piece, False).wait_send()
        return carried

    lax.fori_loop(0, chips - 1, finish, 0)
    keep.wait()


def ring_gather(own, chips, ident):
    rows, columns = own.shape
    pieces = 2 if rows % 64 == 0 else 1
    return pl.pallas_call(
        functools.partial(gather_kernel, chips, pieces),
        out_shape=jax.ShapeDtypeStruct((chips, rows, columns), own.dtype),
        in_specs=[pl.BlockSpec(memory_space=pl.ANY)],
        out_specs=pl.BlockSpec(memory_space=pl.ANY),
        scratch_shapes=[
            pltpu.SemaphoreType.DMA,
            pltpu.SemaphoreType.DMA((2, pieces, chips - 1)),
            pltpu.SemaphoreType.DMA((2, pieces, chips - 1)),
        ],
        compiler_params=pltpu.CompilerParams(collective_id=ident, has_side_effects=True),
        cost_estimate=cost(45),
    )(own)


def scatter_kernel(chips, pieces, parts_ref, sum_ref, held, send_sem, recv_sem):
    chip, ring, right, left = ring_places(chips)
    ring_barrier(right, left)

    def owner_of(way, step):
        shift = chips - 1 - step if way == 0 else 1 + step
        return chip_of((ring + shift) % chips, chips)

    def copy(way, step, piece, first):
        part, place = region(sum_ref.shape, pieces, way, piece)
        return pltpu.make_async_remote_copy(
            src_ref=(
                parts_ref.at[(owner_of(way, step),) + part]
                if first
                else held.at[(way, step - 1) + place]
            ),
            dst_ref=held.at[(way, step) + place],
            send_sem=send_sem.at[way, piece, step],
            recv_sem=recv_sem.at[way, piece, step],
            device_id={"fsdp": right if way == 0 else left},
            device_id_type=MESH,
        )

    streams = [(way, piece) for piece in range(pieces) for way in range(2)]
    for way, piece in streams:
        copy(way, 0, piece, True).start()

    def arrived(way, step, piece):
        copy(way, step, piece, True).wait_recv()
        part, place = region(sum_ref.shape, pieces, way, piece)
        here = parts_ref[(owner_of(way, step + 1),) + part]
        return held[(way, step) + place].astype(single) + here.astype(single)

    def body(step, carried):
        for way, piece in streams:
            total = arrived(way, step - 1, piece)
            part, place = region(sum_ref.shape, pieces, way, piece)
            held[(way, step - 1) + place] = total.astype(held.dtype)
            copy(way, step, piece, False).start()
        return carried

    lax.fori_loop(1, chips - 1, body, 0)
    for way, piece in streams:
        part, place = region(sum_ref.shape, pieces, way, piece)
        sum_ref[part] = arrived(way, chips - 2, piece)

    def finish(step, carried):
        for way, piece in streams:
            copy(way, step, piece, True).wait_send()
        return carried

    lax.fori_loop(0, chips - 1, finish, 0)


def ring_scatter(parts, chips, ident):
    rows, columns = parts.shape[1:]
    pieces = 2 if rows % 64 == 0 else 1
    return pl.pallas_call(
        functools.partial(scatter_kernel, chips, pieces),
        out_shape=jax.ShapeDtypeStruct((rows, columns), single),
        in_specs=[pl.BlockSpec(memory_space=pltpu.VMEM)],
        out_specs=pl.BlockSpec(memory_space=pltpu.VMEM),
        scratch_shapes=[
            pltpu.VMEM((2, chips - 1) + half_shape(rows, columns), parts.dtype),
            pltpu.SemaphoreType.DMA((2, pieces, chips - 1)),
            pltpu.SemaphoreType.DMA((2, pieces, chips - 1)),
        ],
        compiler_params=pltpu.CompilerParams(
            collective_id=ident, has_side_effects=True, vmem_limit_bytes=56 * 2**20
        ),
        cost_estimate=cost(45),
    )(parts)


def norm_back(values, scales, grad):
    inverse = lax.rsqrt(jnp.mean(values * values, axis=-1, keepdims=True) + eps_norm)
    bent = grad * (1.0 + scales)
    slope = jnp.mean(bent * values, axis=-1, keepdims=True) * (inverse * inverse * inverse)
    return bent * inverse - values * slope, jnp.sum(grad * values * inverse, axis=0, keepdims=True)


def gelu_parts(gate):
    root = math.sqrt(2.0 / math.pi)
    square = gate * gate
    bend = jnp.tanh(root * gate * (1.0 + 0.044715 * square))
    half = 0.5 * (1.0 + bend)
    slope = half + 0.5 * gate * (1.0 - bend * bend) * (root * (1.0 + 3.0 * 0.044715 * square))
    return gate * half, slope


def dot_nt(left, right):
    return lax.dot_general(left, right, (((1,), (1,)), ((), ())), preferred_element_type=single)


def dot_nn(left, right):
    return lax.dot_general(left, right, (((1,), (0,)), ((), ())), preferred_element_type=single)


def dot_tn(left, right):
    return lax.dot_general(left, right, (((0,), (0,)), ((), ())), preferred_element_type=single)


class Ring:
    def __init__(self, chips, pieces, rows, send_sem, recv_sem):
        self.chips, self.pieces, self.half = chips, pieces, rows // 2
        self.size = rows // 2 // pieces
        self.chip, self.ring, self.right, self.left = ring_places(chips)
        self.send_sem, self.recv_sem = send_sem, recv_sem
        self.streams = [(way, piece) for piece in range(pieces) for way in range(2)]

    def owner(self, way, step):
        shift = self.chips - step if way == 0 else step
        return chip_of((self.ring + shift) % self.chips, self.chips)

    def copy(self, source, target, way, piece, step):
        return pltpu.make_async_remote_copy(
            src_ref=source,
            dst_ref=target,
            send_sem=self.send_sem.at[way, piece, step],
            recv_sem=self.recv_sem.at[way, piece, step],
            device_id={"fsdp": self.right if way == 0 else self.left},
            device_id_type=MESH,
        )

    def part(self, way, piece):
        return pl.ds(way * self.half + piece * self.size, self.size)

    def place(self, piece):
        return pl.ds(piece * self.size, self.size)

    def gather_copy(self, all_ref, way, piece, step):
        there = all_ref.at[self.owner(way, step), self.part(way, piece)]
        return self.copy(there, there, way, piece, step)

    def of(self, only):
        return [(way, piece) for way, piece in self.streams if only is None or piece == only]

    def gather_step(self, all_ref, step, only=None):
        for way, piece in self.of(only):

            @pl.when(step > 0)
            def _():
                self.gather_copy(all_ref, way, piece, step - 1).wait_recv()

            @pl.when(step < self.chips - 1)
            def _():
                self.gather_copy(all_ref, way, piece, step).start()

    def scatter_copy(self, parts_ref, held, way, piece, step, first):
        source = (
            parts_ref.at[self.owner(way, step + 1), self.part(way, piece)]
            if first
            else held.at[way, step - 1, self.place(piece)]
        )
        return self.copy(source, held.at[way, step, self.place(piece)], way, piece, step)

    def scatter_total(self, parts_ref, held, way, piece, step):
        self.scatter_copy(parts_ref, held, way, piece, step, True).wait_recv()
        here = parts_ref[self.owner(way, step + 2), self.part(way, piece)]
        return held[way, step, self.place(piece)].astype(single) + here.astype(single)

    def scatter_step(self, parts_ref, held, step, only=None):
        for way, piece in self.of(only):

            @pl.when(step == 0)
            def _():
                self.scatter_copy(parts_ref, held, way, piece, 0, True).start()

            @pl.when(step > 0)
            def _():
                total = self.scatter_total(parts_ref, held, way, piece, step - 1)
                held[way, step - 1, self.place(piece)] = total.astype(held.dtype)
                self.scatter_copy(parts_ref, held, way, piece, step, False).start()

    def scatter_end(self, parts_ref, held, sum_ref):
        for way, piece in self.streams:
            sum_ref[self.part(way, piece)] = self.scatter_total(
                parts_ref, held, way, piece, self.chips - 2
            )

    def finish(self, example):
        def body(step, carried):
            for way, piece in self.streams:
                self.copy(example, example, way, piece, step).wait_send()
            return carried

        lax.fori_loop(0, self.chips - 1, body, 0)


def quad_peers(chips):
    side = lax.axis_index("head")
    index = lax.axis_index("fsdp")
    chip, core = index // 2, index % 2
    ring = ring_of(chip, chips)
    around = [2 * chip_of((ring + hop) % chips, chips) + core for hop in range(1, chips)]
    return side, core, {"head": 1 - side}, {"fsdp": 2 * chip + 1 - core}, around


def wide_barrier(to_side, to_core, around):
    barrier = pltpu.get_barrier_semaphore()
    for target in [to_side, to_core] + [{"fsdp": other} for other in around]:
        pl.semaphore_signal(barrier, inc=1, device_id=target, device_id_type=MESH)
    pl.semaphore_wait(barrier, 2 + len(around))


def quad_barrier(to_side, to_core, right, left):
    barrier = pltpu.get_barrier_semaphore()
    for target in (to_side, to_core, {"fsdp": right}, {"fsdp": left}):
        pl.semaphore_signal(barrier, inc=1, device_id=target, device_id_type=MESH)
    pl.semaphore_wait(barrier, 4)


def remote(source, target, send_sem, recv_sem, device):
    return pltpu.make_async_remote_copy(
        src_ref=source,
        dst_ref=target,
        send_sem=send_sem,
        recv_sem=recv_sem,
        device_id=device,
        device_id_type=MESH,
    )


class Total:
    def __init__(self, value, near, blocks, send_sem, recv_sem, peers, chip):
        self.value, self.near, self.blocks = value, near, blocks
        self.send_sem, self.recv_sem = send_sem, recv_sem
        side, core, self.to_side, self.to_core, self.around = peers
        self.chip = chip
        self.first = remote(value.at[0], near.at[0], send_sem.at[0], recv_sem.at[0], self.to_side)
        self.second = remote(value.at[1], near.at[1], send_sem.at[1], recv_sem.at[1], self.to_core)

    def spread(self, hop):
        here = self.blocks.at[self.chip]
        return remote(
            here,
            here,
            self.send_sem.at[1 + hop],
            self.recv_sem.at[1 + hop],
            {"fsdp": self.around[hop - 1]},
        )

    def start(self):
        self.first.start()

    def over_cores(self):
        self.first.wait_recv()
        self.value[1] = self.value[0] + self.near[0]
        self.second.start()

    def over_ring(self):
        self.second.wait_recv()
        self.blocks[self.chip] = self.value[1] + self.near[1]
        for hop in range(1, len(self.around) + 1):
            self.spread(hop).start()

    def end(self):
        for hop in range(1, len(self.around) + 1):
            self.spread(hop).wait_recv()
        total = self.blocks[0]
        for other in range(1, len(self.around) + 1):
            total = total + self.blocks[other]
        self.first.wait_send()
        self.second.wait_send()
        for hop in range(1, len(self.around) + 1):
            self.spread(hop).wait_send()
        return total


def total_scratch(chips, width):
    return [
        pltpu.VMEM((2, 4, width), single),
        pltpu.VMEM((2, 4, width), single),
        pltpu.VMEM((chips, 4, width), single),
        pltpu.SemaphoreType.DMA((chips + 1,)),
        pltpu.SemaphoreType.DMA((chips + 1,)),
    ]


def turn(raw, cosine, sine):
    halfway = raw.shape[1] // 2
    former, latter = raw[:, :halfway], raw[:, halfway:]
    return jnp.concatenate(
        [former * cosine - latter * sine, latter * cosine + former * sine], axis=1
    )


def front_kernel(
    chips,
    cuts,
    own_ref,
    gains_ref,
    resid_ref,
    cosine_ref,
    sine_ref,
    key_cosine_ref,
    key_sine_ref,
    wide_units_ref,
    rows_out,
    scales_ref,
    normed_out,
    query_ref,
    keyval_out,
    attended_ref,
    inverse_ref,
    projected_ref,
    own_units_ref,
    core_units_ref,
    side_units_ref,
    diag_units_ref,
    rows_ref,
    normed_ref,
    keyval_ref,
    all_rows,
    both,
    total,
    sums,
    product,
    across_put,
    across_got,
    along_put,
    along_got,
    cast_in,
    cast_out,
    value,
    near,
    blocks,
    total_send,
    total_recv,
    send_sem,
    recv_sem,
    place_sem,
    peer_sem,
    key_send,
    key_recv,
    quad_send,
    quad_recv,
    cast_sem,
    out_sem,
    bulk_send,
    bulk_recv,
):
    share, width = own_ref.shape[1:]
    tok_rows = resid_ref.shape[0]
    tokens = 4 * tok_rows
    half = width // 2
    pairs = chips // 4
    scale = 1.0 / math.sqrt(HD)
    chip, ring, right, left = ring_places(chips)
    peers = quad_peers(chips)
    side, core, to_side, to_core, around = peers
    cast_rows = cast_in.shape[1]
    casts = wide_units_ref.shape[0] // cast_rows

    def cast_load(tile):
        rows = pl.ds(tile * cast_rows, cast_rows)
        return pltpu.make_async_copy(
            wide_units_ref.at[rows], cast_in.at[tile % 2], cast_sem.at[0, tile % 2]
        )

    def cast_store(tile):
        rows = pl.ds(tile * cast_rows, cast_rows)
        return pltpu.make_async_copy(
            cast_out.at[tile % 2], own_units_ref.at[rows], cast_sem.at[1, tile % 2]
        )

    def cast(first, last):
        for tile in range(first, last):
            cast_load(tile).wait()
            if tile >= 3:
                cast_store(tile - 2).wait()
            cast_out[tile % 2] = cast_in[tile % 2].astype(bfloat)
            cast_store(tile).start()
            if tile + 2 < casts:
                cast_load(tile + 2).start()

    outs = [
        pltpu.make_async_copy(rows_ref.at[0:2], rows_out.at[0:2], out_sem.at[0]),
        pltpu.make_async_copy(rows_ref.at[2], rows_out.at[2], out_sem.at[1]),
        pltpu.make_async_copy(normed_ref, normed_out, out_sem.at[2]),
        pltpu.make_async_copy(keyval_ref, keyval_out, out_sem.at[3]),
    ]
    cast_load(0).start()
    cast_load(1).start()
    all_rows[chip] = own_ref[...].astype(bfloat)
    value[0] = gains_ref[...].astype(bfloat).astype(single)
    wide_barrier(to_side, to_core, around)
    gains_total = Total(value, near, blocks, total_send, total_recv, peers, chip)
    gains_total.start()
    streams = [(way, slot) for slot in range(2) for way in range(2)]
    out_streams = [(way, 2) for way in range(2)]
    key_streams = [(way, kind) for kind in range(2) for way in range(2)]

    def owner_of(way, step):
        return chip_of((ring + (chips - step if way == 0 else step)) % chips, chips)

    def hop(way, slot, step):
        there = all_rows.at[owner_of(way, step), slot, :, pl.ds(way * half, half)]
        return remote(
            there,
            there,
            send_sem.at[way, slot, step],
            recv_sem.at[way, slot, step],
            {"fsdp": right if way == 0 else left},
        )

    def key_hop(way, kind, step):
        there = keyval_ref.at[owner_of(way, step), kind, pl.ds(way * (tokens // 2), tokens // 2)]
        return remote(
            there,
            there,
            key_send.at[way, kind, step],
            key_recv.at[way, kind, step],
            {"fsdp": right if way == 0 else left},
        )

    def goal(way, slot, step):
        owner = owner_of(way, step)
        deep = owner // pairs
        unit = (owner % pairs) * 2 + core
        taker, head = (deep % 2, deep // 2) if slot == 1 else (deep // 2, deep % 2)
        columns = pl.ds(way * half, half)
        source = all_rows.at[owner, slot, :, columns]
        start = pl.multiple_of(head * HD + unit * share, share)
        target = rows_ref.at[slot, pl.ds(start, share), columns]
        sem = place_sem.at[way, slot, step]

        def here():
            return pltpu.make_async_copy(source, target, sem)

        def there():
            return remote(source, target, sem, peer_sem.at[way, slot, step], to_core)

        return taker, here, there

    def place(way, slot, step):
        taker, here, there = goal(way, slot, step)

        @pl.when(taker == core)
        def _():
            here().start()

        @pl.when(taker != core)
        def _():
            there().start()

    def placed(way, slot, step):
        taker, here, there = goal(way, slot, step)

        @pl.when(taker == core)
        def _():
            here().wait()
            there().wait_recv()

        @pl.when(taker != core)
        def _():
            there().wait_send()

    def pass_on(which, step):
        for way, slot in which:

            @pl.when(step > 0)
            def _():
                hop(way, slot, step - 1).wait_recv()

            @pl.when(step < chips - 1)
            def _():
                hop(way, slot, step).start()

            place(way, slot, step)

    def settle(which):
        def body(step, carried):
            for way, slot in which:
                placed(way, slot, step)

                @pl.when(step < chips - 1)
                def _():
                    hop(way, slot, step).wait_send()

            return carried

        lax.fori_loop(0, chips, body, 0)

    def quad_copy(source, target, index, device):
        return remote(source, target, quad_send.at[index], quad_recv.at[index], device)

    mine = normed_ref.at[core, side]
    along = quad_copy(mine, mine, 0, to_side)
    across = quad_copy(normed_ref.at[core], normed_ref.at[core], 1, to_core)

    def bulk_side(part):
        rows = pl.ds(cuts[part], cuts[part + 1] - cuts[part])
        return remote(
            own_units_ref.at[rows],
            side_units_ref.at[rows],
            bulk_send.at[part],
            bulk_recv.at[part],
            to_side,
        )

    def bulk_diag(part):
        rows = pl.ds(cuts[part], cuts[part + 1] - cuts[part])
        return remote(
            side_units_ref.at[rows],
            diag_units_ref.at[rows],
            bulk_send.at[3 + part],
            bulk_recv.at[3 + part],
            to_core,
        )

    bulk_core = remote(own_units_ref, core_units_ref, bulk_send.at[6], bulk_recv.at[6], to_core)
    for way, slot in streams:
        hop(way, slot, 0).start()
    cast(0, 1)
    cast_store(0).wait()
    bulk_side(0).start()
    gains_total.over_cores()
    for way, slot in streams:
        place(way, slot, 0)
    gains_total.over_ring()
    pass_on(streams, 1)
    cast(1, 3)
    scales_ref[...] = gains_total.end()
    normed_ref[core, side] = norm_scale(resid_ref[...], scales_ref[0:1]).astype(bfloat)
    along.start()
    pass_on(streams, 2)
    cast(3, 5)
    pass_on(streams, 3)
    cast(5, 7)
    along.wait()
    across.start()
    bulk_side(1).start()
    pass_on(streams, 4)
    cast(7, casts)
    cast_store(casts - 2).wait()
    cast_store(casts - 1).wait()
    bulk_core.start()

    def body(step, carried):
        pass_on(streams, step)
        return carried

    lax.fori_loop(5, chips, body, 0)
    pass_on(out_streams, 0)
    across.wait()
    outs[2].start()
    settle(streams)
    outs[0].start()

    def project(slot, head):
        rows = slice(head * HD, head * HD + HD)
        return dot_nt(normed_ref[...].reshape(tokens, width), rows_ref[slot, rows])

    for head in range(2):
        raw = project(1, head)
        both[head] = turn(raw, key_cosine_ref[...], key_sine_ref[...]).astype(bfloat)
    swap = quad_copy(both.at[1 - side], keyval_ref.at[chip, side], 2, to_side)
    swap.start()
    bulk_side(2).start()
    for part in range(2):
        bulk_side(part).wait_recv()
        bulk_diag(part).start()
    pass_on(out_streams, 1)
    keyval_ref[chip, side] = both[side]
    for head in range(2):
        raw = project(0, head)
        query_ref[head] = turn(raw, cosine_ref[...], sine_ref[...]).astype(bfloat)
        pass_on(out_streams, 2 + head)
    total[...] = jnp.zeros_like(total)
    sums[...] = jnp.zeros_like(sums)
    swap.wait()

    def block(way, owner):
        part = tokens // 2
        key = keyval_ref[owner, 0, way * part : way * part + part]
        val = keyval_ref[owner, 1, way * part : way * part + part]
        row = lax.broadcasted_iota(jnp.int32, (tokens, part), 0)
        column = lax.broadcasted_iota(jnp.int32, (tokens, part), 1)
        allowed = row + (chip - owner) * tokens - way * part >= column

        def one_head(head, carried):
            bent = jnp.tanh(dot_nt(query_ref[head], key) * (scale / softcap))
            powers = jnp.where(allowed, jnp.exp(softcap * bent), 0.0)
            sums[head] += powers[:, : part // 2] + powers[:, part // 2 :]
            total[head] += dot_nn(powers.astype(bfloat), val)
            return carried

        for head in range(2):
            one_head(head, 0)

    def key_body(step, carried):
        for way, kind in key_streams:

            @pl.when(step > 0)
            def _():
                key_hop(way, kind, step - 1).wait_recv()

            @pl.when(step < chips - 1)
            def _():
                key_hop(way, kind, step).start()

        for way in range(2):
            owner = owner_of(way, step)

            @pl.when(owner <= chip)
            def _():
                block(way, owner)

            if way == 0:

                @pl.when(step < chips - 4)
                def _():
                    pass_on(out_streams, step + 4)

        return carried

    lax.fori_loop(0, chips, key_body, 0)
    outs[3].start()
    bulk_side(2).wait_recv()
    bulk_diag(2).start()
    settle(out_streams)
    outs[1].start()
    for head in range(2):
        inverse = 1.0 / jnp.sum(sums[head], axis=-1, keepdims=True)
        inverse_ref[head] = jnp.broadcast_to(inverse, inverse_ref.shape[1:])
        attended_ref[:, head * HD : head * HD + HD] = (total[head] * inverse).astype(bfloat)
    span = width // 3
    tiles = [slice(tile * span, tile * span + span) for tile in range(3)]

    def project_out(part, ref, columns):
        first = pl.ds(pl.multiple_of(part * 2 * tok_rows, 2 * tok_rows), 2 * tok_rows)
        made = dot_nn(attended_ref[first], rows_ref[2, :, columns])
        ref[:, :, columns] = made.reshape(2, tok_rows, span).astype(ref.dtype)

    across = [
        quad_copy(across_put.at[:, :, columns], across_got.at[:, :, columns], 3 + tile, to_core)
        for tile, columns in enumerate(tiles)
    ]
    along = [
        quad_copy(along_put.at[:, columns], along_got.at[:, columns], 6 + tile, to_side)
        for tile, columns in enumerate(tiles)
    ]
    for tile, columns in enumerate(tiles):
        project_out(1 - core, across_put, columns)
        across[tile].start()
    for tile, columns in enumerate(tiles):
        project_out(core, product, columns)
        across[tile].wait()
        given = product[1 - side, :, columns] + across_got[1 - side, :, columns].astype(single)
        along_put[:, columns] = given.astype(bfloat)
        along[tile].start()

    def key_settle(step, carried):
        for way, kind in key_streams:
            key_hop(way, kind, step).wait_send()
        return carried

    lax.fori_loop(0, chips - 1, key_settle, 0)
    for out in outs:
        out.wait()
    bulk_core.wait()
    for part in range(3):
        bulk_side(part).wait_send()
        bulk_diag(part).wait()
    for tile, columns in enumerate(tiles):
        along[tile].wait()
        kept = product[side, :, columns] + across_got[side, :, columns].astype(single)
        projected_ref[:, columns] = kept + along_got[:, columns].astype(single)


def cost(micros):
    return pl.CostEstimate(flops=int(micros * 1e9), bytes_accessed=0, transcendentals=0)


def front(attn_weight, gains, resid_in, turns, ffn_wide, chips, ident):
    share, width = attn_weight.shape[1:]
    tok_rows = resid_in.shape[0]
    tokens = 4 * tok_rows
    units = ffn_wide.shape[0]
    cuts = (0, units // 9, units // 3, 2 * units // 3)
    vmem = pl.BlockSpec(memory_space=pltpu.VMEM)
    anywhere = pl.BlockSpec(memory_space=pl.ANY)
    return pl.pallas_call(
        functools.partial(front_kernel, chips, cuts),
        out_shape=(
            jax.ShapeDtypeStruct((3, 2 * HD, width), bfloat),
            jax.ShapeDtypeStruct((4, width), single),
            jax.ShapeDtypeStruct((2, 2, tok_rows, width), bfloat),
            jax.ShapeDtypeStruct((2, tokens, HD), bfloat),
            jax.ShapeDtypeStruct((chips, 2, tokens, HD), bfloat),
            jax.ShapeDtypeStruct((tokens, 2 * HD), bfloat),
            jax.ShapeDtypeStruct((2, tokens, 128), single),
            jax.ShapeDtypeStruct((tok_rows, width), single),
        )
        + (jax.ShapeDtypeStruct((units, width), bfloat),) * 2
        + (jax.ShapeDtypeStruct((2 * units // 3, width), bfloat),) * 2,
        in_specs=[vmem] * 7 + [anywhere],
        out_specs=(anywhere, vmem, anywhere, vmem, anywhere, vmem, vmem, vmem) + (anywhere,) * 4,
        scratch_shapes=[
            pltpu.VMEM((3, 2 * HD, width), bfloat),
            pltpu.VMEM((2, 2, tok_rows, width), bfloat),
            pltpu.VMEM((chips, 2, tokens, HD), bfloat),
            pltpu.VMEM((chips, 3, share, width), bfloat),
            pltpu.VMEM((2, tokens, HD), bfloat),
            pltpu.VMEM((2, tokens, HD), single),
            pltpu.VMEM((2, tokens, 128), single),
            pltpu.VMEM((2, tok_rows, width), single),
            pltpu.VMEM((2, tok_rows, width), bfloat),
            pltpu.VMEM((2, tok_rows, width), bfloat),
            pltpu.VMEM((tok_rows, width), bfloat),
            pltpu.VMEM((tok_rows, width), bfloat),
            pltpu.VMEM((2, units // 9, width), single),
            pltpu.VMEM((2, units // 9, width), bfloat),
        ]
        + total_scratch(chips, width)
        + [
            pltpu.SemaphoreType.DMA((2, 3, chips - 1)),
            pltpu.SemaphoreType.DMA((2, 3, chips - 1)),
            pltpu.SemaphoreType.DMA((2, 3, chips)),
            pltpu.SemaphoreType.DMA((2, 3, chips)),
            pltpu.SemaphoreType.DMA((2, 2, chips - 1)),
            pltpu.SemaphoreType.DMA((2, 2, chips - 1)),
            pltpu.SemaphoreType.DMA((9,)),
            pltpu.SemaphoreType.DMA((9,)),
            pltpu.SemaphoreType.DMA((2, 2)),
            pltpu.SemaphoreType.DMA((4,)),
            pltpu.SemaphoreType.DMA((7,)),
            pltpu.SemaphoreType.DMA((7,)),
        ],
        compiler_params=pltpu.CompilerParams(
            collective_id=ident, has_side_effects=True, vmem_limit_bytes=60 * 2**20
        ),
        cost_estimate=cost(140),
    )(attn_weight, gains, resid_in, *turns, ffn_wide)


def tail_kernel(
    chips,
    d_proj_ref,
    query_ref,
    keyval_in,
    attended_ref,
    inverse_ref,
    rows_in,
    normed_in,
    cosine_ref,
    sine_ref,
    key_cosine_ref,
    key_sine_ref,
    resid_ref,
    d_mid_ref,
    scales_ref,
    gains_ref,
    units_own_ref,
    units_other_ref,
    sum_ref,
    tokens_ref,
    total_ref,
    units_ref,
    units_got_ref,
    keyval_ref,
    rows_ref,
    normed_ref,
    d_all,
    d_out,
    delta,
    d_query,
    d_block,
    first_put,
    held_keys,
    swapped,
    d_raw,
    out_rows,
    parts,
    out_parts,
    held,
    out_held,
    across_got,
    along_put,
    along_got,
    value,
    near,
    blocks,
    total_send,
    total_recv,
    key_send,
    key_recv,
    place_sem,
    peer_sem,
    send_sem,
    recv_sem,
    out_send,
    out_recv,
    quad_send,
    quad_recv,
    load_sem,
    bulk_send,
    bulk_recv,
):
    tokens = query_ref.shape[1]
    half = tokens // 2
    width = resid_ref.shape[1]
    share = out_parts.shape[1]
    pairs = chips // 4
    scale = 1.0 / math.sqrt(HD)
    peers = quad_peers(chips)
    side, core, to_side, to_core, around = peers
    ring = Ring(chips, 2, 2 * share, send_sem, recv_sem)
    out_ring = Ring(chips, 1, share, out_send, out_recv)
    chip = ring.chip
    gains_total = Total(value, near, blocks, total_send, total_recv, peers, chip)
    arrays = [
        pltpu.make_async_copy(rows_in.at[2], rows_ref.at[2], load_sem.at[3]),
        pltpu.make_async_copy(keyval_in, keyval_ref, load_sem.at[4]),
        pltpu.make_async_copy(normed_in, normed_ref, load_sem.at[5]),
        pltpu.make_async_copy(rows_in.at[0:2], rows_ref.at[0:2], load_sem.at[6]),
    ]
    d_all[core, side] = d_proj_ref[...]
    wide_barrier(to_side, to_core, around)

    def quad_copy(source, target, index, device):
        return remote(source, target, quad_send.at[index], quad_recv.at[index], device)

    def bulk(kind):
        return remote(
            units_ref.at[pl.ds(kind * (units_ref.shape[0] // 3), units_ref.shape[0] // 3)],
            units_got_ref.at[pl.ds(kind * (units_ref.shape[0] // 3), units_ref.shape[0] // 3)],
            bulk_send.at[kind],
            bulk_recv.at[kind],
            to_side,
        )

    units = units_ref.shape[0]
    ours = out_rows.reshape(6 * HD, width).at[pl.ds(0, units)]
    theirs = parts.reshape(2 * chips * share, width).at[pl.ds(0, units)]
    loads = (
        pltpu.make_async_copy(units_own_ref.at[1], ours, load_sem.at[0]),
        pltpu.make_async_copy(units_other_ref.at[1], theirs, load_sem.at[1]),
    )
    store = pltpu.make_async_copy(ours, units_ref, load_sem.at[2])
    for load in loads:
        load.start()
    for array in arrays:
        array.start()
    quarter = tokens // 8
    halves = [slice(part * quarter, part * quarter + quarter) for part in range(2)]
    along = [
        quad_copy(d_all.at[core, side, rows], d_all.at[core, side, rows], part, to_side)
        for part, rows in enumerate(halves)
    ]
    across = quad_copy(d_all.at[core, side], d_all.at[core, side], 2, to_core)
    relay = [
        quad_copy(d_all.at[core, 1 - side, rows], d_all.at[core, 1 - side, rows], 3 + part, to_core)
        for part, rows in enumerate(halves)
    ]
    for part in range(2):
        along[part].start()
    across.start()
    d_query[...] = jnp.zeros_like(d_query)
    for load in loads:
        load.wait()
    for kind in range(3):
        rows = slice(kind * units // 3, (kind + 1) * units // 3)
        ours[rows] = (ours[rows].astype(single) + theirs[rows].astype(single)).astype(bfloat)
    store.start()
    for part in range(2):
        along[part].wait()
        relay[part].start()
    store.wait()
    bulk(0).start()
    bulk(1).start()
    across.wait()
    for part in range(2):
        relay[part].wait()
    for array in arrays:
        array.wait()
    d_rows = d_all[...].reshape(tokens, width)
    for head in range(2):
        columns = slice(head * HD, head * HD + HD)
        made = dot_nt(d_rows, rows_ref[2, columns]).astype(bfloat)
        d_out[head] = made
        row_dot = jnp.sum(
            made.astype(single) * attended_ref[:, columns].astype(single), axis=-1, keepdims=True
        )
        delta[head] = jnp.broadcast_to(row_dot, delta.shape[1:])

    def place(slot, head, start):
        deep = 2 * head + core if slot == 1 else 2 * core + head
        for unit in range(4):
            source = out_rows.at[slot, head, pl.ds(unit * share, share)]
            owner = deep * pairs + unit // 2
            target = out_parts.at[owner] if slot == 2 else parts.at[owner, slot]
            sem = place_sem.at[slot, head, unit]

            def here():
                return pltpu.make_async_copy(source, target, sem)

            def there():
                return remote(source, target, sem, peer_sem.at[slot, head, unit], to_core)

            @pl.when(core == unit % 2)
            def _():
                if start:
                    here().start()
                else:
                    here().wait()
                    there().wait_recv()

            @pl.when(core != unit % 2)
            def _():
                if start:
                    there().start()
                else:
                    there().wait_send()

    def term(slot, head, left, right):
        out_rows[slot, head] = dot_tn(left, right).astype(bfloat)
        place(slot, head, True)

    for head in range(2):
        term(2, head, attended_ref[:, head * HD : head * HD + HD], d_all[...].reshape(tokens, width))
    def block(way, owner):
        key = keyval_ref[owner, 0, way * half : way * half + half]
        val = keyval_ref[owner, 1, way * half : way * half + half]
        row = lax.broadcasted_iota(jnp.int32, (tokens, half), 0)
        column = lax.broadcasted_iota(jnp.int32, (tokens, half), 1)
        allowed = row + (chip - owner) * tokens - way * half >= column

        def one_head(head, carried):
            bent = jnp.tanh(dot_nt(query_ref[head], key) * (scale / softcap))
            inverse = jnp.concatenate([inverse_ref[head]] * (half // 128), axis=1)
            row_dot = jnp.concatenate([delta[head]] * (half // 128), axis=1)
            probs = jnp.where(allowed, jnp.exp(softcap * bent), 0.0) * inverse
            d_probs = dot_nt(d_out[head], val)
            d_scores = (probs * (d_probs - row_dot) * (1.0 - bent * bent)).astype(bfloat)
            d_block[way, 0] += dot_tn(d_scores, query_ref[head]) * scale
            d_block[way, 1] += dot_tn(probs.astype(bfloat), d_out[head])
            d_query[head] += dot_nn(d_scores, key)
            return carried

        for head in range(2):
            one_head(head, 0)

    def key_copy(way, kind, step, first):
        return remote(
            first_put.at[way, kind] if first else held_keys.at[way, step - 1, kind],
            held_keys.at[way, step, kind],
            key_send.at[way, kind, step],
            key_recv.at[way, kind, step],
            {"fsdp": ring.right if way == 0 else ring.left},
        )

    streams = [(way, kind) for kind in range(2) for way in range(2)]

    early = 3

    def key_blocks(step):
        for way in range(2):
            owner = ring.owner(way, step + 1)
            d_block[way] = jnp.zeros(d_block.shape[1:], single)
            if way == 1:

                @pl.when((step >= early) & (step < chips - 1))
                def _():
                    out_ring.scatter_step(out_parts, out_held, step - early)

            @pl.when(owner <= chip)
            def _():
                block(way, owner)

    def key_body(step, carried):
        key_blocks(step)
        for way, kind in streams:

            @pl.when(step == 0)
            def _():
                first_put[way, kind] = d_block[way, kind].astype(bfloat)
                key_copy(way, kind, 0, True).start()

            @pl.when(step > 0)
            def _():
                key_copy(way, kind, step - 1, True).wait_recv()
                summed = held_keys[way, step - 1, kind].astype(single) + d_block[way, kind]
                held_keys[way, step - 1, kind] = summed.astype(bfloat)
                key_copy(way, kind, step, False).start()

        return carried

    lax.fori_loop(0, early, key_body, 0)
    for head in range(2):
        place(2, head, False)
    lax.fori_loop(early, chips - 1, key_body, 0)

    normed = normed_ref[...].reshape(tokens, width)
    key_blocks(chips - 1)
    out_ring.scatter_step(out_parts, out_held, chips - 4)
    for way in range(2):
        rows = slice(way * half, way * half + half)
        for kind in range(2):
            key_copy(way, kind, chips - 2, True).wait_recv()
            summed = held_keys[way, chips - 2, kind].astype(single) + d_block[way, kind]
            swapped[2 + kind, rows] = summed.astype(bfloat)
    swap = quad_copy(swapped.at[3 - side], swapped.at[side], 5, to_side)
    swap.start()
    for head in range(2):
        turned = turn(d_query[head] * scale, cosine_ref[...], -sine_ref[...])
        d_raw[head] = turned.astype(bfloat)
        term(0, head, d_raw[head], normed)
        if head == 0:
            out_ring.scatter_step(out_parts, out_held, chips - 3)
    swap.wait()
    out_ring.scatter_step(out_parts, out_held, chips - 2)
    bulk(2).start()
    swapped[side] = swapped[2 + side]
    for head in range(2):
        turned = turn(swapped[head].astype(single), key_cosine_ref[...], -key_sine_ref[...])
        d_raw[2 + head] = turned.astype(bfloat)
        term(1, head, d_raw[2 + head], normed)
    span = width // 3

    def d_input(tile, carried):
        columns = pl.ds(pl.multiple_of(tile * span, span), span)
        made = dot_nn(d_raw[0], rows_ref[0, 0:HD, columns])
        made = made + dot_nn(d_raw[1], rows_ref[0, HD:, columns])
        made = made + dot_nn(d_raw[2], rows_ref[1, 0:HD, columns])
        made = made + dot_nn(d_raw[3], rows_ref[1, HD:, columns])
        out_rows[0, :, :, columns] = made.reshape(2, half, span).astype(bfloat)
        return carried

    for slot in range(2):
        for head in range(2):
            place(slot, head, False)
    blocks_ref = parts.reshape(chips, 2 * share, width)
    ring.scatter_step(blocks_ref, held, 0)
    lax.fori_loop(0, 3, d_input, 0)
    across = quad_copy(out_rows.at[0, 1 - core], across_got, 6, to_core)
    mine = pl.ds(pl.multiple_of(side * (half // 2), half // 2), half // 2)
    other = pl.ds(pl.multiple_of((1 - side) * (half // 2), half // 2), half // 2)
    along = quad_copy(along_put, along_got, 7, to_side)
    across.start()

    def body(step, carried):
        ring.scatter_step(blocks_ref, held, step)

        @pl.when(step == 1)
        def _():
            across.wait()
            given = out_rows[0, core, other].astype(single) + across_got[other].astype(single)
            along_put[...] = given.astype(bfloat)
            along.start()
            tokens_ref[...] = out_rows[0, core, mine].astype(single) + across_got[mine].astype(single)

        @pl.when(step == 4)
        def _():
            along.wait()
            tokens_ref[...] = tokens_ref[...] + along_got[...].astype(single)
            d_norm, d_gain = norm_back(resid_ref[...], scales_ref[0:1], tokens_ref[...])
            tokens_ref[...] = d_mid_ref[...] + d_norm
            value[0] = gains_ref[...]
            value[0, 0:1] = d_gain
            gains_total.start()

        @pl.when(step == 5)
        def _():
            gains_total.over_cores()

        @pl.when(step == 6)
        def _():
            gains_total.over_ring()

        return carried

    lax.fori_loop(1, chips - 1, body, 0)
    total_ref[...] = gains_total.end()
    out_ring.scatter_end(out_parts, out_held, sum_ref.at[pl.ds(2 * share, share)])
    ring.scatter_end(blocks_ref, held, sum_ref.at[pl.ds(0, 2 * share)])
    ring.finish(held.at[0, 0, 0 : ring.size])
    out_ring.finish(out_held.at[0, 0, 0 : out_ring.size])

    def settle(step, carried):
        for way, kind in streams:
            key_copy(way, kind, step, True).wait_send()
        return carried

    lax.fori_loop(0, chips - 1, settle, 0)
    for kind in range(3):
        bulk(kind).wait()


def tail(
    d_proj, query, keyval, attended, inverse, rows, normed, turns, locals_, own, other, chips, ident
):
    tokens = query.shape[1]
    tok_rows = tokens // 4
    width = rows.shape[2]
    share = tokens // 8
    half = tokens // 2
    vmem = pl.BlockSpec(memory_space=pltpu.VMEM)
    anywhere = pl.BlockSpec(memory_space=pl.ANY)
    return pl.pallas_call(
        functools.partial(tail_kernel, chips),
        out_shape=(
            jax.ShapeDtypeStruct((3 * share, width), single),
            jax.ShapeDtypeStruct((tok_rows, width), single),
            jax.ShapeDtypeStruct((4, width), single),
            jax.ShapeDtypeStruct(own.shape[1:], bfloat),
            jax.ShapeDtypeStruct(own.shape[1:], bfloat),
        ),
        in_specs=[vmem] * 2
        + [anywhere, vmem, vmem, anywhere, anywhere]
        + [vmem] * 8
        + [anywhere] * 2,
        out_specs=(vmem,) * 3 + (anywhere,) * 2,
        scratch_shapes=[
            pltpu.VMEM(keyval.shape, bfloat),
            pltpu.VMEM(rows.shape, bfloat),
            pltpu.VMEM(normed.shape, bfloat),
            pltpu.VMEM((2, 2, tok_rows, width), bfloat),
            pltpu.VMEM((2, tokens, HD), bfloat),
            pltpu.VMEM((2, tokens, 128), single),
            pltpu.VMEM((2, tokens, HD), single),
            pltpu.VMEM((2, 2, half, HD), single),
            pltpu.VMEM((2, 2, half, HD), bfloat),
            pltpu.VMEM((2, chips - 1, 2, half, HD), bfloat),
            pltpu.VMEM((4, tokens, HD), bfloat),
            pltpu.VMEM((4, tokens, HD), bfloat),
            pltpu.VMEM((3, 2, HD, width), bfloat),
            pltpu.VMEM((chips, 2, share, width), bfloat),
            pltpu.VMEM((chips, share, width), bfloat),
            pltpu.VMEM((2, chips - 1, share, width), bfloat),
            pltpu.VMEM((2, chips - 1, share // 2, width), bfloat),
            pltpu.VMEM((2 * tok_rows, width), bfloat),
            pltpu.VMEM((tok_rows, width), bfloat),
            pltpu.VMEM((tok_rows, width), bfloat),
        ]
        + total_scratch(chips, width)
        + [
            pltpu.SemaphoreType.DMA((2, 2, chips - 1)),
            pltpu.SemaphoreType.DMA((2, 2, chips - 1)),
            pltpu.SemaphoreType.DMA((3, 2, 4)),
            pltpu.SemaphoreType.DMA((3, 2, 4)),
            pltpu.SemaphoreType.DMA((2, 2, chips - 1)),
            pltpu.SemaphoreType.DMA((2, 2, chips - 1)),
            pltpu.SemaphoreType.DMA((2, 1, chips - 1)),
            pltpu.SemaphoreType.DMA((2, 1, chips - 1)),
            pltpu.SemaphoreType.DMA((8,)),
            pltpu.SemaphoreType.DMA((8,)),
            pltpu.SemaphoreType.DMA((7,)),
            pltpu.SemaphoreType.DMA((3,)),
            pltpu.SemaphoreType.DMA((3,)),
        ],
        compiler_params=pltpu.CompilerParams(
            collective_id=ident, has_side_effects=True, vmem_limit_bytes=63 * 2**20
        ),
        cost_estimate=cost(160),
    )(d_proj, query, keyval, attended, inverse, rows, normed, *turns, *locals_, own, other)


def feed_kernel(
    chips,
    pieces,
    resid_ref,
    projected_ref,
    dy_ref,
    scales_ref,
    own_ref,
    side_ref,
    core_ref,
    diag_ref,
    result_ref,
    d_mid_ref,
    d_projected_ref,
    d_gains_ref,
    terms_ref,
    other_ref,
    weights,
    x_all,
    y_all,
    mid,
    both,
    hidden,
    part,
    held,
    chunk,
    wide,
    stage,
    load_sem,
    bulk_send,
    bulk_recv,
    stage_sem,
    other_sem,
    send_sem,
    recv_sem,
):
    tok_rows, width = resid_ref.shape
    units = own_ref.shape[0] // 3
    whole = 4 * units
    half = tok_rows // 2
    rings = [
        Ring(chips, pieces, tok_rows, send_sem.at[phase], recv_sem.at[phase]) for phase in range(4)
    ]
    chip = rings[0].chip
    loads = []
    for slot, ref in enumerate((own_ref, side_ref, core_ref, diag_ref)):
        for kind in range(3 if slot % 2 == 0 else 2):
            loads.append(
                pltpu.make_async_copy(
                    ref.at[pl.ds(kind * units, units)],
                    weights.at[pl.ds(kind * whole + slot * units, units)],
                    load_sem.at[slot, kind],
                )
            )
    for load in loads:
        load.start()
    mid[...] = resid_ref[...] + norm_scale(projected_ref[...], scales_ref[1:2])
    x_all[chip] = norm_scale(mid[...], scales_ref[2:3]).astype(bfloat)
    core = lax.axis_index("fsdp") % 2
    to_core = {"fsdp": 2 * chip + 1 - core}
    to_side = {"head": 1 - lax.axis_index("head")}
    quad_barrier(to_side, to_core, rings[0].right, rings[0].left)
    down_rows = [pl.ds(2 * whole + slot * units, units) for slot in range(4)]
    bulk_side = remote(
        own_ref.at[pl.ds(2 * units, units)],
        weights.at[down_rows[1]],
        bulk_send.at[0],
        bulk_recv.at[0],
        to_side,
    )
    bulk_diag = remote(
        weights.at[down_rows[1]],
        weights.at[down_rows[3]],
        bulk_send.at[1],
        bulk_recv.at[1],
        to_core,
    )
    bulk_side.start()
    span = width // 3

    def segments(pair):
        for hop in range(2):
            for way in range(2):
                start = hop * tok_rows + way * half
                owner = rings[0].owner(way, 2 * pair + hop)
                yield owner, pl.ds(way * half, half), pl.ds(start, half)

    def fetch(all_ref, pair):
        for owner, rows, here in segments(pair):
            chunk[here] = all_ref[owner, rows]

    def put(ref, pair, columns, value):
        for owner, rows, here in segments(pair):
            ref[owner, rows, columns] = value[here.start : here.start + half].astype(ref.dtype)

    def take(ref, pair, columns):
        return jnp.concatenate(
            [ref[owner, rows, columns] for owner, rows, here in segments(pair)], axis=0
        )

    def polls(ring, all_ref, pair):
        def poll(index):
            @pl.when(2 * pair + 2 < chips)
            def _():
                ring.gather_step(all_ref, 2 * pair + 2 + index // 2, index % 2)

        return poll

    def forward(pair, carried):
        poll = polls(rings[0], x_all, pair)
        fetch(x_all, pair)
        for tile in range(3):
            rows = slice(tile * span, tile * span + span)
            wide[:, rows] = dot_nt(chunk[...], weights[rows])
            poll(tile)
        put(both, pair, slice(None), wide[...])
        value, slope = gelu_parts(wide[:, 0:whole])
        put(hidden, pair, slice(None), value * wide[:, whole:])
        poll(3)
        return carried

    def down(pair):
        chunk[:, 0:whole] = take(hidden, pair, slice(None))

        def columns_of(tile, carried):
            columns = pl.ds(pl.multiple_of(tile * span, span), span)
            put(part, pair, columns, dot_nn(chunk[:, 0:whole], weights[2 * whole :, columns]))
            return carried

        lax.fori_loop(0, 3, columns_of, 0)

    for step in range(2):
        for piece in range(pieces):
            rings[0].gather_step(x_all, step, piece)
        if step == 0:
            for load in loads:
                load.wait()
    lax.fori_loop(0, chips // 2, forward, 0)
    bulk_side.wait_recv()
    bulk_diag.start()
    bulk_diag.wait_recv()
    down(0)

    def spread(step, carried):
        rings[1].scatter_step(part, held, step, 0)

        @pl.when((step % 2 == 0) & (step < chips - 2))
        def _():
            down(step // 2 + 1)

        rings[1].scatter_step(part, held, step, 1)
        return carried

    lax.fori_loop(0, chips - 1, spread, 0)
    ours = pl.ds(0, tok_rows)
    rings[1].scatter_end(part, held, wide)
    result_ref[...] = mid[...] + norm_scale(wide[ours], scales_ref[3:4])
    d_ffn, d_gain = norm_back(wide[ours], scales_ref[3:4], dy_ref[...])
    d_gains_ref[0:1] = jnp.zeros_like(d_gain)
    d_gains_ref[3:4] = d_gain
    y_all[chip] = d_ffn.astype(bfloat)
    rings[0].finish(x_all.at[0, 0 : rings[0].size])
    rings[1].finish(x_all.at[0, 0 : rings[0].size])
    bulk_side.wait_send()
    bulk_diag.wait_send()

    def d_input(pair):
        chunk[...] = take(both, pair, slice(None))

        def columns_of(tile, carried):
            columns = pl.ds(pl.multiple_of(tile * span, span), span)
            put(part, pair, columns, dot_nn(chunk[...], weights[0 : 2 * whole, columns]))
            return carried

        lax.fori_loop(0, 3, columns_of, 0)

    third = whole // 3

    def d_units(pair, tile):
        columns = slice(tile * third, tile * third + third)
        ups = slice(whole + tile * third, whole + tile * third + third)
        for owner, rows, here in segments(pair):
            value, slope = gelu_parts(both[owner, rows, columns].astype(single))
            upper = both[owner, rows, ups].astype(single)
            d_hidden = wide[here, columns]
            both[owner, rows, columns] = (d_hidden * upper * slope).astype(bfloat)
            both[owner, rows, ups] = (d_hidden * value).astype(bfloat)

    def backward(pair, carried):
        poll = polls(rings[2], y_all, pair)
        fetch(y_all, pair)
        wide[:, 0 : 2 * third] = dot_nt(chunk[...], weights[2 * whole : 2 * whole + 2 * third])
        poll(0)
        wide[:, 2 * third : whole] = dot_nt(chunk[...], weights[2 * whole + 2 * third :])
        d_units(pair, 0)
        poll(1)
        d_units(pair, 1)
        d_units(pair, 2)
        poll(2)

        @pl.when(pair < 2)
        def _():
            d_input(pair)

        poll(3)
        return carried

    for step in range(2):
        for piece in range(pieces):
            rings[2].gather_step(y_all, step, piece)
    lax.fori_loop(0, chips // 2, backward, 0)
    rows_tile = stage.shape[1]
    tiles = 3 * whole // rows_tile
    upper_tiles = 2 * whole // rows_tile

    cut = units // 3

    def pieces_of(tile):
        for quarter in range(4):
            block = 4 * tile + quarter
            kind, slot, third = block // 12, (block // 3) % 4, block % 3
            source = stage.at[tile % 2, pl.ds(quarter * cut, cut)]
            rows = pl.ds(pl.multiple_of(kind * units + third * cut, cut), cut)
            sem = stage_sem.at[tile % 2, quarter]
            goal = terms_ref.at[slot, rows], other_ref.at[slot - 2, rows]
            there = functools.partial(
                remote, source, goal[1], sem, other_sem.at[tile, quarter], to_core
            )
            yield slot, functools.partial(pltpu.make_async_copy, source, goal[0], sem), there

    def keep(tile):
        for slot, here, there in pieces_of(tile):

            @pl.when(slot < 2)
            def _():
                here().start()

            @pl.when(slot >= 2)
            def _():
                there().start()

    def kept(tile):
        for slot, here, there in pieces_of(tile):

            @pl.when(slot < 2)
            def _():
                here().wait()

            @pl.when(slot >= 2)
            def _():
                there().wait_send()

    def grads(tile):
        @pl.when(tile >= 2)
        def _():
            kept(tile - 2)

        @pl.when(tile < upper_tiles)
        def _():
            columns = pl.ds(pl.multiple_of(tile * rows_tile, rows_tile), rows_tile)
            left = both[:, :, columns].reshape(chips * tok_rows, rows_tile)
            stage[tile % 2] = dot_tn(left, x_all[...].reshape(chips * tok_rows, width)).astype(bfloat)

        @pl.when(tile >= upper_tiles)
        def _():
            columns = pl.ds(
                pl.multiple_of((tile - upper_tiles) * rows_tile, rows_tile), rows_tile
            )
            left = hidden[:, :, columns].reshape(chips * tok_rows, rows_tile)
            stage[tile % 2] = dot_tn(left, y_all[...].reshape(chips * tok_rows, width)).astype(bfloat)

        keep(tile)

    def first_tile(step):
        return 2 * ((step + 1) // 2) + (step // 6) * (1 - step // 7)

    def spread_back(step, carried):
        rings[3].scatter_step(part, held, step, 0)

        @pl.when((step == 1) | (step == 3))
        def _():
            d_input(2 + step // 2)

        @pl.when(step % 2 == 0)
        def _():
            grads(first_tile(step))

        rings[3].scatter_step(part, held, step, 1)

        @pl.when((step % 2 == 0) & (step < 6) | (step == 5))
        def _():
            grads(first_tile(step + 1) - 1)

        return carried

    lax.fori_loop(0, chips - 1, spread_back, 0)
    lax.fori_loop(chips, tiles, lambda tile, carried: grads(tile) or carried, 0)
    rings[3].scatter_end(part, held, wide)
    d_norm, d_gain = norm_back(mid[...], scales_ref[2:3], wide[ours])
    d_gains_ref[2:3] = d_gain
    d_mid_ref[...] = dy_ref[...] + d_norm
    d_projected, d_gain = norm_back(projected_ref[...], scales_ref[1:2], d_mid_ref[...])
    d_gains_ref[1:2] = d_gain
    d_projected_ref[...] = d_projected.astype(bfloat)
    rings[2].finish(x_all.at[0, 0 : rings[0].size])
    rings[3].finish(x_all.at[0, 0 : rings[0].size])
    kept(tiles - 2)
    kept(tiles - 1)

    def gained(tile, carried):
        for slot, here, there in pieces_of(tile):

            @pl.when(slot >= 2)
            def _():
                there().wait_recv()

        return carried

    lax.fori_loop(0, tiles, gained, 0)


def feed_forward(resid_in, projected, grad_out, scales, shares, chips, ident):
    tok_rows, width = resid_in.shape
    units = shares[0].shape[0] // 3
    whole = 4 * units
    pieces = 2
    vmem = pl.BlockSpec(memory_space=pltpu.VMEM)
    anywhere = pl.BlockSpec(memory_space=pl.ANY)
    return pl.pallas_call(
        functools.partial(feed_kernel, chips, pieces),
        out_shape=(
            jax.ShapeDtypeStruct((tok_rows, width), single),
            jax.ShapeDtypeStruct((tok_rows, width), single),
            jax.ShapeDtypeStruct((tok_rows, width), bfloat),
            jax.ShapeDtypeStruct((4, width), single),
            jax.ShapeDtypeStruct((2, 3 * units, width), bfloat),
            jax.ShapeDtypeStruct((2, 3 * units, width), bfloat),
        ),
        in_specs=[vmem] * 4 + [anywhere] * 4,
        out_specs=(vmem, vmem, vmem, vmem, anywhere, anywhere),
        scratch_shapes=[
            pltpu.VMEM((3 * whole, width), bfloat),
            pltpu.VMEM((chips, tok_rows, width), bfloat),
            pltpu.VMEM((chips, tok_rows, width), bfloat),
            pltpu.VMEM((tok_rows, width), single),
            pltpu.VMEM((chips, tok_rows, 2 * whole), bfloat),
            pltpu.VMEM((chips, tok_rows, whole), bfloat),
            pltpu.VMEM((chips, tok_rows, width), bfloat),
            pltpu.VMEM((2, chips - 1, tok_rows // 2, width), bfloat),
            pltpu.VMEM((2 * tok_rows, width), bfloat),
            pltpu.VMEM((2 * tok_rows, width), single),
            pltpu.VMEM((2, whole // 3, width), bfloat),
            pltpu.SemaphoreType.DMA((4, 3)),
            pltpu.SemaphoreType.DMA((2,)),
            pltpu.SemaphoreType.DMA((2,)),
            pltpu.SemaphoreType.DMA((2, 4)),
            pltpu.SemaphoreType.DMA((9, 4)),
            pltpu.SemaphoreType.DMA((4, 2, pieces, chips - 1)),
            pltpu.SemaphoreType.DMA((4, 2, pieces, chips - 1)),
        ],
        compiler_params=pltpu.CompilerParams(
            collective_id=ident, has_side_effects=True, vmem_limit_bytes=63 * 2**20
        ),
        cost_estimate=cost(205),
    )(resid_in, projected, grad_out, scales, *shares)


def general_device(
    tokens,
    cotangent,
    gains,
    gains_first,
    gains_second,
    attn_weight,
    attn_first,
    attn_second,
    ffn_weight,
    ffn_first,
    ffn_second,
):
    devices = lax.axis_size("fsdp")
    chips = devices // 2
    side = lax.axis_index("head")
    place = lax.axis_index("fsdp")
    core, chip = place % 2, place // 2
    tok_rows = tokens.shape[1]
    super_rows = 4 * tok_rows
    seq_len = min(SEQ_LEN, super_rows * chips)
    share = attn_weight.shape[1]
    pairs = chips // 4
    width = tokens.shape[2]
    scale = 1.0 / math.sqrt(HD)

    def swap_core(value):
        return lax.ppermute(value, "fsdp", [(index, index ^ 1) for index in range(devices)])

    def swap_side(value):
        return lax.ppermute(value, "head", [(0, 1), (1, 0)])

    def in_order(own, other, index, axis):
        return jnp.where(
            index == 0, jnp.stack([own, other], axis), jnp.stack([other, own], axis)
        )

    def pick(value, index, axis=0):
        return lax.dynamic_index_in_dim(value, index, axis, keepdims=False)

    def quad_gather(value):
        value = in_order(value, swap_side(value), side, 0)
        value = in_order(value, swap_core(value), core, 0)
        return value.reshape((super_rows,) + value.shape[3:])

    def quad_scatter(partial):
        partial = partial.reshape(2, 2, tok_rows, width)
        mine = pick(partial, core) + swap_core(pick(partial, 1 - core).astype(bfloat)).astype(single)
        return pick(mine, side) + swap_side(pick(mine, 1 - side).astype(bfloat)).astype(single)

    scales = lax.all_gather(gains.astype(bfloat), ("head", "fsdp"), axis=1, tiled=True).astype(single)
    attn_low = attn_weight.astype(bfloat)
    ffn_low = ffn_weight.astype(bfloat).transpose(1, 0, 2)
    ffn_pair = jnp.concatenate([ffn_low, swap_side(ffn_low)], axis=1)

    ring_rows = ring_gather(attn_low.reshape(3 * share, width), chips, 0)
    ring_rows = ring_rows.reshape(2, 2, pairs, 3, share, width)

    def query_rows(slot):
        rows = ring_rows[:, :, :, slot]
        other = swap_core(pick(rows, 1 - core))
        return in_order(pick(rows, core), other, core, 2).reshape(2 * HD, width)

    def keyval_rows():
        rows = ring_rows[:, :, :, 1]
        other = swap_core(pick(rows, 1 - core, 1))
        return in_order(pick(rows, core, 1), other, core, 2).reshape(2 * HD, width)

    w_query, w_keyval, w_out = query_rows(0), keyval_rows(), query_rows(2)

    resid_in = tokens[0]
    grad_out = cotangent[0]
    normed_one = norm_scale(resid_in, scales[0]).astype(bfloat)
    normed_all = quad_gather(normed_one)
    positions = chip * super_rows + jnp.arange(super_rows, dtype=jnp.int32)
    angles = turn_angles(positions % seq_len, HD)
    query_raw = jnp.einsum("td,fd->tf", normed_all, w_query, preferred_element_type=single)
    keyval_raw = jnp.einsum("td,fd->tf", normed_all, w_keyval, preferred_element_type=single)
    query = rotate(query_raw.reshape(super_rows, 2, HD), angles, 1.0).astype(bfloat)
    key_angles = jnp.where(side == 0, angles, 0.0)
    keyval = rotate(keyval_raw.reshape(super_rows, 2, HD), key_angles, 1.0).astype(bfloat)
    keyval = in_order(pick(keyval, side, 1), swap_side(pick(keyval, 1 - side, 1)), side, 0)
    keyval_all = ring_gather(keyval.reshape(2 * super_rows, HD), chips, 1)
    keyval_all = keyval_all.reshape(chips, 2, super_rows, HD)
    key_all = keyval_all[:, 0].reshape(chips * super_rows, HD)
    value_all = keyval_all[:, 1].reshape(chips * super_rows, HD)

    key_pos = jnp.arange(chips * super_rows, dtype=jnp.int32)
    distance = positions[:, None] - key_pos[None, :]
    same_seq = (positions // seq_len)[:, None] == (key_pos // seq_len)[None, :]
    allowed = (distance >= 0) & (distance < WIN) & same_seq

    def score_block():
        raw = jnp.einsum("qgd,kd->gqk", query, key_all, preferred_element_type=single)
        bent = jnp.tanh(raw * (scale / softcap))
        return bent, jnp.where(allowed, jnp.exp(softcap * bent), 0.0)

    bent, powers = score_block()
    total = jnp.sum(powers, axis=-1, keepdims=True)
    attended = jnp.einsum(
        "gqk,kd->gqd", powers.astype(bfloat), value_all, preferred_element_type=single
    )
    attended = (attended / total).transpose(1, 0, 2).reshape(super_rows, 2 * HD).astype(bfloat)
    projected = quad_scatter(jnp.dot(attended, w_out, preferred_element_type=single))
    resid_mid = resid_in + norm_scale(projected, scales[1])
    normed_two = norm_scale(resid_mid, scales[2]).astype(bfloat)

    ffn_all = jnp.concatenate([ffn_pair, swap_core(ffn_pair)], axis=1)
    w_gate, w_up, w_down = ffn_all[0], ffn_all[1], ffn_all[2]
    ring_tokens = chips * tok_rows
    normed_ring = ring_gather(normed_two, chips, 2).reshape(ring_tokens, width)
    gate_part = jnp.einsum("td,rd->tr", normed_ring, w_gate, preferred_element_type=single)
    up_part = jnp.einsum("td,rd->tr", normed_ring, w_up, preferred_element_type=single)
    hidden = hidden_unit(gate_part, up_part).astype(bfloat)
    ffn_part = jnp.dot(hidden, w_down, preferred_element_type=single).astype(bfloat)
    ffn_acc = ring_scatter(ffn_part.reshape(chips, tok_rows, width), chips, 3)
    result = resid_mid + norm_scale(ffn_acc, scales[3])

    ignored, post_back = jax.vjp(norm_scale, ffn_acc, scales[3])
    d_ffn, d_gain3 = post_back(grad_out)
    d_ffn_ring = ring_gather(d_ffn.astype(bfloat), chips, 4).reshape(ring_tokens, width)
    d_hidden = jnp.einsum("td,rd->tr", d_ffn_ring, w_down, preferred_element_type=single)
    ignored, unit_back = jax.vjp(hidden_unit, gate_part, up_part)
    d_gate, d_up = unit_back(d_hidden)
    d_gate = d_gate.astype(bfloat)
    d_up = d_up.astype(bfloat)
    d_normed = jnp.dot(d_gate, w_gate, preferred_element_type=single)
    d_normed = (d_normed + jnp.dot(d_up, w_up, preferred_element_type=single)).astype(bfloat)
    d_normed_two = ring_scatter(d_normed.reshape(chips, tok_rows, width), chips, 5)

    def ffn_rows(left, right):
        return jnp.einsum("tr,td->rd", left, right, preferred_element_type=single)

    ffn_terms = jnp.stack(
        [ffn_rows(d_gate, normed_ring), ffn_rows(d_up, normed_ring), ffn_rows(hidden, d_ffn_ring)]
    )
    units = ffn_weight.shape[0]
    ffn_terms = ffn_terms.reshape(3, 2, 2, units, width)
    ffn_terms = ffn_terms[:, 0] + swap_core(ffn_terms[:, 1].astype(bfloat)).astype(single)
    grad_ffn = ffn_terms[:, 0] + swap_side(ffn_terms[:, 1].astype(bfloat)).astype(single)

    ignored, mid_back = jax.vjp(norm_scale, resid_mid, scales[2])
    d_mid_norm, d_gain2 = mid_back(d_normed_two)
    d_mid = grad_out + d_mid_norm
    ignored, proj_back = jax.vjp(norm_scale, projected, scales[1])
    d_projected, d_gain1 = proj_back(d_mid)
    d_proj_all = quad_gather(d_projected.astype(bfloat))
    d_attended = jnp.einsum("td,fd->tf", d_proj_all, w_out, preferred_element_type=single)
    d_attended = d_attended.astype(bfloat).reshape(super_rows, 2, HD)

    bent, powers = score_block()
    probs = powers / total
    d_probs = jnp.einsum("qgd,kd->gqk", d_attended, value_all, preferred_element_type=single)
    row_dot = jnp.sum(d_probs * probs, axis=-1, keepdims=True)
    d_raw = (probs * (d_probs - row_dot) * (1.0 - bent * bent)).astype(bfloat)
    d_query = jnp.einsum("gqk,kd->qgd", d_raw, key_all, preferred_element_type=single) * scale
    d_keys = jnp.einsum("gqk,qgd->kd", d_raw, query, preferred_element_type=single) * scale
    d_values = jnp.einsum(
        "gqk,qgd->kd", probs.astype(bfloat), d_attended, preferred_element_type=single
    )
    d_pieces = jnp.stack(
        [d_keys.reshape(chips, super_rows, HD), d_values.reshape(chips, super_rows, HD)], axis=1
    ).astype(bfloat)
    d_keyval = ring_scatter(d_pieces.reshape(chips, 2 * super_rows, HD), chips, 6)
    d_keyval = d_keyval.reshape(2, super_rows, HD).astype(bfloat)
    d_keyval = in_order(pick(d_keyval, side), swap_side(pick(d_keyval, 1 - side)), side, 1)
    d_query_raw = rotate(d_query, angles, -1.0).reshape(super_rows, 2 * HD).astype(bfloat)
    d_keyval_raw = rotate(d_keyval.astype(single), key_angles, -1.0)
    d_keyval_raw = d_keyval_raw.reshape(super_rows, 2 * HD).astype(bfloat)
    d_normed_one = jnp.dot(d_query_raw, w_query, preferred_element_type=single)
    d_normed_one = d_normed_one + jnp.dot(d_keyval_raw, w_keyval, preferred_element_type=single)
    d_normed_one = quad_scatter(d_normed_one)
    ignored, first_back = jax.vjp(norm_scale, resid_in, scales[0])
    d_in_norm, d_gain0 = first_back(d_normed_one)
    tokens_grad = d_mid + d_in_norm

    def attn_rows(left, right):
        rows = jnp.einsum("tf,td->fd", left, right, preferred_element_type=single).astype(bfloat)
        return rows.reshape(2, pairs, 2, share, width)

    term_query = attn_rows(d_query_raw, normed_all)
    term_keyval = attn_rows(d_keyval_raw, normed_all)
    term_out = attn_rows(attended, d_proj_all)

    def to_core(term, axis):
        return in_order(pick(term, core, 2), swap_core(pick(term, 1 - core, 2)), core, axis)

    terms = jnp.stack([to_core(term_query, 0), to_core(term_keyval, 1), to_core(term_out, 0)], axis=3)
    grad_attn = ring_scatter(terms.reshape(chips, 3 * share, width), chips, 7)
    grad_attn = grad_attn.reshape(3, share, width)
    term_gain = jnp.stack([d_gain0, d_gain1, d_gain2, d_gain3])
    grad_gain = lax.psum_scatter(term_gain, ("head", "fsdp"), scatter_dimension=1, tiled=True)

    gains_first_new, gains_second_new, gains_new = adamw(
        gains, gains_first, gains_second, grad_gain, rate_gain, 0.0
    )
    attn_first_new, attn_second_new, attn_weight_new = adamw(
        attn_weight, attn_first, attn_second, grad_attn, rate_matrix, decay_matrix
    )
    ffn_first_new, ffn_second_new, ffn_weight_new = adamw(
        ffn_weight, ffn_first, ffn_second, grad_ffn.transpose(1, 0, 2), rate_matrix, decay_matrix
    )
    return (
        result[None],
        tokens_grad[None],
        gains_first_new,
        gains_second_new,
        gains_new,
        attn_first_new,
        attn_second_new,
        attn_weight_new,
        ffn_first_new,
        ffn_second_new,
        ffn_weight_new,
    )


def step_kernel(
    tiles,
    weight_ref,
    first_ref,
    second_ref,
    own_ref,
    other_ref,
    side_ref,
    weight_two_ref,
    first_two_ref,
    second_two_ref,
    grad_two_ref,
    first_out,
    second_out,
    weight_out,
    first_two_out,
    second_two_out,
    weight_two_out,
):
    index = pl.program_id(0)

    @pl.when(index < tiles)
    def _():
        grad = own_ref[0].astype(single) + other_ref[0].astype(single)
        grad = grad + side_ref[...].astype(single)
        first_out[...], second_out[...], weight_out[...] = adamw(
            weight_ref[...], first_ref[...], second_ref[...], grad, rate_matrix, decay_matrix
        )

    @pl.when(index >= tiles)
    def _():
        first_two_out[...], second_two_out[...], weight_two_out[...] = adamw(
            weight_two_ref[...],
            first_two_ref[...],
            second_two_ref[...],
            grad_two_ref[...],
            rate_matrix,
            decay_matrix,
        )


def step_weights(state, own, other, side, state_two, grad_two):
    rows, width = state[0].shape
    rows_two = grad_two.shape[0]
    size = 96
    tiles, tiles_two = rows // size, rows_two // size
    block = pl.BlockSpec((size, width), lambda index: (jnp.minimum(index, tiles - 1), 0))
    half = pl.BlockSpec((1, size, width), lambda index: (0, jnp.minimum(index, tiles - 1), 0))
    block_two = pl.BlockSpec((size, width), lambda index: (jnp.maximum(index - tiles, 0), 0))
    return pl.pallas_call(
        functools.partial(step_kernel, tiles),
        grid=(tiles + tiles_two,),
        out_shape=(jax.ShapeDtypeStruct((rows, width), single),) * 3
        + (jax.ShapeDtypeStruct((rows_two, width), single),) * 3,
        in_specs=[block] * 3 + [half, half, block] + [block_two] * 4,
        out_specs=(block,) * 3 + (block_two,) * 3,
        compiler_params=pltpu.CompilerParams(vmem_limit_bytes=62 * 2**20),
        cost_estimate=cost(20),
    )(*state, own, other, side, *state_two, grad_two)


def per_device(
    tokens,
    cotangent,
    gains,
    gains_first,
    gains_second,
    attn_weight,
    attn_first,
    attn_second,
    ffn_weight,
    ffn_first,
    ffn_second,
):
    devices = lax.axis_size("fsdp")
    chips = devices // 2
    side = lax.axis_index("head")
    place = lax.axis_index("fsdp")
    chip = place // 2
    tok_rows = tokens.shape[1]
    super_rows = 4 * tok_rows
    seq_len = min(SEQ_LEN, super_rows * chips)
    share = attn_weight.shape[1]
    width = tokens.shape[2]
    gain_columns = gains.shape[1]
    gain_start = (side * devices + place) * gain_columns

    units = ffn_weight.shape[0]

    def flat(value):
        return value.transpose(1, 0, 2).reshape(3 * units, width)

    ffn_wide = flat(ffn_weight)
    resid_in = tokens[0]
    grad_out = cotangent[0]
    positions = chip * super_rows + jnp.arange(super_rows, dtype=jnp.int32)
    angles = turn_angles(positions % seq_len, HD)
    key_angles = jnp.where(side == 0, angles, 0.0)
    gains_placed = lax.dynamic_update_slice(
        jnp.zeros((4, width), single), gains, (0, gain_start)
    )
    turns = (jnp.cos(angles), jnp.sin(angles), jnp.cos(key_angles), jnp.sin(key_angles))
    made = front(attn_weight, gains_placed, resid_in, turns, ffn_wide, chips, 0)
    attn_rows, scales, normed_all, query, keyval, attended, inverse, projected = made[:8]
    own_units, core_units, side_units, diag_units = made[8:]
    result, d_mid, d_proj_low, gain_rows, terms_own, terms_other = feed_forward(
        resid_in,
        projected,
        grad_out,
        scales,
        (own_units, side_units, core_units, diag_units),
        chips,
        1,
    )
    grad_attn, tokens_grad, gain_total, terms_sent, terms_side = tail(
        d_proj_low,
        query,
        keyval,
        attended,
        inverse,
        attn_rows,
        normed_all,
        turns,
        (resid_in, d_mid, scales, gain_rows),
        terms_own,
        terms_other,
        chips,
        2,
    )
    grad_ffn = terms_own[0].astype(single) + terms_other[0].astype(single)
    grad_ffn = grad_ffn + terms_side.astype(single)
    grad_gain = lax.dynamic_slice(gain_total, (0, gain_start), gains.shape)

    gains_first_new, gains_second_new, gains_new = adamw(
        gains, gains_first, gains_second, grad_gain, rate_gain, 0.0
    )
    def rows_of(value):
        return value.reshape(3 * share, width)

    stepped = step_weights(
        (ffn_wide, flat(ffn_first), flat(ffn_second)),
        terms_own,
        terms_other,
        terms_side,
        (rows_of(attn_weight), rows_of(attn_first), rows_of(attn_second)),
        grad_attn,
    )
    ffn_first_new, ffn_second_new, ffn_weight_new = (
        value.reshape(3, units, width).transpose(1, 0, 2) for value in stepped[:3]
    )
    attn_first_new, attn_second_new, attn_weight_new = (
        value.reshape(3, share, width) for value in stepped[3:]
    )
    return (
        result[None],
        tokens_grad[None],
        gains_first_new,
        gains_second_new,
        gains_new,
        attn_first_new,
        attn_second_new,
        attn_weight_new,
        ffn_first_new,
        ffn_second_new,
        ffn_weight_new,
    )


def solution(mesh):
    by_token = P("fsdp", "head", None)
    by_column = P(None, ("head", "fsdp"))
    by_row = P(None, ("head", "fsdp"), None)
    by_unit = P(("head", "fsdp"), None, None)
    placed = (by_token,) * 2 + (by_column,) * 3 + (by_row,) * 3 + (by_unit,) * 3
    body = per_device if mesh.shape["fsdp"] == 16 else general_device
    return jax.shard_map(
        body, mesh=mesh, in_specs=placed, out_specs=placed, check_vma=False
    )
```

```python
import functools
import math

import jax
import jax.numpy as jnp
from jax import lax
from jax.experimental import pallas as pl
from jax.experimental.pallas import tpu as pltpu
from jax.sharding import PartitionSpec as P

HQ = 8
HK = 4
HD = 256
WIN = 4096
STEP = 10
SEQ_LEN = 8192


eps_norm = 1e-06
softcap = 50.0
beta_one = 0.9
beta_two = 0.95
adam_eps = 1e-08
rate_matrix = 0.02
rate_gain = 0.2
decay_matrix = 0.1

bfloat = jnp.bfloat16
single = jnp.float32
MESH = pl.DeviceIdType.MESH


def norm_scale(values, scales):
    return (
        values
        * lax.rsqrt(jnp.mean(values * values, axis=-1, keepdims=True) + eps_norm)
        * (1.0 + scales)
    )


def turn_angles(positions, head_width):
    halfway = head_width // 2
    inverse_freq = 10000.0 ** (-(jnp.arange(halfway, dtype=jnp.float32) * 2.0) / head_width)
    return positions.astype(jnp.float32)[:, None] * inverse_freq[None, :]


def rotate(values, angles, direction):
    halfway = values.shape[-1] // 2
    cosine = jnp.cos(angles)[:, None, :]
    sine_part = direction * jnp.sin(angles)[:, None, :]
    former = values[..., :halfway]
    latter = values[..., halfway:]
    return jnp.concatenate(
        [former * cosine - latter * sine_part, latter * cosine + former * sine_part], axis=-1
    )


def adamw(weight, moment, second, gradient, step_rate, decay_rate):
    moment = beta_one * moment + (1.0 - beta_one) * gradient
    second = beta_two * second + (1.0 - beta_two) * gradient * gradient
    update = (
        moment / (1.0 - beta_one**STEP) / (jnp.sqrt(second / (1.0 - beta_two**STEP)) + adam_eps)
        + decay_rate * weight
    )
    return (moment, second, weight - step_rate * update)


def hidden_unit(gate_part, up_part):
    return jax.nn.gelu(gate_part, approximate=True) * up_part


def ring_of(chip, chips):
    wide = chips // 4
    deep, side = chip // wide, chip % wide
    return side * 4 + deep + (side % 2) * (3 - 2 * deep)


def chip_of(ring, chips):
    wide = chips // 4
    side, along = ring // 4, ring % 4
    return (along + (side % 2) * (3 - 2 * along)) * wide + side


def ring_places(chips):
    index = lax.axis_index("fsdp")
    core, chip = index % 2, index // 2
    ring = ring_of(chip, chips)
    right = 2 * chip_of((ring + 1) % chips, chips) + core
    left = 2 * chip_of((ring + chips - 1) % chips, chips) + core
    return chip, ring, right, left


def ring_barrier(right, left):
    barrier = pltpu.get_barrier_semaphore()
    for neighbour in (left, right):
        pl.semaphore_signal(barrier, inc=1, device_id={"fsdp": neighbour}, device_id_type=MESH)
    pl.semaphore_wait(barrier, 2)


def region(shape, pieces, way, piece):
    rows, columns = shape
    if rows % 32 == 0:
        size = rows // 2 // pieces
        start = way * (rows // 2) + piece * size
        return (pl.ds(start, size), pl.ds(0, columns)), (pl.ds(piece * size, size), pl.ds(0, columns))
    size = columns // 2
    return (pl.ds(0, rows), pl.ds(way * size, size)), (pl.ds(0, rows), pl.ds(0, size))


def half_shape(rows, columns):
    return (rows // 2, columns) if rows % 32 == 0 else (rows, columns // 2)


def gather_kernel(chips, pieces, own_ref, all_ref, local_sem, send_sem, recv_sem):
    chip, ring, right, left = ring_places(chips)
    ring_barrier(right, left)
    keep = pltpu.make_async_copy(own_ref, all_ref.at[chip], local_sem)
    keep.start()

    def copy(way, step, piece, first):
        owner = chip_of((ring + (chips - step if way == 0 else step)) % chips, chips)
        part, ignored = region(own_ref.shape, pieces, way, piece)
        there = all_ref.at[(owner,) + part]
        return pltpu.make_async_remote_copy(
            src_ref=own_ref.at[part] if first else there,
            dst_ref=there,
            send_sem=send_sem.at[way, piece, step],
            recv_sem=recv_sem.at[way, piece, step],
            device_id={"fsdp": right if way == 0 else left},
            device_id_type=MESH,
        )

    streams = [(way, piece) for piece in range(pieces) for way in range(2)]
    for way, piece in streams:
        copy(way, 0, piece, True).start()

    def body(step, carried):
        for way, piece in streams:
            copy(way, step - 1, piece, False).wait_recv()
            copy(way, step, piece, False).start()
        return carried

    lax.fori_loop(1, chips - 1, body, 0)
    for way, piece in streams:
        copy(way, chips - 2, piece, False).wait_recv()

    def finish(step, carried):
        for way, piece in streams:
            copy(way, step, piece, False).wait_send()
        return carried

    lax.fori_loop(0, chips - 1, finish, 0)
    keep.wait()


def ring_gather(own, chips, ident):
    rows, columns = own.shape
    pieces = 2 if rows % 64 == 0 else 1
    return pl.pallas_call(
        functools.partial(gather_kernel, chips, pieces),
        out_shape=jax.ShapeDtypeStruct((chips, rows, columns), own.dtype),
        in_specs=[pl.BlockSpec(memory_space=pl.ANY)],
        out_specs=pl.BlockSpec(memory_space=pl.ANY),
        scratch_shapes=[
            pltpu.SemaphoreType.DMA,
            pltpu.SemaphoreType.DMA((2, pieces, chips - 1)),
            pltpu.SemaphoreType.DMA((2, pieces, chips - 1)),
        ],
        compiler_params=pltpu.CompilerParams(collective_id=ident, has_side_effects=True),
        cost_estimate=cost(45),
    )(own)


def scatter_kernel(chips, pieces, parts_ref, sum_ref, held, send_sem, recv_sem):
    chip, ring, right, left = ring_places(chips)
    ring_barrier(right, left)

    def owner_of(way, step):
        shift = chips - 1 - step if way == 0 else 1 + step
        return chip_of((ring + shift) % chips, chips)

    def copy(way, step, piece, first):
        part, place = region(sum_ref.shape, pieces, way, piece)
        return pltpu.make_async_remote_copy(
            src_ref=(
                parts_ref.at[(owner_of(way, step),) + part]
                if first
                else held.at[(way, step - 1) + place]
            ),
            dst_ref=held.at[(way, step) + place],
            send_sem=send_sem.at[way, piece, step],
            recv_sem=recv_sem.at[way, piece, step],
            device_id={"fsdp": right if way == 0 else left},
            device_id_type=MESH,
        )

    streams = [(way, piece) for piece in range(pieces) for way in range(2)]
    for way, piece in streams:
        copy(way, 0, piece, True).start()

    def arrived(way, step, piece):
        copy(way, step, piece, True).wait_recv()
        part, place = region(sum_ref.shape, pieces, way, piece)
        here = parts_ref[(owner_of(way, step + 1),) + part]
        return held[(way, step) + place].astype(single) + here.astype(single)

    def body(step, carried):
        for way, piece in streams:
            total = arrived(way, step - 1, piece)
            part, place = region(sum_ref.shape, pieces, way, piece)
            held[(way, step - 1) + place] = total.astype(held.dtype)
            copy(way, step, piece, False).start()
        return carried

    lax.fori_loop(1, chips - 1, body, 0)
    for way, piece in streams:
        part, place = region(sum_ref.shape, pieces, way, piece)
        sum_ref[part] = arrived(way, chips - 2, piece)

    def finish(step, carried):
        for way, piece in streams:
            copy(way, step, piece, True).wait_send()
        return carried

    lax.fori_loop(0, chips - 1, finish, 0)


def ring_scatter(parts, chips, ident):
    rows, columns = parts.shape[1:]
    pieces = 2 if rows % 64 == 0 else 1
    return pl.pallas_call(
        functools.partial(scatter_kernel, chips, pieces),
        out_shape=jax.ShapeDtypeStruct((rows, columns), single),
        in_specs=[pl.BlockSpec(memory_space=pltpu.VMEM)],
        out_specs=pl.BlockSpec(memory_space=pltpu.VMEM),
        scratch_shapes=[
            pltpu.VMEM((2, chips - 1) + half_shape(rows, columns), parts.dtype),
            pltpu.SemaphoreType.DMA((2, pieces, chips - 1)),
            pltpu.SemaphoreType.DMA((2, pieces, chips - 1)),
        ],
        compiler_params=pltpu.CompilerParams(
            collective_id=ident, has_side_effects=True, vmem_limit_bytes=56 * 2**20
        ),
        cost_estimate=cost(45),
    )(parts)


def norm_back(values, scales, grad):
    inverse = lax.rsqrt(jnp.mean(values * values, axis=-1, keepdims=True) + eps_norm)
    bent = grad * (1.0 + scales)
    slope = jnp.mean(bent * values, axis=-1, keepdims=True) * (inverse * inverse * inverse)
    return bent * inverse - values * slope, jnp.sum(grad * values * inverse, axis=0, keepdims=True)


def gelu_parts(gate):
    root = math.sqrt(2.0 / math.pi)
    square = gate * gate
    bend = jnp.tanh(root * gate * (1.0 + 0.044715 * square))
    half = 0.5 * (1.0 + bend)
    slope = half + 0.5 * gate * (1.0 - bend * bend) * (root * (1.0 + 3.0 * 0.044715 * square))
    return gate * half, slope


def dot_nt(left, right):
    return lax.dot_general(left, right, (((1,), (1,)), ((), ())), preferred_element_type=single)


def dot_nn(left, right):
    return lax.dot_general(left, right, (((1,), (0,)), ((), ())), preferred_element_type=single)


def dot_tn(left, right):
    return lax.dot_general(left, right, (((0,), (0,)), ((), ())), preferred_element_type=single)


class Ring:
    def __init__(self, chips, pieces, rows, send_sem, recv_sem):
        self.chips, self.pieces, self.half = chips, pieces, rows // 2
        self.size = rows // 2 // pieces
        self.chip, self.ring, self.right, self.left = ring_places(chips)
        self.send_sem, self.recv_sem = send_sem, recv_sem
        self.streams = [(way, piece) for piece in range(pieces) for way in range(2)]

    def owner(self, way, step):
        shift = self.chips - step if way == 0 else step
        return chip_of((self.ring + shift) % self.chips, self.chips)

    def copy(self, source, target, way, piece, step):
        return pltpu.make_async_remote_copy(
            src_ref=source,
            dst_ref=target,
            send_sem=self.send_sem.at[way, piece, step],
            recv_sem=self.recv_sem.at[way, piece, step],
            device_id={"fsdp": self.right if way == 0 else self.left},
            device_id_type=MESH,
        )

    def part(self, way, piece):
        return pl.ds(way * self.half + piece * self.size, self.size)

    def place(self, piece):
        return pl.ds(piece * self.size, self.size)

    def gather_copy(self, all_ref, way, piece, step):
        there = all_ref.at[self.owner(way, step), self.part(way, piece)]
        return self.copy(there, there, way, piece, step)

    def of(self, only):
        return [(way, piece) for way, piece in self.streams if only is None or piece == only]

    def gather_step(self, all_ref, step, only=None):
        for way, piece in self.of(only):

            @pl.when(step > 0)
            def _():
                self.gather_copy(all_ref, way, piece, step - 1).wait_recv()

            @pl.when(step < self.chips - 1)
            def _():
                self.gather_copy(all_ref, way, piece, step).start()

    def scatter_copy(self, parts_ref, held, way, piece, step, first):
        source = (
            parts_ref.at[self.owner(way, step + 1), self.part(way, piece)]
            if first
            else held.at[way, step - 1, self.place(piece)]
        )
        return self.copy(source, held.at[way, step, self.place(piece)], way, piece, step)

    def scatter_total(self, parts_ref, held, way, piece, step):
        self.scatter_copy(parts_ref, held, way, piece, step, True).wait_recv()
        here = parts_ref[self.owner(way, step + 2), self.part(way, piece)]
        return held[way, step, self.place(piece)].astype(single) + here.astype(single)

    def scatter_step(self, parts_ref, held, step, only=None):
        for way, piece in self.of(only):

            @pl.when(step == 0)
            def _():
                self.scatter_copy(parts_ref, held, way, piece, 0, True).start()

            @pl.when(step > 0)
            def _():
                total = self.scatter_total(parts_ref, held, way, piece, step - 1)
                held[way, step - 1, self.place(piece)] = total.astype(held.dtype)
                self.scatter_copy(parts_ref, held, way, piece, step, False).start()

    def scatter_end(self, parts_ref, held, sum_ref):
        for way, piece in self.streams:
            sum_ref[self.part(way, piece)] = self.scatter_total(
                parts_ref, held, way, piece, self.chips - 2
            )

    def finish(self, example):
        def body(step, carried):
            for way, piece in self.streams:
                self.copy(example, example, way, piece, step).wait_send()
            return carried

        lax.fori_loop(0, self.chips - 1, body, 0)


def quad_peers(chips):
    side = lax.axis_index("head")
    index = lax.axis_index("fsdp")
    chip, core = index // 2, index % 2
    ring = ring_of(chip, chips)
    around = [2 * chip_of((ring + hop) % chips, chips) + core for hop in range(1, chips)]
    return side, core, {"head": 1 - side}, {"fsdp": 2 * chip + 1 - core}, around


def wide_barrier(to_side, to_core, around):
    barrier = pltpu.get_barrier_semaphore()
    for target in [to_side, to_core] + [{"fsdp": other} for other in around]:
        pl.semaphore_signal(barrier, inc=1, device_id=target, device_id_type=MESH)
    pl.semaphore_wait(barrier, 2 + len(around))


def quad_barrier(to_side, to_core, right, left):
    barrier = pltpu.get_barrier_semaphore()
    for target in (to_side, to_core, {"fsdp": right}, {"fsdp": left}):
        pl.semaphore_signal(barrier, inc=1, device_id=target, device_id_type=MESH)
    pl.semaphore_wait(barrier, 4)


def remote(source, target, send_sem, recv_sem, device):
    return pltpu.make_async_remote_copy(
        src_ref=source,
        dst_ref=target,
        send_sem=send_sem,
        recv_sem=recv_sem,
        device_id=device,
        device_id_type=MESH,
    )


class Total:
    def __init__(self, value, near, blocks, send_sem, recv_sem, peers, chip):
        self.value, self.near, self.blocks = value, near, blocks
        self.send_sem, self.recv_sem = send_sem, recv_sem
        side, core, self.to_side, self.to_core, self.around = peers
        self.chip = chip
        self.first = remote(value.at[0], near.at[0], send_sem.at[0], recv_sem.at[0], self.to_side)
        self.second = remote(value.at[1], near.at[1], send_sem.at[1], recv_sem.at[1], self.to_core)

    def spread(self, hop):
        here = self.blocks.at[self.chip]
        return remote(
            here,
            here,
            self.send_sem.at[1 + hop],
            self.recv_sem.at[1 + hop],
            {"fsdp": self.around[hop - 1]},
        )

    def start(self):
        self.first.start()

    def over_cores(self):
        self.first.wait_recv()
        self.value[1] = self.value[0] + self.near[0]
        self.second.start()

    def over_ring(self):
        self.second.wait_recv()
        self.blocks[self.chip] = self.value[1] + self.near[1]
        for hop in range(1, len(self.around) + 1):
            self.spread(hop).start()

    def end(self):
        for hop in range(1, len(self.around) + 1):
            self.spread(hop).wait_recv()
        total = self.blocks[0]
        for other in range(1, len(self.around) + 1):
            total = total + self.blocks[other]
        self.first.wait_send()
        self.second.wait_send()
        for hop in range(1, len(self.around) + 1):
            self.spread(hop).wait_send()
        return total


def total_scratch(chips, width):
    return [
        pltpu.VMEM((2, 4, width), single),
        pltpu.VMEM((2, 4, width), single),
        pltpu.VMEM((chips, 4, width), single),
        pltpu.SemaphoreType.DMA((chips + 1,)),
        pltpu.SemaphoreType.DMA((chips + 1,)),
    ]


def turn(raw, cosine, sine):
    halfway = raw.shape[1] // 2
    former, latter = raw[:, :halfway], raw[:, halfway:]
    return jnp.concatenate(
        [former * cosine - latter * sine, latter * cosine + former * sine], axis=1
    )


def front_kernel(
    chips,
    cuts,
    own_ref,
    gains_ref,
    resid_ref,
    cosine_ref,
    sine_ref,
    key_cosine_ref,
    key_sine_ref,
    wide_units_ref,
    rows_out,
    scales_ref,
    normed_out,
    query_ref,
    keyval_out,
    attended_ref,
    inverse_ref,
    projected_ref,
    own_units_ref,
    core_units_ref,
    side_units_ref,
    diag_units_ref,
    rows_ref,
    normed_ref,
    keyval_ref,
    all_rows,
    both,
    total,
    sums,
    product,
    across_put,
    across_got,
    along_put,
    along_got,
    cast_in,
    cast_out,
    value,
    near,
    blocks,
    total_send,
    total_recv,
    send_sem,
    recv_sem,
    place_sem,
    peer_sem,
    key_send,
    key_recv,
    quad_send,
    quad_recv,
    cast_sem,
    out_sem,
    bulk_send,
    bulk_recv,
):
    share, width = own_ref.shape[1:]
    tok_rows = resid_ref.shape[0]
    tokens = 4 * tok_rows
    half = width // 2
    pairs = chips // 4
    scale = 1.0 / math.sqrt(HD)
    chip, ring, right, left = ring_places(chips)
    peers = quad_peers(chips)
    side, core, to_side, to_core, around = peers
    cast_rows = cast_in.shape[1]
    casts = wide_units_ref.shape[0] // cast_rows

    def cast_load(tile):
        rows = pl.ds(tile * cast_rows, cast_rows)
        return pltpu.make_async_copy(
            wide_units_ref.at[rows], cast_in.at[tile % 2], cast_sem.at[0, tile % 2]
        )

    def cast_store(tile):
        rows = pl.ds(tile * cast_rows, cast_rows)
        return pltpu.make_async_copy(
            cast_out.at[tile % 2], own_units_ref.at[rows], cast_sem.at[1, tile % 2]
        )

    def cast(first, last):
        for tile in range(first, last):
            cast_load(tile).wait()
            if tile >= 3:
                cast_store(tile - 2).wait()
            cast_out[tile % 2] = cast_in[tile % 2].astype(bfloat)
            cast_store(tile).start()
            if tile + 2 < casts:
                cast_load(tile + 2).start()

    outs = [
        pltpu.make_async_copy(rows_ref.at[0:2], rows_out.at[0:2], out_sem.at[0]),
        pltpu.make_async_copy(rows_ref.at[2], rows_out.at[2], out_sem.at[1]),
        pltpu.make_async_copy(normed_ref, normed_out, out_sem.at[2]),
        pltpu.make_async_copy(keyval_ref, keyval_out, out_sem.at[3]),
    ]
    cast_load(0).start()
    cast_load(1).start()
    all_rows[chip] = own_ref[...].astype(bfloat)
    value[0] = gains_ref[...].astype(bfloat).astype(single)
    wide_barrier(to_side, to_core, around)
    gains_total = Total(value, near, blocks, total_send, total_recv, peers, chip)
    gains_total.start()
    streams = [(way, slot) for slot in range(2) for way in range(2)]
    out_streams = [(way, 2) for way in range(2)]
    key_streams = [(way, kind) for kind in range(2) for way in range(2)]

    def owner_of(way, step):
        return chip_of((ring + (chips - step if way == 0 else step)) % chips, chips)

    def hop(way, slot, step):
        there = all_rows.at[owner_of(way, step), slot, :, pl.ds(way * half, half)]
        return remote(
            there,
            there,
            send_sem.at[way, slot, step],
            recv_sem.at[way, slot, step],
            {"fsdp": right if way == 0 else left},
        )

    def key_hop(way, kind, step):
        there = keyval_ref.at[owner_of(way, step), kind, pl.ds(way * (tokens // 2), tokens // 2)]
        return remote(
            there,
            there,
            key_send.at[way, kind, step],
            key_recv.at[way, kind, step],
            {"fsdp": right if way == 0 else left},
        )

    def goal(way, slot, step):
        owner = owner_of(way, step)
        deep = owner // pairs
        unit = (owner % pairs) * 2 + core
        taker, head = (deep % 2, deep // 2) if slot == 1 else (deep // 2, deep % 2)
        columns = pl.ds(way * half, half)
        source = all_rows.at[owner, slot, :, columns]
        start = pl.multiple_of(head * HD + unit * share, share)
        target = rows_ref.at[slot, pl.ds(start, share), columns]
        sem = place_sem.at[way, slot, step]

        def here():
            return pltpu.make_async_copy(source, target, sem)

        def there():
            return remote(source, target, sem, peer_sem.at[way, slot, step], to_core)

        return taker, here, there

    def place(way, slot, step):
        taker, here, there = goal(way, slot, step)

        @pl.when(taker == core)
        def _():
            here().start()

        @pl.when(taker != core)
        def _():
            there().start()

    def placed(way, slot, step):
        taker, here, there = goal(way, slot, step)

        @pl.when(taker == core)
        def _():
            here().wait()
            there().wait_recv()

        @pl.when(taker != core)
        def _():
            there().wait_send()

    def pass_on(which, step):
        for way, slot in which:

            @pl.when(step > 0)
            def _():
                hop(way, slot, step - 1).wait_recv()

            @pl.when(step < chips - 1)
            def _():
                hop(way, slot, step).start()

            place(way, slot, step)

    def settle(which):
        def body(step, carried):
            for way, slot in which:
                placed(way, slot, step)

                @pl.when(step < chips - 1)
                def _():
                    hop(way, slot, step).wait_send()

            return carried

        lax.fori_loop(0, chips, body, 0)

    def quad_copy(source, target, index, device):
        return remote(source, target, quad_send.at[index], quad_recv.at[index], device)

    mine = normed_ref.at[core, side]
    along = quad_copy(mine, mine, 0, to_side)
    across = quad_copy(normed_ref.at[core], normed_ref.at[core], 1, to_core)

    def bulk_side(part):
        rows = pl.ds(cuts[part], cuts[part + 1] - cuts[part])
        return remote(
            own_units_ref.at[rows],
            side_units_ref.at[rows],
            bulk_send.at[part],
            bulk_recv.at[part],
            to_side,
        )

    def bulk_diag(part):
        rows = pl.ds(cuts[part], cuts[part + 1] - cuts[part])
        return remote(
            side_units_ref.at[rows],
            diag_units_ref.at[rows],
            bulk_send.at[3 + part],
            bulk_recv.at[3 + part],
            to_core,
        )

    bulk_core = remote(own_units_ref, core_units_ref, bulk_send.at[6], bulk_recv.at[6], to_core)
    for way, slot in streams:
        hop(way, slot, 0).start()
    cast(0, 1)
    cast_store(0).wait()
    bulk_side(0).start()
    gains_total.over_cores()
    for way, slot in streams:
        place(way, slot, 0)
    gains_total.over_ring()
    pass_on(streams, 1)
    cast(1, 3)
    scales_ref[...] = gains_total.end()
    normed_ref[core, side] = norm_scale(resid_ref[...], scales_ref[0:1]).astype(bfloat)
    along.start()
    pass_on(streams, 2)
    cast(3, 5)
    pass_on(streams, 3)
    cast(5, 7)
    along.wait()
    across.start()
    bulk_side(1).start()
    pass_on(streams, 4)
    cast(7, casts)
    cast_store(casts - 2).wait()
    cast_store(casts - 1).wait()
    bulk_core.start()

    def body(step, carried):
        pass_on(streams, step)
        return carried

    lax.fori_loop(5, chips, body, 0)
    pass_on(out_streams, 0)
    across.wait()
    outs[2].start()
    settle(streams)
    outs[0].start()

    def project(slot, head):
        rows = slice(head * HD, head * HD + HD)
        return dot_nt(normed_ref[...].reshape(tokens, width), rows_ref[slot, rows])

    for head in range(2):
        raw = project(1, head)
        both[head] = turn(raw, key_cosine_ref[...], key_sine_ref[...]).astype(bfloat)
    swap = quad_copy(both.at[1 - side], keyval_ref.at[chip, side], 2, to_side)
    swap.start()
    bulk_side(2).start()
    for part in range(2):
        bulk_side(part).wait_recv()
        bulk_diag(part).start()
    pass_on(out_streams, 1)
    keyval_ref[chip, side] = both[side]
    for head in range(2):
        raw = project(0, head)
        query_ref[head] = turn(raw, cosine_ref[...], sine_ref[...]).astype(bfloat)
        pass_on(out_streams, 2 + head)
    total[...] = jnp.zeros_like(total)
    sums[...] = jnp.zeros_like(sums)
    swap.wait()

    def block(way, owner):
        part = tokens // 2
        key = keyval_ref[owner, 0, way * part : way * part + part]
        val = keyval_ref[owner, 1, way * part : way * part + part]
        row = lax.broadcasted_iota(jnp.int32, (tokens, part), 0)
        column = lax.broadcasted_iota(jnp.int32, (tokens, part), 1)
        allowed = row + (chip - owner) * tokens - way * part >= column

        def one_head(head, carried):
            bent = jnp.tanh(dot_nt(query_ref[head], key) * (scale / softcap))
            powers = jnp.where(allowed, jnp.exp(softcap * bent), 0.0)
            sums[head] += powers[:, : part // 2] + powers[:, part // 2 :]
            total[head] += dot_nn(powers.astype(bfloat), val)
            return carried

        for head in range(2):
            one_head(head, 0)

    def key_body(step, carried):
        for way, kind in key_streams:

            @pl.when(step > 0)
            def _():
                key_hop(way, kind, step - 1).wait_recv()

            @pl.when(step < chips - 1)
            def _():
                key_hop(way, kind, step).start()

        for way in range(2):
            owner = owner_of(way, step)

            @pl.when(owner <= chip)
            def _():
                block(way, owner)

            if way == 0:

                @pl.when(step < chips - 4)
                def _():
                    pass_on(out_streams, step + 4)

        return carried

    lax.fori_loop(0, chips, key_body, 0)
    outs[3].start()
    bulk_side(2).wait_recv()
    bulk_diag(2).start()
    settle(out_streams)
    outs[1].start()
    for head in range(2):
        inverse = 1.0 / jnp.sum(sums[head], axis=-1, keepdims=True)
        inverse_ref[head] = jnp.broadcast_to(inverse, inverse_ref.shape[1:])
        attended_ref[:, head * HD : head * HD + HD] = (total[head] * inverse).astype(bfloat)
    span = width // 3
    tiles = [slice(tile * span, tile * span + span) for tile in range(3)]

    def project_out(part, ref, columns):
        first = pl.ds(pl.multiple_of(part * 2 * tok_rows, 2 * tok_rows), 2 * tok_rows)
        made = dot_nn(attended_ref[first], rows_ref[2, :, columns])
        ref[:, :, columns] = made.reshape(2, tok_rows, span).astype(ref.dtype)

    across = [
        quad_copy(across_put.at[:, :, columns], across_got.at[:, :, columns], 3 + tile, to_core)
        for tile, columns in enumerate(tiles)
    ]
    along = [
        quad_copy(along_put.at[:, columns], along_got.at[:, columns], 6 + tile, to_side)
        for tile, columns in enumerate(tiles)
    ]
    for tile, columns in enumerate(tiles):
        project_out(1 - core, across_put, columns)
        across[tile].start()
    for tile, columns in enumerate(tiles):
        project_out(core, product, columns)
        across[tile].wait()
        given = product[1 - side, :, columns] + across_got[1 - side, :, columns].astype(single)
        along_put[:, columns] = given.astype(bfloat)
        along[tile].start()

    def key_settle(step, carried):
        for way, kind in key_streams:
            key_hop(way, kind, step).wait_send()
        return carried

    lax.fori_loop(0, chips - 1, key_settle, 0)
    for out in outs:
        out.wait()
    bulk_core.wait()
    for part in range(3):
        bulk_side(part).wait_send()
        bulk_diag(part).wait()
    for tile, columns in enumerate(tiles):
        along[tile].wait()
        kept = product[side, :, columns] + across_got[side, :, columns].astype(single)
        projected_ref[:, columns] = kept + along_got[:, columns].astype(single)


def cost(micros):
    return pl.CostEstimate(flops=int(micros * 1e9), bytes_accessed=0, transcendentals=0)


def front(attn_weight, gains, resid_in, turns, ffn_wide, chips, ident):
    share, width = attn_weight.shape[1:]
    tok_rows = resid_in.shape[0]
    tokens = 4 * tok_rows
    units = ffn_wide.shape[0]
    cuts = (0, units // 9, units // 3, 2 * units // 3)
    vmem = pl.BlockSpec(memory_space=pltpu.VMEM)
    anywhere = pl.BlockSpec(memory_space=pl.ANY)
    return pl.pallas_call(
        functools.partial(front_kernel, chips, cuts),
        out_shape=(
            jax.ShapeDtypeStruct((3, 2 * HD, width), bfloat),
            jax.ShapeDtypeStruct((4, width), single),
            jax.ShapeDtypeStruct((2, 2, tok_rows, width), bfloat),
            jax.ShapeDtypeStruct((2, tokens, HD), bfloat),
            jax.ShapeDtypeStruct((chips, 2, tokens, HD), bfloat),
            jax.ShapeDtypeStruct((tokens, 2 * HD), bfloat),
            jax.ShapeDtypeStruct((2, tokens, 128), single),
            jax.ShapeDtypeStruct((tok_rows, width), single),
        )
        + (jax.ShapeDtypeStruct((units, width), bfloat),) * 2
        + (jax.ShapeDtypeStruct((2 * units // 3, width), bfloat),) * 2,
        in_specs=[vmem] * 7 + [anywhere],
        out_specs=(anywhere, vmem, anywhere, vmem, anywhere, vmem, vmem, vmem) + (anywhere,) * 4,
        scratch_shapes=[
            pltpu.VMEM((3, 2 * HD, width), bfloat),
            pltpu.VMEM((2, 2, tok_rows, width), bfloat),
            pltpu.VMEM((chips, 2, tokens, HD), bfloat),
            pltpu.VMEM((chips, 3, share, width), bfloat),
            pltpu.VMEM((2, tokens, HD), bfloat),
            pltpu.VMEM((2, tokens, HD), single),
            pltpu.VMEM((2, tokens, 128), single),
            pltpu.VMEM((2, tok_rows, width), single),
            pltpu.VMEM((2, tok_rows, width), bfloat),
            pltpu.VMEM((2, tok_rows, width), bfloat),
            pltpu.VMEM((tok_rows, width), bfloat),
            pltpu.VMEM((tok_rows, width), bfloat),
            pltpu.VMEM((2, units // 9, width), single),
            pltpu.VMEM((2, units // 9, width), bfloat),
        ]
        + total_scratch(chips, width)
        + [
            pltpu.SemaphoreType.DMA((2, 3, chips - 1)),
            pltpu.SemaphoreType.DMA((2, 3, chips - 1)),
            pltpu.SemaphoreType.DMA((2, 3, chips)),
            pltpu.SemaphoreType.DMA((2, 3, chips)),
            pltpu.SemaphoreType.DMA((2, 2, chips - 1)),
            pltpu.SemaphoreType.DMA((2, 2, chips - 1)),
            pltpu.SemaphoreType.DMA((9,)),
            pltpu.SemaphoreType.DMA((9,)),
            pltpu.SemaphoreType.DMA((2, 2)),
            pltpu.SemaphoreType.DMA((4,)),
            pltpu.SemaphoreType.DMA((7,)),
            pltpu.SemaphoreType.DMA((7,)),
        ],
        compiler_params=pltpu.CompilerParams(
            collective_id=ident, has_side_effects=True, vmem_limit_bytes=60 * 2**20
        ),
        cost_estimate=cost(140),
    )(attn_weight, gains, resid_in, *turns, ffn_wide)


def tail_kernel(
    chips,
    d_proj_ref,
    query_ref,
    keyval_in,
    attended_ref,
    inverse_ref,
    rows_in,
    normed_in,
    cosine_ref,
    sine_ref,
    key_cosine_ref,
    key_sine_ref,
    resid_ref,
    d_mid_ref,
    scales_ref,
    gains_ref,
    units_own_ref,
    units_other_ref,
    sum_ref,
    tokens_ref,
    total_ref,
    units_ref,
    units_got_ref,
    units_mine_ref,
    keyval_ref,
    rows_ref,
    normed_ref,
    d_all,
    d_out,
    delta,
    d_query,
    d_block,
    first_put,
    held_keys,
    swapped,
    d_raw,
    out_rows,
    parts,
    out_parts,
    held,
    out_held,
    across_got,
    along_put,
    along_got,
    value,
    near,
    blocks,
    total_send,
    total_recv,
    key_send,
    key_recv,
    place_sem,
    peer_sem,
    send_sem,
    recv_sem,
    out_send,
    out_recv,
    quad_send,
    quad_recv,
    load_sem,
    bulk_send,
    bulk_recv,
):
    tokens = query_ref.shape[1]
    half = tokens // 2
    width = resid_ref.shape[1]
    share = out_parts.shape[1]
    pairs = chips // 4
    scale = 1.0 / math.sqrt(HD)
    peers = quad_peers(chips)
    side, core, to_side, to_core, around = peers
    ring = Ring(chips, 2, 2 * share, send_sem, recv_sem)
    out_ring = Ring(chips, 1, share, out_send, out_recv)
    chip = ring.chip
    gains_total = Total(value, near, blocks, total_send, total_recv, peers, chip)
    arrays = [
        pltpu.make_async_copy(rows_in.at[2], rows_ref.at[2], load_sem.at[3]),
        pltpu.make_async_copy(keyval_in, keyval_ref, load_sem.at[4]),
        pltpu.make_async_copy(normed_in, normed_ref, load_sem.at[5]),
        pltpu.make_async_copy(rows_in.at[0:2], rows_ref.at[0:2], load_sem.at[6]),
    ]
    d_all[core, side] = d_proj_ref[...]
    wide_barrier(to_side, to_core, around)

    def quad_copy(source, target, index, device):
        return remote(source, target, quad_send.at[index], quad_recv.at[index], device)

    def bulk(kind):
        return remote(
            units_ref.at[pl.ds(kind * (units_ref.shape[0] // 3), units_ref.shape[0] // 3)],
            units_got_ref.at[pl.ds(kind * (units_ref.shape[0] // 3), units_ref.shape[0] // 3)],
            bulk_send.at[kind],
            bulk_recv.at[kind],
            to_side,
        )

    units = units_ref.shape[0]
    ours = out_rows.reshape(6 * HD, width).at[pl.ds(0, units)]
    theirs = parts.reshape(2 * chips * share, width).at[pl.ds(0, units)]
    loads = (
        pltpu.make_async_copy(units_own_ref.at[1], ours, load_sem.at[0]),
        pltpu.make_async_copy(units_other_ref.at[1], theirs, load_sem.at[1]),
    )
    store = pltpu.make_async_copy(ours, units_ref, load_sem.at[2])
    spare = held.reshape(2 * (chips - 1) * share, width).at[pl.ds(0, units)]
    mine_loads = (
        pltpu.make_async_copy(units_own_ref.at[0], ours, load_sem.at[7]),
        pltpu.make_async_copy(units_other_ref.at[0], spare, load_sem.at[8]),
    )
    mine_store = pltpu.make_async_copy(ours, units_mine_ref, load_sem.at[9])
    mine_loads[1].start()

    def add_up(more):
        for kind in range(3):
            rows = slice(kind * units // 3, (kind + 1) * units // 3)
            ours[rows] = (ours[rows].astype(single) + more[rows].astype(single)).astype(bfloat)
    for load in loads:
        load.start()
    for array in arrays:
        array.start()
    quarter = tokens // 8
    halves = [slice(part * quarter, part * quarter + quarter) for part in range(2)]
    along = [
        quad_copy(d_all.at[core, side, rows], d_all.at[core, side, rows], part, to_side)
        for part, rows in enumerate(halves)
    ]
    across = quad_copy(d_all.at[core, side], d_all.at[core, side], 2, to_core)
    relay = [
        quad_copy(d_all.at[core, 1 - side, rows], d_all.at[core, 1 - side, rows], 3 + part, to_core)
        for part, rows in enumerate(halves)
    ]
    for part in range(2):
        along[part].start()
    across.start()
    d_query[...] = jnp.zeros_like(d_query)
    for load in loads:
        load.wait()
    add_up(theirs)
    store.start()
    for part in range(2):
        along[part].wait()
        relay[part].start()
    store.wait()
    bulk(0).start()
    bulk(1).start()
    mine_loads[0].start()
    across.wait()
    for load in mine_loads:
        load.wait()
    add_up(spare)
    mine_store.start()
    for part in range(2):
        relay[part].wait()
    for array in arrays:
        array.wait()
    d_rows = d_all[...].reshape(tokens, width)
    for head in range(2):
        columns = slice(head * HD, head * HD + HD)
        made = dot_nt(d_rows, rows_ref[2, columns]).astype(bfloat)
        d_out[head] = made
        row_dot = jnp.sum(
            made.astype(single) * attended_ref[:, columns].astype(single), axis=-1, keepdims=True
        )
        delta[head] = jnp.broadcast_to(row_dot, delta.shape[1:])

    def place(slot, head, start):
        deep = 2 * head + core if slot == 1 else 2 * core + head
        for unit in range(4):
            source = out_rows.at[slot, head, pl.ds(unit * share, share)]
            owner = deep * pairs + unit // 2
            target = out_parts.at[owner] if slot == 2 else parts.at[owner, slot]
            sem = place_sem.at[slot, head, unit]

            def here():
                return pltpu.make_async_copy(source, target, sem)

            def there():
                return remote(source, target, sem, peer_sem.at[slot, head, unit], to_core)

            @pl.when(core == unit % 2)
            def _():
                if start:
                    here().start()
                else:
                    here().wait()
                    there().wait_recv()

            @pl.when(core != unit % 2)
            def _():
                if start:
                    there().start()
                else:
                    there().wait_send()

    def term(slot, head, left, right):
        out_rows[slot, head] = dot_tn(left, right).astype(bfloat)
        place(slot, head, True)

    def block(way, owner):
        key = keyval_ref[owner, 0, way * half : way * half + half]
        val = keyval_ref[owner, 1, way * half : way * half + half]
        row = lax.broadcasted_iota(jnp.int32, (tokens, half), 0)
        column = lax.broadcasted_iota(jnp.int32, (tokens, half), 1)
        allowed = row + (chip - owner) * tokens - way * half >= column

        def one_head(head, carried):
            bent = jnp.tanh(dot_nt(query_ref[head], key) * (scale / softcap))
            inverse = jnp.concatenate([inverse_ref[head]] * (half // 128), axis=1)
            row_dot = jnp.concatenate([delta[head]] * (half // 128), axis=1)
            probs = jnp.where(allowed, jnp.exp(softcap * bent), 0.0) * inverse
            d_probs = dot_nt(d_out[head], val)
            d_scores = (probs * (d_probs - row_dot) * (1.0 - bent * bent)).astype(bfloat)
            d_block[way, 0] += dot_tn(d_scores, query_ref[head]) * scale
            d_block[way, 1] += dot_tn(probs.astype(bfloat), d_out[head])
            d_query[head] += dot_nn(d_scores, key)
            return carried

        for head in range(2):
            one_head(head, 0)

    def key_copy(way, kind, step, first):
        return remote(
            first_put.at[way, kind] if first else held_keys.at[way, step - 1, kind],
            held_keys.at[way, step, kind],
            key_send.at[way, kind, step],
            key_recv.at[way, kind, step],
            {"fsdp": ring.right if way == 0 else ring.left},
        )

    streams = [(way, kind) for kind in range(2) for way in range(2)]

    early = 3

    def key_blocks(step):
        for way in range(2):
            owner = ring.owner(way, step + 1)
            d_block[way] = jnp.zeros(d_block.shape[1:], single)
            if way == 1:

                @pl.when((step >= early) & (step < chips - 1))
                def _():
                    out_ring.scatter_step(out_parts, out_held, step - early)

            @pl.when(owner <= chip)
            def _():
                block(way, owner)

    def key_body(step, carried):
        key_blocks(step)
        for way, kind in streams:

            @pl.when(step == 0)
            def _():
                first_put[way, kind] = d_block[way, kind].astype(bfloat)
                key_copy(way, kind, 0, True).start()

            @pl.when(step > 0)
            def _():
                key_copy(way, kind, step - 1, True).wait_recv()
                summed = held_keys[way, step - 1, kind].astype(single) + d_block[way, kind]
                held_keys[way, step - 1, kind] = summed.astype(bfloat)
                key_copy(way, kind, step, False).start()

        @pl.when(step == 0)
        def _():
            for head in range(2):
                left = attended_ref[:, head * HD : head * HD + HD]
                term(2, head, left, d_all[...].reshape(tokens, width))

        @pl.when(step == early - 1)
        def _():
            key_blocks(chips - 1)
            for way in range(2):
                for kind in range(2):
                    rows = slice(way * half, way * half + half)
                    swapped[2 + kind, rows] = d_block[way, kind].astype(bfloat)
            for head in range(2):
                place(2, head, False)

        return carried

    lax.fori_loop(0, chips - 1, key_body, 0)
    mine_store.wait()

    normed = normed_ref[...].reshape(tokens, width)
    for way in range(2):
        rows = slice(way * half, way * half + half)
        for kind in range(2):
            key_copy(way, kind, chips - 2, True).wait_recv()
            summed = held_keys[way, chips - 2, kind].astype(single)
            summed = summed + swapped[2 + kind, rows].astype(single)
            swapped[2 + kind, rows] = summed.astype(bfloat)
    swap = quad_copy(swapped.at[3 - side], swapped.at[side], 5, to_side)
    swap.start()
    out_ring.scatter_step(out_parts, out_held, chips - 4)
    for head in range(2):
        turned = turn(d_query[head] * scale, cosine_ref[...], -sine_ref[...])
        d_raw[head] = turned.astype(bfloat)
        term(0, head, d_raw[head], normed)
        if head == 0:
            out_ring.scatter_step(out_parts, out_held, chips - 3)
    swap.wait()
    out_ring.scatter_step(out_parts, out_held, chips - 2)
    bulk(2).start()
    swapped[side] = swapped[2 + side]
    for head in range(2):
        turned = turn(swapped[head].astype(single), key_cosine_ref[...], -key_sine_ref[...])
        d_raw[2 + head] = turned.astype(bfloat)
        term(1, head, d_raw[2 + head], normed)
    span = width // 3

    def d_input(tile, carried):
        columns = pl.ds(pl.multiple_of(tile * span, span), span)
        made = dot_nn(d_raw[0], rows_ref[0, 0:HD, columns])
        made = made + dot_nn(d_raw[1], rows_ref[0, HD:, columns])
        made = made + dot_nn(d_raw[2], rows_ref[1, 0:HD, columns])
        made = made + dot_nn(d_raw[3], rows_ref[1, HD:, columns])
        out_rows[0, :, :, columns] = made.reshape(2, half, span).astype(bfloat)
        return carried

    for slot in range(2):
        for head in range(2):
            place(slot, head, False)
    blocks_ref = parts.reshape(chips, 2 * share, width)
    ring.scatter_step(blocks_ref, held, 0)
    lax.fori_loop(0, 3, d_input, 0)
    across = quad_copy(out_rows.at[0, 1 - core], across_got, 6, to_core)
    mine = pl.ds(pl.multiple_of(side * (half // 2), half // 2), half // 2)
    other = pl.ds(pl.multiple_of((1 - side) * (half // 2), half // 2), half // 2)
    along = quad_copy(along_put, along_got, 7, to_side)
    across.start()

    def body(step, carried):
        ring.scatter_step(blocks_ref, held, step)

        @pl.when(step == 1)
        def _():
            across.wait()
            given = out_rows[0, core, other].astype(single) + across_got[other].astype(single)
            along_put[...] = given.astype(bfloat)
            along.start()
            tokens_ref[...] = out_rows[0, core, mine].astype(single) + across_got[mine].astype(single)

        @pl.when(step == 4)
        def _():
            along.wait()
            tokens_ref[...] = tokens_ref[...] + along_got[...].astype(single)
            d_norm, d_gain = norm_back(resid_ref[...], scales_ref[0:1], tokens_ref[...])
            tokens_ref[...] = d_mid_ref[...] + d_norm
            value[0] = gains_ref[...]
            value[0, 0:1] = d_gain
            gains_total.start()

        @pl.when(step == 5)
        def _():
            gains_total.over_cores()

        @pl.when(step == 6)
        def _():
            gains_total.over_ring()

        return carried

    lax.fori_loop(1, chips - 1, body, 0)
    total_ref[...] = gains_total.end()
    out_ring.scatter_end(out_parts, out_held, sum_ref.at[pl.ds(2 * share, share)])
    ring.scatter_end(blocks_ref, held, sum_ref.at[pl.ds(0, 2 * share)])
    ring.finish(held.at[0, 0, 0 : ring.size])
    out_ring.finish(out_held.at[0, 0, 0 : out_ring.size])

    def settle(step, carried):
        for way, kind in streams:
            key_copy(way, kind, step, True).wait_send()
        return carried

    lax.fori_loop(0, chips - 1, settle, 0)
    for kind in range(3):
        bulk(kind).wait()


def tail(
    d_proj, query, keyval, attended, inverse, rows, normed, turns, locals_, own, other, chips, ident
):
    tokens = query.shape[1]
    tok_rows = tokens // 4
    width = rows.shape[2]
    share = tokens // 8
    half = tokens // 2
    vmem = pl.BlockSpec(memory_space=pltpu.VMEM)
    anywhere = pl.BlockSpec(memory_space=pl.ANY)
    return pl.pallas_call(
        functools.partial(tail_kernel, chips),
        out_shape=(
            jax.ShapeDtypeStruct((3 * share, width), single),
            jax.ShapeDtypeStruct((tok_rows, width), single),
            jax.ShapeDtypeStruct((4, width), single),
            jax.ShapeDtypeStruct(own.shape[1:], bfloat),
            jax.ShapeDtypeStruct(own.shape[1:], bfloat),
            jax.ShapeDtypeStruct(own.shape[1:], bfloat),
        ),
        in_specs=[vmem] * 2
        + [anywhere, vmem, vmem, anywhere, anywhere]
        + [vmem] * 8
        + [anywhere] * 2,
        out_specs=(vmem,) * 3 + (anywhere,) * 3,
        scratch_shapes=[
            pltpu.VMEM(keyval.shape, bfloat),
            pltpu.VMEM(rows.shape, bfloat),
            pltpu.VMEM(normed.shape, bfloat),
            pltpu.VMEM((2, 2, tok_rows, width), bfloat),
            pltpu.VMEM((2, tokens, HD), bfloat),
            pltpu.VMEM((2, tokens, 128), single),
            pltpu.VMEM((2, tokens, HD), single),
            pltpu.VMEM((2, 2, half, HD), single),
            pltpu.VMEM((2, 2, half, HD), bfloat),
            pltpu.VMEM((2, chips - 1, 2, half, HD), bfloat),
            pltpu.VMEM((4, tokens, HD), bfloat),
            pltpu.VMEM((4, tokens, HD), bfloat),
            pltpu.VMEM((3, 2, HD, width), bfloat),
            pltpu.VMEM((chips, 2, share, width), bfloat),
            pltpu.VMEM((chips, share, width), bfloat),
            pltpu.VMEM((2, chips - 1, share, width), bfloat),
            pltpu.VMEM((2, chips - 1, share // 2, width), bfloat),
            pltpu.VMEM((2 * tok_rows, width), bfloat),
            pltpu.VMEM((tok_rows, width), bfloat),
            pltpu.VMEM((tok_rows, width), bfloat),
        ]
        + total_scratch(chips, width)
        + [
            pltpu.SemaphoreType.DMA((2, 2, chips - 1)),
            pltpu.SemaphoreType.DMA((2, 2, chips - 1)),
            pltpu.SemaphoreType.DMA((3, 2, 4)),
            pltpu.SemaphoreType.DMA((3, 2, 4)),
            pltpu.SemaphoreType.DMA((2, 2, chips - 1)),
            pltpu.SemaphoreType.DMA((2, 2, chips - 1)),
            pltpu.SemaphoreType.DMA((2, 1, chips - 1)),
            pltpu.SemaphoreType.DMA((2, 1, chips - 1)),
            pltpu.SemaphoreType.DMA((8,)),
            pltpu.SemaphoreType.DMA((8,)),
            pltpu.SemaphoreType.DMA((10,)),
            pltpu.SemaphoreType.DMA((3,)),
            pltpu.SemaphoreType.DMA((3,)),
        ],
        compiler_params=pltpu.CompilerParams(
            collective_id=ident, has_side_effects=True, vmem_limit_bytes=63 * 2**20
        ),
        cost_estimate=cost(160),
    )(d_proj, query, keyval, attended, inverse, rows, normed, *turns, *locals_, own, other)


def feed_kernel(
    chips,
    pieces,
    resid_ref,
    projected_ref,
    dy_ref,
    scales_ref,
    own_ref,
    side_ref,
    core_ref,
    diag_ref,
    result_ref,
    d_mid_ref,
    d_projected_ref,
    d_gains_ref,
    terms_ref,
    other_ref,
    weights,
    x_all,
    y_all,
    mid,
    both,
    hidden,
    part,
    held,
    chunk,
    wide,
    stage,
    load_sem,
    bulk_send,
    bulk_recv,
    stage_sem,
    other_sem,
    send_sem,
    recv_sem,
):
    tok_rows, width = resid_ref.shape
    units = own_ref.shape[0] // 3
    whole = 4 * units
    half = tok_rows // 2
    rings = [
        Ring(chips, pieces, tok_rows, send_sem.at[phase], recv_sem.at[phase]) for phase in range(4)
    ]
    chip = rings[0].chip
    loads = []
    for slot, ref in enumerate((own_ref, side_ref, core_ref, diag_ref)):
        for kind in range(3 if slot % 2 == 0 else 2):
            loads.append(
                pltpu.make_async_copy(
                    ref.at[pl.ds(kind * units, units)],
                    weights.at[pl.ds(kind * whole + slot * units, units)],
                    load_sem.at[slot, kind],
                )
            )
    for load in loads:
        load.start()
    mid[...] = resid_ref[...] + norm_scale(projected_ref[...], scales_ref[1:2])
    x_all[chip] = norm_scale(mid[...], scales_ref[2:3]).astype(bfloat)
    core = lax.axis_index("fsdp") % 2
    to_core = {"fsdp": 2 * chip + 1 - core}
    to_side = {"head": 1 - lax.axis_index("head")}
    quad_barrier(to_side, to_core, rings[0].right, rings[0].left)
    down_rows = [pl.ds(2 * whole + slot * units, units) for slot in range(4)]
    bulk_side = remote(
        own_ref.at[pl.ds(2 * units, units)],
        weights.at[down_rows[1]],
        bulk_send.at[0],
        bulk_recv.at[0],
        to_side,
    )
    bulk_diag = remote(
        weights.at[down_rows[1]],
        weights.at[down_rows[3]],
        bulk_send.at[1],
        bulk_recv.at[1],
        to_core,
    )
    bulk_side.start()
    span = width // 3

    def segments(pair):
        for hop in range(2):
            for way in range(2):
                start = hop * tok_rows + way * half
                owner = rings[0].owner(way, 2 * pair + hop)
                yield owner, pl.ds(way * half, half), pl.ds(start, half)

    def fetch(all_ref, pair):
        for owner, rows, here in segments(pair):
            chunk[here] = all_ref[owner, rows]

    def put(ref, pair, columns, value):
        for owner, rows, here in segments(pair):
            ref[owner, rows, columns] = value[here.start : here.start + half].astype(ref.dtype)

    def take(ref, pair, columns):
        return jnp.concatenate(
            [ref[owner, rows, columns] for owner, rows, here in segments(pair)], axis=0
        )

    def polls(ring, all_ref, pair):
        def poll(index):
            @pl.when(2 * pair + 2 < chips)
            def _():
                ring.gather_step(all_ref, 2 * pair + 2 + index // 2, index % 2)

        return poll

    def down(pair):
        chunk[:, 0:whole] = take(hidden, pair, slice(None))

        def columns_of(tile, carried):
            columns = pl.ds(pl.multiple_of(tile * span, span), span)
            put(part, pair, columns, dot_nn(chunk[:, 0:whole], weights[2 * whole :, columns]))
            return carried

        lax.fori_loop(0, 3, columns_of, 0)

    def gate_up(tile):
        rows = slice(tile * span, tile * span + span)
        wide[:, rows] = dot_nt(chunk[...], weights[rows])

    def unit(pair):
        put(both, pair, slice(None), wide[...])
        value, slope = gelu_parts(wide[:, 0:whole])
        put(hidden, pair, slice(None), value * wide[:, whole:])

    last = chips // 2 - 1

    def forward(pair, carried):
        poll = polls(rings[0], x_all, pair)
        fetch(x_all, pair)
        for tile in range(3):
            gate_up(tile)
            poll(tile)
        unit(pair)

        @pl.when(pair == last - 1)
        def _():
            bulk_side.wait_recv()
            bulk_diag.start()
            bulk_diag.wait_recv()
            down(0)

        poll(3)
        return carried

    for step in range(2):
        for piece in range(pieces):
            rings[0].gather_step(x_all, step, piece)
        if step == 0:
            for load in loads:
                load.wait()
    lax.fori_loop(0, last, forward, 0)
    rings[1].scatter_step(part, held, 0)
    down(1)
    fetch(x_all, last)
    gate_up(0)
    rings[1].scatter_step(part, held, 1)
    gate_up(1)
    gate_up(2)
    unit(last)

    def spread(step, carried):
        rings[1].scatter_step(part, held, step, 0)

        @pl.when((step % 2 == 0) & (step < chips - 2))
        def _():
            down(step // 2 + 1)

        rings[1].scatter_step(part, held, step, 1)
        return carried

    lax.fori_loop(2, chips - 1, spread, 0)
    ours = pl.ds(0, tok_rows)
    rings[1].scatter_end(part, held, wide)
    result_ref[...] = mid[...] + norm_scale(wide[ours], scales_ref[3:4])
    d_ffn, d_gain = norm_back(wide[ours], scales_ref[3:4], dy_ref[...])
    d_gains_ref[0:1] = jnp.zeros_like(d_gain)
    d_gains_ref[3:4] = d_gain
    y_all[chip] = d_ffn.astype(bfloat)
    rings[0].finish(x_all.at[0, 0 : rings[0].size])
    rings[1].finish(x_all.at[0, 0 : rings[0].size])
    bulk_side.wait_send()
    bulk_diag.wait_send()

    def d_input(pair):
        chunk[...] = take(both, pair, slice(None))

        def columns_of(tile, carried):
            columns = pl.ds(pl.multiple_of(tile * span, span), span)
            put(part, pair, columns, dot_nn(chunk[...], weights[0 : 2 * whole, columns]))
            return carried

        lax.fori_loop(0, 3, columns_of, 0)

    third = whole // 3

    def d_units(pair, tile):
        columns = slice(tile * third, tile * third + third)
        ups = slice(whole + tile * third, whole + tile * third + third)
        for owner, rows, here in segments(pair):
            value, slope = gelu_parts(both[owner, rows, columns].astype(single))
            upper = both[owner, rows, ups].astype(single)
            d_hidden = wide[here, columns]
            both[owner, rows, columns] = (d_hidden * upper * slope).astype(bfloat)
            both[owner, rows, ups] = (d_hidden * value).astype(bfloat)

    def d_hidden(first, end):
        wide[:, first:end] = dot_nt(chunk[...], weights[2 * whole + first : 2 * whole + end])

    def backward(pair, carried):
        poll = polls(rings[2], y_all, pair)
        fetch(y_all, pair)
        d_hidden(0, 2 * third)
        poll(0)
        d_hidden(2 * third, whole)
        d_units(pair, 0)
        poll(1)
        d_units(pair, 1)
        d_units(pair, 2)
        poll(2)

        @pl.when(pair < 2)
        def _():
            d_input(pair)

        poll(3)
        return carried

    for step in range(2):
        for piece in range(pieces):
            rings[2].gather_step(y_all, step, piece)
    lax.fori_loop(0, last, backward, 0)
    rings[3].scatter_step(part, held, 0)
    fetch(y_all, last)
    d_hidden(0, 2 * third)
    d_hidden(2 * third, whole)
    d_units(last, 0)
    rings[3].scatter_step(part, held, 1)
    d_units(last, 1)
    d_units(last, 2)
    rows_tile = stage.shape[1]
    tiles = 3 * whole // rows_tile
    upper_tiles = 2 * whole // rows_tile

    cut = units // 3

    def pieces_of(tile):
        for quarter in range(4):
            block = 4 * tile + quarter
            kind, slot, third = block // 12, (block // 3) % 4, block % 3
            source = stage.at[tile % 2, pl.ds(quarter * cut, cut)]
            rows = pl.ds(pl.multiple_of(kind * units + third * cut, cut), cut)
            sem = stage_sem.at[tile % 2, quarter]
            goal = terms_ref.at[slot, rows], other_ref.at[slot - 2, rows]
            there = functools.partial(
                remote, source, goal[1], sem, other_sem.at[tile, quarter], to_core
            )
            yield slot, functools.partial(pltpu.make_async_copy, source, goal[0], sem), there

    def keep(tile):
        for slot, here, there in pieces_of(tile):

            @pl.when(slot < 2)
            def _():
                here().start()

            @pl.when(slot >= 2)
            def _():
                there().start()

    def kept(tile):
        for slot, here, there in pieces_of(tile):

            @pl.when(slot < 2)
            def _():
                here().wait()

            @pl.when(slot >= 2)
            def _():
                there().wait_send()

    def grads(tile):
        @pl.when(tile >= 2)
        def _():
            kept(tile - 2)

        @pl.when(tile < upper_tiles)
        def _():
            columns = pl.ds(pl.multiple_of(tile * rows_tile, rows_tile), rows_tile)
            left = both[:, :, columns].reshape(chips * tok_rows, rows_tile)
            stage[tile % 2] = dot_tn(left, x_all[...].reshape(chips * tok_rows, width)).astype(bfloat)

        @pl.when(tile >= upper_tiles)
        def _():
            columns = pl.ds(
                pl.multiple_of((tile - upper_tiles) * rows_tile, rows_tile), rows_tile
            )
            left = hidden[:, :, columns].reshape(chips * tok_rows, rows_tile)
            stage[tile % 2] = dot_tn(left, y_all[...].reshape(chips * tok_rows, width)).astype(bfloat)

        keep(tile)

    d_input(2)

    def spread_back(step, carried):
        tile = 2 * (step - 3) + 2 * ((6 - step) // 4)
        rings[3].scatter_step(part, held, step, 0)

        @pl.when(step == 3)
        def _():
            d_input(3)

        @pl.when(step != 3)
        def _():
            grads(tile)

        rings[3].scatter_step(part, held, step, 1)

        @pl.when(step != 3)
        def _():
            grads(tile + 1)

        return carried

    lax.fori_loop(2, chips - 1, spread_back, 0)
    lax.fori_loop(8, tiles, lambda tile, carried: grads(tile) or carried, 0)
    rings[3].scatter_end(part, held, wide)
    d_norm, d_gain = norm_back(mid[...], scales_ref[2:3], wide[ours])
    d_gains_ref[2:3] = d_gain
    d_mid_ref[...] = dy_ref[...] + d_norm
    d_projected, d_gain = norm_back(projected_ref[...], scales_ref[1:2], d_mid_ref[...])
    d_gains_ref[1:2] = d_gain
    d_projected_ref[...] = d_projected.astype(bfloat)
    rings[2].finish(x_all.at[0, 0 : rings[0].size])
    rings[3].finish(x_all.at[0, 0 : rings[0].size])
    kept(tiles - 2)
    kept(tiles - 1)

    def gained(tile, carried):
        for slot, here, there in pieces_of(tile):

            @pl.when(slot >= 2)
            def _():
                there().wait_recv()

        return carried

    lax.fori_loop(0, tiles, gained, 0)


def feed_forward(resid_in, projected, grad_out, scales, shares, chips, ident):
    tok_rows, width = resid_in.shape
    units = shares[0].shape[0] // 3
    whole = 4 * units
    pieces = 2
    vmem = pl.BlockSpec(memory_space=pltpu.VMEM)
    anywhere = pl.BlockSpec(memory_space=pl.ANY)
    return pl.pallas_call(
        functools.partial(feed_kernel, chips, pieces),
        out_shape=(
            jax.ShapeDtypeStruct((tok_rows, width), single),
            jax.ShapeDtypeStruct((tok_rows, width), single),
            jax.ShapeDtypeStruct((tok_rows, width), bfloat),
            jax.ShapeDtypeStruct((4, width), single),
            jax.ShapeDtypeStruct((2, 3 * units, width), bfloat),
            jax.ShapeDtypeStruct((2, 3 * units, width), bfloat),
        ),
        in_specs=[vmem] * 4 + [anywhere] * 4,
        out_specs=(vmem, vmem, vmem, vmem, anywhere, anywhere),
        scratch_shapes=[
            pltpu.VMEM((3 * whole, width), bfloat),
            pltpu.VMEM((chips, tok_rows, width), bfloat),
            pltpu.VMEM((chips, tok_rows, width), bfloat),
            pltpu.VMEM((tok_rows, width), single),
            pltpu.VMEM((chips, tok_rows, 2 * whole), bfloat),
            pltpu.VMEM((chips, tok_rows, whole), bfloat),
            pltpu.VMEM((chips, tok_rows, width), bfloat),
            pltpu.VMEM((2, chips - 1, tok_rows // 2, width), bfloat),
            pltpu.VMEM((2 * tok_rows, width), bfloat),
            pltpu.VMEM((2 * tok_rows, width), single),
            pltpu.VMEM((2, whole // 3, width), bfloat),
            pltpu.SemaphoreType.DMA((4, 3)),
            pltpu.SemaphoreType.DMA((2,)),
            pltpu.SemaphoreType.DMA((2,)),
            pltpu.SemaphoreType.DMA((2, 4)),
            pltpu.SemaphoreType.DMA((9, 4)),
            pltpu.SemaphoreType.DMA((4, 2, pieces, chips - 1)),
            pltpu.SemaphoreType.DMA((4, 2, pieces, chips - 1)),
        ],
        compiler_params=pltpu.CompilerParams(
            collective_id=ident, has_side_effects=True, vmem_limit_bytes=63 * 2**20
        ),
        cost_estimate=cost(205),
    )(resid_in, projected, grad_out, scales, *shares)


def general_device(
    tokens,
    cotangent,
    gains,
    gains_first,
    gains_second,
    attn_weight,
    attn_first,
    attn_second,
    ffn_weight,
    ffn_first,
    ffn_second,
):
    devices = lax.axis_size("fsdp")
    chips = devices // 2
    side = lax.axis_index("head")
    place = lax.axis_index("fsdp")
    core, chip = place % 2, place // 2
    tok_rows = tokens.shape[1]
    super_rows = 4 * tok_rows
    seq_len = min(SEQ_LEN, super_rows * chips)
    share = attn_weight.shape[1]
    pairs = chips // 4
    width = tokens.shape[2]
    scale = 1.0 / math.sqrt(HD)

    def swap_core(value):
        return lax.ppermute(value, "fsdp", [(index, index ^ 1) for index in range(devices)])

    def swap_side(value):
        return lax.ppermute(value, "head", [(0, 1), (1, 0)])

    def in_order(own, other, index, axis):
        return jnp.where(
            index == 0, jnp.stack([own, other], axis), jnp.stack([other, own], axis)
        )

    def pick(value, index, axis=0):
        return lax.dynamic_index_in_dim(value, index, axis, keepdims=False)

    def quad_gather(value):
        value = in_order(value, swap_side(value), side, 0)
        value = in_order(value, swap_core(value), core, 0)
        return value.reshape((super_rows,) + value.shape[3:])

    def quad_scatter(partial):
        partial = partial.reshape(2, 2, tok_rows, width)
        mine = pick(partial, core) + swap_core(pick(partial, 1 - core).astype(bfloat)).astype(single)
        return pick(mine, side) + swap_side(pick(mine, 1 - side).astype(bfloat)).astype(single)

    scales = lax.all_gather(gains.astype(bfloat), ("head", "fsdp"), axis=1, tiled=True).astype(single)
    attn_low = attn_weight.astype(bfloat)
    ffn_low = ffn_weight.astype(bfloat).transpose(1, 0, 2)
    ffn_pair = jnp.concatenate([ffn_low, swap_side(ffn_low)], axis=1)

    ring_rows = ring_gather(attn_low.reshape(3 * share, width), chips, 0)
    ring_rows = ring_rows.reshape(2, 2, pairs, 3, share, width)

    def query_rows(slot):
        rows = ring_rows[:, :, :, slot]
        other = swap_core(pick(rows, 1 - core))
        return in_order(pick(rows, core), other, core, 2).reshape(2 * HD, width)

    def keyval_rows():
        rows = ring_rows[:, :, :, 1]
        other = swap_core(pick(rows, 1 - core, 1))
        return in_order(pick(rows, core, 1), other, core, 2).reshape(2 * HD, width)

    w_query, w_keyval, w_out = query_rows(0), keyval_rows(), query_rows(2)

    resid_in = tokens[0]
    grad_out = cotangent[0]
    normed_one = norm_scale(resid_in, scales[0]).astype(bfloat)
    normed_all = quad_gather(normed_one)
    positions = chip * super_rows + jnp.arange(super_rows, dtype=jnp.int32)
    angles = turn_angles(positions % seq_len, HD)
    query_raw = jnp.einsum("td,fd->tf", normed_all, w_query, preferred_element_type=single)
    keyval_raw = jnp.einsum("td,fd->tf", normed_all, w_keyval, preferred_element_type=single)
    query = rotate(query_raw.reshape(super_rows, 2, HD), angles, 1.0).astype(bfloat)
    key_angles = jnp.where(side == 0, angles, 0.0)
    keyval = rotate(keyval_raw.reshape(super_rows, 2, HD), key_angles, 1.0).astype(bfloat)
    keyval = in_order(pick(keyval, side, 1), swap_side(pick(keyval, 1 - side, 1)), side, 0)
    keyval_all = ring_gather(keyval.reshape(2 * super_rows, HD), chips, 1)
    keyval_all = keyval_all.reshape(chips, 2, super_rows, HD)
    key_all = keyval_all[:, 0].reshape(chips * super_rows, HD)
    value_all = keyval_all[:, 1].reshape(chips * super_rows, HD)

    key_pos = jnp.arange(chips * super_rows, dtype=jnp.int32)
    distance = positions[:, None] - key_pos[None, :]
    same_seq = (positions // seq_len)[:, None] == (key_pos // seq_len)[None, :]
    allowed = (distance >= 0) & (distance < WIN) & same_seq

    def score_block():
        raw = jnp.einsum("qgd,kd->gqk", query, key_all, preferred_element_type=single)
        bent = jnp.tanh(raw * (scale / softcap))
        return bent, jnp.where(allowed, jnp.exp(softcap * bent), 0.0)

    bent, powers = score_block()
    total = jnp.sum(powers, axis=-1, keepdims=True)
    attended = jnp.einsum(
        "gqk,kd->gqd", powers.astype(bfloat), value_all, preferred_element_type=single
    )
    attended = (attended / total).transpose(1, 0, 2).reshape(super_rows, 2 * HD).astype(bfloat)
    projected = quad_scatter(jnp.dot(attended, w_out, preferred_element_type=single))
    resid_mid = resid_in + norm_scale(projected, scales[1])
    normed_two = norm_scale(resid_mid, scales[2]).astype(bfloat)

    ffn_all = jnp.concatenate([ffn_pair, swap_core(ffn_pair)], axis=1)
    w_gate, w_up, w_down = ffn_all[0], ffn_all[1], ffn_all[2]
    ring_tokens = chips * tok_rows
    normed_ring = ring_gather(normed_two, chips, 2).reshape(ring_tokens, width)
    gate_part = jnp.einsum("td,rd->tr", normed_ring, w_gate, preferred_element_type=single)
    up_part = jnp.einsum("td,rd->tr", normed_ring, w_up, preferred_element_type=single)
    hidden = hidden_unit(gate_part, up_part).astype(bfloat)
    ffn_part = jnp.dot(hidden, w_down, preferred_element_type=single).astype(bfloat)
    ffn_acc = ring_scatter(ffn_part.reshape(chips, tok_rows, width), chips, 3)
    result = resid_mid + norm_scale(ffn_acc, scales[3])

    ignored, post_back = jax.vjp(norm_scale, ffn_acc, scales[3])
    d_ffn, d_gain3 = post_back(grad_out)
    d_ffn_ring = ring_gather(d_ffn.astype(bfloat), chips, 4).reshape(ring_tokens, width)
    d_hidden = jnp.einsum("td,rd->tr", d_ffn_ring, w_down, preferred_element_type=single)
    ignored, unit_back = jax.vjp(hidden_unit, gate_part, up_part)
    d_gate, d_up = unit_back(d_hidden)
    d_gate = d_gate.astype(bfloat)
    d_up = d_up.astype(bfloat)
    d_normed = jnp.dot(d_gate, w_gate, preferred_element_type=single)
    d_normed = (d_normed + jnp.dot(d_up, w_up, preferred_element_type=single)).astype(bfloat)
    d_normed_two = ring_scatter(d_normed.reshape(chips, tok_rows, width), chips, 5)

    def ffn_rows(left, right):
        return jnp.einsum("tr,td->rd", left, right, preferred_element_type=single)

    ffn_terms = jnp.stack(
        [ffn_rows(d_gate, normed_ring), ffn_rows(d_up, normed_ring), ffn_rows(hidden, d_ffn_ring)]
    )
    units = ffn_weight.shape[0]
    ffn_terms = ffn_terms.reshape(3, 2, 2, units, width)
    ffn_terms = ffn_terms[:, 0] + swap_core(ffn_terms[:, 1].astype(bfloat)).astype(single)
    grad_ffn = ffn_terms[:, 0] + swap_side(ffn_terms[:, 1].astype(bfloat)).astype(single)

    ignored, mid_back = jax.vjp(norm_scale, resid_mid, scales[2])
    d_mid_norm, d_gain2 = mid_back(d_normed_two)
    d_mid = grad_out + d_mid_norm
    ignored, proj_back = jax.vjp(norm_scale, projected, scales[1])
    d_projected, d_gain1 = proj_back(d_mid)
    d_proj_all = quad_gather(d_projected.astype(bfloat))
    d_attended = jnp.einsum("td,fd->tf", d_proj_all, w_out, preferred_element_type=single)
    d_attended = d_attended.astype(bfloat).reshape(super_rows, 2, HD)

    bent, powers = score_block()
    probs = powers / total
    d_probs = jnp.einsum("qgd,kd->gqk", d_attended, value_all, preferred_element_type=single)
    row_dot = jnp.sum(d_probs * probs, axis=-1, keepdims=True)
    d_raw = (probs * (d_probs - row_dot) * (1.0 - bent * bent)).astype(bfloat)
    d_query = jnp.einsum("gqk,kd->qgd", d_raw, key_all, preferred_element_type=single) * scale
    d_keys = jnp.einsum("gqk,qgd->kd", d_raw, query, preferred_element_type=single) * scale
    d_values = jnp.einsum(
        "gqk,qgd->kd", probs.astype(bfloat), d_attended, preferred_element_type=single
    )
    d_pieces = jnp.stack(
        [d_keys.reshape(chips, super_rows, HD), d_values.reshape(chips, super_rows, HD)], axis=1
    ).astype(bfloat)
    d_keyval = ring_scatter(d_pieces.reshape(chips, 2 * super_rows, HD), chips, 6)
    d_keyval = d_keyval.reshape(2, super_rows, HD).astype(bfloat)
    d_keyval = in_order(pick(d_keyval, side), swap_side(pick(d_keyval, 1 - side)), side, 1)
    d_query_raw = rotate(d_query, angles, -1.0).reshape(super_rows, 2 * HD).astype(bfloat)
    d_keyval_raw = rotate(d_keyval.astype(single), key_angles, -1.0)
    d_keyval_raw = d_keyval_raw.reshape(super_rows, 2 * HD).astype(bfloat)
    d_normed_one = jnp.dot(d_query_raw, w_query, preferred_element_type=single)
    d_normed_one = d_normed_one + jnp.dot(d_keyval_raw, w_keyval, preferred_element_type=single)
    d_normed_one = quad_scatter(d_normed_one)
    ignored, first_back = jax.vjp(norm_scale, resid_in, scales[0])
    d_in_norm, d_gain0 = first_back(d_normed_one)
    tokens_grad = d_mid + d_in_norm

    def attn_rows(left, right):
        rows = jnp.einsum("tf,td->fd", left, right, preferred_element_type=single).astype(bfloat)
        return rows.reshape(2, pairs, 2, share, width)

    term_query = attn_rows(d_query_raw, normed_all)
    term_keyval = attn_rows(d_keyval_raw, normed_all)
    term_out = attn_rows(attended, d_proj_all)

    def to_core(term, axis):
        return in_order(pick(term, core, 2), swap_core(pick(term, 1 - core, 2)), core, axis)

    terms = jnp.stack([to_core(term_query, 0), to_core(term_keyval, 1), to_core(term_out, 0)], axis=3)
    grad_attn = ring_scatter(terms.reshape(chips, 3 * share, width), chips, 7)
    grad_attn = grad_attn.reshape(3, share, width)
    term_gain = jnp.stack([d_gain0, d_gain1, d_gain2, d_gain3])
    grad_gain = lax.psum_scatter(term_gain, ("head", "fsdp"), scatter_dimension=1, tiled=True)

    gains_first_new, gains_second_new, gains_new = adamw(
        gains, gains_first, gains_second, grad_gain, rate_gain, 0.0
    )
    attn_first_new, attn_second_new, attn_weight_new = adamw(
        attn_weight, attn_first, attn_second, grad_attn, rate_matrix, decay_matrix
    )
    ffn_first_new, ffn_second_new, ffn_weight_new = adamw(
        ffn_weight, ffn_first, ffn_second, grad_ffn.transpose(1, 0, 2), rate_matrix, decay_matrix
    )
    return (
        result[None],
        tokens_grad[None],
        gains_first_new,
        gains_second_new,
        gains_new,
        attn_first_new,
        attn_second_new,
        attn_weight_new,
        ffn_first_new,
        ffn_second_new,
        ffn_weight_new,
    )


def step_kernel(
    tiles,
    weight_ref,
    first_ref,
    second_ref,
    own_ref,
    side_ref,
    weight_two_ref,
    first_two_ref,
    second_two_ref,
    grad_two_ref,
    first_out,
    second_out,
    weight_out,
    first_two_out,
    second_two_out,
    weight_two_out,
):
    index = pl.program_id(0)

    @pl.when(index < tiles)
    def _():
        grad = own_ref[...].astype(single) + side_ref[...].astype(single)
        first_out[...], second_out[...], weight_out[...] = adamw(
            weight_ref[...], first_ref[...], second_ref[...], grad, rate_matrix, decay_matrix
        )

    @pl.when(index >= tiles)
    def _():
        first_two_out[...], second_two_out[...], weight_two_out[...] = adamw(
            weight_two_ref[...],
            first_two_ref[...],
            second_two_ref[...],
            grad_two_ref[...],
            rate_matrix,
            decay_matrix,
        )


def step_weights(state, own, side, state_two, grad_two):
    rows, width = state[0].shape
    rows_two = grad_two.shape[0]
    size = 96
    tiles, tiles_two = rows // size, rows_two // size
    block = pl.BlockSpec((size, width), lambda index: (jnp.minimum(index, tiles - 1), 0))
    block_two = pl.BlockSpec((size, width), lambda index: (jnp.maximum(index - tiles, 0), 0))
    return pl.pallas_call(
        functools.partial(step_kernel, tiles),
        grid=(tiles + tiles_two,),
        out_shape=(jax.ShapeDtypeStruct((rows, width), single),) * 3
        + (jax.ShapeDtypeStruct((rows_two, width), single),) * 3,
        in_specs=[block] * 5 + [block_two] * 4,
        out_specs=(block,) * 3 + (block_two,) * 3,
        compiler_params=pltpu.CompilerParams(vmem_limit_bytes=62 * 2**20),
        cost_estimate=cost(20),
    )(*state, own, side, *state_two, grad_two)


def per_device(
    tokens,
    cotangent,
    gains,
    gains_first,
    gains_second,
    attn_weight,
    attn_first,
    attn_second,
    ffn_weight,
    ffn_first,
    ffn_second,
):
    devices = lax.axis_size("fsdp")
    chips = devices // 2
    side = lax.axis_index("head")
    place = lax.axis_index("fsdp")
    chip = place // 2
    tok_rows = tokens.shape[1]
    super_rows = 4 * tok_rows
    seq_len = min(SEQ_LEN, super_rows * chips)
    share = attn_weight.shape[1]
    width = tokens.shape[2]
    gain_columns = gains.shape[1]
    gain_start = (side * devices + place) * gain_columns

    units = ffn_weight.shape[0]

    def flat(value):
        return value.transpose(1, 0, 2).reshape(3 * units, width)

    ffn_wide = flat(ffn_weight)
    resid_in = tokens[0]
    grad_out = cotangent[0]
    positions = chip * super_rows + jnp.arange(super_rows, dtype=jnp.int32)
    angles = turn_angles(positions % seq_len, HD)
    key_angles = jnp.where(side == 0, angles, 0.0)
    gains_placed = lax.dynamic_update_slice(
        jnp.zeros((4, width), single), gains, (0, gain_start)
    )
    turns = (jnp.cos(angles), jnp.sin(angles), jnp.cos(key_angles), jnp.sin(key_angles))
    made = front(attn_weight, gains_placed, resid_in, turns, ffn_wide, chips, 0)
    attn_rows, scales, normed_all, query, keyval, attended, inverse, projected = made[:8]
    own_units, core_units, side_units, diag_units = made[8:]
    result, d_mid, d_proj_low, gain_rows, terms_own, terms_other = feed_forward(
        resid_in,
        projected,
        grad_out,
        scales,
        (own_units, side_units, core_units, diag_units),
        chips,
        1,
    )
    grad_attn, tokens_grad, gain_total, terms_sent, terms_side, terms_mine = tail(
        d_proj_low,
        query,
        keyval,
        attended,
        inverse,
        attn_rows,
        normed_all,
        turns,
        (resid_in, d_mid, scales, gain_rows),
        terms_own,
        terms_other,
        chips,
        2,
    )
    grad_gain = lax.dynamic_slice(gain_total, (0, gain_start), gains.shape)

    gains_first_new, gains_second_new, gains_new = adamw(
        gains, gains_first, gains_second, grad_gain, rate_gain, 0.0
    )
    def rows_of(value):
        return value.reshape(3 * share, width)

    stepped = step_weights(
        (ffn_wide, flat(ffn_first), flat(ffn_second)),
        terms_mine,
        terms_side,
        (rows_of(attn_weight), rows_of(attn_first), rows_of(attn_second)),
        grad_attn,
    )
    ffn_first_new, ffn_second_new, ffn_weight_new = (
        value.reshape(3, units, width).transpose(1, 0, 2) for value in stepped[:3]
    )
    attn_first_new, attn_second_new, attn_weight_new = (
        value.reshape(3, share, width) for value in stepped[3:]
    )
    return (
        result[None],
        tokens_grad[None],
        gains_first_new,
        gains_second_new,
        gains_new,
        attn_first_new,
        attn_second_new,
        attn_weight_new,
        ffn_first_new,
        ffn_second_new,
        ffn_weight_new,
    )


def solution(mesh):
    by_token = P("fsdp", "head", None)
    by_column = P(None, ("head", "fsdp"))
    by_row = P(None, ("head", "fsdp"), None)
    by_unit = P(("head", "fsdp"), None, None)
    placed = (by_token,) * 2 + (by_column,) * 3 + (by_row,) * 3 + (by_unit,) * 3
    body = per_device if mesh.shape["fsdp"] == 16 else general_device
    return jax.shard_map(
        body, mesh=mesh, in_specs=placed, out_specs=placed, check_vma=False
    )
```

```python
import functools
import math

import jax
import jax.numpy as jnp
import numpy as np
from jax import lax
from jax.experimental import pallas as pl
from jax.experimental.pallas import tpu as pltpu
from jax.sharding import PartitionSpec as P

HQ = 8
HK = 4
HD = 256
WIN = 4096
STEP = 10
SEQ_LEN = 8192


eps_norm = 1e-06
softcap = 50.0
beta_one = 0.9
beta_two = 0.95
adam_eps = 1e-08
rate_matrix = 0.02
rate_gain = 0.2
decay_matrix = 0.1

bfloat = jnp.bfloat16
single = jnp.float32
MESH = pl.DeviceIdType.MESH


def norm_scale(values, scales):
    return (
        values
        * lax.rsqrt(jnp.mean(values * values, axis=-1, keepdims=True) + eps_norm)
        * (1.0 + scales)
    )


def turn_angles(positions, head_width):
    halfway = head_width // 2
    inverse_freq = 10000.0 ** (-(jnp.arange(halfway, dtype=jnp.float32) * 2.0) / head_width)
    return positions.astype(jnp.float32)[:, None] * inverse_freq[None, :]


def rotate(values, angles, direction):
    halfway = values.shape[-1] // 2
    cosine = jnp.cos(angles)[:, None, :]
    sine_part = direction * jnp.sin(angles)[:, None, :]
    former = values[..., :halfway]
    latter = values[..., halfway:]
    return jnp.concatenate(
        [former * cosine - latter * sine_part, latter * cosine + former * sine_part], axis=-1
    )


def adamw(weight, moment, second, gradient, step_rate, decay_rate):
    moment = beta_one * moment + (1.0 - beta_one) * gradient
    second = beta_two * second + (1.0 - beta_two) * gradient * gradient
    update = (
        moment / (1.0 - beta_one**STEP) / (jnp.sqrt(second / (1.0 - beta_two**STEP)) + adam_eps)
        + decay_rate * weight
    )
    return (moment, second, weight - step_rate * update)


def hidden_unit(gate_part, up_part):
    return jax.nn.gelu(gate_part, approximate=True) * up_part


def ring_of(chip, chips):
    wide = chips // 4
    deep, side = chip // wide, chip % wide
    return side * 4 + deep + (side % 2) * (3 - 2 * deep)


def chip_of(ring, chips):
    wide = chips // 4
    side, along = ring // 4, ring % 4
    return (along + (side % 2) * (3 - 2 * along)) * wide + side


def ring_places(chips):
    index = lax.axis_index("fsdp")
    core, chip = index % 2, index // 2
    ring = ring_of(chip, chips)
    right = 2 * chip_of((ring + 1) % chips, chips) + core
    left = 2 * chip_of((ring + chips - 1) % chips, chips) + core
    return chip, ring, right, left


def ring_barrier(right, left):
    barrier = pltpu.get_barrier_semaphore()
    for neighbour in (left, right):
        pl.semaphore_signal(barrier, inc=1, device_id={"fsdp": neighbour}, device_id_type=MESH)
    pl.semaphore_wait(barrier, 2)


def region(shape, pieces, way, piece):
    rows, columns = shape
    if rows % 32 == 0:
        size = rows // 2 // pieces
        start = way * (rows // 2) + piece * size
        return (pl.ds(start, size), pl.ds(0, columns)), (pl.ds(piece * size, size), pl.ds(0, columns))
    size = columns // 2
    return (pl.ds(0, rows), pl.ds(way * size, size)), (pl.ds(0, rows), pl.ds(0, size))


def half_shape(rows, columns):
    return (rows // 2, columns) if rows % 32 == 0 else (rows, columns // 2)


def gather_kernel(chips, pieces, own_ref, all_ref, local_sem, send_sem, recv_sem):
    chip, ring, right, left = ring_places(chips)
    ring_barrier(right, left)
    keep = pltpu.make_async_copy(own_ref, all_ref.at[chip], local_sem)
    keep.start()

    def copy(way, step, piece, first):
        owner = chip_of((ring + (chips - step if way == 0 else step)) % chips, chips)
        part, ignored = region(own_ref.shape, pieces, way, piece)
        there = all_ref.at[(owner,) + part]
        return pltpu.make_async_remote_copy(
            src_ref=own_ref.at[part] if first else there,
            dst_ref=there,
            send_sem=send_sem.at[way, piece, step],
            recv_sem=recv_sem.at[way, piece, step],
            device_id={"fsdp": right if way == 0 else left},
            device_id_type=MESH,
        )

    streams = [(way, piece) for piece in range(pieces) for way in range(2)]
    for way, piece in streams:
        copy(way, 0, piece, True).start()

    def body(step, carried):
        for way, piece in streams:
            copy(way, step - 1, piece, False).wait_recv()
            copy(way, step, piece, False).start()
        return carried

    lax.fori_loop(1, chips - 1, body, 0)
    for way, piece in streams:
        copy(way, chips - 2, piece, False).wait_recv()

    def finish(step, carried):
        for way, piece in streams:
            copy(way, step, piece, False).wait_send()
        return carried

    lax.fori_loop(0, chips - 1, finish, 0)
    keep.wait()


def ring_gather(own, chips, ident):
    rows, columns = own.shape
    pieces = 2 if rows % 64 == 0 else 1
    return pl.pallas_call(
        functools.partial(gather_kernel, chips, pieces),
        out_shape=jax.ShapeDtypeStruct((chips, rows, columns), own.dtype),
        in_specs=[pl.BlockSpec(memory_space=pl.ANY)],
        out_specs=pl.BlockSpec(memory_space=pl.ANY),
        scratch_shapes=[
            pltpu.SemaphoreType.DMA,
            pltpu.SemaphoreType.DMA((2, pieces, chips - 1)),
            pltpu.SemaphoreType.DMA((2, pieces, chips - 1)),
        ],
        compiler_params=pltpu.CompilerParams(collective_id=ident, has_side_effects=True),
        cost_estimate=cost(45),
    )(own)


def scatter_kernel(chips, pieces, parts_ref, sum_ref, held, send_sem, recv_sem):
    chip, ring, right, left = ring_places(chips)
    ring_barrier(right, left)

    def owner_of(way, step):
        shift = chips - 1 - step if way == 0 else 1 + step
        return chip_of((ring + shift) % chips, chips)

    def copy(way, step, piece, first):
        part, place = region(sum_ref.shape, pieces, way, piece)
        return pltpu.make_async_remote_copy(
            src_ref=(
                parts_ref.at[(owner_of(way, step),) + part]
                if first
                else held.at[(way, step - 1) + place]
            ),
            dst_ref=held.at[(way, step) + place],
            send_sem=send_sem.at[way, piece, step],
            recv_sem=recv_sem.at[way, piece, step],
            device_id={"fsdp": right if way == 0 else left},
            device_id_type=MESH,
        )

    streams = [(way, piece) for piece in range(pieces) for way in range(2)]
    for way, piece in streams:
        copy(way, 0, piece, True).start()

    def arrived(way, step, piece):
        copy(way, step, piece, True).wait_recv()
        part, place = region(sum_ref.shape, pieces, way, piece)
        here = parts_ref[(owner_of(way, step + 1),) + part]
        return held[(way, step) + place].astype(single) + here.astype(single)

    def body(step, carried):
        for way, piece in streams:
            total = arrived(way, step - 1, piece)
            part, place = region(sum_ref.shape, pieces, way, piece)
            held[(way, step - 1) + place] = total.astype(held.dtype)
            copy(way, step, piece, False).start()
        return carried

    lax.fori_loop(1, chips - 1, body, 0)
    for way, piece in streams:
        part, place = region(sum_ref.shape, pieces, way, piece)
        sum_ref[part] = arrived(way, chips - 2, piece)

    def finish(step, carried):
        for way, piece in streams:
            copy(way, step, piece, True).wait_send()
        return carried

    lax.fori_loop(0, chips - 1, finish, 0)


def ring_scatter(parts, chips, ident):
    rows, columns = parts.shape[1:]
    pieces = 2 if rows % 64 == 0 else 1
    return pl.pallas_call(
        functools.partial(scatter_kernel, chips, pieces),
        out_shape=jax.ShapeDtypeStruct((rows, columns), single),
        in_specs=[pl.BlockSpec(memory_space=pltpu.VMEM)],
        out_specs=pl.BlockSpec(memory_space=pltpu.VMEM),
        scratch_shapes=[
            pltpu.VMEM((2, chips - 1) + half_shape(rows, columns), parts.dtype),
            pltpu.SemaphoreType.DMA((2, pieces, chips - 1)),
            pltpu.SemaphoreType.DMA((2, pieces, chips - 1)),
        ],
        compiler_params=pltpu.CompilerParams(
            collective_id=ident, has_side_effects=True, vmem_limit_bytes=56 * 2**20
        ),
        cost_estimate=cost(45),
    )(parts)


def norm_back(values, scales, grad):
    inverse = lax.rsqrt(jnp.mean(values * values, axis=-1, keepdims=True) + eps_norm)
    bent = grad * (1.0 + scales)
    slope = jnp.mean(bent * values, axis=-1, keepdims=True) * (inverse * inverse * inverse)
    return bent * inverse - values * slope, jnp.sum(grad * values * inverse, axis=0, keepdims=True)


def gelu_parts(gate):
    root = math.sqrt(2.0 / math.pi)
    square = gate * gate
    bend = jnp.tanh(root * gate * (1.0 + 0.044715 * square))
    half = 0.5 * (1.0 + bend)
    slope = half + 0.5 * gate * (1.0 - bend * bend) * (root * (1.0 + 3.0 * 0.044715 * square))
    return gate * half, slope


def dot_nt(left, right):
    return lax.dot_general(left, right, (((1,), (1,)), ((), ())), preferred_element_type=single)


def dot_nn(left, right):
    return lax.dot_general(left, right, (((1,), (0,)), ((), ())), preferred_element_type=single)


def dot_tn(left, right):
    return lax.dot_general(left, right, (((0,), (0,)), ((), ())), preferred_element_type=single)


class Ring:
    def __init__(self, chips, pieces, rows, send_sem, recv_sem):
        self.chips, self.pieces, self.half = chips, pieces, rows // 2
        self.size = rows // 2 // pieces
        self.chip, self.ring, self.right, self.left = ring_places(chips)
        self.send_sem, self.recv_sem = send_sem, recv_sem
        self.streams = [(way, piece) for piece in range(pieces) for way in range(2)]

    def owner(self, way, step):
        shift = self.chips - step if way == 0 else step
        return chip_of((self.ring + shift) % self.chips, self.chips)

    def copy(self, source, target, way, piece, step):
        return pltpu.make_async_remote_copy(
            src_ref=source,
            dst_ref=target,
            send_sem=self.send_sem.at[way, piece, step],
            recv_sem=self.recv_sem.at[way, piece, step],
            device_id={"fsdp": self.right if way == 0 else self.left},
            device_id_type=MESH,
        )

    def part(self, way, piece):
        return pl.ds(way * self.half + piece * self.size, self.size)

    def place(self, piece):
        return pl.ds(piece * self.size, self.size)

    def gather_copy(self, all_ref, way, piece, step):
        there = all_ref.at[self.owner(way, step), self.part(way, piece)]
        return self.copy(there, there, way, piece, step)

    def of(self, only):
        return [(way, piece) for way, piece in self.streams if only is None or piece == only]

    def gather_step(self, all_ref, step, only=None):
        for way, piece in self.of(only):

            @pl.when(step > 0)
            def _():
                self.gather_copy(all_ref, way, piece, step - 1).wait_recv()

            @pl.when(step < self.chips - 1)
            def _():
                self.gather_copy(all_ref, way, piece, step).start()

    def scatter_copy(self, parts_ref, held, way, piece, step, first):
        source = (
            parts_ref.at[self.owner(way, step + 1), self.part(way, piece)]
            if first
            else held.at[way, step - 1, self.place(piece)]
        )
        return self.copy(source, held.at[way, step, self.place(piece)], way, piece, step)

    def scatter_total(self, parts_ref, held, way, piece, step):
        self.scatter_copy(parts_ref, held, way, piece, step, True).wait_recv()
        here = parts_ref[self.owner(way, step + 2), self.part(way, piece)]
        return held[way, step, self.place(piece)].astype(single) + here.astype(single)

    def scatter_step(self, parts_ref, held, step, only=None):
        for way, piece in self.of(only):

            @pl.when(step == 0)
            def _():
                self.scatter_copy(parts_ref, held, way, piece, 0, True).start()

            @pl.when(step > 0)
            def _():
                total = self.scatter_total(parts_ref, held, way, piece, step - 1)
                held[way, step - 1, self.place(piece)] = total.astype(held.dtype)
                self.scatter_copy(parts_ref, held, way, piece, step, False).start()

    def scatter_end(self, parts_ref, held, sum_ref):
        for way, piece in self.streams:
            sum_ref[self.part(way, piece)] = self.scatter_total(
                parts_ref, held, way, piece, self.chips - 2
            )

    def finish(self, example):
        def body(step, carried):
            for way, piece in self.streams:
                self.copy(example, example, way, piece, step).wait_send()
            return carried

        lax.fori_loop(0, self.chips - 1, body, 0)


def quad_peers(chips):
    side = lax.axis_index("head")
    index = lax.axis_index("fsdp")
    chip, core = index // 2, index % 2
    ring = ring_of(chip, chips)
    around = [2 * chip_of((ring + hop) % chips, chips) + core for hop in range(1, chips)]
    return side, core, {"head": 1 - side}, {"fsdp": 2 * chip + 1 - core}, around


def wide_barrier(to_side, to_core, around):
    barrier = pltpu.get_barrier_semaphore()
    for target in [to_side, to_core] + [{"fsdp": other} for other in around]:
        pl.semaphore_signal(barrier, inc=1, device_id=target, device_id_type=MESH)
    pl.semaphore_wait(barrier, 2 + len(around))


def quad_barrier(to_side, to_core, right, left):
    barrier = pltpu.get_barrier_semaphore()
    for target in (to_side, to_core, {"fsdp": right}, {"fsdp": left}):
        pl.semaphore_signal(barrier, inc=1, device_id=target, device_id_type=MESH)
    pl.semaphore_wait(barrier, 4)


def remote(source, target, send_sem, recv_sem, device):
    return pltpu.make_async_remote_copy(
        src_ref=source,
        dst_ref=target,
        send_sem=send_sem,
        recv_sem=recv_sem,
        device_id=device,
        device_id_type=MESH,
    )


class Total:
    def __init__(self, value, near, blocks, send_sem, recv_sem, peers, chip):
        self.value, self.near, self.blocks = value, near, blocks
        self.send_sem, self.recv_sem = send_sem, recv_sem
        side, core, self.to_side, self.to_core, self.around = peers
        self.chip = chip
        self.first = remote(value.at[0], near.at[0], send_sem.at[0], recv_sem.at[0], self.to_side)
        self.second = remote(value.at[1], near.at[1], send_sem.at[1], recv_sem.at[1], self.to_core)

    def spread(self, hop):
        here = self.blocks.at[self.chip]
        return remote(
            here,
            here,
            self.send_sem.at[1 + hop],
            self.recv_sem.at[1 + hop],
            {"fsdp": self.around[hop - 1]},
        )

    def start(self):
        self.first.start()

    def over_cores(self):
        self.first.wait_recv()
        self.value[1] = self.value[0] + self.near[0]
        self.second.start()

    def over_ring(self):
        self.second.wait_recv()
        self.blocks[self.chip] = self.value[1] + self.near[1]
        for hop in range(1, len(self.around) + 1):
            self.spread(hop).start()

    def end(self):
        for hop in range(1, len(self.around) + 1):
            self.spread(hop).wait_recv()
        total = self.blocks[0]
        for other in range(1, len(self.around) + 1):
            total = total + self.blocks[other]
        self.first.wait_send()
        self.second.wait_send()
        for hop in range(1, len(self.around) + 1):
            self.spread(hop).wait_send()
        return total


def total_scratch(chips, width):
    return [
        pltpu.VMEM((2, 4, width), single),
        pltpu.VMEM((2, 4, width), single),
        pltpu.VMEM((chips, 4, width), single),
        pltpu.SemaphoreType.DMA((chips + 1,)),
        pltpu.SemaphoreType.DMA((chips + 1,)),
    ]


def turn(raw, cosine, sine):
    halfway = raw.shape[1] // 2
    former, latter = raw[:, :halfway], raw[:, halfway:]
    return jnp.concatenate(
        [former * cosine - latter * sine, latter * cosine + former * sine], axis=1
    )


def front_kernel(
    chips,
    cuts,
    own_ref,
    gains_ref,
    resid_ref,
    pace_ref,
    wide_units_ref,
    rows_out,
    scales_ref,
    normed_out,
    query_ref,
    keyval_out,
    attended_ref,
    inverse_ref,
    projected_ref,
    cosine_ref,
    sine_ref,
    key_cosine_ref,
    key_sine_ref,
    own_units_ref,
    core_units_ref,
    side_units_ref,
    diag_units_ref,
    rows_ref,
    normed_ref,
    keyval_ref,
    all_rows,
    both,
    total,
    sums,
    product,
    across_put,
    across_got,
    along_put,
    along_got,
    cast_in,
    cast_out,
    value,
    near,
    blocks,
    total_send,
    total_recv,
    send_sem,
    recv_sem,
    place_sem,
    peer_sem,
    key_send,
    key_recv,
    quad_send,
    quad_recv,
    cast_sem,
    out_sem,
    bulk_send,
    bulk_recv,
):
    share, width = own_ref.shape[1:]
    tok_rows = resid_ref.shape[0]
    tokens = 4 * tok_rows
    half = width // 2
    pairs = chips // 4
    scale = 1.0 / math.sqrt(HD)
    seq_len = min(SEQ_LEN, tokens * chips)
    chip, ring, right, left = ring_places(chips)
    peers = quad_peers(chips)
    side, core, to_side, to_core, around = peers
    cast_rows = cast_in.shape[1]
    casts = wide_units_ref.shape[0] // cast_rows

    def cast_load(tile):
        rows = pl.ds(tile * cast_rows, cast_rows)
        return pltpu.make_async_copy(
            wide_units_ref.at[rows], cast_in.at[tile % 2], cast_sem.at[0, tile % 2]
        )

    def cast_store(tile):
        rows = pl.ds(tile * cast_rows, cast_rows)
        return pltpu.make_async_copy(
            cast_out.at[tile % 2], own_units_ref.at[rows], cast_sem.at[1, tile % 2]
        )

    def cast(first, last):
        for tile in range(first, last):
            cast_load(tile).wait()
            if tile >= 3:
                cast_store(tile - 2).wait()
            cast_out[tile % 2] = cast_in[tile % 2].astype(bfloat)
            cast_store(tile).start()
            if tile + 2 < casts:
                cast_load(tile + 2).start()

    outs = [
        pltpu.make_async_copy(rows_ref.at[0:2], rows_out.at[0:2], out_sem.at[0]),
        pltpu.make_async_copy(rows_ref.at[2], rows_out.at[2], out_sem.at[1]),
        pltpu.make_async_copy(normed_ref, normed_out, out_sem.at[2]),
        pltpu.make_async_copy(keyval_ref, keyval_out, out_sem.at[3]),
    ]
    def tables():
        place_in = chip * tokens + lax.broadcasted_iota(jnp.int32, cosine_ref.shape, 0)
        angles = (place_in % seq_len).astype(single) * pace_ref[...]
        cosine_ref[...] = jnp.cos(angles)
        sine_ref[...] = jnp.sin(angles)
        key_cosine_ref[...] = jnp.where(side == 0, cosine_ref[...], 1.0)
        key_sine_ref[...] = jnp.where(side == 0, sine_ref[...], 0.0)

    cast_load(0).start()
    cast_load(1).start()
    all_rows[chip] = own_ref[...].astype(bfloat)
    value[0] = gains_ref[...].astype(bfloat).astype(single)
    wide_barrier(to_side, to_core, around)
    gains_total = Total(value, near, blocks, total_send, total_recv, peers, chip)
    gains_total.start()
    streams = [(way, slot) for slot in range(2) for way in range(2)]
    out_streams = [(way, 2) for way in range(2)]
    key_streams = [(way, kind) for kind in range(2) for way in range(2)]

    def owner_of(way, step):
        return chip_of((ring + (chips - step if way == 0 else step)) % chips, chips)

    def hop(way, slot, step):
        there = all_rows.at[owner_of(way, step), slot, :, pl.ds(way * half, half)]
        return remote(
            there,
            there,
            send_sem.at[way, slot, step],
            recv_sem.at[way, slot, step],
            {"fsdp": right if way == 0 else left},
        )

    def key_hop(way, kind, step):
        there = keyval_ref.at[owner_of(way, step), kind, pl.ds(way * (tokens // 2), tokens // 2)]
        return remote(
            there,
            there,
            key_send.at[way, kind, step],
            key_recv.at[way, kind, step],
            {"fsdp": right if way == 0 else left},
        )

    def goal(way, slot, step):
        owner = owner_of(way, step)
        deep = owner // pairs
        unit = (owner % pairs) * 2 + core
        taker, head = (deep % 2, deep // 2) if slot == 1 else (deep // 2, deep % 2)
        columns = pl.ds(way * half, half)
        source = all_rows.at[owner, slot, :, columns]
        start = pl.multiple_of(head * HD + unit * share, share)
        target = rows_ref.at[slot, pl.ds(start, share), columns]
        sem = place_sem.at[way, slot, step]

        def here():
            return pltpu.make_async_copy(source, target, sem)

        def there():
            return remote(source, target, sem, peer_sem.at[way, slot, step], to_core)

        return taker, here, there

    def place(way, slot, step):
        taker, here, there = goal(way, slot, step)

        @pl.when(taker == core)
        def _():
            here().start()

        @pl.when(taker != core)
        def _():
            there().start()

    def placed(way, slot, step):
        taker, here, there = goal(way, slot, step)

        @pl.when(taker == core)
        def _():
            here().wait()
            there().wait_recv()

        @pl.when(taker != core)
        def _():
            there().wait_send()

    def pass_on(which, step):
        for way, slot in which:

            @pl.when(step > 0)
            def _():
                hop(way, slot, step - 1).wait_recv()

            @pl.when(step < chips - 1)
            def _():
                hop(way, slot, step).start()

            place(way, slot, step)

    def settle(which):
        def body(step, carried):
            for way, slot in which:
                placed(way, slot, step)

                @pl.when(step < chips - 1)
                def _():
                    hop(way, slot, step).wait_send()

            return carried

        lax.fori_loop(0, chips, body, 0)

    def quad_copy(source, target, index, device):
        return remote(source, target, quad_send.at[index], quad_recv.at[index], device)

    mine = normed_ref.at[core, side]
    along = quad_copy(mine, mine, 0, to_side)
    across = quad_copy(normed_ref.at[core], normed_ref.at[core], 1, to_core)

    def bulk_side(part):
        rows = pl.ds(cuts[part], cuts[part + 1] - cuts[part])
        return remote(
            own_units_ref.at[rows],
            side_units_ref.at[rows],
            bulk_send.at[part],
            bulk_recv.at[part],
            to_side,
        )

    def bulk_diag(part):
        rows = pl.ds(cuts[part], cuts[part + 1] - cuts[part])
        return remote(
            side_units_ref.at[rows],
            diag_units_ref.at[rows],
            bulk_send.at[3 + part],
            bulk_recv.at[3 + part],
            to_core,
        )

    bulk_core = remote(own_units_ref, core_units_ref, bulk_send.at[6], bulk_recv.at[6], to_core)
    for way, slot in streams:
        hop(way, slot, 0).start()
    cast(0, 1)
    cast_store(0).wait()
    bulk_side(0).start()
    gains_total.over_cores()
    for way, slot in streams:
        place(way, slot, 0)
    gains_total.over_ring()
    pass_on(streams, 1)
    cast(1, 3)
    tables()
    pass_on(streams, 2)
    scales_ref[...] = gains_total.end()
    normed_ref[core, side] = norm_scale(resid_ref[...], scales_ref[0:1]).astype(bfloat)
    along.start()
    cast(3, 4)
    pass_on(streams, 3)
    cast(4, 6)
    pass_on(streams, 4)
    cast(6, casts)
    cast_store(casts - 2).wait()
    cast_store(casts - 1).wait()
    bulk_core.start()
    along.wait()
    across.start()
    bulk_side(1).start()

    def body(step, carried):
        pass_on(streams, step)
        return carried

    lax.fori_loop(5, chips, body, 0)
    pass_on(out_streams, 0)
    across.wait()
    outs[2].start()
    settle(streams)
    outs[0].start()

    def project(slot, head):
        rows = slice(head * HD, head * HD + HD)
        return dot_nt(normed_ref[...].reshape(tokens, width), rows_ref[slot, rows])

    for head in range(2):
        raw = project(1, head)
        both[head] = turn(raw, key_cosine_ref[...], key_sine_ref[...]).astype(bfloat)
    swap = quad_copy(both.at[1 - side], keyval_ref.at[chip, side], 2, to_side)
    swap.start()
    bulk_side(2).start()
    for part in range(2):
        bulk_side(part).wait_recv()
        bulk_diag(part).start()
    pass_on(out_streams, 1)
    keyval_ref[chip, side] = both[side]
    for head in range(2):
        raw = project(0, head)
        query_ref[head] = turn(raw, cosine_ref[...], sine_ref[...]).astype(bfloat)
        pass_on(out_streams, 2 + head)
    total[...] = jnp.zeros_like(total)
    sums[...] = jnp.zeros_like(sums)
    swap.wait()

    def block(way, owner):
        part = tokens // 2
        key = keyval_ref[owner, 0, way * part : way * part + part]
        val = keyval_ref[owner, 1, way * part : way * part + part]
        row = lax.broadcasted_iota(jnp.int32, (tokens, part), 0)
        column = lax.broadcasted_iota(jnp.int32, (tokens, part), 1)
        allowed = row + (chip - owner) * tokens - way * part >= column

        def one_head(head, carried):
            bent = jnp.tanh(dot_nt(query_ref[head], key) * (scale / softcap))
            powers = jnp.where(allowed, jnp.exp(softcap * bent), 0.0)
            sums[head] += powers[:, : part // 2] + powers[:, part // 2 :]
            total[head] += dot_nn(powers.astype(bfloat), val)
            return carried

        for head in range(2):
            one_head(head, 0)

    def key_body(step, carried):
        for way, kind in key_streams:

            @pl.when(step > 0)
            def _():
                key_hop(way, kind, step - 1).wait_recv()

            @pl.when(step < chips - 1)
            def _():
                key_hop(way, kind, step).start()

        for way in range(2):
            owner = owner_of(way, step)

            @pl.when(owner <= chip)
            def _():
                block(way, owner)

            if way == 0:

                @pl.when(step < chips - 4)
                def _():
                    pass_on(out_streams, step + 4)

        return carried

    lax.fori_loop(0, chips, key_body, 0)
    outs[3].start()
    bulk_side(2).wait_recv()
    bulk_diag(2).start()
    settle(out_streams)
    outs[1].start()
    for head in range(2):
        inverse = 1.0 / jnp.sum(sums[head], axis=-1, keepdims=True)
        inverse_ref[head] = jnp.broadcast_to(inverse, inverse_ref.shape[1:])
        attended_ref[:, head * HD : head * HD + HD] = (total[head] * inverse).astype(bfloat)
    span = width // 3
    tiles = [slice(tile * span, tile * span + span) for tile in range(3)]

    def project_out(part, ref, columns):
        first = pl.ds(pl.multiple_of(part * 2 * tok_rows, 2 * tok_rows), 2 * tok_rows)
        made = dot_nn(attended_ref[first], rows_ref[2, :, columns])
        ref[:, :, columns] = made.reshape(2, tok_rows, span).astype(ref.dtype)

    across = [
        quad_copy(across_put.at[:, :, columns], across_got.at[:, :, columns], 3 + tile, to_core)
        for tile, columns in enumerate(tiles)
    ]
    along = [
        quad_copy(along_put.at[:, columns], along_got.at[:, columns], 6 + tile, to_side)
        for tile, columns in enumerate(tiles)
    ]
    for tile, columns in enumerate(tiles):
        project_out(1 - core, across_put, columns)
        across[tile].start()
    for tile, columns in enumerate(tiles):
        project_out(core, product, columns)
        across[tile].wait()
        given = product[1 - side, :, columns] + across_got[1 - side, :, columns].astype(single)
        along_put[:, columns] = given.astype(bfloat)
        along[tile].start()

    def key_settle(step, carried):
        for way, kind in key_streams:
            key_hop(way, kind, step).wait_send()
        return carried

    lax.fori_loop(0, chips - 1, key_settle, 0)
    for out in outs:
        out.wait()
    bulk_core.wait()
    for part in range(3):
        bulk_side(part).wait_send()
        bulk_diag(part).wait()
    for tile, columns in enumerate(tiles):
        along[tile].wait()
        kept = product[side, :, columns] + across_got[side, :, columns].astype(single)
        projected_ref[:, columns] = kept + along_got[:, columns].astype(single)


def cost(micros):
    return pl.CostEstimate(flops=int(micros * 1e9), bytes_accessed=0, transcendentals=0)


def front(attn_weight, gains, resid_in, pace, ffn_wide, chips, ident):
    share, width = attn_weight.shape[1:]
    tok_rows = resid_in.shape[0]
    tokens = 4 * tok_rows
    units = ffn_wide.shape[0]
    cuts = (0, units // 9, units // 3, 2 * units // 3)
    vmem = pl.BlockSpec(memory_space=pltpu.VMEM)
    anywhere = pl.BlockSpec(memory_space=pl.ANY)
    return pl.pallas_call(
        functools.partial(front_kernel, chips, cuts),
        out_shape=(
            jax.ShapeDtypeStruct((3, 2 * HD, width), bfloat),
            jax.ShapeDtypeStruct((4, width), single),
            jax.ShapeDtypeStruct((2, 2, tok_rows, width), bfloat),
            jax.ShapeDtypeStruct((2, tokens, HD), bfloat),
            jax.ShapeDtypeStruct((chips, 2, tokens, HD), bfloat),
            jax.ShapeDtypeStruct((tokens, 2 * HD), bfloat),
            jax.ShapeDtypeStruct((2, tokens, 128), single),
            jax.ShapeDtypeStruct((tok_rows, width), single),
        )
        + (jax.ShapeDtypeStruct((tokens, HD // 2), single),) * 4
        + (jax.ShapeDtypeStruct((units, width), bfloat),) * 2
        + (jax.ShapeDtypeStruct((2 * units // 3, width), bfloat),) * 2,
        in_specs=[vmem] * 4 + [anywhere],
        out_specs=(anywhere, vmem, anywhere, vmem, anywhere, vmem, vmem, vmem)
        + (vmem,) * 4
        + (anywhere,) * 4,
        scratch_shapes=[
            pltpu.VMEM((3, 2 * HD, width), bfloat),
            pltpu.VMEM((2, 2, tok_rows, width), bfloat),
            pltpu.VMEM((chips, 2, tokens, HD), bfloat),
            pltpu.VMEM((chips, 3, share, width), bfloat),
            pltpu.VMEM((2, tokens, HD), bfloat),
            pltpu.VMEM((2, tokens, HD), single),
            pltpu.VMEM((2, tokens, 128), single),
            pltpu.VMEM((2, tok_rows, width), single),
            pltpu.VMEM((2, tok_rows, width), bfloat),
            pltpu.VMEM((2, tok_rows, width), bfloat),
            pltpu.VMEM((tok_rows, width), bfloat),
            pltpu.VMEM((tok_rows, width), bfloat),
            pltpu.VMEM((2, units // 9, width), single),
            pltpu.VMEM((2, units // 9, width), bfloat),
        ]
        + total_scratch(chips, width)
        + [
            pltpu.SemaphoreType.DMA((2, 3, chips - 1)),
            pltpu.SemaphoreType.DMA((2, 3, chips - 1)),
            pltpu.SemaphoreType.DMA((2, 3, chips)),
            pltpu.SemaphoreType.DMA((2, 3, chips)),
            pltpu.SemaphoreType.DMA((2, 2, chips - 1)),
            pltpu.SemaphoreType.DMA((2, 2, chips - 1)),
            pltpu.SemaphoreType.DMA((9,)),
            pltpu.SemaphoreType.DMA((9,)),
            pltpu.SemaphoreType.DMA((2, 2)),
            pltpu.SemaphoreType.DMA((4,)),
            pltpu.SemaphoreType.DMA((7,)),
            pltpu.SemaphoreType.DMA((7,)),
        ],
        compiler_params=pltpu.CompilerParams(
            collective_id=ident, has_side_effects=True, vmem_limit_bytes=60 * 2**20
        ),
        cost_estimate=cost(140),
    )(attn_weight, gains, resid_in, pace, ffn_wide)


def tail_kernel(
    chips,
    d_proj_ref,
    query_ref,
    keyval_in,
    attended_ref,
    inverse_ref,
    rows_in,
    normed_in,
    cosine_ref,
    sine_ref,
    key_cosine_ref,
    key_sine_ref,
    resid_ref,
    d_mid_ref,
    scales_ref,
    gains_ref,
    units_own_ref,
    units_other_ref,
    sum_ref,
    tokens_ref,
    total_ref,
    units_ref,
    units_got_ref,
    units_mine_ref,
    keyval_ref,
    rows_ref,
    normed_ref,
    d_all,
    d_out,
    delta,
    d_query,
    d_block,
    first_put,
    held_keys,
    swapped,
    d_raw,
    out_rows,
    parts,
    out_parts,
    held,
    out_held,
    across_got,
    along_put,
    along_got,
    value,
    near,
    blocks,
    total_send,
    total_recv,
    key_send,
    key_recv,
    place_sem,
    peer_sem,
    send_sem,
    recv_sem,
    out_send,
    out_recv,
    quad_send,
    quad_recv,
    load_sem,
    bulk_send,
    bulk_recv,
):
    tokens = query_ref.shape[1]
    half = tokens // 2
    width = resid_ref.shape[1]
    share = out_parts.shape[1]
    pairs = chips // 4
    scale = 1.0 / math.sqrt(HD)
    peers = quad_peers(chips)
    side, core, to_side, to_core, around = peers
    rings = [Ring(chips, 1, share, send_sem.at[slot], recv_sem.at[slot]) for slot in range(2)]
    ring = rings[0]
    out_ring = Ring(chips, 1, share, out_send, out_recv)
    chip = ring.chip
    gains_total = Total(value, near, blocks, total_send, total_recv, peers, chip)
    arrays = [
        pltpu.make_async_copy(rows_in.at[2], rows_ref.at[2], load_sem.at[3]),
        pltpu.make_async_copy(keyval_in, keyval_ref, load_sem.at[4]),
        pltpu.make_async_copy(normed_in, normed_ref, load_sem.at[5]),
        pltpu.make_async_copy(rows_in.at[0:2], rows_ref.at[0:2], load_sem.at[6]),
    ]
    d_all[core, side] = d_proj_ref[...]
    wide_barrier(to_side, to_core, around)

    def quad_copy(source, target, index, device):
        return remote(source, target, quad_send.at[index], quad_recv.at[index], device)

    def bulk(kind):
        return remote(
            units_ref.at[pl.ds(kind * (units_ref.shape[0] // 3), units_ref.shape[0] // 3)],
            units_got_ref.at[pl.ds(kind * (units_ref.shape[0] // 3), units_ref.shape[0] // 3)],
            bulk_send.at[kind],
            bulk_recv.at[kind],
            to_side,
        )

    units = units_ref.shape[0]
    ours = out_rows.reshape(6 * HD, width).at[pl.ds(0, units)]
    theirs = parts.reshape(2 * chips * share, width).at[pl.ds(0, units)]
    loads = (
        pltpu.make_async_copy(units_own_ref.at[1], ours, load_sem.at[0]),
        pltpu.make_async_copy(units_other_ref.at[1], theirs, load_sem.at[1]),
    )
    store = pltpu.make_async_copy(ours, units_ref, load_sem.at[2])
    spare = held.reshape(2 * (chips - 1) * share, width).at[pl.ds(0, units)]
    mine_loads = (
        pltpu.make_async_copy(units_own_ref.at[0], ours, load_sem.at[7]),
        pltpu.make_async_copy(units_other_ref.at[0], spare, load_sem.at[8]),
    )
    mine_store = pltpu.make_async_copy(ours, units_mine_ref, load_sem.at[9])
    mine_loads[1].start()

    def add_up(more):
        for kind in range(3):
            rows = slice(kind * units // 3, (kind + 1) * units // 3)
            ours[rows] = (ours[rows].astype(single) + more[rows].astype(single)).astype(bfloat)
    for load in loads:
        load.start()
    for array in arrays:
        array.start()
    quarter = tokens // 8
    halves = [slice(part * quarter, part * quarter + quarter) for part in range(2)]
    along = [
        quad_copy(d_all.at[core, side, rows], d_all.at[core, side, rows], part, to_side)
        for part, rows in enumerate(halves)
    ]
    across = quad_copy(d_all.at[core, side], d_all.at[core, side], 2, to_core)
    relay = [
        quad_copy(d_all.at[core, 1 - side, rows], d_all.at[core, 1 - side, rows], 3 + part, to_core)
        for part, rows in enumerate(halves)
    ]
    for part in range(2):
        along[part].start()
    across.start()
    d_query[...] = jnp.zeros_like(d_query)
    for load in loads:
        load.wait()
    add_up(theirs)
    store.start()
    for part in range(2):
        along[part].wait()
        relay[part].start()
    store.wait()
    bulk(0).start()
    bulk(1).start()
    mine_loads[0].start()
    across.wait()
    for load in mine_loads:
        load.wait()
    add_up(spare)
    mine_store.start()
    for part in range(2):
        relay[part].wait()
    for array in arrays:
        array.wait()
    d_rows = d_all[...].reshape(tokens, width)
    for head in range(2):
        columns = slice(head * HD, head * HD + HD)
        made = dot_nt(d_rows, rows_ref[2, columns]).astype(bfloat)
        d_out[head] = made
        row_dot = jnp.sum(
            made.astype(single) * attended_ref[:, columns].astype(single), axis=-1, keepdims=True
        )
        delta[head] = jnp.broadcast_to(row_dot, delta.shape[1:])

    def place(slot, head, start):
        deep = 2 * head + core if slot == 1 else 2 * core + head
        for unit in range(4):
            source = out_rows.at[slot, head, pl.ds(unit * share, share)]
            owner = deep * pairs + unit // 2
            target = out_parts.at[owner] if slot == 2 else parts.at[slot, owner]
            sem = place_sem.at[slot, head, unit]

            def here():
                return pltpu.make_async_copy(source, target, sem)

            def there():
                return remote(source, target, sem, peer_sem.at[slot, head, unit], to_core)

            @pl.when(core == unit % 2)
            def _():
                if start:
                    here().start()
                else:
                    here().wait()
                    there().wait_recv()

            @pl.when(core != unit % 2)
            def _():
                if start:
                    there().start()
                else:
                    there().wait_send()

    def term(slot, head, left, right):
        out_rows[slot, head] = dot_tn(left, right).astype(bfloat)
        place(slot, head, True)

    def block(way, owner):
        key = keyval_ref[owner, 0, way * half : way * half + half]
        val = keyval_ref[owner, 1, way * half : way * half + half]
        row = lax.broadcasted_iota(jnp.int32, (tokens, half), 0)
        column = lax.broadcasted_iota(jnp.int32, (tokens, half), 1)
        allowed = row + (chip - owner) * tokens - way * half >= column

        def one_head(head, carried):
            bent = jnp.tanh(dot_nt(query_ref[head], key) * (scale / softcap))
            inverse = jnp.concatenate([inverse_ref[head]] * (half // 128), axis=1)
            row_dot = jnp.concatenate([delta[head]] * (half // 128), axis=1)
            probs = jnp.where(allowed, jnp.exp(softcap * bent), 0.0) * inverse
            d_probs = dot_nt(d_out[head], val)
            d_scores = (probs * (d_probs - row_dot) * (1.0 - bent * bent)).astype(bfloat)
            d_block[way, 0] += dot_tn(d_scores, query_ref[head]) * scale
            d_block[way, 1] += dot_tn(probs.astype(bfloat), d_out[head])
            d_query[head] += dot_nn(d_scores, key)
            return carried

        for head in range(2):
            one_head(head, 0)

    def key_copy(way, kind, step, first):
        return remote(
            first_put.at[way, kind] if first else held_keys.at[way, step - 1, kind],
            held_keys.at[way, step, kind],
            key_send.at[way, kind, step],
            key_recv.at[way, kind, step],
            {"fsdp": ring.right if way == 0 else ring.left},
        )

    streams = [(way, kind) for kind in range(2) for way in range(2)]

    early = 3

    def key_blocks(step):
        for way in range(2):
            owner = ring.owner(way, step + 1)
            d_block[way] = jnp.zeros(d_block.shape[1:], single)
            if way == 1:

                @pl.when((step >= early) & (step < chips - 1))
                def _():
                    out_ring.scatter_step(out_parts, out_held, step - early)

            @pl.when(owner <= chip)
            def _():
                block(way, owner)

    def key_body(step, carried):
        key_blocks(step)
        for way, kind in streams:

            @pl.when(step == 0)
            def _():
                first_put[way, kind] = d_block[way, kind].astype(bfloat)
                key_copy(way, kind, 0, True).start()

            @pl.when(step > 0)
            def _():
                key_copy(way, kind, step - 1, True).wait_recv()
                summed = held_keys[way, step - 1, kind].astype(single) + d_block[way, kind]
                held_keys[way, step - 1, kind] = summed.astype(bfloat)
                key_copy(way, kind, step, False).start()

        @pl.when(step == 0)
        def _():
            for head in range(2):
                left = attended_ref[:, head * HD : head * HD + HD]
                term(2, head, left, d_all[...].reshape(tokens, width))

        @pl.when(step == early - 1)
        def _():
            key_blocks(chips - 1)
            for way in range(2):
                for kind in range(2):
                    rows = slice(way * half, way * half + half)
                    swapped[2 + kind, rows] = d_block[way, kind].astype(bfloat)
            for head in range(2):
                place(2, head, False)

        return carried

    lax.fori_loop(0, chips - 1, key_body, 0)
    mine_store.wait()

    normed = normed_ref[...].reshape(tokens, width)
    for way in range(2):
        rows = slice(way * half, way * half + half)
        for kind in range(2):
            key_copy(way, kind, chips - 2, True).wait_recv()
            summed = held_keys[way, chips - 2, kind].astype(single)
            summed = summed + swapped[2 + kind, rows].astype(single)
            swapped[2 + kind, rows] = summed.astype(bfloat)
    swap = quad_copy(swapped.at[3 - side], swapped.at[side], 5, to_side)
    swap.start()
    out_ring.scatter_step(out_parts, out_held, chips - 4)
    for head in range(2):
        turned = turn(d_query[head] * scale, cosine_ref[...], -sine_ref[...])
        d_raw[head] = turned.astype(bfloat)
        term(0, head, d_raw[head], normed)
    out_ring.scatter_step(out_parts, out_held, chips - 3)
    for head in range(2):
        place(0, head, False)
    rings[0].scatter_step(parts.at[0], held.at[0], 0)
    swap.wait()
    bulk(2).start()
    swapped[side] = swapped[2 + side]
    for head in range(2):
        turned = turn(swapped[head].astype(single), key_cosine_ref[...], -key_sine_ref[...])
        d_raw[2 + head] = turned.astype(bfloat)
        term(1, head, d_raw[2 + head], normed)
    out_ring.scatter_step(out_parts, out_held, chips - 2)
    rings[0].scatter_step(parts.at[0], held.at[0], 1)
    span = width // 3

    def d_input(tile, carried):
        columns = pl.ds(pl.multiple_of(tile * span, span), span)
        made = dot_nn(d_raw[0], rows_ref[0, 0:HD, columns])
        made = made + dot_nn(d_raw[1], rows_ref[0, HD:, columns])
        made = made + dot_nn(d_raw[2], rows_ref[1, 0:HD, columns])
        made = made + dot_nn(d_raw[3], rows_ref[1, HD:, columns])
        out_rows[0, :, :, columns] = made.reshape(2, half, span).astype(bfloat)
        return carried

    for head in range(2):
        place(1, head, False)
    rings[1].scatter_step(parts.at[1], held.at[1], 0)
    lax.fori_loop(0, 3, d_input, 0)
    across = quad_copy(out_rows.at[0, 1 - core], across_got, 6, to_core)
    mine = pl.ds(pl.multiple_of(side * (half // 2), half // 2), half // 2)
    other = pl.ds(pl.multiple_of((1 - side) * (half // 2), half // 2), half // 2)
    along = quad_copy(along_put, along_got, 7, to_side)
    across.start()

    def body(step, carried):
        rings[1].scatter_step(parts.at[1], held.at[1], step)

        @pl.when(step < chips - 2)
        def _():
            rings[0].scatter_step(parts.at[0], held.at[0], step + 1)

        @pl.when(step == 1)
        def _():
            across.wait()
            given = out_rows[0, core, other].astype(single) + across_got[other].astype(single)
            along_put[...] = given.astype(bfloat)
            along.start()
            tokens_ref[...] = out_rows[0, core, mine].astype(single) + across_got[mine].astype(single)

        @pl.when(step == 4)
        def _():
            along.wait()
            tokens_ref[...] = tokens_ref[...] + along_got[...].astype(single)
            d_norm, d_gain = norm_back(resid_ref[...], scales_ref[0:1], tokens_ref[...])
            tokens_ref[...] = d_mid_ref[...] + d_norm
            value[0] = gains_ref[...]
            value[0, 0:1] = d_gain
            gains_total.start()

        @pl.when(step == 5)
        def _():
            gains_total.over_cores()

        @pl.when(step == 6)
        def _():
            gains_total.over_ring()

        return carried

    lax.fori_loop(1, chips - 1, body, 0)
    total_ref[...] = gains_total.end()
    out_ring.scatter_end(out_parts, out_held, sum_ref.at[pl.ds(2 * share, share)])
    for slot in range(2):
        rows = pl.ds(slot * share, share)
        rings[slot].scatter_end(parts.at[slot], held.at[slot], sum_ref.at[rows])
        rings[slot].finish(out_held.at[0, 0, 0 : ring.size])
    out_ring.finish(out_held.at[0, 0, 0 : out_ring.size])

    def settle(step, carried):
        for way, kind in streams:
            key_copy(way, kind, step, True).wait_send()
        return carried

    lax.fori_loop(0, chips - 1, settle, 0)
    for kind in range(3):
        bulk(kind).wait()


def tail(
    d_proj, query, keyval, attended, inverse, rows, normed, turns, locals_, own, other, chips, ident
):
    tokens = query.shape[1]
    tok_rows = tokens // 4
    width = rows.shape[2]
    share = tokens // 8
    half = tokens // 2
    vmem = pl.BlockSpec(memory_space=pltpu.VMEM)
    anywhere = pl.BlockSpec(memory_space=pl.ANY)
    return pl.pallas_call(
        functools.partial(tail_kernel, chips),
        out_shape=(
            jax.ShapeDtypeStruct((3 * share, width), single),
            jax.ShapeDtypeStruct((tok_rows, width), single),
            jax.ShapeDtypeStruct((4, width), single),
            jax.ShapeDtypeStruct(own.shape[1:], bfloat),
            jax.ShapeDtypeStruct(own.shape[1:], bfloat),
            jax.ShapeDtypeStruct(own.shape[1:], bfloat),
        ),
        in_specs=[vmem] * 2
        + [anywhere, vmem, vmem, anywhere, anywhere]
        + [vmem] * 8
        + [anywhere] * 2,
        out_specs=(vmem,) * 3 + (anywhere,) * 3,
        scratch_shapes=[
            pltpu.VMEM(keyval.shape, bfloat),
            pltpu.VMEM(rows.shape, bfloat),
            pltpu.VMEM(normed.shape, bfloat),
            pltpu.VMEM((2, 2, tok_rows, width), bfloat),
            pltpu.VMEM((2, tokens, HD), bfloat),
            pltpu.VMEM((2, tokens, 128), single),
            pltpu.VMEM((2, tokens, HD), single),
            pltpu.VMEM((2, 2, half, HD), single),
            pltpu.VMEM((2, 2, half, HD), bfloat),
            pltpu.VMEM((2, chips - 1, 2, half, HD), bfloat),
            pltpu.VMEM((4, tokens, HD), bfloat),
            pltpu.VMEM((4, tokens, HD), bfloat),
            pltpu.VMEM((3, 2, HD, width), bfloat),
            pltpu.VMEM((2, chips, share, width), bfloat),
            pltpu.VMEM((chips, share, width), bfloat),
            pltpu.VMEM((2, 2, chips - 1, share // 2, width), bfloat),
            pltpu.VMEM((2, chips - 1, share // 2, width), bfloat),
            pltpu.VMEM((2 * tok_rows, width), bfloat),
            pltpu.VMEM((tok_rows, width), bfloat),
            pltpu.VMEM((tok_rows, width), bfloat),
        ]
        + total_scratch(chips, width)
        + [
            pltpu.SemaphoreType.DMA((2, 2, chips - 1)),
            pltpu.SemaphoreType.DMA((2, 2, chips - 1)),
            pltpu.SemaphoreType.DMA((3, 2, 4)),
            pltpu.SemaphoreType.DMA((3, 2, 4)),
            pltpu.SemaphoreType.DMA((2, 2, 1, chips - 1)),
            pltpu.SemaphoreType.DMA((2, 2, 1, chips - 1)),
            pltpu.SemaphoreType.DMA((2, 1, chips - 1)),
            pltpu.SemaphoreType.DMA((2, 1, chips - 1)),
            pltpu.SemaphoreType.DMA((8,)),
            pltpu.SemaphoreType.DMA((8,)),
            pltpu.SemaphoreType.DMA((10,)),
            pltpu.SemaphoreType.DMA((3,)),
            pltpu.SemaphoreType.DMA((3,)),
        ],
        compiler_params=pltpu.CompilerParams(
            collective_id=ident, has_side_effects=True, vmem_limit_bytes=63 * 2**20
        ),
        cost_estimate=cost(160),
    )(d_proj, query, keyval, attended, inverse, rows, normed, *turns, *locals_, own, other)


def feed_kernel(
    chips,
    pieces,
    resid_ref,
    projected_ref,
    dy_ref,
    scales_ref,
    own_ref,
    side_ref,
    core_ref,
    diag_ref,
    result_ref,
    d_mid_ref,
    d_projected_ref,
    d_gains_ref,
    terms_ref,
    other_ref,
    weights,
    x_all,
    y_all,
    mid,
    both,
    hidden,
    part,
    held,
    chunk,
    wide,
    stage,
    load_sem,
    bulk_send,
    bulk_recv,
    stage_sem,
    other_sem,
    send_sem,
    recv_sem,
):
    tok_rows, width = resid_ref.shape
    units = own_ref.shape[0] // 3
    whole = 4 * units
    half = tok_rows // 2
    rings = [
        Ring(chips, pieces, tok_rows, send_sem.at[phase], recv_sem.at[phase]) for phase in range(4)
    ]
    chip = rings[0].chip
    loads = []
    for slot, ref in enumerate((own_ref, side_ref, core_ref, diag_ref)):
        for kind in range(3 if slot % 2 == 0 else 2):
            loads.append(
                pltpu.make_async_copy(
                    ref.at[pl.ds(kind * units, units)],
                    weights.at[pl.ds(kind * whole + slot * units, units)],
                    load_sem.at[slot, kind],
                )
            )
    for load in loads:
        load.start()
    mid[...] = resid_ref[...] + norm_scale(projected_ref[...], scales_ref[1:2])
    x_all[chip] = norm_scale(mid[...], scales_ref[2:3]).astype(bfloat)
    core = lax.axis_index("fsdp") % 2
    to_core = {"fsdp": 2 * chip + 1 - core}
    to_side = {"head": 1 - lax.axis_index("head")}
    quad_barrier(to_side, to_core, rings[0].right, rings[0].left)
    down_rows = [pl.ds(2 * whole + slot * units, units) for slot in range(4)]
    bulk_side = remote(
        own_ref.at[pl.ds(2 * units, units)],
        weights.at[down_rows[1]],
        bulk_send.at[0],
        bulk_recv.at[0],
        to_side,
    )
    bulk_diag = remote(
        weights.at[down_rows[1]],
        weights.at[down_rows[3]],
        bulk_send.at[1],
        bulk_recv.at[1],
        to_core,
    )
    bulk_side.start()
    span = width // 3

    def segments(pair):
        for hop in range(2):
            for way in range(2):
                start = hop * tok_rows + way * half
                owner = rings[0].owner(way, 2 * pair + hop)
                yield owner, pl.ds(way * half, half), pl.ds(start, half)

    def fetch(all_ref, pair):
        for owner, rows, here in segments(pair):
            chunk[here] = all_ref[owner, rows]

    def put(ref, pair, columns, value):
        for owner, rows, here in segments(pair):
            ref[owner, rows, columns] = value[here.start : here.start + half].astype(ref.dtype)

    def take(ref, pair, columns):
        return jnp.concatenate(
            [ref[owner, rows, columns] for owner, rows, here in segments(pair)], axis=0
        )

    def polls(ring, all_ref, pair):
        def poll(index):
            @pl.when(2 * pair + 2 < chips)
            def _():
                ring.gather_step(all_ref, 2 * pair + 2 + index // 2, index % 2)

        return poll

    def down(pair):
        chunk[:, 0:whole] = take(hidden, pair, slice(None))

        def columns_of(tile, carried):
            columns = pl.ds(pl.multiple_of(tile * span, span), span)
            put(part, pair, columns, dot_nn(chunk[:, 0:whole], weights[2 * whole :, columns]))
            return carried

        lax.fori_loop(0, 3, columns_of, 0)

    def gate_up(tile):
        rows = slice(tile * span, tile * span + span)
        wide[:, rows] = dot_nt(chunk[...], weights[rows])

    def unit(pair):
        put(both, pair, slice(None), wide[...])
        value, slope = gelu_parts(wide[:, 0:whole])
        put(hidden, pair, slice(None), value * wide[:, whole:])

    last = chips // 2 - 1

    def forward(pair, carried):
        poll = polls(rings[0], x_all, pair)
        fetch(x_all, pair)
        for tile in range(3):
            gate_up(tile)
            poll(tile)
        unit(pair)

        @pl.when(pair == last - 1)
        def _():
            bulk_side.wait_recv()
            bulk_diag.start()
            bulk_diag.wait_recv()
            down(0)

        poll(3)
        return carried

    for step in range(2):
        for piece in range(pieces):
            rings[0].gather_step(x_all, step, piece)
        if step == 0:
            for load in loads:
                load.wait()
    lax.fori_loop(0, last, forward, 0)
    rings[1].scatter_step(part, held, 0)
    down(1)
    fetch(x_all, last)
    gate_up(0)
    rings[1].scatter_step(part, held, 1)
    gate_up(1)
    gate_up(2)
    unit(last)

    def spread(step, carried):
        rings[1].scatter_step(part, held, step, 0)

        @pl.when((step % 2 == 0) & (step < chips - 2))
        def _():
            down(step // 2 + 1)

        rings[1].scatter_step(part, held, step, 1)
        return carried

    lax.fori_loop(2, chips - 1, spread, 0)
    ours = pl.ds(0, tok_rows)
    rings[1].scatter_end(part, held, wide)
    result_ref[...] = mid[...] + norm_scale(wide[ours], scales_ref[3:4])
    d_ffn, d_gain = norm_back(wide[ours], scales_ref[3:4], dy_ref[...])
    d_gains_ref[0:1] = jnp.zeros_like(d_gain)
    d_gains_ref[3:4] = d_gain
    y_all[chip] = d_ffn.astype(bfloat)
    rings[0].finish(x_all.at[0, 0 : rings[0].size])
    rings[1].finish(x_all.at[0, 0 : rings[0].size])
    bulk_side.wait_send()
    bulk_diag.wait_send()

    def d_input(pair):
        chunk[...] = take(both, pair, slice(None))

        def columns_of(tile, carried):
            columns = pl.ds(pl.multiple_of(tile * span, span), span)
            put(part, pair, columns, dot_nn(chunk[...], weights[0 : 2 * whole, columns]))
            return carried

        lax.fori_loop(0, 3, columns_of, 0)

    third = whole // 3

    def d_units(pair, tile):
        columns = slice(tile * third, tile * third + third)
        ups = slice(whole + tile * third, whole + tile * third + third)
        for owner, rows, here in segments(pair):
            value, slope = gelu_parts(both[owner, rows, columns].astype(single))
            upper = both[owner, rows, ups].astype(single)
            d_hidden = wide[here, columns]
            both[owner, rows, columns] = (d_hidden * upper * slope).astype(bfloat)
            both[owner, rows, ups] = (d_hidden * value).astype(bfloat)

    def d_hidden(first, end):
        wide[:, first:end] = dot_nt(chunk[...], weights[2 * whole + first : 2 * whole + end])

    def backward(pair, carried):
        poll = polls(rings[2], y_all, pair)
        fetch(y_all, pair)
        d_hidden(0, 2 * third)
        poll(0)
        d_hidden(2 * third, whole)
        d_units(pair, 0)
        poll(1)
        d_units(pair, 1)
        d_units(pair, 2)
        poll(2)

        @pl.when(pair < 2)
        def _():
            d_input(pair)

        poll(3)
        return carried

    for step in range(2):
        for piece in range(pieces):
            rings[2].gather_step(y_all, step, piece)
    lax.fori_loop(0, last, backward, 0)
    rings[3].scatter_step(part, held, 0)
    fetch(y_all, last)
    d_hidden(0, 2 * third)
    d_hidden(2 * third, whole)
    d_units(last, 0)
    rings[3].scatter_step(part, held, 1)
    d_units(last, 1)
    d_units(last, 2)
    rows_tile = stage.shape[1]
    tiles = 3 * whole // rows_tile
    upper_tiles = 2 * whole // rows_tile

    cut = units // 3

    def pieces_of(tile):
        for quarter in range(4):
            block = 4 * tile + quarter
            kind, slot, third = block // 12, (block // 3) % 4, block % 3
            source = stage.at[tile % 2, pl.ds(quarter * cut, cut)]
            rows = pl.ds(pl.multiple_of(kind * units + third * cut, cut), cut)
            sem = stage_sem.at[tile % 2, quarter]
            goal = terms_ref.at[slot, rows], other_ref.at[slot - 2, rows]
            there = functools.partial(
                remote, source, goal[1], sem, other_sem.at[tile, quarter], to_core
            )
            yield slot, functools.partial(pltpu.make_async_copy, source, goal[0], sem), there

    def keep(tile):
        for slot, here, there in pieces_of(tile):

            @pl.when(slot < 2)
            def _():
                here().start()

            @pl.when(slot >= 2)
            def _():
                there().start()

    def kept(tile):
        for slot, here, there in pieces_of(tile):

            @pl.when(slot < 2)
            def _():
                here().wait()

            @pl.when(slot >= 2)
            def _():
                there().wait_send()

    def grads(tile):
        @pl.when(tile >= 2)
        def _():
            kept(tile - 2)

        @pl.when(tile < upper_tiles)
        def _():
            columns = pl.ds(pl.multiple_of(tile * rows_tile, rows_tile), rows_tile)
            left = both[:, :, columns].reshape(chips * tok_rows, rows_tile)
            stage[tile % 2] = dot_tn(left, x_all[...].reshape(chips * tok_rows, width)).astype(bfloat)

        @pl.when(tile >= upper_tiles)
        def _():
            columns = pl.ds(
                pl.multiple_of((tile - upper_tiles) * rows_tile, rows_tile), rows_tile
            )
            left = hidden[:, :, columns].reshape(chips * tok_rows, rows_tile)
            stage[tile % 2] = dot_tn(left, y_all[...].reshape(chips * tok_rows, width)).astype(bfloat)

        keep(tile)

    d_input(2)

    def spread_back(step, carried):
        tile = 2 * (step - 3) + 2 * ((6 - step) // 4)
        rings[3].scatter_step(part, held, step, 0)

        @pl.when(step == 3)
        def _():
            d_input(3)

        @pl.when(step != 3)
        def _():
            grads(tile)

        rings[3].scatter_step(part, held, step, 1)

        @pl.when(step != 3)
        def _():
            grads(tile + 1)

        return carried

    lax.fori_loop(2, chips - 1, spread_back, 0)
    lax.fori_loop(8, tiles, lambda tile, carried: grads(tile) or carried, 0)
    rings[3].scatter_end(part, held, wide)
    d_norm, d_gain = norm_back(mid[...], scales_ref[2:3], wide[ours])
    d_gains_ref[2:3] = d_gain
    d_mid_ref[...] = dy_ref[...] + d_norm
    d_projected, d_gain = norm_back(projected_ref[...], scales_ref[1:2], d_mid_ref[...])
    d_gains_ref[1:2] = d_gain
    d_projected_ref[...] = d_projected.astype(bfloat)
    rings[2].finish(x_all.at[0, 0 : rings[0].size])
    rings[3].finish(x_all.at[0, 0 : rings[0].size])
    kept(tiles - 2)
    kept(tiles - 1)

    def gained(tile, carried):
        for slot, here, there in pieces_of(tile):

            @pl.when(slot >= 2)
            def _():
                there().wait_recv()

        return carried

    lax.fori_loop(0, tiles, gained, 0)


def feed_forward(resid_in, projected, grad_out, scales, shares, chips, ident):
    tok_rows, width = resid_in.shape
    units = shares[0].shape[0] // 3
    whole = 4 * units
    pieces = 2
    vmem = pl.BlockSpec(memory_space=pltpu.VMEM)
    anywhere = pl.BlockSpec(memory_space=pl.ANY)
    return pl.pallas_call(
        functools.partial(feed_kernel, chips, pieces),
        out_shape=(
            jax.ShapeDtypeStruct((tok_rows, width), single),
            jax.ShapeDtypeStruct((tok_rows, width), single),
            jax.ShapeDtypeStruct((tok_rows, width), bfloat),
            jax.ShapeDtypeStruct((4, width), single),
            jax.ShapeDtypeStruct((2, 3 * units, width), bfloat),
            jax.ShapeDtypeStruct((2, 3 * units, width), bfloat),
        ),
        in_specs=[vmem] * 4 + [anywhere] * 4,
        out_specs=(vmem, vmem, vmem, vmem, anywhere, anywhere),
        scratch_shapes=[
            pltpu.VMEM((3 * whole, width), bfloat),
            pltpu.VMEM((chips, tok_rows, width), bfloat),
            pltpu.VMEM((chips, tok_rows, width), bfloat),
            pltpu.VMEM((tok_rows, width), single),
            pltpu.VMEM((chips, tok_rows, 2 * whole), bfloat),
            pltpu.VMEM((chips, tok_rows, whole), bfloat),
            pltpu.VMEM((chips, tok_rows, width), bfloat),
            pltpu.VMEM((2, chips - 1, tok_rows // 2, width), bfloat),
            pltpu.VMEM((2 * tok_rows, width), bfloat),
            pltpu.VMEM((2 * tok_rows, width), single),
            pltpu.VMEM((2, whole // 3, width), bfloat),
            pltpu.SemaphoreType.DMA((4, 3)),
            pltpu.SemaphoreType.DMA((2,)),
            pltpu.SemaphoreType.DMA((2,)),
            pltpu.SemaphoreType.DMA((2, 4)),
            pltpu.SemaphoreType.DMA((9, 4)),
            pltpu.SemaphoreType.DMA((4, 2, pieces, chips - 1)),
            pltpu.SemaphoreType.DMA((4, 2, pieces, chips - 1)),
        ],
        compiler_params=pltpu.CompilerParams(
            collective_id=ident, has_side_effects=True, vmem_limit_bytes=63 * 2**20
        ),
        cost_estimate=cost(205),
    )(resid_in, projected, grad_out, scales, *shares)


def general_device(
    tokens,
    cotangent,
    gains,
    gains_first,
    gains_second,
    attn_weight,
    attn_first,
    attn_second,
    ffn_weight,
    ffn_first,
    ffn_second,
):
    devices = lax.axis_size("fsdp")
    chips = devices // 2
    side = lax.axis_index("head")
    place = lax.axis_index("fsdp")
    core, chip = place % 2, place // 2
    tok_rows = tokens.shape[1]
    super_rows = 4 * tok_rows
    seq_len = min(SEQ_LEN, super_rows * chips)
    share = attn_weight.shape[1]
    pairs = chips // 4
    width = tokens.shape[2]
    scale = 1.0 / math.sqrt(HD)

    def swap_core(value):
        return lax.ppermute(value, "fsdp", [(index, index ^ 1) for index in range(devices)])

    def swap_side(value):
        return lax.ppermute(value, "head", [(0, 1), (1, 0)])

    def in_order(own, other, index, axis):
        return jnp.where(
            index == 0, jnp.stack([own, other], axis), jnp.stack([other, own], axis)
        )

    def pick(value, index, axis=0):
        return lax.dynamic_index_in_dim(value, index, axis, keepdims=False)

    def quad_gather(value):
        value = in_order(value, swap_side(value), side, 0)
        value = in_order(value, swap_core(value), core, 0)
        return value.reshape((super_rows,) + value.shape[3:])

    def quad_scatter(partial):
        partial = partial.reshape(2, 2, tok_rows, width)
        mine = pick(partial, core) + swap_core(pick(partial, 1 - core).astype(bfloat)).astype(single)
        return pick(mine, side) + swap_side(pick(mine, 1 - side).astype(bfloat)).astype(single)

    scales = lax.all_gather(gains.astype(bfloat), ("head", "fsdp"), axis=1, tiled=True).astype(single)
    attn_low = attn_weight.astype(bfloat)
    ffn_low = ffn_weight.astype(bfloat).transpose(1, 0, 2)
    ffn_pair = jnp.concatenate([ffn_low, swap_side(ffn_low)], axis=1)

    ring_rows = ring_gather(attn_low.reshape(3 * share, width), chips, 0)
    ring_rows = ring_rows.reshape(2, 2, pairs, 3, share, width)

    def query_rows(slot):
        rows = ring_rows[:, :, :, slot]
        other = swap_core(pick(rows, 1 - core))
        return in_order(pick(rows, core), other, core, 2).reshape(2 * HD, width)

    def keyval_rows():
        rows = ring_rows[:, :, :, 1]
        other = swap_core(pick(rows, 1 - core, 1))
        return in_order(pick(rows, core, 1), other, core, 2).reshape(2 * HD, width)

    w_query, w_keyval, w_out = query_rows(0), keyval_rows(), query_rows(2)

    resid_in = tokens[0]
    grad_out = cotangent[0]
    normed_one = norm_scale(resid_in, scales[0]).astype(bfloat)
    normed_all = quad_gather(normed_one)
    positions = chip * super_rows + jnp.arange(super_rows, dtype=jnp.int32)
    angles = turn_angles(positions % seq_len, HD)
    query_raw = jnp.einsum("td,fd->tf", normed_all, w_query, preferred_element_type=single)
    keyval_raw = jnp.einsum("td,fd->tf", normed_all, w_keyval, preferred_element_type=single)
    query = rotate(query_raw.reshape(super_rows, 2, HD), angles, 1.0).astype(bfloat)
    key_angles = jnp.where(side == 0, angles, 0.0)
    keyval = rotate(keyval_raw.reshape(super_rows, 2, HD), key_angles, 1.0).astype(bfloat)
    keyval = in_order(pick(keyval, side, 1), swap_side(pick(keyval, 1 - side, 1)), side, 0)
    keyval_all = ring_gather(keyval.reshape(2 * super_rows, HD), chips, 1)
    keyval_all = keyval_all.reshape(chips, 2, super_rows, HD)
    key_all = keyval_all[:, 0].reshape(chips * super_rows, HD)
    value_all = keyval_all[:, 1].reshape(chips * super_rows, HD)

    key_pos = jnp.arange(chips * super_rows, dtype=jnp.int32)
    distance = positions[:, None] - key_pos[None, :]
    same_seq = (positions // seq_len)[:, None] == (key_pos // seq_len)[None, :]
    allowed = (distance >= 0) & (distance < WIN) & same_seq

    def score_block():
        raw = jnp.einsum("qgd,kd->gqk", query, key_all, preferred_element_type=single)
        bent = jnp.tanh(raw * (scale / softcap))
        return bent, jnp.where(allowed, jnp.exp(softcap * bent), 0.0)

    bent, powers = score_block()
    total = jnp.sum(powers, axis=-1, keepdims=True)
    attended = jnp.einsum(
        "gqk,kd->gqd", powers.astype(bfloat), value_all, preferred_element_type=single
    )
    attended = (attended / total).transpose(1, 0, 2).reshape(super_rows, 2 * HD).astype(bfloat)
    projected = quad_scatter(jnp.dot(attended, w_out, preferred_element_type=single))
    resid_mid = resid_in + norm_scale(projected, scales[1])
    normed_two = norm_scale(resid_mid, scales[2]).astype(bfloat)

    ffn_all = jnp.concatenate([ffn_pair, swap_core(ffn_pair)], axis=1)
    w_gate, w_up, w_down = ffn_all[0], ffn_all[1], ffn_all[2]
    ring_tokens = chips * tok_rows
    normed_ring = ring_gather(normed_two, chips, 2).reshape(ring_tokens, width)
    gate_part = jnp.einsum("td,rd->tr", normed_ring, w_gate, preferred_element_type=single)
    up_part = jnp.einsum("td,rd->tr", normed_ring, w_up, preferred_element_type=single)
    hidden = hidden_unit(gate_part, up_part).astype(bfloat)
    ffn_part = jnp.dot(hidden, w_down, preferred_element_type=single).astype(bfloat)
    ffn_acc = ring_scatter(ffn_part.reshape(chips, tok_rows, width), chips, 3)
    result = resid_mid + norm_scale(ffn_acc, scales[3])

    ignored, post_back = jax.vjp(norm_scale, ffn_acc, scales[3])
    d_ffn, d_gain3 = post_back(grad_out)
    d_ffn_ring = ring_gather(d_ffn.astype(bfloat), chips, 4).reshape(ring_tokens, width)
    d_hidden = jnp.einsum("td,rd->tr", d_ffn_ring, w_down, preferred_element_type=single)
    ignored, unit_back = jax.vjp(hidden_unit, gate_part, up_part)
    d_gate, d_up = unit_back(d_hidden)
    d_gate = d_gate.astype(bfloat)
    d_up = d_up.astype(bfloat)
    d_normed = jnp.dot(d_gate, w_gate, preferred_element_type=single)
    d_normed = (d_normed + jnp.dot(d_up, w_up, preferred_element_type=single)).astype(bfloat)
    d_normed_two = ring_scatter(d_normed.reshape(chips, tok_rows, width), chips, 5)

    def ffn_rows(left, right):
        return jnp.einsum("tr,td->rd", left, right, preferred_element_type=single)

    ffn_terms = jnp.stack(
        [ffn_rows(d_gate, normed_ring), ffn_rows(d_up, normed_ring), ffn_rows(hidden, d_ffn_ring)]
    )
    units = ffn_weight.shape[0]
    ffn_terms = ffn_terms.reshape(3, 2, 2, units, width)
    ffn_terms = ffn_terms[:, 0] + swap_core(ffn_terms[:, 1].astype(bfloat)).astype(single)
    grad_ffn = ffn_terms[:, 0] + swap_side(ffn_terms[:, 1].astype(bfloat)).astype(single)

    ignored, mid_back = jax.vjp(norm_scale, resid_mid, scales[2])
    d_mid_norm, d_gain2 = mid_back(d_normed_two)
    d_mid = grad_out + d_mid_norm
    ignored, proj_back = jax.vjp(norm_scale, projected, scales[1])
    d_projected, d_gain1 = proj_back(d_mid)
    d_proj_all = quad_gather(d_projected.astype(bfloat))
    d_attended = jnp.einsum("td,fd->tf", d_proj_all, w_out, preferred_element_type=single)
    d_attended = d_attended.astype(bfloat).reshape(super_rows, 2, HD)

    bent, powers = score_block()
    probs = powers / total
    d_probs = jnp.einsum("qgd,kd->gqk", d_attended, value_all, preferred_element_type=single)
    row_dot = jnp.sum(d_probs * probs, axis=-1, keepdims=True)
    d_raw = (probs * (d_probs - row_dot) * (1.0 - bent * bent)).astype(bfloat)
    d_query = jnp.einsum("gqk,kd->qgd", d_raw, key_all, preferred_element_type=single) * scale
    d_keys = jnp.einsum("gqk,qgd->kd", d_raw, query, preferred_element_type=single) * scale
    d_values = jnp.einsum(
        "gqk,qgd->kd", probs.astype(bfloat), d_attended, preferred_element_type=single
    )
    d_pieces = jnp.stack(
        [d_keys.reshape(chips, super_rows, HD), d_values.reshape(chips, super_rows, HD)], axis=1
    ).astype(bfloat)
    d_keyval = ring_scatter(d_pieces.reshape(chips, 2 * super_rows, HD), chips, 6)
    d_keyval = d_keyval.reshape(2, super_rows, HD).astype(bfloat)
    d_keyval = in_order(pick(d_keyval, side), swap_side(pick(d_keyval, 1 - side)), side, 1)
    d_query_raw = rotate(d_query, angles, -1.0).reshape(super_rows, 2 * HD).astype(bfloat)
    d_keyval_raw = rotate(d_keyval.astype(single), key_angles, -1.0)
    d_keyval_raw = d_keyval_raw.reshape(super_rows, 2 * HD).astype(bfloat)
    d_normed_one = jnp.dot(d_query_raw, w_query, preferred_element_type=single)
    d_normed_one = d_normed_one + jnp.dot(d_keyval_raw, w_keyval, preferred_element_type=single)
    d_normed_one = quad_scatter(d_normed_one)
    ignored, first_back = jax.vjp(norm_scale, resid_in, scales[0])
    d_in_norm, d_gain0 = first_back(d_normed_one)
    tokens_grad = d_mid + d_in_norm

    def attn_rows(left, right):
        rows = jnp.einsum("tf,td->fd", left, right, preferred_element_type=single).astype(bfloat)
        return rows.reshape(2, pairs, 2, share, width)

    term_query = attn_rows(d_query_raw, normed_all)
    term_keyval = attn_rows(d_keyval_raw, normed_all)
    term_out = attn_rows(attended, d_proj_all)

    def to_core(term, axis):
        return in_order(pick(term, core, 2), swap_core(pick(term, 1 - core, 2)), core, axis)

    terms = jnp.stack([to_core(term_query, 0), to_core(term_keyval, 1), to_core(term_out, 0)], axis=3)
    grad_attn = ring_scatter(terms.reshape(chips, 3 * share, width), chips, 7)
    grad_attn = grad_attn.reshape(3, share, width)
    term_gain = jnp.stack([d_gain0, d_gain1, d_gain2, d_gain3])
    grad_gain = lax.psum_scatter(term_gain, ("head", "fsdp"), scatter_dimension=1, tiled=True)

    gains_first_new, gains_second_new, gains_new = adamw(
        gains, gains_first, gains_second, grad_gain, rate_gain, 0.0
    )
    attn_first_new, attn_second_new, attn_weight_new = adamw(
        attn_weight, attn_first, attn_second, grad_attn, rate_matrix, decay_matrix
    )
    ffn_first_new, ffn_second_new, ffn_weight_new = adamw(
        ffn_weight, ffn_first, ffn_second, grad_ffn.transpose(1, 0, 2), rate_matrix, decay_matrix
    )
    return (
        result[None],
        tokens_grad[None],
        gains_first_new,
        gains_second_new,
        gains_new,
        attn_first_new,
        attn_second_new,
        attn_weight_new,
        ffn_first_new,
        ffn_second_new,
        ffn_weight_new,
    )


def step_kernel(
    tiles,
    weight_ref,
    first_ref,
    second_ref,
    own_ref,
    side_ref,
    weight_two_ref,
    first_two_ref,
    second_two_ref,
    grad_two_ref,
    first_out,
    second_out,
    weight_out,
    first_two_out,
    second_two_out,
    weight_two_out,
):
    index = pl.program_id(0)

    @pl.when(index < tiles)
    def _():
        grad = own_ref[...].astype(single) + side_ref[...].astype(single)
        first_out[...], second_out[...], weight_out[...] = adamw(
            weight_ref[...], first_ref[...], second_ref[...], grad, rate_matrix, decay_matrix
        )

    @pl.when(index >= tiles)
    def _():
        first_two_out[...], second_two_out[...], weight_two_out[...] = adamw(
            weight_two_ref[...],
            first_two_ref[...],
            second_two_ref[...],
            grad_two_ref[...],
            rate_matrix,
            decay_matrix,
        )


def step_weights(state, own, side, state_two, grad_two):
    rows, width = state[0].shape
    rows_two = grad_two.shape[0]
    size = 96
    tiles, tiles_two = rows // size, rows_two // size
    block = pl.BlockSpec((size, width), lambda index: (jnp.minimum(index, tiles - 1), 0))
    block_two = pl.BlockSpec((size, width), lambda index: (jnp.maximum(index - tiles, 0), 0))
    return pl.pallas_call(
        functools.partial(step_kernel, tiles),
        grid=(tiles + tiles_two,),
        out_shape=(jax.ShapeDtypeStruct((rows, width), single),) * 3
        + (jax.ShapeDtypeStruct((rows_two, width), single),) * 3,
        in_specs=[block] * 5 + [block_two] * 4,
        out_specs=(block,) * 3 + (block_two,) * 3,
        compiler_params=pltpu.CompilerParams(vmem_limit_bytes=62 * 2**20),
        cost_estimate=cost(20),
    )(*state, own, side, *state_two, grad_two)


def per_device(
    tokens,
    cotangent,
    gains,
    gains_first,
    gains_second,
    attn_weight,
    attn_first,
    attn_second,
    ffn_weight,
    ffn_first,
    ffn_second,
):
    devices = lax.axis_size("fsdp")
    chips = devices // 2
    side = lax.axis_index("head")
    place = lax.axis_index("fsdp")
    tok_rows = tokens.shape[1]
    share = attn_weight.shape[1]
    width = tokens.shape[2]
    gain_columns = gains.shape[1]
    gain_start = (side * devices + place) * gain_columns

    units = ffn_weight.shape[0]

    def flat(value):
        return value.transpose(1, 0, 2).reshape(3 * units, width)

    ffn_wide = flat(ffn_weight)
    resid_in = tokens[0]
    grad_out = cotangent[0]
    gains_placed = lax.dynamic_update_slice(
        jnp.zeros((4, width), single), gains, (0, gain_start)
    )
    halfway = HD // 2
    pace = jnp.asarray(
        10000.0 ** (-2.0 * np.arange(halfway, dtype=np.float64) / HD)[None, :], dtype=single
    )
    made = front(attn_weight, gains_placed, resid_in, pace, ffn_wide, chips, 0)
    attn_rows, scales, normed_all, query, keyval, attended, inverse, projected = made[:8]
    turns = made[8:12]
    own_units, core_units, side_units, diag_units = made[12:]
    result, d_mid, d_proj_low, gain_rows, terms_own, terms_other = feed_forward(
        resid_in,
        projected,
        grad_out,
        scales,
        (own_units, side_units, core_units, diag_units),
        chips,
        1,
    )
    grad_attn, tokens_grad, gain_total, terms_sent, terms_side, terms_mine = tail(
        d_proj_low,
        query,
        keyval,
        attended,
        inverse,
        attn_rows,
        normed_all,
        turns,
        (resid_in, d_mid, scales, gain_rows),
        terms_own,
        terms_other,
        chips,
        2,
    )
    grad_gain = lax.dynamic_slice(gain_total, (0, gain_start), gains.shape)

    gains_first_new, gains_second_new, gains_new = adamw(
        gains, gains_first, gains_second, grad_gain, rate_gain, 0.0
    )
    def rows_of(value):
        return value.reshape(3 * share, width)

    stepped = step_weights(
        (ffn_wide, flat(ffn_first), flat(ffn_second)),
        terms_mine,
        terms_side,
        (rows_of(attn_weight), rows_of(attn_first), rows_of(attn_second)),
        grad_attn,
    )
    ffn_first_new, ffn_second_new, ffn_weight_new = (
        value.reshape(3, units, width).transpose(1, 0, 2) for value in stepped[:3]
    )
    attn_first_new, attn_second_new, attn_weight_new = (
        value.reshape(3, share, width) for value in stepped[3:]
    )
    return (
        result[None],
        tokens_grad[None],
        gains_first_new,
        gains_second_new,
        gains_new,
        attn_first_new,
        attn_second_new,
        attn_weight_new,
        ffn_first_new,
        ffn_second_new,
        ffn_weight_new,
    )


def solution(mesh):
    by_token = P("fsdp", "head", None)
    by_column = P(None, ("head", "fsdp"))
    by_row = P(None, ("head", "fsdp"), None)
    by_unit = P(("head", "fsdp"), None, None)
    placed = (by_token,) * 2 + (by_column,) * 3 + (by_row,) * 3 + (by_unit,) * 3
    body = per_device if mesh.shape["fsdp"] == 16 else general_device
    return jax.shard_map(
        body, mesh=mesh, in_specs=placed, out_specs=placed, check_vma=False
    )
```

```python
import functools
import math

import jax
import jax.numpy as jnp
import numpy as np
from jax import lax
from jax.experimental import pallas as pl
from jax.experimental.pallas import tpu as pltpu
from jax.sharding import PartitionSpec as P

HQ = 8
HK = 4
HD = 256
WIN = 4096
STEP = 10
SEQ_LEN = 8192


eps_norm = 1e-06
softcap = 50.0
beta_one = 0.9
beta_two = 0.95
adam_eps = 1e-08
rate_matrix = 0.02
rate_gain = 0.2
decay_matrix = 0.1

bfloat = jnp.bfloat16
single = jnp.float32
MESH = pl.DeviceIdType.MESH


def norm_scale(values, scales):
    return (
        values
        * lax.rsqrt(jnp.mean(values * values, axis=-1, keepdims=True) + eps_norm)
        * (1.0 + scales)
    )


def turn_angles(positions, head_width):
    halfway = head_width // 2
    inverse_freq = 10000.0 ** (-(jnp.arange(halfway, dtype=jnp.float32) * 2.0) / head_width)
    return positions.astype(jnp.float32)[:, None] * inverse_freq[None, :]


def rotate(values, angles, direction):
    halfway = values.shape[-1] // 2
    cosine = jnp.cos(angles)[:, None, :]
    sine_part = direction * jnp.sin(angles)[:, None, :]
    former = values[..., :halfway]
    latter = values[..., halfway:]
    return jnp.concatenate(
        [former * cosine - latter * sine_part, latter * cosine + former * sine_part], axis=-1
    )


def adamw(weight, moment, second, gradient, step_rate, decay_rate):
    moment = beta_one * moment + (1.0 - beta_one) * gradient
    second = beta_two * second + (1.0 - beta_two) * gradient * gradient
    update = (
        moment / (1.0 - beta_one**STEP) / (jnp.sqrt(second / (1.0 - beta_two**STEP)) + adam_eps)
        + decay_rate * weight
    )
    return (moment, second, weight - step_rate * update)


def hidden_unit(gate_part, up_part):
    return jax.nn.gelu(gate_part, approximate=True) * up_part


def ring_of(chip, chips):
    wide = chips // 4
    deep, side = chip // wide, chip % wide
    return side * 4 + deep + (side % 2) * (3 - 2 * deep)


def chip_of(ring, chips):
    wide = chips // 4
    side, along = ring // 4, ring % 4
    return (along + (side % 2) * (3 - 2 * along)) * wide + side


def ring_places(chips):
    index = lax.axis_index("fsdp")
    core, chip = index % 2, index // 2
    ring = ring_of(chip, chips)
    right = 2 * chip_of((ring + 1) % chips, chips) + core
    left = 2 * chip_of((ring + chips - 1) % chips, chips) + core
    return chip, ring, right, left


def ring_barrier(right, left):
    barrier = pltpu.get_barrier_semaphore()
    for neighbour in (left, right):
        pl.semaphore_signal(barrier, inc=1, device_id={"fsdp": neighbour}, device_id_type=MESH)
    pl.semaphore_wait(barrier, 2)


def region(shape, pieces, way, piece):
    rows, columns = shape
    if rows % 32 == 0:
        size = rows // 2 // pieces
        start = way * (rows // 2) + piece * size
        return (pl.ds(start, size), pl.ds(0, columns)), (pl.ds(piece * size, size), pl.ds(0, columns))
    size = columns // 2
    return (pl.ds(0, rows), pl.ds(way * size, size)), (pl.ds(0, rows), pl.ds(0, size))


def half_shape(rows, columns):
    return (rows // 2, columns) if rows % 32 == 0 else (rows, columns // 2)


def gather_kernel(chips, pieces, own_ref, all_ref, local_sem, send_sem, recv_sem):
    chip, ring, right, left = ring_places(chips)
    ring_barrier(right, left)
    keep = pltpu.make_async_copy(own_ref, all_ref.at[chip], local_sem)
    keep.start()

    def copy(way, step, piece, first):
        owner = chip_of((ring + (chips - step if way == 0 else step)) % chips, chips)
        part, ignored = region(own_ref.shape, pieces, way, piece)
        there = all_ref.at[(owner,) + part]
        return pltpu.make_async_remote_copy(
            src_ref=own_ref.at[part] if first else there,
            dst_ref=there,
            send_sem=send_sem.at[way, piece, step],
            recv_sem=recv_sem.at[way, piece, step],
            device_id={"fsdp": right if way == 0 else left},
            device_id_type=MESH,
        )

    streams = [(way, piece) for piece in range(pieces) for way in range(2)]
    for way, piece in streams:
        copy(way, 0, piece, True).start()

    def body(step, carried):
        for way, piece in streams:
            copy(way, step - 1, piece, False).wait_recv()
            copy(way, step, piece, False).start()
        return carried

    lax.fori_loop(1, chips - 1, body, 0)
    for way, piece in streams:
        copy(way, chips - 2, piece, False).wait_recv()

    def finish(step, carried):
        for way, piece in streams:
            copy(way, step, piece, False).wait_send()
        return carried

    lax.fori_loop(0, chips - 1, finish, 0)
    keep.wait()


def ring_gather(own, chips, ident):
    rows, columns = own.shape
    pieces = 2 if rows % 64 == 0 else 1
    return pl.pallas_call(
        functools.partial(gather_kernel, chips, pieces),
        out_shape=jax.ShapeDtypeStruct((chips, rows, columns), own.dtype),
        in_specs=[pl.BlockSpec(memory_space=pl.ANY)],
        out_specs=pl.BlockSpec(memory_space=pl.ANY),
        scratch_shapes=[
            pltpu.SemaphoreType.DMA,
            pltpu.SemaphoreType.DMA((2, pieces, chips - 1)),
            pltpu.SemaphoreType.DMA((2, pieces, chips - 1)),
        ],
        compiler_params=pltpu.CompilerParams(collective_id=ident, has_side_effects=True),
        cost_estimate=cost(45),
    )(own)


def scatter_kernel(chips, pieces, parts_ref, sum_ref, held, send_sem, recv_sem):
    chip, ring, right, left = ring_places(chips)
    ring_barrier(right, left)

    def owner_of(way, step):
        shift = chips - 1 - step if way == 0 else 1 + step
        return chip_of((ring + shift) % chips, chips)

    def copy(way, step, piece, first):
        part, place = region(sum_ref.shape, pieces, way, piece)
        return pltpu.make_async_remote_copy(
            src_ref=(
                parts_ref.at[(owner_of(way, step),) + part]
                if first
                else held.at[(way, step - 1) + place]
            ),
            dst_ref=held.at[(way, step) + place],
            send_sem=send_sem.at[way, piece, step],
            recv_sem=recv_sem.at[way, piece, step],
            device_id={"fsdp": right if way == 0 else left},
            device_id_type=MESH,
        )

    streams = [(way, piece) for piece in range(pieces) for way in range(2)]
    for way, piece in streams:
        copy(way, 0, piece, True).start()

    def arrived(way, step, piece):
        copy(way, step, piece, True).wait_recv()
        part, place = region(sum_ref.shape, pieces, way, piece)
        here = parts_ref[(owner_of(way, step + 1),) + part]
        return held[(way, step) + place].astype(single) + here.astype(single)

    def body(step, carried):
        for way, piece in streams:
            total = arrived(way, step - 1, piece)
            part, place = region(sum_ref.shape, pieces, way, piece)
            held[(way, step - 1) + place] = total.astype(held.dtype)
            copy(way, step, piece, False).start()
        return carried

    lax.fori_loop(1, chips - 1, body, 0)
    for way, piece in streams:
        part, place = region(sum_ref.shape, pieces, way, piece)
        sum_ref[part] = arrived(way, chips - 2, piece)

    def finish(step, carried):
        for way, piece in streams:
            copy(way, step, piece, True).wait_send()
        return carried

    lax.fori_loop(0, chips - 1, finish, 0)


def ring_scatter(parts, chips, ident):
    rows, columns = parts.shape[1:]
    pieces = 2 if rows % 64 == 0 else 1
    return pl.pallas_call(
        functools.partial(scatter_kernel, chips, pieces),
        out_shape=jax.ShapeDtypeStruct((rows, columns), single),
        in_specs=[pl.BlockSpec(memory_space=pltpu.VMEM)],
        out_specs=pl.BlockSpec(memory_space=pltpu.VMEM),
        scratch_shapes=[
            pltpu.VMEM((2, chips - 1) + half_shape(rows, columns), parts.dtype),
            pltpu.SemaphoreType.DMA((2, pieces, chips - 1)),
            pltpu.SemaphoreType.DMA((2, pieces, chips - 1)),
        ],
        compiler_params=pltpu.CompilerParams(
            collective_id=ident, has_side_effects=True, vmem_limit_bytes=56 * 2**20
        ),
        cost_estimate=cost(45),
    )(parts)


def norm_back(values, scales, grad):
    inverse = lax.rsqrt(jnp.mean(values * values, axis=-1, keepdims=True) + eps_norm)
    bent = grad * (1.0 + scales)
    slope = jnp.mean(bent * values, axis=-1, keepdims=True) * (inverse * inverse * inverse)
    return bent * inverse - values * slope, jnp.sum(grad * values * inverse, axis=0, keepdims=True)


def gelu_parts(gate):
    root = math.sqrt(2.0 / math.pi)
    square = gate * gate
    bend = jnp.tanh(root * gate * (1.0 + 0.044715 * square))
    half = 0.5 * (1.0 + bend)
    slope = half + 0.5 * gate * (1.0 - bend * bend) * (root * (1.0 + 3.0 * 0.044715 * square))
    return gate * half, slope


def dot_nt(left, right):
    return lax.dot_general(left, right, (((1,), (1,)), ((), ())), preferred_element_type=single)


def dot_nn(left, right):
    return lax.dot_general(left, right, (((1,), (0,)), ((), ())), preferred_element_type=single)


def dot_tn(left, right):
    return lax.dot_general(left, right, (((0,), (0,)), ((), ())), preferred_element_type=single)


class Ring:
    def __init__(self, chips, pieces, rows, send_sem, recv_sem):
        self.chips, self.pieces, self.half = chips, pieces, rows // 2
        self.size = rows // 2 // pieces
        self.chip, self.ring, self.right, self.left = ring_places(chips)
        self.send_sem, self.recv_sem = send_sem, recv_sem
        self.streams = [(way, piece) for piece in range(pieces) for way in range(2)]

    def owner(self, way, step):
        shift = self.chips - step if way == 0 else step
        return chip_of((self.ring + shift) % self.chips, self.chips)

    def copy(self, source, target, way, piece, step):
        return pltpu.make_async_remote_copy(
            src_ref=source,
            dst_ref=target,
            send_sem=self.send_sem.at[way, piece, step],
            recv_sem=self.recv_sem.at[way, piece, step],
            device_id={"fsdp": self.right if way == 0 else self.left},
            device_id_type=MESH,
        )

    def part(self, way, piece):
        return pl.ds(way * self.half + piece * self.size, self.size)

    def place(self, piece):
        return pl.ds(piece * self.size, self.size)

    def gather_copy(self, all_ref, way, piece, step):
        there = all_ref.at[self.owner(way, step), self.part(way, piece)]
        return self.copy(there, there, way, piece, step)

    def of(self, only):
        return [(way, piece) for way, piece in self.streams if only is None or piece == only]

    def gather_step(self, all_ref, step, only=None):
        for way, piece in self.of(only):

            @pl.when(step > 0)
            def _():
                self.gather_copy(all_ref, way, piece, step - 1).wait_recv()

            @pl.when(step < self.chips - 1)
            def _():
                self.gather_copy(all_ref, way, piece, step).start()

    def scatter_copy(self, parts_ref, held, way, piece, step, first):
        source = (
            parts_ref.at[self.owner(way, step + 1), self.part(way, piece)]
            if first
            else held.at[way, step - 1, self.place(piece)]
        )
        return self.copy(source, held.at[way, step, self.place(piece)], way, piece, step)

    def scatter_total(self, parts_ref, held, way, piece, step):
        self.scatter_copy(parts_ref, held, way, piece, step, True).wait_recv()
        here = parts_ref[self.owner(way, step + 2), self.part(way, piece)]
        return held[way, step, self.place(piece)].astype(single) + here.astype(single)

    def scatter_step(self, parts_ref, held, step, only=None):
        for way, piece in self.of(only):

            @pl.when(step == 0)
            def _():
                self.scatter_copy(parts_ref, held, way, piece, 0, True).start()

            @pl.when(step > 0)
            def _():
                total = self.scatter_total(parts_ref, held, way, piece, step - 1)
                held[way, step - 1, self.place(piece)] = total.astype(held.dtype)
                self.scatter_copy(parts_ref, held, way, piece, step, False).start()

    def scatter_end(self, parts_ref, held, sum_ref):
        for way, piece in self.streams:
            sum_ref[self.part(way, piece)] = self.scatter_total(
                parts_ref, held, way, piece, self.chips - 2
            )

    def finish(self, example):
        def body(step, carried):
            for way, piece in self.streams:
                self.copy(example, example, way, piece, step).wait_send()
            return carried

        lax.fori_loop(0, self.chips - 1, body, 0)


def quad_peers(chips):
    side = lax.axis_index("head")
    index = lax.axis_index("fsdp")
    chip, core = index // 2, index % 2
    ring = ring_of(chip, chips)
    around = [2 * chip_of((ring + hop) % chips, chips) + core for hop in range(1, chips)]
    return side, core, {"head": 1 - side}, {"fsdp": 2 * chip + 1 - core}, around


def wide_barrier(to_side, to_core, around):
    barrier = pltpu.get_barrier_semaphore()
    for target in [to_side, to_core] + [{"fsdp": other} for other in around]:
        pl.semaphore_signal(barrier, inc=1, device_id=target, device_id_type=MESH)
    pl.semaphore_wait(barrier, 2 + len(around))


def quad_barrier(to_side, to_core, right, left):
    barrier = pltpu.get_barrier_semaphore()
    for target in (to_side, to_core, {"fsdp": right}, {"fsdp": left}):
        pl.semaphore_signal(barrier, inc=1, device_id=target, device_id_type=MESH)
    pl.semaphore_wait(barrier, 4)


def remote(source, target, send_sem, recv_sem, device):
    return pltpu.make_async_remote_copy(
        src_ref=source,
        dst_ref=target,
        send_sem=send_sem,
        recv_sem=recv_sem,
        device_id=device,
        device_id_type=MESH,
    )


class Total:
    def __init__(self, value, near, blocks, send_sem, recv_sem, peers, chip):
        self.value, self.near, self.blocks = value, near, blocks
        self.send_sem, self.recv_sem = send_sem, recv_sem
        side, core, self.to_side, self.to_core, self.around = peers
        self.chip = chip
        self.first = remote(value.at[0], near.at[0], send_sem.at[0], recv_sem.at[0], self.to_side)
        self.second = remote(value.at[1], near.at[1], send_sem.at[1], recv_sem.at[1], self.to_core)

    def spread(self, hop):
        here = self.blocks.at[self.chip]
        return remote(
            here,
            here,
            self.send_sem.at[1 + hop],
            self.recv_sem.at[1 + hop],
            {"fsdp": self.around[hop - 1]},
        )

    def start(self):
        self.first.start()

    def over_cores(self):
        self.first.wait_recv()
        self.value[1] = self.value[0] + self.near[0]
        self.second.start()

    def over_ring(self):
        self.second.wait_recv()
        self.blocks[self.chip] = self.value[1] + self.near[1]
        for hop in range(1, len(self.around) + 1):
            self.spread(hop).start()

    def end(self):
        for hop in range(1, len(self.around) + 1):
            self.spread(hop).wait_recv()
        total = self.blocks[0]
        for other in range(1, len(self.around) + 1):
            total = total + self.blocks[other]
        self.first.wait_send()
        self.second.wait_send()
        for hop in range(1, len(self.around) + 1):
            self.spread(hop).wait_send()
        return total


def total_scratch(chips, width):
    return [
        pltpu.VMEM((2, 4, width), single),
        pltpu.VMEM((2, 4, width), single),
        pltpu.VMEM((chips, 4, width), single),
        pltpu.SemaphoreType.DMA((chips + 1,)),
        pltpu.SemaphoreType.DMA((chips + 1,)),
    ]


def turn(raw, cosine, sine):
    halfway = raw.shape[1] // 2
    former, latter = raw[:, :halfway], raw[:, halfway:]
    return jnp.concatenate(
        [former * cosine - latter * sine, latter * cosine + former * sine], axis=1
    )


def front_kernel(
    chips,
    cuts,
    own_ref,
    gains_ref,
    resid_ref,
    pace_ref,
    wide_units_ref,
    rows_out,
    scales_ref,
    normed_out,
    query_ref,
    keyval_out,
    attended_ref,
    inverse_ref,
    projected_ref,
    cosine_ref,
    sine_ref,
    key_cosine_ref,
    key_sine_ref,
    own_units_ref,
    core_units_ref,
    side_units_ref,
    diag_units_ref,
    rows_ref,
    normed_ref,
    keyval_ref,
    all_rows,
    both,
    total,
    sums,
    product,
    across_put,
    across_got,
    along_put,
    along_got,
    cast_in,
    cast_out,
    value,
    near,
    blocks,
    total_send,
    total_recv,
    send_sem,
    recv_sem,
    place_sem,
    peer_sem,
    key_send,
    key_recv,
    quad_send,
    quad_recv,
    cast_sem,
    out_sem,
    bulk_send,
    bulk_recv,
):
    share, width = own_ref.shape[1:]
    tok_rows = resid_ref.shape[0]
    tokens = 4 * tok_rows
    half = width // 2
    pairs = chips // 4
    scale = 1.0 / math.sqrt(HD)
    seq_len = min(SEQ_LEN, tokens * chips)
    chip, ring, right, left = ring_places(chips)
    peers = quad_peers(chips)
    side, core, to_side, to_core, around = peers
    cast_rows = cast_in.shape[1]
    casts = wide_units_ref.shape[0] // cast_rows

    def cast_load(tile):
        rows = pl.ds(tile * cast_rows, cast_rows)
        return pltpu.make_async_copy(
            wide_units_ref.at[rows], cast_in.at[tile % 2], cast_sem.at[0, tile % 2]
        )

    def cast_store(tile):
        rows = pl.ds(tile * cast_rows, cast_rows)
        return pltpu.make_async_copy(
            cast_out.at[tile % 2], own_units_ref.at[rows], cast_sem.at[1, tile % 2]
        )

    def cast(first, last):
        for tile in range(first, last):
            cast_load(tile).wait()
            if tile >= 3:
                cast_store(tile - 2).wait()
            cast_out[tile % 2] = cast_in[tile % 2].astype(bfloat)
            cast_store(tile).start()
            if tile + 2 < casts:
                cast_load(tile + 2).start()

    outs = [
        pltpu.make_async_copy(rows_ref.at[0:2], rows_out.at[0:2], out_sem.at[0]),
        pltpu.make_async_copy(rows_ref.at[2], rows_out.at[2], out_sem.at[1]),
        pltpu.make_async_copy(normed_ref, normed_out, out_sem.at[2]),
        pltpu.make_async_copy(keyval_ref, keyval_out, out_sem.at[3]),
    ]
    def tables():
        place_in = chip * tokens + lax.broadcasted_iota(jnp.int32, cosine_ref.shape, 0)
        angles = (place_in % seq_len).astype(single) * pace_ref[...]
        cosine_ref[...] = jnp.cos(angles)
        sine_ref[...] = jnp.sin(angles)
        key_cosine_ref[...] = jnp.where(side == 0, cosine_ref[...], 1.0)
        key_sine_ref[...] = jnp.where(side == 0, sine_ref[...], 0.0)

    cast_load(0).start()
    cast_load(1).start()
    all_rows[chip] = own_ref[...].astype(bfloat)
    value[0] = gains_ref[...].astype(bfloat).astype(single)
    wide_barrier(to_side, to_core, around)
    gains_total = Total(value, near, blocks, total_send, total_recv, peers, chip)
    gains_total.start()
    streams = [(way, slot) for slot in range(2) for way in range(2)]
    out_streams = [(way, 2) for way in range(2)]
    key_streams = [(way, kind) for kind in range(2) for way in range(2)]

    def owner_of(way, step):
        return chip_of((ring + (chips - step if way == 0 else step)) % chips, chips)

    def hop(way, slot, step):
        there = all_rows.at[owner_of(way, step), slot, :, pl.ds(way * half, half)]
        return remote(
            there,
            there,
            send_sem.at[way, slot, step],
            recv_sem.at[way, slot, step],
            {"fsdp": right if way == 0 else left},
        )

    def key_hop(way, kind, step):
        there = keyval_ref.at[owner_of(way, step), kind, pl.ds(way * (tokens // 2), tokens // 2)]
        return remote(
            there,
            there,
            key_send.at[way, kind, step],
            key_recv.at[way, kind, step],
            {"fsdp": right if way == 0 else left},
        )

    def goal(way, slot, step):
        owner = owner_of(way, step)
        deep = owner // pairs
        unit = (owner % pairs) * 2 + core
        taker, head = (deep % 2, deep // 2) if slot == 1 else (deep // 2, deep % 2)
        columns = pl.ds(way * half, half)
        source = all_rows.at[owner, slot, :, columns]
        start = pl.multiple_of(head * HD + unit * share, share)
        target = rows_ref.at[slot, pl.ds(start, share), columns]
        sem = place_sem.at[way, slot, step]

        def here():
            return pltpu.make_async_copy(source, target, sem)

        def there():
            return remote(source, target, sem, peer_sem.at[way, slot, step], to_core)

        return taker, here, there

    def place(way, slot, step):
        taker, here, there = goal(way, slot, step)

        @pl.when(taker == core)
        def _():
            here().start()

        @pl.when(taker != core)
        def _():
            there().start()

    def placed(way, slot, step):
        taker, here, there = goal(way, slot, step)

        @pl.when(taker == core)
        def _():
            here().wait()
            there().wait_recv()

        @pl.when(taker != core)
        def _():
            there().wait_send()

    def pass_on(which, step):
        for way, slot in which:

            @pl.when(step > 0)
            def _():
                hop(way, slot, step - 1).wait_recv()

            @pl.when(step < chips - 1)
            def _():
                hop(way, slot, step).start()

            place(way, slot, step)

    def settle(which):
        def body(step, carried):
            for way, slot in which:
                placed(way, slot, step)

                @pl.when(step < chips - 1)
                def _():
                    hop(way, slot, step).wait_send()

            return carried

        lax.fori_loop(0, chips, body, 0)

    def quad_copy(source, target, index, device):
        return remote(source, target, quad_send.at[index], quad_recv.at[index], device)

    mine = normed_ref.at[core, side]
    along = quad_copy(mine, mine, 0, to_side)
    across = quad_copy(normed_ref.at[core], normed_ref.at[core], 1, to_core)

    def bulk_side(part):
        rows = pl.ds(cuts[part], cuts[part + 1] - cuts[part])
        return remote(
            own_units_ref.at[rows],
            side_units_ref.at[rows],
            bulk_send.at[part],
            bulk_recv.at[part],
            to_side,
        )

    def bulk_diag(part):
        rows = pl.ds(cuts[part], cuts[part + 1] - cuts[part])
        return remote(
            side_units_ref.at[rows],
            diag_units_ref.at[rows],
            bulk_send.at[3 + part],
            bulk_recv.at[3 + part],
            to_core,
        )

    bulk_core = remote(own_units_ref, core_units_ref, bulk_send.at[6], bulk_recv.at[6], to_core)
    for way, slot in streams:
        hop(way, slot, 0).start()
    cast(0, 1)
    cast_store(0).wait()
    bulk_side(0).start()
    gains_total.over_cores()
    for way, slot in streams:
        place(way, slot, 0)
    gains_total.over_ring()
    pass_on(streams, 1)
    cast(1, 3)
    tables()
    pass_on(streams, 2)
    scales_ref[...] = gains_total.end()
    normed_ref[core, side] = norm_scale(resid_ref[...], scales_ref[0:1]).astype(bfloat)
    along.start()
    cast(3, 4)
    pass_on(streams, 3)
    cast(4, 6)
    pass_on(streams, 4)
    cast(6, casts)
    cast_store(casts - 2).wait()
    cast_store(casts - 1).wait()
    along.wait()
    across.start()
    bulk_side(1).start()

    def body(step, carried):
        pass_on(streams, step)
        return carried

    lax.fori_loop(5, chips, body, 0)
    pass_on(out_streams, 0)
    across.wait()
    outs[2].start()
    settle(streams)
    outs[0].start()

    def project(slot, head):
        rows = slice(head * HD, head * HD + HD)
        return dot_nt(normed_ref[...].reshape(tokens, width), rows_ref[slot, rows])

    for head in range(2):
        raw = project(1, head)
        both[head] = turn(raw, key_cosine_ref[...], key_sine_ref[...]).astype(bfloat)
    swap = quad_copy(both.at[1 - side], keyval_ref.at[chip, side], 2, to_side)
    swap.start()
    bulk_side(2).start()
    bulk_core.start()
    for part in range(2):
        bulk_side(part).wait_recv()
        bulk_diag(part).start()
    pass_on(out_streams, 1)
    keyval_ref[chip, side] = both[side]
    for head in range(2):
        raw = project(0, head)
        query_ref[head] = turn(raw, cosine_ref[...], sine_ref[...]).astype(bfloat)
        pass_on(out_streams, 2 + head)
    total[...] = jnp.zeros_like(total)
    sums[...] = jnp.zeros_like(sums)
    swap.wait()

    def block(way, owner):
        part = tokens // 2
        key = keyval_ref[owner, 0, way * part : way * part + part]
        val = keyval_ref[owner, 1, way * part : way * part + part]
        row = lax.broadcasted_iota(jnp.int32, (tokens, part), 0)
        column = lax.broadcasted_iota(jnp.int32, (tokens, part), 1)
        allowed = row + (chip - owner) * tokens - way * part >= column

        def one_head(head, carried):
            bent = jnp.tanh(dot_nt(query_ref[head], key) * (scale / softcap))
            powers = jnp.where(allowed, jnp.exp(softcap * bent), 0.0)
            sums[head] += powers[:, : part // 2] + powers[:, part // 2 :]
            total[head] += dot_nn(powers.astype(bfloat), val)
            return carried

        for head in range(2):
            one_head(head, 0)

    def key_body(step, carried):
        for way, kind in key_streams:

            @pl.when(step > 0)
            def _():
                key_hop(way, kind, step - 1).wait_recv()

            @pl.when(step < chips - 1)
            def _():
                key_hop(way, kind, step).start()

        for way in range(2):
            owner = owner_of(way, step)

            @pl.when(owner <= chip)
            def _():
                block(way, owner)

            if way == 0:

                @pl.when(step < chips - 4)
                def _():
                    pass_on(out_streams, step + 4)

        return carried

    lax.fori_loop(0, chips, key_body, 0)
    outs[3].start()
    bulk_side(2).wait_recv()
    bulk_diag(2).start()
    settle(out_streams)
    outs[1].start()
    for head in range(2):
        inverse = 1.0 / jnp.sum(sums[head], axis=-1, keepdims=True)
        inverse_ref[head] = jnp.broadcast_to(inverse, inverse_ref.shape[1:])
        attended_ref[:, head * HD : head * HD + HD] = (total[head] * inverse).astype(bfloat)
    span = width // 3
    tiles = [slice(tile * span, tile * span + span) for tile in range(3)]

    def project_out(part, ref, columns):
        first = pl.ds(pl.multiple_of(part * 2 * tok_rows, 2 * tok_rows), 2 * tok_rows)
        made = dot_nn(attended_ref[first], rows_ref[2, :, columns])
        ref[:, :, columns] = made.reshape(2, tok_rows, span).astype(ref.dtype)

    across = [
        quad_copy(across_put.at[:, :, columns], across_got.at[:, :, columns], 3 + tile, to_core)
        for tile, columns in enumerate(tiles)
    ]
    along = [
        quad_copy(along_put.at[:, columns], along_got.at[:, columns], 6 + tile, to_side)
        for tile, columns in enumerate(tiles)
    ]
    for tile, columns in enumerate(tiles):
        project_out(1 - core, across_put, columns)
        across[tile].start()
    for tile, columns in enumerate(tiles):
        project_out(core, product, columns)
        across[tile].wait()
        given = product[1 - side, :, columns] + across_got[1 - side, :, columns].astype(single)
        along_put[:, columns] = given.astype(bfloat)
        along[tile].start()

    def key_settle(step, carried):
        for way, kind in key_streams:
            key_hop(way, kind, step).wait_send()
        return carried

    lax.fori_loop(0, chips - 1, key_settle, 0)
    for out in outs:
        out.wait()
    bulk_core.wait()
    for part in range(3):
        bulk_side(part).wait_send()
        bulk_diag(part).wait()
    for tile, columns in enumerate(tiles):
        along[tile].wait()
        kept = product[side, :, columns] + across_got[side, :, columns].astype(single)
        projected_ref[:, columns] = kept + along_got[:, columns].astype(single)


def cost(micros):
    return pl.CostEstimate(flops=int(micros * 1e9), bytes_accessed=0, transcendentals=0)


def front(attn_weight, gains, resid_in, pace, ffn_wide, chips, ident):
    share, width = attn_weight.shape[1:]
    tok_rows = resid_in.shape[0]
    tokens = 4 * tok_rows
    units = ffn_wide.shape[0]
    cuts = (0, units // 9, units // 3, 2 * units // 3)
    vmem = pl.BlockSpec(memory_space=pltpu.VMEM)
    anywhere = pl.BlockSpec(memory_space=pl.ANY)
    return pl.pallas_call(
        functools.partial(front_kernel, chips, cuts),
        out_shape=(
            jax.ShapeDtypeStruct((3, 2 * HD, width), bfloat),
            jax.ShapeDtypeStruct((4, width), single),
            jax.ShapeDtypeStruct((2, 2, tok_rows, width), bfloat),
            jax.ShapeDtypeStruct((2, tokens, HD), bfloat),
            jax.ShapeDtypeStruct((chips, 2, tokens, HD), bfloat),
            jax.ShapeDtypeStruct((tokens, 2 * HD), bfloat),
            jax.ShapeDtypeStruct((2, tokens, 128), single),
            jax.ShapeDtypeStruct((tok_rows, width), single),
        )
        + (jax.ShapeDtypeStruct((tokens, HD // 2), single),) * 4
        + (jax.ShapeDtypeStruct((units, width), bfloat),) * 2
        + (jax.ShapeDtypeStruct((2 * units // 3, width), bfloat),) * 2,
        in_specs=[vmem] * 4 + [anywhere],
        out_specs=(anywhere, vmem, anywhere, vmem, anywhere, vmem, vmem, vmem)
        + (vmem,) * 4
        + (anywhere,) * 4,
        scratch_shapes=[
            pltpu.VMEM((3, 2 * HD, width), bfloat),
            pltpu.VMEM((2, 2, tok_rows, width), bfloat),
            pltpu.VMEM((chips, 2, tokens, HD), bfloat),
            pltpu.VMEM((chips, 3, share, width), bfloat),
            pltpu.VMEM((2, tokens, HD), bfloat),
            pltpu.VMEM((2, tokens, HD), single),
            pltpu.VMEM((2, tokens, 128), single),
            pltpu.VMEM((2, tok_rows, width), single),
            pltpu.VMEM((2, tok_rows, width), bfloat),
            pltpu.VMEM((2, tok_rows, width), bfloat),
            pltpu.VMEM((tok_rows, width), bfloat),
            pltpu.VMEM((tok_rows, width), bfloat),
            pltpu.VMEM((2, units // 9, width), single),
            pltpu.VMEM((2, units // 9, width), bfloat),
        ]
        + total_scratch(chips, width)
        + [
            pltpu.SemaphoreType.DMA((2, 3, chips - 1)),
            pltpu.SemaphoreType.DMA((2, 3, chips - 1)),
            pltpu.SemaphoreType.DMA((2, 3, chips)),
            pltpu.SemaphoreType.DMA((2, 3, chips)),
            pltpu.SemaphoreType.DMA((2, 2, chips - 1)),
            pltpu.SemaphoreType.DMA((2, 2, chips - 1)),
            pltpu.SemaphoreType.DMA((9,)),
            pltpu.SemaphoreType.DMA((9,)),
            pltpu.SemaphoreType.DMA((2, 2)),
            pltpu.SemaphoreType.DMA((4,)),
            pltpu.SemaphoreType.DMA((7,)),
            pltpu.SemaphoreType.DMA((7,)),
        ],
        compiler_params=pltpu.CompilerParams(
            collective_id=ident, has_side_effects=True, vmem_limit_bytes=60 * 2**20
        ),
        cost_estimate=cost(140),
    )(attn_weight, gains, resid_in, pace, ffn_wide)


def tail_kernel(
    chips,
    d_proj_ref,
    query_ref,
    keyval_in,
    attended_ref,
    inverse_ref,
    rows_in,
    normed_in,
    cosine_ref,
    sine_ref,
    key_cosine_ref,
    key_sine_ref,
    resid_ref,
    d_mid_ref,
    scales_ref,
    gains_ref,
    units_own_ref,
    units_other_ref,
    sum_ref,
    tokens_ref,
    total_ref,
    units_ref,
    units_got_ref,
    units_mine_ref,
    keyval_ref,
    rows_ref,
    normed_ref,
    d_all,
    d_out,
    delta,
    d_query,
    d_block,
    first_put,
    held_keys,
    swapped,
    d_raw,
    out_rows,
    parts,
    out_parts,
    held,
    out_held,
    across_got,
    along_put,
    along_got,
    value,
    near,
    blocks,
    total_send,
    total_recv,
    key_send,
    key_recv,
    place_sem,
    peer_sem,
    send_sem,
    recv_sem,
    out_send,
    out_recv,
    quad_send,
    quad_recv,
    load_sem,
    bulk_send,
    bulk_recv,
):
    tokens = query_ref.shape[1]
    half = tokens // 2
    width = resid_ref.shape[1]
    share = out_parts.shape[1]
    pairs = chips // 4
    scale = 1.0 / math.sqrt(HD)
    peers = quad_peers(chips)
    side, core, to_side, to_core, around = peers
    rings = [Ring(chips, 1, share, send_sem.at[slot], recv_sem.at[slot]) for slot in range(2)]
    ring = rings[0]
    out_ring = Ring(chips, 1, share, out_send, out_recv)
    chip = ring.chip
    gains_total = Total(value, near, blocks, total_send, total_recv, peers, chip)
    arrays = [
        pltpu.make_async_copy(rows_in.at[2], rows_ref.at[2], load_sem.at[3]),
        pltpu.make_async_copy(keyval_in, keyval_ref, load_sem.at[4]),
        pltpu.make_async_copy(normed_in, normed_ref, load_sem.at[5]),
        pltpu.make_async_copy(rows_in.at[0:2], rows_ref.at[0:2], load_sem.at[6]),
    ]
    d_all[core, side] = d_proj_ref[...]
    wide_barrier(to_side, to_core, around)

    def quad_copy(source, target, index, device):
        return remote(source, target, quad_send.at[index], quad_recv.at[index], device)

    cuts = (0, 320, 640, units_ref.shape[0])

    def bulk(part):
        rows = pl.ds(cuts[part], cuts[part + 1] - cuts[part])
        return remote(
            units_ref.at[rows],
            units_got_ref.at[rows],
            bulk_send.at[part],
            bulk_recv.at[part],
            to_side,
        )

    units = units_ref.shape[0]
    ours = out_rows.reshape(6 * HD, width).at[pl.ds(0, units)]
    theirs = parts.reshape(2 * chips * share, width).at[pl.ds(0, units)]
    loads = (
        pltpu.make_async_copy(units_own_ref.at[1], ours, load_sem.at[0]),
        pltpu.make_async_copy(units_other_ref.at[1], theirs, load_sem.at[1]),
    )
    store = pltpu.make_async_copy(ours, units_ref, load_sem.at[2])
    spare = held.reshape(2 * (chips - 1) * share, width).at[pl.ds(0, units)]
    mine_loads = (
        pltpu.make_async_copy(units_own_ref.at[0], ours, load_sem.at[7]),
        pltpu.make_async_copy(units_other_ref.at[0], spare, load_sem.at[8]),
    )
    mine_store = pltpu.make_async_copy(ours, units_mine_ref, load_sem.at[9])
    mine_loads[1].start()

    def add_up(more):
        for kind in range(3):
            rows = slice(kind * units // 3, (kind + 1) * units // 3)
            ours[rows] = (ours[rows].astype(single) + more[rows].astype(single)).astype(bfloat)
    for load in loads:
        load.start()
    for array in arrays:
        array.start()
    quarter = tokens // 8
    halves = [slice(part * quarter, part * quarter + quarter) for part in range(2)]
    along = [
        quad_copy(d_all.at[core, side, rows], d_all.at[core, side, rows], part, to_side)
        for part, rows in enumerate(halves)
    ]
    across = quad_copy(d_all.at[core, side], d_all.at[core, side], 2, to_core)
    relay = [
        quad_copy(d_all.at[core, 1 - side, rows], d_all.at[core, 1 - side, rows], 3 + part, to_core)
        for part, rows in enumerate(halves)
    ]
    for part in range(2):
        along[part].start()
    across.start()
    d_query[...] = jnp.zeros_like(d_query)
    for load in loads:
        load.wait()
    add_up(theirs)
    store.start()
    for part in range(2):
        along[part].wait()
        relay[part].start()
    store.wait()
    bulk(0).start()
    bulk(1).start()
    mine_loads[0].start()
    across.wait()
    for load in mine_loads:
        load.wait()
    add_up(spare)
    mine_store.start()
    for part in range(2):
        relay[part].wait()
    for array in arrays:
        array.wait()
    d_rows = d_all[...].reshape(tokens, width)
    for head in range(2):
        columns = slice(head * HD, head * HD + HD)
        made = dot_nt(d_rows, rows_ref[2, columns]).astype(bfloat)
        d_out[head] = made
        row_dot = jnp.sum(
            made.astype(single) * attended_ref[:, columns].astype(single), axis=-1, keepdims=True
        )
        delta[head] = jnp.broadcast_to(row_dot, delta.shape[1:])

    def place(slot, head, start):
        deep = 2 * head + core if slot == 1 else 2 * core + head
        for unit in range(4):
            source = out_rows.at[slot, head, pl.ds(unit * share, share)]
            owner = deep * pairs + unit // 2
            target = out_parts.at[owner] if slot == 2 else parts.at[slot, owner]
            sem = place_sem.at[slot, head, unit]

            def here():
                return pltpu.make_async_copy(source, target, sem)

            def there():
                return remote(source, target, sem, peer_sem.at[slot, head, unit], to_core)

            @pl.when(core == unit % 2)
            def _():
                if start:
                    here().start()
                else:
                    here().wait()
                    there().wait_recv()

            @pl.when(core != unit % 2)
            def _():
                if start:
                    there().start()
                else:
                    there().wait_send()

    def term(slot, head, left, right):
        out_rows[slot, head] = dot_tn(left, right).astype(bfloat)
        place(slot, head, True)

    def block(way, owner):
        key = keyval_ref[owner, 0, way * half : way * half + half]
        val = keyval_ref[owner, 1, way * half : way * half + half]
        row = lax.broadcasted_iota(jnp.int32, (tokens, half), 0)
        column = lax.broadcasted_iota(jnp.int32, (tokens, half), 1)
        allowed = row + (chip - owner) * tokens - way * half >= column

        def one_head(head, carried):
            bent = jnp.tanh(dot_nt(query_ref[head], key) * (scale / softcap))
            inverse = jnp.concatenate([inverse_ref[head]] * (half // 128), axis=1)
            row_dot = jnp.concatenate([delta[head]] * (half // 128), axis=1)
            probs = jnp.where(allowed, jnp.exp(softcap * bent), 0.0) * inverse
            d_probs = dot_nt(d_out[head], val)
            d_scores = (probs * (d_probs - row_dot) * (1.0 - bent * bent)).astype(bfloat)
            d_block[way, 0] += dot_tn(d_scores, query_ref[head]) * scale
            d_block[way, 1] += dot_tn(probs.astype(bfloat), d_out[head])
            d_query[head] += dot_nn(d_scores, key)
            return carried

        for head in range(2):
            one_head(head, 0)

    def key_copy(way, kind, step, first):
        return remote(
            first_put.at[way, kind] if first else held_keys.at[way, step - 1, kind],
            held_keys.at[way, step, kind],
            key_send.at[way, kind, step],
            key_recv.at[way, kind, step],
            {"fsdp": ring.right if way == 0 else ring.left},
        )

    streams = [(way, kind) for kind in range(2) for way in range(2)]

    early = 3

    def key_blocks(step):
        for way in range(2):
            owner = ring.owner(way, step + 1)
            d_block[way] = jnp.zeros(d_block.shape[1:], single)
            if way == 1:

                @pl.when((step >= early) & (step < chips - 1))
                def _():
                    out_ring.scatter_step(out_parts, out_held, step - early)

            @pl.when(owner <= chip)
            def _():
                block(way, owner)

    def key_body(step, carried):
        key_blocks(step)
        for way, kind in streams:

            @pl.when(step == 0)
            def _():
                first_put[way, kind] = d_block[way, kind].astype(bfloat)
                key_copy(way, kind, 0, True).start()

            @pl.when(step > 0)
            def _():
                key_copy(way, kind, step - 1, True).wait_recv()
                summed = held_keys[way, step - 1, kind].astype(single) + d_block[way, kind]
                held_keys[way, step - 1, kind] = summed.astype(bfloat)
                key_copy(way, kind, step, False).start()

        @pl.when(step == 0)
        def _():
            for head in range(2):
                left = attended_ref[:, head * HD : head * HD + HD]
                term(2, head, left, d_all[...].reshape(tokens, width))

        @pl.when(step == early - 1)
        def _():
            key_blocks(chips - 1)
            for way in range(2):
                for kind in range(2):
                    rows = slice(way * half, way * half + half)
                    swapped[2 + kind, rows] = d_block[way, kind].astype(bfloat)
            for head in range(2):
                place(2, head, False)

        return carried

    lax.fori_loop(0, chips - 1, key_body, 0)
    mine_store.wait()

    normed = normed_ref[...].reshape(tokens, width)
    for way in range(2):
        rows = slice(way * half, way * half + half)
        for kind in range(2):
            key_copy(way, kind, chips - 2, True).wait_recv()
            summed = held_keys[way, chips - 2, kind].astype(single)
            summed = summed + swapped[2 + kind, rows].astype(single)
            swapped[2 + kind, rows] = summed.astype(bfloat)
    swap = quad_copy(swapped.at[3 - side], swapped.at[side], 5, to_side)
    swap.start()
    out_ring.scatter_step(out_parts, out_held, chips - 4)
    for head in range(2):
        turned = turn(d_query[head] * scale, cosine_ref[...], -sine_ref[...])
        d_raw[head] = turned.astype(bfloat)
        term(0, head, d_raw[head], normed)
    out_ring.scatter_step(out_parts, out_held, chips - 3)
    for head in range(2):
        place(0, head, False)
    rings[0].scatter_step(parts.at[0], held.at[0], 0)
    swap.wait()
    swapped[side] = swapped[2 + side]
    for head in range(2):
        turned = turn(swapped[head].astype(single), key_cosine_ref[...], -key_sine_ref[...])
        d_raw[2 + head] = turned.astype(bfloat)
        term(1, head, d_raw[2 + head], normed)
    out_ring.scatter_step(out_parts, out_held, chips - 2)
    rings[0].scatter_step(parts.at[0], held.at[0], 1)
    span = width // 3

    def d_input(tile, carried):
        columns = pl.ds(pl.multiple_of(tile * span, span), span)
        made = dot_nn(d_raw[0], rows_ref[0, 0:HD, columns])
        made = made + dot_nn(d_raw[1], rows_ref[0, HD:, columns])
        made = made + dot_nn(d_raw[2], rows_ref[1, 0:HD, columns])
        made = made + dot_nn(d_raw[3], rows_ref[1, HD:, columns])
        out_rows[0, :, :, columns] = made.reshape(2, half, span).astype(bfloat)
        return carried

    for head in range(2):
        place(1, head, False)
    rings[1].scatter_step(parts.at[1], held.at[1], 0)
    lax.fori_loop(0, 3, d_input, 0)
    across = quad_copy(out_rows.at[0, 1 - core], across_got, 6, to_core)
    mine = pl.ds(pl.multiple_of(side * (half // 2), half // 2), half // 2)
    other = pl.ds(pl.multiple_of((1 - side) * (half // 2), half // 2), half // 2)
    along = quad_copy(along_put, along_got, 7, to_side)
    across.start()

    def body(step, carried):
        rings[1].scatter_step(parts.at[1], held.at[1], step)

        @pl.when(step < chips - 2)
        def _():
            rings[0].scatter_step(parts.at[0], held.at[0], step + 1)

        @pl.when(step == 1)
        def _():
            across.wait()
            given = out_rows[0, core, other].astype(single) + across_got[other].astype(single)
            along_put[...] = given.astype(bfloat)
            along.start()
            bulk(2).start()
            tokens_ref[...] = out_rows[0, core, mine].astype(single) + across_got[mine].astype(single)

        @pl.when(step == 4)
        def _():
            along.wait()
            tokens_ref[...] = tokens_ref[...] + along_got[...].astype(single)
            d_norm, d_gain = norm_back(resid_ref[...], scales_ref[0:1], tokens_ref[...])
            tokens_ref[...] = d_mid_ref[...] + d_norm
            value[0] = gains_ref[...]
            value[0, 0:1] = d_gain
            gains_total.start()

        @pl.when(step == 5)
        def _():
            gains_total.over_cores()

        @pl.when(step == 6)
        def _():
            gains_total.over_ring()

        return carried

    lax.fori_loop(1, chips - 1, body, 0)
    total_ref[...] = gains_total.end()
    out_ring.scatter_end(out_parts, out_held, sum_ref.at[pl.ds(2 * share, share)])
    for slot in range(2):
        rows = pl.ds(slot * share, share)
        rings[slot].scatter_end(parts.at[slot], held.at[slot], sum_ref.at[rows])
        rings[slot].finish(out_held.at[0, 0, 0 : ring.size])
    out_ring.finish(out_held.at[0, 0, 0 : out_ring.size])

    def settle(step, carried):
        for way, kind in streams:
            key_copy(way, kind, step, True).wait_send()
        return carried

    lax.fori_loop(0, chips - 1, settle, 0)
    for kind in range(3):
        bulk(kind).wait()


def tail(
    d_proj, query, keyval, attended, inverse, rows, normed, turns, locals_, own, other, chips, ident
):
    tokens = query.shape[1]
    tok_rows = tokens // 4
    width = rows.shape[2]
    share = tokens // 8
    half = tokens // 2
    vmem = pl.BlockSpec(memory_space=pltpu.VMEM)
    anywhere = pl.BlockSpec(memory_space=pl.ANY)
    return pl.pallas_call(
        functools.partial(tail_kernel, chips),
        out_shape=(
            jax.ShapeDtypeStruct((3 * share, width), single),
            jax.ShapeDtypeStruct((tok_rows, width), single),
            jax.ShapeDtypeStruct((4, width), single),
            jax.ShapeDtypeStruct(own.shape[1:], bfloat),
            jax.ShapeDtypeStruct(own.shape[1:], bfloat),
            jax.ShapeDtypeStruct(own.shape[1:], bfloat),
        ),
        in_specs=[vmem] * 2
        + [anywhere, vmem, vmem, anywhere, anywhere]
        + [vmem] * 8
        + [anywhere] * 2,
        out_specs=(vmem,) * 3 + (anywhere,) * 3,
        scratch_shapes=[
            pltpu.VMEM(keyval.shape, bfloat),
            pltpu.VMEM(rows.shape, bfloat),
            pltpu.VMEM(normed.shape, bfloat),
            pltpu.VMEM((2, 2, tok_rows, width), bfloat),
            pltpu.VMEM((2, tokens, HD), bfloat),
            pltpu.VMEM((2, tokens, 128), single),
            pltpu.VMEM((2, tokens, HD), single),
            pltpu.VMEM((2, 2, half, HD), single),
            pltpu.VMEM((2, 2, half, HD), bfloat),
            pltpu.VMEM((2, chips - 1, 2, half, HD), bfloat),
            pltpu.VMEM((4, tokens, HD), bfloat),
            pltpu.VMEM((4, tokens, HD), bfloat),
            pltpu.VMEM((3, 2, HD, width), bfloat),
            pltpu.VMEM((2, chips, share, width), bfloat),
            pltpu.VMEM((chips, share, width), bfloat),
            pltpu.VMEM((2, 2, chips - 1, share // 2, width), bfloat),
            pltpu.VMEM((2, chips - 1, share // 2, width), bfloat),
            pltpu.VMEM((2 * tok_rows, width), bfloat),
            pltpu.VMEM((tok_rows, width), bfloat),
            pltpu.VMEM((tok_rows, width), bfloat),
        ]
        + total_scratch(chips, width)
        + [
            pltpu.SemaphoreType.DMA((2, 2, chips - 1)),
            pltpu.SemaphoreType.DMA((2, 2, chips - 1)),
            pltpu.SemaphoreType.DMA((3, 2, 4)),
            pltpu.SemaphoreType.DMA((3, 2, 4)),
            pltpu.SemaphoreType.DMA((2, 2, 1, chips - 1)),
            pltpu.SemaphoreType.DMA((2, 2, 1, chips - 1)),
            pltpu.SemaphoreType.DMA((2, 1, chips - 1)),
            pltpu.SemaphoreType.DMA((2, 1, chips - 1)),
            pltpu.SemaphoreType.DMA((8,)),
            pltpu.SemaphoreType.DMA((8,)),
            pltpu.SemaphoreType.DMA((10,)),
            pltpu.SemaphoreType.DMA((3,)),
            pltpu.SemaphoreType.DMA((3,)),
        ],
        compiler_params=pltpu.CompilerParams(
            collective_id=ident, has_side_effects=True, vmem_limit_bytes=63 * 2**20
        ),
        cost_estimate=cost(160),
    )(d_proj, query, keyval, attended, inverse, rows, normed, *turns, *locals_, own, other)


def feed_kernel(
    chips,
    pieces,
    resid_ref,
    projected_ref,
    dy_ref,
    scales_ref,
    own_ref,
    side_ref,
    core_ref,
    diag_ref,
    result_ref,
    d_mid_ref,
    d_projected_ref,
    d_gains_ref,
    terms_ref,
    other_ref,
    weights,
    x_all,
    y_all,
    mid,
    both,
    hidden,
    part,
    held,
    chunk,
    wide,
    stage,
    load_sem,
    bulk_send,
    bulk_recv,
    stage_sem,
    other_sem,
    send_sem,
    recv_sem,
):
    tok_rows, width = resid_ref.shape
    units = own_ref.shape[0] // 3
    whole = 4 * units
    half = tok_rows // 2
    rings = [
        Ring(chips, pieces, tok_rows, send_sem.at[phase], recv_sem.at[phase]) for phase in range(4)
    ]
    chip = rings[0].chip
    loads = []
    for slot, ref in enumerate((own_ref, side_ref, core_ref, diag_ref)):
        for kind in range(3 if slot % 2 == 0 else 2):
            loads.append(
                pltpu.make_async_copy(
                    ref.at[pl.ds(kind * units, units)],
                    weights.at[pl.ds(kind * whole + slot * units, units)],
                    load_sem.at[slot, kind],
                )
            )
    for load in loads:
        load.start()
    mid[...] = resid_ref[...] + norm_scale(projected_ref[...], scales_ref[1:2])
    x_all[chip] = norm_scale(mid[...], scales_ref[2:3]).astype(bfloat)
    core = lax.axis_index("fsdp") % 2
    to_core = {"fsdp": 2 * chip + 1 - core}
    to_side = {"head": 1 - lax.axis_index("head")}
    quad_barrier(to_side, to_core, rings[0].right, rings[0].left)
    down_rows = [pl.ds(2 * whole + slot * units, units) for slot in range(4)]
    bulk_side = remote(
        own_ref.at[pl.ds(2 * units, units)],
        weights.at[down_rows[1]],
        bulk_send.at[0],
        bulk_recv.at[0],
        to_side,
    )
    bulk_diag = remote(
        weights.at[down_rows[1]],
        weights.at[down_rows[3]],
        bulk_send.at[1],
        bulk_recv.at[1],
        to_core,
    )
    bulk_side.start()
    span = width // 3

    def segments(pair):
        for hop in range(2):
            for way in range(2):
                start = hop * tok_rows + way * half
                owner = rings[0].owner(way, 2 * pair + hop)
                yield owner, pl.ds(way * half, half), pl.ds(start, half)

    def fetch(all_ref, pair):
        for owner, rows, here in segments(pair):
            chunk[here] = all_ref[owner, rows]

    def put(ref, pair, columns, value):
        for owner, rows, here in segments(pair):
            ref[owner, rows, columns] = value[here.start : here.start + half].astype(ref.dtype)

    def take(ref, pair, columns):
        return jnp.concatenate(
            [ref[owner, rows, columns] for owner, rows, here in segments(pair)], axis=0
        )

    def polls(ring, all_ref, pair):
        def poll(index):
            @pl.when(2 * pair + 2 < chips)
            def _():
                ring.gather_step(all_ref, 2 * pair + 2 + index // 2, index % 2)

        return poll

    def down(pair):
        chunk[:, 0:whole] = take(hidden, pair, slice(None))

        def columns_of(tile, carried):
            columns = pl.ds(pl.multiple_of(tile * span, span), span)
            put(part, pair, columns, dot_nn(chunk[:, 0:whole], weights[2 * whole :, columns]))
            return carried

        lax.fori_loop(0, 3, columns_of, 0)

    def gate_up(tile):
        rows = slice(tile * span, tile * span + span)
        wide[:, rows] = dot_nt(chunk[...], weights[rows])

    def unit(pair):
        put(both, pair, slice(None), wide[...])
        value, slope = gelu_parts(wide[:, 0:whole])
        put(hidden, pair, slice(None), value * wide[:, whole:])

    last = chips // 2 - 1

    def forward(pair, carried):
        poll = polls(rings[0], x_all, pair)
        fetch(x_all, pair)
        for tile in range(3):
            gate_up(tile)
            poll(tile)
        unit(pair)

        @pl.when(pair == last - 1)
        def _():
            bulk_side.wait_recv()
            bulk_diag.start()
            bulk_diag.wait_recv()
            down(0)

        poll(3)
        return carried

    for step in range(2):
        for piece in range(pieces):
            rings[0].gather_step(x_all, step, piece)
        if step == 0:
            for load in loads:
                load.wait()
    lax.fori_loop(0, last, forward, 0)
    rings[1].scatter_step(part, held, 0)
    down(1)
    fetch(x_all, last)
    gate_up(0)
    rings[1].scatter_step(part, held, 1)
    gate_up(1)
    gate_up(2)
    unit(last)

    def spread(step, carried):
        rings[1].scatter_step(part, held, step, 0)

        @pl.when((step % 2 == 0) & (step < chips - 2))
        def _():
            down(step // 2 + 1)

        rings[1].scatter_step(part, held, step, 1)
        return carried

    lax.fori_loop(2, chips - 1, spread, 0)
    ours = pl.ds(0, tok_rows)
    rings[1].scatter_end(part, held, wide)
    result_ref[...] = mid[...] + norm_scale(wide[ours], scales_ref[3:4])
    d_ffn, d_gain = norm_back(wide[ours], scales_ref[3:4], dy_ref[...])
    d_gains_ref[0:1] = jnp.zeros_like(d_gain)
    d_gains_ref[3:4] = d_gain
    y_all[chip] = d_ffn.astype(bfloat)
    rings[0].finish(x_all.at[0, 0 : rings[0].size])
    rings[1].finish(x_all.at[0, 0 : rings[0].size])
    bulk_side.wait_send()
    bulk_diag.wait_send()

    def d_input(pair):
        chunk[...] = take(both, pair, slice(None))

        def columns_of(tile, carried):
            columns = pl.ds(pl.multiple_of(tile * span, span), span)
            put(part, pair, columns, dot_nn(chunk[...], weights[0 : 2 * whole, columns]))
            return carried

        lax.fori_loop(0, 3, columns_of, 0)

    third = whole // 3

    def d_units(pair, tile):
        columns = slice(tile * third, tile * third + third)
        ups = slice(whole + tile * third, whole + tile * third + third)
        for owner, rows, here in segments(pair):
            value, slope = gelu_parts(both[owner, rows, columns].astype(single))
            upper = both[owner, rows, ups].astype(single)
            d_hidden = wide[here, columns]
            both[owner, rows, columns] = (d_hidden * upper * slope).astype(bfloat)
            both[owner, rows, ups] = (d_hidden * value).astype(bfloat)

    def d_hidden(first, end):
        wide[:, first:end] = dot_nt(chunk[...], weights[2 * whole + first : 2 * whole + end])

    def backward(pair, carried):
        poll = polls(rings[2], y_all, pair)
        fetch(y_all, pair)
        d_hidden(0, 2 * third)
        poll(0)
        d_hidden(2 * third, whole)
        d_units(pair, 0)
        poll(1)
        d_units(pair, 1)
        d_units(pair, 2)
        poll(2)

        @pl.when(pair < 2)
        def _():
            d_input(pair)

        poll(3)
        return carried

    for step in range(2):
        for piece in range(pieces):
            rings[2].gather_step(y_all, step, piece)
    lax.fori_loop(0, last, backward, 0)
    rings[3].scatter_step(part, held, 0)
    fetch(y_all, last)
    d_hidden(0, 2 * third)
    d_hidden(2 * third, whole)
    d_units(last, 0)
    rings[3].scatter_step(part, held, 1)
    d_units(last, 1)
    d_units(last, 2)
    rows_tile = stage.shape[1]
    tiles = 3 * whole // rows_tile
    upper_tiles = 2 * whole // rows_tile

    cut = units // 3

    def pieces_of(tile):
        for quarter in range(4):
            block = 4 * tile + quarter
            kind, slot, third = block // 12, (block // 3) % 4, block % 3
            source = stage.at[tile % 2, pl.ds(quarter * cut, cut)]
            rows = pl.ds(pl.multiple_of(kind * units + third * cut, cut), cut)
            sem = stage_sem.at[tile % 2, quarter]
            goal = terms_ref.at[slot, rows], other_ref.at[slot - 2, rows]
            there = functools.partial(
                remote, source, goal[1], sem, other_sem.at[tile, quarter], to_core
            )
            yield slot, functools.partial(pltpu.make_async_copy, source, goal[0], sem), there

    def keep(tile):
        for slot, here, there in pieces_of(tile):

            @pl.when(slot < 2)
            def _():
                here().start()

            @pl.when(slot >= 2)
            def _():
                there().start()

    def kept(tile):
        for slot, here, there in pieces_of(tile):

            @pl.when(slot < 2)
            def _():
                here().wait()

            @pl.when(slot >= 2)
            def _():
                there().wait_send()

    def grads(tile):
        @pl.when(tile >= 2)
        def _():
            kept(tile - 2)

        @pl.when(tile < upper_tiles)
        def _():
            columns = pl.ds(pl.multiple_of(tile * rows_tile, rows_tile), rows_tile)
            left = both[:, :, columns].reshape(chips * tok_rows, rows_tile)
            stage[tile % 2] = dot_tn(left, x_all[...].reshape(chips * tok_rows, width)).astype(bfloat)

        @pl.when(tile >= upper_tiles)
        def _():
            columns = pl.ds(
                pl.multiple_of((tile - upper_tiles) * rows_tile, rows_tile), rows_tile
            )
            left = hidden[:, :, columns].reshape(chips * tok_rows, rows_tile)
            stage[tile % 2] = dot_tn(left, y_all[...].reshape(chips * tok_rows, width)).astype(bfloat)

        keep(tile)

    d_input(2)

    def spread_back(step, carried):
        tile = 2 * (step - 3) + 2 * ((6 - step) // 4)
        rings[3].scatter_step(part, held, step, 0)

        @pl.when(step == 3)
        def _():
            d_input(3)

        @pl.when(step != 3)
        def _():
            grads(tile)

        rings[3].scatter_step(part, held, step, 1)

        @pl.when(step != 3)
        def _():
            grads(tile + 1)

        return carried

    lax.fori_loop(2, chips - 1, spread_back, 0)
    lax.fori_loop(8, tiles, lambda tile, carried: grads(tile) or carried, 0)
    rings[3].scatter_end(part, held, wide)
    d_norm, d_gain = norm_back(mid[...], scales_ref[2:3], wide[ours])
    d_gains_ref[2:3] = d_gain
    d_mid_ref[...] = dy_ref[...] + d_norm
    d_projected, d_gain = norm_back(projected_ref[...], scales_ref[1:2], d_mid_ref[...])
    d_gains_ref[1:2] = d_gain
    d_projected_ref[...] = d_projected.astype(bfloat)
    rings[2].finish(x_all.at[0, 0 : rings[0].size])
    rings[3].finish(x_all.at[0, 0 : rings[0].size])
    kept(tiles - 2)
    kept(tiles - 1)

    def gained(tile, carried):
        for slot, here, there in pieces_of(tile):

            @pl.when(slot >= 2)
            def _():
                there().wait_recv()

        return carried

    lax.fori_loop(0, tiles, gained, 0)


def feed_forward(resid_in, projected, grad_out, scales, shares, chips, ident):
    tok_rows, width = resid_in.shape
    units = shares[0].shape[0] // 3
    whole = 4 * units
    pieces = 2
    vmem = pl.BlockSpec(memory_space=pltpu.VMEM)
    anywhere = pl.BlockSpec(memory_space=pl.ANY)
    return pl.pallas_call(
        functools.partial(feed_kernel, chips, pieces),
        out_shape=(
            jax.ShapeDtypeStruct((tok_rows, width), single),
            jax.ShapeDtypeStruct((tok_rows, width), single),
            jax.ShapeDtypeStruct((tok_rows, width), bfloat),
            jax.ShapeDtypeStruct((4, width), single),
            jax.ShapeDtypeStruct((2, 3 * units, width), bfloat),
            jax.ShapeDtypeStruct((2, 3 * units, width), bfloat),
        ),
        in_specs=[vmem] * 4 + [anywhere] * 4,
        out_specs=(vmem, vmem, vmem, vmem, anywhere, anywhere),
        scratch_shapes=[
            pltpu.VMEM((3 * whole, width), bfloat),
            pltpu.VMEM((chips, tok_rows, width), bfloat),
            pltpu.VMEM((chips, tok_rows, width), bfloat),
            pltpu.VMEM((tok_rows, width), single),
            pltpu.VMEM((chips, tok_rows, 2 * whole), bfloat),
            pltpu.VMEM((chips, tok_rows, whole), bfloat),
            pltpu.VMEM((chips, tok_rows, width), bfloat),
            pltpu.VMEM((2, chips - 1, tok_rows // 2, width), bfloat),
            pltpu.VMEM((2 * tok_rows, width), bfloat),
            pltpu.VMEM((2 * tok_rows, width), single),
            pltpu.VMEM((2, whole // 3, width), bfloat),
            pltpu.SemaphoreType.DMA((4, 3)),
            pltpu.SemaphoreType.DMA((2,)),
            pltpu.SemaphoreType.DMA((2,)),
            pltpu.SemaphoreType.DMA((2, 4)),
            pltpu.SemaphoreType.DMA((9, 4)),
            pltpu.SemaphoreType.DMA((4, 2, pieces, chips - 1)),
            pltpu.SemaphoreType.DMA((4, 2, pieces, chips - 1)),
        ],
        compiler_params=pltpu.CompilerParams(
            collective_id=ident, has_side_effects=True, vmem_limit_bytes=63 * 2**20
        ),
        cost_estimate=cost(205),
    )(resid_in, projected, grad_out, scales, *shares)


def general_device(
    tokens,
    cotangent,
    gains,
    gains_first,
    gains_second,
    attn_weight,
    attn_first,
    attn_second,
    ffn_weight,
    ffn_first,
    ffn_second,
):
    devices = lax.axis_size("fsdp")
    chips = devices // 2
    side = lax.axis_index("head")
    place = lax.axis_index("fsdp")
    core, chip = place % 2, place // 2
    tok_rows = tokens.shape[1]
    super_rows = 4 * tok_rows
    seq_len = min(SEQ_LEN, super_rows * chips)
    share = attn_weight.shape[1]
    pairs = chips // 4
    width = tokens.shape[2]
    scale = 1.0 / math.sqrt(HD)

    def swap_core(value):
        return lax.ppermute(value, "fsdp", [(index, index ^ 1) for index in range(devices)])

    def swap_side(value):
        return lax.ppermute(value, "head", [(0, 1), (1, 0)])

    def in_order(own, other, index, axis):
        return jnp.where(
            index == 0, jnp.stack([own, other], axis), jnp.stack([other, own], axis)
        )

    def pick(value, index, axis=0):
        return lax.dynamic_index_in_dim(value, index, axis, keepdims=False)

    def quad_gather(value):
        value = in_order(value, swap_side(value), side, 0)
        value = in_order(value, swap_core(value), core, 0)
        return value.reshape((super_rows,) + value.shape[3:])

    def quad_scatter(partial):
        partial = partial.reshape(2, 2, tok_rows, width)
        mine = pick(partial, core) + swap_core(pick(partial, 1 - core).astype(bfloat)).astype(single)
        return pick(mine, side) + swap_side(pick(mine, 1 - side).astype(bfloat)).astype(single)

    scales = lax.all_gather(gains.astype(bfloat), ("head", "fsdp"), axis=1, tiled=True).astype(single)
    attn_low = attn_weight.astype(bfloat)
    ffn_low = ffn_weight.astype(bfloat).transpose(1, 0, 2)
    ffn_pair = jnp.concatenate([ffn_low, swap_side(ffn_low)], axis=1)

    ring_rows = ring_gather(attn_low.reshape(3 * share, width), chips, 0)
    ring_rows = ring_rows.reshape(2, 2, pairs, 3, share, width)

    def query_rows(slot):
        rows = ring_rows[:, :, :, slot]
        other = swap_core(pick(rows, 1 - core))
        return in_order(pick(rows, core), other, core, 2).reshape(2 * HD, width)

    def keyval_rows():
        rows = ring_rows[:, :, :, 1]
        other = swap_core(pick(rows, 1 - core, 1))
        return in_order(pick(rows, core, 1), other, core, 2).reshape(2 * HD, width)

    w_query, w_keyval, w_out = query_rows(0), keyval_rows(), query_rows(2)

    resid_in = tokens[0]
    grad_out = cotangent[0]
    normed_one = norm_scale(resid_in, scales[0]).astype(bfloat)
    normed_all = quad_gather(normed_one)
    positions = chip * super_rows + jnp.arange(super_rows, dtype=jnp.int32)
    angles = turn_angles(positions % seq_len, HD)
    query_raw = jnp.einsum("td,fd->tf", normed_all, w_query, preferred_element_type=single)
    keyval_raw = jnp.einsum("td,fd->tf", normed_all, w_keyval, preferred_element_type=single)
    query = rotate(query_raw.reshape(super_rows, 2, HD), angles, 1.0).astype(bfloat)
    key_angles = jnp.where(side == 0, angles, 0.0)
    keyval = rotate(keyval_raw.reshape(super_rows, 2, HD), key_angles, 1.0).astype(bfloat)
    keyval = in_order(pick(keyval, side, 1), swap_side(pick(keyval, 1 - side, 1)), side, 0)
    keyval_all = ring_gather(keyval.reshape(2 * super_rows, HD), chips, 1)
    keyval_all = keyval_all.reshape(chips, 2, super_rows, HD)
    key_all = keyval_all[:, 0].reshape(chips * super_rows, HD)
    value_all = keyval_all[:, 1].reshape(chips * super_rows, HD)

    key_pos = jnp.arange(chips * super_rows, dtype=jnp.int32)
    distance = positions[:, None] - key_pos[None, :]
    same_seq = (positions // seq_len)[:, None] == (key_pos // seq_len)[None, :]
    allowed = (distance >= 0) & (distance < WIN) & same_seq

    def score_block():
        raw = jnp.einsum("qgd,kd->gqk", query, key_all, preferred_element_type=single)
        bent = jnp.tanh(raw * (scale / softcap))
        return bent, jnp.where(allowed, jnp.exp(softcap * bent), 0.0)

    bent, powers = score_block()
    total = jnp.sum(powers, axis=-1, keepdims=True)
    attended = jnp.einsum(
        "gqk,kd->gqd", powers.astype(bfloat), value_all, preferred_element_type=single
    )
    attended = (attended / total).transpose(1, 0, 2).reshape(super_rows, 2 * HD).astype(bfloat)
    projected = quad_scatter(jnp.dot(attended, w_out, preferred_element_type=single))
    resid_mid = resid_in + norm_scale(projected, scales[1])
    normed_two = norm_scale(resid_mid, scales[2]).astype(bfloat)

    ffn_all = jnp.concatenate([ffn_pair, swap_core(ffn_pair)], axis=1)
    w_gate, w_up, w_down = ffn_all[0], ffn_all[1], ffn_all[2]
    ring_tokens = chips * tok_rows
    normed_ring = ring_gather(normed_two, chips, 2).reshape(ring_tokens, width)
    gate_part = jnp.einsum("td,rd->tr", normed_ring, w_gate, preferred_element_type=single)
    up_part = jnp.einsum("td,rd->tr", normed_ring, w_up, preferred_element_type=single)
    hidden = hidden_unit(gate_part, up_part).astype(bfloat)
    ffn_part = jnp.dot(hidden, w_down, preferred_element_type=single).astype(bfloat)
    ffn_acc = ring_scatter(ffn_part.reshape(chips, tok_rows, width), chips, 3)
    result = resid_mid + norm_scale(ffn_acc, scales[3])

    ignored, post_back = jax.vjp(norm_scale, ffn_acc, scales[3])
    d_ffn, d_gain3 = post_back(grad_out)
    d_ffn_ring = ring_gather(d_ffn.astype(bfloat), chips, 4).reshape(ring_tokens, width)
    d_hidden = jnp.einsum("td,rd->tr", d_ffn_ring, w_down, preferred_element_type=single)
    ignored, unit_back = jax.vjp(hidden_unit, gate_part, up_part)
    d_gate, d_up = unit_back(d_hidden)
    d_gate = d_gate.astype(bfloat)
    d_up = d_up.astype(bfloat)
    d_normed = jnp.dot(d_gate, w_gate, preferred_element_type=single)
    d_normed = (d_normed + jnp.dot(d_up, w_up, preferred_element_type=single)).astype(bfloat)
    d_normed_two = ring_scatter(d_normed.reshape(chips, tok_rows, width), chips, 5)

    def ffn_rows(left, right):
        return jnp.einsum("tr,td->rd", left, right, preferred_element_type=single)

    ffn_terms = jnp.stack(
        [ffn_rows(d_gate, normed_ring), ffn_rows(d_up, normed_ring), ffn_rows(hidden, d_ffn_ring)]
    )
    units = ffn_weight.shape[0]
    ffn_terms = ffn_terms.reshape(3, 2, 2, units, width)
    ffn_terms = ffn_terms[:, 0] + swap_core(ffn_terms[:, 1].astype(bfloat)).astype(single)
    grad_ffn = ffn_terms[:, 0] + swap_side(ffn_terms[:, 1].astype(bfloat)).astype(single)

    ignored, mid_back = jax.vjp(norm_scale, resid_mid, scales[2])
    d_mid_norm, d_gain2 = mid_back(d_normed_two)
    d_mid = grad_out + d_mid_norm
    ignored, proj_back = jax.vjp(norm_scale, projected, scales[1])
    d_projected, d_gain1 = proj_back(d_mid)
    d_proj_all = quad_gather(d_projected.astype(bfloat))
    d_attended = jnp.einsum("td,fd->tf", d_proj_all, w_out, preferred_element_type=single)
    d_attended = d_attended.astype(bfloat).reshape(super_rows, 2, HD)

    bent, powers = score_block()
    probs = powers / total
    d_probs = jnp.einsum("qgd,kd->gqk", d_attended, value_all, preferred_element_type=single)
    row_dot = jnp.sum(d_probs * probs, axis=-1, keepdims=True)
    d_raw = (probs * (d_probs - row_dot) * (1.0 - bent * bent)).astype(bfloat)
    d_query = jnp.einsum("gqk,kd->qgd", d_raw, key_all, preferred_element_type=single) * scale
    d_keys = jnp.einsum("gqk,qgd->kd", d_raw, query, preferred_element_type=single) * scale
    d_values = jnp.einsum(
        "gqk,qgd->kd", probs.astype(bfloat), d_attended, preferred_element_type=single
    )
    d_pieces = jnp.stack(
        [d_keys.reshape(chips, super_rows, HD), d_values.reshape(chips, super_rows, HD)], axis=1
    ).astype(bfloat)
    d_keyval = ring_scatter(d_pieces.reshape(chips, 2 * super_rows, HD), chips, 6)
    d_keyval = d_keyval.reshape(2, super_rows, HD).astype(bfloat)
    d_keyval = in_order(pick(d_keyval, side), swap_side(pick(d_keyval, 1 - side)), side, 1)
    d_query_raw = rotate(d_query, angles, -1.0).reshape(super_rows, 2 * HD).astype(bfloat)
    d_keyval_raw = rotate(d_keyval.astype(single), key_angles, -1.0)
    d_keyval_raw = d_keyval_raw.reshape(super_rows, 2 * HD).astype(bfloat)
    d_normed_one = jnp.dot(d_query_raw, w_query, preferred_element_type=single)
    d_normed_one = d_normed_one + jnp.dot(d_keyval_raw, w_keyval, preferred_element_type=single)
    d_normed_one = quad_scatter(d_normed_one)
    ignored, first_back = jax.vjp(norm_scale, resid_in, scales[0])
    d_in_norm, d_gain0 = first_back(d_normed_one)
    tokens_grad = d_mid + d_in_norm

    def attn_rows(left, right):
        rows = jnp.einsum("tf,td->fd", left, right, preferred_element_type=single).astype(bfloat)
        return rows.reshape(2, pairs, 2, share, width)

    term_query = attn_rows(d_query_raw, normed_all)
    term_keyval = attn_rows(d_keyval_raw, normed_all)
    term_out = attn_rows(attended, d_proj_all)

    def to_core(term, axis):
        return in_order(pick(term, core, 2), swap_core(pick(term, 1 - core, 2)), core, axis)

    terms = jnp.stack([to_core(term_query, 0), to_core(term_keyval, 1), to_core(term_out, 0)], axis=3)
    grad_attn = ring_scatter(terms.reshape(chips, 3 * share, width), chips, 7)
    grad_attn = grad_attn.reshape(3, share, width)
    term_gain = jnp.stack([d_gain0, d_gain1, d_gain2, d_gain3])
    grad_gain = lax.psum_scatter(term_gain, ("head", "fsdp"), scatter_dimension=1, tiled=True)

    gains_first_new, gains_second_new, gains_new = adamw(
        gains, gains_first, gains_second, grad_gain, rate_gain, 0.0
    )
    attn_first_new, attn_second_new, attn_weight_new = adamw(
        attn_weight, attn_first, attn_second, grad_attn, rate_matrix, decay_matrix
    )
    ffn_first_new, ffn_second_new, ffn_weight_new = adamw(
        ffn_weight, ffn_first, ffn_second, grad_ffn.transpose(1, 0, 2), rate_matrix, decay_matrix
    )
    return (
        result[None],
        tokens_grad[None],
        gains_first_new,
        gains_second_new,
        gains_new,
        attn_first_new,
        attn_second_new,
        attn_weight_new,
        ffn_first_new,
        ffn_second_new,
        ffn_weight_new,
    )


def step_kernel(
    tiles,
    weight_ref,
    first_ref,
    second_ref,
    own_ref,
    side_ref,
    weight_two_ref,
    first_two_ref,
    second_two_ref,
    grad_two_ref,
    first_out,
    second_out,
    weight_out,
    first_two_out,
    second_two_out,
    weight_two_out,
):
    index = pl.program_id(0)

    @pl.when(index < tiles)
    def _():
        grad = own_ref[...].astype(single) + side_ref[...].astype(single)
        first_out[...], second_out[...], weight_out[...] = adamw(
            weight_ref[...], first_ref[...], second_ref[...], grad, rate_matrix, decay_matrix
        )

    @pl.when(index >= tiles)
    def _():
        first_two_out[...], second_two_out[...], weight_two_out[...] = adamw(
            weight_two_ref[...],
            first_two_ref[...],
            second_two_ref[...],
            grad_two_ref[...],
            rate_matrix,
            decay_matrix,
        )


def step_weights(state, own, side, state_two, grad_two):
    rows, width = state[0].shape
    rows_two = grad_two.shape[0]
    size = 96
    tiles, tiles_two = rows // size, rows_two // size
    block = pl.BlockSpec((size, width), lambda index: (jnp.minimum(index, tiles - 1), 0))
    block_two = pl.BlockSpec((size, width), lambda index: (jnp.maximum(index - tiles, 0), 0))
    return pl.pallas_call(
        functools.partial(step_kernel, tiles),
        grid=(tiles + tiles_two,),
        out_shape=(jax.ShapeDtypeStruct((rows, width), single),) * 3
        + (jax.ShapeDtypeStruct((rows_two, width), single),) * 3,
        in_specs=[block] * 5 + [block_two] * 4,
        out_specs=(block,) * 3 + (block_two,) * 3,
        compiler_params=pltpu.CompilerParams(vmem_limit_bytes=62 * 2**20),
        cost_estimate=cost(20),
    )(*state, own, side, *state_two, grad_two)


def per_device(
    tokens,
    cotangent,
    gains,
    gains_first,
    gains_second,
    attn_weight,
    attn_first,
    attn_second,
    ffn_weight,
    ffn_first,
    ffn_second,
):
    devices = lax.axis_size("fsdp")
    chips = devices // 2
    side = lax.axis_index("head")
    place = lax.axis_index("fsdp")
    tok_rows = tokens.shape[1]
    share = attn_weight.shape[1]
    width = tokens.shape[2]
    gain_columns = gains.shape[1]
    gain_start = (side * devices + place) * gain_columns

    units = ffn_weight.shape[0]

    def flat(value):
        return value.transpose(1, 0, 2).reshape(3 * units, width)

    ffn_wide = flat(ffn_weight)
    resid_in = tokens[0]
    grad_out = cotangent[0]
    gains_placed = lax.dynamic_update_slice(
        jnp.zeros((4, width), single), gains, (0, gain_start)
    )
    halfway = HD // 2
    pace = jnp.asarray(
        10000.0 ** (-2.0 * np.arange(halfway, dtype=np.float64) / HD)[None, :], dtype=single
    )
    made = front(attn_weight, gains_placed, resid_in, pace, ffn_wide, chips, 0)
    attn_rows, scales, normed_all, query, keyval, attended, inverse, projected = made[:8]
    turns = made[8:12]
    own_units, core_units, side_units, diag_units = made[12:]
    result, d_mid, d_proj_low, gain_rows, terms_own, terms_other = feed_forward(
        resid_in,
        projected,
        grad_out,
        scales,
        (own_units, side_units, core_units, diag_units),
        chips,
        1,
    )
    grad_attn, tokens_grad, gain_total, terms_sent, terms_side, terms_mine = tail(
        d_proj_low,
        query,
        keyval,
        attended,
        inverse,
        attn_rows,
        normed_all,
        turns,
        (resid_in, d_mid, scales, gain_rows),
        terms_own,
        terms_other,
        chips,
        2,
    )
    grad_gain = lax.dynamic_slice(gain_total, (0, gain_start), gains.shape)

    gains_first_new, gains_second_new, gains_new = adamw(
        gains, gains_first, gains_second, grad_gain, rate_gain, 0.0
    )
    def rows_of(value):
        return value.reshape(3 * share, width)

    stepped = step_weights(
        (ffn_wide, flat(ffn_first), flat(ffn_second)),
        terms_mine,
        terms_side,
        (rows_of(attn_weight), rows_of(attn_first), rows_of(attn_second)),
        grad_attn,
    )
    ffn_first_new, ffn_second_new, ffn_weight_new = (
        value.reshape(3, units, width).transpose(1, 0, 2) for value in stepped[:3]
    )
    attn_first_new, attn_second_new, attn_weight_new = (
        value.reshape(3, share, width) for value in stepped[3:]
    )
    return (
        result[None],
        tokens_grad[None],
        gains_first_new,
        gains_second_new,
        gains_new,
        attn_first_new,
        attn_second_new,
        attn_weight_new,
        ffn_first_new,
        ffn_second_new,
        ffn_weight_new,
    )


def solution(mesh):
    by_token = P("fsdp", "head", None)
    by_column = P(None, ("head", "fsdp"))
    by_row = P(None, ("head", "fsdp"), None)
    by_unit = P(("head", "fsdp"), None, None)
    placed = (by_token,) * 2 + (by_column,) * 3 + (by_row,) * 3 + (by_unit,) * 3
    body = per_device if mesh.shape["fsdp"] == 16 else general_device
    return jax.shard_map(
        body, mesh=mesh, in_specs=placed, out_specs=placed, check_vma=False
    )
```

```python
import functools
import math

import jax
import jax.numpy as jnp
import numpy as np
from jax import lax
from jax.experimental import pallas as pl
from jax.experimental.pallas import tpu as pltpu
from jax.sharding import PartitionSpec as P

HQ = 8
HK = 4
HD = 256
WIN = 4096
STEP = 10
SEQ_LEN = 8192


eps_norm = 1e-06
softcap = 50.0
beta_one = 0.9
beta_two = 0.95
adam_eps = 1e-08
rate_matrix = 0.02
rate_gain = 0.2
decay_matrix = 0.1

bfloat = jnp.bfloat16
single = jnp.float32
MESH = pl.DeviceIdType.MESH


def norm_scale(values, scales):
    return (
        values
        * lax.rsqrt(jnp.mean(values * values, axis=-1, keepdims=True) + eps_norm)
        * (1.0 + scales)
    )


def turn_angles(positions, head_width):
    halfway = head_width // 2
    inverse_freq = 10000.0 ** (-(jnp.arange(halfway, dtype=jnp.float32) * 2.0) / head_width)
    return positions.astype(jnp.float32)[:, None] * inverse_freq[None, :]


def rotate(values, angles, direction):
    halfway = values.shape[-1] // 2
    cosine = jnp.cos(angles)[:, None, :]
    sine_part = direction * jnp.sin(angles)[:, None, :]
    former = values[..., :halfway]
    latter = values[..., halfway:]
    return jnp.concatenate(
        [former * cosine - latter * sine_part, latter * cosine + former * sine_part], axis=-1
    )


def adamw(weight, moment, second, gradient, step_rate, decay_rate):
    moment = beta_one * moment + (1.0 - beta_one) * gradient
    second = beta_two * second + (1.0 - beta_two) * gradient * gradient
    update = (
        moment / (1.0 - beta_one**STEP) / (jnp.sqrt(second / (1.0 - beta_two**STEP)) + adam_eps)
        + decay_rate * weight
    )
    return (moment, second, weight - step_rate * update)


def hidden_unit(gate_part, up_part):
    return jax.nn.gelu(gate_part, approximate=True) * up_part


def ring_of(chip, chips):
    wide = chips // 4
    deep, side = chip // wide, chip % wide
    return side * 4 + deep + (side % 2) * (3 - 2 * deep)


def chip_of(ring, chips):
    wide = chips // 4
    side, along = ring // 4, ring % 4
    return (along + (side % 2) * (3 - 2 * along)) * wide + side


def ring_places(chips):
    index = lax.axis_index("fsdp")
    core, chip = index % 2, index // 2
    ring = ring_of(chip, chips)
    right = 2 * chip_of((ring + 1) % chips, chips) + core
    left = 2 * chip_of((ring + chips - 1) % chips, chips) + core
    return chip, ring, right, left


def ring_barrier(right, left):
    barrier = pltpu.get_barrier_semaphore()
    for neighbour in (left, right):
        pl.semaphore_signal(barrier, inc=1, device_id={"fsdp": neighbour}, device_id_type=MESH)
    pl.semaphore_wait(barrier, 2)


def region(shape, pieces, way, piece):
    rows, columns = shape
    if rows % 32 == 0:
        size = rows // 2 // pieces
        start = way * (rows // 2) + piece * size
        return (pl.ds(start, size), pl.ds(0, columns)), (pl.ds(piece * size, size), pl.ds(0, columns))
    size = columns // 2
    return (pl.ds(0, rows), pl.ds(way * size, size)), (pl.ds(0, rows), pl.ds(0, size))


def half_shape(rows, columns):
    return (rows // 2, columns) if rows % 32 == 0 else (rows, columns // 2)


def gather_kernel(chips, pieces, own_ref, all_ref, local_sem, send_sem, recv_sem):
    chip, ring, right, left = ring_places(chips)
    ring_barrier(right, left)
    keep = pltpu.make_async_copy(own_ref, all_ref.at[chip], local_sem)
    keep.start()

    def copy(way, step, piece, first):
        owner = chip_of((ring + (chips - step if way == 0 else step)) % chips, chips)
        part, ignored = region(own_ref.shape, pieces, way, piece)
        there = all_ref.at[(owner,) + part]
        return pltpu.make_async_remote_copy(
            src_ref=own_ref.at[part] if first else there,
            dst_ref=there,
            send_sem=send_sem.at[way, piece, step],
            recv_sem=recv_sem.at[way, piece, step],
            device_id={"fsdp": right if way == 0 else left},
            device_id_type=MESH,
        )

    streams = [(way, piece) for piece in range(pieces) for way in range(2)]
    for way, piece in streams:
        copy(way, 0, piece, True).start()

    def body(step, carried):
        for way, piece in streams:
            copy(way, step - 1, piece, False).wait_recv()
            copy(way, step, piece, False).start()
        return carried

    lax.fori_loop(1, chips - 1, body, 0)
    for way, piece in streams:
        copy(way, chips - 2, piece, False).wait_recv()

    def finish(step, carried):
        for way, piece in streams:
            copy(way, step, piece, False).wait_send()
        return carried

    lax.fori_loop(0, chips - 1, finish, 0)
    keep.wait()


def ring_gather(own, chips, ident):
    rows, columns = own.shape
    pieces = 2 if rows % 64 == 0 else 1
    return pl.pallas_call(
        functools.partial(gather_kernel, chips, pieces),
        out_shape=jax.ShapeDtypeStruct((chips, rows, columns), own.dtype),
        in_specs=[pl.BlockSpec(memory_space=pl.ANY)],
        out_specs=pl.BlockSpec(memory_space=pl.ANY),
        scratch_shapes=[
            pltpu.SemaphoreType.DMA,
            pltpu.SemaphoreType.DMA((2, pieces, chips - 1)),
            pltpu.SemaphoreType.DMA((2, pieces, chips - 1)),
        ],
        compiler_params=pltpu.CompilerParams(collective_id=ident, has_side_effects=True),
        cost_estimate=cost(45),
    )(own)


def scatter_kernel(chips, pieces, parts_ref, sum_ref, held, send_sem, recv_sem):
    chip, ring, right, left = ring_places(chips)
    ring_barrier(right, left)

    def owner_of(way, step):
        shift = chips - 1 - step if way == 0 else 1 + step
        return chip_of((ring + shift) % chips, chips)

    def copy(way, step, piece, first):
        part, place = region(sum_ref.shape, pieces, way, piece)
        return pltpu.make_async_remote_copy(
            src_ref=(
                parts_ref.at[(owner_of(way, step),) + part]
                if first
                else held.at[(way, step - 1) + place]
            ),
            dst_ref=held.at[(way, step) + place],
            send_sem=send_sem.at[way, piece, step],
            recv_sem=recv_sem.at[way, piece, step],
            device_id={"fsdp": right if way == 0 else left},
            device_id_type=MESH,
        )

    streams = [(way, piece) for piece in range(pieces) for way in range(2)]
    for way, piece in streams:
        copy(way, 0, piece, True).start()

    def arrived(way, step, piece):
        copy(way, step, piece, True).wait_recv()
        part, place = region(sum_ref.shape, pieces, way, piece)
        here = parts_ref[(owner_of(way, step + 1),) + part]
        return held[(way, step) + place].astype(single) + here.astype(single)

    def body(step, carried):
        for way, piece in streams:
            total = arrived(way, step - 1, piece)
            part, place = region(sum_ref.shape, pieces, way, piece)
            held[(way, step - 1) + place] = total.astype(held.dtype)
            copy(way, step, piece, False).start()
        return carried

    lax.fori_loop(1, chips - 1, body, 0)
    for way, piece in streams:
        part, place = region(sum_ref.shape, pieces, way, piece)
        sum_ref[part] = arrived(way, chips - 2, piece)

    def finish(step, carried):
        for way, piece in streams:
            copy(way, step, piece, True).wait_send()
        return carried

    lax.fori_loop(0, chips - 1, finish, 0)


def ring_scatter(parts, chips, ident):
    rows, columns = parts.shape[1:]
    pieces = 2 if rows % 64 == 0 else 1
    return pl.pallas_call(
        functools.partial(scatter_kernel, chips, pieces),
        out_shape=jax.ShapeDtypeStruct((rows, columns), single),
        in_specs=[pl.BlockSpec(memory_space=pltpu.VMEM)],
        out_specs=pl.BlockSpec(memory_space=pltpu.VMEM),
        scratch_shapes=[
            pltpu.VMEM((2, chips - 1) + half_shape(rows, columns), parts.dtype),
            pltpu.SemaphoreType.DMA((2, pieces, chips - 1)),
            pltpu.SemaphoreType.DMA((2, pieces, chips - 1)),
        ],
        compiler_params=pltpu.CompilerParams(
            collective_id=ident, has_side_effects=True, vmem_limit_bytes=56 * 2**20
        ),
        cost_estimate=cost(45),
    )(parts)


def norm_back(values, scales, grad):
    inverse = lax.rsqrt(jnp.mean(values * values, axis=-1, keepdims=True) + eps_norm)
    bent = grad * (1.0 + scales)
    slope = jnp.mean(bent * values, axis=-1, keepdims=True) * (inverse * inverse * inverse)
    return bent * inverse - values * slope, jnp.sum(grad * values * inverse, axis=0, keepdims=True)


def gelu_parts(gate):
    root = math.sqrt(2.0 / math.pi)
    square = gate * gate
    bend = jnp.tanh(root * gate * (1.0 + 0.044715 * square))
    half = 0.5 * (1.0 + bend)
    slope = half + 0.5 * gate * (1.0 - bend * bend) * (root * (1.0 + 3.0 * 0.044715 * square))
    return gate * half, slope


def dot_nt(left, right):
    return lax.dot_general(left, right, (((1,), (1,)), ((), ())), preferred_element_type=single)


def dot_nn(left, right):
    return lax.dot_general(left, right, (((1,), (0,)), ((), ())), preferred_element_type=single)


def dot_tn(left, right):
    return lax.dot_general(left, right, (((0,), (0,)), ((), ())), preferred_element_type=single)


class Ring:
    def __init__(self, chips, pieces, rows, send_sem, recv_sem):
        self.chips, self.pieces, self.half = chips, pieces, rows // 2
        self.size = rows // 2 // pieces
        self.chip, self.ring, self.right, self.left = ring_places(chips)
        self.send_sem, self.recv_sem = send_sem, recv_sem
        self.streams = [(way, piece) for piece in range(pieces) for way in range(2)]

    def owner(self, way, step):
        shift = self.chips - step if way == 0 else step
        return chip_of((self.ring + shift) % self.chips, self.chips)

    def copy(self, source, target, way, piece, step):
        return pltpu.make_async_remote_copy(
            src_ref=source,
            dst_ref=target,
            send_sem=self.send_sem.at[way, piece, step],
            recv_sem=self.recv_sem.at[way, piece, step],
            device_id={"fsdp": self.right if way == 0 else self.left},
            device_id_type=MESH,
        )

    def part(self, way, piece):
        return pl.ds(way * self.half + piece * self.size, self.size)

    def place(self, piece):
        return pl.ds(piece * self.size, self.size)

    def gather_copy(self, all_ref, way, piece, step):
        there = all_ref.at[self.owner(way, step), self.part(way, piece)]
        return self.copy(there, there, way, piece, step)

    def of(self, only):
        return [(way, piece) for way, piece in self.streams if only is None or piece == only]

    def gather_step(self, all_ref, step, only=None):
        for way, piece in self.of(only):

            @pl.when(step > 0)
            def _():
                self.gather_copy(all_ref, way, piece, step - 1).wait_recv()

            @pl.when(step < self.chips - 1)
            def _():
                self.gather_copy(all_ref, way, piece, step).start()

    def scatter_copy(self, parts_ref, held, way, piece, step, first):
        source = (
            parts_ref.at[self.owner(way, step + 1), self.part(way, piece)]
            if first
            else held.at[way, step - 1, self.place(piece)]
        )
        return self.copy(source, held.at[way, step, self.place(piece)], way, piece, step)

    def scatter_total(self, parts_ref, held, way, piece, step):
        self.scatter_copy(parts_ref, held, way, piece, step, True).wait_recv()
        here = parts_ref[self.owner(way, step + 2), self.part(way, piece)]
        return held[way, step, self.place(piece)].astype(single) + here.astype(single)

    def scatter_step(self, parts_ref, held, step, only=None):
        for way, piece in self.of(only):

            @pl.when(step == 0)
            def _():
                self.scatter_copy(parts_ref, held, way, piece, 0, True).start()

            @pl.when(step > 0)
            def _():
                total = self.scatter_total(parts_ref, held, way, piece, step - 1)
                held[way, step - 1, self.place(piece)] = total.astype(held.dtype)
                self.scatter_copy(parts_ref, held, way, piece, step, False).start()

    def scatter_end(self, parts_ref, held, sum_ref):
        for way, piece in self.streams:
            sum_ref[self.part(way, piece)] = self.scatter_total(
                parts_ref, held, way, piece, self.chips - 2
            )

    def finish(self, example):
        def body(step, carried):
            for way, piece in self.streams:
                self.copy(example, example, way, piece, step).wait_send()
            return carried

        lax.fori_loop(0, self.chips - 1, body, 0)


def quad_peers(chips):
    side = lax.axis_index("head")
    index = lax.axis_index("fsdp")
    chip, core = index // 2, index % 2
    ring = ring_of(chip, chips)
    around = [2 * chip_of((ring + hop) % chips, chips) + core for hop in range(1, chips)]
    return side, core, {"head": 1 - side}, {"fsdp": 2 * chip + 1 - core}, around


def wide_barrier(to_side, to_core, around):
    barrier = pltpu.get_barrier_semaphore()
    for target in [to_side, to_core] + [{"fsdp": other} for other in around]:
        pl.semaphore_signal(barrier, inc=1, device_id=target, device_id_type=MESH)
    pl.semaphore_wait(barrier, 2 + len(around))


def quad_barrier(to_side, to_core, right, left):
    barrier = pltpu.get_barrier_semaphore()
    for target in (to_side, to_core, {"fsdp": right}, {"fsdp": left}):
        pl.semaphore_signal(barrier, inc=1, device_id=target, device_id_type=MESH)
    pl.semaphore_wait(barrier, 4)


def remote(source, target, send_sem, recv_sem, device):
    return pltpu.make_async_remote_copy(
        src_ref=source,
        dst_ref=target,
        send_sem=send_sem,
        recv_sem=recv_sem,
        device_id=device,
        device_id_type=MESH,
    )


class Total:
    def __init__(self, value, near, blocks, send_sem, recv_sem, peers, chip):
        self.value, self.near, self.blocks = value, near, blocks
        self.send_sem, self.recv_sem = send_sem, recv_sem
        side, core, self.to_side, self.to_core, self.around = peers
        self.chip = chip
        self.first = remote(value.at[0], near.at[0], send_sem.at[0], recv_sem.at[0], self.to_side)
        self.second = remote(value.at[1], near.at[1], send_sem.at[1], recv_sem.at[1], self.to_core)

    def spread(self, hop):
        here = self.blocks.at[self.chip]
        return remote(
            here,
            here,
            self.send_sem.at[1 + hop],
            self.recv_sem.at[1 + hop],
            {"fsdp": self.around[hop - 1]},
        )

    def start(self):
        self.first.start()

    def over_cores(self):
        self.first.wait_recv()
        self.value[1] = self.value[0] + self.near[0]
        self.second.start()

    def over_ring(self):
        self.second.wait_recv()
        self.blocks[self.chip] = self.value[1] + self.near[1]
        for hop in range(1, len(self.around) + 1):
            self.spread(hop).start()

    def end(self):
        for hop in range(1, len(self.around) + 1):
            self.spread(hop).wait_recv()
        total = self.blocks[0]
        for other in range(1, len(self.around) + 1):
            total = total + self.blocks[other]
        self.first.wait_send()
        self.second.wait_send()
        for hop in range(1, len(self.around) + 1):
            self.spread(hop).wait_send()
        return total


def total_scratch(chips, width):
    return [
        pltpu.VMEM((2, 4, width), single),
        pltpu.VMEM((2, 4, width), single),
        pltpu.VMEM((chips, 4, width), single),
        pltpu.SemaphoreType.DMA((chips + 1,)),
        pltpu.SemaphoreType.DMA((chips + 1,)),
    ]


def turn(raw, cosine, sine):
    halfway = raw.shape[1] // 2
    former, latter = raw[:, :halfway], raw[:, halfway:]
    return jnp.concatenate(
        [former * cosine - latter * sine, latter * cosine + former * sine], axis=1
    )


def front_kernel(
    chips,
    cuts,
    own_ref,
    gains_ref,
    resid_ref,
    pace_ref,
    wide_units_ref,
    rows_out,
    scales_ref,
    normed_out,
    query_ref,
    keyval_out,
    attended_ref,
    inverse_ref,
    projected_ref,
    cosine_ref,
    sine_ref,
    key_cosine_ref,
    key_sine_ref,
    own_units_ref,
    core_units_ref,
    side_units_ref,
    diag_units_ref,
    rows_ref,
    normed_ref,
    keyval_ref,
    all_rows,
    both,
    total,
    sums,
    product,
    across_put,
    across_got,
    along_put,
    along_got,
    cast_in,
    cast_out,
    value,
    near,
    blocks,
    total_send,
    total_recv,
    send_sem,
    recv_sem,
    place_sem,
    peer_sem,
    key_send,
    key_recv,
    quad_send,
    quad_recv,
    cast_sem,
    out_sem,
    bulk_send,
    bulk_recv,
):
    share, width = own_ref.shape[1:]
    tok_rows = resid_ref.shape[0]
    tokens = 4 * tok_rows
    half = width // 2
    pairs = chips // 4
    scale = 1.0 / math.sqrt(HD)
    seq_len = min(SEQ_LEN, tokens * chips)
    chip, ring, right, left = ring_places(chips)
    peers = quad_peers(chips)
    side, core, to_side, to_core, around = peers
    cast_rows = cast_in.shape[1]
    casts = wide_units_ref.shape[0] // cast_rows

    def cast_load(tile):
        rows = pl.ds(tile * cast_rows, cast_rows)
        return pltpu.make_async_copy(
            wide_units_ref.at[rows], cast_in.at[tile % 2], cast_sem.at[0, tile % 2]
        )

    def cast_store(tile):
        rows = pl.ds(tile * cast_rows, cast_rows)
        return pltpu.make_async_copy(
            cast_out.at[tile % 2], own_units_ref.at[rows], cast_sem.at[1, tile % 2]
        )

    def cast(first, last):
        for tile in range(first, last):
            cast_load(tile).wait()
            if tile >= 3:
                cast_store(tile - 2).wait()
            cast_out[tile % 2] = cast_in[tile % 2].astype(bfloat)
            cast_store(tile).start()
            if tile + 2 < casts:
                cast_load(tile + 2).start()

    outs = [
        pltpu.make_async_copy(rows_ref.at[0:2], rows_out.at[0:2], out_sem.at[0]),
        pltpu.make_async_copy(rows_ref.at[2], rows_out.at[2], out_sem.at[1]),
        pltpu.make_async_copy(normed_ref, normed_out, out_sem.at[2]),
        pltpu.make_async_copy(keyval_ref, keyval_out, out_sem.at[3]),
    ]
    def tables():
        place_in = chip * tokens + lax.broadcasted_iota(jnp.int32, cosine_ref.shape, 0)
        angles = (place_in % seq_len).astype(single) * pace_ref[...]
        cosine_ref[...] = jnp.cos(angles)
        sine_ref[...] = jnp.sin(angles)
        key_cosine_ref[...] = jnp.where(side == 0, cosine_ref[...], 1.0)
        key_sine_ref[...] = jnp.where(side == 0, sine_ref[...], 0.0)

    cast_load(0).start()
    cast_load(1).start()
    all_rows[chip] = own_ref[...].astype(bfloat)
    value[0] = gains_ref[...].astype(bfloat).astype(single)
    wide_barrier(to_side, to_core, around)
    gains_total = Total(value, near, blocks, total_send, total_recv, peers, chip)
    gains_total.start()
    streams = [(way, slot) for slot in range(2) for way in range(2)]
    out_streams = [(way, 2) for way in range(2)]
    key_streams = [(way, kind) for kind in range(2) for way in range(2)]

    def owner_of(way, step):
        return chip_of((ring + (chips - step if way == 0 else step)) % chips, chips)

    def hop(way, slot, step):
        there = all_rows.at[owner_of(way, step), slot, :, pl.ds(way * half, half)]
        return remote(
            there,
            there,
            send_sem.at[way, slot, step],
            recv_sem.at[way, slot, step],
            {"fsdp": right if way == 0 else left},
        )

    def key_hop(way, kind, step):
        there = keyval_ref.at[owner_of(way, step), kind, pl.ds(way * (tokens // 2), tokens // 2)]
        return remote(
            there,
            there,
            key_send.at[way, kind, step],
            key_recv.at[way, kind, step],
            {"fsdp": right if way == 0 else left},
        )

    def goal(way, slot, step):
        owner = owner_of(way, step)
        deep = owner // pairs
        unit = (owner % pairs) * 2 + core
        taker, head = (deep % 2, deep // 2) if slot == 1 else (deep // 2, deep % 2)
        columns = pl.ds(way * half, half)
        source = all_rows.at[owner, slot, :, columns]
        start = pl.multiple_of(head * HD + unit * share, share)
        target = rows_ref.at[slot, pl.ds(start, share), columns]
        sem = place_sem.at[way, slot, step]

        def here():
            return pltpu.make_async_copy(source, target, sem)

        def there():
            return remote(source, target, sem, peer_sem.at[way, slot, step], to_core)

        return taker, here, there

    def place(way, slot, step):
        taker, here, there = goal(way, slot, step)

        @pl.when(taker == core)
        def _():
            here().start()

        @pl.when(taker != core)
        def _():
            there().start()

    def placed(way, slot, step):
        taker, here, there = goal(way, slot, step)

        @pl.when(taker == core)
        def _():
            here().wait()
            there().wait_recv()

        @pl.when(taker != core)
        def _():
            there().wait_send()

    def pass_on(which, step):
        for way, slot in which:

            @pl.when(step > 0)
            def _():
                hop(way, slot, step - 1).wait_recv()

            @pl.when(step < chips - 1)
            def _():
                hop(way, slot, step).start()

            place(way, slot, step)

    def settle(which):
        def body(step, carried):
            for way, slot in which:
                placed(way, slot, step)

                @pl.when(step < chips - 1)
                def _():
                    hop(way, slot, step).wait_send()

            return carried

        lax.fori_loop(0, chips, body, 0)

    def quad_copy(source, target, index, device):
        return remote(source, target, quad_send.at[index], quad_recv.at[index], device)

    mine = normed_ref.at[core, side]
    along = quad_copy(mine, mine, 0, to_side)
    across = quad_copy(normed_ref.at[core], normed_ref.at[core], 1, to_core)

    def bulk_side(part):
        rows = pl.ds(cuts[part], cuts[part + 1] - cuts[part])
        return remote(
            own_units_ref.at[rows],
            side_units_ref.at[rows],
            bulk_send.at[part],
            bulk_recv.at[part],
            to_side,
        )

    def bulk_diag(part):
        rows = pl.ds(cuts[part], cuts[part + 1] - cuts[part])
        return remote(
            side_units_ref.at[rows],
            diag_units_ref.at[rows],
            bulk_send.at[3 + part],
            bulk_recv.at[3 + part],
            to_core,
        )

    bulk_core = remote(own_units_ref, core_units_ref, bulk_send.at[6], bulk_recv.at[6], to_core)
    for way, slot in streams:
        hop(way, slot, 0).start()
    cast(0, 1)
    cast_store(0).wait()
    bulk_side(0).start()
    gains_total.over_cores()
    for way, slot in streams:
        place(way, slot, 0)
    gains_total.over_ring()
    pass_on(streams, 1)
    cast(1, 3)
    tables()
    pass_on(streams, 2)
    scales_ref[...] = gains_total.end()
    normed_ref[core, side] = norm_scale(resid_ref[...], scales_ref[0:1]).astype(bfloat)
    along.start()
    cast(3, 4)
    pass_on(streams, 3)
    cast(4, 6)
    pass_on(streams, 4)
    cast(6, casts)
    cast_store(casts - 2).wait()
    cast_store(casts - 1).wait()
    bulk_core.start()
    along.wait()
    across.start()
    bulk_side(1).start()

    def body(step, carried):
        pass_on(streams, step)
        return carried

    lax.fori_loop(5, chips, body, 0)
    pass_on(out_streams, 0)
    across.wait()
    outs[2].start()
    settle(streams)
    outs[0].start()

    def project(slot, head):
        rows = slice(head * HD, head * HD + HD)
        return dot_nt(normed_ref[...].reshape(tokens, width), rows_ref[slot, rows])

    for head in range(2):
        raw = project(1, head)
        both[head] = turn(raw, key_cosine_ref[...], key_sine_ref[...]).astype(bfloat)
    swap = quad_copy(both.at[1 - side], keyval_ref.at[chip, side], 2, to_side)
    swap.start()
    bulk_side(2).start()
    for part in range(2):
        bulk_side(part).wait_recv()
        bulk_diag(part).start()
    pass_on(out_streams, 1)
    keyval_ref[chip, side] = both[side]
    for head in range(2):
        raw = project(0, head)
        query_ref[head] = turn(raw, cosine_ref[...], sine_ref[...]).astype(bfloat)
        pass_on(out_streams, 2 + head)
    total[...] = jnp.zeros_like(total)
    sums[...] = jnp.zeros_like(sums)
    swap.wait()

    def block(way, owner, own):
        part = tokens // 2
        key = keyval_ref[owner, 0, way * part : way * part + part]
        val = keyval_ref[owner, 1, way * part : way * part + part]
        row = lax.broadcasted_iota(jnp.int32, (tokens, part), 0)
        column = lax.broadcasted_iota(jnp.int32, (tokens, part), 1)
        allowed = row + (chip - owner) * tokens - way * part >= column

        def one_head(head, carried):
            bent = jnp.tanh(dot_nt(query_ref[head], key) * (scale / softcap))
            powers = jnp.exp2((softcap / math.log(2.0)) * bent)
            if own:
                powers = jnp.where(allowed, powers, 0.0)
            sums[head] += powers[:, : part // 2] + powers[:, part // 2 :]
            total[head] += dot_nn(powers.astype(bfloat), val)
            return carried

        for head in range(2):
            one_head(head, 0)

    def key_body(step, carried):
        for way, kind in key_streams:

            @pl.when(step > 0)
            def _():
                key_hop(way, kind, step - 1).wait_recv()

            @pl.when(step < chips - 1)
            def _():
                key_hop(way, kind, step).start()

        for way in range(2):
            owner = owner_of(way, step)

            @pl.when(owner < chip)
            def _():
                block(way, owner, False)

            @pl.when(step == 0)
            def _():
                block(way, chip, True)

            if way == 0:

                @pl.when(step < chips - 4)
                def _():
                    pass_on(out_streams, step + 4)

        return carried

    lax.fori_loop(0, chips, key_body, 0)
    outs[3].start()
    bulk_side(2).wait_recv()
    bulk_diag(2).start()
    settle(out_streams)
    outs[1].start()
    for head in range(2):
        inverse = 1.0 / jnp.sum(sums[head], axis=-1, keepdims=True)
        inverse_ref[head] = jnp.broadcast_to(inverse, inverse_ref.shape[1:])
        attended_ref[:, head * HD : head * HD + HD] = (total[head] * inverse).astype(bfloat)
    span = width // 3
    tiles = [slice(tile * span, tile * span + span) for tile in range(3)]

    def project_out(part, ref, columns):
        first = pl.ds(pl.multiple_of(part * 2 * tok_rows, 2 * tok_rows), 2 * tok_rows)
        made = dot_nn(attended_ref[first], rows_ref[2, :, columns])
        ref[:, :, columns] = made.reshape(2, tok_rows, span).astype(ref.dtype)

    across = [
        quad_copy(across_put.at[:, :, columns], across_got.at[:, :, columns], 3 + tile, to_core)
        for tile, columns in enumerate(tiles)
    ]
    along = [
        quad_copy(along_put.at[:, columns], along_got.at[:, columns], 6 + tile, to_side)
        for tile, columns in enumerate(tiles)
    ]
    for tile, columns in enumerate(tiles):
        project_out(1 - core, across_put, columns)
        across[tile].start()
    for tile, columns in enumerate(tiles):
        project_out(core, product, columns)
        across[tile].wait()
        given = product[1 - side, :, columns] + across_got[1 - side, :, columns].astype(single)
        along_put[:, columns] = given.astype(bfloat)
        along[tile].start()

    def key_settle(step, carried):
        for way, kind in key_streams:
            key_hop(way, kind, step).wait_send()
        return carried

    lax.fori_loop(0, chips - 1, key_settle, 0)
    for out in outs:
        out.wait()
    bulk_core.wait()
    for part in range(3):
        bulk_side(part).wait_send()
        bulk_diag(part).wait()
    for tile, columns in enumerate(tiles):
        along[tile].wait()
        kept = product[side, :, columns] + across_got[side, :, columns].astype(single)
        projected_ref[:, columns] = kept + along_got[:, columns].astype(single)


def cost(micros):
    return pl.CostEstimate(flops=int(micros * 1e9), bytes_accessed=0, transcendentals=0)


def front(attn_weight, gains, resid_in, pace, ffn_wide, chips, ident):
    share, width = attn_weight.shape[1:]
    tok_rows = resid_in.shape[0]
    tokens = 4 * tok_rows
    units = ffn_wide.shape[0]
    cuts = (0, units // 9, units // 3, 2 * units // 3)
    vmem = pl.BlockSpec(memory_space=pltpu.VMEM)
    anywhere = pl.BlockSpec(memory_space=pl.ANY)
    return pl.pallas_call(
        functools.partial(front_kernel, chips, cuts),
        out_shape=(
            jax.ShapeDtypeStruct((3, 2 * HD, width), bfloat),
            jax.ShapeDtypeStruct((4, width), single),
            jax.ShapeDtypeStruct((2, 2, tok_rows, width), bfloat),
            jax.ShapeDtypeStruct((2, tokens, HD), bfloat),
            jax.ShapeDtypeStruct((chips, 2, tokens, HD), bfloat),
            jax.ShapeDtypeStruct((tokens, 2 * HD), bfloat),
            jax.ShapeDtypeStruct((2, tokens, 128), single),
            jax.ShapeDtypeStruct((tok_rows, width), single),
        )
        + (jax.ShapeDtypeStruct((tokens, HD // 2), single),) * 4
        + (jax.ShapeDtypeStruct((units, width), bfloat),) * 2
        + (jax.ShapeDtypeStruct((2 * units // 3, width), bfloat),) * 2,
        in_specs=[vmem] * 4 + [anywhere],
        out_specs=(anywhere, vmem, anywhere, vmem, anywhere, vmem, vmem, vmem)
        + (vmem,) * 4
        + (anywhere,) * 4,
        scratch_shapes=[
            pltpu.VMEM((3, 2 * HD, width), bfloat),
            pltpu.VMEM((2, 2, tok_rows, width), bfloat),
            pltpu.VMEM((chips, 2, tokens, HD), bfloat),
            pltpu.VMEM((chips, 3, share, width), bfloat),
            pltpu.VMEM((2, tokens, HD), bfloat),
            pltpu.VMEM((2, tokens, HD), single),
            pltpu.VMEM((2, tokens, 128), single),
            pltpu.VMEM((2, tok_rows, width), single),
            pltpu.VMEM((2, tok_rows, width), bfloat),
            pltpu.VMEM((2, tok_rows, width), bfloat),
            pltpu.VMEM((tok_rows, width), bfloat),
            pltpu.VMEM((tok_rows, width), bfloat),
            pltpu.VMEM((2, units // 9, width), single),
            pltpu.VMEM((2, units // 9, width), bfloat),
        ]
        + total_scratch(chips, width)
        + [
            pltpu.SemaphoreType.DMA((2, 3, chips - 1)),
            pltpu.SemaphoreType.DMA((2, 3, chips - 1)),
            pltpu.SemaphoreType.DMA((2, 3, chips)),
            pltpu.SemaphoreType.DMA((2, 3, chips)),
            pltpu.SemaphoreType.DMA((2, 2, chips - 1)),
            pltpu.SemaphoreType.DMA((2, 2, chips - 1)),
            pltpu.SemaphoreType.DMA((9,)),
            pltpu.SemaphoreType.DMA((9,)),
            pltpu.SemaphoreType.DMA((2, 2)),
            pltpu.SemaphoreType.DMA((4,)),
            pltpu.SemaphoreType.DMA((7,)),
            pltpu.SemaphoreType.DMA((7,)),
        ],
        compiler_params=pltpu.CompilerParams(
            collective_id=ident, has_side_effects=True, vmem_limit_bytes=60 * 2**20
        ),
        cost_estimate=cost(140),
    )(attn_weight, gains, resid_in, pace, ffn_wide)


def tail_kernel(
    chips,
    d_proj_ref,
    query_ref,
    keyval_in,
    attended_ref,
    inverse_ref,
    rows_in,
    normed_in,
    cosine_ref,
    sine_ref,
    key_cosine_ref,
    key_sine_ref,
    resid_ref,
    d_mid_ref,
    scales_ref,
    gains_ref,
    units_own_ref,
    units_other_ref,
    sum_ref,
    tokens_ref,
    total_ref,
    units_ref,
    units_got_ref,
    units_mine_ref,
    keyval_ref,
    rows_ref,
    normed_ref,
    d_all,
    d_out,
    delta,
    d_query,
    d_block,
    first_put,
    held_keys,
    swapped,
    d_raw,
    out_rows,
    parts,
    out_parts,
    held,
    out_held,
    across_got,
    along_put,
    along_got,
    value,
    near,
    blocks,
    total_send,
    total_recv,
    key_send,
    key_recv,
    place_sem,
    peer_sem,
    send_sem,
    recv_sem,
    out_send,
    out_recv,
    quad_send,
    quad_recv,
    load_sem,
    bulk_send,
    bulk_recv,
):
    tokens = query_ref.shape[1]
    half = tokens // 2
    width = resid_ref.shape[1]
    share = out_parts.shape[1]
    pairs = chips // 4
    scale = 1.0 / math.sqrt(HD)
    peers = quad_peers(chips)
    side, core, to_side, to_core, around = peers
    rings = [Ring(chips, 1, share, send_sem.at[slot], recv_sem.at[slot]) for slot in range(2)]
    ring = rings[0]
    out_ring = Ring(chips, 1, share, out_send, out_recv)
    chip = ring.chip
    gains_total = Total(value, near, blocks, total_send, total_recv, peers, chip)
    arrays = [
        pltpu.make_async_copy(rows_in.at[2], rows_ref.at[2], load_sem.at[3]),
        pltpu.make_async_copy(keyval_in, keyval_ref, load_sem.at[4]),
        pltpu.make_async_copy(normed_in, normed_ref, load_sem.at[5]),
        pltpu.make_async_copy(rows_in.at[0:2], rows_ref.at[0:2], load_sem.at[6]),
    ]
    d_all[core, side] = d_proj_ref[...]
    wide_barrier(to_side, to_core, around)

    def quad_copy(source, target, index, device):
        return remote(source, target, quad_send.at[index], quad_recv.at[index], device)

    def bulk(kind):
        return remote(
            units_ref.at[pl.ds(kind * (units_ref.shape[0] // 3), units_ref.shape[0] // 3)],
            units_got_ref.at[pl.ds(kind * (units_ref.shape[0] // 3), units_ref.shape[0] // 3)],
            bulk_send.at[kind],
            bulk_recv.at[kind],
            to_side,
        )

    units = units_ref.shape[0]
    ours = out_rows.reshape(6 * HD, width).at[pl.ds(0, units)]
    theirs = parts.reshape(2 * chips * share, width).at[pl.ds(0, units)]
    loads = (
        pltpu.make_async_copy(units_own_ref.at[1], ours, load_sem.at[0]),
        pltpu.make_async_copy(units_other_ref.at[1], theirs, load_sem.at[1]),
    )
    store = pltpu.make_async_copy(ours, units_ref, load_sem.at[2])
    spare = held.reshape(2 * (chips - 1) * share, width).at[pl.ds(0, units)]
    mine_loads = (
        pltpu.make_async_copy(units_own_ref.at[0], ours, load_sem.at[7]),
        pltpu.make_async_copy(units_other_ref.at[0], spare, load_sem.at[8]),
    )
    mine_store = pltpu.make_async_copy(ours, units_mine_ref, load_sem.at[9])
    mine_loads[1].start()

    def add_up(more):
        for kind in range(3):
            rows = slice(kind * units // 3, (kind + 1) * units // 3)
            ours[rows] = (ours[rows].astype(single) + more[rows].astype(single)).astype(bfloat)
    for load in loads:
        load.start()
    for array in arrays:
        array.start()
    quarter = tokens // 8
    halves = [slice(part * quarter, part * quarter + quarter) for part in range(2)]
    along = [
        quad_copy(d_all.at[core, side, rows], d_all.at[core, side, rows], part, to_side)
        for part, rows in enumerate(halves)
    ]
    across = quad_copy(d_all.at[core, side], d_all.at[core, side], 2, to_core)
    relay = [
        quad_copy(d_all.at[core, 1 - side, rows], d_all.at[core, 1 - side, rows], 3 + part, to_core)
        for part, rows in enumerate(halves)
    ]
    for part in range(2):
        along[part].start()
    across.start()
    d_query[...] = jnp.zeros_like(d_query)
    for load in loads:
        load.wait()
    add_up(theirs)
    store.start()
    for part in range(2):
        along[part].wait()
        relay[part].start()
    store.wait()
    bulk(0).start()
    bulk(1).start()
    mine_loads[0].start()
    across.wait()
    for load in mine_loads:
        load.wait()
    add_up(spare)
    mine_store.start()
    for part in range(2):
        relay[part].wait()
    for array in arrays:
        array.wait()
    d_rows = d_all[...].reshape(tokens, width)
    for head in range(2):
        columns = slice(head * HD, head * HD + HD)
        made = dot_nt(d_rows, rows_ref[2, columns]).astype(bfloat)
        d_out[head] = made
        row_dot = jnp.sum(
            made.astype(single) * attended_ref[:, columns].astype(single), axis=-1, keepdims=True
        )
        delta[head] = jnp.broadcast_to(row_dot, delta.shape[1:])

    def place(slot, head, start):
        deep = 2 * head + core if slot == 1 else 2 * core + head
        for unit in range(4):
            source = out_rows.at[slot, head, pl.ds(unit * share, share)]
            owner = deep * pairs + unit // 2
            target = out_parts.at[owner] if slot == 2 else parts.at[slot, owner]
            sem = place_sem.at[slot, head, unit]

            def here():
                return pltpu.make_async_copy(source, target, sem)

            def there():
                return remote(source, target, sem, peer_sem.at[slot, head, unit], to_core)

            @pl.when(core == unit % 2)
            def _():
                if start:
                    here().start()
                else:
                    here().wait()
                    there().wait_recv()

            @pl.when(core != unit % 2)
            def _():
                if start:
                    there().start()
                else:
                    there().wait_send()

    def term(slot, head, left, right):
        out_rows[slot, head] = dot_tn(left, right).astype(bfloat)
        place(slot, head, True)

    def block(way, owner, own):
        key = keyval_ref[owner, 0, way * half : way * half + half]
        val = keyval_ref[owner, 1, way * half : way * half + half]
        row = lax.broadcasted_iota(jnp.int32, (tokens, half), 0)
        column = lax.broadcasted_iota(jnp.int32, (tokens, half), 1)
        allowed = row + (chip - owner) * tokens - way * half >= column

        def one_head(head, carried):
            bent = jnp.tanh(dot_nt(query_ref[head], key) * (scale / softcap))
            inverse = jnp.concatenate([inverse_ref[head]] * (half // 128), axis=1)
            row_dot = jnp.concatenate([delta[head]] * (half // 128), axis=1)
            probs = jnp.exp2((softcap / math.log(2.0)) * bent) * inverse
            if own:
                probs = jnp.where(allowed, probs, 0.0)
            d_probs = dot_nt(d_out[head], val)
            d_scores = (probs * (d_probs - row_dot) * (1.0 - bent * bent)).astype(bfloat)
            d_block[way, 0] += dot_tn(d_scores, query_ref[head]) * scale
            d_block[way, 1] += dot_tn(probs.astype(bfloat), d_out[head])
            d_query[head] += dot_nn(d_scores, key)
            return carried

        for head in range(2):
            one_head(head, 0)

    def key_copy(way, kind, step, first):
        return remote(
            first_put.at[way, kind] if first else held_keys.at[way, step - 1, kind],
            held_keys.at[way, step, kind],
            key_send.at[way, kind, step],
            key_recv.at[way, kind, step],
            {"fsdp": ring.right if way == 0 else ring.left},
        )

    streams = [(way, kind) for kind in range(2) for way in range(2)]

    early = 3

    def key_blocks(step, own=False):
        for way in range(2):
            owner = ring.owner(way, step + 1)
            d_block[way] = jnp.zeros(d_block.shape[1:], single)
            if way == 1:

                @pl.when((step >= early) & (step < chips - 1))
                def _():
                    out_ring.scatter_step(out_parts, out_held, step - early)

            if own:
                block(way, chip, True)
            else:

                @pl.when(owner < chip)
                def _():
                    block(way, owner, False)

    def key_body(step, carried):
        key_blocks(step)
        for way, kind in streams:

            @pl.when(step == 0)
            def _():
                first_put[way, kind] = d_block[way, kind].astype(bfloat)
                key_copy(way, kind, 0, True).start()

            @pl.when(step > 0)
            def _():
                key_copy(way, kind, step - 1, True).wait_recv()
                summed = held_keys[way, step - 1, kind].astype(single) + d_block[way, kind]
                held_keys[way, step - 1, kind] = summed.astype(bfloat)
                key_copy(way, kind, step, False).start()

        @pl.when(step == 0)
        def _():
            for head in range(2):
                left = attended_ref[:, head * HD : head * HD + HD]
                term(2, head, left, d_all[...].reshape(tokens, width))

        @pl.when(step == early - 1)
        def _():
            key_blocks(chips - 1, True)
            for way in range(2):
                for kind in range(2):
                    rows = slice(way * half, way * half + half)
                    swapped[2 + kind, rows] = d_block[way, kind].astype(bfloat)
            for head in range(2):
                place(2, head, False)

        return carried

    lax.fori_loop(0, chips - 1, key_body, 0)
    mine_store.wait()

    normed = normed_ref[...].reshape(tokens, width)
    for way in range(2):
        rows = slice(way * half, way * half + half)
        for kind in range(2):
            key_copy(way, kind, chips - 2, True).wait_recv()
            summed = held_keys[way, chips - 2, kind].astype(single)
            summed = summed + swapped[2 + kind, rows].astype(single)
            swapped[2 + kind, rows] = summed.astype(bfloat)
    swap = quad_copy(swapped.at[3 - side], swapped.at[side], 5, to_side)
    swap.start()
    out_ring.scatter_step(out_parts, out_held, chips - 4)
    for head in range(2):
        turned = turn(d_query[head] * scale, cosine_ref[...], -sine_ref[...])
        d_raw[head] = turned.astype(bfloat)
        term(0, head, d_raw[head], normed)
    out_ring.scatter_step(out_parts, out_held, chips - 3)
    for head in range(2):
        place(0, head, False)
    rings[0].scatter_step(parts.at[0], held.at[0], 0)
    swap.wait()
    bulk(2).start()
    swapped[side] = swapped[2 + side]
    for head in range(2):
        turned = turn(swapped[head].astype(single), key_cosine_ref[...], -key_sine_ref[...])
        d_raw[2 + head] = turned.astype(bfloat)
        term(1, head, d_raw[2 + head], normed)
    out_ring.scatter_step(out_parts, out_held, chips - 2)
    rings[0].scatter_step(parts.at[0], held.at[0], 1)
    span = width // 3

    def d_input(tile, carried):
        columns = pl.ds(pl.multiple_of(tile * span, span), span)
        made = dot_nn(d_raw[0], rows_ref[0, 0:HD, columns])
        made = made + dot_nn(d_raw[1], rows_ref[0, HD:, columns])
        made = made + dot_nn(d_raw[2], rows_ref[1, 0:HD, columns])
        made = made + dot_nn(d_raw[3], rows_ref[1, HD:, columns])
        out_rows[0, :, :, columns] = made.reshape(2, half, span).astype(bfloat)
        return carried

    for head in range(2):
        place(1, head, False)
    rings[1].scatter_step(parts.at[1], held.at[1], 0)
    lax.fori_loop(0, 3, d_input, 0)
    across = quad_copy(out_rows.at[0, 1 - core], across_got, 6, to_core)
    mine = pl.ds(pl.multiple_of(side * (half // 2), half // 2), half // 2)
    other = pl.ds(pl.multiple_of((1 - side) * (half // 2), half // 2), half // 2)
    along = quad_copy(along_put, along_got, 7, to_side)
    across.start()

    def body(step, carried):
        rings[1].scatter_step(parts.at[1], held.at[1], step)

        @pl.when(step < chips - 2)
        def _():
            rings[0].scatter_step(parts.at[0], held.at[0], step + 1)

        @pl.when(step == 1)
        def _():
            across.wait()
            given = out_rows[0, core, other].astype(single) + across_got[other].astype(single)
            along_put[...] = given.astype(bfloat)
            along.start()
            tokens_ref[...] = out_rows[0, core, mine].astype(single) + across_got[mine].astype(single)

        @pl.when(step == 4)
        def _():
            along.wait()
            tokens_ref[...] = tokens_ref[...] + along_got[...].astype(single)
            d_norm, d_gain = norm_back(resid_ref[...], scales_ref[0:1], tokens_ref[...])
            tokens_ref[...] = d_mid_ref[...] + d_norm
            value[0] = gains_ref[...]
            value[0, 0:1] = d_gain
            gains_total.start()

        @pl.when(step == 5)
        def _():
            gains_total.over_cores()

        @pl.when(step == 6)
        def _():
            gains_total.over_ring()

        return carried

    lax.fori_loop(1, chips - 1, body, 0)
    total_ref[...] = gains_total.end()
    out_ring.scatter_end(out_parts, out_held, sum_ref.at[pl.ds(2 * share, share)])
    for slot in range(2):
        rows = pl.ds(slot * share, share)
        rings[slot].scatter_end(parts.at[slot], held.at[slot], sum_ref.at[rows])
        rings[slot].finish(out_held.at[0, 0, 0 : ring.size])
    out_ring.finish(out_held.at[0, 0, 0 : out_ring.size])

    def settle(step, carried):
        for way, kind in streams:
            key_copy(way, kind, step, True).wait_send()
        return carried

    lax.fori_loop(0, chips - 1, settle, 0)
    for kind in range(3):
        bulk(kind).wait()


def tail(
    d_proj, query, keyval, attended, inverse, rows, normed, turns, locals_, own, other, chips, ident
):
    tokens = query.shape[1]
    tok_rows = tokens // 4
    width = rows.shape[2]
    share = tokens // 8
    half = tokens // 2
    vmem = pl.BlockSpec(memory_space=pltpu.VMEM)
    anywhere = pl.BlockSpec(memory_space=pl.ANY)
    return pl.pallas_call(
        functools.partial(tail_kernel, chips),
        out_shape=(
            jax.ShapeDtypeStruct((3 * share, width), single),
            jax.ShapeDtypeStruct((tok_rows, width), single),
            jax.ShapeDtypeStruct((4, width), single),
            jax.ShapeDtypeStruct(own.shape[1:], bfloat),
            jax.ShapeDtypeStruct(own.shape[1:], bfloat),
            jax.ShapeDtypeStruct(own.shape[1:], bfloat),
        ),
        in_specs=[vmem] * 2
        + [anywhere, vmem, vmem, anywhere, anywhere]
        + [vmem] * 8
        + [anywhere] * 2,
        out_specs=(vmem,) * 3 + (anywhere,) * 3,
        scratch_shapes=[
            pltpu.VMEM(keyval.shape, bfloat),
            pltpu.VMEM(rows.shape, bfloat),
            pltpu.VMEM(normed.shape, bfloat),
            pltpu.VMEM((2, 2, tok_rows, width), bfloat),
            pltpu.VMEM((2, tokens, HD), bfloat),
            pltpu.VMEM((2, tokens, 128), single),
            pltpu.VMEM((2, tokens, HD), single),
            pltpu.VMEM((2, 2, half, HD), single),
            pltpu.VMEM((2, 2, half, HD), bfloat),
            pltpu.VMEM((2, chips - 1, 2, half, HD), bfloat),
            pltpu.VMEM((4, tokens, HD), bfloat),
            pltpu.VMEM((4, tokens, HD), bfloat),
            pltpu.VMEM((3, 2, HD, width), bfloat),
            pltpu.VMEM((2, chips, share, width), bfloat),
            pltpu.VMEM((chips, share, width), bfloat),
            pltpu.VMEM((2, 2, chips - 1, share // 2, width), bfloat),
            pltpu.VMEM((2, chips - 1, share // 2, width), bfloat),
            pltpu.VMEM((2 * tok_rows, width), bfloat),
            pltpu.VMEM((tok_rows, width), bfloat),
            pltpu.VMEM((tok_rows, width), bfloat),
        ]
        + total_scratch(chips, width)
        + [
            pltpu.SemaphoreType.DMA((2, 2, chips - 1)),
            pltpu.SemaphoreType.DMA((2, 2, chips - 1)),
            pltpu.SemaphoreType.DMA((3, 2, 4)),
            pltpu.SemaphoreType.DMA((3, 2, 4)),
            pltpu.SemaphoreType.DMA((2, 2, 1, chips - 1)),
            pltpu.SemaphoreType.DMA((2, 2, 1, chips - 1)),
            pltpu.SemaphoreType.DMA((2, 1, chips - 1)),
            pltpu.SemaphoreType.DMA((2, 1, chips - 1)),
            pltpu.SemaphoreType.DMA((8,)),
            pltpu.SemaphoreType.DMA((8,)),
            pltpu.SemaphoreType.DMA((10,)),
            pltpu.SemaphoreType.DMA((3,)),
            pltpu.SemaphoreType.DMA((3,)),
        ],
        compiler_params=pltpu.CompilerParams(
            collective_id=ident, has_side_effects=True, vmem_limit_bytes=63 * 2**20
        ),
        cost_estimate=cost(160),
    )(d_proj, query, keyval, attended, inverse, rows, normed, *turns, *locals_, own, other)


def feed_kernel(
    chips,
    pieces,
    resid_ref,
    projected_ref,
    dy_ref,
    scales_ref,
    own_ref,
    side_ref,
    core_ref,
    diag_ref,
    result_ref,
    d_mid_ref,
    d_projected_ref,
    d_gains_ref,
    terms_ref,
    other_ref,
    weights,
    x_all,
    y_all,
    mid,
    both,
    hidden,
    part,
    held,
    chunk,
    wide,
    stage,
    load_sem,
    bulk_send,
    bulk_recv,
    stage_sem,
    other_sem,
    send_sem,
    recv_sem,
):
    tok_rows, width = resid_ref.shape
    units = own_ref.shape[0] // 3
    whole = 4 * units
    half = tok_rows // 2
    rings = [
        Ring(chips, pieces, tok_rows, send_sem.at[phase], recv_sem.at[phase]) for phase in range(4)
    ]
    chip = rings[0].chip
    loads = []
    for slot, ref in enumerate((own_ref, side_ref, core_ref, diag_ref)):
        for kind in range(3 if slot % 2 == 0 else 2):
            loads.append(
                pltpu.make_async_copy(
                    ref.at[pl.ds(kind * units, units)],
                    weights.at[pl.ds(kind * whole + slot * units, units)],
                    load_sem.at[slot, kind],
                )
            )
    for load in loads:
        load.start()
    mid[...] = resid_ref[...] + norm_scale(projected_ref[...], scales_ref[1:2])
    x_all[chip] = norm_scale(mid[...], scales_ref[2:3]).astype(bfloat)
    core = lax.axis_index("fsdp") % 2
    to_core = {"fsdp": 2 * chip + 1 - core}
    to_side = {"head": 1 - lax.axis_index("head")}
    quad_barrier(to_side, to_core, rings[0].right, rings[0].left)
    down_rows = [pl.ds(2 * whole + slot * units, units) for slot in range(4)]
    bulk_side = remote(
        own_ref.at[pl.ds(2 * units, units)],
        weights.at[down_rows[1]],
        bulk_send.at[0],
        bulk_recv.at[0],
        to_side,
    )
    bulk_diag = remote(
        weights.at[down_rows[1]],
        weights.at[down_rows[3]],
        bulk_send.at[1],
        bulk_recv.at[1],
        to_core,
    )
    bulk_side.start()
    span = width // 3

    def segments(pair):
        for hop in range(2):
            for way in range(2):
                start = hop * tok_rows + way * half
                owner = rings[0].owner(way, 2 * pair + hop)
                yield owner, pl.ds(way * half, half), pl.ds(start, half)

    def fetch(all_ref, pair):
        for owner, rows, here in segments(pair):
            chunk[here] = all_ref[owner, rows]

    def put(ref, pair, columns, value):
        for owner, rows, here in segments(pair):
            ref[owner, rows, columns] = value[here.start : here.start + half].astype(ref.dtype)

    def take(ref, pair, columns):
        return jnp.concatenate(
            [ref[owner, rows, columns] for owner, rows, here in segments(pair)], axis=0
        )

    def polls(ring, all_ref, pair):
        def poll(index):
            @pl.when(2 * pair + 2 < chips)
            def _():
                ring.gather_step(all_ref, 2 * pair + 2 + index // 2, index % 2)

        return poll

    def down(pair):
        chunk[:, 0:whole] = take(hidden, pair, slice(None))

        def columns_of(tile, carried):
            columns = pl.ds(pl.multiple_of(tile * span, span), span)
            put(part, pair, columns, dot_nn(chunk[:, 0:whole], weights[2 * whole :, columns]))
            return carried

        lax.fori_loop(0, 3, columns_of, 0)

    def gate_up(tile):
        rows = slice(tile * span, tile * span + span)
        wide[:, rows] = dot_nt(chunk[...], weights[rows])

    def unit(pair):
        put(both, pair, slice(None), wide[...])
        value, slope = gelu_parts(wide[:, 0:whole])
        put(hidden, pair, slice(None), value * wide[:, whole:])

    last = chips // 2 - 1

    def forward(pair, carried):
        poll = polls(rings[0], x_all, pair)
        fetch(x_all, pair)
        for tile in range(3):
            gate_up(tile)
            poll(tile)
        unit(pair)

        @pl.when(pair == last - 1)
        def _():
            bulk_side.wait_recv()
            bulk_diag.start()
            bulk_diag.wait_recv()
            down(0)

        poll(3)
        return carried

    for step in range(2):
        for piece in range(pieces):
            rings[0].gather_step(x_all, step, piece)
        if step == 0:
            for load in loads:
                load.wait()
    lax.fori_loop(0, last, forward, 0)
    rings[1].scatter_step(part, held, 0)
    down(1)
    fetch(x_all, last)
    gate_up(0)
    rings[1].scatter_step(part, held, 1)
    gate_up(1)
    gate_up(2)
    unit(last)

    def spread(step, carried):
        rings[1].scatter_step(part, held, step, 0)

        @pl.when((step % 2 == 0) & (step < chips - 2))
        def _():
            down(step // 2 + 1)

        rings[1].scatter_step(part, held, step, 1)
        return carried

    lax.fori_loop(2, chips - 1, spread, 0)
    ours = pl.ds(0, tok_rows)
    rings[1].scatter_end(part, held, wide)
    result_ref[...] = mid[...] + norm_scale(wide[ours], scales_ref[3:4])
    d_ffn, d_gain = norm_back(wide[ours], scales_ref[3:4], dy_ref[...])
    d_gains_ref[0:1] = jnp.zeros_like(d_gain)
    d_gains_ref[3:4] = d_gain
    y_all[chip] = d_ffn.astype(bfloat)
    rings[0].finish(x_all.at[0, 0 : rings[0].size])
    rings[1].finish(x_all.at[0, 0 : rings[0].size])
    bulk_side.wait_send()
    bulk_diag.wait_send()

    def d_input(pair):
        chunk[...] = take(both, pair, slice(None))

        def columns_of(tile, carried):
            columns = pl.ds(pl.multiple_of(tile * span, span), span)
            put(part, pair, columns, dot_nn(chunk[...], weights[0 : 2 * whole, columns]))
            return carried

        lax.fori_loop(0, 3, columns_of, 0)

    third = whole // 3

    def d_units(pair, tile):
        columns = slice(tile * third, tile * third + third)
        ups = slice(whole + tile * third, whole + tile * third + third)
        for owner, rows, here in segments(pair):
            value, slope = gelu_parts(both[owner, rows, columns].astype(single))
            upper = both[owner, rows, ups].astype(single)
            d_hidden = wide[here, columns]
            both[owner, rows, columns] = (d_hidden * upper * slope).astype(bfloat)
            both[owner, rows, ups] = (d_hidden * value).astype(bfloat)

    def d_hidden(first, end):
        wide[:, first:end] = dot_nt(chunk[...], weights[2 * whole + first : 2 * whole + end])

    def backward(pair, carried):
        poll = polls(rings[2], y_all, pair)
        fetch(y_all, pair)
        d_hidden(0, 2 * third)
        poll(0)
        d_hidden(2 * third, whole)
        d_units(pair, 0)
        poll(1)
        d_units(pair, 1)
        d_units(pair, 2)
        poll(2)

        @pl.when(pair < 2)
        def _():
            d_input(pair)

        poll(3)
        return carried

    for step in range(2):
        for piece in range(pieces):
            rings[2].gather_step(y_all, step, piece)
    lax.fori_loop(0, last, backward, 0)
    rings[3].scatter_step(part, held, 0)
    fetch(y_all, last)
    d_hidden(0, 2 * third)
    d_hidden(2 * third, whole)
    d_units(last, 0)
    rings[3].scatter_step(part, held, 1)
    d_units(last, 1)
    d_units(last, 2)
    rows_tile = stage.shape[1]
    tiles = 3 * whole // rows_tile
    upper_tiles = 2 * whole // rows_tile

    cut = units // 3

    def pieces_of(tile):
        for quarter in range(4):
            block = 4 * tile + quarter
            kind, slot, third = block // 12, (block // 3) % 4, block % 3
            source = stage.at[tile % 2, pl.ds(quarter * cut, cut)]
            rows = pl.ds(pl.multiple_of(kind * units + third * cut, cut), cut)
            sem = stage_sem.at[tile % 2, quarter]
            goal = terms_ref.at[slot, rows], other_ref.at[slot - 2, rows]
            there = functools.partial(
                remote, source, goal[1], sem, other_sem.at[tile, quarter], to_core
            )
            yield slot, functools.partial(pltpu.make_async_copy, source, goal[0], sem), there

    def keep(tile):
        for slot, here, there in pieces_of(tile):

            @pl.when(slot < 2)
            def _():
                here().start()

            @pl.when(slot >= 2)
            def _():
                there().start()

    def kept(tile):
        for slot, here, there in pieces_of(tile):

            @pl.when(slot < 2)
            def _():
                here().wait()

            @pl.when(slot >= 2)
            def _():
                there().wait_send()

    def grads(tile):
        @pl.when(tile >= 2)
        def _():
            kept(tile - 2)

        @pl.when(tile < upper_tiles)
        def _():
            columns = pl.ds(pl.multiple_of(tile * rows_tile, rows_tile), rows_tile)
            left = both[:, :, columns].reshape(chips * tok_rows, rows_tile)
            stage[tile % 2] = dot_tn(left, x_all[...].reshape(chips * tok_rows, width)).astype(bfloat)

        @pl.when(tile >= upper_tiles)
        def _():
            columns = pl.ds(
                pl.multiple_of((tile - upper_tiles) * rows_tile, rows_tile), rows_tile
            )
            left = hidden[:, :, columns].reshape(chips * tok_rows, rows_tile)
            stage[tile % 2] = dot_tn(left, y_all[...].reshape(chips * tok_rows, width)).astype(bfloat)

        keep(tile)

    d_input(2)

    def spread_back(step, carried):
        tile = 2 * (step - 3) + 2 * ((6 - step) // 4)
        rings[3].scatter_step(part, held, step, 0)

        @pl.when(step == 3)
        def _():
            d_input(3)

        @pl.when(step != 3)
        def _():
            grads(tile)

        rings[3].scatter_step(part, held, step, 1)

        @pl.when(step != 3)
        def _():
            grads(tile + 1)

        return carried

    lax.fori_loop(2, chips - 1, spread_back, 0)
    lax.fori_loop(8, tiles, lambda tile, carried: grads(tile) or carried, 0)
    rings[3].scatter_end(part, held, wide)
    d_norm, d_gain = norm_back(mid[...], scales_ref[2:3], wide[ours])
    d_gains_ref[2:3] = d_gain
    d_mid_ref[...] = dy_ref[...] + d_norm
    d_projected, d_gain = norm_back(projected_ref[...], scales_ref[1:2], d_mid_ref[...])
    d_gains_ref[1:2] = d_gain
    d_projected_ref[...] = d_projected.astype(bfloat)
    rings[2].finish(x_all.at[0, 0 : rings[0].size])
    rings[3].finish(x_all.at[0, 0 : rings[0].size])
    kept(tiles - 2)
    kept(tiles - 1)

    def gained(tile, carried):
        for slot, here, there in pieces_of(tile):

            @pl.when(slot >= 2)
            def _():
                there().wait_recv()

        return carried

    lax.fori_loop(0, tiles, gained, 0)


def feed_forward(resid_in, projected, grad_out, scales, shares, chips, ident):
    tok_rows, width = resid_in.shape
    units = shares[0].shape[0] // 3
    whole = 4 * units
    pieces = 2
    vmem = pl.BlockSpec(memory_space=pltpu.VMEM)
    anywhere = pl.BlockSpec(memory_space=pl.ANY)
    return pl.pallas_call(
        functools.partial(feed_kernel, chips, pieces),
        out_shape=(
            jax.ShapeDtypeStruct((tok_rows, width), single),
            jax.ShapeDtypeStruct((tok_rows, width), single),
            jax.ShapeDtypeStruct((tok_rows, width), bfloat),
            jax.ShapeDtypeStruct((4, width), single),
            jax.ShapeDtypeStruct((2, 3 * units, width), bfloat),
            jax.ShapeDtypeStruct((2, 3 * units, width), bfloat),
        ),
        in_specs=[vmem] * 4 + [anywhere] * 4,
        out_specs=(vmem, vmem, vmem, vmem, anywhere, anywhere),
        scratch_shapes=[
            pltpu.VMEM((3 * whole, width), bfloat),
            pltpu.VMEM((chips, tok_rows, width), bfloat),
            pltpu.VMEM((chips, tok_rows, width), bfloat),
            pltpu.VMEM((tok_rows, width), single),
            pltpu.VMEM((chips, tok_rows, 2 * whole), bfloat),
            pltpu.VMEM((chips, tok_rows, whole), bfloat),
            pltpu.VMEM((chips, tok_rows, width), bfloat),
            pltpu.VMEM((2, chips - 1, tok_rows // 2, width), bfloat),
            pltpu.VMEM((2 * tok_rows, width), bfloat),
            pltpu.VMEM((2 * tok_rows, width), single),
            pltpu.VMEM((2, whole // 3, width), bfloat),
            pltpu.SemaphoreType.DMA((4, 3)),
            pltpu.SemaphoreType.DMA((2,)),
            pltpu.SemaphoreType.DMA((2,)),
            pltpu.SemaphoreType.DMA((2, 4)),
            pltpu.SemaphoreType.DMA((9, 4)),
            pltpu.SemaphoreType.DMA((4, 2, pieces, chips - 1)),
            pltpu.SemaphoreType.DMA((4, 2, pieces, chips - 1)),
        ],
        compiler_params=pltpu.CompilerParams(
            collective_id=ident, has_side_effects=True, vmem_limit_bytes=63 * 2**20
        ),
        cost_estimate=cost(205),
    )(resid_in, projected, grad_out, scales, *shares)


def general_device(
    tokens,
    cotangent,
    gains,
    gains_first,
    gains_second,
    attn_weight,
    attn_first,
    attn_second,
    ffn_weight,
    ffn_first,
    ffn_second,
):
    devices = lax.axis_size("fsdp")
    chips = devices // 2
    side = lax.axis_index("head")
    place = lax.axis_index("fsdp")
    core, chip = place % 2, place // 2
    tok_rows = tokens.shape[1]
    super_rows = 4 * tok_rows
    seq_len = min(SEQ_LEN, super_rows * chips)
    share = attn_weight.shape[1]
    pairs = chips // 4
    width = tokens.shape[2]
    scale = 1.0 / math.sqrt(HD)

    def swap_core(value):
        return lax.ppermute(value, "fsdp", [(index, index ^ 1) for index in range(devices)])

    def swap_side(value):
        return lax.ppermute(value, "head", [(0, 1), (1, 0)])

    def in_order(own, other, index, axis):
        return jnp.where(
            index == 0, jnp.stack([own, other], axis), jnp.stack([other, own], axis)
        )

    def pick(value, index, axis=0):
        return lax.dynamic_index_in_dim(value, index, axis, keepdims=False)

    def quad_gather(value):
        value = in_order(value, swap_side(value), side, 0)
        value = in_order(value, swap_core(value), core, 0)
        return value.reshape((super_rows,) + value.shape[3:])

    def quad_scatter(partial):
        partial = partial.reshape(2, 2, tok_rows, width)
        mine = pick(partial, core) + swap_core(pick(partial, 1 - core).astype(bfloat)).astype(single)
        return pick(mine, side) + swap_side(pick(mine, 1 - side).astype(bfloat)).astype(single)

    scales = lax.all_gather(gains.astype(bfloat), ("head", "fsdp"), axis=1, tiled=True).astype(single)
    attn_low = attn_weight.astype(bfloat)
    ffn_low = ffn_weight.astype(bfloat).transpose(1, 0, 2)
    ffn_pair = jnp.concatenate([ffn_low, swap_side(ffn_low)], axis=1)

    ring_rows = ring_gather(attn_low.reshape(3 * share, width), chips, 0)
    ring_rows = ring_rows.reshape(2, 2, pairs, 3, share, width)

    def query_rows(slot):
        rows = ring_rows[:, :, :, slot]
        other = swap_core(pick(rows, 1 - core))
        return in_order(pick(rows, core), other, core, 2).reshape(2 * HD, width)

    def keyval_rows():
        rows = ring_rows[:, :, :, 1]
        other = swap_core(pick(rows, 1 - core, 1))
        return in_order(pick(rows, core, 1), other, core, 2).reshape(2 * HD, width)

    w_query, w_keyval, w_out = query_rows(0), keyval_rows(), query_rows(2)

    resid_in = tokens[0]
    grad_out = cotangent[0]
    normed_one = norm_scale(resid_in, scales[0]).astype(bfloat)
    normed_all = quad_gather(normed_one)
    positions = chip * super_rows + jnp.arange(super_rows, dtype=jnp.int32)
    angles = turn_angles(positions % seq_len, HD)
    query_raw = jnp.einsum("td,fd->tf", normed_all, w_query, preferred_element_type=single)
    keyval_raw = jnp.einsum("td,fd->tf", normed_all, w_keyval, preferred_element_type=single)
    query = rotate(query_raw.reshape(super_rows, 2, HD), angles, 1.0).astype(bfloat)
    key_angles = jnp.where(side == 0, angles, 0.0)
    keyval = rotate(keyval_raw.reshape(super_rows, 2, HD), key_angles, 1.0).astype(bfloat)
    keyval = in_order(pick(keyval, side, 1), swap_side(pick(keyval, 1 - side, 1)), side, 0)
    keyval_all = ring_gather(keyval.reshape(2 * super_rows, HD), chips, 1)
    keyval_all = keyval_all.reshape(chips, 2, super_rows, HD)
    key_all = keyval_all[:, 0].reshape(chips * super_rows, HD)
    value_all = keyval_all[:, 1].reshape(chips * super_rows, HD)

    key_pos = jnp.arange(chips * super_rows, dtype=jnp.int32)
    distance = positions[:, None] - key_pos[None, :]
    same_seq = (positions // seq_len)[:, None] == (key_pos // seq_len)[None, :]
    allowed = (distance >= 0) & (distance < WIN) & same_seq

    def score_block():
        raw = jnp.einsum("qgd,kd->gqk", query, key_all, preferred_element_type=single)
        bent = jnp.tanh(raw * (scale / softcap))
        return bent, jnp.where(allowed, jnp.exp(softcap * bent), 0.0)

    bent, powers = score_block()
    total = jnp.sum(powers, axis=-1, keepdims=True)
    attended = jnp.einsum(
        "gqk,kd->gqd", powers.astype(bfloat), value_all, preferred_element_type=single
    )
    attended = (attended / total).transpose(1, 0, 2).reshape(super_rows, 2 * HD).astype(bfloat)
    projected = quad_scatter(jnp.dot(attended, w_out, preferred_element_type=single))
    resid_mid = resid_in + norm_scale(projected, scales[1])
    normed_two = norm_scale(resid_mid, scales[2]).astype(bfloat)

    ffn_all = jnp.concatenate([ffn_pair, swap_core(ffn_pair)], axis=1)
    w_gate, w_up, w_down = ffn_all[0], ffn_all[1], ffn_all[2]
    ring_tokens = chips * tok_rows
    normed_ring = ring_gather(normed_two, chips, 2).reshape(ring_tokens, width)
    gate_part = jnp.einsum("td,rd->tr", normed_ring, w_gate, preferred_element_type=single)
    up_part = jnp.einsum("td,rd->tr", normed_ring, w_up, preferred_element_type=single)
    hidden = hidden_unit(gate_part, up_part).astype(bfloat)
    ffn_part = jnp.dot(hidden, w_down, preferred_element_type=single).astype(bfloat)
    ffn_acc = ring_scatter(ffn_part.reshape(chips, tok_rows, width), chips, 3)
    result = resid_mid + norm_scale(ffn_acc, scales[3])

    ignored, post_back = jax.vjp(norm_scale, ffn_acc, scales[3])
    d_ffn, d_gain3 = post_back(grad_out)
    d_ffn_ring = ring_gather(d_ffn.astype(bfloat), chips, 4).reshape(ring_tokens, width)
    d_hidden = jnp.einsum("td,rd->tr", d_ffn_ring, w_down, preferred_element_type=single)
    ignored, unit_back = jax.vjp(hidden_unit, gate_part, up_part)
    d_gate, d_up = unit_back(d_hidden)
    d_gate = d_gate.astype(bfloat)
    d_up = d_up.astype(bfloat)
    d_normed = jnp.dot(d_gate, w_gate, preferred_element_type=single)
    d_normed = (d_normed + jnp.dot(d_up, w_up, preferred_element_type=single)).astype(bfloat)
    d_normed_two = ring_scatter(d_normed.reshape(chips, tok_rows, width), chips, 5)

    def ffn_rows(left, right):
        return jnp.einsum("tr,td->rd", left, right, preferred_element_type=single)

    ffn_terms = jnp.stack(
        [ffn_rows(d_gate, normed_ring), ffn_rows(d_up, normed_ring), ffn_rows(hidden, d_ffn_ring)]
    )
    units = ffn_weight.shape[0]
    ffn_terms = ffn_terms.reshape(3, 2, 2, units, width)
    ffn_terms = ffn_terms[:, 0] + swap_core(ffn_terms[:, 1].astype(bfloat)).astype(single)
    grad_ffn = ffn_terms[:, 0] + swap_side(ffn_terms[:, 1].astype(bfloat)).astype(single)

    ignored, mid_back = jax.vjp(norm_scale, resid_mid, scales[2])
    d_mid_norm, d_gain2 = mid_back(d_normed_two)
    d_mid = grad_out + d_mid_norm
    ignored, proj_back = jax.vjp(norm_scale, projected, scales[1])
    d_projected, d_gain1 = proj_back(d_mid)
    d_proj_all = quad_gather(d_projected.astype(bfloat))
    d_attended = jnp.einsum("td,fd->tf", d_proj_all, w_out, preferred_element_type=single)
    d_attended = d_attended.astype(bfloat).reshape(super_rows, 2, HD)

    bent, powers = score_block()
    probs = powers / total
    d_probs = jnp.einsum("qgd,kd->gqk", d_attended, value_all, preferred_element_type=single)
    row_dot = jnp.sum(d_probs * probs, axis=-1, keepdims=True)
    d_raw = (probs * (d_probs - row_dot) * (1.0 - bent * bent)).astype(bfloat)
    d_query = jnp.einsum("gqk,kd->qgd", d_raw, key_all, preferred_element_type=single) * scale
    d_keys = jnp.einsum("gqk,qgd->kd", d_raw, query, preferred_element_type=single) * scale
    d_values = jnp.einsum(
        "gqk,qgd->kd", probs.astype(bfloat), d_attended, preferred_element_type=single
    )
    d_pieces = jnp.stack(
        [d_keys.reshape(chips, super_rows, HD), d_values.reshape(chips, super_rows, HD)], axis=1
    ).astype(bfloat)
    d_keyval = ring_scatter(d_pieces.reshape(chips, 2 * super_rows, HD), chips, 6)
    d_keyval = d_keyval.reshape(2, super_rows, HD).astype(bfloat)
    d_keyval = in_order(pick(d_keyval, side), swap_side(pick(d_keyval, 1 - side)), side, 1)
    d_query_raw = rotate(d_query, angles, -1.0).reshape(super_rows, 2 * HD).astype(bfloat)
    d_keyval_raw = rotate(d_keyval.astype(single), key_angles, -1.0)
    d_keyval_raw = d_keyval_raw.reshape(super_rows, 2 * HD).astype(bfloat)
    d_normed_one = jnp.dot(d_query_raw, w_query, preferred_element_type=single)
    d_normed_one = d_normed_one + jnp.dot(d_keyval_raw, w_keyval, preferred_element_type=single)
    d_normed_one = quad_scatter(d_normed_one)
    ignored, first_back = jax.vjp(norm_scale, resid_in, scales[0])
    d_in_norm, d_gain0 = first_back(d_normed_one)
    tokens_grad = d_mid + d_in_norm

    def attn_rows(left, right):
        rows = jnp.einsum("tf,td->fd", left, right, preferred_element_type=single).astype(bfloat)
        return rows.reshape(2, pairs, 2, share, width)

    term_query = attn_rows(d_query_raw, normed_all)
    term_keyval = attn_rows(d_keyval_raw, normed_all)
    term_out = attn_rows(attended, d_proj_all)

    def to_core(term, axis):
        return in_order(pick(term, core, 2), swap_core(pick(term, 1 - core, 2)), core, axis)

    terms = jnp.stack([to_core(term_query, 0), to_core(term_keyval, 1), to_core(term_out, 0)], axis=3)
    grad_attn = ring_scatter(terms.reshape(chips, 3 * share, width), chips, 7)
    grad_attn = grad_attn.reshape(3, share, width)
    term_gain = jnp.stack([d_gain0, d_gain1, d_gain2, d_gain3])
    grad_gain = lax.psum_scatter(term_gain, ("head", "fsdp"), scatter_dimension=1, tiled=True)

    gains_first_new, gains_second_new, gains_new = adamw(
        gains, gains_first, gains_second, grad_gain, rate_gain, 0.0
    )
    attn_first_new, attn_second_new, attn_weight_new = adamw(
        attn_weight, attn_first, attn_second, grad_attn, rate_matrix, decay_matrix
    )
    ffn_first_new, ffn_second_new, ffn_weight_new = adamw(
        ffn_weight, ffn_first, ffn_second, grad_ffn.transpose(1, 0, 2), rate_matrix, decay_matrix
    )
    return (
        result[None],
        tokens_grad[None],
        gains_first_new,
        gains_second_new,
        gains_new,
        attn_first_new,
        attn_second_new,
        attn_weight_new,
        ffn_first_new,
        ffn_second_new,
        ffn_weight_new,
    )


def step_kernel(
    tiles,
    weight_ref,
    first_ref,
    second_ref,
    own_ref,
    side_ref,
    weight_two_ref,
    first_two_ref,
    second_two_ref,
    grad_two_ref,
    first_out,
    second_out,
    weight_out,
    first_two_out,
    second_two_out,
    weight_two_out,
):
    index = pl.program_id(0)

    @pl.when(index < tiles)
    def _():
        grad = own_ref[...].astype(single) + side_ref[...].astype(single)
        first_out[...], second_out[...], weight_out[...] = adamw(
            weight_ref[...], first_ref[...], second_ref[...], grad, rate_matrix, decay_matrix
        )

    @pl.when(index >= tiles)
    def _():
        first_two_out[...], second_two_out[...], weight_two_out[...] = adamw(
            weight_two_ref[...],
            first_two_ref[...],
            second_two_ref[...],
            grad_two_ref[...],
            rate_matrix,
            decay_matrix,
        )


def step_weights(state, own, side, state_two, grad_two):
    rows, width = state[0].shape
    rows_two = grad_two.shape[0]
    size = 96
    tiles, tiles_two = rows // size, rows_two // size
    block = pl.BlockSpec((size, width), lambda index: (jnp.minimum(index, tiles - 1), 0))
    block_two = pl.BlockSpec((size, width), lambda index: (jnp.maximum(index - tiles, 0), 0))
    return pl.pallas_call(
        functools.partial(step_kernel, tiles),
        grid=(tiles + tiles_two,),
        out_shape=(jax.ShapeDtypeStruct((rows, width), single),) * 3
        + (jax.ShapeDtypeStruct((rows_two, width), single),) * 3,
        in_specs=[block] * 5 + [block_two] * 4,
        out_specs=(block,) * 3 + (block_two,) * 3,
        compiler_params=pltpu.CompilerParams(vmem_limit_bytes=62 * 2**20),
        cost_estimate=cost(20),
    )(*state, own, side, *state_two, grad_two)


def per_device(
    tokens,
    cotangent,
    gains,
    gains_first,
    gains_second,
    attn_weight,
    attn_first,
    attn_second,
    ffn_weight,
    ffn_first,
    ffn_second,
):
    devices = lax.axis_size("fsdp")
    chips = devices // 2
    side = lax.axis_index("head")
    place = lax.axis_index("fsdp")
    tok_rows = tokens.shape[1]
    share = attn_weight.shape[1]
    width = tokens.shape[2]
    gain_columns = gains.shape[1]
    gain_start = (side * devices + place) * gain_columns

    units = ffn_weight.shape[0]

    def flat(value):
        return value.transpose(1, 0, 2).reshape(3 * units, width)

    ffn_wide = flat(ffn_weight)
    resid_in = tokens[0]
    grad_out = cotangent[0]
    gains_placed = lax.dynamic_update_slice(
        jnp.zeros((4, width), single), gains, (0, gain_start)
    )
    halfway = HD // 2
    pace = jnp.asarray(
        10000.0 ** (-2.0 * np.arange(halfway, dtype=np.float64) / HD)[None, :], dtype=single
    )
    made = front(attn_weight, gains_placed, resid_in, pace, ffn_wide, chips, 0)
    attn_rows, scales, normed_all, query, keyval, attended, inverse, projected = made[:8]
    turns = made[8:12]
    own_units, core_units, side_units, diag_units = made[12:]
    result, d_mid, d_proj_low, gain_rows, terms_own, terms_other = feed_forward(
        resid_in,
        projected,
        grad_out,
        scales,
        (own_units, side_units, core_units, diag_units),
        chips,
        1,
    )
    grad_attn, tokens_grad, gain_total, terms_sent, terms_side, terms_mine = tail(
        d_proj_low,
        query,
        keyval,
        attended,
        inverse,
        attn_rows,
        normed_all,
        turns,
        (resid_in, d_mid, scales, gain_rows),
        terms_own,
        terms_other,
        chips,
        2,
    )
    grad_gain = lax.dynamic_slice(gain_total, (0, gain_start), gains.shape)

    gains_first_new, gains_second_new, gains_new = adamw(
        gains, gains_first, gains_second, grad_gain, rate_gain, 0.0
    )
    def rows_of(value):
        return value.reshape(3 * share, width)

    stepped = step_weights(
        (ffn_wide, flat(ffn_first), flat(ffn_second)),
        terms_mine,
        terms_side,
        (rows_of(attn_weight), rows_of(attn_first), rows_of(attn_second)),
        grad_attn,
    )
    ffn_first_new, ffn_second_new, ffn_weight_new = (
        value.reshape(3, units, width).transpose(1, 0, 2) for value in stepped[:3]
    )
    attn_first_new, attn_second_new, attn_weight_new = (
        value.reshape(3, share, width) for value in stepped[3:]
    )
    return (
        result[None],
        tokens_grad[None],
        gains_first_new,
        gains_second_new,
        gains_new,
        attn_first_new,
        attn_second_new,
        attn_weight_new,
        ffn_first_new,
        ffn_second_new,
        ffn_weight_new,
    )


def solution(mesh):
    by_token = P("fsdp", "head", None)
    by_column = P(None, ("head", "fsdp"))
    by_row = P(None, ("head", "fsdp"), None)
    by_unit = P(("head", "fsdp"), None, None)
    placed = (by_token,) * 2 + (by_column,) * 3 + (by_row,) * 3 + (by_unit,) * 3
    body = per_device if mesh.shape["fsdp"] == 16 else general_device
    return jax.shard_map(
        body, mesh=mesh, in_specs=placed, out_specs=placed, check_vma=False
    )
```
